128 devices in a mesh: rows: 32 (over z, x_lo, y), seq: 4 (over x_hi, core).
Axes of the slice: x: 4 (x_hi: 2, x_lo: 2; x = x_hi * 2 + x_lo), y: 4, z: 4, core: 2. Of those that a mesh axis runs over, the one named last changes fastest.
Arguments:
- tokens: bfloat16 [32, 1024, 768], P('rows', 'seq'), may hold values from -6 to 6
- first_gain: float32 [768], replicated, may hold values from 0.1 to 1.9
- first_shift: float32 [768], replicated, may hold values from -1 to 1
- w_qkv: bfloat16 [768, 2304], replicated, may hold values from -0.21875 to 0.21875
- w_out: bfloat16 [768, 768], replicated, may hold values from -0.875 to 0.875
- second_gain: float32 [768], replicated, may hold values from 0.1 to 1.9
- second_shift: float32 [768], replicated, may hold values from -1 to 1
- w_up: bfloat16 [2, 768, 3072], replicated, may hold values from -0.21875 to 0.21875
- w_down: bfloat16 [2, 3072, 768], replicated, may hold values from -0.109375 to 0.109375
- modality: int32 [32, 1024], P('rows', 'seq'), may hold values from 0 to 1, as said below
- segments: int32 [32, 1024], P('rows', 'seq'), may hold values from 0 to 7, as said below
- partner: int32 [32, 8], P('rows'), may hold values from 0 to 3, as said below
- cotangent: bfloat16 [32, 1024, 768], P('rows', 'seq'), may hold values from -6 to 6
Outputs:
- layer_output: bfloat16 [32, 1024, 768], P('rows', 'seq')
- token_grad: float32 [32, 1024, 768], P('rows', 'seq')
- first_gain_grad: float32 [768], P(('rows', 'seq'))
- first_shift_grad: float32 [768], P(('rows', 'seq'))
- qkv_grad: float32 [768, 2304], P(('rows', 'seq'))
- out_grad: float32 [768, 768], P(('rows', 'seq'))
- second_gain_grad: float32 [768], P(('rows', 'seq'))
- second_shift_grad: float32 [768], P(('rows', 'seq'))
- up_grad: float32 [2, 768, 3072], P(None, ('rows', 'seq'))
- down_grad: float32 [2, 3072, 768], P(None, ('rows', 'seq'))
The draws below stay inside these ranges and needn't reach their ends.
Inputs may be any that keep to these rules, and one draw needn't show every extreme that they name: `segments`: in each row: the document number of each slot among the row's 2 * 4 documents, never falling; 4 documents are images of 197 slots and 4 are captions of one or more slots that fill the other 236; the first document is an image and the last is its caption. `modality`: 0 on slots of image documents, 1 on caption slots. `partner`: for each document of a row in order: the images carry each pair number once, so do the captions; the first and the last document carry the same one.
All inputs are finite; a program needn't handle non-finite values.
Results may differ from the reference program's by a relative error of at most 0.02.
Values may be sent and summed in bfloat16 or wider, within the bound.
No kernel may reach another device: no remote copies, remote signals or barrier semaphores. Data moves between devices by JAX's collectives and lax.ppermute only.
A program may use at most 256 MiB of HBM per device.

```python
import jax
import jax.numpy as jnp
from jax import lax

D = 768
HEADS = 12
HD = 64
FF = 3072
EXPERTS = 2
IMG = 197
NIMG = 4
SLOTS = 1024
TEXT = 236
ROWS = 32


def row_layout(key):
    key_pairs, key_order, key_cuts = jax.random.split(key, 3)
    pair_perm = jax.random.permutation(key_pairs, NIMG).astype(jnp.int32)
    middle = jax.random.permutation(key_order, 2 * NIMG - 2).astype(jnp.int32)
    cut_points = jnp.sort(jax.random.permutation(key_cuts, TEXT - 1)[:NIMG - 1].astype(jnp.int32) + 1)
    boundary = jnp.concatenate([jnp.zeros((1,), jnp.int32), cut_points, jnp.full((1,), TEXT, jnp.int32)])
    cap_lengths = boundary[1:] - boundary[:-1]
    middle_kind = (middle >= NIMG - 1).astype(jnp.int32)
    middle_pair = pair_perm[1 + middle % (NIMG - 1)]
    doc_kind = jnp.concatenate([jnp.zeros((1,), jnp.int32), middle_kind, jnp.ones((1,), jnp.int32)])
    doc_pair = jnp.concatenate([pair_perm[:1], middle_pair, pair_perm[:1]]).astype(jnp.int32)
    doc_lengths = jnp.where(doc_kind == 0, IMG, cap_lengths[doc_pair]).astype(jnp.int32)
    doc_ends = jnp.cumsum(doc_lengths).astype(jnp.int32)
    slot_index = jnp.arange(SLOTS, dtype=jnp.int32)
    doc_index = jnp.sum((slot_index[:, None] >= doc_ends[None, :]).astype(jnp.int32), axis=1).astype(jnp.int32)
    doc_match = doc_index[:, None] == jnp.arange(2 * NIMG, dtype=jnp.int32)[None, :]
    slot_kind = jnp.sum(jnp.where(doc_match, doc_kind[None, :], 0), axis=1).astype(jnp.int32)
    return (slot_kind, doc_index, doc_pair)


def layout(key):
    row_keys = jax.random.split(key, ROWS)
    return jax.vmap(row_layout)(row_keys)


def draw_modality(key, part):
    shared = layout(key)
    return shared[0].astype(jnp.int32)


def draw_segments(key, part):
    shared = layout(key)
    return shared[1].astype(jnp.int32)


def draw_partner(key, part):
    shared = layout(key)
    return shared[2].astype(jnp.int32)


def strengthened(values, stream_key, source, target, shards_of, factor):
    owner, partner = [(jnp.arange(values.shape[dim]) // (values.shape[dim] // shards_of)).reshape([-1 if axis == dim else 1 for axis in range(values.ndim)]) for dim in (source, target)]
    chosen = jax.random.permutation(stream_key, shards_of)[partner]
    strong = (owner == chosen) | (owner == (partner + shards_of // 2) % shards_of)
    return jnp.where(strong, factor * values, values)


def shard_levels(own_key, extent, shards, least, high):
    gain = 1.0
    for dim, blocks in shards:
        steps = jax.random.uniform(jax.random.fold_in(jax.random.fold_in(own_key, 6), dim), (blocks,), jnp.float32, least / len(shards), high / len(shards))
        gain = gain * jnp.repeat(jnp.exp(steps), extent[dim] // blocks).reshape((-1,) + (1,) * (len(extent) - 1 - dim))
    return gain


def bell_draw(key, dims, width, reach, cuts=(), kind=jnp.bfloat16):
    values = jax.random.normal(key, dims, jnp.float32) * width
    if len(cuts) > 0:
        values = shard_levels(key, dims, cuts, -0.22, 0.18) * values
    return jnp.clip(values, min=-reach, max=reach).astype(kind)


def bell_draw_with(rng, extent, width, limit, cuts, heavy, kind=jnp.bfloat16):
    values = width * jax.random.normal(rng, extent, jnp.float32)
    if cuts:
        values = values * shard_levels(rng, extent, cuts, -0.22, 0.18)
    return jnp.clip(strengthened(values, jax.random.fold_in(rng, 3), *heavy), -limit, limit).astype(kind)


def setup_inputs(seed: int = 0) -> dict:
    key_of = jax.random.split(jax.random.key(seed), 14)
    return {
        "tokens": bell_draw_with(key_of[0], (ROWS, SLOTS, D), 1.0, 6.0, ((0, 32), (1, 4)), (0, 2, 32, 2.75)),
        "first_gain": jnp.clip(1.0 + 0.18 * jax.random.normal(key_of[1], (D,), jnp.float32), 0.1, 1.9),
        "first_shift": bell_draw(key_of[2], (D,), 0.2, 1.0, (), jnp.float32),
        "w_qkv": bell_draw(key_of[3], (D, 3 * D), D ** -0.5, 0.21875),
        "w_out": bell_draw(key_of[4], (D, D), (D // 16) ** -0.5, 0.875),
        "second_gain": jnp.clip(1.0 + 0.18 * jax.random.normal(key_of[5], (D,), jnp.float32), 0.1, 1.9),
        "second_shift": bell_draw(key_of[6], (D,), 0.2, 1.0, (), jnp.float32),
        "w_up": bell_draw(key_of[7], (EXPERTS, D, FF), D ** -0.5, 0.21875),
        "w_down": bell_draw(key_of[8], (EXPERTS, FF, D), FF ** -0.5, 0.109375),
        "modality": draw_modality(jax.random.fold_in(key_of[13], 71), 0),
        "segments": draw_segments(jax.random.fold_in(key_of[13], 71), 0),
        "partner": draw_partner(jax.random.fold_in(key_of[13], 71), 0),
        "cotangent": bell_draw(key_of[12], (ROWS, SLOTS, D), 1.0, 6.0, ((0, 32), (1, 4))),
    }


@jax.custom_vjp
def low(v):
    return lax.optimization_barrier(v.astype(jnp.bfloat16)).astype(jnp.float32)

@jax.custom_vjp
def low_back(v):
    return v

def low_keep(v):
    return (low(v), None)

def low_pass(kept, grad):
    return (grad,)

def back_keep(v):
    return (v, None)

def back_low(kept, grad):
    return (low(grad),)
low.defvjp(low_keep, low_pass)
low_back.defvjp(back_keep, back_low)

def matmul(left, right):
    return jnp.dot(left, right, precision=lax.Precision.HIGHEST, preferred_element_type=jnp.float32)

def layer_norm(inputs, gain_vec, shift_vec):
    centred = inputs - lax.optimization_barrier(jnp.mean(inputs, axis=-1, keepdims=True))
    factor = lax.rsqrt(lax.optimization_barrier(jnp.mean(centred * centred, axis=-1, keepdims=True)) + 1e-05)
    return centred * factor * gain_vec + shift_vec

def attend_row(row_items):
    queries, key_rows, value_rows, allowed = row_items
    query_heads = queries.reshape(SLOTS, HEADS, HD)
    key_heads = key_rows.reshape(SLOTS, HEADS, HD)
    value_heads = value_rows.reshape(SLOTS, HEADS, HD)
    scores = jnp.einsum('qhd,khd->hqk', query_heads, key_heads, precision=lax.Precision.HIGHEST)
    scores = low_back(scores)
    scores = jnp.where(allowed[None], scores, -1e+30)
    row_peak = lax.optimization_barrier(jnp.max(scores, axis=-1, keepdims=True))
    exp_scores = jnp.exp(scores - row_peak)
    probability = exp_scores / lax.optimization_barrier(jnp.sum(exp_scores, axis=-1, keepdims=True))
    prob_low = low(probability)
    mixed = jnp.einsum('hqk,khd->qhd', prob_low, value_heads, precision=lax.Precision.HIGHEST)
    return mixed.reshape(SLOTS, D)

def forward(tokens, first_gain, first_shift, w_qkv, w_out, second_gain, second_shift, w_up, w_down, allowed, select):
    act1 = low(layer_norm(tokens, first_gain, first_shift)).reshape(ROWS * SLOTS, D)
    projected = matmul(act1, w_qkv).reshape(ROWS, SLOTS, 3 * D)
    queries = low_back(low(0.125 * projected[:, :, :D]))
    key_rows = low_back(low(projected[:, :, D:2 * D]))
    value_rows = low_back(low(projected[:, :, 2 * D:]))
    mixed = lax.map(jax.checkpoint(attend_row), (queries, key_rows, value_rows, allowed))
    attended = low_back(low(mixed)).reshape(ROWS * SLOTS, D)
    branch_out = low_back(matmul(attended, w_out))
    hidden1 = tokens.reshape(ROWS * SLOTS, D) + branch_out
    act2 = low(layer_norm(hidden1, second_gain, second_shift))
    output = hidden1
    for expert in range(EXPERTS):
        pre_act = low_back(matmul(act2, w_up[expert]))
        inner_act = low(jax.nn.gelu(pre_act, approximate=False))
        output = output + select[:, expert:expert + 1] * matmul(inner_act, w_down[expert])
    return output.reshape(ROWS, SLOTS, D)

def reference(tokens, first_gain, first_shift, w_qkv, w_out, second_gain, second_shift, w_up, w_down, modality, segments, partner, cotangent):
    match = segments[:, :, None] == jnp.arange(2 * NIMG, dtype=jnp.int32)[None, None, :]
    pair_ids = lax.optimization_barrier(jnp.sum(jnp.where(match, partner[:, None, :], 0), axis=2)).astype(jnp.int32)
    allowed = pair_ids[:, :, None] == pair_ids[:, None, :]
    expert_hit = modality.reshape(ROWS * SLOTS)[:, None] == jnp.arange(EXPERTS, dtype=jnp.int32)[None, :]
    select = expert_hit.astype(jnp.float32)
    row_counts = lax.optimization_barrier(jnp.sum(expert_hit.astype(jnp.float32), axis=0)) / ROWS
    params = (tokens.astype(jnp.float32), first_gain.astype(jnp.float32), first_shift.astype(jnp.float32), w_qkv.astype(jnp.float32), w_out.astype(jnp.float32), second_gain.astype(jnp.float32), second_shift.astype(jnp.float32), w_up.astype(jnp.float32), w_down.astype(jnp.float32))

    def layer_fn(*inputs):
        return forward(*inputs, allowed, select)
    result, pullback = jax.vjp(layer_fn, *params)
    grads = pullback(cotangent.astype(jnp.float32))
    factor = SLOTS / (EXPERTS * row_counts)
    up_grad = grads[7] * factor[:, None, None]
    down_grad = grads[8] * factor[:, None, None]
    return (result.astype(jnp.bfloat16), grads[0], grads[1], grads[2], grads[3], grads[4], grads[5], grads[6], up_grad, down_grad)
```

```python
import jax
import jax.numpy as jnp
from jax import lax
from jax.experimental import pallas as pl
from jax.experimental.pallas import tpu as pltpu
from jax.sharding import PartitionSpec as P

HD = 64
OWN = 6
IMG = 197
NIMG = 4
BOTH = ("rows", "seq")
F32 = jnp.float32
BF16 = jnp.bfloat16
MASKED = -1e30


def route(step):
    pairs = []
    for r in range(32):
        z, x_lo, y = r // 8, (r // 4) % 2, r % 4
        for s in range(4):
            x, c = (s // 2) * 2 + x_lo, s % 2
            tx, ty, tz, tc = step(x, y, z, c)
            target = (tz * 8 + (tx % 2) * 4 + ty) * 4 + (tx // 2) * 2 + tc
            pairs.append((r * 4 + s, target))
    return pairs


def send(values, step):
    return lax.ppermute(values, BOTH, route(step))


def swap_core(values):
    return send(values, lambda x, y, z, c: (x, y, z, 1 - c))


def swap_far(values):
    return send(values, lambda x, y, z, c: (x ^ 2, y, z, c))


def axis_step(axis, first):
    def step(x, y, z, c):
        flip = 1 if (c == 0) == first else 3
        at = {"x": x, "y": y, "z": z}
        at[axis] ^= flip
        return (at["x"], at["y"], at["z"], c)

    return step


def add_low(kept, arrived):
    return (kept.astype(F32) + arrived.astype(F32)).astype(BF16)


def scatter_axis(blocks, axis, place, core):
    order = jnp.where(core == 0, jnp.array([0, 3, 1, 2]), jnp.array([0, 1, 3, 2])) ^ place
    pick = [lax.dynamic_index_in_dim(blocks, order[k], 0, keepdims=False) for k in range(4)]
    arrived = send(jnp.stack([pick[2], pick[3]]), axis_step(axis, True))
    kept = add_low(pick[0], arrived[0])
    passed = add_low(pick[1], arrived[1])
    return add_low(kept, send(passed, axis_step(axis, False)))


ORDERS = (("x", "y", "z"), ("y", "z", "x"), ("z", "x", "y"))


def scatter_chips(groups, places, core):
    dims = {"z": 0, "y": 1, "x": 2}
    current = []
    for g, blocks in enumerate(groups):
        order = ORDERS[g]
        rest = tuple(range(3, blocks.ndim))
        current.append(blocks.transpose(tuple(dims[a] for a in order) + rest))
    for stage in range(3):
        current = [
            scatter_axis(blocks, ORDERS[g][stage], places[ORDERS[g][stage]], core)
            for g, blocks in enumerate(current)
        ]
    return current


def rows_to_cells(part, groups):
    cells = part.reshape(4, 2, 4, 24, groups, 2, 256).transpose(4, 0, 2, 5, 1, 3, 6)
    return cells.reshape(groups, 4, 4, 4, 24, 256)


def spread_rows(held, core, far):
    held = held.reshape((2, 2, 6) + held.shape[1:])
    def rows_for(flip_far, flip_core):
        part = lax.dynamic_index_in_dim(held, far ^ flip_far, 0, keepdims=False)
        return lax.dynamic_index_in_dim(part, core ^ flip_core, 0, keepdims=False)
    own = rows_for(0, 0)
    near = swap_core(rows_for(0, 1))
    away = swap_far(rows_for(1, 0))
    cross = send(rows_for(1, 1), lambda x, y, z, c: (x ^ 2, y, z, 1 - c))
    even, odd = jnp.where(core == 0, own, near), jnp.where(core == 0, near, own)
    even_away, odd_away = jnp.where(core == 0, away, cross), jnp.where(core == 0, cross, away)
    first = [jnp.where(far == 0, even, even_away), jnp.where(far == 0, odd, odd_away)]
    second = [jnp.where(far == 0, even_away, even), jnp.where(far == 0, odd_away, odd)]
    return jnp.stack([jnp.stack(first), jnp.stack(second)])


def normalize(inputs):
    centred = inputs - jnp.mean(inputs, axis=-1, keepdims=True)
    factor = lax.rsqrt(jnp.mean(centred * centred, axis=-1, keepdims=True) + 1e-05)
    return centred * factor, factor


def normalize_back(grad, xhat, factor, gain):
    gy = grad * gain
    mean_gy = jnp.mean(gy, axis=-1, keepdims=True)
    mean_gx = jnp.mean(gy * xhat, axis=-1, keepdims=True)
    return factor * (gy - mean_gy - xhat * mean_gx)


def gelu_parts(pre):
    phi = 0.5 * (1.0 + lax.erf(pre * 0.7071067811865476))
    slope = phi + pre * (0.3989422804014327 * jnp.exp(-0.5 * pre * pre))
    return pre * phi, slope


NT = (((1,), (1,)), ((), ()))
TN = (((0,), (0,)), ((), ()))
NN = (((1,), (0,)), ((), ()))


def mm(left, right, dims=NN):
    return lax.dot_general(left, right, dims, preferred_element_type=F32)


def head_lanes(shape, h):
    lane = lax.broadcasted_iota(jnp.int32, shape, len(shape) - 1)
    return (lane >= HD) == (h == 1)


def forward_kernel(q_ref, k_ref, v_ref, qx_ref, kx_ref, out_ref, lse_ref):
    keys = jnp.concatenate([k_ref[...], kx_ref[...]], axis=1)
    values = v_ref[...]
    q_pair = q_ref[...]
    lanes = head_lanes(q_pair.shape, 0)
    mixed = []
    for h in range(2):
        mine = lanes if h == 0 else jnp.logical_not(lanes)
        query = jnp.concatenate([jnp.where(mine, q_pair, 0), qx_ref[...]], axis=1)
        scores = mm(keys, query, NT)
        peak = jnp.max(scores, axis=0, keepdims=True)
        weights = jnp.exp(scores - peak)
        total = jnp.sum(weights, axis=0, keepdims=True)
        inverse = 1.0 / total
        low = (weights * inverse).astype(BF16)
        mixed.append(mm(low, values, TN))
        lse_ref[0, h : h + 1, :] = peak + jnp.log(total)
    out_ref[...] = jnp.where(lanes, mixed[0], mixed[1]).astype(BF16)


def attend_forward(q, k, v, qx, kx):
    queries, keys = q.shape[0], k.shape[0]
    pairs = OWN // 2
    return pl.pallas_call(
        forward_kernel,
        grid=(pairs,),
        in_specs=[
            pl.BlockSpec((queries, 128), lambda p: (0, p)),
            pl.BlockSpec((keys, 128), lambda p: (0, p)),
            pl.BlockSpec((keys, 128), lambda p: (0, p)),
            pl.BlockSpec((queries, 128), lambda p: (0, 0)),
            pl.BlockSpec((keys, 128), lambda p: (0, 0)),
        ],
        out_specs=[
            pl.BlockSpec((queries, 128), lambda p: (0, p)),
            pl.BlockSpec((1, 2, queries), lambda p: (p, 0, 0)),
        ],
        out_shape=[
            jax.ShapeDtypeStruct((queries, pairs * 128), BF16),
            jax.ShapeDtypeStruct((pairs, 2, queries), F32),
        ],
        compiler_params=pltpu.CompilerParams(vmem_limit_bytes=50 * 2**20),
        cost_estimate=pl.CostEstimate(
            flops=2 * 2 * OWN * queries * keys * 256, bytes_accessed=4 * 2**20,
            transcendentals=OWN * queries * keys),
        name="attend_forward",
    )(q, k, v, qx, kx)


def backward_kernel(q_ref, k_ref, v_ref, do_ref, o_ref, qx_ref, kx_ref, lse_ref, dq_ref, dk_ref, dv_ref):
    keys = jnp.concatenate([k_ref[...], kx_ref[...]], axis=1)
    k_pair, values, q_pair, grads = k_ref[...], v_ref[...], q_ref[...], do_ref[...]
    lanes = head_lanes(q_pair.shape, 0)
    product = grads.astype(F32) * o_ref[...].astype(F32)
    dq = jnp.zeros(q_pair.shape, F32)
    dk = jnp.zeros(k_pair.shape, F32)
    dv = jnp.zeros(k_pair.shape, F32)
    for h in range(2):
        mine = lanes if h == 0 else jnp.logical_not(lanes)
        q_head = jnp.where(mine, q_pair, 0)
        g_head = jnp.where(mine, grads, 0)
        dot_row = jnp.transpose(jnp.sum(jnp.where(mine, product, 0.0), axis=1, keepdims=True))
        scores = mm(keys, jnp.concatenate([q_head, qx_ref[...]], axis=1), NT)
        prob = jnp.exp(scores - lse_ref[0, h : h + 1, :])
        dv += mm(prob.astype(BF16), g_head)
        grad_prob = mm(values, g_head, NT)
        grad_scores = (prob * (grad_prob - dot_row)).astype(BF16)
        dk += mm(grad_scores, q_head)
        part = mm(grad_scores, k_pair, TN)
        dq += jnp.where(mine, part, 0.0)
    dq_ref[...] = dq.astype(BF16) * jnp.asarray(0.125, BF16)
    dk_ref[...] = dk.astype(BF16)
    dv_ref[...] = dv.astype(BF16)


def attend_backward(q, k, v, do, o, qx, kx, lse):
    queries, keys = q.shape[0], k.shape[0]
    pairs = OWN // 2
    by_query = pl.BlockSpec((queries, 128), lambda p: (0, p))
    by_key = pl.BlockSpec((keys, 128), lambda p: (0, p))
    return pl.pallas_call(
        backward_kernel,
        grid=(pairs,),
        in_specs=[
            by_query, by_key, by_key, by_query, by_query,
            pl.BlockSpec((queries, 128), lambda p: (0, 0)),
            pl.BlockSpec((keys, 128), lambda p: (0, 0)),
            pl.BlockSpec((1, 2, queries), lambda p: (p, 0, 0)),
        ],
        out_specs=[by_query, by_key, by_key],
        out_shape=[
            jax.ShapeDtypeStruct((queries, pairs * 128), BF16),
            jax.ShapeDtypeStruct((keys, pairs * 128), BF16),
            jax.ShapeDtypeStruct((keys, pairs * 128), BF16),
        ],
        compiler_params=pltpu.CompilerParams(vmem_limit_bytes=50 * 2**20),
        cost_estimate=pl.CostEstimate(
            flops=2 * 5 * OWN * queries * keys * 256, bytes_accessed=6 * 2**20,
            transcendentals=OWN * queries * keys),
        name="attend_backward",
    )(q, k, v, do, o, qx, kx, lse)


def shards(tokens, first_gain, first_shift, w_qkv, w_out, second_gain, second_shift,
           w_up, w_down, modality, segments, partner, cotangent):
    own_n = tokens.shape[1]
    chip_n = 2 * own_n
    width = tokens.shape[2]
    row_index, seq_index = lax.axis_index("rows"), lax.axis_index("seq")
    core, far = seq_index % 2, seq_index // 2
    places = {"z": row_index // 8, "y": row_index % 4, "x": far * 2 + (row_index // 4) % 2}

    doc_match = segments[0][:, None] == jnp.arange(partner.shape[1], dtype=jnp.int32)[None, :]
    tag = jnp.sum(jnp.where(doc_match, partner[0][None, :], 0), axis=1)
    marks = jnp.concatenate([tag, modality[0], jnp.zeros((width - 2 * own_n,), jnp.int32)])
    marks = jnp.concatenate([marks[None], jnp.zeros((15, width), jnp.int32)]).astype(BF16)
    own_ext = jnp.concatenate([tokens[0], marks])
    far_ext = swap_far(own_ext)
    sib_ext = swap_core(own_ext)
    far_sib_ext = swap_core(far_ext)
    cot_own = cotangent[0]
    cot = jnp.concatenate([cot_own, swap_core(cot_own)])

    def unpack(*parts):
        body = jnp.concatenate([p[:own_n] for p in parts])
        tags = jnp.concatenate([p[own_n, :own_n] for p in parts]).astype(jnp.int32)
        kinds = jnp.concatenate([p[own_n, own_n : 2 * own_n] for p in parts]).astype(jnp.int32)
        return body.astype(F32), tags, kinds

    near_tokens, near_tags, near_kinds = unpack(own_ext, sib_ext)
    away_tokens, away_tags, _ = unpack(far_ext, far_sib_ext)

    own_w = OWN * HD
    def own_columns(weight, at):
        return lax.dynamic_slice_in_dim(weight, at + core * own_w, own_w, axis=1)
    w_q, w_k, w_v = (own_columns(w_qkv, n * width) for n in range(3))
    w_kv = jnp.concatenate([w_k, w_v], axis=1)
    w_all = jnp.concatenate([w_q, w_kv], axis=1)

    xhat_near, factor_near = normalize(near_tokens)
    act1 = (xhat_near * first_gain + first_shift).astype(BF16)
    xhat_away, _ = normalize(away_tokens)
    act1_away = (xhat_away * first_gain + first_shift).astype(BF16)
    proj = mm(act1, w_all)
    queries = (0.125 * proj[:, :own_w]).astype(BF16)
    kv_away = mm(act1_away, w_kv).astype(BF16)
    kv = jnp.concatenate([proj[:, own_w:].astype(BF16), kv_away])
    keys, values = kv[:, :own_w], kv[:, own_w:]

    lane = jnp.arange(128, dtype=jnp.int32)[None, :]
    tags = jnp.concatenate([near_tags, away_tags])
    kx = (lane == tags[:, None]).astype(BF16)
    qx = jnp.where((lane < NIMG) & (lane != near_tags[:, None]), MASKED, 0.0).astype(BF16)

    attended_own, lse = attend_forward(queries, keys, values, qx, kx)
    attended_sib = swap_core(attended_own)
    flipped = jnp.concatenate([attended_sib[own_n:], attended_sib[:own_n]])
    attended = jnp.concatenate([
        jnp.where(core == 0, attended_own, flipped),
        jnp.where(core == 0, flipped, attended_own)], axis=1)

    hidden1 = near_tokens + mm(attended, w_out)
    xhat2, factor2 = normalize(hidden1)
    act2 = (xhat2 * second_gain + second_shift).astype(BF16)

    half_ff = w_up.shape[2] // 2
    wu = lax.dynamic_slice_in_dim(w_up, core * half_ff, half_ff, axis=2)
    wd = lax.dynamic_slice_in_dim(w_down, core * half_ff, half_ff, axis=1)
    text = (near_kinds == 1)[:, None]
    pre = jnp.where(text, mm(act2, wu[1]), mm(act2, wu[0]))
    inner, slope = gelu_parts(pre)
    inner = inner.astype(BF16)
    grad_inner = jnp.where(text, mm(cot, wd[1], NT), mm(cot, wd[0], NT))
    grad_pre = (grad_inner * slope).astype(BF16)
    zero = jnp.zeros((), BF16)
    inners = [jnp.where(text, zero, inner), jnp.where(text, inner, zero)]
    grad_pres = [jnp.where(text, zero, grad_pre), jnp.where(text, grad_pre, zero)]
    branch = sum(mm(inners[e], wd[e]) for e in range(2))
    grad_act2 = sum(mm(grad_pres[e], wu[e], NT) for e in range(2))
    up = jnp.stack([mm(act2, grad_pres[e], TN).astype(BF16) for e in range(2)])
    down = jnp.stack([mm(inners[e], cot, TN).astype(BF16) for e in range(2)])

    up_cells = jnp.stack([rows_to_cells(up[e], 3) for e in range(2)], axis=4)
    up_cells = up_cells.reshape(3, 4, 4, 4, 48, 256)
    down_cells = down.reshape(2, 2, 2, 4, 2, 2, 24, 3, 256).transpose(7, 5, 1, 3, 4, 2, 0, 6, 8)
    down_cells = down_cells.reshape(3, 4, 4, 4, 48, 256)
    ff_cells = jnp.concatenate([up_cells, down_cells], axis=4)
    ff_done = scatter_chips([ff_cells[g] for g in range(3)], places, core)

    branch_send = swap_core(branch[own_n:].astype(BF16))
    layer_output = (hidden1[:own_n] + branch[:own_n] + branch_send.astype(F32)).astype(BF16)

    grad_sib = swap_core(grad_act2.astype(BF16)).astype(F32)
    grad_act2 = grad_act2 + jnp.concatenate([grad_sib[own_n:], grad_sib[:own_n]])
    grad_hidden1 = cot.astype(F32) + normalize_back(grad_act2, xhat2, factor2, second_gain)
    second_gain_part = jnp.sum((grad_act2 * xhat2)[:own_n], axis=0)
    second_shift_part = jnp.sum(grad_act2[:own_n], axis=0)
    grad_proj = grad_hidden1.astype(BF16)
    w_out_rows = lax.dynamic_slice_in_dim(w_out, core * own_w, own_w, axis=0)
    grad_att = mm(grad_proj, w_out_rows, NT).astype(BF16)
    out_half = mm(attended, lax.dynamic_slice_in_dim(grad_proj, core * own_w, own_w, axis=1), TN)

    grad_q, grad_k, grad_v = attend_backward(
        queries, keys, values, grad_att, attended_own, qx, kx, lse)
    grad_kv = jnp.concatenate([grad_k, grad_v], axis=1)
    grad_near = jnp.concatenate([grad_q, grad_kv[:chip_n]], axis=1)
    grad_away = grad_kv[chip_n:]
    dw_q = mm(act1, grad_q, TN)
    dw_kv = mm(jnp.concatenate([act1, act1_away]), grad_kv, TN)
    tail = jnp.concatenate([dw_q, dw_kv, out_half], axis=1).astype(BF16)
    tail_cells = rows_to_cells(tail, 3)

    act_near = mm(grad_near, w_all, NT)
    act_away = mm(grad_away, w_kv, NT)
    first_gain_part = jnp.sum(act_near * xhat_near, axis=0) + jnp.sum(act_away * xhat_away, axis=0)
    first_shift_part = jnp.sum(act_near, axis=0) + jnp.sum(act_away, axis=0)
    vectors = jnp.stack([first_gain_part, first_shift_part, second_gain_part, second_shift_part])
    vectors = vectors.reshape(4, 4, 2, 4, 2, 12).transpose(1, 3, 4, 2, 0, 5).reshape(4, 4, 4, 1, 48)
    vectors = jnp.pad(vectors, ((0, 0),) * 3 + ((0, 7), (0, 256 - 48))).astype(BF16)
    tail_groups = [jnp.concatenate([tail_cells[0], vectors], axis=3), tail_cells[1], tail_cells[2]]
    tail_done = scatter_chips(tail_groups, places, core)

    def add_sibling(partial):
        return partial[:own_n] + swap_core(partial[own_n:].astype(BF16)).astype(F32)
    from_far = swap_far(add_sibling(act_away).astype(BF16)).astype(F32)
    grad_act1 = add_sibling(act_near) + from_far
    token_grad = grad_hidden1[:own_n] + normalize_back(
        grad_act1, xhat_near[:own_n], factor_near[:own_n], first_gain)

    vec = tail_done[0][24, :48].reshape(4, 2, 6).astype(F32)
    vec_own = lax.dynamic_index_in_dim(vec, core, 1, keepdims=False)
    vec_sib = lax.dynamic_index_in_dim(vec, 1 - core, 1, keepdims=False)
    vec_sum = vec_own + swap_core(jnp.pad(vec_sib, ((0, 4), (0, 122))))[:4, :6]

    held = [jnp.concatenate([ff_done[g][:24], ff_done[g][24:48], tail_done[g][:24]], axis=1)
            for g in range(3)]
    held = jnp.stack(held, axis=1)
    rows = spread_rows(held, core, far)
    rows = rows.reshape(2, 2, 6, 3, 3, 256).transpose(4, 2, 1, 3, 0, 5).reshape(3, 6, 2, 1536).astype(F32)
    up_rows = rows[:2].reshape(2, 6, 2 * 1536)
    qkv_grad = rows[2][:, :, : 3 * own_w].reshape(6, 2, 3, own_w).transpose(0, 2, 1, 3).reshape(6, 3 * width)
    out_grad = rows[2][:, :, 3 * own_w :].reshape(6, width)

    down_held = jnp.concatenate([ff_done[g][48:] for g in range(3)], axis=1)
    down_rows = send(down_held, lambda x, y, z, c: (x, y, 2 * c + z % 2, z // 2)).astype(F32)
    down_rows = down_rows.reshape(2, 24, width)

    slots = 4 * own_n
    factors = jnp.asarray([slots / (2 * NIMG * IMG), slots / (2 * (slots - NIMG * IMG))], F32)[:, None, None]
    return (
        layer_output[None], token_grad[None], vec_sum[0], vec_sum[1], qkv_grad, out_grad,
        vec_sum[2], vec_sum[3], up_rows * factors, down_rows * factors)


def solution(mesh):
    cut = P("rows", "seq", None)
    flat = P(BOTH)
    placed = (cut,) + (P(),) * 8 + (P("rows", "seq"), P("rows", "seq"), P("rows", None), cut)
    return jax.shard_map(
        shards, mesh=mesh, in_specs=placed,
        out_specs=(cut, cut, flat, flat, P(BOTH, None), P(BOTH, None), flat, flat,
                   P(None, BOTH, None), P(None, BOTH, None)),
        check_vma=False)
```

```python
import jax
import jax.numpy as jnp
from jax import lax
from jax.experimental import pallas as pl
from jax.experimental.pallas import tpu as pltpu
from jax.sharding import PartitionSpec as P

HD = 64
OWN = 6
IMG = 197
NIMG = 4
BOTH = ("rows", "seq")
F32 = jnp.float32
BF16 = jnp.bfloat16
MASKED = -1e30


def route(step):
    pairs = []
    for r in range(32):
        z, x_lo, y = r // 8, (r // 4) % 2, r % 4
        for s in range(4):
            x, c = (s // 2) * 2 + x_lo, s % 2
            tx, ty, tz, tc = step(x, y, z, c)
            target = (tz * 8 + (tx % 2) * 4 + ty) * 4 + (tx // 2) * 2 + tc
            pairs.append((r * 4 + s, target))
    return pairs


def send(values, step):
    return lax.ppermute(values, BOTH, route(step))


def swap_core(values):
    return send(values, lambda x, y, z, c: (x, y, z, 1 - c))


def swap_far(values):
    return send(values, lambda x, y, z, c: (x ^ 2, y, z, c))


def axis_step(axis, first):
    def step(x, y, z, c):
        flip = 1 if (c == 0) == first else 3
        at = {"x": x, "y": y, "z": z}
        at[axis] ^= flip
        return (at["x"], at["y"], at["z"], c)

    return step


def add_low(kept, arrived):
    return (kept.astype(F32) + arrived.astype(F32)).astype(BF16)


ORDERS = (("x", "y", "z"), ("y", "z", "x"), ("z", "x", "y"))


def spread_rows(held, core, far):
    held = held.reshape((2, 2, 6) + held.shape[1:])
    def rows_for(flip_far, flip_core):
        part = lax.dynamic_index_in_dim(held, far ^ flip_far, 0, keepdims=False)
        return lax.dynamic_index_in_dim(part, core ^ flip_core, 0, keepdims=False)
    own = rows_for(0, 0)
    near = swap_core(rows_for(0, 1))
    away = swap_far(rows_for(1, 0))
    cross = send(rows_for(1, 1), lambda x, y, z, c: (x ^ 2, y, z, 1 - c))
    even, odd = jnp.where(core == 0, own, near), jnp.where(core == 0, near, own)
    even_away, odd_away = jnp.where(core == 0, away, cross), jnp.where(core == 0, cross, away)
    first = [jnp.where(far == 0, even, even_away), jnp.where(far == 0, odd, odd_away)]
    second = [jnp.where(far == 0, even_away, even), jnp.where(far == 0, odd_away, odd)]
    return jnp.stack([jnp.stack(first), jnp.stack(second)])


def normalize(inputs):
    centred = inputs - jnp.mean(inputs, axis=-1, keepdims=True)
    factor = lax.rsqrt(jnp.mean(centred * centred, axis=-1, keepdims=True) + 1e-05)
    return centred * factor, factor


def normalize_back(grad, xhat, factor, gain):
    gy = grad * gain
    mean_gy = jnp.mean(gy, axis=-1, keepdims=True)
    mean_gx = jnp.mean(gy * xhat, axis=-1, keepdims=True)
    return factor * (gy - mean_gy - xhat * mean_gx)


def gelu_parts(pre):
    phi = 0.5 * (1.0 + lax.erf(pre * 0.7071067811865476))
    slope = phi + pre * (0.3989422804014327 * jnp.exp(-0.5 * pre * pre))
    return pre * phi, slope


NT = (((1,), (1,)), ((), ()))
TN = (((0,), (0,)), ((), ()))
NN = (((1,), (0,)), ((), ()))


def mm(left, right, dims=NN):
    return lax.dot_general(left, right, dims, preferred_element_type=F32)


def head_lanes(shape, h):
    lane = lax.broadcasted_iota(jnp.int32, shape, len(shape) - 1)
    return (lane >= HD) == (h == 1)


def forward_kernel(q_ref, k_ref, v_ref, qx_ref, kx_ref, out_ref, lse_ref):
    keys = jnp.concatenate([k_ref[...], kx_ref[...]], axis=1)
    values = v_ref[...]
    q_pair = q_ref[...]
    lanes = head_lanes(q_pair.shape, 0)
    mixed = []
    for h in range(2):
        mine = lanes if h == 0 else jnp.logical_not(lanes)
        query = jnp.concatenate([jnp.where(mine, q_pair, 0), qx_ref[...]], axis=1)
        scores = mm(keys, query, NT)
        peak = jnp.max(scores, axis=0, keepdims=True)
        weights = jnp.exp(scores - peak)
        total = jnp.sum(weights, axis=0, keepdims=True)
        inverse = 1.0 / total
        low = (weights * inverse).astype(BF16)
        mixed.append(mm(low, values, TN))
        lse_ref[0, h : h + 1, :] = peak + jnp.log(total)
    out_ref[...] = jnp.where(lanes, mixed[0], mixed[1]).astype(BF16)


def attend_forward(q, k, v, qx, kx):
    queries, keys = q.shape[0], k.shape[0]
    pairs = OWN // 2
    return pl.pallas_call(
        forward_kernel,
        grid=(pairs,),
        in_specs=[
            pl.BlockSpec((queries, 128), lambda p: (0, p)),
            pl.BlockSpec((keys, 128), lambda p: (0, p)),
            pl.BlockSpec((keys, 128), lambda p: (0, p)),
            pl.BlockSpec((queries, 128), lambda p: (0, 0)),
            pl.BlockSpec((keys, 128), lambda p: (0, 0)),
        ],
        out_specs=[
            pl.BlockSpec((queries, 128), lambda p: (0, p)),
            pl.BlockSpec((1, 2, queries), lambda p: (p, 0, 0)),
        ],
        out_shape=[
            jax.ShapeDtypeStruct((queries, pairs * 128), BF16),
            jax.ShapeDtypeStruct((pairs, 2, queries), F32),
        ],
        compiler_params=pltpu.CompilerParams(vmem_limit_bytes=50 * 2**20),
        cost_estimate=pl.CostEstimate(
            flops=2 * 2 * OWN * queries * keys * 256, bytes_accessed=4 * 2**20,
            transcendentals=OWN * queries * keys),
        name="attend_forward",
    )(q, k, v, qx, kx)


def backward_kernel(q_ref, k_ref, v_ref, do_ref, o_ref, qx_ref, kx_ref, lse_ref, dq_ref, dk_ref, dv_ref):
    keys = jnp.concatenate([k_ref[...], kx_ref[...]], axis=1)
    k_pair, values, q_pair, grads = k_ref[...], v_ref[...], q_ref[...], do_ref[...]
    lanes = head_lanes(q_pair.shape, 0)
    product = grads.astype(F32) * o_ref[...].astype(F32)
    dq = jnp.zeros(q_pair.shape, F32)
    dk = jnp.zeros(k_pair.shape, F32)
    dv = jnp.zeros(k_pair.shape, F32)
    for h in range(2):
        mine = lanes if h == 0 else jnp.logical_not(lanes)
        q_head = jnp.where(mine, q_pair, 0)
        g_head = jnp.where(mine, grads, 0)
        dot_row = jnp.transpose(jnp.sum(jnp.where(mine, product, 0.0), axis=1, keepdims=True))
        scores = mm(keys, jnp.concatenate([q_head, qx_ref[...]], axis=1), NT)
        prob = jnp.exp(scores - lse_ref[0, h : h + 1, :])
        dv += mm(prob.astype(BF16), g_head)
        grad_prob = mm(values, g_head, NT)
        grad_scores = (prob * (grad_prob - dot_row)).astype(BF16)
        dk += mm(grad_scores, q_head)
        part = mm(grad_scores, k_pair, TN)
        dq += jnp.where(mine, part, 0.0)
    dq_ref[...] = dq.astype(BF16) * jnp.asarray(0.125, BF16)
    dk_ref[...] = dk.astype(BF16)
    dv_ref[...] = dv.astype(BF16)


def attend_backward(q, k, v, do, o, qx, kx, lse):
    queries, keys = q.shape[0], k.shape[0]
    pairs = OWN // 2
    by_query = pl.BlockSpec((queries, 128), lambda p: (0, p))
    by_key = pl.BlockSpec((keys, 128), lambda p: (0, p))
    return pl.pallas_call(
        backward_kernel,
        grid=(pairs,),
        in_specs=[
            by_query, by_key, by_key, by_query, by_query,
            pl.BlockSpec((queries, 128), lambda p: (0, 0)),
            pl.BlockSpec((keys, 128), lambda p: (0, 0)),
            pl.BlockSpec((1, 2, queries), lambda p: (p, 0, 0)),
        ],
        out_specs=[by_query, by_key, by_key],
        out_shape=[
            jax.ShapeDtypeStruct((queries, pairs * 128), BF16),
            jax.ShapeDtypeStruct((keys, pairs * 128), BF16),
            jax.ShapeDtypeStruct((keys, pairs * 128), BF16),
        ],
        compiler_params=pltpu.CompilerParams(vmem_limit_bytes=50 * 2**20),
        cost_estimate=pl.CostEstimate(
            flops=2 * 5 * OWN * queries * keys * 256, bytes_accessed=6 * 2**20,
            transcendentals=OWN * queries * keys),
        name="attend_backward",
    )(q, k, v, do, o, qx, kx, lse)


FF_STEP = 512


def expert_kernel(at_ref, up_at, half_at, down_at, act_ref, cot_ref, text_ref, wu_ref, wd_ref,
                  branch_ref, grad_ref, *refs):
    keeps, sends, (up_acc, down_acc) = refs[:3], refs[3:6], refs[6:]
    f = pl.program_id(0)
    act, cot = act_ref[...], cot_ref[...]
    text = text_ref[...] > 0.0
    pre = jnp.where(text, mm(act, wu_ref[1]), mm(act, wu_ref[0]))
    inner, slope = gelu_parts(pre)
    grad_pre = jnp.where(text, mm(cot, wd_ref[1], NT), mm(cot, wd_ref[0], NT)) * slope
    branch = jnp.zeros(branch_ref.shape, F32)
    grad = jnp.zeros(branch_ref.shape, F32)
    for e in range(2):
        mine = text if e == 1 else jnp.logical_not(text)
        inner_e = jnp.where(mine, inner, 0.0).astype(BF16)
        grad_e = jnp.where(mine, grad_pre, 0.0).astype(BF16)
        branch += mm(inner_e, wd_ref[e])
        grad += mm(grad_e, wu_ref[e], NT)
        up = mm(act, grad_e, TN)
        up_acc[e, 0] = up[:, :256]
        up_acc[e, 1] = up[:, 256:]
        down_acc[e, pl.ds(pl.multiple_of(f * FF_STEP, FF_STEP), FF_STEP), :] = mm(inner_e, cot, TN)

    @pl.when(f == 0)
    def _():
        branch_ref[...] = branch
        grad_ref[...] = grad

    @pl.when(f > 0)
    def _():
        branch_ref[...] += branch
        grad_ref[...] += grad

    def spill(target, g, base, up_part):
        def cell(i, carry):
            slot = g * 64 + base + i
            if up_part:
                rows = pl.ds(pl.multiple_of(up_at[slot], 8), 24)
                half = half_at[slot]
                both = jnp.concatenate([up_acc[0, half, rows, :], up_acc[1, half, rows, :]], axis=0)
                target[i, :48, :] = both.astype(BF16)
            else:
                rows = pl.ds(pl.multiple_of(down_at[slot], 8), 24)
                lanes = slice(g * 256, (g + 1) * 256)
                both = jnp.concatenate([down_acc[0, rows, lanes], down_acc[1, rows, lanes]], axis=0)
                target[i, 48:, :] = both.astype(BF16)
            return carry
        lax.fori_loop(0, 32, cell, 0, unroll=4)

    for g in range(3):
        @pl.when(f == g)
        def _():
            spill(keeps[g], g, 0, True)
            spill(sends[g], g, 32, True)

    @pl.when(f == 2)
    def _():
        for g in range(3):
            spill(keeps[g], g, 0, False)
            spill(sends[g], g, 32, False)


def experts(core, tables, act, cot, text, w_up, w_down):
    slots, width = act.shape
    steps = w_up.shape[2] // 2 // FF_STEP
    whole = pl.BlockSpec((slots, width), lambda f, *_: (0, 0))
    cells = pl.BlockSpec((32, 96, 256), lambda f, *_: (0, 0, 0))
    return pl.pallas_call(
        expert_kernel,
        grid_spec=pltpu.PrefetchScalarGridSpec(
            num_scalar_prefetch=4,
            grid=(steps,),
            in_specs=[
                whole, whole,
                pl.BlockSpec((slots, 1), lambda f, *_: (0, 0)),
                pl.BlockSpec((2, width, FF_STEP), lambda f, at, *_: (0, 0, at[0] * steps + f)),
                pl.BlockSpec((2, FF_STEP, width), lambda f, at, *_: (0, at[0] * steps + f, 0)),
            ],
            out_specs=[whole, whole] + [cells] * 6,
            scratch_shapes=[
                pltpu.VMEM((2, 2, width, 256), F32),
                pltpu.VMEM((2, steps * FF_STEP, width), F32),
            ],
        ),
        out_shape=[jax.ShapeDtypeStruct((slots, width), F32)] * 2
        + [jax.ShapeDtypeStruct((32, 96, 256), BF16)] * 6,
        compiler_params=pltpu.CompilerParams(
            vmem_limit_bytes=60 * 2**20, dimension_semantics=("arbitrary",)),
        cost_estimate=pl.CostEstimate(
            flops=12 * 2 * slots * width * steps * FF_STEP, bytes_accessed=24 * 2**20,
            transcendentals=2 * slots * steps * FF_STEP),
        name="experts",
    )(core.reshape(1), *tables, act, cot, text, w_up, w_down)


def cell_tables(places, core):
    flips = jnp.where(core == 0, jnp.array([0, 3, 1, 2]), jnp.array([0, 1, 3, 2]))
    ups, halves, downs = [], [], []
    for order in ORDERS:
        at = {}
        for n, a in enumerate(order):
            shape = [1, 1, 1]
            shape[n] = 4
            at[a] = jnp.broadcast_to((flips ^ places[a]).reshape(shape), (4, 4, 4))
        x_hi, x_lo = at["x"] // 2, at["x"] % 2
        ups.append(24 * (at["z"] * 8 + x_lo * 4 + at["y"]))
        halves.append(x_hi)
        downs.append(24 * ((at["z"] % 2) * 32 + x_lo * 16 + at["y"] * 4 + x_hi * 2 + at["z"] // 2))
    return [jnp.stack(t).reshape(-1).astype(jnp.int32) for t in (ups, halves, downs)]


def halve(kept, sent, axis):
    arrived = send(sent, axis_step(axis, True))
    mine = add_low(kept[0], arrived[0])
    passed = add_low(kept[1], arrived[1])
    return add_low(mine, send(passed, axis_step(axis, False)))


def scatter_cells(keeps, sends):
    done = []
    for g in range(3):
        kept = keeps[g].reshape(2, 4, 4, 96, 256)
        sent = sends[g].reshape(2, 4, 4, 96, 256)
        for axis in ORDERS[g]:
            block = halve(kept, sent, axis)
            kept, sent = block[:2], block[2:]
        done.append(block)
    return done


def shards(tokens, first_gain, first_shift, w_qkv, w_out, second_gain, second_shift,
           w_up, w_down, modality, segments, partner, cotangent):
    own_n = tokens.shape[1]
    chip_n = 2 * own_n
    width = tokens.shape[2]
    row_index, seq_index = lax.axis_index("rows"), lax.axis_index("seq")
    core, far = seq_index % 2, seq_index // 2
    places = {"z": row_index // 8, "y": row_index % 4, "x": far * 2 + (row_index // 4) % 2}

    doc_match = segments[0][:, None] == jnp.arange(partner.shape[1], dtype=jnp.int32)[None, :]
    tag = jnp.sum(jnp.where(doc_match, partner[0][None, :], 0), axis=1)
    marks = jnp.concatenate([tag, modality[0], jnp.zeros((width - 2 * own_n,), jnp.int32)])
    marks = jnp.concatenate([marks[None], jnp.zeros((15, width), jnp.int32)]).astype(BF16)
    own_ext = jnp.concatenate([tokens[0], marks])
    far_ext = swap_far(own_ext)
    sib_ext = swap_core(own_ext)
    far_sib_ext = swap_core(far_ext)
    cot_own = cotangent[0]
    cot = jnp.concatenate([cot_own, swap_core(cot_own)])

    def unpack(*parts):
        body = jnp.concatenate([p[:own_n] for p in parts])
        tags = jnp.concatenate([p[own_n, :own_n] for p in parts]).astype(jnp.int32)
        kinds = jnp.concatenate([p[own_n, own_n : 2 * own_n] for p in parts]).astype(jnp.int32)
        return body.astype(F32), tags, kinds

    near_tokens, near_tags, near_kinds = unpack(own_ext, sib_ext)
    away_tokens, away_tags, _ = unpack(far_ext, far_sib_ext)

    own_w = OWN * HD
    def own_columns(weight, at):
        return lax.dynamic_slice_in_dim(weight, at + core * own_w, own_w, axis=1)
    w_q, w_k, w_v = (own_columns(w_qkv, n * width) for n in range(3))
    w_kv = jnp.concatenate([w_k, w_v], axis=1)
    w_all = jnp.concatenate([w_q, w_kv], axis=1)

    xhat_near, factor_near = normalize(near_tokens)
    act1 = (xhat_near * first_gain + first_shift).astype(BF16)
    xhat_away, _ = normalize(away_tokens)
    act1_away = (xhat_away * first_gain + first_shift).astype(BF16)
    proj = mm(act1, w_all)
    queries = (0.125 * proj[:, :own_w]).astype(BF16)
    kv_away = mm(act1_away, w_kv).astype(BF16)
    kv = jnp.concatenate([proj[:, own_w:].astype(BF16), kv_away])
    keys, values = kv[:, :own_w], kv[:, own_w:]

    lane = jnp.arange(128, dtype=jnp.int32)[None, :]
    tags = jnp.concatenate([near_tags, away_tags])
    kx = (lane == tags[:, None]).astype(BF16)
    qx = jnp.where((lane < NIMG) & (lane != near_tags[:, None]), MASKED, 0.0).astype(BF16)

    attended_own, lse = attend_forward(queries, keys, values, qx, kx)
    attended_sib = swap_core(attended_own)
    flipped = jnp.concatenate([attended_sib[own_n:], attended_sib[:own_n]])
    attended = jnp.concatenate([
        jnp.where(core == 0, attended_own, flipped),
        jnp.where(core == 0, flipped, attended_own)], axis=1)

    hidden1 = near_tokens + mm(attended, w_out)
    xhat2, factor2 = normalize(hidden1)
    act2 = (xhat2 * second_gain + second_shift).astype(BF16)

    text = (near_kinds == 1).astype(F32)[:, None]
    outcome = experts(core, cell_tables(places, core), act2, cot, text, w_up, w_down)
    branch, grad_act2 = outcome[:2]
    ff_done = scatter_cells(outcome[2:5], outcome[5:8])

    branch_send = swap_core(branch[own_n:].astype(BF16))
    layer_output = (hidden1[:own_n] + branch[:own_n] + branch_send.astype(F32)).astype(BF16)

    grad_sib = swap_core(grad_act2.astype(BF16)).astype(F32)
    grad_act2 = grad_act2 + jnp.concatenate([grad_sib[own_n:], grad_sib[:own_n]])
    grad_hidden1 = cot.astype(F32) + normalize_back(grad_act2, xhat2, factor2, second_gain)
    second_gain_part = jnp.sum((grad_act2 * xhat2)[:own_n], axis=0)
    second_shift_part = jnp.sum(grad_act2[:own_n], axis=0)
    grad_proj = grad_hidden1.astype(BF16)
    w_out_rows = lax.dynamic_slice_in_dim(w_out, core * own_w, own_w, axis=0)
    grad_att = mm(grad_proj, w_out_rows, NT).astype(BF16)
    out_half = mm(attended, lax.dynamic_slice_in_dim(grad_proj, core * own_w, own_w, axis=1), TN)

    grad_q, grad_k, grad_v = attend_backward(
        queries, keys, values, grad_att, attended_own, qx, kx, lse)
    grad_kv = jnp.concatenate([grad_k, grad_v], axis=1)
    grad_near = jnp.concatenate([grad_q, grad_kv[:chip_n]], axis=1)
    grad_away = grad_kv[chip_n:]
    act_near = mm(grad_near, w_all, NT)
    act_away = mm(grad_away, w_kv, NT)
    first_gain_part = jnp.sum(act_near * xhat_near, axis=0) + jnp.sum(act_away * xhat_away, axis=0)
    first_shift_part = jnp.sum(act_near, axis=0) + jnp.sum(act_away, axis=0)
    vectors = jnp.stack([first_gain_part, first_shift_part, second_gain_part, second_shift_part])
    vectors = jnp.pad(vectors.T, ((0, 0), (0, 124))).astype(BF16)
    act_all = jnp.concatenate([act1, act1_away])
    same_core = [list(range(c, 128, 2)) for c in range(2)]
    tail = []
    for g in range(3):
        at = slice(g * 128, (g + 1) * 128)
        parts = [mm(act1, grad_q[:, at], TN), mm(act_all, grad_k[:, at], TN),
                 mm(act_all, grad_v[:, at], TN), out_half[:, at]]
        parts = [p.astype(BF16) for p in parts] + ([vectors] if g == 2 else [])
        moved = lax.all_to_all(jnp.concatenate(parts, axis=1).reshape(64, 12, -1), BOTH, 0, 0,
                               tiled=True, axis_index_groups=same_core)
        tail.append(jnp.sum(moved.astype(F32), axis=0))

    def add_sibling(partial):
        return partial[:own_n] + swap_core(partial[own_n:].astype(BF16)).astype(F32)
    from_far = swap_far(add_sibling(act_away).astype(BF16)).astype(F32)
    grad_act1 = add_sibling(act_near) + from_far
    token_grad = grad_hidden1[:own_n] + normalize_back(
        grad_act1, xhat_near[:own_n], factor_near[:own_n], first_gain)

    tail = jnp.concatenate([t[:, :512] for t in tail] + [tail[2][:, 512:]], axis=1)
    tail = tail.reshape(2, 6, 1664)
    tail_own = lax.dynamic_index_in_dim(tail, core, 0, keepdims=False)
    tail_sib = swap_core(lax.dynamic_index_in_dim(tail, 1 - core, 0, keepdims=False).astype(BF16)).astype(F32)
    vec_sum = (tail_own + tail_sib)[:, 1536:1540].T
    both = jnp.where(core == 0, jnp.stack([tail_own, tail_sib]), jnp.stack([tail_sib, tail_own]))
    both = both[:, :, :1536].reshape(2, 6, 3, 4, 128).transpose(3, 1, 0, 2, 4).reshape(4, 6, width)
    qkv_grad = both[:3].transpose(1, 0, 2).reshape(6, 3 * width)
    out_grad = both[3]

    held = jnp.stack([jnp.concatenate([ff_done[g][:24], ff_done[g][24:48]], axis=1)
                      for g in range(3)], axis=1)
    rows = spread_rows(held, core, far)
    rows = rows.reshape(2, 2, 6, 3, 2, 256).transpose(4, 2, 1, 3, 0, 5)
    up_rows = rows.reshape(2, 6, 2 * 1536).astype(F32)

    down_held = jnp.concatenate([ff_done[g][48:] for g in range(3)], axis=1)
    down_rows = send(down_held, lambda x, y, z, c: (x, y, 2 * c + z % 2, z // 2)).astype(F32)
    down_rows = down_rows.reshape(2, 24, width)

    slots = 4 * own_n
    factors = jnp.asarray([slots / (2 * NIMG * IMG), slots / (2 * (slots - NIMG * IMG))], F32)[:, None, None]
    return (
        layer_output[None], token_grad[None], vec_sum[0], vec_sum[1], qkv_grad, out_grad,
        vec_sum[2], vec_sum[3], up_rows * factors, down_rows * factors)


def solution(mesh):
    cut = P("rows", "seq", None)
    flat = P(BOTH)
    placed = (cut,) + (P(),) * 8 + (P("rows", "seq"), P("rows", "seq"), P("rows", None), cut)
    return jax.shard_map(
        shards, mesh=mesh, in_specs=placed,
        out_specs=(cut, cut, flat, flat, P(BOTH, None), P(BOTH, None), flat, flat,
                   P(None, BOTH, None), P(None, BOTH, None)),
        check_vma=False)
```

```python
import jax
import jax.numpy as jnp
import numpy as np
from jax import lax
from jax.experimental import pallas as pl
from jax.experimental.pallas import tpu as pltpu
from jax.sharding import PartitionSpec as P

HD = 64
OWN = 6
IMG = 197
NIMG = 4
BOTH = ("rows", "seq")
F32 = jnp.float32
BF16 = jnp.bfloat16
MASKED = -1e30


def route(step):
    pairs = []
    for r in range(32):
        z, x_lo, y = r // 8, (r // 4) % 2, r % 4
        for s in range(4):
            x, c = (s // 2) * 2 + x_lo, s % 2
            tx, ty, tz, tc = step(x, y, z, c)
            target = (tz * 8 + (tx % 2) * 4 + ty) * 4 + (tx // 2) * 2 + tc
            pairs.append((r * 4 + s, target))
    return pairs


def send(values, step):
    return lax.ppermute(values, BOTH, route(step))


def swap_core(values):
    return send(values, lambda x, y, z, c: (x, y, z, 1 - c))


def swap_far(values):
    return send(values, lambda x, y, z, c: (x ^ 2, y, z, c))


def axis_step(axis, first):
    def step(x, y, z, c):
        flip = 1 if (c == 0) == first else 3
        at = {"x": x, "y": y, "z": z}
        at[axis] ^= flip
        return (at["x"], at["y"], at["z"], c)

    return step


def add_low(kept, arrived):
    return (kept.astype(F32) + arrived.astype(F32)).astype(BF16)


ORDERS = (("x", "y", "z"), ("y", "z", "x"), ("z", "x", "y"))


def spread_rows(held, core, far):
    held = held.reshape((2, 2, 6) + held.shape[1:])
    def rows_for(flip_far, flip_core):
        part = lax.dynamic_index_in_dim(held, far ^ flip_far, 0, keepdims=False)
        return lax.dynamic_index_in_dim(part, core ^ flip_core, 0, keepdims=False)
    own = rows_for(0, 0)
    near = swap_core(rows_for(0, 1))
    away = swap_far(rows_for(1, 0))
    cross = send(rows_for(1, 1), lambda x, y, z, c: (x ^ 2, y, z, 1 - c))
    even, odd = jnp.where(core == 0, own, near), jnp.where(core == 0, near, own)
    even_away, odd_away = jnp.where(core == 0, away, cross), jnp.where(core == 0, cross, away)
    first = [jnp.where(far == 0, even, even_away), jnp.where(far == 0, odd, odd_away)]
    second = [jnp.where(far == 0, even_away, even), jnp.where(far == 0, odd_away, odd)]
    return jnp.stack([jnp.stack(first), jnp.stack(second)])


def normalize(inputs):
    centred = inputs - jnp.mean(inputs, axis=-1, keepdims=True)
    factor = lax.rsqrt(jnp.mean(centred * centred, axis=-1, keepdims=True) + 1e-05)
    return centred * factor, factor


def normalize_back(grad, xhat, factor, gain):
    gy = grad * gain
    mean_gy = jnp.mean(gy, axis=-1, keepdims=True)
    mean_gx = jnp.mean(gy * xhat, axis=-1, keepdims=True)
    return factor * (gy - mean_gy - xhat * mean_gx)


def gelu_parts(pre):
    phi = 0.5 * (1.0 + lax.erf(pre * 0.7071067811865476))
    slope = phi + pre * (0.3989422804014327 * jnp.exp(-0.5 * pre * pre))
    return pre * phi, slope


NT = (((1,), (1,)), ((), ()))
TN = (((0,), (0,)), ((), ()))
NN = (((1,), (0,)), ((), ()))


def mm(left, right, dims=NN):
    return lax.dot_general(left, right, dims, preferred_element_type=F32)


def head_lanes(shape, h):
    lane = lax.broadcasted_iota(jnp.int32, shape, len(shape) - 1)
    return (lane >= HD) == (h == 1)


def forward_kernel(q_ref, k_ref, v_ref, qx_ref, kx_ref, out_ref, lse_ref):
    keys = jnp.concatenate([k_ref[...], kx_ref[...]], axis=1)
    values = v_ref[...]
    q_pair = q_ref[...]
    lanes = head_lanes(q_pair.shape, 0)
    mixed = []
    for h in range(2):
        mine = lanes if h == 0 else jnp.logical_not(lanes)
        query = jnp.concatenate([jnp.where(mine, q_pair, 0), qx_ref[...]], axis=1)
        scores = mm(keys, query, NT)
        peak = jnp.max(scores, axis=0, keepdims=True)
        weights = jnp.exp(scores - peak)
        total = jnp.sum(weights, axis=0, keepdims=True)
        inverse = 1.0 / total
        low = (weights * inverse).astype(BF16)
        mixed.append(mm(low, values, TN))
        lse_ref[0, h : h + 1, :] = peak + jnp.log(total)
    out_ref[...] = jnp.where(lanes, mixed[0], mixed[1]).astype(BF16)


def attend_forward(q, k, v, qx, kx):
    queries, keys = q.shape[0], k.shape[0]
    pairs = OWN // 2
    return pl.pallas_call(
        forward_kernel,
        grid=(pairs,),
        in_specs=[
            pl.BlockSpec((queries, 128), lambda p: (0, p)),
            pl.BlockSpec((keys, 128), lambda p: (0, p)),
            pl.BlockSpec((keys, 128), lambda p: (0, p)),
            pl.BlockSpec((queries, 128), lambda p: (0, 0)),
            pl.BlockSpec((keys, 128), lambda p: (0, 0)),
        ],
        out_specs=[
            pl.BlockSpec((queries, 128), lambda p: (0, p)),
            pl.BlockSpec((1, 2, queries), lambda p: (p, 0, 0)),
        ],
        out_shape=[
            jax.ShapeDtypeStruct((queries, pairs * 128), BF16),
            jax.ShapeDtypeStruct((pairs, 2, queries), F32),
        ],
        compiler_params=pltpu.CompilerParams(vmem_limit_bytes=50 * 2**20),
        cost_estimate=pl.CostEstimate(
            flops=2 * 2 * OWN * queries * keys * 256, bytes_accessed=4 * 2**20,
            transcendentals=OWN * queries * keys),
        name="attend_forward",
    )(q, k, v, qx, kx)


def backward_kernel(q_ref, k_ref, v_ref, do_ref, o_ref, qx_ref, kx_ref, lse_ref, *refs):
    dq_ref, dk_ref, dv_ref = refs[-3:]
    keys = jnp.concatenate([k_ref[...], kx_ref[...]], axis=1)
    k_pair, values, q_pair, grads = k_ref[...], v_ref[...], q_ref[...], do_ref[...]
    lanes = head_lanes(q_pair.shape, 0)
    product = grads.astype(F32) * o_ref[...].astype(F32)
    dq = jnp.zeros(q_pair.shape, F32)
    dk = jnp.zeros(k_pair.shape, F32)
    dv = jnp.zeros(k_pair.shape, F32)
    for h in range(2):
        mine = lanes if h == 0 else jnp.logical_not(lanes)
        q_head = jnp.where(mine, q_pair, 0)
        g_head = jnp.where(mine, grads, 0)
        dot_row = jnp.transpose(jnp.sum(jnp.where(mine, product, 0.0), axis=1, keepdims=True))
        scores = mm(keys, jnp.concatenate([q_head, qx_ref[...]], axis=1), NT)
        prob = jnp.exp(scores - lse_ref[0, h : h + 1, :])
        dv += mm(prob.astype(BF16), g_head)
        grad_prob = mm(values, g_head, NT)
        grad_scores = (prob * (grad_prob - dot_row)).astype(BF16)
        dk += mm(grad_scores, q_head)
        part = mm(grad_scores, k_pair, TN)
        dq += jnp.where(mine, part, 0.0)
    dq_ref[...] = dq.astype(BF16) * jnp.asarray(0.125, BF16)
    dk_ref[...] = dk.astype(BF16)
    dv_ref[...] = dv.astype(BF16)


def attend_backward(q, k, v, do, o, qx, kx, lse, first, pairs, gates):
    queries, keys = q.shape[0], k.shape[0]
    by_query = pl.BlockSpec((queries, 128), lambda p: (0, first + p))
    by_key = pl.BlockSpec((keys, 128), lambda p: (0, first + p))
    return pl.pallas_call(
        backward_kernel,
        grid=(pairs,),
        in_specs=[
            by_query, by_key, by_key, by_query, by_query,
            pl.BlockSpec((queries, 128), lambda p: (0, 0)),
            pl.BlockSpec((keys, 128), lambda p: (0, 0)),
            pl.BlockSpec((1, 2, queries), lambda p: (first + p, 0, 0)),
        ] + [pl.BlockSpec(memory_space=pl.ANY)] * len(gates),
        out_specs=[
            pl.BlockSpec((queries, 128), lambda p: (0, p)),
            pl.BlockSpec((keys, 128), lambda p: (0, p)),
            pl.BlockSpec((keys, 128), lambda p: (0, p))],
        out_shape=[
            jax.ShapeDtypeStruct((queries, pairs * 128), BF16),
            jax.ShapeDtypeStruct((keys, pairs * 128), BF16),
            jax.ShapeDtypeStruct((keys, pairs * 128), BF16),
        ],
        compiler_params=pltpu.CompilerParams(vmem_limit_bytes=50 * 2**20),
        cost_estimate=pl.CostEstimate(
            flops=2 * 5 * 2 * pairs * queries * keys * 256, bytes_accessed=6 * 2**20,
            transcendentals=2 * pairs * queries * keys),
        name="attend_backward",
    )(q, k, v, do, o, qx, kx, lse, *gates)


FF_STEP = 512


def expert_kernel(at_ref, at_slot, act_ref, cot_ref, text_ref, wu_ref, wd_ref,
                  branch_ref, grad_ref, *refs):
    keeps, sends, (up_acc, down_acc) = refs[:3], refs[3:6], refs[6:]
    f = pl.program_id(0)
    act, cot = act_ref[...], cot_ref[...]
    text = text_ref[...] > 0.0
    pre = jnp.where(text, mm(act, wu_ref[1]), mm(act, wu_ref[0]))
    inner, slope = gelu_parts(pre)
    grad_pre = jnp.where(text, mm(cot, wd_ref[1], NT), mm(cot, wd_ref[0], NT)) * slope
    branch = jnp.zeros(branch_ref.shape, F32)
    grad = jnp.zeros(branch_ref.shape, F32)
    for e in range(2):
        mine = text if e == 1 else jnp.logical_not(text)
        inner_e = jnp.where(mine, inner, 0.0).astype(BF16)
        grad_e = jnp.where(mine, grad_pre, 0.0).astype(BF16)
        branch += mm(inner_e, wd_ref[e])
        grad += mm(grad_e, wu_ref[e], NT)
        up = mm(act, grad_e, TN)
        up_acc[e, 0] = up[:, :256]
        up_acc[e, 1] = up[:, 256:]
        down_acc[e, pl.ds(pl.multiple_of(f * FF_STEP, FF_STEP), FF_STEP), :] = mm(inner_e, cot, TN)

    @pl.when(f == 0)
    def _():
        branch_ref[...] = branch
        grad_ref[...] = grad

    @pl.when(f > 0)
    def _():
        branch_ref[...] += branch
        grad_ref[...] += grad

    def spill(target, g, base, up_part):
        def cell(i, carry):
            slot = g * 64 + base + i
            if up_part:
                rows = pl.ds(pl.multiple_of(at_slot[slot], 8), 24)
                half = at_slot[192 + slot]
                both = jnp.concatenate([up_acc[0, half, rows, :], up_acc[1, half, rows, :]], axis=0)
                target[i, :48, :] = both.astype(BF16)
            else:
                rows = pl.ds(pl.multiple_of(at_slot[384 + slot], 8), 24)
                lanes = slice(g * 256, (g + 1) * 256)
                both = jnp.concatenate([down_acc[0, rows, lanes], down_acc[1, rows, lanes]], axis=0)
                target[i, 48:, :] = both.astype(BF16)
            return carry
        lax.fori_loop(0, 32, cell, 0, unroll=4)

    for g in range(3):
        @pl.when(f == g)
        def _():
            spill(keeps[g], g, 0, True)
            spill(sends[g], g, 32, True)

    @pl.when(f == 2)
    def _():
        for g in range(3):
            spill(keeps[g], g, 0, False)
            spill(sends[g], g, 32, False)


def experts(core, table, act, cot, text, w_up, w_down):
    slots, width = act.shape
    steps = w_up.shape[2] // 2 // FF_STEP
    whole = pl.BlockSpec((slots, width), lambda f, *_: (0, 0))
    cells = pl.BlockSpec((32, 96, 256), lambda f, *_: (0, 0, 0))
    return pl.pallas_call(
        expert_kernel,
        grid_spec=pltpu.PrefetchScalarGridSpec(
            num_scalar_prefetch=2,
            grid=(steps,),
            in_specs=[
                whole, whole,
                pl.BlockSpec((slots, 1), lambda f, *_: (0, 0)),
                pl.BlockSpec((2, width, FF_STEP), lambda f, at, *_: (0, 0, at[0] * steps + f)),
                pl.BlockSpec((2, FF_STEP, width), lambda f, at, *_: (0, at[0] * steps + f, 0)),
            ],
            out_specs=[whole, whole] + [cells] * 6,
            scratch_shapes=[
                pltpu.VMEM((2, 2, width, 256), F32),
                pltpu.VMEM((2, steps * FF_STEP, width), F32),
            ],
        ),
        out_shape=[jax.ShapeDtypeStruct((slots, width), F32)] * 2
        + [jax.ShapeDtypeStruct((32, 96, 256), BF16)] * 6,
        compiler_params=pltpu.CompilerParams(
            vmem_limit_bytes=60 * 2**20, dimension_semantics=("arbitrary",)),
        cost_estimate=pl.CostEstimate(
            flops=12 * 2 * slots * width * steps * FF_STEP, bytes_accessed=24 * 2**20,
            transcendentals=2 * slots * steps * FF_STEP),
        name="experts",
    )(core.reshape(1), table, act, cot, text, w_up, w_down)


def cell_places():
    table = np.zeros((32, 4, 3, 3, 4, 4, 4), np.int32)
    for r, s in np.ndindex(32, 4):
        here = {"z": r // 8, "y": r % 4, "x": (s // 2) * 2 + (r // 4) % 2}
        flips = (0, 1, 3, 2) if s % 2 else (0, 3, 1, 2)
        for g, order in enumerate(ORDERS):
            for slot in np.ndindex(4, 4, 4):
                at = {a: here[a] ^ flips[n] for a, n in zip(order, slot)}
                x_hi, x_lo = at["x"] // 2, at["x"] % 2
                table[(r, s, 0, g) + slot] = 24 * (at["z"] * 8 + x_lo * 4 + at["y"])
                table[(r, s, 1, g) + slot] = x_hi
                table[(r, s, 2, g) + slot] = 24 * (
                    (at["z"] % 2) * 32 + x_lo * 16 + at["y"] * 4 + x_hi * 2 + at["z"] // 2)
    return table.reshape(128, 1, 576)


def halving(keeps, sends):
    kept = [k.reshape(2, 4, 4, 96, 256) for k in keeps]
    sent = [s.reshape(2, 4, 4, 96, 256) for s in sends]
    for stage in range(3):
        arrived = [send(sent[g], axis_step(ORDERS[g][stage], True)) for g in range(3)]
        yield arrived
        passed = [add_low(kept[g][1], arrived[g][1]) for g in range(3)]
        mine = [add_low(kept[g][0], arrived[g][0]) for g in range(3)]
        arrived = [send(passed[g], axis_step(ORDERS[g][stage], False)) for g in range(3)]
        yield arrived
        if stage < 2:
            kept = [add_low(mine[g][:2], arrived[g][:2]) for g in range(3)]
            sent = [add_low(mine[g][2:], arrived[g][2:]) for g in range(3)]
    yield [add_low(mine[g], arrived[g]) for g in range(3)]


def copy_kernel(values_ref, *refs):
    refs[-1][...] = values_ref[...]


def after(values, gates):
    return pl.pallas_call(
        copy_kernel,
        in_specs=[pl.BlockSpec(memory_space=pltpu.VMEM)] + [pl.BlockSpec(memory_space=pl.ANY)] * len(gates),
        out_specs=pl.BlockSpec(memory_space=pltpu.VMEM),
        out_shape=jax.ShapeDtypeStruct(values.shape, values.dtype),
        name="after",
    )(values, *gates)


def total_kernel(parts_ref, *refs):
    refs[-1][...] = jnp.sum(parts_ref[...].astype(F32), axis=0)


def total(parts, gates):
    return pl.pallas_call(
        total_kernel,
        in_specs=[pl.BlockSpec(memory_space=pltpu.VMEM)] + [pl.BlockSpec(memory_space=pl.ANY)] * len(gates),
        out_specs=pl.BlockSpec(memory_space=pltpu.VMEM),
        out_shape=jax.ShapeDtypeStruct(parts.shape[1:], F32),
        compiler_params=pltpu.CompilerParams(vmem_limit_bytes=32 * 2**20),
        name="total",
    )(parts, *gates)


def shards(tokens, first_gain, first_shift, w_qkv, w_out, second_gain, second_shift,
           w_up, w_down, modality, segments, partner, cotangent):
    own_n = tokens.shape[1]
    chip_n = 2 * own_n
    width = tokens.shape[2]
    row_index, seq_index = lax.axis_index("rows"), lax.axis_index("seq")
    core, far = seq_index % 2, seq_index // 2
    table = lax.dynamic_index_in_dim(
        jnp.asarray(cell_places()), row_index * 4 + seq_index, 0, keepdims=False).reshape(576)

    doc_match = segments[0][:, None] == jnp.arange(partner.shape[1], dtype=jnp.int32)[None, :]
    tag = jnp.sum(jnp.where(doc_match, partner[0][None, :], 0), axis=1)
    marks = jnp.concatenate([tag, modality[0], jnp.zeros((width - 2 * own_n,), jnp.int32)])
    marks = jnp.concatenate([marks[None], jnp.zeros((15, width), jnp.int32)]).astype(BF16)
    own_ext = jnp.concatenate([tokens[0], marks])
    far_ext = swap_far(own_ext)
    sib_ext = swap_core(own_ext)
    far_sib_ext = swap_core(far_ext)
    cot_own = cotangent[0]
    cot = jnp.concatenate([cot_own, swap_core(cot_own)])

    def unpack(*parts):
        body = jnp.concatenate([p[:own_n] for p in parts])
        tags = jnp.concatenate([p[own_n, :own_n] for p in parts]).astype(jnp.int32)
        kinds = jnp.concatenate([p[own_n, own_n : 2 * own_n] for p in parts]).astype(jnp.int32)
        return body.astype(F32), tags, kinds

    near_tokens, near_tags, near_kinds = unpack(own_ext, sib_ext)
    away_tokens, away_tags, _ = unpack(far_ext, far_sib_ext)

    own_w = OWN * HD
    def own_columns(weight, at):
        return lax.dynamic_slice_in_dim(weight, at + core * own_w, own_w, axis=1)
    w_q, w_k, w_v = (own_columns(w_qkv, n * width) for n in range(3))
    w_kv = jnp.concatenate([w_k, w_v], axis=1)
    w_all = jnp.concatenate([w_q, w_kv], axis=1)

    xhat_near, factor_near = normalize(near_tokens)
    act1 = (xhat_near * first_gain + first_shift).astype(BF16)
    xhat_away, _ = normalize(away_tokens)
    act1_away = (xhat_away * first_gain + first_shift).astype(BF16)
    proj = mm(act1, w_all)
    queries = (0.125 * proj[:, :own_w]).astype(BF16)
    kv_away = mm(act1_away, w_kv).astype(BF16)
    kv = jnp.concatenate([proj[:, own_w:].astype(BF16), kv_away])
    keys, values = kv[:, :own_w], kv[:, own_w:]

    lane = jnp.arange(128, dtype=jnp.int32)[None, :]
    tags = jnp.concatenate([near_tags, away_tags])
    kx = (lane == tags[:, None]).astype(BF16)
    qx = jnp.where((lane < NIMG) & (lane != near_tags[:, None]), MASKED, 0.0).astype(BF16)

    attended_own, lse = attend_forward(queries, keys, values, qx, kx)
    attended_sib = swap_core(attended_own)
    flipped = jnp.concatenate([attended_sib[own_n:], attended_sib[:own_n]])
    attended = jnp.concatenate([
        jnp.where(core == 0, attended_own, flipped),
        jnp.where(core == 0, flipped, attended_own)], axis=1)

    hidden1 = near_tokens + mm(attended, w_out)
    xhat2, factor2 = normalize(hidden1)
    act2 = (xhat2 * second_gain + second_shift).astype(BF16)

    text = (near_kinds == 1).astype(F32)[:, None]
    outcome = experts(core, table, act2, cot, text, w_up, w_down)
    branch, grad_act2 = outcome[:2]
    ff_steps = halving(outcome[2:5], outcome[5:8])

    branch_send = swap_core(branch[own_n:].astype(BF16))
    layer_output = (hidden1[:own_n] + branch[:own_n] + branch_send.astype(F32)).astype(BF16)

    grad_sib = swap_core(grad_act2.astype(BF16)).astype(F32)
    grad_act2 = grad_act2 + jnp.concatenate([grad_sib[own_n:], grad_sib[:own_n]])
    grad_hidden1 = cot.astype(F32) + normalize_back(grad_act2, xhat2, factor2, second_gain)
    second_gain_part = jnp.sum((grad_act2 * xhat2)[:own_n], axis=0)
    second_shift_part = jnp.sum(grad_act2[:own_n], axis=0)
    grad_proj = grad_hidden1.astype(BF16)
    w_out_rows = lax.dynamic_slice_in_dim(w_out, core * own_w, own_w, axis=0)
    grad_att = mm(grad_proj, w_out_rows, NT).astype(BF16)
    out_half = mm(attended, lax.dynamic_slice_in_dim(grad_proj, core * own_w, own_w, axis=1), TN)

    taken = (queries, keys, values, grad_att, attended_own, qx, kx, lse)
    grads = [attend_backward(*taken, 0, 2, next(ff_steps)),
             attend_backward(*taken, 2, 1, next(ff_steps))]
    grad_q, grad_k, grad_v = (jnp.concatenate([a, b], axis=1) for a, b in zip(*grads))
    grad_kv = jnp.concatenate([grad_k, grad_v], axis=1)
    grad_near = jnp.concatenate([grad_q, grad_kv[:chip_n]], axis=1)
    grad_away = grad_kv[chip_n:]
    act_near = mm(grad_near, w_all, NT)
    act_away = mm(grad_away, w_kv, NT)
    first_gain_part = jnp.sum(act_near * xhat_near, axis=0) + jnp.sum(act_away * xhat_away, axis=0)
    first_shift_part = jnp.sum(act_near, axis=0) + jnp.sum(act_away, axis=0)
    vectors = jnp.stack([first_gain_part, first_shift_part, second_gain_part, second_shift_part])
    vectors = after(jnp.pad(vectors.T, ((0, 0), (0, 124))).astype(BF16), next(ff_steps))
    act_all = jnp.concatenate([act1, act1_away])
    same_core = [list(range(c, 128, 2)) for c in range(2)]
    tail = [mm(act1, grad_q, TN), mm(act_all, grad_kv, TN), out_half]
    tail = jnp.concatenate([t.astype(BF16) for t in tail] + [vectors], axis=1)
    moved = lax.all_to_all(tail.reshape(64, 12, -1), BOTH, 0, 0,
                           tiled=True, axis_index_groups=same_core)
    tail = total(moved, next(ff_steps))

    def add_sibling(partial):
        return partial[:own_n] + swap_core(partial[own_n:].astype(BF16)).astype(F32)
    from_far = swap_far(add_sibling(act_away).astype(BF16)).astype(F32)
    grad_act1 = add_sibling(act_near) + from_far
    token_grad = grad_hidden1[:own_n] + normalize_back(
        grad_act1, xhat_near[:own_n], factor_near[:own_n], first_gain)

    tail = tail.reshape(2, 6, 1664)
    tail_own = lax.dynamic_index_in_dim(tail, core, 0, keepdims=False)
    tail_sib = swap_core(lax.dynamic_index_in_dim(tail, 1 - core, 0, keepdims=False).astype(BF16)).astype(F32)
    vec_sum = (tail_own + tail_sib)[:, 1536:1540].T
    both = jnp.where(core == 0, jnp.stack([tail_own, tail_sib]), jnp.stack([tail_sib, tail_own]))
    both = both[:, :, :1536].reshape(2, 6, 4, own_w).transpose(2, 1, 0, 3).reshape(4, 6, width)
    qkv_grad = both[:3].transpose(1, 0, 2).reshape(6, 3 * width)
    out_grad = both[3]

    for ff_done in ff_steps:
        pass
    held = jnp.stack([jnp.concatenate([ff_done[g][:24], ff_done[g][24:48]], axis=1)
                      for g in range(3)], axis=1)
    rows = spread_rows(held, core, far)
    rows = rows.reshape(2, 2, 6, 3, 2, 256).transpose(4, 2, 1, 3, 0, 5)
    up_rows = rows.reshape(2, 6, 2 * 1536).astype(F32)

    down_held = jnp.concatenate([ff_done[g][48:] for g in range(3)], axis=1)
    down_rows = send(down_held, lambda x, y, z, c: (x, y, 2 * c + z % 2, z // 2)).astype(F32)
    down_rows = down_rows.reshape(2, 24, width)

    slots = 4 * own_n
    factors = jnp.asarray([slots / (2 * NIMG * IMG), slots / (2 * (slots - NIMG * IMG))], F32)[:, None, None]
    return (
        layer_output[None], token_grad[None], vec_sum[0], vec_sum[1], qkv_grad, out_grad,
        vec_sum[2], vec_sum[3], up_rows * factors, down_rows * factors)


def solution(mesh):
    cut = P("rows", "seq", None)
    flat = P(BOTH)
    placed = (cut,) + (P(),) * 8 + (P("rows", "seq"), P("rows", "seq"), P("rows", None), cut)
    return jax.shard_map(
        shards, mesh=mesh, in_specs=placed,
        out_specs=(cut, cut, flat, flat, P(BOTH, None), P(BOTH, None), flat, flat,
                   P(None, BOTH, None), P(None, BOTH, None)),
        check_vma=False)
```

```python
import jax
import jax.numpy as jnp
import numpy as np
from jax import lax
from jax.experimental import pallas as pl
from jax.experimental.pallas import tpu as pltpu
from jax.sharding import PartitionSpec as P

HD = 64
OWN = 6
IMG = 197
NIMG = 4
BOTH = ("rows", "seq")
F32 = jnp.float32
BF16 = jnp.bfloat16
MASKED = -1e30


def route(step):
    pairs = []
    for r in range(32):
        z, x_lo, y = r // 8, (r // 4) % 2, r % 4
        for s in range(4):
            x, c = (s // 2) * 2 + x_lo, s % 2
            tx, ty, tz, tc = step(x, y, z, c)
            target = (tz * 8 + (tx % 2) * 4 + ty) * 4 + (tx // 2) * 2 + tc
            pairs.append((r * 4 + s, target))
    return pairs


def send(values, step):
    return lax.ppermute(values, BOTH, route(step))


def swap_core(values):
    return send(values, lambda x, y, z, c: (x, y, z, 1 - c))


def swap_far(values):
    return send(values, lambda x, y, z, c: (x ^ 2, y, z, c))


def axis_step(axis, first):
    def step(x, y, z, c):
        flip = 1 if (c == 0) == first else 3
        at = {"x": x, "y": y, "z": z}
        at[axis] ^= flip
        return (at["x"], at["y"], at["z"], c)

    return step


UP_FACTORS = (1024 / (2 * 788), 1024 / (2 * 236))
ORDERS = (("x", "y", "z"), ("y", "z", "x"), ("z", "x", "y"))


def normalize(inputs):
    centred = inputs - jnp.mean(inputs, axis=-1, keepdims=True)
    factor = lax.rsqrt(jnp.mean(centred * centred, axis=-1, keepdims=True) + 1e-05)
    return centred * factor, factor


def normalize_back(grad, xhat, factor, gain):
    gy = grad * gain
    mean_gy = jnp.mean(gy, axis=-1, keepdims=True)
    mean_gx = jnp.mean(gy * xhat, axis=-1, keepdims=True)
    return factor * (gy - mean_gy - xhat * mean_gx)


def gelu_parts(pre):
    phi = 0.5 * (1.0 + lax.erf(pre * 0.7071067811865476))
    slope = phi + pre * (0.3989422804014327 * jnp.exp(-0.5 * pre * pre))
    return pre * phi, slope


NT = (((1,), (1,)), ((), ()))
TN = (((0,), (0,)), ((), ()))
NN = (((1,), (0,)), ((), ()))


def mm(left, right, dims=NN):
    return lax.dot_general(left, right, dims, preferred_element_type=F32)


def head_lanes(shape, h):
    lane = lax.broadcasted_iota(jnp.int32, shape, len(shape) - 1)
    return (lane >= HD) == (h == 1)


def forward_kernel(q_ref, k_ref, v_ref, qx_ref, kx_ref, out_ref, lse_ref):
    keys = jnp.concatenate([k_ref[...], kx_ref[...]], axis=1)
    values = v_ref[...]
    q_pair = q_ref[...]
    lanes = head_lanes(q_pair.shape, 0)
    mixed = []
    for h in range(2):
        mine = lanes if h == 0 else jnp.logical_not(lanes)
        query = jnp.concatenate([jnp.where(mine, q_pair, 0), qx_ref[...]], axis=1)
        scores = mm(keys, query, NT)
        peak = jnp.max(scores, axis=0, keepdims=True)
        weights = jnp.exp(scores - peak)
        total = jnp.sum(weights, axis=0, keepdims=True)
        inverse = 1.0 / total
        low = (weights * inverse).astype(BF16)
        mixed.append(mm(low, values, TN))
        lse_ref[0, h : h + 1, :] = peak + jnp.log(total)
    out_ref[...] = jnp.where(lanes, mixed[0], mixed[1]).astype(BF16)


def attend_forward(q, k, v, qx, kx):
    queries, keys = q.shape[0], k.shape[0]
    pairs = OWN // 2
    return pl.pallas_call(
        forward_kernel,
        grid=(pairs,),
        in_specs=[
            pl.BlockSpec((queries, 128), lambda p: (0, p)),
            pl.BlockSpec((keys, 128), lambda p: (0, p)),
            pl.BlockSpec((keys, 128), lambda p: (0, p)),
            pl.BlockSpec((queries, 128), lambda p: (0, 0)),
            pl.BlockSpec((keys, 128), lambda p: (0, 0)),
        ],
        out_specs=[
            pl.BlockSpec((queries, 128), lambda p: (0, p)),
            pl.BlockSpec((1, 2, queries), lambda p: (p, 0, 0)),
        ],
        out_shape=[
            jax.ShapeDtypeStruct((queries, pairs * 128), BF16),
            jax.ShapeDtypeStruct((pairs, 2, queries), F32),
        ],
        compiler_params=pltpu.CompilerParams(vmem_limit_bytes=50 * 2**20),
        cost_estimate=pl.CostEstimate(
            flops=2 * 2 * OWN * queries * keys * 256, bytes_accessed=4 * 2**20,
            transcendentals=OWN * queries * keys),
        name="attend_forward",
    )(q, k, v, qx, kx)


def backward_kernel(q_ref, k_ref, v_ref, do_ref, o_ref, qx_ref, kx_ref, lse_ref, *refs):
    dq_ref, dk_ref, dv_ref = refs[-3:]
    keys = jnp.concatenate([k_ref[...], kx_ref[...]], axis=1)
    k_pair, values, q_pair, grads = k_ref[...], v_ref[...], q_ref[...], do_ref[...]
    lanes = head_lanes(q_pair.shape, 0)
    product = grads.astype(F32) * o_ref[...].astype(F32)
    dq = jnp.zeros(q_pair.shape, F32)
    dk = jnp.zeros(k_pair.shape, F32)
    dv = jnp.zeros(k_pair.shape, F32)
    for h in range(2):
        mine = lanes if h == 0 else jnp.logical_not(lanes)
        q_head = jnp.where(mine, q_pair, 0)
        g_head = jnp.where(mine, grads, 0)
        dot_row = jnp.transpose(jnp.sum(jnp.where(mine, product, 0.0), axis=1, keepdims=True))
        scores = mm(keys, jnp.concatenate([q_head, qx_ref[...]], axis=1), NT)
        prob = jnp.exp(scores - lse_ref[0, h : h + 1, :])
        dv += mm(prob.astype(BF16), g_head)
        grad_prob = mm(values, g_head, NT)
        grad_scores = (prob * (grad_prob - dot_row)).astype(BF16)
        dk += mm(grad_scores, q_head)
        part = mm(grad_scores, k_pair, TN)
        dq += jnp.where(mine, part, 0.0)
    dq_ref[...] = dq.astype(BF16) * jnp.asarray(0.125, BF16)
    dk_ref[...] = dk.astype(BF16)
    dv_ref[...] = dv.astype(BF16)


def attend_backward(q, k, v, do, o, qx, kx, lse, first, pairs, gates):
    queries, keys = q.shape[0], k.shape[0]
    by_query = pl.BlockSpec((queries, 128), lambda p: (0, first + p))
    by_key = pl.BlockSpec((keys, 128), lambda p: (0, first + p))
    return pl.pallas_call(
        backward_kernel,
        grid=(pairs,),
        in_specs=[
            by_query, by_key, by_key, by_query, by_query,
            pl.BlockSpec((queries, 128), lambda p: (0, 0)),
            pl.BlockSpec((keys, 128), lambda p: (0, 0)),
            pl.BlockSpec((1, 2, queries), lambda p: (first + p, 0, 0)),
        ] + [pl.BlockSpec(memory_space=pl.ANY)] * len(gates),
        out_specs=[
            pl.BlockSpec((queries, 128), lambda p: (0, p)),
            pl.BlockSpec((keys, 128), lambda p: (0, p)),
            pl.BlockSpec((keys, 128), lambda p: (0, p))],
        out_shape=[
            jax.ShapeDtypeStruct((queries, pairs * 128), BF16),
            jax.ShapeDtypeStruct((keys, pairs * 128), BF16),
            jax.ShapeDtypeStruct((keys, pairs * 128), BF16),
        ],
        compiler_params=pltpu.CompilerParams(vmem_limit_bytes=50 * 2**20),
        cost_estimate=pl.CostEstimate(
            flops=2 * 5 * 2 * pairs * queries * keys * 256, bytes_accessed=6 * 2**20,
            transcendentals=2 * pairs * queries * keys),
        name="attend_backward",
    )(q, k, v, do, o, qx, kx, lse, *gates)


FF_STEP = 512


def expert_kernel(at_ref, at_slot, act_ref, cot_ref, text_ref, wu_ref, wd_ref,
                  branch_ref, grad_ref, *refs):
    keeps, sends, (up_acc, down_acc) = refs[:3], refs[3:6], refs[6:]
    f = pl.program_id(0)
    act, cot = act_ref[...], cot_ref[...]
    text = text_ref[...] > 0.0
    pre = jnp.where(text, mm(act, wu_ref[1]), mm(act, wu_ref[0]))
    inner, slope = gelu_parts(pre)
    grad_pre = jnp.where(text, mm(cot, wd_ref[1], NT), mm(cot, wd_ref[0], NT)) * slope
    branch = jnp.zeros(branch_ref.shape, F32)
    grad = jnp.zeros(branch_ref.shape, F32)
    for e in range(2):
        mine = text if e == 1 else jnp.logical_not(text)
        inner_e = jnp.where(mine, inner, 0.0).astype(BF16)
        grad_e = jnp.where(mine, grad_pre, 0.0).astype(BF16)
        branch += mm(inner_e, wd_ref[e])
        grad += mm(grad_e, wu_ref[e], NT)
        up = mm(act, grad_e, TN)
        up_acc[e, 0] = up[:, :256]
        up_acc[e, 1] = up[:, 256:]
        down_acc[e, pl.ds(pl.multiple_of(f * FF_STEP, FF_STEP), FF_STEP), :] = mm(inner_e, cot, TN)

    @pl.when(f == 0)
    def _():
        branch_ref[...] = branch
        grad_ref[...] = grad

    @pl.when(f > 0)
    def _():
        branch_ref[...] += branch
        grad_ref[...] += grad

    def spill(target, g, base, up_part):
        def cell(i, carry):
            slot = g * 64 + base + i
            if up_part:
                rows = pl.ds(pl.multiple_of(at_slot[slot], 8), 24)
                half = at_slot[192 + slot]
                both = jnp.concatenate([up_acc[0, half, rows, :], up_acc[1, half, rows, :]], axis=0)
                target[i, :48, :] = both.astype(BF16)
            else:
                rows = pl.ds(pl.multiple_of(at_slot[384 + slot], 8), 24)
                lanes = slice(g * 256, (g + 1) * 256)
                both = jnp.concatenate([down_acc[0, rows, lanes], down_acc[1, rows, lanes]], axis=0)
                target[i, 48:, :] = both.astype(BF16)
            return carry
        lax.fori_loop(0, 32, cell, 0, unroll=4)

    for g in range(3):
        @pl.when(f == g)
        def _():
            spill(keeps[g], g, 0, True)
            spill(sends[g], g, 32, True)

    @pl.when(f == 2)
    def _():
        for g in range(3):
            spill(keeps[g], g, 0, False)
            spill(sends[g], g, 32, False)


def experts(core, table, act, cot, text, w_up, w_down):
    slots, width = act.shape
    steps = w_up.shape[2] // 2 // FF_STEP
    whole = pl.BlockSpec((slots, width), lambda f, *_: (0, 0))
    cells = pl.BlockSpec((32, 96, 256), lambda f, *_: (0, 0, 0))
    return pl.pallas_call(
        expert_kernel,
        grid_spec=pltpu.PrefetchScalarGridSpec(
            num_scalar_prefetch=2,
            grid=(steps,),
            in_specs=[
                whole, whole,
                pl.BlockSpec((slots, 1), lambda f, *_: (0, 0)),
                pl.BlockSpec((2, width, FF_STEP), lambda f, at, *_: (0, 0, at[0] * steps + f)),
                pl.BlockSpec((2, FF_STEP, width), lambda f, at, *_: (0, at[0] * steps + f, 0)),
            ],
            out_specs=[whole, whole] + [cells] * 6,
            scratch_shapes=[
                pltpu.VMEM((2, 2, width, 256), F32),
                pltpu.VMEM((2, steps * FF_STEP, width), F32),
            ],
        ),
        out_shape=[jax.ShapeDtypeStruct((slots, width), F32)] * 2
        + [jax.ShapeDtypeStruct((32, 96, 256), BF16)] * 6,
        compiler_params=pltpu.CompilerParams(
            vmem_limit_bytes=60 * 2**20, dimension_semantics=("arbitrary",)),
        cost_estimate=pl.CostEstimate(
            flops=12 * 2 * slots * width * steps * FF_STEP, bytes_accessed=24 * 2**20,
            transcendentals=2 * slots * steps * FF_STEP),
        name="experts",
    )(core.reshape(1), table, act, cot, text, w_up, w_down)


def cell_places():
    table = np.zeros((32, 4, 3, 3, 4, 4, 4), np.int32)
    for r, s in np.ndindex(32, 4):
        here = {"z": r // 8, "y": r % 4, "x": (s // 2) * 2 + (r // 4) % 2}
        flips = (0, 1, 3, 2) if s % 2 else (0, 3, 1, 2)
        for g, order in enumerate(ORDERS):
            for slot in np.ndindex(4, 4, 4):
                at = {a: here[a] ^ flips[n] for a, n in zip(order, slot)}
                x_hi, x_lo = at["x"] // 2, at["x"] % 2
                table[(r, s, 0, g) + slot] = 24 * (at["z"] * 8 + x_lo * 4 + at["y"])
                table[(r, s, 1, g) + slot] = x_hi
                table[(r, s, 2, g) + slot] = 24 * (
                    (at["z"] % 2) * 32 + x_lo * 16 + at["y"] * 4 + x_hi * 2 + at["z"] // 2)
    return table.reshape(128, 1, 576)


def add_up(parts):
    total = parts[0].astype(F32)
    for part in parts[1:]:
        total = total + part.astype(F32)
    return total.astype(BF16)


def pass_kernel(*refs):
    count = len(refs) // 3
    for g in range(count):
        refs[2 * count + g][...] = add_up([refs[2 * g][...], refs[2 * g + 1][...]])


def pass_on(kept, arrived, name):
    _, slots, rows, lanes = kept[0].shape
    block = max(slots // 4, 1)
    one = pl.BlockSpec((None, block, rows, lanes), lambda i: (1, i, 0, 0))
    return pl.pallas_call(
        pass_kernel,
        grid=(slots // block,),
        in_specs=[one] * (2 * len(kept)),
        out_specs=[pl.BlockSpec((block, rows, lanes), lambda i: (i, 0, 0))] * len(kept),
        out_shape=[jax.ShapeDtypeStruct((slots, rows, lanes), BF16)] * len(kept),
        compiler_params=pltpu.CompilerParams(vmem_limit_bytes=32 * 2**20),
        cost_estimate=pl.CostEstimate(
            flops=0, transcendentals=0, bytes_accessed=6 * len(kept) * slots * rows * lanes),
        name=name,
    )(*[v for pair in zip(kept, arrived) for v in pair])


def settle_kernel(groups, sizes, *refs):
    ins, outs = refs[: -2 * groups], refs[-2 * groups :]
    at = 0
    for g in range(groups):
        row = 0
        for size in sizes:
            for half in range(2):
                parts = [ins[at + k][...] for k in range(3)]
                outs[2 * g + half][:, row : row + size, :] = add_up(parts)
                at += 3
            row += size


def settle(pieces, name):
    groups = len(pieces[0])
    sizes = [p[0][0].shape[2] for p in pieces]
    _, slots, _, lanes = pieces[0][0][0].shape
    half = slots // 2
    block = max(half // 4, 1)
    steps = half // block
    operands, specs = [], []
    for g in range(groups):
        for p, size in zip(pieces, sizes):
            for h in range(2):
                wide = pl.BlockSpec(
                    (None, block, size, lanes), lambda i, h=h: (0, i + h * steps, 0, 0))
                flat = pl.BlockSpec((block, size, lanes), lambda i, h=h: (i + h * steps, 0, 0))
                operands += list(p[g])
                specs += [wide, wide, flat]
    rows = sum(sizes)
    outs = pl.pallas_call(
        lambda *refs: settle_kernel(groups, sizes, *refs),
        grid=(steps,),
        in_specs=specs,
        out_specs=[pl.BlockSpec((block, rows, lanes), lambda i: (i, 0, 0))] * (2 * groups),
        out_shape=[jax.ShapeDtypeStruct((half, rows, lanes), BF16)] * (2 * groups),
        compiler_params=pltpu.CompilerParams(vmem_limit_bytes=32 * 2**20),
        cost_estimate=pl.CostEstimate(
            flops=0, transcendentals=0, bytes_accessed=8 * groups * slots * rows * lanes),
        name=name,
    )(*operands)
    quarter = half // 2
    shaped = [o.reshape(2, quarter, rows, lanes) for o in outs]
    return shaped[0::2], shaped[1::2]


def finish_kernel(*refs):
    held_ref, down_ref = refs[-2:]
    for g in range(3):
        cell = add_up([refs[3 * g + k][...] for k in range(3)])
        held_ref[g, :48, :] = cell[:48]
        held_ref[g, 48:, :] = cell[96:]
        down_ref[g] = cell[48:96]


def finish(kept, first, second):
    wide = pl.BlockSpec((None, None, 128, 256), lambda i: (0, 0, 0, 0))
    flat = pl.BlockSpec((None, 128, 256), lambda i: (0, 0, 0))
    return pl.pallas_call(
        finish_kernel,
        grid=(1,),
        in_specs=[wide, wide, flat] * 3,
        out_specs=[pl.BlockSpec((3, 80, 256), lambda i: (0, 0, 0)),
                   pl.BlockSpec((3, 48, 256), lambda i: (0, 0, 0))],
        out_shape=[jax.ShapeDtypeStruct((3, 80, 256), BF16), jax.ShapeDtypeStruct((3, 48, 256), BF16)],
        name="finish",
    )(*[v for g in range(3) for v in (kept[g], first[g], second[g])])


def tail_kernel(at_slot, act_ref, away_ref, q_ref, ka_ref, kb_ref, va_ref, vb_ref,
                att_ref, proj_ref, *refs):
    keeps, sends, acc = refs[:3], refs[3:6], refs[6]

    def put(first, part):
        for n in range(part.shape[1] // 128):
            column = first + n * 128
            lanes = slice(column % 256, column % 256 + 128)
            acc[column // 256, :, lanes] = part[:, n * 128 : (n + 1) * 128]

    act, away = act_ref[...], away_ref[...]
    half = act.shape[0]
    put(0, mm(act, q_ref[...], TN))
    for first, refs_of in ((384, (ka_ref, kb_ref)), (768, (va_ref, vb_ref))):
        for ref in refs_of:
            put(first, mm(act, ref[:half, :], TN) + mm(away, ref[half:, :], TN))
            first += ref.shape[1]
    put(1152, mm(att_ref[...], proj_ref[...], TN))

    def spill(target, g, base):
        def cell(i, carry):
            slot = g * 64 + base + i
            rows = pl.ds(pl.multiple_of(at_slot[slot], 8), 24)
            part = acc[2 * g + at_slot[192 + slot], rows, :]
            target[i] = jnp.concatenate([part, jnp.zeros((8, 256), F32)], axis=0).astype(BF16)
            return carry
        lax.fori_loop(0, 32, cell, 0, unroll=4)

    for g in range(3):
        spill(keeps[g], g, 0)
        spill(sends[g], g, 32)


def tail_cells(table, *operands):
    vmem = pl.BlockSpec(memory_space=pltpu.VMEM)
    return pl.pallas_call(
        tail_kernel,
        in_specs=[pl.BlockSpec(memory_space=pltpu.SMEM)] + [vmem] * len(operands),
        out_specs=[vmem] * 6,
        out_shape=[jax.ShapeDtypeStruct((32, 32, 256), BF16)] * 6,
        scratch_shapes=[pltpu.VMEM((6, 768, 256), F32)],
        compiler_params=pltpu.CompilerParams(vmem_limit_bytes=40 * 2**20),
        cost_estimate=pl.CostEstimate(
            flops=2 * 768 * 384 * 512 * 6, bytes_accessed=10 * 2**20, transcendentals=0),
        name="tail_cells",
    )(table, *operands)


def assemble_kernel(place, own_ref, near_ref, away_ref, cross_ref, up_ref, qkv_ref, out_ref, held):
    core, far = place[0], place[1]
    held[far * 2 + core] = own_ref[...]
    held[far * 2 + 1 - core] = near_ref[...]
    held[2 - far * 2 + core] = away_ref[...]
    held[2 - far * 2 + 1 - core] = cross_ref[...]
    row = lax.broadcasted_iota(jnp.int32, (24, 80), 0)
    column = lax.broadcasted_iota(jnp.int32, (24, 80), 1)
    wanted = (row // 8) * 24 + far * 12 + core * 6 + row % 8
    select = jnp.where((column == wanted) & (row % 8 < 6), 1.0, 0.0).astype(BF16)
    for x_hi in range(2):
        for c in range(2):
            for g in range(3):
                rows = mm(select, held[x_hi * 2 + c, g])
                first = c * 1536 + g * 512 + x_hi * 256
                for e in range(2):
                    factor = UP_FACTORS[e]
                    up_ref[e, :, first : first + 256] = rows[8 * e : 8 * e + 6] * factor
                for n in range(2):
                    at = g * 512 + x_hi * 256 + n * 128
                    kind, within = at // 384, at % 384 + c * 384
                    part = rows[16:22, n * 128 : (n + 1) * 128]
                    if kind < 3:
                        qkv_ref[:, kind * 768 + within : kind * 768 + within + 128] = part
                    else:
                        out_ref[:, within : within + 128] = part


def assemble(place, *parts):
    vmem = pl.BlockSpec(memory_space=pltpu.VMEM)
    return pl.pallas_call(
        assemble_kernel,
        in_specs=[pl.BlockSpec(memory_space=pltpu.SMEM)] + [vmem] * 4,
        out_specs=[vmem] * 3,
        out_shape=[
            jax.ShapeDtypeStruct((2, 6, 3072), F32),
            jax.ShapeDtypeStruct((6, 2304), F32),
            jax.ShapeDtypeStruct((6, 768), F32),
        ],
        scratch_shapes=[pltpu.VMEM((4, 3, 80, 256), BF16)],
        name="assemble",
    )(place, *parts)


def shards(tokens, first_gain, first_shift, w_qkv, w_out, second_gain, second_shift,
           w_up, w_down, modality, segments, partner, cotangent):
    own_n = tokens.shape[1]
    chip_n = 2 * own_n
    width = tokens.shape[2]
    row_index, seq_index = lax.axis_index("rows"), lax.axis_index("seq")
    core, far = seq_index % 2, seq_index // 2
    table = lax.dynamic_index_in_dim(
        jnp.asarray(cell_places()), row_index * 4 + seq_index, 0, keepdims=False).reshape(576)

    doc_match = segments[0][:, None] == jnp.arange(partner.shape[1], dtype=jnp.int32)[None, :]
    tag = jnp.sum(jnp.where(doc_match, partner[0][None, :], 0), axis=1)
    marks = jnp.concatenate([tag, modality[0], jnp.zeros((width - 2 * own_n,), jnp.int32)])
    marks = jnp.concatenate([marks[None], jnp.zeros((15, width), jnp.int32)]).astype(BF16)
    own_ext = jnp.concatenate([tokens[0], marks])
    far_ext = swap_far(own_ext)
    sib_ext = swap_core(own_ext)
    far_sib_ext = swap_core(far_ext)
    cot_own = cotangent[0]
    cot = jnp.concatenate([cot_own, swap_core(cot_own)])

    def unpack(*parts):
        body = jnp.concatenate([p[:own_n] for p in parts])
        tags = jnp.concatenate([p[own_n, :own_n] for p in parts]).astype(jnp.int32)
        kinds = jnp.concatenate([p[own_n, own_n : 2 * own_n] for p in parts]).astype(jnp.int32)
        return body.astype(F32), tags, kinds

    near_tokens, near_tags, near_kinds = unpack(own_ext, sib_ext)
    away_tokens, away_tags, _ = unpack(far_ext, far_sib_ext)

    own_w = OWN * HD
    def own_columns(weight, at):
        return lax.dynamic_slice_in_dim(weight, at + core * own_w, own_w, axis=1)
    w_q, w_k, w_v = (own_columns(w_qkv, n * width) for n in range(3))
    w_kv = jnp.concatenate([w_k, w_v], axis=1)
    w_all = jnp.concatenate([w_q, w_kv], axis=1)

    xhat_near, factor_near = normalize(near_tokens)
    act1 = (xhat_near * first_gain + first_shift).astype(BF16)
    xhat_away, _ = normalize(away_tokens)
    act1_away = (xhat_away * first_gain + first_shift).astype(BF16)
    proj = mm(act1, w_all)
    queries = (0.125 * proj[:, :own_w]).astype(BF16)
    kv_away = mm(act1_away, w_kv).astype(BF16)
    kv = jnp.concatenate([proj[:, own_w:].astype(BF16), kv_away])
    keys, values = kv[:, :own_w], kv[:, own_w:]

    lane = jnp.arange(128, dtype=jnp.int32)[None, :]
    tags = jnp.concatenate([near_tags, away_tags])
    kx = (lane == tags[:, None]).astype(BF16)
    qx = jnp.where((lane < NIMG) & (lane != near_tags[:, None]), MASKED, 0.0).astype(BF16)

    attended_own, lse = attend_forward(queries, keys, values, qx, kx)
    attended_sib = swap_core(attended_own)
    flipped = jnp.concatenate([attended_sib[own_n:], attended_sib[:own_n]])
    attended = jnp.concatenate([
        jnp.where(core == 0, attended_own, flipped),
        jnp.where(core == 0, flipped, attended_own)], axis=1)

    hidden1 = near_tokens + mm(attended, w_out)
    xhat2, factor2 = normalize(hidden1)
    act2 = (xhat2 * second_gain + second_shift).astype(BF16)

    text = (near_kinds == 1).astype(F32)[:, None]
    outcome = experts(core, table, act2, cot, text, w_up, w_down)
    branch, grad_act2 = outcome[:2]
    ff_kept = [v.reshape(2, 16, 96, 256) for v in outcome[2:5]]
    ff_first = [send(v.reshape(2, 16, 96, 256), axis_step(ORDERS[g][0], True))
                for g, v in enumerate(outcome[5:8])]
    ff_passed = pass_on(ff_kept, ff_first, "pass_experts")
    ff_second = [send(v, axis_step(ORDERS[g][0], False)) for g, v in enumerate(ff_passed)]

    branch_send = swap_core(branch[own_n:].astype(BF16))
    layer_output = (hidden1[:own_n] + branch[:own_n] + branch_send.astype(F32)).astype(BF16)

    grad_sib = swap_core(grad_act2.astype(BF16)).astype(F32)
    grad_act2 = grad_act2 + jnp.concatenate([grad_sib[own_n:], grad_sib[:own_n]])
    grad_hidden1 = cot.astype(F32) + normalize_back(grad_act2, xhat2, factor2, second_gain)
    second_gain_part = jnp.sum((grad_act2 * xhat2)[:own_n], axis=0)
    second_shift_part = jnp.sum(grad_act2[:own_n], axis=0)
    grad_proj = grad_hidden1.astype(BF16)
    w_out_rows = lax.dynamic_slice_in_dim(w_out, core * own_w, own_w, axis=0)
    grad_att = mm(grad_proj, w_out_rows, NT).astype(BF16)
    proj_half = lax.dynamic_slice_in_dim(grad_proj, core * own_w, own_w, axis=1)

    taken = (queries, keys, values, grad_att, attended_own, qx, kx, lse)
    grads = [attend_backward(*taken, 0, 2, ff_first), attend_backward(*taken, 2, 1, ff_second)]
    grad_q, grad_k, grad_v = (jnp.concatenate([a, b], axis=1) for a, b in zip(*grads))
    cells = tail_cells(table, act1, act1_away, grad_q, grads[0][1], grads[1][1],
                       grads[0][2], grads[1][2], attended, proj_half)
    kept = [v.reshape(2, 16, 32, 256) for v in cells[:3]]
    first = [send(v.reshape(2, 16, 32, 256), axis_step(ORDERS[g][0], True))
             for g, v in enumerate(cells[3:])]
    second = [send(v, axis_step(ORDERS[g][0], False))
              for g, v in enumerate(pass_on(kept, first, "pass_tail"))]
    kept, sent = settle(
        [list(zip(ff_kept, ff_first, ff_second)), list(zip(kept, first, second))], "settle_all")
    for stage in (1, 2):
        first = [send(v, axis_step(ORDERS[g][stage], True)) for g, v in enumerate(sent)]
        second = [send(v, axis_step(ORDERS[g][stage], False))
                  for g, v in enumerate(pass_on(kept, first, "pass"))]
        if stage == 1:
            kept, sent = settle([list(zip(kept, first, second))], "settle")
    held, down_held = finish(kept, first, second)
    grad_kv = jnp.concatenate([grad_k, grad_v], axis=1)
    grad_near = jnp.concatenate([grad_q, grad_kv[:chip_n]], axis=1)
    grad_away = grad_kv[chip_n:]
    act_near = mm(grad_near, w_all, NT)
    act_away = mm(grad_away, w_kv, NT)
    first_gain_part = jnp.sum(act_near * xhat_near, axis=0) + jnp.sum(act_away * xhat_away, axis=0)
    first_shift_part = jnp.sum(act_near, axis=0) + jnp.sum(act_away, axis=0)
    vectors = jnp.stack([first_gain_part, first_shift_part, second_gain_part, second_shift_part])
    vectors = vectors.reshape(4, 128, 6).transpose(1, 0, 2).reshape(128, 24)
    vectors = jnp.pad(vectors, ((0, 0), (0, 104)))[:, None]
    vec_sum = jnp.sum(lax.all_to_all(vectors, BOTH, 0, 0, tiled=True), axis=(0, 1))[:24].reshape(4, 6)

    def add_sibling(partial):
        return partial[:own_n] + swap_core(partial[own_n:].astype(BF16)).astype(F32)
    from_far = swap_far(add_sibling(act_away).astype(BF16)).astype(F32)
    grad_act1 = add_sibling(act_near) + from_far
    token_grad = grad_hidden1[:own_n] + normalize_back(
        grad_act1, xhat_near[:own_n], factor_near[:own_n], first_gain)

    near = swap_core(held)
    away = swap_far(held)
    cross = send(held, lambda x, y, z, c: (x ^ 2, y, z, 1 - c))
    up_grad, qkv_grad, out_grad = assemble(jnp.stack([core, far]), held, near, away, cross)

    down_rows = send(down_held, lambda x, y, z, c: (x, y, 2 * c + z % 2, z // 2)).astype(F32)
    down_rows = down_rows.reshape(3, 2, 24, 256).transpose(1, 2, 0, 3).reshape(2, 24, width)
    factors = jnp.asarray(UP_FACTORS, F32)[:, None, None]
    return (
        layer_output[None], token_grad[None], vec_sum[0], vec_sum[1], qkv_grad, out_grad,
        vec_sum[2], vec_sum[3], up_grad, down_rows * factors)


def solution(mesh):
    cut = P("rows", "seq", None)
    flat = P(BOTH)
    placed = (cut,) + (P(),) * 8 + (P("rows", "seq"), P("rows", "seq"), P("rows", None), cut)
    return jax.shard_map(
        shards, mesh=mesh, in_specs=placed,
        out_specs=(cut, cut, flat, flat, P(BOTH, None), P(BOTH, None), flat, flat,
                   P(None, BOTH, None), P(None, BOTH, None)),
        check_vma=False)
```

```python
import jax
import jax.numpy as jnp
import numpy as np
from jax import lax
from jax.experimental import pallas as pl
from jax.experimental.pallas import tpu as pltpu
from jax.sharding import PartitionSpec as P

HD = 64
OWN = 6
IMG = 197
NIMG = 4
BOTH = ("rows", "seq")
F32 = jnp.float32
BF16 = jnp.bfloat16
MASKED = -1e30


def route(step):
    pairs = []
    for r in range(32):
        z, x_lo, y = r // 8, (r // 4) % 2, r % 4
        for s in range(4):
            x, c = (s // 2) * 2 + x_lo, s % 2
            tx, ty, tz, tc = step(x, y, z, c)
            target = (tz * 8 + (tx % 2) * 4 + ty) * 4 + (tx // 2) * 2 + tc
            pairs.append((r * 4 + s, target))
    return pairs


def send(values, step):
    return lax.ppermute(values, BOTH, route(step))


def swap_core(values):
    return send(values, lambda x, y, z, c: (x, y, z, 1 - c))


def swap_far(values):
    return send(values, lambda x, y, z, c: (x ^ 2, y, z, c))


def axis_step(axis, first):
    def step(x, y, z, c):
        flip = 1 if (c == 0) == first else 3
        at = {"x": x, "y": y, "z": z}
        at[axis] ^= flip
        return (at["x"], at["y"], at["z"], c)

    return step


UP_FACTORS = (1024 / (2 * 788), 1024 / (2 * 236))
ORDERS = (("x", "y", "z"), ("y", "z", "x"), ("z", "x", "y"))


def normalize(inputs):
    centred = inputs - jnp.mean(inputs, axis=-1, keepdims=True)
    factor = lax.rsqrt(jnp.mean(centred * centred, axis=-1, keepdims=True) + 1e-05)
    return centred * factor, factor


def normalize_back(grad, xhat, factor, gain):
    gy = grad * gain
    mean_gy = jnp.mean(gy, axis=-1, keepdims=True)
    mean_gx = jnp.mean(gy * xhat, axis=-1, keepdims=True)
    return factor * (gy - mean_gy - xhat * mean_gx)


SMALL = pl.BlockSpec(memory_space=pltpu.SMEM)
WHOLE = pl.BlockSpec(memory_space=pltpu.VMEM)
N = 256


def marked_kernel(partner, tokens_ref, segments_ref, modality_ref, out_ref):
    segments = segments_ref[...]
    tag = jnp.zeros(segments.shape, jnp.int32)
    for n in range(8):
        tag = jnp.where(segments == n, partner[0, n], tag)
    marks = jnp.concatenate(
        [tag, modality_ref[...], jnp.zeros((1, 256), jnp.int32)], axis=1).astype(F32)
    out_ref[:N, :] = tokens_ref[...]
    out_ref[N:, :] = jnp.concatenate([marks, jnp.zeros((15, 768), F32)], axis=0).astype(BF16)


def marked(partner, tokens, segments, modality):
    return pl.pallas_call(
        marked_kernel,
        in_specs=[SMALL, WHOLE, WHOLE, WHOLE],
        out_specs=WHOLE,
        out_shape=jax.ShapeDtypeStruct((N + 16, 768), BF16),
        name="marked",
    )(partner, tokens, segments, modality)


def mark_lanes(ext):
    row = ext[N:, :].astype(F32)
    place = lax.broadcasted_iota(jnp.int32, (128, N), 0)
    tag = jnp.broadcast_to(row[:1, :N], (128, N))
    kind = jnp.broadcast_to(row[:1, N : 2 * N], (128, N))
    hot = jnp.where((place < NIMG) & (place.astype(F32) == tag), 1.0, 0.0)
    return jnp.transpose(jnp.where(place == 8, kind, hot))


def project_kernel(at_ref, near, a_ref, b_ref, gain_ref, shift_ref, *refs):
    count = 3 if near else 2
    weights, outs = refs[:count], refs[count:]
    for n, ext_ref in enumerate((a_ref, b_ref)):
        rows = slice(n * N, (n + 1) * N)
        ext = ext_ref[...]
        xhat, _ = normalize(ext[:N].astype(F32))
        act = (xhat * gain_ref[...] + shift_ref[...]).astype(BF16)
        outs[0][rows, :] = act
        marks = mark_lanes(ext)
        outs[1][rows, :] = marks.astype(BF16)
        for m in range(count):
            part = mm(act, weights[m][...])
            outs[2 + m][rows, :] = (0.125 * part if near and m == 0 else part).astype(BF16)
        if near:
            lane = lax.broadcasted_iota(jnp.int32, marks.shape, 1)
            outs[5][rows, :] = jnp.where((lane < NIMG) & (marks == 0.0), MASKED, 0.0).astype(BF16)


def project(core, first, second, gain, shift, w_qkv, near):
    kinds = (0, 1, 2) if near else (1, 2)
    sizes = [768, 128] + [384] * len(kinds) + ([128] if near else [])
    whole = lambda shape: pl.BlockSpec(shape, lambda i, at: (0, 0))
    return pl.pallas_call(
        lambda at_ref, *refs: project_kernel(at_ref, near, *refs),
        grid_spec=pltpu.PrefetchScalarGridSpec(
            num_scalar_prefetch=1,
            grid=(1,),
            in_specs=[whole((N + 16, 768))] * 2 + [whole((1, 768))] * 2
            + [pl.BlockSpec((768, 384), lambda i, at, n=n: (0, 2 * n + at[0])) for n in kinds],
            out_specs=[whole((2 * N, size)) for size in sizes],
        ),
        out_shape=[jax.ShapeDtypeStruct((2 * N, size), BF16) for size in sizes],
        compiler_params=pltpu.CompilerParams(vmem_limit_bytes=60 * 2**20),
        cost_estimate=pl.CostEstimate(
            flops=2 * 512 * 768 * 384 * len(kinds), bytes_accessed=4 * 2**20, transcendentals=0),
        name="project_near" if near else "project_away",
    )(core, first, second, gain, shift, *[w_qkv] * len(kinds))


def middle_kernel(place, grad_ref, sib_ref, xhat_ref, factor_ref, cot_own_ref, cot_sib_ref,
                  gain_ref, w_out_ref, hidden_ref, att_ref, proj_ref, vec_ref):
    core = place[0]
    for n, cot_ref in enumerate((cot_own_ref, cot_sib_ref)):
        rows, other = slice(n * N, (n + 1) * N), slice((1 - n) * N, (2 - n) * N)
        grad = grad_ref[rows, :] + sib_ref[other, :].astype(F32)
        xhat = xhat_ref[rows, :]
        total = cot_ref[...].astype(F32) + normalize_back(grad, xhat, factor_ref[rows, :], gain_ref[...])
        low = total.astype(BF16)
        if n == 0:
            hidden_ref[...] = total
            vec_ref[0:1, :] = jnp.sum(grad * xhat, axis=0, keepdims=True)
            vec_ref[1:2, :] = jnp.sum(grad, axis=0, keepdims=True)
        mine = w_out_ref[pl.ds(pl.multiple_of(core * 384, 384), 384), :]
        att_ref[rows, :] = mm(low, mine, NT).astype(BF16)
        proj_ref[rows, :] = jnp.where(core == 0, low[:, :384], low[:, 384:])


def middle(place, *operands):
    return pl.pallas_call(
        middle_kernel,
        in_specs=[SMALL] + [WHOLE] * len(operands),
        out_specs=[WHOLE] * 4,
        out_shape=[
            jax.ShapeDtypeStruct((N, 768), F32),
            jax.ShapeDtypeStruct((2 * N, 384), BF16),
            jax.ShapeDtypeStruct((2 * N, 384), BF16),
            jax.ShapeDtypeStruct((2, 768), F32),
        ],
        compiler_params=pltpu.CompilerParams(vmem_limit_bytes=60 * 2**20),
        cost_estimate=pl.CostEstimate(
            flops=2 * 512 * 768 * 384, bytes_accessed=8 * 2**20, transcendentals=0),
        name="middle",
    )(place, *operands)


def gelu_parts(pre):
    phi = 0.5 * (1.0 + lax.erf(pre * 0.7071067811865476))
    slope = phi + pre * (0.3989422804014327 * jnp.exp(-0.5 * pre * pre))
    return pre * phi, slope


NT = (((1,), (1,)), ((), ()))
TN = (((0,), (0,)), ((), ()))
NN = (((1,), (0,)), ((), ()))


def mm(left, right, dims=NN):
    return lax.dot_general(left, right, dims, preferred_element_type=F32)


def head_lanes(shape, h):
    lane = lax.broadcasted_iota(jnp.int32, shape, len(shape) - 1)
    return (lane >= HD) == (h == 1)


def stacked(near_ref, away_ref):
    return jnp.concatenate([near_ref[...], away_ref[...]], axis=0)


def forward_kernel(q_ref, kn_ref, ka_ref, vn_ref, va_ref, qx_ref, xn_ref, xa_ref, out_ref, lse_ref):
    keys = jnp.concatenate([stacked(kn_ref, ka_ref), stacked(xn_ref, xa_ref)], axis=1)
    values = stacked(vn_ref, va_ref)
    q_pair = q_ref[...]
    lanes = head_lanes(q_pair.shape, 0)
    mixed = []
    for h in range(2):
        mine = lanes if h == 0 else jnp.logical_not(lanes)
        query = jnp.concatenate([jnp.where(mine, q_pair, 0), qx_ref[...]], axis=1)
        scores = mm(keys, query, NT)
        peak = jnp.max(scores, axis=0, keepdims=True)
        weights = jnp.exp(scores - peak)
        total = jnp.sum(weights, axis=0, keepdims=True)
        inverse = 1.0 / total
        low = (weights * inverse).astype(BF16)
        mixed.append(mm(low, values, TN))
        lse_ref[0, h : h + 1, :] = peak + jnp.log(total)
    out_ref[...] = jnp.where(lanes, mixed[0], mixed[1]).astype(BF16)


BY_PAIR = pl.BlockSpec((2 * N, 128), lambda p: (0, p))
FIXED = pl.BlockSpec((2 * N, 128), lambda p: (0, 0))


def attend_forward(*operands):
    return pl.pallas_call(
        forward_kernel,
        grid=(3,),
        in_specs=[BY_PAIR] * 5 + [FIXED] * 3,
        out_specs=[BY_PAIR, pl.BlockSpec((1, 2, 2 * N), lambda p: (p, 0, 0))],
        out_shape=[
            jax.ShapeDtypeStruct((2 * N, 384), BF16),
            jax.ShapeDtypeStruct((3, 2, 2 * N), F32),
        ],
        compiler_params=pltpu.CompilerParams(vmem_limit_bytes=60 * 2**20),
        cost_estimate=pl.CostEstimate(
            flops=2 * 2 * OWN * 512 * 1024 * 256, bytes_accessed=4 * 2**20,
            transcendentals=OWN * 512 * 1024),
        name="attend_forward",
    )(*operands)


def backward_kernel(q_ref, kn_ref, ka_ref, vn_ref, va_ref, do_ref, o_ref, qx_ref, xn_ref, xa_ref,
                    lse_ref, *refs):
    dq_ref, dk_ref, dv_ref = refs[-3:]
    k_pair, values = stacked(kn_ref, ka_ref), stacked(vn_ref, va_ref)
    keys = jnp.concatenate([k_pair, stacked(xn_ref, xa_ref)], axis=1)
    q_pair, grads = q_ref[...], do_ref[...]
    lanes = head_lanes(q_pair.shape, 0)
    product = grads.astype(F32) * o_ref[...].astype(F32)
    dq = jnp.zeros(q_pair.shape, F32)
    dk = jnp.zeros(k_pair.shape, F32)
    dv = jnp.zeros(k_pair.shape, F32)
    for h in range(2):
        mine = lanes if h == 0 else jnp.logical_not(lanes)
        q_head = jnp.where(mine, q_pair, 0)
        g_head = jnp.where(mine, grads, 0)
        dot_row = jnp.transpose(jnp.sum(jnp.where(mine, product, 0.0), axis=1, keepdims=True))
        scores = mm(keys, jnp.concatenate([q_head, qx_ref[...]], axis=1), NT)
        prob = jnp.exp(scores - lse_ref[0, h : h + 1, :])
        dv += mm(prob.astype(BF16), g_head)
        grad_prob = mm(values, g_head, NT)
        grad_scores = (prob * (grad_prob - dot_row)).astype(BF16)
        dk += mm(grad_scores, q_head)
        part = mm(grad_scores, k_pair, TN)
        dq += jnp.where(mine, part, 0.0)
    dq_ref[...] = dq.astype(BF16) * jnp.asarray(0.125, BF16)
    dk_ref[...] = dk.astype(BF16)
    dv_ref[...] = dv.astype(BF16)


def attend_backward(operands, first, pairs, gates):
    by_pair = pl.BlockSpec((2 * N, 128), lambda p: (0, first + p))
    sizes = (2 * N, 4 * N, 4 * N)
    return pl.pallas_call(
        backward_kernel,
        grid=(pairs,),
        in_specs=[by_pair] * 7 + [FIXED] * 3
        + [pl.BlockSpec((1, 2, 2 * N), lambda p: (first + p, 0, 0))]
        + [pl.BlockSpec(memory_space=pl.ANY)] * len(gates),
        out_specs=[pl.BlockSpec((size, 128), lambda p: (0, p)) for size in sizes],
        out_shape=[jax.ShapeDtypeStruct((size, pairs * 128), BF16) for size in sizes],
        compiler_params=pltpu.CompilerParams(vmem_limit_bytes=60 * 2**20),
        cost_estimate=pl.CostEstimate(
            flops=2 * 5 * 2 * pairs * 512 * 1024 * 256, bytes_accessed=6 * 2**20,
            transcendentals=2 * pairs * 512 * 1024),
        name="attend_backward",
    )(*operands, *gates)


FF_STEP = 512


def expert_kernel(at_ref, at_slot, att_own_ref, att_sib_ref, own_ref, sib_ref, cot_own_ref,
                  cot_sib_ref, marks_ref, gain_ref, shift_ref, w_out_ref, wu_ref, wd_ref,
                  out_ref, out_sib_ref, grad_ref, grad_low_ref, xhat_ref, factor_ref, *refs):
    keeps, sends = refs[:3], refs[3:6]
    up_acc, down_acc, act_acc, branch_ref = refs[6:]
    f = pl.program_id(0)
    core = at_ref[0]

    @pl.when(f == 0)
    def _():
        mine = w_out_ref[pl.ds(pl.multiple_of(core * 384, 384), 384), :]
        other = w_out_ref[pl.ds(pl.multiple_of((1 - core) * 384, 384), 384), :]
        for n, ext_ref in enumerate((own_ref, sib_ref)):
            rows, theirs = slice(n * N, (n + 1) * N), slice((1 - n) * N, (2 - n) * N)
            hidden = ext_ref[:N, :].astype(F32) + (
                mm(att_own_ref[rows, :], mine) + mm(att_sib_ref[theirs, :], other))
            xhat, factor = normalize(hidden)
            xhat_ref[rows, :] = xhat
            factor_ref[rows, :] = factor
            act_acc[rows, :] = (xhat * gain_ref[...] + shift_ref[...]).astype(BF16)
            if n == 0:
                branch_ref[rows, :] = hidden
            else:
                branch_ref[rows, :] = jnp.zeros_like(hidden)
        grad_ref[...] = jnp.zeros(grad_ref.shape, F32)

    act = act_acc[...]
    cot = jnp.concatenate([cot_own_ref[...], cot_sib_ref[...]], axis=0)
    text = marks_ref[:, 8:9].astype(F32) > 0.0
    pre = jnp.where(text, mm(act, wu_ref[1]), mm(act, wu_ref[0]))
    inner, slope = gelu_parts(pre)
    grad_pre = jnp.where(text, mm(cot, wd_ref[1], NT), mm(cot, wd_ref[0], NT)) * slope
    branch = jnp.zeros(branch_ref.shape, F32)
    grad = jnp.zeros(branch_ref.shape, F32)
    for e in range(2):
        mine = text if e == 1 else jnp.logical_not(text)
        inner_e = jnp.where(mine, inner, 0.0).astype(BF16)
        grad_e = jnp.where(mine, grad_pre, 0.0).astype(BF16)
        branch += mm(inner_e, wd_ref[e])
        grad += mm(grad_e, wu_ref[e], NT)
        up = mm(act, grad_e, TN)
        up_acc[e, 0] = up[:, :256]
        up_acc[e, 1] = up[:, 256:]
        down_acc[e, pl.ds(pl.multiple_of(f * FF_STEP, FF_STEP), FF_STEP), :] = mm(inner_e, cot, TN)

    branch_ref[...] += branch
    grad_ref[...] += grad

    def spill(target, g, base, up_part):
        def cell(i, carry):
            slot = g * 64 + base + i
            if up_part:
                rows = pl.ds(pl.multiple_of(at_slot[slot], 8), 24)
                half = at_slot[192 + slot]
                both = jnp.concatenate([up_acc[0, half, rows, :], up_acc[1, half, rows, :]], axis=0)
                target[i, :48, :] = both.astype(BF16)
            else:
                rows = pl.ds(pl.multiple_of(at_slot[384 + slot], 8), 24)
                lanes = slice(g * 256, (g + 1) * 256)
                both = jnp.concatenate([down_acc[0, rows, lanes], down_acc[1, rows, lanes]], axis=0)
                target[i, 48:, :] = both.astype(BF16)
            return carry
        lax.fori_loop(0, 32, cell, 0, unroll=4)

    for g in range(3):
        @pl.when(f == g)
        def _():
            spill(keeps[g], g, 0, True)
            spill(sends[g], g, 32, True)

    @pl.when(f == 2)
    def _():
        out_ref[...] = branch_ref[:N, :]
        out_sib_ref[...] = branch_ref[N:, :].astype(BF16)
        grad_low_ref[...] = grad_ref[...].astype(BF16)
        for g in range(3):
            spill(keeps[g], g, 0, False)
            spill(sends[g], g, 32, False)


def experts(core, table, *operands):
    steps = 3
    shapes = [((N, 768), F32), ((N, 768), BF16), ((2 * N, 768), F32), ((2 * N, 768), BF16),
              ((2 * N, 768), F32), ((2 * N, 1), F32)] + [((32, 96, 256), BF16)] * 6
    fixed = lambda shape: pl.BlockSpec(shape, lambda f, *_: (0,) * len(shape))
    return pl.pallas_call(
        expert_kernel,
        grid_spec=pltpu.PrefetchScalarGridSpec(
            num_scalar_prefetch=2,
            grid=(steps,),
            in_specs=[fixed(v.shape) for v in operands[:-2]] + [
                pl.BlockSpec((2, 768, FF_STEP), lambda f, at, *_: (0, 0, at[0] * steps + f)),
                pl.BlockSpec((2, FF_STEP, 768), lambda f, at, *_: (0, at[0] * steps + f, 0)),
            ],
            out_specs=[fixed(shape) for shape, _ in shapes],
            scratch_shapes=[
                pltpu.VMEM((2, 2, 768, 256), F32),
                pltpu.VMEM((2, steps * FF_STEP, 768), F32),
                pltpu.VMEM((2 * N, 768), BF16),
                pltpu.VMEM((2 * N, 768), F32),
            ],
        ),
        out_shape=[jax.ShapeDtypeStruct(*v) for v in shapes],
        compiler_params=pltpu.CompilerParams(
            vmem_limit_bytes=62 * 2**20, dimension_semantics=("arbitrary",)),
        cost_estimate=pl.CostEstimate(
            flops=12 * 2 * 512 * 768 * 1536 + 2 * 512 * 768 * 768, bytes_accessed=30 * 2**20,
            transcendentals=2 * 512 * 1536),
        name="experts",
    )(core, table, *operands)


def cell_places():
    table = np.zeros((32, 4, 4, 3, 4, 4, 4), np.int32)
    for r, s in np.ndindex(32, 4):
        here = {"z": r // 8, "y": r % 4, "x": (s // 2) * 2 + (r // 4) % 2}
        flips = (0, 1, 3, 2) if s % 2 else (0, 3, 1, 2)
        for g, order in enumerate(ORDERS):
            for slot in np.ndindex(4, 4, 4):
                at = {a: here[a] ^ flips[n] for a, n in zip(order, slot)}
                x_hi, x_lo = at["x"] // 2, at["x"] % 2
                table[(r, s, 0, g) + slot] = 24 * (at["z"] * 8 + x_lo * 4 + at["y"])
                table[(r, s, 1, g) + slot] = x_hi
                table[(r, s, 2, g) + slot] = 24 * (
                    (at["z"] % 2) * 32 + x_lo * 16 + at["y"] * 4 + x_hi * 2 + at["z"] // 2)
                table[(r, s, 3, g) + slot] = at["z"] * 16 + x_lo * 8 + at["y"] * 2 + x_hi
    return table.reshape(128, 768)


def add_up(parts):
    total = parts[0].astype(F32)
    for part in parts[1:]:
        total = total + part.astype(F32)
    return total.astype(BF16)


def pass_kernel(*refs):
    count = len(refs) // 3
    for g in range(count):
        refs[2 * count + g][...] = add_up([refs[2 * g][...], refs[2 * g + 1][...]])


def pass_on(kept, arrived, name):
    _, slots, rows, lanes = kept[0].shape
    block = max(slots // 4, 1)
    one = pl.BlockSpec((None, block, rows, lanes), lambda i: (1, i, 0, 0))
    return pl.pallas_call(
        pass_kernel,
        grid=(slots // block,),
        in_specs=[one] * (2 * len(kept)),
        out_specs=[pl.BlockSpec((block, rows, lanes), lambda i: (i, 0, 0))] * len(kept),
        out_shape=[jax.ShapeDtypeStruct((slots, rows, lanes), BF16)] * len(kept),
        compiler_params=pltpu.CompilerParams(vmem_limit_bytes=60 * 2**20),
        cost_estimate=pl.CostEstimate(
            flops=0, transcendentals=0, bytes_accessed=6 * len(kept) * slots * rows * lanes),
        name=name,
    )(*[v for pair in zip(kept, arrived) for v in pair])


def settle_kernel(groups, sizes, *refs):
    ins, outs = refs[: -2 * groups], refs[-2 * groups :]
    at = 0
    for g in range(groups):
        row = 0
        for size in sizes:
            for half in range(2):
                parts = [ins[at + k][...] for k in range(3)]
                outs[2 * g + half][:, row : row + size, :] = add_up(parts)
                at += 3
            row += size


def settle(pieces, name):
    groups = len(pieces[0])
    sizes = [p[0][0].shape[2] for p in pieces]
    _, slots, _, lanes = pieces[0][0][0].shape
    half = slots // 2
    block = max(half // 4, 1)
    steps = half // block
    operands, specs = [], []
    for g in range(groups):
        for p, size in zip(pieces, sizes):
            for h in range(2):
                wide = pl.BlockSpec(
                    (None, block, size, lanes), lambda i, h=h: (0, i + h * steps, 0, 0))
                flat = pl.BlockSpec((block, size, lanes), lambda i, h=h: (i + h * steps, 0, 0))
                operands += list(p[g])
                specs += [wide, wide, flat]
    rows = sum(sizes)
    outs = pl.pallas_call(
        lambda *refs: settle_kernel(groups, sizes, *refs),
        grid=(steps,),
        in_specs=specs,
        out_specs=[pl.BlockSpec((block, rows, lanes), lambda i: (i, 0, 0))] * (2 * groups),
        out_shape=[jax.ShapeDtypeStruct((half, rows, lanes), BF16)] * (2 * groups),
        compiler_params=pltpu.CompilerParams(vmem_limit_bytes=60 * 2**20),
        cost_estimate=pl.CostEstimate(
            flops=0, transcendentals=0, bytes_accessed=8 * groups * slots * rows * lanes),
        name=name,
    )(*operands)
    quarter = half // 2
    shaped = [o.reshape(2, quarter, rows, lanes) for o in outs]
    return shaped[0::2], shaped[1::2]


def finish_kernel(*refs):
    held_ref, down_ref = refs[-2:]
    for g in range(3):
        cell = add_up([refs[3 * g + k][...] for k in range(3)])
        held_ref[g, :48, :] = cell[:48]
        held_ref[g, 48:, :] = cell[96:]
        down_ref[g] = cell[48:96]


def finish(kept, first, second):
    wide = pl.BlockSpec((None, None, 128, 256), lambda i: (0, 0, 0, 0))
    flat = pl.BlockSpec((None, 128, 256), lambda i: (0, 0, 0))
    return pl.pallas_call(
        finish_kernel,
        grid=(1,),
        in_specs=[wide, wide, flat] * 3,
        out_specs=[pl.BlockSpec((3, 80, 256), lambda i: (0, 0, 0)),
                   pl.BlockSpec((3, 48, 256), lambda i: (0, 0, 0))],
        out_shape=[jax.ShapeDtypeStruct((3, 80, 256), BF16), jax.ShapeDtypeStruct((3, 48, 256), BF16)],
        name="finish",
    )(*[v for g in range(3) for v in (kept[g], first[g], second[g])])


def tail_kernel(at_slot, place, act_ref, away_ref, q_ref, qb_ref, ka_ref, kb_ref, va_ref, vb_ref,
                att_own_ref, att_sib_ref, proj_ref, own_ref, sib_ref, far_ref, far_sib_ref, vec_ref,
                wq_ref, wk_ref, wv_ref, keep_ref, send_ref, *refs):
    keeps, sends, acc, table = refs[:3], refs[3:6], refs[6], refs[7]
    core = place[0]

    def put(first, part, rows=slice(None)):
        for n in range(part.shape[1] // 128):
            column = first + n * 128
            lanes = slice(column % 256, column % 256 + 128)
            acc[column // 256, rows, lanes] = part[:, n * 128 : (n + 1) * 128]

    act, away = act_ref[...], away_ref[...]
    first = 0
    for ref in (q_ref, qb_ref):
        put(first, mm(act, ref[...], TN))
        first += ref.shape[1]
    for ref in (ka_ref, kb_ref, va_ref, vb_ref):
        put(first, mm(act, ref[: 2 * N, :], TN) + mm(away, ref[2 * N :, :], TN))
        first += ref.shape[1]
    mine = pl.ds(pl.multiple_of(core * 384, 384), 384)
    other = pl.ds(pl.multiple_of((1 - core) * 384, 384), 384)
    put(1152, mm(att_own_ref[...], proj_ref[...], TN), mine)
    put(1152, mm(att_sib_ref[:N, :], proj_ref[N:, :], TN)
        + mm(att_sib_ref[N:, :], proj_ref[:N, :], TN), other)

    vectors = [jnp.zeros((1, 768), F32), jnp.zeros((1, 768), F32), vec_ref[0:1, :], vec_ref[1:2, :]]
    wide = ((q_ref, qb_ref, wq_ref), (ka_ref, kb_ref, wk_ref), (va_ref, vb_ref, wv_ref))
    for n, ext_ref in enumerate((own_ref, sib_ref, far_ref, far_sib_ref)):
        rows = slice(n * N, (n + 1) * N)
        total = jnp.zeros((N, 768), F32)
        for a_ref, b_ref, w_ref in wide[0 if n < 2 else 1 :]:
            total += mm(a_ref[rows, :], w_ref[:, :256], NT) + mm(b_ref[rows, :], w_ref[:, 256:], NT)
        xhat, _ = normalize(ext_ref[:N, :].astype(F32))
        vectors[0] += jnp.sum(total * xhat, axis=0, keepdims=True)
        vectors[1] += jnp.sum(total, axis=0, keepdims=True)
        half = slice((n // 2) * N, (n // 2 + 1) * N)
        if n % 2 == 0:
            keep_ref[half, :] = total
        else:
            send_ref[half, :] = total.astype(BF16)

    chip = lax.broadcasted_iota(jnp.int32, (64, 768), 0)
    owner = lax.broadcasted_iota(jnp.int32, (64, 768), 1) // 12
    feature = lax.broadcasted_iota(jnp.int32, (768, 128), 0) % 12
    lane = lax.broadcasted_iota(jnp.int32, (768, 128), 1)
    spread = jnp.zeros((64, 128), F32)
    for n in range(4):
        values = jnp.where(chip == owner, jnp.broadcast_to(vectors[n], (64, 768)), 0.0).astype(BF16)
        spread += mm(values, jnp.where(lane == feature + 12 * n, 1.0, 0.0).astype(BF16))
    table[...] = spread

    def spill(target, g, base):
        def cell(i, carry):
            slot = g * 64 + base + i
            rows = pl.ds(pl.multiple_of(at_slot[slot], 8), 24)
            part = acc[2 * g + at_slot[192 + slot], rows, :]
            if g == 0:
                row = table[pl.ds(at_slot[576 + slot], 1), :]
                extra = jnp.concatenate([jnp.broadcast_to(row, (8, 128)), jnp.zeros((8, 128), F32)], axis=1)
            else:
                extra = jnp.zeros((8, 256), F32)
            target[i] = jnp.concatenate([part, extra], axis=0).astype(BF16)
            return carry
        lax.fori_loop(0, 32, cell, 0, unroll=4)

    for g in range(3):
        spill(keeps[g], g, 0)
        spill(sends[g], g, 32)


def tail_cells(table, core, *operands):
    whole = lambda shape: pl.BlockSpec(shape, lambda i, *_: (0,) * len(shape))
    shapes = [((2 * N, 768), F32), ((2 * N, 768), BF16)] + [((32, 32, 256), BF16)] * 6
    return pl.pallas_call(
        tail_kernel,
        grid_spec=pltpu.PrefetchScalarGridSpec(
            num_scalar_prefetch=2,
            grid=(1,),
            in_specs=[whole(v.shape) for v in operands[:-1]]
            + [pl.BlockSpec((768, 384), lambda i, t, at, n=n: (0, 2 * n + at[0])) for n in range(3)],
            out_specs=[whole(shape) for shape, _ in shapes],
            scratch_shapes=[pltpu.VMEM((6, 768, 256), F32), pltpu.VMEM((64, 128), F32)],
        ),
        out_shape=[jax.ShapeDtypeStruct(*v) for v in shapes],
        compiler_params=pltpu.CompilerParams(vmem_limit_bytes=60 * 2**20),
        cost_estimate=pl.CostEstimate(
            flops=2 * 768 * 384 * 512 * 11, bytes_accessed=14 * 2**20, transcendentals=0),
        name="tail_cells",
    )(table, core, *operands, *[operands[-1]] * 2)


def assemble_kernel(place, own_ref, near_ref, away_ref, cross_ref, up_ref, qkv_ref, out_ref, vec_ref, held):
    core, far = place[0], place[1]
    held[far * 2 + core] = own_ref[...]
    held[far * 2 + 1 - core] = near_ref[...]
    held[2 - far * 2 + core] = away_ref[...]
    held[2 - far * 2 + 1 - core] = cross_ref[...]
    line = held[far * 2, 0, 64:, :128].astype(F32) + held[far * 2 + 1, 0, 64:, :128].astype(F32)
    vec_ref[...] = jnp.where(core == 0, line, pltpu.roll(line, 122, 1))[8:]
    row = lax.broadcasted_iota(jnp.int32, (24, 80), 0)
    column = lax.broadcasted_iota(jnp.int32, (24, 80), 1)
    wanted = (row // 8) * 24 + far * 12 + core * 6 + row % 8
    select = jnp.where((column == wanted) & (row % 8 < 6), 1.0, 0.0).astype(BF16)
    for x_hi in range(2):
        for c in range(2):
            for g in range(3):
                rows = mm(select, held[x_hi * 2 + c, g])
                first = c * 1536 + g * 512 + x_hi * 256
                for e in range(2):
                    factor = UP_FACTORS[e]
                    up_ref[e, :, first : first + 256] = rows[8 * e : 8 * e + 6] * factor
                for n in range(2):
                    at = g * 512 + x_hi * 256 + n * 128
                    kind, within = at // 384, at % 384 + c * 384
                    part = rows[16:22, n * 128 : (n + 1) * 128]
                    if kind < 3:
                        qkv_ref[:, kind * 768 + within : kind * 768 + within + 128] = part
                    else:
                        out_ref[:, within : within + 128] = part


def assemble(place, *parts):
    vmem = pl.BlockSpec(memory_space=pltpu.VMEM)
    return pl.pallas_call(
        assemble_kernel,
        in_specs=[pl.BlockSpec(memory_space=pltpu.SMEM)] + [vmem] * 4,
        out_specs=[vmem] * 4,
        out_shape=[
            jax.ShapeDtypeStruct((2, 6, 3072), F32),
            jax.ShapeDtypeStruct((6, 2304), F32),
            jax.ShapeDtypeStruct((6, 768), F32),
            jax.ShapeDtypeStruct((8, 128), F32),
        ],
        scratch_shapes=[pltpu.VMEM((4, 3, 80, 256), BF16)],
        name="assemble",
    )(place, *parts)


def shards(tokens, first_gain, first_shift, w_qkv, w_out, second_gain, second_shift,
           w_up, w_down, modality, segments, partner, cotangent):
    row_index, seq_index = lax.axis_index("rows"), lax.axis_index("seq")
    core, far = seq_index % 2, seq_index // 2
    place = jnp.stack([core, far]).astype(jnp.int32)
    table = lax.dynamic_index_in_dim(
        jnp.asarray(cell_places()), row_index * 4 + seq_index, 0, keepdims=False)
    gain1, shift1, gain2, shift2 = (
        v.reshape(1, 768) for v in (first_gain, first_shift, second_gain, second_shift))

    own = marked(partner, tokens[0], segments, modality)
    away = swap_far(own)
    sib = swap_core(own)
    away_sib = swap_core(away)
    cot_own = cotangent[0]
    cot_sib = swap_core(cot_own)

    act1, marks, queries, k_near, v_near, qx = project(place, own, sib, gain1, shift1, w_qkv, True)
    act1_away, marks_away, k_away, v_away = project(
        place, away, away_sib, gain1, shift1, w_qkv, False)
    attended, lse = attend_forward(
        queries, k_near, k_away, v_near, v_away, qx, marks, marks_away)
    attended_sib = swap_core(attended)

    outcome = experts(
        place, table, attended, attended_sib, own, sib, cot_own, cot_sib, marks, gain2, shift2,
        w_out, w_up, w_down)
    out_own, out_sib, grad_act2, grad_low, xhat2, factor2 = outcome[:6]
    outcome = outcome[4:]
    ff_kept = [v.reshape(2, 16, 96, 256) for v in outcome[2:5]]
    ff_first = [send(v.reshape(2, 16, 96, 256), axis_step(ORDERS[g][0], True))
                for g, v in enumerate(outcome[5:8])]
    ff_passed = pass_on(ff_kept, ff_first, "pass_experts")
    ff_second = [send(v, axis_step(ORDERS[g][0], False)) for g, v in enumerate(ff_passed)]

    grad_sib = swap_core(grad_low)
    hidden_grad, grad_att, proj_half, vectors = middle(
        place, grad_act2, grad_sib, xhat2, factor2, cot_own, cot_sib, gain2, w_out)

    taken = (queries, k_near, k_away, v_near, v_away, grad_att, attended, qx, marks, marks_away, lse)
    (q_a, k_a, v_a), (q_b, k_b, v_b) = (
        attend_backward(taken, 0, 2, ff_first), attend_backward(taken, 2, 1, ff_second))
    partial_own, partial_sib, *cells = tail_cells(
        table, place, act1, act1_away, q_a, q_b, k_a, k_b, v_a, v_b, attended, attended_sib,
        proj_half, own, sib, away, away_sib, vectors, w_qkv)
    kept = [v.reshape(2, 16, 32, 256) for v in cells[:3]]
    first = [send(v.reshape(2, 16, 32, 256), axis_step(ORDERS[g][0], True))
             for g, v in enumerate(cells[3:])]
    second = [send(v, axis_step(ORDERS[g][0], False))
              for g, v in enumerate(pass_on(kept, first, "pass_tail"))]
    kept, sent = settle(
        [list(zip(ff_kept, ff_first, ff_second)), list(zip(kept, first, second))], "settle_all")
    for stage in (1, 2):
        first = [send(v, axis_step(ORDERS[g][stage], True)) for g, v in enumerate(sent)]
        second = [send(v, axis_step(ORDERS[g][stage], False))
                  for g, v in enumerate(pass_on(kept, first, "pass"))]
        if stage == 1:
            kept, sent = settle([list(zip(kept, first, second))], "settle")
    held, down_held = finish(kept, first, second)
    partial = partial_own + swap_core(partial_sib).astype(F32)
    grad_act1 = partial[:N] + swap_far(partial[N:].astype(BF16)).astype(F32)
    xhat1, factor1 = normalize(tokens[0].astype(F32))
    token_grad = hidden_grad + normalize_back(grad_act1, xhat1, factor1, first_gain)
    layer_output = (out_own + swap_core(out_sib).astype(F32)).astype(BF16)

    near, beyond = swap_core(held), swap_far(held)
    cross = send(held, lambda x, y, z, c: (x ^ 2, y, z, 1 - c))
    up_grad, qkv_grad, out_grad, line = assemble(place, held, near, beyond, cross)

    down_rows = send(down_held, lambda x, y, z, c: (x, y, 2 * c + z % 2, z // 2)).astype(F32)
    down_rows = down_rows.reshape(3, 2, 24, 256).transpose(1, 2, 0, 3).reshape(2, 24, 768)
    factors = jnp.asarray(UP_FACTORS, F32)[:, None, None]
    return (
        layer_output[None], token_grad[None], line[0, :6], line[0, 12:18], qkv_grad, out_grad,
        line[0, 24:30], line[0, 36:42], up_grad, down_rows * factors)


def solution(mesh):
    cut = P("rows", "seq", None)
    flat = P(BOTH)
    placed = (cut,) + (P(),) * 8 + (P("rows", "seq"), P("rows", "seq"), P("rows", None), cut)
    return jax.shard_map(
        shards, mesh=mesh, in_specs=placed,
        out_specs=(cut, cut, flat, flat, P(BOTH, None), P(BOTH, None), flat, flat,
                   P(None, BOTH, None), P(None, BOTH, None)),
        check_vma=False)
```

```python
import jax
import jax.numpy as jnp
import numpy as np
from jax import lax
from jax.experimental import pallas as pl
from jax.experimental.pallas import tpu as pltpu
from jax.sharding import PartitionSpec as P

HD = 64
OWN = 6
IMG = 197
NIMG = 4
BOTH = ("rows", "seq")
F32 = jnp.float32
BF16 = jnp.bfloat16
MASKED = -1e30


def route(step):
    pairs = []
    for r in range(32):
        z, x_lo, y = r // 8, (r // 4) % 2, r % 4
        for s in range(4):
            x, c = (s // 2) * 2 + x_lo, s % 2
            tx, ty, tz, tc = step(x, y, z, c)
            target = (tz * 8 + (tx % 2) * 4 + ty) * 4 + (tx // 2) * 2 + tc
            pairs.append((r * 4 + s, target))
    return pairs


def send(values, step):
    return lax.ppermute(values, BOTH, route(step))


def swap_core(values):
    return send(values, lambda x, y, z, c: (x, y, z, 1 - c))


def swap_far(values):
    return send(values, lambda x, y, z, c: (x ^ 2, y, z, c))


def axis_step(axis, first):
    def step(x, y, z, c):
        flip = 1 if (c == 0) == first else 3
        at = {"x": x, "y": y, "z": z}
        at[axis] ^= flip
        return (at["x"], at["y"], at["z"], c)

    return step


UP_FACTORS = (1024 / (2 * 788), 1024 / (2 * 236))
ORDERS = (("x", "y", "z"), ("y", "z", "x"), ("z", "x", "y"))


def normalize(inputs):
    centred = inputs - jnp.mean(inputs, axis=-1, keepdims=True)
    factor = lax.rsqrt(jnp.mean(centred * centred, axis=-1, keepdims=True) + 1e-05)
    return centred * factor, factor


def normalize_back(grad, xhat, factor, gain):
    gy = grad * gain
    mean_gy = jnp.mean(gy, axis=-1, keepdims=True)
    mean_gx = jnp.mean(gy * xhat, axis=-1, keepdims=True)
    return factor * (gy - mean_gy - xhat * mean_gx)


SMALL = pl.BlockSpec(memory_space=pltpu.SMEM)
WHOLE = pl.BlockSpec(memory_space=pltpu.VMEM)
N = 256


def marked_kernel(partner, tokens_ref, segments_ref, modality_ref, out_ref):
    segments = segments_ref[...]
    tag = jnp.zeros(segments.shape, jnp.int32)
    for n in range(8):
        tag = jnp.where(segments == n, partner[0, n], tag)
    marks = jnp.concatenate(
        [tag, modality_ref[...], jnp.zeros((1, 256), jnp.int32)], axis=1).astype(F32)
    out_ref[:N, :] = tokens_ref[...]
    out_ref[N:, :] = jnp.concatenate([marks, jnp.zeros((15, 768), F32)], axis=0).astype(BF16)


def marked(partner, tokens, segments, modality):
    return pl.pallas_call(
        marked_kernel,
        in_specs=[SMALL, WHOLE, WHOLE, WHOLE],
        out_specs=WHOLE,
        out_shape=jax.ShapeDtypeStruct((N + 16, 768), BF16),
        name="marked",
    )(partner, tokens, segments, modality)


def mark_lanes(ext):
    row = ext[N:, :].astype(F32)
    place = lax.broadcasted_iota(jnp.int32, (128, N), 0)
    tag = jnp.broadcast_to(row[:1, :N], (128, N))
    kind = jnp.broadcast_to(row[:1, N : 2 * N], (128, N))
    hot = jnp.where((place < NIMG) & (place.astype(F32) == tag), 1.0, 0.0)
    return jnp.transpose(jnp.where(place == 8, kind, hot))


def project_kernel(at_ref, near, a_ref, b_ref, gain_ref, shift_ref, *refs):
    count = 3 if near else 2
    weights, outs = refs[:count], refs[count:]
    for n, ext_ref in enumerate((a_ref, b_ref)):
        rows = slice(n * N, (n + 1) * N)
        ext = ext_ref[...]
        xhat, _ = normalize(ext[:N].astype(F32))
        act = (xhat * gain_ref[...] + shift_ref[...]).astype(BF16)
        outs[0][rows, :] = act
        marks = mark_lanes(ext)
        outs[1][rows, :] = marks.astype(BF16)
        for m in range(count):
            part = mm(act, weights[m][...])
            outs[2 + m][rows, :] = (0.125 * part if near and m == 0 else part).astype(BF16)
        if near:
            lane = lax.broadcasted_iota(jnp.int32, marks.shape, 1)
            outs[5][rows, :] = jnp.where((lane < NIMG) & (marks == 0.0), MASKED, 0.0).astype(BF16)


def project(core, first, second, gain, shift, w_qkv, near):
    kinds = (0, 1, 2) if near else (1, 2)
    sizes = [768, 128] + [384] * len(kinds) + ([128] if near else [])
    whole = lambda shape: pl.BlockSpec(shape, lambda i, at: (0, 0))
    return pl.pallas_call(
        lambda at_ref, *refs: project_kernel(at_ref, near, *refs),
        grid_spec=pltpu.PrefetchScalarGridSpec(
            num_scalar_prefetch=1,
            grid=(1,),
            in_specs=[whole((N + 16, 768))] * 2 + [whole((1, 768))] * 2
            + [pl.BlockSpec((768, 384), lambda i, at, n=n: (0, 2 * n + at[0])) for n in kinds],
            out_specs=[whole((2 * N, size)) for size in sizes],
        ),
        out_shape=[jax.ShapeDtypeStruct((2 * N, size), BF16) for size in sizes],
        compiler_params=pltpu.CompilerParams(vmem_limit_bytes=24 * 2**20),
        cost_estimate=pl.CostEstimate(
            flops=2 * 512 * 768 * 384 * len(kinds), bytes_accessed=4 * 2**20, transcendentals=0),
        name="project_near" if near else "project_away",
    )(core, first, second, gain, shift, *[w_qkv] * len(kinds))


def middle_kernel(place, grad_ref, sib_ref, xhat_ref, factor_ref, cot_own_ref, cot_sib_ref,
                  gain_ref, w_out_ref, hidden_ref, att_ref, proj_ref, vec_ref):
    core = place[0]
    for n, cot_ref in enumerate((cot_own_ref, cot_sib_ref)):
        rows, other = slice(n * N, (n + 1) * N), slice((1 - n) * N, (2 - n) * N)
        grad = grad_ref[rows, :] + sib_ref[other, :].astype(F32)
        xhat = xhat_ref[rows, :]
        total = cot_ref[...].astype(F32) + normalize_back(grad, xhat, factor_ref[rows, :], gain_ref[...])
        low = total.astype(BF16)
        if n == 0:
            hidden_ref[...] = total
            vec_ref[0:1, :] = jnp.sum(grad * xhat, axis=0, keepdims=True)
            vec_ref[1:2, :] = jnp.sum(grad, axis=0, keepdims=True)
        mine = w_out_ref[pl.ds(pl.multiple_of(core * 384, 384), 384), :]
        att_ref[rows, :] = mm(low, mine, NT).astype(BF16)
        proj_ref[rows, :] = jnp.where(core == 0, low[:, :384], low[:, 384:])


def middle(place, *operands):
    return pl.pallas_call(
        middle_kernel,
        in_specs=[SMALL] + [WHOLE] * len(operands),
        out_specs=[WHOLE] * 4,
        out_shape=[
            jax.ShapeDtypeStruct((N, 768), F32),
            jax.ShapeDtypeStruct((2 * N, 384), BF16),
            jax.ShapeDtypeStruct((2 * N, 384), BF16),
            jax.ShapeDtypeStruct((2, 768), F32),
        ],
        compiler_params=pltpu.CompilerParams(vmem_limit_bytes=24 * 2**20),
        cost_estimate=pl.CostEstimate(
            flops=2 * 512 * 768 * 384, bytes_accessed=8 * 2**20, transcendentals=0),
        name="middle",
    )(place, *operands)


def gelu_parts(pre):
    phi = 0.5 * (1.0 + lax.erf(pre * 0.7071067811865476))
    slope = phi + pre * (0.3989422804014327 * jnp.exp(-0.5 * pre * pre))
    return pre * phi, slope


NT = (((1,), (1,)), ((), ()))
TN = (((0,), (0,)), ((), ()))
NN = (((1,), (0,)), ((), ()))


def mm(left, right, dims=NN):
    return lax.dot_general(left, right, dims, preferred_element_type=F32)


def head_lanes(shape, h):
    lane = lax.broadcasted_iota(jnp.int32, shape, len(shape) - 1)
    return (lane >= HD) == (h == 1)


def stacked(near_ref, away_ref):
    return jnp.concatenate([near_ref[...], away_ref[...]], axis=0)


def forward_kernel(q_ref, kn_ref, ka_ref, vn_ref, va_ref, qx_ref, xn_ref, xa_ref, out_ref, lse_ref):
    keys = jnp.concatenate([stacked(kn_ref, ka_ref), stacked(xn_ref, xa_ref)], axis=1)
    values = stacked(vn_ref, va_ref)
    q_pair = q_ref[...]
    lanes = head_lanes(q_pair.shape, 0)
    mixed = []
    for h in range(2):
        mine = lanes if h == 0 else jnp.logical_not(lanes)
        query = jnp.concatenate([jnp.where(mine, q_pair, 0), qx_ref[...]], axis=1)
        scores = mm(keys, query, NT)
        peak = jnp.max(scores, axis=0, keepdims=True)
        weights = jnp.exp(scores - peak)
        total = jnp.sum(weights, axis=0, keepdims=True)
        inverse = 1.0 / total
        low = (weights * inverse).astype(BF16)
        mixed.append(mm(low, values, TN))
        lse_ref[0, h : h + 1, :] = peak + jnp.log(total)
    out_ref[...] = jnp.where(lanes, mixed[0], mixed[1]).astype(BF16)


BY_PAIR = pl.BlockSpec((2 * N, 128), lambda p: (0, p))
FIXED = pl.BlockSpec((2 * N, 128), lambda p: (0, 0))


def attend_forward(*operands):
    return pl.pallas_call(
        forward_kernel,
        grid=(3,),
        in_specs=[BY_PAIR] * 5 + [FIXED] * 3,
        out_specs=[BY_PAIR, pl.BlockSpec((1, 2, 2 * N), lambda p: (p, 0, 0))],
        out_shape=[
            jax.ShapeDtypeStruct((2 * N, 384), BF16),
            jax.ShapeDtypeStruct((3, 2, 2 * N), F32),
        ],
        compiler_params=pltpu.CompilerParams(vmem_limit_bytes=44 * 2**20),
        cost_estimate=pl.CostEstimate(
            flops=2 * 2 * OWN * 512 * 1024 * 256, bytes_accessed=4 * 2**20,
            transcendentals=OWN * 512 * 1024),
        name="attend_forward",
    )(*operands)


def backward_kernel(q_ref, kn_ref, ka_ref, vn_ref, va_ref, do_ref, o_ref, qx_ref, xn_ref, xa_ref,
                    lse_ref, *refs):
    dq_ref, dk_ref, dv_ref = refs[-3:]
    k_pair, values = stacked(kn_ref, ka_ref), stacked(vn_ref, va_ref)
    keys = jnp.concatenate([k_pair, stacked(xn_ref, xa_ref)], axis=1)
    q_pair, grads = q_ref[...], do_ref[...]
    lanes = head_lanes(q_pair.shape, 0)
    product = grads.astype(F32) * o_ref[...].astype(F32)
    dq = jnp.zeros(q_pair.shape, F32)
    dk = jnp.zeros(k_pair.shape, F32)
    dv = jnp.zeros(k_pair.shape, F32)
    for h in range(2):
        mine = lanes if h == 0 else jnp.logical_not(lanes)
        q_head = jnp.where(mine, q_pair, 0)
        g_head = jnp.where(mine, grads, 0)
        dot_row = jnp.transpose(jnp.sum(jnp.where(mine, product, 0.0), axis=1, keepdims=True))
        scores = mm(keys, jnp.concatenate([q_head, qx_ref[...]], axis=1), NT)
        prob = jnp.exp(scores - lse_ref[0, h : h + 1, :])
        dv += mm(prob.astype(BF16), g_head)
        grad_prob = mm(values, g_head, NT)
        grad_scores = (prob * (grad_prob - dot_row)).astype(BF16)
        dk += mm(grad_scores, q_head)
        part = mm(grad_scores, k_pair, TN)
        dq += jnp.where(mine, part, 0.0)
    dq_ref[...] = dq.astype(BF16) * jnp.asarray(0.125, BF16)
    dk_ref[...] = dk.astype(BF16)
    dv_ref[...] = dv.astype(BF16)


def attend_backward(operands, first, pairs, gates):
    by_pair = pl.BlockSpec((2 * N, 128), lambda p: (0, first + p))
    sizes = (2 * N, 4 * N, 4 * N)
    return pl.pallas_call(
        backward_kernel,
        grid=(pairs,),
        in_specs=[by_pair] * 7 + [FIXED] * 3
        + [pl.BlockSpec((1, 2, 2 * N), lambda p: (first + p, 0, 0))]
        + [pl.BlockSpec(memory_space=pl.ANY)] * len(gates),
        out_specs=[pl.BlockSpec((size, 128), lambda p: (0, p)) for size in sizes],
        out_shape=[jax.ShapeDtypeStruct((size, pairs * 128), BF16) for size in sizes],
        compiler_params=pltpu.CompilerParams(vmem_limit_bytes=44 * 2**20),
        cost_estimate=pl.CostEstimate(
            flops=2 * 5 * 2 * pairs * 512 * 1024 * 256, bytes_accessed=6 * 2**20,
            transcendentals=2 * pairs * 512 * 1024),
        name="attend_backward",
    )(*operands, *gates)


FF_STEP = 512


def expert_kernel(at_ref, at_slot, att_own_ref, att_sib_ref, own_ref, sib_ref, cot_own_ref,
                  cot_sib_ref, marks_ref, gain_ref, shift_ref, w_out_ref, wu_ref, wd_ref,
                  out_ref, out_sib_ref, grad_ref, grad_low_ref, xhat_ref, factor_ref, *refs):
    keeps, sends = refs[:3], refs[3:6]
    up_acc, down_acc, act_acc, branch_ref = refs[6:]
    f = pl.program_id(0)
    core = at_ref[0]

    @pl.when(f == 0)
    def _():
        mine = w_out_ref[pl.ds(pl.multiple_of(core * 384, 384), 384), :]
        other = w_out_ref[pl.ds(pl.multiple_of((1 - core) * 384, 384), 384), :]
        for n, ext_ref in enumerate((own_ref, sib_ref)):
            rows, theirs = slice(n * N, (n + 1) * N), slice((1 - n) * N, (2 - n) * N)
            hidden = ext_ref[:N, :].astype(F32) + (
                mm(att_own_ref[rows, :], mine) + mm(att_sib_ref[theirs, :], other))
            xhat, factor = normalize(hidden)
            xhat_ref[rows, :] = xhat
            factor_ref[rows, :] = factor
            act_acc[rows, :] = (xhat * gain_ref[...] + shift_ref[...]).astype(BF16)
            if n == 0:
                branch_ref[rows, :] = hidden
            else:
                branch_ref[rows, :] = jnp.zeros_like(hidden)
        grad_ref[...] = jnp.zeros(grad_ref.shape, F32)

    act = act_acc[...]
    cot = jnp.concatenate([cot_own_ref[...], cot_sib_ref[...]], axis=0)
    text = marks_ref[:, 8:9].astype(F32) > 0.0
    pre = jnp.where(text, mm(act, wu_ref[1]), mm(act, wu_ref[0]))
    inner, slope = gelu_parts(pre)
    grad_pre = jnp.where(text, mm(cot, wd_ref[1], NT), mm(cot, wd_ref[0], NT)) * slope
    branch = jnp.zeros(branch_ref.shape, F32)
    grad = jnp.zeros(branch_ref.shape, F32)
    for e in range(2):
        mine = text if e == 1 else jnp.logical_not(text)
        inner_e = jnp.where(mine, inner, 0.0).astype(BF16)
        grad_e = jnp.where(mine, grad_pre, 0.0).astype(BF16)
        branch += mm(inner_e, wd_ref[e])
        grad += mm(grad_e, wu_ref[e], NT)
        up = mm(act, grad_e, TN)
        up_acc[e, 0] = up[:, :256]
        up_acc[e, 1] = up[:, 256:]
        down_acc[e, pl.ds(pl.multiple_of(f * FF_STEP, FF_STEP), FF_STEP), :] = mm(inner_e, cot, TN)

    branch_ref[...] += branch
    grad_ref[...] += grad

    def spill(target, g, base, up_part):
        def cell(i, carry):
            slot = g * 64 + base + i
            if up_part:
                rows = pl.ds(pl.multiple_of(at_slot[slot], 8), 24)
                half = at_slot[192 + slot]
                both = jnp.concatenate([up_acc[0, half, rows, :], up_acc[1, half, rows, :]], axis=0)
                target[i, :48, :] = both.astype(BF16)
            else:
                rows = pl.ds(pl.multiple_of(at_slot[384 + slot], 8), 24)
                lanes = slice(g * 256, (g + 1) * 256)
                both = jnp.concatenate([down_acc[0, rows, lanes], down_acc[1, rows, lanes]], axis=0)
                target[i, 48:, :] = both.astype(BF16)
            return carry
        lax.fori_loop(0, 32, cell, 0, unroll=4)

    for g in range(3):
        @pl.when(f == g)
        def _():
            spill(keeps[g], g, 0, True)
            spill(sends[g], g, 32, True)

    @pl.when(f == 2)
    def _():
        out_ref[...] = branch_ref[:N, :]
        out_sib_ref[...] = branch_ref[N:, :].astype(BF16)
        grad_low_ref[...] = grad_ref[...].astype(BF16)
        for g in range(3):
            spill(keeps[g], g, 0, False)
            spill(sends[g], g, 32, False)


def experts(core, table, *operands):
    steps = 3
    shapes = [((N, 768), F32), ((N, 768), BF16), ((2 * N, 768), F32), ((2 * N, 768), BF16),
              ((2 * N, 768), F32), ((2 * N, 1), F32)] + [((32, 96, 256), BF16)] * 6
    fixed = lambda shape: pl.BlockSpec(shape, lambda f, *_: (0,) * len(shape))
    return pl.pallas_call(
        expert_kernel,
        grid_spec=pltpu.PrefetchScalarGridSpec(
            num_scalar_prefetch=2,
            grid=(steps,),
            in_specs=[fixed(v.shape) for v in operands[:-2]] + [
                pl.BlockSpec((2, 768, FF_STEP), lambda f, at, *_: (0, 0, at[0] * steps + f)),
                pl.BlockSpec((2, FF_STEP, 768), lambda f, at, *_: (0, at[0] * steps + f, 0)),
            ],
            out_specs=[fixed(shape) for shape, _ in shapes],
            scratch_shapes=[
                pltpu.VMEM((2, 2, 768, 256), F32),
                pltpu.VMEM((2, steps * FF_STEP, 768), F32),
                pltpu.VMEM((2 * N, 768), BF16),
                pltpu.VMEM((2 * N, 768), F32),
            ],
        ),
        out_shape=[jax.ShapeDtypeStruct(*v) for v in shapes],
        compiler_params=pltpu.CompilerParams(
            vmem_limit_bytes=62 * 2**20, dimension_semantics=("arbitrary",)),
        cost_estimate=pl.CostEstimate(
            flops=12 * 2 * 512 * 768 * 1536 + 2 * 512 * 768 * 768, bytes_accessed=30 * 2**20,
            transcendentals=2 * 512 * 1536),
        name="experts",
    )(core, table, *operands)


def cell_places():
    table = np.zeros((32, 4, 3, 3, 4, 4, 4), np.int32)
    for r, s in np.ndindex(32, 4):
        here = {"z": r // 8, "y": r % 4, "x": (s // 2) * 2 + (r // 4) % 2}
        flips = (0, 1, 3, 2) if s % 2 else (0, 3, 1, 2)
        for g, order in enumerate(ORDERS):
            for slot in np.ndindex(4, 4, 4):
                at = {a: here[a] ^ flips[n] for a, n in zip(order, slot)}
                x_hi, x_lo = at["x"] // 2, at["x"] % 2
                table[(r, s, 0, g) + slot] = 24 * (at["z"] * 8 + x_lo * 4 + at["y"])
                table[(r, s, 1, g) + slot] = x_hi
                table[(r, s, 2, g) + slot] = 24 * (
                    (at["z"] % 2) * 32 + x_lo * 16 + at["y"] * 4 + x_hi * 2 + at["z"] // 2)
    return table.reshape(128, 576)


def add_up(parts):
    total = parts[0].astype(F32)
    for part in parts[1:]:
        total = total + part.astype(F32)
    return total.astype(BF16)


def pass_kernel(gates, *refs):
    count = (len(refs) - gates) // 3
    for g in range(count):
        refs[2 * count + gates + g][...] = add_up([refs[2 * g][...], refs[2 * g + 1][...]])


ANYWHERE = pl.BlockSpec(memory_space=pl.ANY)


def pass_on(kept, arrived, name, limit, gates=()):
    _, slots, rows, lanes = kept[0].shape
    block = max(slots // 4, 1)
    one = pl.BlockSpec((None, block, rows, lanes), lambda i: (1, i, 0, 0))
    return pl.pallas_call(
        lambda *refs: pass_kernel(len(gates), *refs),
        grid=(slots // block,),
        in_specs=[one] * (2 * len(kept)) + [ANYWHERE] * len(gates),
        out_specs=[pl.BlockSpec((block, rows, lanes), lambda i: (i, 0, 0))] * len(kept),
        out_shape=[jax.ShapeDtypeStruct((slots, rows, lanes), BF16)] * len(kept),
        compiler_params=pltpu.CompilerParams(vmem_limit_bytes=limit * 2**20),
        cost_estimate=pl.CostEstimate(
            flops=0, transcendentals=0, bytes_accessed=6 * len(kept) * slots * rows * lanes),
        name=name,
    )(*[v for pair in zip(kept, arrived) for v in pair], *gates)


def settle_kernel(groups, *refs):
    ins, outs = refs, refs[-2 * groups :]
    for n in range(2 * groups):
        outs[n][...] = add_up([ins[3 * n + k][...] for k in range(3)])


def settle(pieces, name, limit, gates=()):
    groups = len(pieces)
    _, slots, rows, lanes = pieces[0][0].shape
    half = slots // 2
    block = max(half // 4, 1)
    steps = half // block
    operands, specs = [], []
    for piece in pieces:
        for h in range(2):
            wide = pl.BlockSpec((None, block, rows, lanes), lambda i, h=h: (0, i + h * steps, 0, 0))
            flat = pl.BlockSpec((block, rows, lanes), lambda i, h=h: (i + h * steps, 0, 0))
            operands += list(piece)
            specs += [wide, wide, flat]
    outs = pl.pallas_call(
        lambda *refs: settle_kernel(groups, *refs),
        grid=(steps,),
        in_specs=specs + [ANYWHERE] * len(gates),
        out_specs=[pl.BlockSpec((block, rows, lanes), lambda i: (i, 0, 0))] * (2 * groups),
        out_shape=[jax.ShapeDtypeStruct((half, rows, lanes), BF16)] * (2 * groups),
        compiler_params=pltpu.CompilerParams(vmem_limit_bytes=limit * 2**20),
        cost_estimate=pl.CostEstimate(
            flops=0, transcendentals=0, bytes_accessed=8 * groups * slots * rows * lanes),
        name=name,
    )(*operands, *gates)
    shaped = [o.reshape(2, half // 2, rows, lanes) for o in outs]
    return shaped[0::2], shaped[1::2]


def finish_kernel(*refs):
    up_ref, down_ref = refs[-2:]
    for g in range(3):
        cell = add_up([refs[3 * g + k][...] for k in range(3)])
        up_ref[g] = cell[:48]
        down_ref[g] = cell[48:]


def finish(kept, first, second):
    wide = pl.BlockSpec((None, None, 96, 256), lambda i: (0, 0, 0, 0))
    flat = pl.BlockSpec((None, 96, 256), lambda i: (0, 0, 0))
    return pl.pallas_call(
        finish_kernel,
        grid=(1,),
        in_specs=[wide, wide, flat] * 3,
        out_specs=[pl.BlockSpec((3, 48, 256), lambda i: (0, 0, 0))] * 2,
        out_shape=[jax.ShapeDtypeStruct((3, 48, 256), BF16)] * 2,
        name="finish",
    )(*[v for g in range(3) for v in (kept[g], first[g], second[g])])


def after_kernel(values_ref, *refs):
    refs[-1][...] = values_ref[...]


def after(values, gates):
    return pl.pallas_call(
        after_kernel,
        in_specs=[WHOLE] + [ANYWHERE] * len(gates),
        out_specs=WHOLE,
        out_shape=jax.ShapeDtypeStruct(values.shape, values.dtype),
        name="after",
    )(values, *gates)


def tail_kernel(place, act_ref, away_ref, q_ref, qb_ref, ka_ref, kb_ref, va_ref, vb_ref,
                att_own_ref, att_sib_ref, proj_ref, own_ref, sib_ref, far_ref, far_sib_ref, vec_ref,
                wq_ref, wk_ref, wv_ref, *refs):
    keep_ref, send_ref, rows_ref, acc, table = refs[-5:]
    core = place[0]

    def put(first, part, rows=slice(None)):
        acc[rows, first : first + part.shape[1]] = part

    act, away = act_ref[...], away_ref[...]
    first = 0
    for ref in (q_ref, qb_ref):
        put(first, mm(act, ref[...], TN))
        first += ref.shape[1]
    for ref in (ka_ref, kb_ref, va_ref, vb_ref):
        put(first, mm(act, ref[: 2 * N, :], TN) + mm(away, ref[2 * N :, :], TN))
        first += ref.shape[1]
    mine = pl.ds(pl.multiple_of(core * 384, 384), 384)
    other = pl.ds(pl.multiple_of((1 - core) * 384, 384), 384)
    put(1152, mm(att_own_ref[...], proj_ref[...], TN), mine)
    put(1152, mm(att_sib_ref[:N, :], proj_ref[N:, :], TN)
        + mm(att_sib_ref[N:, :], proj_ref[:N, :], TN), other)

    vectors = [jnp.zeros((1, 768), F32), jnp.zeros((1, 768), F32), vec_ref[0:1, :], vec_ref[1:2, :]]
    wide = ((q_ref, qb_ref, wq_ref), (ka_ref, kb_ref, wk_ref), (va_ref, vb_ref, wv_ref))
    for n, ext_ref in enumerate((own_ref, sib_ref, far_ref, far_sib_ref)):
        rows = slice(n * N, (n + 1) * N)
        total = jnp.zeros((N, 768), F32)
        for a_ref, b_ref, w_ref in wide[0 if n < 2 else 1 :]:
            total += mm(a_ref[rows, :], w_ref[:, :256], NT) + mm(b_ref[rows, :], w_ref[:, 256:], NT)
        xhat, _ = normalize(ext_ref[:N, :].astype(F32))
        vectors[0] += jnp.sum(total * xhat, axis=0, keepdims=True)
        vectors[1] += jnp.sum(total, axis=0, keepdims=True)
        half = slice((n // 2) * N, (n // 2 + 1) * N)
        if n % 2 == 0:
            keep_ref[half, :] = total
        else:
            send_ref[half, :] = total.astype(BF16)

    chip = lax.broadcasted_iota(jnp.int32, (64, 768), 0)
    owner = lax.broadcasted_iota(jnp.int32, (64, 768), 1) // 12
    feature = lax.broadcasted_iota(jnp.int32, (768, 128), 0) % 12
    lane = lax.broadcasted_iota(jnp.int32, (768, 128), 1)
    spread = jnp.zeros((64, 128), F32)
    for n in range(4):
        values = jnp.where(chip == owner, jnp.broadcast_to(vectors[n], (64, 768)), 0.0).astype(BF16)
        spread += mm(values, jnp.where(lane == feature + 12 * n, 1.0, 0.0).astype(BF16))
    table[...] = spread

    upper = lax.broadcasted_iota(jnp.int32, (8, 768), 0) < 4

    def unit(u, carry):
        top, mid, low = (
            acc[pl.ds(pl.multiple_of(24 * u + 8 * n, 8), 8), :] for n in range(3))
        turned = pltpu.roll(mid, 4, 0)
        first = jnp.where(upper, mid[:, :768], turned[:, 768:])
        second = jnp.where(upper, turned[:, :768], mid[:, 768:])
        lines = [jnp.broadcast_to(table[pl.ds(2 * u + n, 1), :], (8, 128)) for n in range(2)]
        both = jnp.concatenate([
            jnp.concatenate([top, first, lines[0]], axis=1),
            jnp.concatenate([low, second, lines[1]], axis=1)], axis=0)
        rows_ref[pl.ds(pl.multiple_of(16 * u, 16), 16), :] = both.astype(BF16)
        return carry

    lax.fori_loop(0, 32, unit, 0, unroll=2)


def tail_rows(core, operands, gates):
    whole = lambda shape: pl.BlockSpec(shape, lambda i, *_: (0,) * len(shape))
    shapes = [((2 * N, 768), F32), ((2 * N, 768), BF16), ((512, 2432), BF16)]
    return pl.pallas_call(
        tail_kernel,
        grid_spec=pltpu.PrefetchScalarGridSpec(
            num_scalar_prefetch=1,
            grid=(1,),
            in_specs=[whole(v.shape) for v in operands[:-1]]
            + [pl.BlockSpec((768, 384), lambda i, at, n=n: (0, 2 * n + at[0])) for n in range(3)]
            + [ANYWHERE] * len(gates),
            out_specs=[whole(shape) for shape, _ in shapes],
            scratch_shapes=[pltpu.VMEM((768, 1536), F32), pltpu.VMEM((64, 128), F32)],
        ),
        out_shape=[jax.ShapeDtypeStruct(*v) for v in shapes],
        compiler_params=pltpu.CompilerParams(vmem_limit_bytes=36 * 2**20),
        cost_estimate=pl.CostEstimate(
            flops=2 * 768 * 384 * 512 * 11, bytes_accessed=14 * 2**20, transcendentals=0),
        name="tail_rows",
    )(core, *operands, *[operands[-1]] * 2, *gates)


def total_kernel(parts_ref, *refs):
    out_ref, acc = refs[-2:]
    i = pl.program_id(0)
    part = jnp.sum(parts_ref[...].astype(F32), axis=0)

    @pl.when(i == 0)
    def _():
        acc[...] = part

    @pl.when(i > 0)
    def _():
        acc[...] += part

    @pl.when(i == pl.num_programs(0) - 1)
    def _():
        out_ref[...] = acc[...].astype(BF16)


def total(parts, gates):
    count, rows, lanes = parts.shape
    return pl.pallas_call(
        total_kernel,
        grid=(4,),
        in_specs=[pl.BlockSpec((count // 4, rows, lanes), lambda i: (i, 0, 0))]
        + [ANYWHERE] * len(gates),
        out_specs=pl.BlockSpec((rows, lanes), lambda i: (0, 0)),
        out_shape=jax.ShapeDtypeStruct((rows, lanes), BF16),
        scratch_shapes=[pltpu.VMEM((rows, lanes), F32)],
        compiler_params=pltpu.CompilerParams(vmem_limit_bytes=24 * 2**20),
        name="total",
    )(parts, *gates)


def rows_kernel(place, own_ref, sib_ref, qkv_ref, out_ref, vec_ref):
    core, far = place[0], place[1]
    line = own_ref[:, 2304:].astype(F32) + sib_ref[:, 2304:].astype(F32)
    vec_ref[...] = jnp.where(core == 0, line, pltpu.roll(line, 122, 1))
    row = lax.broadcasted_iota(jnp.int32, (8, 8), 0)
    column = lax.broadcasted_iota(jnp.int32, (8, 8), 1)
    wanted = row + 6 * core - 4 * far
    valid = row < 6
    main = jnp.where((column == wanted) & valid, 1.0, 0.0).astype(BF16)
    rest = wanted + 12 * far - 8
    valid = valid & (rest >= 0) & (rest < 4)
    extra = [jnp.where((column == rest + 4 * n) & valid, 1.0, 0.0).astype(BF16) for n in range(2)]
    for c in range(2):
        part = jnp.where(core == c, own_ref[...], sib_ref[...])
        rows = mm(main, part[:, :1536]) + jnp.concatenate(
            [mm(extra[n], part[:, 1536:2304]) for n in range(2)], axis=1)
        for kind in range(3):
            at = kind * 768 + c * 384
            qkv_ref[:, at : at + 384] = rows[:6, kind * 384 : (kind + 1) * 384]
        out_ref[:, c * 384 : (c + 1) * 384] = rows[:6, 1152:]


def own_rows(place, own, sib):
    return pl.pallas_call(
        rows_kernel,
        in_specs=[SMALL, WHOLE, WHOLE],
        out_specs=[WHOLE] * 3,
        out_shape=[
            jax.ShapeDtypeStruct((6, 2304), F32),
            jax.ShapeDtypeStruct((6, 768), F32),
            jax.ShapeDtypeStruct((8, 128), F32),
        ],
        name="own_rows",
    )(place, own, sib)


def assemble_kernel(place, own_ref, near_ref, away_ref, cross_ref, up_ref, held):
    core, far = place[0], place[1]
    held[far * 2 + core] = own_ref[...]
    held[far * 2 + 1 - core] = near_ref[...]
    held[2 - far * 2 + core] = away_ref[...]
    held[2 - far * 2 + 1 - core] = cross_ref[...]
    row = lax.broadcasted_iota(jnp.int32, (16, 48), 0)
    column = lax.broadcasted_iota(jnp.int32, (16, 48), 1)
    wanted = (row // 8) * 24 + far * 12 + core * 6 + row % 8
    select = jnp.where((column == wanted) & (row % 8 < 6), 1.0, 0.0).astype(BF16)
    for x_hi in range(2):
        for c in range(2):
            for g in range(3):
                rows = mm(select, held[x_hi * 2 + c, g])
                first = c * 1536 + g * 512 + x_hi * 256
                for e in range(2):
                    up_ref[e, :, first : first + 256] = rows[8 * e : 8 * e + 6] * UP_FACTORS[e]


def assemble(place, *parts):
    return pl.pallas_call(
        assemble_kernel,
        in_specs=[SMALL] + [WHOLE] * 4,
        out_specs=WHOLE,
        out_shape=jax.ShapeDtypeStruct((2, 6, 3072), F32),
        scratch_shapes=[pltpu.VMEM((4, 3, 48, 256), BF16)],
        name="assemble",
    )(place, *parts)


def shards(tokens, first_gain, first_shift, w_qkv, w_out, second_gain, second_shift,
           w_up, w_down, modality, segments, partner, cotangent):
    row_index, seq_index = lax.axis_index("rows"), lax.axis_index("seq")
    core, far = seq_index % 2, seq_index // 2
    place = jnp.stack([core, far]).astype(jnp.int32)
    table = lax.dynamic_index_in_dim(
        jnp.asarray(cell_places()), row_index * 4 + seq_index, 0, keepdims=False)
    gain1, shift1, gain2, shift2 = (
        v.reshape(1, 768) for v in (first_gain, first_shift, second_gain, second_shift))

    own = marked(partner, tokens[0], segments, modality)
    away = swap_far(own)
    sib = swap_core(own)
    cot_own = cotangent[0]
    cot_sib = swap_core(cot_own)

    act1, marks, queries, k_near, v_near, qx = project(place, own, sib, gain1, shift1, w_qkv, True)
    away_sib = swap_core(after(away, [qx]))
    act1_away, marks_away, k_away, v_away = project(
        place, away, away_sib, gain1, shift1, w_qkv, False)
    attended, lse = attend_forward(
        queries, k_near, k_away, v_near, v_away, qx, marks, marks_away)
    attended_sib = swap_core(attended)

    outcome = experts(
        place, table, attended, attended_sib, own, sib, cot_own, cot_sib, marks, gain2, shift2,
        w_out, w_up, w_down)
    out_own, out_sib, grad_act2, grad_low, xhat2, factor2 = outcome[:6]
    outcome = outcome[4:]
    ff_kept = [v.reshape(2, 16, 96, 256) for v in outcome[2:5]]
    ff_first = [send(v.reshape(2, 16, 96, 256), axis_step(ORDERS[g][0], True))
                for g, v in enumerate(outcome[5:8])]
    grad_sib = swap_core(grad_low)
    hidden_grad, grad_att, proj_half, vectors = middle(
        place, grad_act2, grad_sib, xhat2, factor2, cot_own, cot_sib, gain2, w_out)

    def along(stage, first, values):
        return [send(v, axis_step(ORDERS[g][stage], first)) for g, v in enumerate(values)]

    taken = (queries, k_near, k_away, v_near, v_away, grad_att, attended, qx, marks, marks_away, lse)
    passed = pass_on(ff_kept, ff_first, "pass_first", 60, [vectors])
    ff_second = along(0, False, passed)
    q_a, k_a, v_a = attend_backward(taken, 0, 2, passed)
    kept, sent = settle(list(zip(ff_kept, ff_first, ff_second)), "settle_first", 60, [q_a])
    first = along(1, True, sent)
    q_b, k_b, v_b = attend_backward(taken, 2, 1, sent)
    passed = pass_on(kept, first, "pass_second", 24)
    second = along(1, False, passed)
    partial_own, partial_sib, tail = tail_rows(
        place, (act1, act1_away, q_a, q_b, k_a, k_b, v_a, v_b, attended, attended_sib,
                proj_half, own, sib, away, away_sib, vectors, w_qkv), passed)
    same_core = [list(range(c, 128, 2)) for c in range(2)]
    moved = lax.all_to_all(tail.reshape(64, 8, 2432), BOTH, 0, 0, tiled=True,
                           axis_index_groups=same_core)
    kept, sent = settle(list(zip(kept, first, second)), "settle_second", 24)
    first = along(2, True, sent)
    second = along(2, False, pass_on(kept, first, "pass_third", 24))
    up_held, down_held = finish(kept, first, second)

    partial = partial_own + swap_core(partial_sib).astype(F32)
    grad_act1 = partial[:N] + swap_far(partial[N:].astype(BF16)).astype(F32)
    xhat1, factor1 = normalize(tokens[0].astype(F32))
    token_grad = hidden_grad + normalize_back(grad_act1, xhat1, factor1, first_gain)
    layer_output = (out_own + swap_core(out_sib).astype(F32)).astype(BF16)

    near, beyond = swap_core(up_held), swap_far(up_held)
    cross = send(up_held, lambda x, y, z, c: (x ^ 2, y, z, 1 - c))
    up_grad = assemble(place, up_held, near, beyond, cross)
    summed = total(moved, ())
    qkv_grad, out_grad, line = own_rows(place, summed, swap_core(summed))

    down_rows = send(down_held, lambda x, y, z, c: (x, y, 2 * c + z % 2, z // 2)).astype(F32)
    down_rows = down_rows.reshape(3, 2, 24, 256).transpose(1, 2, 0, 3).reshape(2, 24, 768)
    factors = jnp.asarray(UP_FACTORS, F32)[:, None, None]
    return (
        layer_output[None], token_grad[None], line[0, :6], line[0, 12:18], qkv_grad, out_grad,
        line[0, 24:30], line[0, 36:42], up_grad, down_rows * factors)


def solution(mesh):
    cut = P("rows", "seq", None)
    flat = P(BOTH)
    placed = (cut,) + (P(),) * 8 + (P("rows", "seq"), P("rows", "seq"), P("rows", None), cut)
    return jax.shard_map(
        shards, mesh=mesh, in_specs=placed,
        out_specs=(cut, cut, flat, flat, P(BOTH, None), P(BOTH, None), flat, flat,
                   P(None, BOTH, None), P(None, BOTH, None)),
        check_vma=False)
```

```python
import jax
import jax.numpy as jnp
import numpy as np
from jax import lax
from jax.experimental import pallas as pl
from jax.experimental.pallas import tpu as pltpu
from jax.sharding import PartitionSpec as P

HD = 64
OWN = 6
IMG = 197
NIMG = 4
BOTH = ("rows", "seq")
F32 = jnp.float32
BF16 = jnp.bfloat16
MASKED = -1e30


def route(step):
    pairs = []
    for r in range(32):
        z, x_lo, y = r // 8, (r // 4) % 2, r % 4
        for s in range(4):
            x, c = (s // 2) * 2 + x_lo, s % 2
            tx, ty, tz, tc = step(x, y, z, c)
            target = (tz * 8 + (tx % 2) * 4 + ty) * 4 + (tx // 2) * 2 + tc
            pairs.append((r * 4 + s, target))
    return pairs


def send(values, step):
    return lax.ppermute(values, BOTH, route(step))


def swap_core(values):
    return send(values, lambda x, y, z, c: (x, y, z, 1 - c))


def swap_far(values):
    return send(values, lambda x, y, z, c: (x ^ 2, y, z, c))


def axis_step(axis, first):
    def step(x, y, z, c):
        flip = 1 if (c == 0) == first else 3
        at = {"x": x, "y": y, "z": z}
        at[axis] ^= flip
        return (at["x"], at["y"], at["z"], c)

    return step


UP_FACTORS = (1024 / (2 * 788), 1024 / (2 * 236))
ORDERS = (("x", "y", "z"), ("y", "z", "x"), ("z", "x", "y"))


def normalize(inputs):
    centred = inputs - jnp.mean(inputs, axis=-1, keepdims=True)
    factor = lax.rsqrt(jnp.mean(centred * centred, axis=-1, keepdims=True) + 1e-05)
    return centred * factor, factor


def normalize_back(grad, xhat, factor, gain):
    gy = grad * gain
    mean_gy = jnp.mean(gy, axis=-1, keepdims=True)
    mean_gx = jnp.mean(gy * xhat, axis=-1, keepdims=True)
    return factor * (gy - mean_gy - xhat * mean_gx)


SMALL = pl.BlockSpec(memory_space=pltpu.SMEM)
WHOLE = pl.BlockSpec(memory_space=pltpu.VMEM)
N = 256


def marked_kernel(partner, tokens_ref, segments_ref, modality_ref, out_ref):
    segments = segments_ref[...]
    tag = jnp.zeros(segments.shape, jnp.int32)
    for n in range(8):
        tag = jnp.where(segments == n, partner[0, n], tag)
    marks = jnp.concatenate(
        [tag, modality_ref[...], jnp.zeros((1, 256), jnp.int32)], axis=1).astype(F32)
    out_ref[:N, :] = tokens_ref[...]
    out_ref[N:, :] = jnp.concatenate([marks, jnp.zeros((15, 768), F32)], axis=0).astype(BF16)


def marked(partner, tokens, segments, modality):
    return pl.pallas_call(
        marked_kernel,
        in_specs=[SMALL, WHOLE, WHOLE, WHOLE],
        out_specs=WHOLE,
        out_shape=jax.ShapeDtypeStruct((N + 16, 768), BF16),
        name="marked",
    )(partner, tokens, segments, modality)


def mark_lanes(ext):
    row = ext[N:, :].astype(F32)
    place = lax.broadcasted_iota(jnp.int32, (128, N), 0)
    tag = jnp.broadcast_to(row[:1, :N], (128, N))
    kind = jnp.broadcast_to(row[:1, N : 2 * N], (128, N))
    hot = jnp.where((place < NIMG) & (place.astype(F32) == tag), 1.0, 0.0)
    return jnp.transpose(jnp.where(place == 8, kind, hot))


def project_kernel(at_ref, near, a_ref, b_ref, gain_ref, shift_ref, *refs):
    count = 3 if near else 2
    weights, outs = refs[:count], refs[count:]
    for n, ext_ref in enumerate((a_ref, b_ref)):
        rows = slice(n * N, (n + 1) * N)
        ext = ext_ref[...]
        xhat, _ = normalize(ext[:N].astype(F32))
        act = (xhat * gain_ref[...] + shift_ref[...]).astype(BF16)
        outs[0][rows, :] = act
        marks = mark_lanes(ext)
        outs[1][rows, :] = marks.astype(BF16)
        for m in range(count):
            part = mm(act, weights[m][...])
            outs[2 + m][rows, :] = (0.125 * part if near and m == 0 else part).astype(BF16)
        if near:
            lane = lax.broadcasted_iota(jnp.int32, marks.shape, 1)
            outs[5][rows, :] = jnp.where((lane < NIMG) & (marks == 0.0), MASKED, 0.0).astype(BF16)


def project(core, first, second, gain, shift, w_qkv, near):
    kinds = (0, 1, 2) if near else (1, 2)
    sizes = [768, 128] + [384] * len(kinds) + ([128] if near else [])
    whole = lambda shape: pl.BlockSpec(shape, lambda i, at: (0, 0))
    return pl.pallas_call(
        lambda at_ref, *refs: project_kernel(at_ref, near, *refs),
        grid_spec=pltpu.PrefetchScalarGridSpec(
            num_scalar_prefetch=1,
            grid=(1,),
            in_specs=[whole((N + 16, 768))] * 2 + [whole((1, 768))] * 2
            + [pl.BlockSpec((768, 384), lambda i, at, n=n: (0, 2 * n + at[0])) for n in kinds],
            out_specs=[whole((2 * N, size)) for size in sizes],
        ),
        out_shape=[jax.ShapeDtypeStruct((2 * N, size), BF16) for size in sizes],
        compiler_params=pltpu.CompilerParams(vmem_limit_bytes=14 * 2**20),
        cost_estimate=pl.CostEstimate(
            flops=2 * 512 * 768 * 384 * len(kinds), bytes_accessed=4 * 2**20, transcendentals=0),
        name="project_near" if near else "project_away",
    )(core, first, second, gain, shift, *[w_qkv] * len(kinds))


def middle_kernel(place, grad_ref, sib_ref, xhat_ref, factor_ref, cot_own_ref, cot_sib_ref,
                  gain_ref, w_out_ref, hidden_ref, att_ref, proj_ref, vec_ref):
    core = place[0]
    for n, cot_ref in enumerate((cot_own_ref, cot_sib_ref)):
        rows, other = slice(n * N, (n + 1) * N), slice((1 - n) * N, (2 - n) * N)
        grad = grad_ref[rows, :] + sib_ref[other, :].astype(F32)
        xhat = xhat_ref[rows, :]
        total = cot_ref[...].astype(F32) + normalize_back(grad, xhat, factor_ref[rows, :], gain_ref[...])
        low = total.astype(BF16)
        if n == 0:
            hidden_ref[...] = total
            vec_ref[0:1, :] = jnp.sum(grad * xhat, axis=0, keepdims=True)
            vec_ref[1:2, :] = jnp.sum(grad, axis=0, keepdims=True)
        mine = w_out_ref[pl.ds(pl.multiple_of(core * 384, 384), 384), :]
        att_ref[rows, :] = mm(low, mine, NT).astype(BF16)
        proj_ref[rows, :] = jnp.where(core == 0, low[:, :384], low[:, 384:])


def middle(place, *operands):
    return pl.pallas_call(
        middle_kernel,
        in_specs=[SMALL] + [WHOLE] * len(operands),
        out_specs=[WHOLE] * 4,
        out_shape=[
            jax.ShapeDtypeStruct((N, 768), F32),
            jax.ShapeDtypeStruct((2 * N, 384), BF16),
            jax.ShapeDtypeStruct((2 * N, 384), BF16),
            jax.ShapeDtypeStruct((2, 768), F32),
        ],
        compiler_params=pltpu.CompilerParams(vmem_limit_bytes=14 * 2**20),
        cost_estimate=pl.CostEstimate(
            flops=2 * 512 * 768 * 384, bytes_accessed=8 * 2**20, transcendentals=0),
        name="middle",
    )(place, *operands)


def gelu_parts(pre):
    phi = 0.5 * (1.0 + lax.erf(pre * 0.7071067811865476))
    slope = phi + pre * (0.3989422804014327 * jnp.exp(-0.5 * pre * pre))
    return pre * phi, slope


NT = (((1,), (1,)), ((), ()))
TN = (((0,), (0,)), ((), ()))
NN = (((1,), (0,)), ((), ()))


def mm(left, right, dims=NN):
    return lax.dot_general(left, right, dims, preferred_element_type=F32)


def head_lanes(shape, h):
    lane = lax.broadcasted_iota(jnp.int32, shape, len(shape) - 1)
    return (lane >= HD) == (h == 1)


def stacked(near_ref, away_ref):
    return jnp.concatenate([near_ref[...], away_ref[...]], axis=0)


def forward_kernel(q_ref, kn_ref, ka_ref, vn_ref, va_ref, qx_ref, xn_ref, xa_ref, out_ref, lse_ref):
    keys = jnp.concatenate([stacked(kn_ref, ka_ref), stacked(xn_ref, xa_ref)], axis=1)
    values = stacked(vn_ref, va_ref)
    q_pair = q_ref[...]
    lanes = head_lanes(q_pair.shape, 0)
    mixed = []
    for h in range(2):
        mine = lanes if h == 0 else jnp.logical_not(lanes)
        query = jnp.concatenate([jnp.where(mine, q_pair, 0), qx_ref[...]], axis=1)
        scores = mm(keys, query, NT)
        peak = jnp.max(scores, axis=0, keepdims=True)
        weights = jnp.exp(scores - peak)
        total = jnp.sum(weights, axis=0, keepdims=True)
        inverse = 1.0 / total
        low = (weights * inverse).astype(BF16)
        mixed.append(mm(low, values, TN))
        lse_ref[0, h : h + 1, :] = peak + jnp.log(total)
    out_ref[...] = jnp.where(lanes, mixed[0], mixed[1]).astype(BF16)


BY_PAIR = pl.BlockSpec((2 * N, 128), lambda p: (0, p))
FIXED = pl.BlockSpec((2 * N, 128), lambda p: (0, 0))


def attend_forward(*operands):
    return pl.pallas_call(
        forward_kernel,
        grid=(3,),
        in_specs=[BY_PAIR] * 5 + [FIXED] * 3,
        out_specs=[BY_PAIR, pl.BlockSpec((1, 2, 2 * N), lambda p: (p, 0, 0))],
        out_shape=[
            jax.ShapeDtypeStruct((2 * N, 384), BF16),
            jax.ShapeDtypeStruct((3, 2, 2 * N), F32),
        ],
        compiler_params=pltpu.CompilerParams(vmem_limit_bytes=20 * 2**20),
        cost_estimate=pl.CostEstimate(
            flops=2 * 2 * OWN * 512 * 1024 * 256, bytes_accessed=4 * 2**20,
            transcendentals=OWN * 512 * 1024),
        name="attend_forward",
    )(*operands)


def backward_kernel(q_ref, kn_ref, ka_ref, vn_ref, va_ref, do_ref, o_ref, qx_ref, xn_ref, xa_ref,
                    lse_ref, *refs):
    dq_ref, dk_ref, dv_ref = refs[-3:]
    k_pair, values = stacked(kn_ref, ka_ref), stacked(vn_ref, va_ref)
    keys = jnp.concatenate([k_pair, stacked(xn_ref, xa_ref)], axis=1)
    q_pair, grads = q_ref[...], do_ref[...]
    lanes = head_lanes(q_pair.shape, 0)
    product = grads.astype(F32) * o_ref[...].astype(F32)
    dq = jnp.zeros(q_pair.shape, F32)
    dk = jnp.zeros(k_pair.shape, F32)
    dv = jnp.zeros(k_pair.shape, F32)
    for h in range(2):
        mine = lanes if h == 0 else jnp.logical_not(lanes)
        q_head = jnp.where(mine, q_pair, 0)
        g_head = jnp.where(mine, grads, 0)
        dot_row = jnp.transpose(jnp.sum(jnp.where(mine, product, 0.0), axis=1, keepdims=True))
        scores = mm(keys, jnp.concatenate([q_head, qx_ref[...]], axis=1), NT)
        prob = jnp.exp(scores - lse_ref[0, h : h + 1, :])
        dv += mm(prob.astype(BF16), g_head)
        grad_prob = mm(values, g_head, NT)
        grad_scores = (prob * (grad_prob - dot_row)).astype(BF16)
        dk += mm(grad_scores, q_head)
        part = mm(grad_scores, k_pair, TN)
        dq += jnp.where(mine, part, 0.0)
    dq_ref[...] = dq.astype(BF16) * jnp.asarray(0.125, BF16)
    dk_ref[...] = dk.astype(BF16)
    dv_ref[...] = dv.astype(BF16)


def attend_backward(operands, first, pairs, gates):
    by_pair = pl.BlockSpec((2 * N, 128), lambda p: (0, first + p))
    sizes = (2 * N, 4 * N, 4 * N)
    return pl.pallas_call(
        backward_kernel,
        grid=(pairs,),
        in_specs=[by_pair] * 7 + [FIXED] * 3
        + [pl.BlockSpec((1, 2, 2 * N), lambda p: (first + p, 0, 0))]
        + [pl.BlockSpec(memory_space=pl.ANY)] * len(gates),
        out_specs=[pl.BlockSpec((size, 128), lambda p: (0, p)) for size in sizes],
        out_shape=[jax.ShapeDtypeStruct((size, pairs * 128), BF16) for size in sizes],
        compiler_params=pltpu.CompilerParams(vmem_limit_bytes=20 * 2**20),
        cost_estimate=pl.CostEstimate(
            flops=2 * 5 * 2 * pairs * 512 * 1024 * 256, bytes_accessed=6 * 2**20,
            transcendentals=2 * pairs * 512 * 1024),
        name="attend_backward",
    )(*operands, *gates)


FF_STEP = 512
EXPERT_MB = 40
CELLS_MB = 28


def expert_kernel(at_ref, att_own_ref, att_sib_ref, own_ref, sib_ref, cot_own_ref, cot_sib_ref,
                  marks_ref, gain_ref, shift_ref, w_out_ref, wu_ref, wd_ref,
                  out_ref, out_sib_ref, grad_ref, grad_low_ref, xhat_ref, factor_ref, act_t_ref,
                  inner_t_ref, slope_ref, act_acc, branch_ref):
    f = pl.program_id(0)
    core = at_ref[0]

    @pl.when(f == 0)
    def _():
        mine = w_out_ref[pl.ds(pl.multiple_of(core * 384, 384), 384), :]
        other = w_out_ref[pl.ds(pl.multiple_of((1 - core) * 384, 384), 384), :]
        for n, ext_ref in enumerate((own_ref, sib_ref)):
            rows, theirs = slice(n * N, (n + 1) * N), slice((1 - n) * N, (2 - n) * N)
            hidden = ext_ref[:N, :].astype(F32) + (
                mm(att_own_ref[rows, :], mine) + mm(att_sib_ref[theirs, :], other))
            xhat, factor = normalize(hidden)
            xhat_ref[rows, :] = xhat
            factor_ref[rows, :] = factor
            act = xhat * gain_ref[...] + shift_ref[...]
            act_acc[rows, :] = act.astype(BF16)
            act_t_ref[:, rows] = jnp.transpose(act).astype(BF16)
            if n == 0:
                branch_ref[rows, :] = hidden
            else:
                branch_ref[rows, :] = jnp.zeros_like(hidden)
        grad_ref[...] = jnp.zeros(grad_ref.shape, F32)

    act = act_acc[...]
    cot = jnp.concatenate([cot_own_ref[...], cot_sib_ref[...]], axis=0)
    text = marks_ref[:, 8:9].astype(F32) > 0.0
    pre = jnp.where(text, mm(act, wu_ref[1]), mm(act, wu_ref[0]))
    inner, slope = gelu_parts(pre)
    grad_pre = jnp.where(text, mm(cot, wd_ref[1], NT), mm(cot, wd_ref[0], NT)) * slope
    for e in range(2):
        mine = text if e == 1 else jnp.logical_not(text)
        inner_e = jnp.where(mine, inner, 0.0)
        grad_e = jnp.where(mine, grad_pre, 0.0).astype(BF16)
        branch_ref[...] += mm(inner_e.astype(BF16), wd_ref[e])
        grad_ref[...] += mm(grad_e, wu_ref[e], NT)
        inner_t_ref[e] = jnp.transpose(inner_e).astype(BF16)
        slope_ref[e] = grad_e

    @pl.when(f == pl.num_programs(0) - 1)
    def _():
        out_ref[...] = branch_ref[:N, :]
        out_sib_ref[...] = branch_ref[N:, :].astype(BF16)
        grad_low_ref[...] = grad_ref[...].astype(BF16)


def experts(core, *operands):
    steps = 3
    shapes = [((N, 768), F32), ((N, 768), BF16), ((2 * N, 768), F32), ((2 * N, 768), BF16),
              ((2 * N, 768), F32), ((2 * N, 1), F32), ((768, 2 * N), BF16)]
    fixed = lambda shape: pl.BlockSpec(shape, lambda f, *_: (0,) * len(shape))
    return pl.pallas_call(
        expert_kernel,
        grid_spec=pltpu.PrefetchScalarGridSpec(
            num_scalar_prefetch=1,
            grid=(steps,),
            in_specs=[fixed(v.shape) for v in operands[:-2]] + [
                pl.BlockSpec((2, 768, FF_STEP), lambda f, at: (0, 0, at[0] * steps + f)),
                pl.BlockSpec((2, FF_STEP, 768), lambda f, at: (0, at[0] * steps + f, 0)),
            ],
            out_specs=[fixed(shape) for shape, _ in shapes] + [
                pl.BlockSpec((2, FF_STEP, 2 * N), lambda f, at: (0, f, 0)),
                pl.BlockSpec((2, 2 * N, FF_STEP), lambda f, at: (0, 0, f)),
            ],
            scratch_shapes=[pltpu.VMEM((2 * N, 768), BF16), pltpu.VMEM((2 * N, 768), F32)],
        ),
        out_shape=[jax.ShapeDtypeStruct(*v) for v in shapes] + [
            jax.ShapeDtypeStruct((2, steps * FF_STEP, 2 * N), BF16),
            jax.ShapeDtypeStruct((2, 2 * N, steps * FF_STEP), BF16)],
        compiler_params=pltpu.CompilerParams(
            vmem_limit_bytes=32 * 2**20, dimension_semantics=("arbitrary",)),
        cost_estimate=pl.CostEstimate(
            flops=8 * 2 * 512 * 768 * 1536 + 2 * 512 * 768 * 768, bytes_accessed=24 * 2**20,
            transcendentals=2 * 512 * 1536),
        name="experts",
    )(core, *operands)


def cells_kernel(g, at_slot, act_t_ref, grad_ref, inner_t_ref, cot_own_ref, cot_sib_ref, *refs):
    keep_ref, send_ref, up_acc, down_acc = refs[-4:]
    e = pl.program_id(0)
    up = mm(act_t_ref[...], grad_ref[...])
    up_acc[e, 0] = up[:, :256]
    up_acc[e, 1] = up[:, 256:]
    cot = jnp.concatenate([cot_own_ref[...], cot_sib_ref[...]], axis=0)
    down_acc[e] = mm(inner_t_ref[...], cot)

    def spill(target, base):
        def cell(i, carry):
            slot = g * 64 + base + i
            half = at_slot[192 + slot]
            rows = pl.ds(pl.multiple_of(at_slot[slot], 8), 24)
            below = pl.ds(pl.multiple_of(at_slot[384 + slot], 8), 24)
            target[i] = jnp.concatenate(
                [up_acc[0, half, rows, :], up_acc[1, half, rows, :],
                 down_acc[0, below, :], down_acc[1, below, :]], axis=0).astype(BF16)
            return carry
        lax.fori_loop(0, 32, cell, 0, unroll=4)

    @pl.when(e == 1)
    def _():
        spill(keep_ref, 0)
        spill(send_ref, 32)


def cells(g, table, act_t, grad_pre, inner_t, cot_own, cot_sib, gates):
    cot = pl.BlockSpec((N, 256), lambda e, t: (0, g))
    out = pl.BlockSpec((32, 96, 256), lambda e, t: (0, 0, 0))
    return pl.pallas_call(
        lambda *refs: cells_kernel(g, *refs),
        grid_spec=pltpu.PrefetchScalarGridSpec(
            num_scalar_prefetch=1,
            grid=(2,),
            in_specs=[
                pl.BlockSpec((768, 2 * N), lambda e, t: (0, 0)),
                pl.BlockSpec((None, 2 * N, FF_STEP), lambda e, t: (e, 0, g)),
                pl.BlockSpec((None, 1536, 2 * N), lambda e, t: (e, 0, 0)),
                cot, cot] + [ANYWHERE] * len(gates),
            out_specs=[out] * 2,
            scratch_shapes=[pltpu.VMEM((2, 2, 768, 256), F32), pltpu.VMEM((2, 1536, 256), F32)],
        ),
        out_shape=[jax.ShapeDtypeStruct((32, 96, 256), BF16)] * 2,
        compiler_params=pltpu.CompilerParams(
            vmem_limit_bytes=20 * 2**20, dimension_semantics=("arbitrary",)),
        cost_estimate=pl.CostEstimate(
            flops=4 * 2 * 512 * 768 * 512, bytes_accessed=8 * 2**20, transcendentals=0),
        name="cells",
    )(table, act_t, grad_pre, inner_t, cot_own, cot_sib, *gates)


def cell_places():
    table = np.zeros((32, 4, 3, 3, 4, 4, 4), np.int32)
    for r, s in np.ndindex(32, 4):
        here = {"z": r // 8, "y": r % 4, "x": (s // 2) * 2 + (r // 4) % 2}
        flips = (0, 1, 3, 2) if s % 2 else (0, 3, 1, 2)
        for g, order in enumerate(ORDERS):
            for slot in np.ndindex(4, 4, 4):
                at = {a: here[a] ^ flips[n] for a, n in zip(order, slot)}
                x_hi, x_lo = at["x"] // 2, at["x"] % 2
                table[(r, s, 0, g) + slot] = 24 * (at["z"] * 8 + x_lo * 4 + at["y"])
                table[(r, s, 1, g) + slot] = x_hi
                table[(r, s, 2, g) + slot] = 24 * (
                    (at["z"] % 2) * 32 + x_lo * 16 + at["y"] * 4 + x_hi * 2 + at["z"] // 2)
    return table.reshape(128, 576)


def add_up(parts):
    total = parts[0].astype(F32)
    for part in parts[1:]:
        total = total + part.astype(F32)
    return total.astype(BF16)


def in_hbm(values):
    return list(values)


def pass_kernel(gates, *refs):
    count = (len(refs) - gates) // 3
    for g in range(count):
        refs[2 * count + gates + g][...] = add_up([refs[2 * g][...], refs[2 * g + 1][...]])


ANYWHERE = pl.BlockSpec(memory_space=pl.ANY)


def pass_on(kept, arrived, name, limit, gates=()):
    _, slots, rows, lanes = kept[0].shape
    block = max(slots // 4, 1)
    one = pl.BlockSpec((None, block, rows, lanes), lambda i: (1, i, 0, 0))
    return pl.pallas_call(
        lambda *refs: pass_kernel(len(gates), *refs),
        grid=(slots // block,),
        in_specs=[one] * (2 * len(kept)) + [ANYWHERE] * len(gates),
        out_specs=[pl.BlockSpec((block, rows, lanes), lambda i: (i, 0, 0))] * len(kept),
        out_shape=[jax.ShapeDtypeStruct((slots, rows, lanes), BF16)] * len(kept),
        compiler_params=pltpu.CompilerParams(vmem_limit_bytes=12 * 2**20),
        cost_estimate=pl.CostEstimate(
            flops=0, transcendentals=0, bytes_accessed=6 * len(kept) * slots * rows * lanes),
        name=name,
    )(*in_hbm([v for pair in zip(kept, arrived) for v in pair]), *gates)


def settle_kernel(groups, *refs):
    ins, outs = refs, refs[-2 * groups :]
    for n in range(2 * groups):
        outs[n][...] = add_up([ins[3 * n + k][...] for k in range(3)])


def settle(pieces, name, limit, gates=()):
    groups = len(pieces)
    _, slots, rows, lanes = pieces[0][0].shape
    half = slots // 2
    block = max(half // 4, 1)
    steps = half // block
    operands, specs = [], []
    for piece in pieces:
        for h in range(2):
            wide = pl.BlockSpec((None, block, rows, lanes), lambda i, h=h: (0, i + h * steps, 0, 0))
            flat = pl.BlockSpec((block, rows, lanes), lambda i, h=h: (i + h * steps, 0, 0))
            operands += list(piece)
            specs += [wide, wide, flat]
    outs = pl.pallas_call(
        lambda *refs: settle_kernel(groups, *refs),
        grid=(steps,),
        in_specs=specs + [ANYWHERE] * len(gates),
        out_specs=[pl.BlockSpec((block, rows, lanes), lambda i: (i, 0, 0))] * (2 * groups),
        out_shape=[jax.ShapeDtypeStruct((half, rows, lanes), BF16)] * (2 * groups),
        compiler_params=pltpu.CompilerParams(vmem_limit_bytes=12 * 2**20),
        cost_estimate=pl.CostEstimate(
            flops=0, transcendentals=0, bytes_accessed=8 * groups * slots * rows * lanes),
        name=name,
    )(*in_hbm(operands), *gates)
    shaped = [o.reshape(2, half // 2, rows, lanes) for o in outs]
    return shaped[0::2], shaped[1::2]


def finish_kernel(*refs):
    up_ref, down_ref = refs[-2:]
    for g in range(3):
        cell = add_up([refs[3 * g + k][...] for k in range(3)])
        up_ref[g] = cell[:48]
        down_ref[g] = cell[48:]


def finish(kept, first, second):
    wide = pl.BlockSpec((None, None, 96, 256), lambda i: (0, 0, 0, 0))
    flat = pl.BlockSpec((None, 96, 256), lambda i: (0, 0, 0))
    return pl.pallas_call(
        finish_kernel,
        grid=(1,),
        in_specs=[wide, wide, flat] * 3,
        out_specs=[pl.BlockSpec((3, 48, 256), lambda i: (0, 0, 0))] * 2,
        out_shape=[jax.ShapeDtypeStruct((3, 48, 256), BF16)] * 2,
        name="finish",
    )(*[v for g in range(3) for v in (kept[g], first[g], second[g])])


def after_kernel(values_ref, *refs):
    refs[-1][...] = values_ref[...]


def after(values, gates):
    return pl.pallas_call(
        after_kernel,
        in_specs=[WHOLE] + [ANYWHERE] * len(gates),
        out_specs=WHOLE,
        out_shape=jax.ShapeDtypeStruct(values.shape, values.dtype),
        name="after",
    )(values, *gates)


def tail_kernel(place, act_ref, away_ref, q_ref, qb_ref, ka_ref, kb_ref, va_ref, vb_ref,
                att_own_ref, att_sib_ref, proj_ref, own_ref, sib_ref, far_ref, far_sib_ref, vec_ref,
                wq_ref, wk_ref, wv_ref, *refs):
    keep_ref, send_ref, rows_ref, acc, table = refs[-5:]
    core = place[0]

    def put(first, part, rows=slice(None)):
        acc[rows, first : first + part.shape[1]] = part

    act, away = act_ref[...], away_ref[...]
    first = 0
    for ref in (q_ref, qb_ref):
        put(first, mm(act, ref[...], TN))
        first += ref.shape[1]
    for ref in (ka_ref, kb_ref, va_ref, vb_ref):
        put(first, mm(act, ref[: 2 * N, :], TN) + mm(away, ref[2 * N :, :], TN))
        first += ref.shape[1]
    mine = pl.ds(pl.multiple_of(core * 384, 384), 384)
    other = pl.ds(pl.multiple_of((1 - core) * 384, 384), 384)
    put(1152, mm(att_own_ref[...], proj_ref[...], TN), mine)
    put(1152, mm(att_sib_ref[:N, :], proj_ref[N:, :], TN)
        + mm(att_sib_ref[N:, :], proj_ref[:N, :], TN), other)

    vectors = [jnp.zeros((1, 768), F32), jnp.zeros((1, 768), F32), vec_ref[0:1, :], vec_ref[1:2, :]]
    wide = ((q_ref, qb_ref, wq_ref), (ka_ref, kb_ref, wk_ref), (va_ref, vb_ref, wv_ref))
    for n, ext_ref in enumerate((own_ref, sib_ref, far_ref, far_sib_ref)):
        rows = slice(n * N, (n + 1) * N)
        total = jnp.zeros((N, 768), F32)
        for a_ref, b_ref, w_ref in wide[0 if n < 2 else 1 :]:
            total += mm(a_ref[rows, :], w_ref[:, :256], NT) + mm(b_ref[rows, :], w_ref[:, 256:], NT)
        xhat, _ = normalize(ext_ref[:N, :].astype(F32))
        vectors[0] += jnp.sum(total * xhat, axis=0, keepdims=True)
        vectors[1] += jnp.sum(total, axis=0, keepdims=True)
        half = slice((n // 2) * N, (n // 2 + 1) * N)
        if n % 2 == 0:
            keep_ref[half, :] = total
        else:
            send_ref[half, :] = total.astype(BF16)

    chip = lax.broadcasted_iota(jnp.int32, (64, 768), 0)
    owner = lax.broadcasted_iota(jnp.int32, (64, 768), 1) // 12
    feature = lax.broadcasted_iota(jnp.int32, (768, 128), 0) % 12
    lane = lax.broadcasted_iota(jnp.int32, (768, 128), 1)
    spread = jnp.zeros((64, 128), F32)
    for n in range(4):
        values = jnp.where(chip == owner, jnp.broadcast_to(vectors[n], (64, 768)), 0.0).astype(BF16)
        spread += mm(values, jnp.where(lane == feature + 12 * n, 1.0, 0.0).astype(BF16))
    table[...] = spread

    upper = lax.broadcasted_iota(jnp.int32, (8, 768), 0) < 4

    def unit(u, carry):
        top, mid, low = (
            acc[pl.ds(pl.multiple_of(24 * u + 8 * n, 8), 8), :] for n in range(3))
        turned = pltpu.roll(mid, 4, 0)
        first = jnp.where(upper, mid[:, :768], turned[:, 768:])
        second = jnp.where(upper, turned[:, :768], mid[:, 768:])
        lines = [jnp.broadcast_to(table[pl.ds(2 * u + n, 1), :], (8, 128)) for n in range(2)]
        both = jnp.concatenate([
            jnp.concatenate([top, first, lines[0]], axis=1),
            jnp.concatenate([low, second, lines[1]], axis=1)], axis=0)
        rows_ref[pl.ds(pl.multiple_of(16 * u, 16), 16), :] = both.astype(BF16)
        return carry

    lax.fori_loop(0, 32, unit, 0, unroll=2)


def tail_rows(core, operands, gates):
    whole = lambda shape: pl.BlockSpec(shape, lambda i, *_: (0,) * len(shape))
    shapes = [((2 * N, 768), F32), ((2 * N, 768), BF16), ((512, 2432), BF16)]
    return pl.pallas_call(
        tail_kernel,
        grid_spec=pltpu.PrefetchScalarGridSpec(
            num_scalar_prefetch=1,
            grid=(1,),
            in_specs=[whole(v.shape) for v in operands[:-1]]
            + [pl.BlockSpec((768, 384), lambda i, at, n=n: (0, 2 * n + at[0])) for n in range(3)]
            + [ANYWHERE] * len(gates),
            out_specs=[whole(shape) for shape, _ in shapes],
            scratch_shapes=[pltpu.VMEM((768, 1536), F32), pltpu.VMEM((64, 128), F32)],
        ),
        out_shape=[jax.ShapeDtypeStruct(*v) for v in shapes],
        compiler_params=pltpu.CompilerParams(vmem_limit_bytes=28 * 2**20),
        cost_estimate=pl.CostEstimate(
            flops=2 * 768 * 384 * 512 * 11, bytes_accessed=14 * 2**20, transcendentals=0),
        name="tail_rows",
    )(core, *operands, *[operands[-1]] * 2, *gates)


def total_kernel(parts_ref, *refs):
    out_ref, acc = refs[-2:]
    i = pl.program_id(0)
    part = jnp.sum(parts_ref[...].astype(F32), axis=0)

    @pl.when(i == 0)
    def _():
        acc[...] = part

    @pl.when(i > 0)
    def _():
        acc[...] += part

    @pl.when(i == pl.num_programs(0) - 1)
    def _():
        out_ref[...] = acc[...].astype(BF16)


def total(parts, gates):
    count, rows, lanes = parts.shape
    return pl.pallas_call(
        total_kernel,
        grid=(4,),
        in_specs=[pl.BlockSpec((count // 4, rows, lanes), lambda i: (i, 0, 0))]
        + [ANYWHERE] * len(gates),
        out_specs=pl.BlockSpec((rows, lanes), lambda i: (0, 0)),
        out_shape=jax.ShapeDtypeStruct((rows, lanes), BF16),
        scratch_shapes=[pltpu.VMEM((rows, lanes), F32)],
        compiler_params=pltpu.CompilerParams(vmem_limit_bytes=24 * 2**20),
        name="total",
    )(parts, *gates)


def rows_kernel(place, own_ref, sib_ref, qkv_ref, out_ref, vec_ref):
    core, far = place[0], place[1]
    line = own_ref[:, 2304:].astype(F32) + sib_ref[:, 2304:].astype(F32)
    vec_ref[...] = jnp.where(core == 0, line, pltpu.roll(line, 122, 1))
    row = lax.broadcasted_iota(jnp.int32, (8, 8), 0)
    column = lax.broadcasted_iota(jnp.int32, (8, 8), 1)
    wanted = row + 6 * core - 4 * far
    valid = row < 6
    main = jnp.where((column == wanted) & valid, 1.0, 0.0).astype(BF16)
    rest = wanted + 12 * far - 8
    valid = valid & (rest >= 0) & (rest < 4)
    extra = [jnp.where((column == rest + 4 * n) & valid, 1.0, 0.0).astype(BF16) for n in range(2)]
    for c in range(2):
        part = jnp.where(core == c, own_ref[...], sib_ref[...])
        rows = mm(main, part[:, :1536]) + jnp.concatenate(
            [mm(extra[n], part[:, 1536:2304]) for n in range(2)], axis=1)
        for kind in range(3):
            at = kind * 768 + c * 384
            qkv_ref[:, at : at + 384] = rows[:6, kind * 384 : (kind + 1) * 384]
        out_ref[:, c * 384 : (c + 1) * 384] = rows[:6, 1152:]


def own_rows(place, own, sib):
    return pl.pallas_call(
        rows_kernel,
        in_specs=[SMALL, WHOLE, WHOLE],
        out_specs=[WHOLE] * 3,
        out_shape=[
            jax.ShapeDtypeStruct((6, 2304), F32),
            jax.ShapeDtypeStruct((6, 768), F32),
            jax.ShapeDtypeStruct((8, 128), F32),
        ],
        name="own_rows",
    )(place, own, sib)


def assemble_kernel(place, own_ref, near_ref, away_ref, cross_ref, up_ref, held):
    core, far = place[0], place[1]
    held[far * 2 + core] = own_ref[...]
    held[far * 2 + 1 - core] = near_ref[...]
    held[2 - far * 2 + core] = away_ref[...]
    held[2 - far * 2 + 1 - core] = cross_ref[...]
    row = lax.broadcasted_iota(jnp.int32, (16, 48), 0)
    column = lax.broadcasted_iota(jnp.int32, (16, 48), 1)
    wanted = (row // 8) * 24 + far * 12 + core * 6 + row % 8
    select = jnp.where((column == wanted) & (row % 8 < 6), 1.0, 0.0).astype(BF16)
    for x_hi in range(2):
        for c in range(2):
            for g in range(3):
                rows = mm(select, held[x_hi * 2 + c, g])
                first = c * 1536 + g * 512 + x_hi * 256
                for e in range(2):
                    up_ref[e, :, first : first + 256] = rows[8 * e : 8 * e + 6] * UP_FACTORS[e]


def assemble(place, *parts):
    return pl.pallas_call(
        assemble_kernel,
        in_specs=[SMALL] + [WHOLE] * 4,
        out_specs=WHOLE,
        out_shape=jax.ShapeDtypeStruct((2, 6, 3072), F32),
        scratch_shapes=[pltpu.VMEM((4, 3, 48, 256), BF16)],
        name="assemble",
    )(place, *parts)


def shards(tokens, first_gain, first_shift, w_qkv, w_out, second_gain, second_shift,
           w_up, w_down, modality, segments, partner, cotangent):
    row_index, seq_index = lax.axis_index("rows"), lax.axis_index("seq")
    core, far = seq_index % 2, seq_index // 2
    place = jnp.stack([core, far]).astype(jnp.int32)
    table = lax.dynamic_index_in_dim(
        jnp.asarray(cell_places()), row_index * 4 + seq_index, 0, keepdims=False)
    gain1, shift1, gain2, shift2 = (
        v.reshape(1, 768) for v in (first_gain, first_shift, second_gain, second_shift))

    own = marked(partner, tokens[0], segments, modality)
    away = swap_far(own)
    sib = swap_core(own)
    cot_own = cotangent[0]
    cot_sib = swap_core(cot_own)

    act1, marks, queries, k_near, v_near, qx = project(place, own, sib, gain1, shift1, w_qkv, True)
    away_sib = swap_core(after(away, [qx]))
    act1_away, marks_away, k_away, v_away = project(
        place, away, away_sib, gain1, shift1, w_qkv, False)
    attended, lse = attend_forward(
        queries, k_near, k_away, v_near, v_away, qx, marks, marks_away)
    attended_sib = swap_core(attended)

    out_own, out_sib, grad_act2, grad_low, xhat2, factor2, act_t, inner_t, grad_pre = experts(
        place, attended, attended_sib, own, sib, cot_own, cot_sib, marks, gain2, shift2,
        w_out, w_up, w_down)
    grad_sib = swap_core(grad_low)
    ff_kept, ff_first, gates = [], [], []
    for g in range(3):
        keep, gone = cells(g, table, act_t, grad_pre, inner_t, cot_own, cot_sib, gates)
        ff_kept.append(keep.reshape(2, 16, 96, 256))
        ff_first.append(send(gone.reshape(2, 16, 96, 256), axis_step(ORDERS[g][0], True)))
        gates = [keep]
    hidden_grad, grad_att, proj_half, vectors = middle(
        place, grad_act2, grad_sib, xhat2, factor2, cot_own, cot_sib, gain2, w_out)

    def along(stage, first, values):
        return [send(v, axis_step(ORDERS[g][stage], first)) for g, v in enumerate(values)]

    taken = (queries, k_near, k_away, v_near, v_away, grad_att, attended, qx, marks, marks_away, lse)
    q_a, k_a, v_a = attend_backward(taken, 0, 2, ())
    q_b, k_b, v_b = attend_backward(taken, 2, 1, ())
    passed = pass_on(ff_kept, ff_first, "pass_first", 16, [q_b])
    ff_second = along(0, False, passed)
    partial_own, partial_sib, tail = tail_rows(
        place, (act1, act1_away, q_a, q_b, k_a, k_b, v_a, v_b, attended, attended_sib,
                proj_half, own, sib, away, away_sib, vectors, w_qkv), passed)
    kept, sent = settle(
        list(zip(ff_kept, ff_first, ff_second)), "settle_first", 24, [partial_sib])
    first = along(1, True, sent)
    second = along(1, False, pass_on(kept, first, "pass_second", 16))
    same_core = [list(range(c, 128, 2)) for c in range(2)]
    moved = lax.all_to_all(tail.reshape(64, 8, 2432), BOTH, 0, 0, tiled=True,
                           axis_index_groups=same_core)
    kept, sent = settle(list(zip(kept, first, second)), "settle_second", 16)
    first = along(2, True, sent)
    second = along(2, False, pass_on(kept, first, "pass_third", 16))
    up_held, down_held = finish(kept, first, second)

    partial = partial_own + swap_core(partial_sib).astype(F32)
    grad_act1 = partial[:N] + swap_far(partial[N:].astype(BF16)).astype(F32)
    xhat1, factor1 = normalize(tokens[0].astype(F32))
    token_grad = hidden_grad + normalize_back(grad_act1, xhat1, factor1, first_gain)
    layer_output = (out_own + swap_core(out_sib).astype(F32)).astype(BF16)

    near, beyond = swap_core(up_held), swap_far(up_held)
    cross = send(up_held, lambda x, y, z, c: (x ^ 2, y, z, 1 - c))
    up_grad = assemble(place, up_held, near, beyond, cross)
    summed = total(moved, ())
    qkv_grad, out_grad, line = own_rows(place, summed, swap_core(summed))

    down_rows = send(down_held, lambda x, y, z, c: (x, y, 2 * c + z % 2, z // 2)).astype(F32)
    down_rows = down_rows.reshape(3, 2, 24, 256).transpose(1, 2, 0, 3).reshape(2, 24, 768)
    factors = jnp.asarray(UP_FACTORS, F32)[:, None, None]
    return (
        layer_output[None], token_grad[None], line[0, :6], line[0, 12:18], qkv_grad, out_grad,
        line[0, 24:30], line[0, 36:42], up_grad, down_rows * factors)


def solution(mesh):
    cut = P("rows", "seq", None)
    flat = P(BOTH)
    placed = (cut,) + (P(),) * 8 + (P("rows", "seq"), P("rows", "seq"), P("rows", None), cut)
    return jax.shard_map(
        shards, mesh=mesh, in_specs=placed,
        out_specs=(cut, cut, flat, flat, P(BOTH, None), P(BOTH, None), flat, flat,
                   P(None, BOTH, None), P(None, BOTH, None)),
        check_vma=False)
```

```python
import jax
import jax.numpy as jnp
import numpy as np
from jax import lax
from jax.experimental import pallas as pl
from jax.experimental.pallas import tpu as pltpu
from jax.sharding import PartitionSpec as P

HD = 64
OWN = 6
CORE, FAR = 768, 769
IMG = 197
NIMG = 4
BOTH = ("rows", "seq")
F32 = jnp.float32
BF16 = jnp.bfloat16
MASKED = -1e30


def route(step):
    pairs = []
    for r in range(32):
        z, x_lo, y = r // 8, (r // 4) % 2, r % 4
        for s in range(4):
            x, c = (s // 2) * 2 + x_lo, s % 2
            tx, ty, tz, tc = step(x, y, z, c)
            target = (tz * 8 + (tx % 2) * 4 + ty) * 4 + (tx // 2) * 2 + tc
            pairs.append((r * 4 + s, target))
    return pairs


def send(values, step):
    return lax.ppermute(values, BOTH, route(step))


def swap_core(values):
    return send(values, lambda x, y, z, c: (x, y, z, 1 - c))


def swap_far(values):
    return send(values, lambda x, y, z, c: (x ^ 2, y, z, c))


def axis_step(axis, first):
    def step(x, y, z, c):
        flip = 1 if (c == 0) == first else 3
        at = {"x": x, "y": y, "z": z}
        at[axis] ^= flip
        return (at["x"], at["y"], at["z"], c)

    return step


UP_FACTORS = (1024 / (2 * 788), 1024 / (2 * 236))
ORDERS = (("x", "y", "z"), ("y", "z", "x"), ("z", "x", "y"))


def normalize(inputs):
    centred = inputs - jnp.mean(inputs, axis=-1, keepdims=True)
    factor = lax.rsqrt(jnp.mean(centred * centred, axis=-1, keepdims=True) + 1e-05)
    return centred * factor, factor


def normalize_back(grad, xhat, factor, gain):
    gy = grad * gain
    mean_gy = jnp.mean(gy, axis=-1, keepdims=True)
    mean_gx = jnp.mean(gy * xhat, axis=-1, keepdims=True)
    return factor * (gy - mean_gy - xhat * mean_gx)


SMALL = pl.BlockSpec(memory_space=pltpu.SMEM)
WHOLE = pl.BlockSpec(memory_space=pltpu.VMEM)
N = 256


def marked_kernel(partner, tokens_ref, segments_ref, modality_ref, out_ref):
    segments = segments_ref[...]
    tag = jnp.zeros(segments.shape, jnp.int32)
    for n in range(8):
        tag = jnp.where(segments == n, partner[0, n], tag)
    marks = jnp.concatenate(
        [tag, modality_ref[...], jnp.zeros((1, 256), jnp.int32)], axis=1).astype(F32)
    out_ref[:N, :] = tokens_ref[...]
    out_ref[N:, :] = jnp.concatenate([marks, jnp.zeros((15, 768), F32)], axis=0).astype(BF16)


def marked(partner, tokens, segments, modality):
    return pl.pallas_call(
        marked_kernel,
        in_specs=[SMALL, WHOLE, WHOLE, WHOLE],
        out_specs=WHOLE,
        out_shape=jax.ShapeDtypeStruct((N + 16, 768), BF16),
        compiler_params=pltpu.CompilerParams(vmem_limit_bytes=8 * 2**20),
        name="marked",
    )(partner, tokens, segments, modality)


def mark_lanes(ext):
    row = ext[N:, :].astype(F32)
    place = lax.broadcasted_iota(jnp.int32, (128, N), 0)
    tag = jnp.broadcast_to(row[:1, :N], (128, N))
    kind = jnp.broadcast_to(row[:1, N : 2 * N], (128, N))
    hot = jnp.where((place < NIMG) & (place.astype(F32) == tag), 1.0, 0.0)
    return jnp.transpose(jnp.where(place == 8, kind, hot))


def project_kernel(at_ref, near, a_ref, b_ref, gains_ref, *refs):
    count = 3 if near else 2
    weights, outs = refs[:count], refs[count:]
    for n, ext_ref in enumerate((a_ref, b_ref)):
        rows = slice(n * N, (n + 1) * N)
        ext = ext_ref[...]
        xhat, _ = normalize(ext[:N].astype(F32))
        act = (xhat * gains_ref[0:1, :] + gains_ref[1:2, :]).astype(BF16)
        outs[0][rows, :] = act
        marks = mark_lanes(ext)
        outs[1][rows, :] = marks.astype(BF16)
        for m in range(count):
            part = mm(act, weights[m][...])
            outs[2 + m][rows, :] = (0.125 * part if near and m == 0 else part).astype(BF16)
        if near:
            lane = lax.broadcasted_iota(jnp.int32, marks.shape, 1)
            outs[5][rows, :] = jnp.where((lane < NIMG) & (marks == 0.0), MASKED, 0.0).astype(BF16)


def project(table, first, second, gains, w_qkv, near):
    kinds = (0, 1, 2) if near else (1, 2)
    sizes = [768, 128] + [384] * len(kinds) + ([128] if near else [])
    whole = lambda shape: pl.BlockSpec(shape, lambda i, at: (0, 0))
    return pl.pallas_call(
        lambda at_ref, *refs: project_kernel(at_ref, near, *refs),
        grid_spec=pltpu.PrefetchScalarGridSpec(
            num_scalar_prefetch=1,
            grid=(1,),
            in_specs=[whole((N + 16, 768))] * 2 + [whole((4, 768))]
            + [pl.BlockSpec((768, 384), lambda i, at, n=n: (0, 2 * n + at[CORE])) for n in kinds],
            out_specs=[whole((2 * N, size)) for size in sizes],
        ),
        out_shape=[jax.ShapeDtypeStruct((2 * N, size), BF16) for size in sizes],
        compiler_params=pltpu.CompilerParams(vmem_limit_bytes=14 * 2**20),
        cost_estimate=pl.CostEstimate(
            flops=2 * 512 * 768 * 384 * len(kinds), bytes_accessed=4 * 2**20, transcendentals=0),
        name="project_near" if near else "project_away",
    )(table, first, second, gains, *[w_qkv] * len(kinds))


def middle_kernel(place, grad_ref, sib_ref, xhat_ref, factor_ref, cot_own_ref, cot_sib_ref,
                  gains_ref, w_out_ref, hidden_ref, att_ref, proj_ref, vec_ref):
    core = place[CORE]
    for n, cot_ref in enumerate((cot_own_ref, cot_sib_ref)):
        rows, other = slice(n * N, (n + 1) * N), slice((1 - n) * N, (2 - n) * N)
        grad = grad_ref[rows, :] + sib_ref[other, :].astype(F32)
        xhat = xhat_ref[rows, :]
        total = cot_ref[...].astype(F32) + normalize_back(grad, xhat, factor_ref[rows, :], gains_ref[2:3, :])
        low = total.astype(BF16)
        if n == 0:
            hidden_ref[...] = total
            vec_ref[0:1, :] = jnp.sum(grad * xhat, axis=0, keepdims=True)
            vec_ref[1:2, :] = jnp.sum(grad, axis=0, keepdims=True)
        mine = w_out_ref[pl.ds(pl.multiple_of(core * 384, 384), 384), :]
        att_ref[rows, :] = mm(low, mine, NT).astype(BF16)
        proj_ref[rows, :] = jnp.where(core == 0, low[:, :384], low[:, 384:])


def middle(place, *operands):
    return pl.pallas_call(
        middle_kernel,
        in_specs=[SMALL] + [WHOLE] * len(operands),
        out_specs=[WHOLE] * 4,
        out_shape=[
            jax.ShapeDtypeStruct((N, 768), F32),
            jax.ShapeDtypeStruct((2 * N, 384), BF16),
            jax.ShapeDtypeStruct((2 * N, 384), BF16),
            jax.ShapeDtypeStruct((2, 768), F32),
        ],
        compiler_params=pltpu.CompilerParams(vmem_limit_bytes=14 * 2**20),
        cost_estimate=pl.CostEstimate(
            flops=2 * 512 * 768 * 384, bytes_accessed=8 * 2**20, transcendentals=0),
        name="middle",
    )(place, *operands)


def gelu_parts(pre):
    phi = 0.5 * (1.0 + lax.erf(pre * 0.7071067811865476))
    slope = phi + pre * (0.3989422804014327 * jnp.exp(-0.5 * pre * pre))
    return pre * phi, slope


NT = (((1,), (1,)), ((), ()))
TN = (((0,), (0,)), ((), ()))
NN = (((1,), (0,)), ((), ()))


def mm(left, right, dims=NN):
    return lax.dot_general(left, right, dims, preferred_element_type=F32)


def head_lanes(shape, h):
    lane = lax.broadcasted_iota(jnp.int32, shape, len(shape) - 1)
    return (lane >= HD) == (h == 1)


def stacked(near_ref, away_ref):
    return jnp.concatenate([near_ref[...], away_ref[...]], axis=0)


def forward_kernel(q_ref, kn_ref, ka_ref, vn_ref, va_ref, qx_ref, xn_ref, xa_ref, out_ref, lse_ref):
    keys = jnp.concatenate([stacked(kn_ref, ka_ref), stacked(xn_ref, xa_ref)], axis=1)
    values = stacked(vn_ref, va_ref)
    q_pair = q_ref[...]
    lanes = head_lanes(q_pair.shape, 0)
    mixed = []
    for h in range(2):
        mine = lanes if h == 0 else jnp.logical_not(lanes)
        query = jnp.concatenate([jnp.where(mine, q_pair, 0), qx_ref[...]], axis=1)
        scores = mm(keys, query, NT)
        peak = jnp.max(scores, axis=0, keepdims=True)
        weights = jnp.exp(scores - peak)
        total = jnp.sum(weights, axis=0, keepdims=True)
        inverse = 1.0 / total
        low = (weights * inverse).astype(BF16)
        mixed.append(mm(low, values, TN))
        lse_ref[0, h : h + 1, :] = peak + jnp.log(total)
    out_ref[...] = jnp.where(lanes, mixed[0], mixed[1]).astype(BF16)


BY_PAIR = pl.BlockSpec((2 * N, 128), lambda p: (0, p))
FIXED = pl.BlockSpec((2 * N, 128), lambda p: (0, 0))


def attend_forward(*operands):
    return pl.pallas_call(
        forward_kernel,
        grid=(3,),
        in_specs=[BY_PAIR] * 5 + [FIXED] * 3,
        out_specs=[BY_PAIR, pl.BlockSpec((1, 2, 2 * N), lambda p: (p, 0, 0))],
        out_shape=[
            jax.ShapeDtypeStruct((2 * N, 384), BF16),
            jax.ShapeDtypeStruct((3, 2, 2 * N), F32),
        ],
        compiler_params=pltpu.CompilerParams(vmem_limit_bytes=16 * 2**20),
        cost_estimate=pl.CostEstimate(
            flops=2 * 2 * OWN * 512 * 1024 * 256, bytes_accessed=4 * 2**20,
            transcendentals=OWN * 512 * 1024),
        name="attend_forward",
    )(*operands)


def backward_kernel(q_ref, kn_ref, ka_ref, vn_ref, va_ref, do_ref, o_ref, qx_ref, xn_ref, xa_ref,
                    lse_ref, *refs):
    dq_ref, dk_ref, dv_ref = refs[-3:]
    k_pair, values = stacked(kn_ref, ka_ref), stacked(vn_ref, va_ref)
    keys = jnp.concatenate([k_pair, stacked(xn_ref, xa_ref)], axis=1)
    q_pair, grads = q_ref[...], do_ref[...]
    lanes = head_lanes(q_pair.shape, 0)
    product = grads.astype(F32) * o_ref[...].astype(F32)
    dq = jnp.zeros(q_pair.shape, F32)
    dk = jnp.zeros(k_pair.shape, F32)
    dv = jnp.zeros(k_pair.shape, F32)
    for h in range(2):
        mine = lanes if h == 0 else jnp.logical_not(lanes)
        q_head = jnp.where(mine, q_pair, 0)
        g_head = jnp.where(mine, grads, 0)
        dot_row = jnp.transpose(jnp.sum(jnp.where(mine, product, 0.0), axis=1, keepdims=True))
        scores = mm(keys, jnp.concatenate([q_head, qx_ref[...]], axis=1), NT)
        prob = jnp.exp(scores - lse_ref[0, h : h + 1, :])
        dv += mm(prob.astype(BF16), g_head)
        grad_prob = mm(values, g_head, NT)
        grad_scores = (prob * (grad_prob - dot_row)).astype(BF16)
        dk += mm(grad_scores, q_head)
        part = mm(grad_scores, k_pair, TN)
        dq += jnp.where(mine, part, 0.0)
    dq_ref[...] = dq.astype(BF16) * jnp.asarray(0.125, BF16)
    dk_ref[...] = dk.astype(BF16)
    dv_ref[...] = dv.astype(BF16)


def attend_backward(operands, first, pairs, gates):
    by_pair = pl.BlockSpec((2 * N, 128), lambda p: (0, first + p))
    sizes = (2 * N, 4 * N, 4 * N)
    return pl.pallas_call(
        backward_kernel,
        grid=(pairs,),
        in_specs=[by_pair] * 7 + [FIXED] * 3
        + [pl.BlockSpec((1, 2, 2 * N), lambda p: (first + p, 0, 0))]
        + [pl.BlockSpec(memory_space=pl.ANY)] * len(gates),
        out_specs=[pl.BlockSpec((size, 128), lambda p: (0, p)) for size in sizes],
        out_shape=[jax.ShapeDtypeStruct((size, pairs * 128), BF16) for size in sizes],
        compiler_params=pltpu.CompilerParams(vmem_limit_bytes=20 * 2**20),
        cost_estimate=pl.CostEstimate(
            flops=2 * 5 * 2 * pairs * 512 * 1024 * 256, bytes_accessed=6 * 2**20,
            transcendentals=2 * pairs * 512 * 1024),
        name="attend_backward",
    )(*operands, *gates)


FF_STEP = 512
EXPERT_MB = 40
CELLS_MB = 28


def expert_kernel(at_ref, att_own_ref, att_sib_ref, own_ref, sib_ref, cot_own_ref, cot_sib_ref,
                  marks_ref, gains_ref, w_out_ref, wu_ref, wd_ref,
                  out_ref, out_sib_ref, grad_ref, grad_low_ref, xhat_ref, factor_ref, act_t_ref,
                  inner_t_ref, slope_ref, act_acc, branch_ref):
    f = pl.program_id(0)
    core = at_ref[CORE]

    @pl.when(f == 0)
    def _():
        mine = w_out_ref[pl.ds(pl.multiple_of(core * 384, 384), 384), :]
        other = w_out_ref[pl.ds(pl.multiple_of((1 - core) * 384, 384), 384), :]
        for n, ext_ref in enumerate((own_ref, sib_ref)):
            rows, theirs = slice(n * N, (n + 1) * N), slice((1 - n) * N, (2 - n) * N)
            hidden = ext_ref[:N, :].astype(F32) + (
                mm(att_own_ref[rows, :], mine) + mm(att_sib_ref[theirs, :], other))
            xhat, factor = normalize(hidden)
            xhat_ref[rows, :] = xhat
            factor_ref[rows, :] = factor
            act = xhat * gains_ref[2:3, :] + gains_ref[3:4, :]
            act_acc[rows, :] = act.astype(BF16)
            act_t_ref[:, rows] = jnp.transpose(act).astype(BF16)
            if n == 0:
                branch_ref[rows, :] = hidden
            else:
                branch_ref[rows, :] = jnp.zeros_like(hidden)
        grad_ref[...] = jnp.zeros(grad_ref.shape, F32)

    act = act_acc[...]
    cot = jnp.concatenate([cot_own_ref[...], cot_sib_ref[...]], axis=0)
    text = marks_ref[:, 8:9].astype(F32) > 0.0
    pre = jnp.where(text, mm(act, wu_ref[1]), mm(act, wu_ref[0]))
    inner, slope = gelu_parts(pre)
    grad_pre = jnp.where(text, mm(cot, wd_ref[1], NT), mm(cot, wd_ref[0], NT)) * slope
    for e in range(2):
        mine = text if e == 1 else jnp.logical_not(text)
        inner_e = jnp.where(mine, inner, 0.0)
        grad_e = jnp.where(mine, grad_pre, 0.0).astype(BF16)
        branch_ref[...] += mm(inner_e.astype(BF16), wd_ref[e])
        grad_ref[...] += mm(grad_e, wu_ref[e], NT)
        inner_t_ref[e] = jnp.transpose(inner_e).astype(BF16)
        slope_ref[e] = grad_e

    @pl.when(f == pl.num_programs(0) - 1)
    def _():
        out_ref[...] = branch_ref[:N, :]
        out_sib_ref[...] = branch_ref[N:, :].astype(BF16)
        grad_low_ref[...] = grad_ref[...].astype(BF16)


def experts(core, *operands):
    steps = 3
    shapes = [((N, 768), F32), ((N, 768), BF16), ((2 * N, 768), F32), ((2 * N, 768), BF16),
              ((2 * N, 768), F32), ((2 * N, 1), F32), ((768, 2 * N), BF16)]
    fixed = lambda shape: pl.BlockSpec(shape, lambda f, *_: (0,) * len(shape))
    return pl.pallas_call(
        expert_kernel,
        grid_spec=pltpu.PrefetchScalarGridSpec(
            num_scalar_prefetch=1,
            grid=(steps,),
            in_specs=[fixed(v.shape) for v in operands[:-2]] + [
                pl.BlockSpec((2, 768, FF_STEP), lambda f, at: (0, 0, at[CORE] * steps + f)),
                pl.BlockSpec((2, FF_STEP, 768), lambda f, at: (0, at[CORE] * steps + f, 0)),
            ],
            out_specs=[fixed(shape) for shape, _ in shapes] + [
                pl.BlockSpec((2, FF_STEP, 2 * N), lambda f, at: (0, f, 0)),
                pl.BlockSpec((2, 2 * N, FF_STEP), lambda f, at: (0, 0, f)),
            ],
            scratch_shapes=[pltpu.VMEM((2 * N, 768), BF16), pltpu.VMEM((2 * N, 768), F32)],
        ),
        out_shape=[jax.ShapeDtypeStruct(*v) for v in shapes] + [
            jax.ShapeDtypeStruct((2, steps * FF_STEP, 2 * N), BF16),
            jax.ShapeDtypeStruct((2, 2 * N, steps * FF_STEP), BF16)],
        compiler_params=pltpu.CompilerParams(
            vmem_limit_bytes=32 * 2**20, dimension_semantics=("arbitrary",)),
        cost_estimate=pl.CostEstimate(
            flops=8 * 2 * 512 * 768 * 1536 + 2 * 512 * 768 * 768, bytes_accessed=24 * 2**20,
            transcendentals=2 * 512 * 1536),
        name="experts",
    )(core, *operands)


def cells_kernel(g, at_slot, act_t_ref, grad_ref, inner_t_ref, cot_own_ref, cot_sib_ref, *refs):
    keep_ref, send_ref, up_acc, down_acc = refs[-4:]
    e = pl.program_id(0)
    up = mm(act_t_ref[...], grad_ref[...])
    up_acc[e, 0] = up[:, :256]
    up_acc[e, 1] = up[:, 256:]
    cot = jnp.concatenate([cot_own_ref[...], cot_sib_ref[...]], axis=0)
    down_acc[e] = mm(inner_t_ref[...], cot)

    def spill(target, base):
        def cell(i, carry):
            slot = g * 64 + base + i
            half = at_slot[192 + slot]
            rows = pl.ds(pl.multiple_of(at_slot[slot], 8), 24)
            below = pl.ds(pl.multiple_of(at_slot[384 + slot], 8), 24)
            target[i] = jnp.concatenate(
                [up_acc[0, half, rows, :], up_acc[1, half, rows, :],
                 down_acc[0, below, :], down_acc[1, below, :]], axis=0).astype(BF16)
            return carry
        lax.fori_loop(0, 32, cell, 0, unroll=4)

    @pl.when(e == 1)
    def _():
        spill(keep_ref, 0)
        spill(send_ref, 32)


def cells(g, table, act_t, grad_pre, inner_t, cot_own, cot_sib, gates):
    cot = pl.BlockSpec((N, 256), lambda e, t: (0, g))
    out = pl.BlockSpec((32, 96, 256), lambda e, t: (0, 0, 0))
    return pl.pallas_call(
        lambda *refs: cells_kernel(g, *refs),
        grid_spec=pltpu.PrefetchScalarGridSpec(
            num_scalar_prefetch=1,
            grid=(2,),
            in_specs=[
                pl.BlockSpec((768, 2 * N), lambda e, t: (0, 0)),
                pl.BlockSpec((None, 2 * N, FF_STEP), lambda e, t: (e, 0, g)),
                pl.BlockSpec((None, 1536, 2 * N), lambda e, t: (e, 0, 0)),
                cot, cot] + [ANYWHERE] * len(gates),
            out_specs=[out] * 2,
            scratch_shapes=[pltpu.VMEM((2, 2, 768, 256), F32), pltpu.VMEM((2, 1536, 256), F32)],
        ),
        out_shape=[jax.ShapeDtypeStruct((32, 96, 256), BF16)] * 2,
        compiler_params=pltpu.CompilerParams(
            vmem_limit_bytes=20 * 2**20, dimension_semantics=("arbitrary",)),
        cost_estimate=pl.CostEstimate(
            flops=4 * 2 * 512 * 768 * 512, bytes_accessed=8 * 2**20, transcendentals=0),
        name="cells",
    )(table, act_t, grad_pre, inner_t, cot_own, cot_sib, *gates)


def cell_places():
    table = np.zeros((32, 4, 4, 3, 4, 4, 4), np.int32)
    for r, s in np.ndindex(32, 4):
        here = {"z": r // 8, "y": r % 4, "x": (s // 2) * 2 + (r // 4) % 2}
        flips = (0, 1, 3, 2) if s % 2 else (0, 3, 1, 2)
        for g, order in enumerate(ORDERS):
            for slot in np.ndindex(4, 4, 4):
                at = {a: here[a] ^ flips[n] for a, n in zip(order, slot)}
                x_hi, x_lo = at["x"] // 2, at["x"] % 2
                table[(r, s, 0, g) + slot] = 24 * (at["z"] * 8 + x_lo * 4 + at["y"])
                table[(r, s, 1, g) + slot] = x_hi
                table[(r, s, 2, g) + slot] = 24 * (
                    (at["z"] % 2) * 32 + x_lo * 16 + at["y"] * 4 + x_hi * 2 + at["z"] // 2)
                table[(r, s, 3, g) + slot] = at["z"] * 16 + x_lo * 8 + at["y"] * 2 + x_hi
    coordinates = np.array([[n % 2, n % 4 // 2] + [0] * 126 for n in range(128)], np.int32)
    return np.concatenate([table.reshape(128, 768), coordinates], axis=1)


def add_up(parts):
    total = parts[0].astype(F32)
    for part in parts[1:]:
        total = total + part.astype(F32)
    return total.astype(BF16)


def in_hbm(values):
    return list(values)


def pass_kernel(gates, *refs):
    count = (len(refs) - gates) // 3
    for g in range(count):
        refs[2 * count + gates + g][...] = add_up([refs[2 * g][...], refs[2 * g + 1][...]])


ANYWHERE = pl.BlockSpec(memory_space=pl.ANY)


def pass_on(kept, arrived, name, limit, gates=()):
    _, slots, rows, lanes = kept[0].shape
    block = max(slots // 4, 1)
    one = pl.BlockSpec((None, block, rows, lanes), lambda i: (1, i, 0, 0))
    return pl.pallas_call(
        lambda *refs: pass_kernel(len(gates), *refs),
        grid=(slots // block,),
        in_specs=[one] * (2 * len(kept)) + [ANYWHERE] * len(gates),
        out_specs=[pl.BlockSpec((block, rows, lanes), lambda i: (i, 0, 0))] * len(kept),
        out_shape=[jax.ShapeDtypeStruct((slots, rows, lanes), BF16)] * len(kept),
        compiler_params=pltpu.CompilerParams(vmem_limit_bytes=12 * 2**20),
        cost_estimate=pl.CostEstimate(
            flops=0, transcendentals=0, bytes_accessed=6 * len(kept) * slots * rows * lanes),
        name=name,
    )(*in_hbm([v for pair in zip(kept, arrived) for v in pair]), *gates)


def settle_kernel(groups, sizes, *refs):
    ins, outs = refs, refs[-2 * groups :]
    at = 0
    for g in range(groups):
        row = 0
        for size in sizes:
            for half in range(2):
                outs[2 * g + half][:, row : row + size, :] = add_up(
                    [ins[at + k][...] for k in range(3)])
                at += 3
            row += size


def settle(pieces, name):
    groups = len(pieces[0])
    sizes = [p[0][0].shape[2] for p in pieces]
    _, slots, _, lanes = pieces[0][0][0].shape
    half = slots // 2
    block = max(half // 4, 1)
    steps = half // block
    operands, specs = [], []
    for g in range(groups):
        for p, size in zip(pieces, sizes):
            for h in range(2):
                wide = pl.BlockSpec(
                    (None, block, size, lanes), lambda i, h=h: (0, i + h * steps, 0, 0))
                flat = pl.BlockSpec((block, size, lanes), lambda i, h=h: (i + h * steps, 0, 0))
                operands += list(p[g])
                specs += [wide, wide, flat]
    rows = sum(sizes)
    outs = pl.pallas_call(
        lambda *refs: settle_kernel(groups, sizes, *refs),
        grid=(steps,),
        in_specs=specs,
        out_specs=[pl.BlockSpec((block, rows, lanes), lambda i: (i, 0, 0))] * (2 * groups),
        out_shape=[jax.ShapeDtypeStruct((half, rows, lanes), BF16)] * (2 * groups),
        compiler_params=pltpu.CompilerParams(vmem_limit_bytes=12 * 2**20),
        cost_estimate=pl.CostEstimate(
            flops=0, transcendentals=0, bytes_accessed=8 * groups * slots * rows * lanes),
        name=name,
    )(*operands)
    shaped = [o.reshape(2, half // 2, rows, lanes) for o in outs]
    return shaped[0::2], shaped[1::2]


def finish_kernel(*refs):
    held_ref, down_ref = refs[-2:]
    for g in range(3):
        cell = add_up([refs[3 * g + k][...] for k in range(3)])
        held_ref[g, :48, :] = cell[:48]
        held_ref[g, 48:, :] = cell[96:]
        down_ref[g] = cell[48:96]


def finish(kept, first, second):
    wide = pl.BlockSpec((None, None, 128, 256), lambda i: (0, 0, 0, 0))
    flat = pl.BlockSpec((None, 128, 256), lambda i: (0, 0, 0))
    return pl.pallas_call(
        finish_kernel,
        grid=(1,),
        in_specs=[wide, wide, flat] * 3,
        out_specs=[pl.BlockSpec((3, 80, 256), lambda i: (0, 0, 0)),
                   pl.BlockSpec((3, 48, 256), lambda i: (0, 0, 0))],
        out_shape=[jax.ShapeDtypeStruct((3, 80, 256), BF16), jax.ShapeDtypeStruct((3, 48, 256), BF16)],
        compiler_params=pltpu.CompilerParams(vmem_limit_bytes=8 * 2**20),
        name="finish",
    )(*[v for g in range(3) for v in (kept[g], first[g], second[g])])


def after_kernel(values_ref, *refs):
    refs[-1][...] = values_ref[...]


def after(values, gates):
    return pl.pallas_call(
        after_kernel,
        in_specs=[WHOLE] + [ANYWHERE] * len(gates),
        out_specs=WHOLE,
        out_shape=jax.ShapeDtypeStruct(values.shape, values.dtype),
        compiler_params=pltpu.CompilerParams(vmem_limit_bytes=8 * 2**20),
        name="after",
    )(values, *gates)


def inputs_kernel(at_ref, q_ref, qb_ref, ka_ref, kb_ref, va_ref, vb_ref, own_ref, sib_ref, far_ref,
                  far_sib_ref, second_ref, wq_ref, wk_ref, wv_ref, keep_ref, send_ref, vec_ref):
    vectors = [jnp.zeros((1, 768), F32)] * 2
    wide = ((q_ref, qb_ref, wq_ref), (ka_ref, kb_ref, wk_ref), (va_ref, vb_ref, wv_ref))
    for n, ext_ref in enumerate((own_ref, sib_ref, far_ref, far_sib_ref)):
        rows = slice(n * N, (n + 1) * N)
        total = jnp.zeros((N, 768), F32)
        for a_ref, b_ref, w_ref in wide[0 if n < 2 else 1 :]:
            grads = jnp.concatenate([a_ref[rows, :], b_ref[rows, :]], axis=1)
            total += mm(grads, w_ref[...], NT)
        xhat, _ = normalize(ext_ref[:N, :].astype(F32))
        vectors[0] += jnp.sum(total * xhat, axis=0, keepdims=True)
        vectors[1] += jnp.sum(total, axis=0, keepdims=True)
        half = slice((n // 2) * N, (n // 2 + 1) * N)
        if n % 2 == 0:
            keep_ref[half, :] = total
        else:
            send_ref[half, :] = total.astype(BF16)
    vec_ref[0:1, :], vec_ref[1:2, :] = vectors
    vec_ref[2:4, :] = second_ref[...]


def input_partials(table, *operands):
    whole = lambda shape: pl.BlockSpec(shape, lambda i, *_: (0,) * len(shape))
    shapes = [((2 * N, 768), F32), ((2 * N, 768), BF16), ((4, 768), F32)]
    return pl.pallas_call(
        inputs_kernel,
        grid_spec=pltpu.PrefetchScalarGridSpec(
            num_scalar_prefetch=1,
            grid=(1,),
            in_specs=[whole(v.shape) for v in operands[:-1]]
            + [pl.BlockSpec((768, 384), lambda i, at, n=n: (0, 2 * n + at[CORE])) for n in range(3)],
            out_specs=[whole(shape) for shape, _ in shapes],
        ),
        out_shape=[jax.ShapeDtypeStruct(*v) for v in shapes],
        compiler_params=pltpu.CompilerParams(vmem_limit_bytes=20 * 2**20),
        cost_estimate=pl.CostEstimate(
            flops=2 * 768 * 384 * 512 * 5, bytes_accessed=8 * 2**20, transcendentals=0),
        name="input_partials",
    )(table, *operands, *[operands[-1]] * 2)


def tail_kernel(at_slot, act_ref, away_ref, q_ref, qb_ref, ka_ref, kb_ref, va_ref, vb_ref,
                att_own_ref, att_sib_ref, proj_ref, vec_ref, *refs):
    keeps, sends, acc, table = refs[-8:-5], refs[-5:-2], refs[-2], refs[-1]
    core = at_slot[CORE]

    def put(first, part, rows=slice(None)):
        for n in range(part.shape[1] // 128):
            column = first + n * 128
            lanes = slice(column % 256, column % 256 + 128)
            acc[column // 256, rows, lanes] = part[:, n * 128 : (n + 1) * 128]

    act, away = act_ref[...], away_ref[...]
    near_grads = jnp.concatenate([r[: 2 * N, :] for r in (q_ref, qb_ref, ka_ref, kb_ref, va_ref, vb_ref)], axis=1)
    away_grads = jnp.concatenate([r[2 * N :, :] for r in (ka_ref, kb_ref, va_ref, vb_ref)], axis=1)
    near = mm(act, near_grads, TN)
    put(0, near[:, :384])
    put(384, near[:, 384:] + mm(away, away_grads, TN))
    mine = pl.ds(pl.multiple_of(core * 384, 384), 384)
    other = pl.ds(pl.multiple_of((1 - core) * 384, 384), 384)
    put(1152, mm(att_own_ref[...], proj_ref[...], TN), mine)
    put(1152, mm(att_sib_ref[:N, :], proj_ref[N:, :], TN)
        + mm(att_sib_ref[N:, :], proj_ref[:N, :], TN), other)

    chip = lax.broadcasted_iota(jnp.int32, (64, 768), 0)
    owner = lax.broadcasted_iota(jnp.int32, (64, 768), 1) // 12
    feature = lax.broadcasted_iota(jnp.int32, (768, 128), 0) % 12
    lane = lax.broadcasted_iota(jnp.int32, (768, 128), 1)
    spread = jnp.zeros((64, 128), F32)
    for n in range(4):
        line = jnp.broadcast_to(vec_ref[n : n + 1, :], (64, 768))
        values = jnp.where(chip == owner, line, 0.0).astype(BF16)
        spread += mm(values, jnp.where(lane == feature + 12 * n, 1.0, 0.0).astype(BF16))
    table[...] = spread

    def spill(target, g, base):
        def cell(i, carry):
            slot = g * 64 + base + i
            rows = pl.ds(pl.multiple_of(at_slot[slot], 8), 24)
            part = acc[2 * g + at_slot[192 + slot], rows, :]
            if g == 0:
                row = table[pl.ds(at_slot[576 + slot], 1), :]
                extra = jnp.concatenate([jnp.broadcast_to(row, (8, 128)), jnp.zeros((8, 128), F32)], axis=1)
            else:
                extra = jnp.zeros((8, 256), F32)
            target[i] = jnp.concatenate([part, extra], axis=0).astype(BF16)
            return carry
        lax.fori_loop(0, 32, cell, 0, unroll=4)

    for g in range(3):
        spill(keeps[g], g, 0)
        spill(sends[g], g, 32)


def tail_cells(table, operands, gates):
    return pl.pallas_call(
        tail_kernel,
        in_specs=[SMALL] + [WHOLE] * len(operands) + [ANYWHERE] * len(gates),
        out_specs=[WHOLE] * 6,
        out_shape=[jax.ShapeDtypeStruct((32, 32, 256), BF16)] * 6,
        scratch_shapes=[pltpu.VMEM((6, 768, 256), F32), pltpu.VMEM((64, 128), F32)],
        compiler_params=pltpu.CompilerParams(vmem_limit_bytes=28 * 2**20),
        cost_estimate=pl.CostEstimate(
            flops=2 * 768 * 384 * 512 * 6, bytes_accessed=10 * 2**20, transcendentals=0),
        name="tail_cells",
    )(table, *operands, *gates)


def sum_core_kernel(own_ref, sib_ref, out_ref):
    out_ref[...] = (own_ref[...] + sib_ref[...].astype(F32)).astype(BF16)


def sum_core(own, sib):
    half = pl.BlockSpec((N, 768), lambda i: (1, 0))
    return pl.pallas_call(
        sum_core_kernel,
        grid=(1,),
        in_specs=[half, half],
        out_specs=pl.BlockSpec((N, 768), lambda i: (0, 0)),
        out_shape=jax.ShapeDtypeStruct((N, 768), BF16),
        compiler_params=pltpu.CompilerParams(vmem_limit_bytes=8 * 2**20),
        name="sum_core",
    )(own, sib)


def token_kernel(tokens_ref, hidden_ref, own_ref, sib_ref, far_ref, gains_ref, out_own_ref,
                 out_sib_ref, grad_ref, out_ref):
    grad = own_ref[...] + sib_ref[...].astype(F32) + far_ref[...].astype(F32)
    xhat, factor = normalize(tokens_ref[...].astype(F32))
    grad_ref[...] = hidden_ref[...] + normalize_back(grad, xhat, factor, gains_ref[0:1, :])
    out_ref[...] = (out_own_ref[...] + out_sib_ref[...].astype(F32)).astype(BF16)


def token_grads(tokens, hidden, own, sib, far, gains, out_own, out_sib):
    half = pl.BlockSpec((N, 768), lambda i: (0, 0))
    return pl.pallas_call(
        token_kernel,
        grid=(1,),
        in_specs=[half] * 5 + [pl.BlockSpec((4, 768), lambda i: (0, 0))] + [half] * 2,
        out_specs=[half] * 2,
        out_shape=[jax.ShapeDtypeStruct((N, 768), F32), jax.ShapeDtypeStruct((N, 768), BF16)],
        compiler_params=pltpu.CompilerParams(vmem_limit_bytes=14 * 2**20),
        name="token_grads",
    )(tokens, hidden, own, sib, far, gains, out_own, out_sib)


def assemble_kernel(at_ref, own_ref, near_ref, away_ref, cross_ref, down_ref, up_ref, qkv_ref, out_ref,
                    vec_ref, below_ref, held):
    core, far = at_ref[CORE], at_ref[FAR]
    held[far * 2 + core] = own_ref[...]
    held[far * 2 + 1 - core] = near_ref[...]
    held[2 - far * 2 + core] = away_ref[...]
    held[2 - far * 2 + 1 - core] = cross_ref[...]
    line = held[far * 2, 0, 64:, :128].astype(F32) + held[far * 2 + 1, 0, 64:, :128].astype(F32)
    vec_ref[...] = jnp.where(core == 0, line, pltpu.roll(line, 122, 1))[8:]
    row = lax.broadcasted_iota(jnp.int32, (24, 80), 0)
    column = lax.broadcasted_iota(jnp.int32, (24, 80), 1)
    wanted = (row // 8) * 24 + far * 12 + core * 6 + row % 8
    select = jnp.where((column == wanted) & (row % 8 < 6), 1.0, 0.0).astype(BF16)
    for x_hi in range(2):
        for c in range(2):
            for g in range(3):
                rows = mm(select, held[x_hi * 2 + c, g])
                first = c * 1536 + g * 512 + x_hi * 256
                for e in range(2):
                    up_ref[e, :, first : first + 256] = rows[8 * e : 8 * e + 6] * UP_FACTORS[e]
                for n in range(2):
                    at = g * 512 + x_hi * 256 + n * 128
                    kind, within = at // 384, at % 384 + c * 384
                    part = rows[16:22, n * 128 : (n + 1) * 128]
                    if kind < 3:
                        qkv_ref[:, kind * 768 + within : kind * 768 + within + 128] = part
                    else:
                        out_ref[:, within : within + 128] = part
    for g in range(3):
        part = down_ref[g].astype(F32)
        for e in range(2):
            below_ref[e, :, g * 256 : (g + 1) * 256] = part[24 * e : 24 * e + 24] * UP_FACTORS[e]


def assemble(table, *parts):
    return pl.pallas_call(
        assemble_kernel,
        in_specs=[SMALL] + [WHOLE] * 5,
        out_specs=[WHOLE] * 5,
        out_shape=[
            jax.ShapeDtypeStruct((2, 6, 3072), F32),
            jax.ShapeDtypeStruct((6, 2304), F32),
            jax.ShapeDtypeStruct((6, 768), F32),
            jax.ShapeDtypeStruct((8, 128), F32),
            jax.ShapeDtypeStruct((2, 24, 768), F32),
        ],
        scratch_shapes=[pltpu.VMEM((4, 3, 80, 256), BF16)],
        compiler_params=pltpu.CompilerParams(vmem_limit_bytes=8 * 2**20),
        name="assemble",
    )(table, *parts)

def shards(tokens, first_gain, first_shift, w_qkv, w_out, second_gain, second_shift,
           w_up, w_down, modality, segments, partner, cotangent):
    table = lax.dynamic_index_in_dim(
        jnp.asarray(cell_places()), lax.axis_index(BOTH), 0, keepdims=False)
    gains = jnp.stack([first_gain, first_shift, second_gain, second_shift])

    own = marked(partner, tokens[0], segments, modality)
    away = swap_far(own)
    sib = swap_core(own)
    cot_own = cotangent[0]
    cot_sib = swap_core(cot_own)

    act1, marks, queries, k_near, v_near, qx = project(table, own, sib, gains, w_qkv, True)
    away_sib = swap_core(after(away, [qx]))
    act1_away, marks_away, k_away, v_away = project(table, away, away_sib, gains, w_qkv, False)
    attended, lse = attend_forward(
        queries, k_near, k_away, v_near, v_away, qx, marks, marks_away)
    attended_sib = swap_core(attended)

    out_own, out_sib, grad_act2, grad_low, xhat2, factor2, act_t, inner_t, grad_pre = experts(
        table, attended, attended_sib, own, sib, cot_own, cot_sib, marks, gains, w_out, w_up, w_down)
    grad_sib = swap_core(grad_low)
    ff_kept, ff_first, gates = [], [], []
    for g in range(3):
        keep, gone = cells(g, table, act_t, grad_pre, inner_t, cot_own, cot_sib, gates)
        ff_kept.append(keep.reshape(2, 16, 96, 256))
        ff_first.append(send(gone.reshape(2, 16, 96, 256), axis_step(ORDERS[g][0], True)))
        gates = [keep]
    hidden_grad, grad_att, proj_half, vectors = middle(
        table, grad_act2, grad_sib, xhat2, factor2, cot_own, cot_sib, gains, w_out)

    def along(stage, first, values):
        return [send(v, axis_step(ORDERS[g][stage], first)) for g, v in enumerate(values)]

    taken = (queries, k_near, k_away, v_near, v_away, grad_att, attended, qx, marks, marks_away, lse)
    q_a, k_a, v_a = attend_backward(taken, 0, 2, ())
    passed = pass_on(ff_kept, ff_first, "pass_first", 12, [q_a])
    ff_second = along(0, False, passed)
    q_b, k_b, v_b = attend_backward(taken, 2, 1, passed)
    partial_own, partial_low, vectors = input_partials(
        table, q_a, q_b, k_a, k_b, v_a, v_b, own, sib, away, away_sib, vectors, w_qkv)
    tail = tail_cells(table, (
        act1, act1_away, q_a, q_b, k_a, k_b, v_a, v_b, attended, attended_sib, proj_half, vectors),
        ff_second)

    kept = [v.reshape(2, 16, 32, 256) for v in tail[:3]]
    first = along(0, True, [v.reshape(2, 16, 32, 256) for v in tail[3:]])
    second = along(0, False, pass_on(kept, first, "pass_tail", 12))
    kept, sent = settle(
        [list(zip(ff_kept, ff_first, ff_second)), list(zip(kept, first, second))], "settle_all")
    first = along(1, True, sent)
    second = along(1, False, pass_on(kept, first, "pass_second", 12))
    kept, sent = settle([list(zip(kept, first, second))], "settle_second")
    first = along(2, True, sent)
    second = along(2, False, pass_on(kept, first, "pass_third", 12))
    held, down_held = finish(kept, first, second)

    near, beyond = swap_core(held), swap_far(held)
    cross = send(held, lambda x, y, z, c: (x ^ 2, y, z, 1 - c))
    below = send(down_held, lambda x, y, z, c: (x, y, 2 * c + z % 2, z // 2))
    up_grad, qkv_grad, out_grad, line, down_grad = assemble(
        table, held, near, beyond, cross, below)

    partial_sib = swap_core(partial_low)
    from_far = swap_far(sum_core(partial_own, partial_sib))
    token_grad, layer_output = token_grads(
        tokens[0], hidden_grad, partial_own, partial_sib, from_far, gains, out_own, swap_core(out_sib))

    return (
        layer_output[None], token_grad[None], line[0, :6], line[0, 12:18], qkv_grad, out_grad,
        line[0, 24:30], line[0, 36:42], up_grad, down_grad)


def solution(mesh):
    cut = P("rows", "seq", None)
    flat = P(BOTH)
    placed = (cut,) + (P(),) * 8 + (P("rows", "seq"), P("rows", "seq"), P("rows", None), cut)
    return jax.shard_map(
        shards, mesh=mesh, in_specs=placed,
        out_specs=(cut, cut, flat, flat, P(BOTH, None), P(BOTH, None), flat, flat,
                   P(None, BOTH, None), P(None, BOTH, None)),
        check_vma=False)
```

```python
import jax
import jax.numpy as jnp
import numpy as np
from jax import lax
from jax.experimental import pallas as pl
from jax.experimental.pallas import tpu as pltpu
from jax.sharding import PartitionSpec as P

HD = 64
OWN = 6
CORE, FAR = 768, 769
IMG = 197
NIMG = 4
BOTH = ("rows", "seq")
F32 = jnp.float32
BF16 = jnp.bfloat16
MASKED = -1e30


def route(step):
    pairs = []
    for r in range(32):
        z, x_lo, y = r // 8, (r // 4) % 2, r % 4
        for s in range(4):
            x, c = (s // 2) * 2 + x_lo, s % 2
            tx, ty, tz, tc = step(x, y, z, c)
            target = (tz * 8 + (tx % 2) * 4 + ty) * 4 + (tx // 2) * 2 + tc
            pairs.append((r * 4 + s, target))
    return pairs


def send(values, step):
    return lax.ppermute(values, BOTH, route(step))


def swap_core(values):
    return send(values, lambda x, y, z, c: (x, y, z, 1 - c))


def swap_far(values):
    return send(values, lambda x, y, z, c: (x ^ 2, y, z, c))


def axis_step(axis, first):
    def step(x, y, z, c):
        flip = 1 if (c == 0) == first else 3
        at = {"x": x, "y": y, "z": z}
        at[axis] ^= flip
        return (at["x"], at["y"], at["z"], c)

    return step


UP_FACTORS = (1024 / (2 * 788), 1024 / (2 * 236))
ORDERS = (("x", "y", "z"), ("y", "z", "x"), ("z", "x", "y"))


def normalize(inputs):
    centred = inputs - jnp.mean(inputs, axis=-1, keepdims=True)
    factor = lax.rsqrt(jnp.mean(centred * centred, axis=-1, keepdims=True) + 1e-05)
    return centred * factor, factor


def normalize_back(grad, xhat, factor, gain):
    gy = grad * gain
    mean_gy = jnp.mean(gy, axis=-1, keepdims=True)
    mean_gx = jnp.mean(gy * xhat, axis=-1, keepdims=True)
    return factor * (gy - mean_gy - xhat * mean_gx)


SMALL = pl.BlockSpec(memory_space=pltpu.SMEM)
WHOLE = pl.BlockSpec(memory_space=pltpu.VMEM)
N = 256


def marked_kernel(partner, tokens_ref, segments_ref, modality_ref, out_ref):
    segments = segments_ref[...]
    tag = jnp.zeros(segments.shape, jnp.int32)
    for n in range(8):
        tag = jnp.where(segments == n, partner[0, n], tag)
    marks = jnp.concatenate(
        [tag, modality_ref[...], jnp.zeros((1, 256), jnp.int32)], axis=1).astype(F32)
    out_ref[:N, :] = tokens_ref[...]
    out_ref[N:, :] = jnp.concatenate([marks, jnp.zeros((15, 768), F32)], axis=0).astype(BF16)


def marked(partner, tokens, segments, modality):
    return pl.pallas_call(
        marked_kernel,
        in_specs=[SMALL, WHOLE, WHOLE, WHOLE],
        out_specs=WHOLE,
        out_shape=jax.ShapeDtypeStruct((N + 16, 768), BF16),
        compiler_params=pltpu.CompilerParams(vmem_limit_bytes=60 * 2**20),
        name="marked",
    )(partner, tokens, segments, modality)


def mark_lanes(ext):
    row = ext[N:, :].astype(F32)
    place = lax.broadcasted_iota(jnp.int32, (128, N), 0)
    tag = jnp.broadcast_to(row[:1, :N], (128, N))
    kind = jnp.broadcast_to(row[:1, N : 2 * N], (128, N))
    hot = jnp.where((place < NIMG) & (place.astype(F32) == tag), 1.0, 0.0)
    return jnp.transpose(jnp.where(place == 8, kind, hot))


def project_kernel(at_ref, near, a_ref, b_ref, gains_ref, *refs):
    count = 3 if near else 2
    weights, outs = refs[:count], refs[count:]
    for n, ext_ref in enumerate((a_ref, b_ref)):
        rows = slice(n * N, (n + 1) * N)
        ext = ext_ref[...]
        xhat, _ = normalize(ext[:N].astype(F32))
        act = (xhat * gains_ref[0:1, :] + gains_ref[1:2, :]).astype(BF16)
        outs[0][rows, :] = act
        marks = mark_lanes(ext)
        outs[1][rows, :] = marks.astype(BF16)
        for m in range(count):
            part = mm(act, weights[m][...])
            outs[2 + m][rows, :] = (0.125 * part if near and m == 0 else part).astype(BF16)
        if near:
            lane = lax.broadcasted_iota(jnp.int32, marks.shape, 1)
            outs[5][rows, :] = jnp.where((lane < NIMG) & (marks == 0.0), MASKED, 0.0).astype(BF16)


def project(table, first, second, gains, w_qkv, near):
    kinds = (0, 1, 2) if near else (1, 2)
    sizes = [768, 128] + [384] * len(kinds) + ([128] if near else [])
    whole = lambda shape: pl.BlockSpec(shape, lambda i, at: (0, 0))
    return pl.pallas_call(
        lambda at_ref, *refs: project_kernel(at_ref, near, *refs),
        grid_spec=pltpu.PrefetchScalarGridSpec(
            num_scalar_prefetch=1,
            grid=(1,),
            in_specs=[whole((N + 16, 768))] * 2 + [whole((4, 768))]
            + [pl.BlockSpec((768, 384), lambda i, at, n=n: (0, 2 * n + at[CORE])) for n in kinds],
            out_specs=[whole((2 * N, size)) for size in sizes],
        ),
        out_shape=[jax.ShapeDtypeStruct((2 * N, size), BF16) for size in sizes],
        compiler_params=pltpu.CompilerParams(vmem_limit_bytes=6 * 2**20),
        cost_estimate=pl.CostEstimate(
            flops=2 * 512 * 768 * 384 * len(kinds), bytes_accessed=4 * 2**20, transcendentals=0),
        name="project_near" if near else "project_away",
    )(table, first, second, gains, *[w_qkv] * len(kinds))


def middle_kernel(place, grad_ref, sib_ref, xhat_ref, factor_ref, cot_own_ref, cot_sib_ref,
                  gains_ref, w_out_ref, hidden_ref, att_ref, proj_ref, vec_ref):
    core = place[CORE]
    for n, cot_ref in enumerate((cot_own_ref, cot_sib_ref)):
        rows, other = slice(n * N, (n + 1) * N), slice((1 - n) * N, (2 - n) * N)
        grad = grad_ref[rows, :] + sib_ref[other, :].astype(F32)
        xhat = xhat_ref[rows, :]
        total = cot_ref[...].astype(F32) + normalize_back(grad, xhat, factor_ref[rows, :], gains_ref[2:3, :])
        low = total.astype(BF16)
        if n == 0:
            hidden_ref[...] = total
            vec_ref[0:1, :] = jnp.sum(grad * xhat, axis=0, keepdims=True)
            vec_ref[1:2, :] = jnp.sum(grad, axis=0, keepdims=True)
        mine = w_out_ref[pl.ds(pl.multiple_of(core * 384, 384), 384), :]
        att_ref[rows, :] = mm(low, mine, NT).astype(BF16)
        proj_ref[rows, :] = jnp.where(core == 0, low[:, :384], low[:, 384:])


def middle(place, *operands):
    return pl.pallas_call(
        middle_kernel,
        in_specs=[SMALL] + [WHOLE] * len(operands),
        out_specs=[WHOLE] * 4,
        out_shape=[
            jax.ShapeDtypeStruct((N, 768), F32),
            jax.ShapeDtypeStruct((2 * N, 384), BF16),
            jax.ShapeDtypeStruct((2 * N, 384), BF16),
            jax.ShapeDtypeStruct((2, 768), F32),
        ],
        compiler_params=pltpu.CompilerParams(vmem_limit_bytes=6 * 2**20),
        cost_estimate=pl.CostEstimate(
            flops=2 * 512 * 768 * 384, bytes_accessed=8 * 2**20, transcendentals=0),
        name="middle",
    )(place, *operands)


def gelu_parts(pre):
    phi = 0.5 * (1.0 + lax.erf(pre * 0.7071067811865476))
    slope = phi + pre * (0.3989422804014327 * jnp.exp(-0.5 * pre * pre))
    return pre * phi, slope


NT = (((1,), (1,)), ((), ()))
TN = (((0,), (0,)), ((), ()))
NN = (((1,), (0,)), ((), ()))


def mm(left, right, dims=NN):
    return lax.dot_general(left, right, dims, preferred_element_type=F32)


def head_lanes(shape, h):
    lane = lax.broadcasted_iota(jnp.int32, shape, len(shape) - 1)
    return (lane >= HD) == (h == 1)


def stacked(near_ref, away_ref):
    return jnp.concatenate([near_ref[...], away_ref[...]], axis=0)


def forward_kernel(q_ref, kn_ref, ka_ref, vn_ref, va_ref, qx_ref, xn_ref, xa_ref, out_ref, lse_ref):
    keys = jnp.concatenate([stacked(kn_ref, ka_ref), stacked(xn_ref, xa_ref)], axis=1)
    values = stacked(vn_ref, va_ref)
    q_pair = q_ref[...]
    lanes = head_lanes(q_pair.shape, 0)
    value_lanes = head_lanes(values.shape, 0)
    mixed = []
    for h in range(2):
        mine = lanes if h == 0 else jnp.logical_not(lanes)
        mine_values = value_lanes if h == 0 else jnp.logical_not(value_lanes)
        query = jnp.concatenate([jnp.where(mine, q_pair, 0), qx_ref[...]], axis=1)
        scores = mm(keys, query, NT)
        peak = jnp.max(scores, axis=0, keepdims=True)
        weights = jnp.exp(scores - peak).astype(BF16)
        both = mm(weights, jnp.where(mine_values, values, 1), TN)
        total = both[:, 127:128] if h == 0 else both[:, 0:1]
        mixed.append(both * (1.0 / total))
        wide = jnp.transpose(jnp.broadcast_to(total, (2 * N, 128)))
        lse_ref[0, h : h + 1, :] = peak + jnp.log(wide[0:1, :])
    out_ref[...] = jnp.where(lanes, mixed[0], mixed[1]).astype(BF16)


BY_PAIR = pl.BlockSpec((2 * N, 128), lambda p: (0, p))
FIXED = pl.BlockSpec((2 * N, 128), lambda p: (0, 0))


def attend_forward(*operands):
    return pl.pallas_call(
        forward_kernel,
        grid=(3,),
        in_specs=[BY_PAIR] * 5 + [FIXED] * 3,
        out_specs=[BY_PAIR, pl.BlockSpec((1, 2, 2 * N), lambda p: (p, 0, 0))],
        out_shape=[
            jax.ShapeDtypeStruct((2 * N, 384), BF16),
            jax.ShapeDtypeStruct((3, 2, 2 * N), F32),
        ],
        compiler_params=pltpu.CompilerParams(vmem_limit_bytes=6 * 2**20),
        cost_estimate=pl.CostEstimate(
            flops=2 * 2 * OWN * 512 * 1024 * 256, bytes_accessed=4 * 2**20,
            transcendentals=OWN * 512 * 1024),
        name="attend_forward",
    )(*operands)


def backward_kernel(q_ref, kn_ref, ka_ref, vn_ref, va_ref, do_ref, o_ref, qx_ref, xn_ref, xa_ref,
                    lse_ref, *refs):
    dq_ref, dk_ref, dv_ref = refs[-3:]
    k_pair, values = stacked(kn_ref, ka_ref), stacked(vn_ref, va_ref)
    keys = jnp.concatenate([k_pair, stacked(xn_ref, xa_ref)], axis=1)
    q_pair, grads = q_ref[...], do_ref[...]
    lanes = head_lanes(q_pair.shape, 0)
    product = grads.astype(F32) * o_ref[...].astype(F32)
    dq = jnp.zeros(q_pair.shape, F32)
    dk = jnp.zeros(k_pair.shape, F32)
    dv = jnp.zeros(k_pair.shape, F32)
    for h in range(2):
        mine = lanes if h == 0 else jnp.logical_not(lanes)
        q_head = jnp.where(mine, q_pair, 0)
        g_head = jnp.where(mine, grads, 0)
        dot_row = jnp.transpose(jnp.sum(jnp.where(mine, product, 0.0), axis=1, keepdims=True))
        scores = mm(keys, jnp.concatenate([q_head, qx_ref[...]], axis=1), NT)
        prob = jnp.exp(scores - lse_ref[0, h : h + 1, :])
        dv += mm(prob.astype(BF16), g_head)
        grad_prob = mm(values, g_head, NT)
        grad_scores = (prob * (grad_prob - dot_row)).astype(BF16)
        dk += mm(grad_scores, q_head)
        part = mm(grad_scores, k_pair, TN)
        dq += jnp.where(mine, part, 0.0)
    dq_ref[...] = dq.astype(BF16) * jnp.asarray(0.125, BF16)
    dk_ref[...] = dk.astype(BF16)
    dv_ref[...] = dv.astype(BF16)


def attend_backward(operands, first, pairs, gates):
    by_pair = pl.BlockSpec((2 * N, 128), lambda p: (0, first + p))
    sizes = (2 * N, 4 * N, 4 * N)
    return pl.pallas_call(
        backward_kernel,
        grid=(pairs,),
        in_specs=[by_pair] * 7 + [FIXED] * 3
        + [pl.BlockSpec((1, 2, 2 * N), lambda p: (first + p, 0, 0))]
        + [pl.BlockSpec(memory_space=pl.ANY)] * len(gates),
        out_specs=[pl.BlockSpec((size, 128), lambda p: (0, p)) for size in sizes],
        out_shape=[jax.ShapeDtypeStruct((size, pairs * 128), BF16) for size in sizes],
        compiler_params=pltpu.CompilerParams(vmem_limit_bytes=10 * 2**20),
        cost_estimate=pl.CostEstimate(
            flops=2 * 5 * 2 * pairs * 512 * 1024 * 256, bytes_accessed=6 * 2**20,
            transcendentals=2 * pairs * 512 * 1024),
        name="attend_backward",
    )(*operands, *gates)


FF_STEP = 512
EXPERT_MB = 40
CELLS_MB = 28


def expert_kernel(at_ref, att_own_ref, att_sib_ref, own_ref, sib_ref, cot_own_ref, cot_sib_ref,
                  marks_ref, gains_ref, w_out_ref, wu_ref, wd_ref,
                  out_ref, out_sib_ref, grad_ref, grad_low_ref, xhat_ref, factor_ref, act_t_ref,
                  inner_t_ref, slope_ref, act_acc, branch_ref):
    f = pl.program_id(0)
    core = at_ref[CORE]

    @pl.when(f == 0)
    def _():
        mine = w_out_ref[pl.ds(pl.multiple_of(core * 384, 384), 384), :]
        other = w_out_ref[pl.ds(pl.multiple_of((1 - core) * 384, 384), 384), :]
        for n, ext_ref in enumerate((own_ref, sib_ref)):
            rows, theirs = slice(n * N, (n + 1) * N), slice((1 - n) * N, (2 - n) * N)
            hidden = ext_ref[:N, :].astype(F32) + (
                mm(att_own_ref[rows, :], mine) + mm(att_sib_ref[theirs, :], other))
            xhat, factor = normalize(hidden)
            xhat_ref[rows, :] = xhat
            factor_ref[rows, :] = factor
            act = xhat * gains_ref[2:3, :] + gains_ref[3:4, :]
            act_acc[rows, :] = act.astype(BF16)
            act_t_ref[:, rows] = jnp.transpose(act).astype(BF16)
            if n == 0:
                branch_ref[rows, :] = hidden
            else:
                branch_ref[rows, :] = jnp.zeros_like(hidden)
        grad_ref[...] = jnp.zeros(grad_ref.shape, F32)

    act = act_acc[...]
    cot = jnp.concatenate([cot_own_ref[...], cot_sib_ref[...]], axis=0)
    text = marks_ref[:, 8:9].astype(F32) > 0.0
    pre = jnp.where(text, mm(act, wu_ref[1]), mm(act, wu_ref[0]))
    inner, slope = gelu_parts(pre)
    grad_pre = jnp.where(text, mm(cot, wd_ref[1], NT), mm(cot, wd_ref[0], NT)) * slope
    for e in range(2):
        mine = text if e == 1 else jnp.logical_not(text)
        inner_e = jnp.where(mine, inner, 0.0)
        grad_e = jnp.where(mine, grad_pre, 0.0).astype(BF16)
        branch_ref[...] += mm(inner_e.astype(BF16), wd_ref[e])
        grad_ref[...] += mm(grad_e, wu_ref[e], NT)
        inner_t_ref[e] = jnp.transpose(inner_e).astype(BF16)
        slope_ref[e] = grad_e

    @pl.when(f == pl.num_programs(0) - 1)
    def _():
        out_ref[...] = branch_ref[:N, :]
        out_sib_ref[...] = branch_ref[N:, :].astype(BF16)
        grad_low_ref[...] = grad_ref[...].astype(BF16)


def experts(core, *operands):
    steps = 3
    shapes = [((N, 768), F32), ((N, 768), BF16), ((2 * N, 768), F32), ((2 * N, 768), BF16),
              ((2 * N, 768), F32), ((2 * N, 1), F32), ((768, 2 * N), BF16)]
    fixed = lambda shape: pl.BlockSpec(shape, lambda f, *_: (0,) * len(shape))
    return pl.pallas_call(
        expert_kernel,
        grid_spec=pltpu.PrefetchScalarGridSpec(
            num_scalar_prefetch=1,
            grid=(steps,),
            in_specs=[fixed(v.shape) for v in operands[:-2]] + [
                pl.BlockSpec((2, 768, FF_STEP), lambda f, at: (0, 0, at[CORE] * steps + f)),
                pl.BlockSpec((2, FF_STEP, 768), lambda f, at: (0, at[CORE] * steps + f, 0)),
            ],
            out_specs=[fixed(shape) for shape, _ in shapes] + [
                pl.BlockSpec((2, FF_STEP, 2 * N), lambda f, at: (0, f, 0)),
                pl.BlockSpec((2, 2 * N, FF_STEP), lambda f, at: (0, 0, f)),
            ],
            scratch_shapes=[pltpu.VMEM((2 * N, 768), BF16), pltpu.VMEM((2 * N, 768), F32)],
        ),
        out_shape=[jax.ShapeDtypeStruct(*v) for v in shapes] + [
            jax.ShapeDtypeStruct((2, steps * FF_STEP, 2 * N), BF16),
            jax.ShapeDtypeStruct((2, 2 * N, steps * FF_STEP), BF16)],
        compiler_params=pltpu.CompilerParams(
            vmem_limit_bytes=24 * 2**20, dimension_semantics=("arbitrary",)),
        cost_estimate=pl.CostEstimate(
            flops=8 * 2 * 512 * 768 * 1536 + 2 * 512 * 768 * 768, bytes_accessed=24 * 2**20,
            transcendentals=2 * 512 * 1536),
        name="experts",
    )(core, *operands)


def cells_kernel(g, at_slot, act_t_ref, grad_ref, inner_t_ref, cot_own_ref, cot_sib_ref, *refs):
    keep_ref, send_ref, up_acc, down_acc = refs[-4:]
    e = pl.program_id(0)
    up = mm(act_t_ref[...], grad_ref[...])
    up_acc[e, 0] = up[:, :256]
    up_acc[e, 1] = up[:, 256:]
    cot = jnp.concatenate([cot_own_ref[...], cot_sib_ref[...]], axis=0)
    down_acc[e] = mm(inner_t_ref[...], cot)

    def spill(target, base):
        def cell(i, carry):
            slot = g * 64 + base + i
            half = at_slot[192 + slot]
            rows = pl.ds(pl.multiple_of(at_slot[slot], 8), 24)
            below = pl.ds(pl.multiple_of(at_slot[384 + slot], 8), 24)
            target[i] = jnp.concatenate(
                [up_acc[0, half, rows, :], up_acc[1, half, rows, :],
                 down_acc[0, below, :], down_acc[1, below, :]], axis=0).astype(BF16)
            return carry
        lax.fori_loop(0, 32, cell, 0, unroll=4)

    @pl.when(e == 1)
    def _():
        spill(keep_ref, 0)
        spill(send_ref, 32)


def cells(g, table, act_t, grad_pre, inner_t, cot_own, cot_sib, gates):
    cot = pl.BlockSpec((N, 256), lambda e, t: (0, g))
    out = pl.BlockSpec((32, 96, 256), lambda e, t: (0, 0, 0))
    return pl.pallas_call(
        lambda *refs: cells_kernel(g, *refs),
        grid_spec=pltpu.PrefetchScalarGridSpec(
            num_scalar_prefetch=1,
            grid=(2,),
            in_specs=[
                pl.BlockSpec((768, 2 * N), lambda e, t: (0, 0)),
                pl.BlockSpec((None, 2 * N, FF_STEP), lambda e, t: (e, 0, g)),
                pl.BlockSpec((None, 1536, 2 * N), lambda e, t: (e, 0, 0)),
                cot, cot] + [ANYWHERE] * len(gates),
            out_specs=[out] * 2,
            scratch_shapes=[pltpu.VMEM((2, 2, 768, 256), F32), pltpu.VMEM((2, 1536, 256), F32)],
        ),
        out_shape=[jax.ShapeDtypeStruct((32, 96, 256), BF16)] * 2,
        compiler_params=pltpu.CompilerParams(
            vmem_limit_bytes=10 * 2**20, dimension_semantics=("arbitrary",)),
        cost_estimate=pl.CostEstimate(
            flops=4 * 2 * 512 * 768 * 512, bytes_accessed=8 * 2**20, transcendentals=0),
        name="cells",
    )(table, act_t, grad_pre, inner_t, cot_own, cot_sib, *gates)


def cell_places():
    table = np.zeros((32, 4, 4, 3, 4, 4, 4), np.int32)
    for r, s in np.ndindex(32, 4):
        here = {"z": r // 8, "y": r % 4, "x": (s // 2) * 2 + (r // 4) % 2}
        flips = (0, 1, 3, 2) if s % 2 else (0, 3, 1, 2)
        for g, order in enumerate(ORDERS):
            for slot in np.ndindex(4, 4, 4):
                at = {a: here[a] ^ flips[n] for a, n in zip(order, slot)}
                x_hi, x_lo = at["x"] // 2, at["x"] % 2
                table[(r, s, 0, g) + slot] = 24 * (at["z"] * 8 + x_lo * 4 + at["y"])
                table[(r, s, 1, g) + slot] = x_hi
                table[(r, s, 2, g) + slot] = 24 * (
                    (at["z"] % 2) * 32 + x_lo * 16 + at["y"] * 4 + x_hi * 2 + at["z"] // 2)
                table[(r, s, 3, g) + slot] = at["z"] * 16 + x_lo * 8 + at["y"] * 2 + x_hi
    coordinates = np.array([[n % 2, n % 4 // 2] + [0] * 126 for n in range(128)], np.int32)
    return np.concatenate([table.reshape(128, 768), coordinates], axis=1)


def add_up(parts):
    total = parts[0].astype(F32)
    for part in parts[1:]:
        total = total + part.astype(F32)
    return total.astype(BF16)


def in_hbm(values):
    return list(values)


def pass_kernel(gates, *refs):
    count = (len(refs) - gates) // 3
    for g in range(count):
        refs[2 * count + gates + g][...] = add_up([refs[2 * g][...], refs[2 * g + 1][...]])


ANYWHERE = pl.BlockSpec(memory_space=pl.ANY)


def pass_on(kept, arrived, name, gates=()):
    _, slots, rows, lanes = kept[0].shape
    block = max(slots // 4, 1)
    one = pl.BlockSpec((None, block, rows, lanes), lambda i: (1, i, 0, 0))
    return pl.pallas_call(
        lambda *refs: pass_kernel(len(gates), *refs),
        grid=(slots // block,),
        in_specs=[one] * (2 * len(kept)) + [ANYWHERE] * len(gates),
        out_specs=[pl.BlockSpec((block, rows, lanes), lambda i: (i, 0, 0))] * len(kept),
        out_shape=[jax.ShapeDtypeStruct((slots, rows, lanes), BF16)] * len(kept),
        compiler_params=pltpu.CompilerParams(vmem_limit_bytes=6 * 2**20),
        cost_estimate=pl.CostEstimate(
            flops=0, transcendentals=0, bytes_accessed=6 * len(kept) * slots * rows * lanes),
        name=name,
    )(*in_hbm([v for pair in zip(kept, arrived) for v in pair]), *gates)


def settle_kernel(groups, sizes, *refs):
    ins, outs = refs, refs[-2 * groups :]
    at = 0
    for g in range(groups):
        row = 0
        for size in sizes:
            for half in range(2):
                outs[2 * g + half][:, row : row + size, :] = add_up(
                    [ins[at + k][...] for k in range(3)])
                at += 3
            row += size


def settle(pieces, name):
    groups = len(pieces[0])
    sizes = [p[0][0].shape[2] for p in pieces]
    _, slots, _, lanes = pieces[0][0][0].shape
    half = slots // 2
    block = max(half // 4, 1)
    steps = half // block
    operands, specs = [], []
    for g in range(groups):
        for p, size in zip(pieces, sizes):
            for h in range(2):
                wide = pl.BlockSpec(
                    (None, block, size, lanes), lambda i, h=h: (0, i + h * steps, 0, 0))
                flat = pl.BlockSpec((block, size, lanes), lambda i, h=h: (i + h * steps, 0, 0))
                operands += list(p[g])
                specs += [wide, wide, flat]
    rows = sum(sizes)
    outs = pl.pallas_call(
        lambda *refs: settle_kernel(groups, sizes, *refs),
        grid=(steps,),
        in_specs=specs,
        out_specs=[pl.BlockSpec((block, rows, lanes), lambda i: (i, 0, 0))] * (2 * groups),
        out_shape=[jax.ShapeDtypeStruct((half, rows, lanes), BF16)] * (2 * groups),
        compiler_params=pltpu.CompilerParams(vmem_limit_bytes=8 * 2**20),
        cost_estimate=pl.CostEstimate(
            flops=0, transcendentals=0, bytes_accessed=8 * groups * slots * rows * lanes),
        name=name,
    )(*operands)
    shaped = [o.reshape(2, half // 2, rows, lanes) for o in outs]
    return shaped[0::2], shaped[1::2]


def finish_kernel(*refs):
    held_ref, down_ref = refs[-2:]
    for g in range(3):
        cell = add_up([refs[3 * g + k][...] for k in range(3)])
        held_ref[g, :48, :] = cell[:48]
        held_ref[g, 48:, :] = cell[96:]
        down_ref[g] = cell[48:96]


def finish(kept, first, second):
    wide = pl.BlockSpec((None, None, 128, 256), lambda i: (0, 0, 0, 0))
    flat = pl.BlockSpec((None, 128, 256), lambda i: (0, 0, 0))
    return pl.pallas_call(
        finish_kernel,
        grid=(1,),
        in_specs=[wide, wide, flat] * 3,
        out_specs=[pl.BlockSpec((3, 80, 256), lambda i: (0, 0, 0)),
                   pl.BlockSpec((3, 48, 256), lambda i: (0, 0, 0))],
        out_shape=[jax.ShapeDtypeStruct((3, 80, 256), BF16), jax.ShapeDtypeStruct((3, 48, 256), BF16)],
        compiler_params=pltpu.CompilerParams(vmem_limit_bytes=4 * 2**20),
        name="finish",
    )(*[v for g in range(3) for v in (kept[g], first[g], second[g])])


def after_kernel(values_ref, *refs):
    refs[-1][...] = values_ref[...]


def after(values, gates):
    return pl.pallas_call(
        after_kernel,
        in_specs=[WHOLE] + [ANYWHERE] * len(gates),
        out_specs=WHOLE,
        out_shape=jax.ShapeDtypeStruct(values.shape, values.dtype),
        compiler_params=pltpu.CompilerParams(vmem_limit_bytes=4 * 2**20),
        name="after",
    )(values, *gates)


def inputs_kernel(at_ref, q_ref, qb_ref, ka_ref, kb_ref, va_ref, vb_ref, own_ref, sib_ref, far_ref,
                  far_sib_ref, second_ref, wq_ref, wk_ref, wv_ref, keep_ref, send_ref, vec_ref):
    vectors = [jnp.zeros((1, 768), F32)] * 2
    wide = ((q_ref, qb_ref, wq_ref), (ka_ref, kb_ref, wk_ref), (va_ref, vb_ref, wv_ref))
    for n, ext_ref in enumerate((own_ref, sib_ref, far_ref, far_sib_ref)):
        rows = slice(n * N, (n + 1) * N)
        total = jnp.zeros((N, 768), F32)
        for a_ref, b_ref, w_ref in wide[0 if n < 2 else 1 :]:
            grads = jnp.concatenate([a_ref[rows, :], b_ref[rows, :]], axis=1)
            total += mm(grads, w_ref[...], NT)
        xhat, _ = normalize(ext_ref[:N, :].astype(F32))
        vectors[0] += jnp.sum(total * xhat, axis=0, keepdims=True)
        vectors[1] += jnp.sum(total, axis=0, keepdims=True)
        half = slice((n // 2) * N, (n // 2 + 1) * N)
        if n % 2 == 0:
            keep_ref[half, :] = total
        else:
            send_ref[half, :] = total.astype(BF16)
    vec_ref[0:1, :], vec_ref[1:2, :] = vectors
    vec_ref[2:4, :] = second_ref[...]


def input_partials(table, *operands):
    whole = lambda shape: pl.BlockSpec(shape, lambda i, *_: (0,) * len(shape))
    shapes = [((2 * N, 768), F32), ((2 * N, 768), BF16), ((4, 768), F32)]
    return pl.pallas_call(
        inputs_kernel,
        grid_spec=pltpu.PrefetchScalarGridSpec(
            num_scalar_prefetch=1,
            grid=(1,),
            in_specs=[whole(v.shape) for v in operands[:-1]]
            + [pl.BlockSpec((768, 384), lambda i, at, n=n: (0, 2 * n + at[CORE])) for n in range(3)],
            out_specs=[whole(shape) for shape, _ in shapes],
        ),
        out_shape=[jax.ShapeDtypeStruct(*v) for v in shapes],
        compiler_params=pltpu.CompilerParams(vmem_limit_bytes=8 * 2**20),
        cost_estimate=pl.CostEstimate(
            flops=2 * 768 * 384 * 512 * 5, bytes_accessed=8 * 2**20, transcendentals=0),
        name="input_partials",
    )(table, *operands, *[operands[-1]] * 2)


def tail_kernel(at_slot, act_ref, away_ref, q_ref, qb_ref, ka_ref, kb_ref, va_ref, vb_ref,
                att_own_ref, att_sib_ref, proj_ref, vec_ref, *refs):
    keeps, sends, acc, table = refs[-8:-5], refs[-5:-2], refs[-2], refs[-1]
    core = at_slot[CORE]

    def put(first, part, rows=slice(None)):
        for n in range(part.shape[1] // 128):
            column = first + n * 128
            lanes = slice(column % 256, column % 256 + 128)
            acc[column // 256, rows, lanes] = part[:, n * 128 : (n + 1) * 128]

    act, away = act_ref[...], away_ref[...]
    near_grads = jnp.concatenate([r[: 2 * N, :] for r in (q_ref, qb_ref, ka_ref, kb_ref, va_ref, vb_ref)], axis=1)
    away_grads = jnp.concatenate([r[2 * N :, :] for r in (ka_ref, kb_ref, va_ref, vb_ref)], axis=1)
    near = mm(act, near_grads, TN)
    put(0, near[:, :384])
    put(384, near[:, 384:] + mm(away, away_grads, TN))
    mine = pl.ds(pl.multiple_of(core * 384, 384), 384)
    other = pl.ds(pl.multiple_of((1 - core) * 384, 384), 384)
    put(1152, mm(att_own_ref[...], proj_ref[...], TN), mine)
    put(1152, mm(att_sib_ref[:N, :], proj_ref[N:, :], TN)
        + mm(att_sib_ref[N:, :], proj_ref[:N, :], TN), other)

    chip = lax.broadcasted_iota(jnp.int32, (64, 768), 0)
    owner = lax.broadcasted_iota(jnp.int32, (64, 768), 1) // 12
    feature = lax.broadcasted_iota(jnp.int32, (768, 128), 0) % 12
    lane = lax.broadcasted_iota(jnp.int32, (768, 128), 1)
    spread = jnp.zeros((64, 128), F32)
    for n in range(4):
        line = jnp.broadcast_to(vec_ref[n : n + 1, :], (64, 768))
        values = jnp.where(chip == owner, line, 0.0).astype(BF16)
        spread += mm(values, jnp.where(lane == feature + 12 * n, 1.0, 0.0).astype(BF16))
    table[...] = spread

    def spill(target, g, base):
        def cell(i, carry):
            slot = g * 64 + base + i
            rows = pl.ds(pl.multiple_of(at_slot[slot], 8), 24)
            part = acc[2 * g + at_slot[192 + slot], rows, :]
            if g == 0:
                row = table[pl.ds(at_slot[576 + slot], 1), :]
                extra = jnp.concatenate([jnp.broadcast_to(row, (8, 128)), jnp.zeros((8, 128), F32)], axis=1)
            else:
                extra = jnp.zeros((8, 256), F32)
            target[i] = jnp.concatenate([part, extra], axis=0).astype(BF16)
            return carry
        lax.fori_loop(0, 32, cell, 0, unroll=4)

    for g in range(3):
        spill(keeps[g], g, 0)
        spill(sends[g], g, 32)


def tail_cells(table, operands, gates):
    return pl.pallas_call(
        tail_kernel,
        in_specs=[SMALL] + [WHOLE] * len(operands) + [ANYWHERE] * len(gates),
        out_specs=[WHOLE] * 6,
        out_shape=[jax.ShapeDtypeStruct((32, 32, 256), BF16)] * 6,
        scratch_shapes=[pltpu.VMEM((6, 768, 256), F32), pltpu.VMEM((64, 128), F32)],
        compiler_params=pltpu.CompilerParams(vmem_limit_bytes=14 * 2**20),
        cost_estimate=pl.CostEstimate(
            flops=2 * 768 * 384 * 512 * 6, bytes_accessed=10 * 2**20, transcendentals=0),
        name="tail_cells",
    )(table, *operands, *gates)


def sum_core_kernel(own_ref, sib_ref, out_ref):
    out_ref[...] = (own_ref[...] + sib_ref[...].astype(F32)).astype(BF16)


def sum_core(own, sib):
    half = pl.BlockSpec((N, 768), lambda i: (1, 0))
    return pl.pallas_call(
        sum_core_kernel,
        grid=(1,),
        in_specs=[half, half],
        out_specs=pl.BlockSpec((N, 768), lambda i: (0, 0)),
        out_shape=jax.ShapeDtypeStruct((N, 768), BF16),
        compiler_params=pltpu.CompilerParams(vmem_limit_bytes=4 * 2**20),
        name="sum_core",
    )(own, sib)


def token_kernel(tokens_ref, hidden_ref, own_ref, sib_ref, far_ref, gains_ref, out_own_ref,
                 out_sib_ref, grad_ref, out_ref):
    grad = own_ref[...] + sib_ref[...].astype(F32) + far_ref[...].astype(F32)
    xhat, factor = normalize(tokens_ref[...].astype(F32))
    grad_ref[...] = hidden_ref[...] + normalize_back(grad, xhat, factor, gains_ref[0:1, :])
    out_ref[...] = (out_own_ref[...] + out_sib_ref[...].astype(F32)).astype(BF16)


def token_grads(tokens, hidden, own, sib, far, gains, out_own, out_sib):
    half = pl.BlockSpec((N, 768), lambda i: (0, 0))
    return pl.pallas_call(
        token_kernel,
        grid=(1,),
        in_specs=[half] * 5 + [pl.BlockSpec((4, 768), lambda i: (0, 0))] + [half] * 2,
        out_specs=[half] * 2,
        out_shape=[jax.ShapeDtypeStruct((N, 768), F32), jax.ShapeDtypeStruct((N, 768), BF16)],
        compiler_params=pltpu.CompilerParams(vmem_limit_bytes=8 * 2**20),
        name="token_grads",
    )(tokens, hidden, own, sib, far, gains, out_own, out_sib)


def assemble_kernel(at_ref, own_ref, near_ref, away_ref, cross_ref, down_ref, up_ref, qkv_ref, out_ref,
                    vec_ref, below_ref, held):
    core, far = at_ref[CORE], at_ref[FAR]
    held[far * 2 + core] = own_ref[...]
    held[far * 2 + 1 - core] = near_ref[...]
    held[2 - far * 2 + core] = away_ref[...]
    held[2 - far * 2 + 1 - core] = cross_ref[...]
    line = held[far * 2, 0, 64:, :128].astype(F32) + held[far * 2 + 1, 0, 64:, :128].astype(F32)
    vec_ref[...] = jnp.where(core == 0, line, pltpu.roll(line, 122, 1))[8:]
    row = lax.broadcasted_iota(jnp.int32, (24, 80), 0)
    column = lax.broadcasted_iota(jnp.int32, (24, 80), 1)
    wanted = (row // 8) * 24 + far * 12 + core * 6 + row % 8
    select = jnp.where((column == wanted) & (row % 8 < 6), 1.0, 0.0).astype(BF16)
    for x_hi in range(2):
        for c in range(2):
            for g in range(3):
                rows = mm(select, held[x_hi * 2 + c, g])
                first = c * 1536 + g * 512 + x_hi * 256
                for e in range(2):
                    up_ref[e, :, first : first + 256] = rows[8 * e : 8 * e + 6] * UP_FACTORS[e]
                for n in range(2):
                    at = g * 512 + x_hi * 256 + n * 128
                    kind, within = at // 384, at % 384 + c * 384
                    part = rows[16:22, n * 128 : (n + 1) * 128]
                    if kind < 3:
                        qkv_ref[:, kind * 768 + within : kind * 768 + within + 128] = part
                    else:
                        out_ref[:, within : within + 128] = part
    for g in range(3):
        part = down_ref[g].astype(F32)
        for e in range(2):
            below_ref[e, :, g * 256 : (g + 1) * 256] = part[24 * e : 24 * e + 24] * UP_FACTORS[e]


def assemble(table, *parts):
    return pl.pallas_call(
        assemble_kernel,
        in_specs=[SMALL] + [WHOLE] * 5,
        out_specs=[WHOLE] * 5,
        out_shape=[
            jax.ShapeDtypeStruct((2, 6, 3072), F32),
            jax.ShapeDtypeStruct((6, 2304), F32),
            jax.ShapeDtypeStruct((6, 768), F32),
            jax.ShapeDtypeStruct((8, 128), F32),
            jax.ShapeDtypeStruct((2, 24, 768), F32),
        ],
        scratch_shapes=[pltpu.VMEM((4, 3, 80, 256), BF16)],
        compiler_params=pltpu.CompilerParams(vmem_limit_bytes=4 * 2**20),
        name="assemble",
    )(table, *parts)

def shards(tokens, first_gain, first_shift, w_qkv, w_out, second_gain, second_shift,
           w_up, w_down, modality, segments, partner, cotangent):
    table = lax.dynamic_index_in_dim(
        jnp.asarray(cell_places()), lax.axis_index(BOTH), 0, keepdims=False)
    gains = jnp.stack([first_gain, first_shift, second_gain, second_shift])

    own = marked(partner, tokens[0], segments, modality)
    away = swap_far(own)
    sib = swap_core(own)
    cot_own = cotangent[0]
    cot_sib = swap_core(cot_own)

    act1, marks, queries, k_near, v_near, qx = project(table, own, sib, gains, w_qkv, True)
    away_sib = swap_core(after(away, [qx]))
    act1_away, marks_away, k_away, v_away = project(table, away, away_sib, gains, w_qkv, False)
    attended, lse = attend_forward(
        queries, k_near, k_away, v_near, v_away, qx, marks, marks_away)
    attended_sib = swap_core(attended)

    out_own, out_sib, grad_act2, grad_low, xhat2, factor2, act_t, inner_t, grad_pre = experts(
        table, attended, attended_sib, own, sib, cot_own, cot_sib, marks, gains, w_out, w_up, w_down)
    grad_sib = swap_core(grad_low)
    ff_kept, ff_first, gates = [], [], []
    for g in range(3):
        keep, gone = cells(g, table, act_t, grad_pre, inner_t, cot_own, cot_sib, gates)
        ff_kept.append(keep.reshape(2, 16, 96, 256))
        ff_first.append(send(gone.reshape(2, 16, 96, 256), axis_step(ORDERS[g][0], True)))
        gates = [keep, grad_sib]
    hidden_grad, grad_att, proj_half, vectors = middle(
        table, grad_act2, grad_sib, xhat2, factor2, cot_own, cot_sib, gains, w_out)

    def along(stage, first, values):
        return [send(v, axis_step(ORDERS[g][stage], first)) for g, v in enumerate(values)]

    taken = (queries, k_near, k_away, v_near, v_away, grad_att, attended, qx, marks, marks_away, lse)
    q_a, k_a, v_a = attend_backward(taken, 0, 2, ())
    passed = pass_on(ff_kept, ff_first, "pass_first", [q_a])
    ff_second = along(0, False, passed)
    q_b, k_b, v_b = attend_backward(taken, 2, 1, passed)
    partial_own, partial_low, vectors = input_partials(
        table, q_a, q_b, k_a, k_b, v_a, v_b, own, sib, away, away_sib, vectors, w_qkv)
    tail = tail_cells(table, (
        act1, act1_away, q_a, q_b, k_a, k_b, v_a, v_b, attended, attended_sib, proj_half, vectors),
        ff_second)

    kept = [v.reshape(2, 16, 32, 256) for v in tail[:3]]
    first = along(0, True, [v.reshape(2, 16, 32, 256) for v in tail[3:]])
    partial_sib = swap_core(partial_low)
    from_far = swap_far(sum_core(partial_own, partial_sib))
    second = along(0, False, pass_on(kept, first, "pass_tail", [from_far]))
    kept, sent = settle(
        [list(zip(ff_kept, ff_first, ff_second)), list(zip(kept, first, second))], "settle_all")
    first = along(1, True, sent)
    second = along(1, False, pass_on(kept, first, "pass_second"))
    kept, sent = settle([list(zip(kept, first, second))], "settle_second")
    first = along(2, True, sent)
    second = along(2, False, pass_on(kept, first, "pass_third"))
    held, down_held = finish(kept, first, second)

    near, beyond = swap_core(held), swap_far(held)
    cross = send(held, lambda x, y, z, c: (x ^ 2, y, z, 1 - c))
    below = send(down_held, lambda x, y, z, c: (x, y, 2 * c + z % 2, z // 2))
    up_grad, qkv_grad, out_grad, line, down_grad = assemble(
        table, held, near, beyond, cross, below)

    token_grad, layer_output = token_grads(
        tokens[0], hidden_grad, partial_own, partial_sib, from_far, gains, out_own, swap_core(out_sib))

    return (
        layer_output[None], token_grad[None], line[0, :6], line[0, 12:18], qkv_grad, out_grad,
        line[0, 24:30], line[0, 36:42], up_grad, down_grad)


def solution(mesh):
    cut = P("rows", "seq", None)
    flat = P(BOTH)
    placed = (cut,) + (P(),) * 8 + (P("rows", "seq"), P("rows", "seq"), P("rows", None), cut)
    return jax.shard_map(
        shards, mesh=mesh, in_specs=placed,
        out_specs=(cut, cut, flat, flat, P(BOTH, None), P(BOTH, None), flat, flat,
                   P(None, BOTH, None), P(None, BOTH, None)),
        check_vma=False)
```

```python
import jax
import jax.numpy as jnp
import numpy as np
from jax import lax
from jax.experimental import pallas as pl
from jax.experimental.pallas import tpu as pltpu
from jax.sharding import PartitionSpec as P

HD = 64
OWN = 6
CORE, FAR = 768, 769
IMG = 197
NIMG = 4
BOTH = ("rows", "seq")
F32 = jnp.float32
BF16 = jnp.bfloat16
MASKED = -1e30


def route(step):
    pairs = []
    for r in range(32):
        z, x_lo, y = r // 8, (r // 4) % 2, r % 4
        for s in range(4):
            x, c = (s // 2) * 2 + x_lo, s % 2
            tx, ty, tz, tc = step(x, y, z, c)
            target = (tz * 8 + (tx % 2) * 4 + ty) * 4 + (tx // 2) * 2 + tc
            pairs.append((r * 4 + s, target))
    return pairs


def send(values, step):
    return lax.ppermute(values, BOTH, route(step))


def swap_core(values):
    return send(values, lambda x, y, z, c: (x, y, z, 1 - c))


def swap_far(values):
    return send(values, lambda x, y, z, c: (x ^ 2, y, z, c))


def axis_step(axis, first):
    def step(x, y, z, c):
        flip = 1 if (c == 0) == first else 3
        at = {"x": x, "y": y, "z": z}
        at[axis] ^= flip
        return (at["x"], at["y"], at["z"], c)

    return step


UP_FACTORS = (1024 / (2 * 788), 1024 / (2 * 236))
ORDERS = (("x", "y", "z"), ("y", "z", "x"), ("z", "x", "y"))


def normalize(inputs):
    centred = inputs - jnp.mean(inputs, axis=-1, keepdims=True)
    factor = lax.rsqrt(jnp.mean(centred * centred, axis=-1, keepdims=True) + 1e-05)
    return centred * factor, factor


def normalize_back(grad, xhat, factor, gain):
    gy = grad * gain
    mean_gy = jnp.mean(gy, axis=-1, keepdims=True)
    mean_gx = jnp.mean(gy * xhat, axis=-1, keepdims=True)
    return factor * (gy - mean_gy - xhat * mean_gx)


SMALL = pl.BlockSpec(memory_space=pltpu.SMEM)
WHOLE = pl.BlockSpec(memory_space=pltpu.VMEM)
N = 256


def marked_kernel(partner, tokens_ref, segments_ref, modality_ref, out_ref):
    segments = segments_ref[...]
    tag = jnp.zeros(segments.shape, jnp.int32)
    for n in range(8):
        tag = jnp.where(segments == n, partner[0, n], tag)
    marks = jnp.concatenate(
        [tag, modality_ref[...], jnp.zeros((1, 256), jnp.int32)], axis=1).astype(F32)
    out_ref[:N, :] = tokens_ref[...]
    out_ref[N:, :] = jnp.concatenate([marks, jnp.zeros((15, 768), F32)], axis=0).astype(BF16)


def marked(partner, tokens, segments, modality):
    return pl.pallas_call(
        marked_kernel,
        in_specs=[SMALL, WHOLE, WHOLE, WHOLE],
        out_specs=WHOLE,
        out_shape=jax.ShapeDtypeStruct((N + 16, 768), BF16),
        compiler_params=pltpu.CompilerParams(vmem_limit_bytes=60 * 2**20),
        name="marked",
    )(partner, tokens, segments, modality)


def mark_lanes(ext):
    row = ext[N:, :].astype(F32)
    place = lax.broadcasted_iota(jnp.int32, (128, N), 0)
    tag = jnp.broadcast_to(row[:1, :N], (128, N))
    kind = jnp.broadcast_to(row[:1, N : 2 * N], (128, N))
    hot = jnp.where((place < NIMG) & (place.astype(F32) == tag), 1.0, 0.0)
    return jnp.transpose(jnp.where(place == 8, kind, hot))


def project_kernel(at_ref, near, a_ref, b_ref, gains_ref, *refs):
    count = 3 if near else 2
    weights, outs = refs[:count], refs[count:]
    for n, ext_ref in enumerate((a_ref, b_ref)):
        rows = slice(n * N, (n + 1) * N)
        ext = ext_ref[...]
        xhat, _ = normalize(ext[:N].astype(F32))
        act = (xhat * gains_ref[0:1, :] + gains_ref[1:2, :]).astype(BF16)
        outs[0][rows, :] = act
        marks = mark_lanes(ext)
        outs[1][rows, :] = marks.astype(BF16)
        for m in range(count):
            part = mm(act, weights[m][...])
            outs[2 + m][rows, :] = (0.125 * part if near and m == 0 else part).astype(BF16)
        if near:
            lane = lax.broadcasted_iota(jnp.int32, marks.shape, 1)
            outs[5][rows, :] = jnp.where((lane < NIMG) & (marks == 0.0), MASKED, 0.0).astype(BF16)


def project(table, first, second, gains, w_qkv, near):
    kinds = (0, 1, 2) if near else (1, 2)
    sizes = [768, 128] + [384] * len(kinds) + ([128] if near else [])
    whole = lambda shape: pl.BlockSpec(shape, lambda i, at: (0, 0))
    return pl.pallas_call(
        lambda at_ref, *refs: project_kernel(at_ref, near, *refs),
        grid_spec=pltpu.PrefetchScalarGridSpec(
            num_scalar_prefetch=1,
            grid=(1,),
            in_specs=[whole((N + 16, 768))] * 2 + [whole((4, 768))]
            + [pl.BlockSpec((768, 384), lambda i, at, n=n: (0, 2 * n + at[CORE])) for n in kinds],
            out_specs=[whole((2 * N, size)) for size in sizes],
        ),
        out_shape=[jax.ShapeDtypeStruct((2 * N, size), BF16) for size in sizes],
        compiler_params=pltpu.CompilerParams(vmem_limit_bytes=6 * 2**20),
        cost_estimate=pl.CostEstimate(
            flops=2 * 512 * 768 * 384 * len(kinds), bytes_accessed=4 * 2**20, transcendentals=0),
        name="project_near" if near else "project_away",
    )(table, first, second, gains, *[w_qkv] * len(kinds))


def middle_kernel(place, grad_ref, sib_ref, xhat_ref, factor_ref, cot_own_ref, cot_sib_ref,
                  gains_ref, w_out_ref, hidden_ref, att_ref, proj_ref, vec_ref):
    core = place[CORE]
    for n, cot_ref in enumerate((cot_own_ref, cot_sib_ref)):
        rows, other = slice(n * N, (n + 1) * N), slice((1 - n) * N, (2 - n) * N)
        grad = grad_ref[rows, :] + sib_ref[other, :].astype(F32)
        xhat = xhat_ref[rows, :]
        total = cot_ref[...].astype(F32) + normalize_back(grad, xhat, factor_ref[rows, :], gains_ref[2:3, :])
        low = total.astype(BF16)
        if n == 0:
            hidden_ref[...] = total
            vec_ref[0:1, :] = jnp.sum(grad * xhat, axis=0, keepdims=True)
            vec_ref[1:2, :] = jnp.sum(grad, axis=0, keepdims=True)
        mine = w_out_ref[pl.ds(pl.multiple_of(core * 384, 384), 384), :]
        att_ref[rows, :] = mm(low, mine, NT).astype(BF16)
        proj_ref[rows, :] = jnp.where(core == 0, low[:, :384], low[:, 384:])


def middle(place, *operands):
    return pl.pallas_call(
        middle_kernel,
        in_specs=[SMALL] + [WHOLE] * len(operands),
        out_specs=[WHOLE] * 4,
        out_shape=[
            jax.ShapeDtypeStruct((N, 768), F32),
            jax.ShapeDtypeStruct((2 * N, 384), BF16),
            jax.ShapeDtypeStruct((2 * N, 384), BF16),
            jax.ShapeDtypeStruct((2, 768), F32),
        ],
        compiler_params=pltpu.CompilerParams(vmem_limit_bytes=6 * 2**20),
        cost_estimate=pl.CostEstimate(
            flops=2 * 512 * 768 * 384, bytes_accessed=8 * 2**20, transcendentals=0),
        name="middle",
    )(place, *operands)


def gelu_parts(pre):
    phi = 0.5 * (1.0 + lax.erf(pre * 0.7071067811865476))
    slope = phi + pre * (0.3989422804014327 * jnp.exp(-0.5 * pre * pre))
    return pre * phi, slope


NT = (((1,), (1,)), ((), ()))
TN = (((0,), (0,)), ((), ()))
NN = (((1,), (0,)), ((), ()))


def mm(left, right, dims=NN):
    return lax.dot_general(left, right, dims, preferred_element_type=F32)


def head_lanes(shape, h):
    lane = lax.broadcasted_iota(jnp.int32, shape, len(shape) - 1)
    return (lane >= HD) == (h == 1)


def turned(values):
    return jnp.transpose(values.astype(F32)).astype(BF16)


def stacked(near_ref, away_ref):
    return jnp.concatenate([near_ref[...], away_ref[...]], axis=0)


def forward_kernel(q_ref, kn_ref, ka_ref, vn_ref, va_ref, qx_ref, xn_ref, xa_ref, out_ref, lse_ref):
    keys = jnp.concatenate([stacked(kn_ref, ka_ref), stacked(xn_ref, xa_ref)], axis=1)
    values = stacked(vn_ref, va_ref)
    q_pair = q_ref[...]
    lanes = head_lanes(q_pair.shape, 0)
    values_t = turned(values)
    value_rows = lax.broadcasted_iota(jnp.int32, values_t.shape, 0) < HD
    mixed = []
    for h in range(2):
        mine = lanes if h == 0 else jnp.logical_not(lanes)
        mine_values = value_rows if h == 0 else jnp.logical_not(value_rows)
        query = jnp.concatenate([jnp.where(mine, q_pair, 0), qx_ref[...]], axis=1)
        scores = mm(keys, query, NT)
        peak = jnp.max(scores, axis=0, keepdims=True)
        weights = jnp.exp(scores - peak).astype(BF16)
        both = mm(jnp.where(mine_values, values_t, 1), weights)
        total = both[127:128, :] if h == 0 else both[0:1, :]
        mixed.append(both * (1.0 / total))
        lse_ref[0, h : h + 1, :] = peak + jnp.log(total)
    out_rows = lax.broadcasted_iota(jnp.int32, mixed[0].shape, 0) < HD
    out_ref[...] = jnp.transpose(jnp.where(out_rows, mixed[0], mixed[1])).astype(BF16)


BY_PAIR = pl.BlockSpec((2 * N, 128), lambda p: (0, p))
FIXED = pl.BlockSpec((2 * N, 128), lambda p: (0, 0))


def attend_forward(*operands):
    return pl.pallas_call(
        forward_kernel,
        grid=(3,),
        in_specs=[BY_PAIR] * 5 + [FIXED] * 3,
        out_specs=[BY_PAIR, pl.BlockSpec((1, 2, 2 * N), lambda p: (p, 0, 0))],
        out_shape=[
            jax.ShapeDtypeStruct((2 * N, 384), BF16),
            jax.ShapeDtypeStruct((3, 2, 2 * N), F32),
        ],
        compiler_params=pltpu.CompilerParams(vmem_limit_bytes=6 * 2**20),
        cost_estimate=pl.CostEstimate(
            flops=2 * 2 * OWN * 512 * 1024 * 256, bytes_accessed=4 * 2**20,
            transcendentals=OWN * 512 * 1024),
        name="attend_forward",
    )(*operands)


def backward_kernel(q_ref, kn_ref, ka_ref, vn_ref, va_ref, do_ref, o_ref, qx_ref, xn_ref, xa_ref,
                    lse_ref, *refs):
    dq_ref, dk_ref, dv_ref = refs[-3:]
    k_pair, values = stacked(kn_ref, ka_ref), stacked(vn_ref, va_ref)
    keys = jnp.concatenate([k_pair, stacked(xn_ref, xa_ref)], axis=1)
    q_pair, grads = q_ref[...], do_ref[...]
    lanes = head_lanes(q_pair.shape, 0)
    product = grads.astype(F32) * o_ref[...].astype(F32)
    k_turned = turned(k_pair)
    rows = lax.broadcasted_iota(jnp.int32, (128, 2 * N), 0) < HD
    dq = jnp.zeros((128, 2 * N), F32)
    dk = jnp.zeros(k_pair.shape, F32)
    dv = jnp.zeros(k_pair.shape, F32)
    for h in range(2):
        mine = lanes if h == 0 else jnp.logical_not(lanes)
        q_head = jnp.where(mine, q_pair, 0)
        g_head = jnp.where(mine, grads, 0)
        dot_row = jnp.transpose(jnp.sum(jnp.where(mine, product, 0.0), axis=1, keepdims=True))
        scores = mm(keys, jnp.concatenate([q_head, qx_ref[...]], axis=1), NT)
        prob = jnp.exp(scores - lse_ref[0, h : h + 1, :])
        dv += mm(prob.astype(BF16), g_head)
        grad_prob = mm(values, g_head, NT)
        grad_scores = (prob * (grad_prob - dot_row)).astype(BF16)
        dk += mm(grad_scores, q_head)
        part = mm(k_turned, grad_scores)
        dq += jnp.where(rows if h == 0 else jnp.logical_not(rows), part, 0.0)
    dq_ref[...] = jnp.transpose(dq).astype(BF16) * jnp.asarray(0.125, BF16)
    dk_ref[...] = dk.astype(BF16)
    dv_ref[...] = dv.astype(BF16)


def attend_backward(operands, first, pairs, gates):
    by_pair = pl.BlockSpec((2 * N, 128), lambda p: (0, first + p))
    sizes = (2 * N, 4 * N, 4 * N)
    return pl.pallas_call(
        backward_kernel,
        grid=(pairs,),
        in_specs=[by_pair] * 7 + [FIXED] * 3
        + [pl.BlockSpec((1, 2, 2 * N), lambda p: (first + p, 0, 0))]
        + [pl.BlockSpec(memory_space=pl.ANY)] * len(gates),
        out_specs=[pl.BlockSpec((size, 128), lambda p: (0, p)) for size in sizes],
        out_shape=[jax.ShapeDtypeStruct((size, pairs * 128), BF16) for size in sizes],
        compiler_params=pltpu.CompilerParams(vmem_limit_bytes=10 * 2**20),
        cost_estimate=pl.CostEstimate(
            flops=2 * 5 * 2 * pairs * 512 * 1024 * 256, bytes_accessed=6 * 2**20,
            transcendentals=2 * pairs * 512 * 1024),
        name="attend_backward",
    )(*operands, *gates)


FF_STEP = 512
EXPERT_MB = 40
CELLS_MB = 28


def expert_kernel(at_ref, att_own_ref, att_sib_ref, own_ref, sib_ref, cot_own_ref, cot_sib_ref,
                  marks_ref, gains_ref, w_out_ref, wu_ref, wd_ref,
                  out_ref, out_sib_ref, grad_ref, grad_low_ref, xhat_ref, factor_ref, act_t_ref,
                  inner_t_ref, slope_ref, act_acc, branch_ref):
    f = pl.program_id(0)
    core = at_ref[CORE]

    @pl.when(f == 0)
    def _():
        mine = w_out_ref[pl.ds(pl.multiple_of(core * 384, 384), 384), :]
        other = w_out_ref[pl.ds(pl.multiple_of((1 - core) * 384, 384), 384), :]
        for n, ext_ref in enumerate((own_ref, sib_ref)):
            rows, theirs = slice(n * N, (n + 1) * N), slice((1 - n) * N, (2 - n) * N)
            hidden = ext_ref[:N, :].astype(F32) + (
                mm(att_own_ref[rows, :], mine) + mm(att_sib_ref[theirs, :], other))
            xhat, factor = normalize(hidden)
            xhat_ref[rows, :] = xhat
            factor_ref[rows, :] = factor
            act = xhat * gains_ref[2:3, :] + gains_ref[3:4, :]
            act_acc[rows, :] = act.astype(BF16)
            act_t_ref[:, rows] = jnp.transpose(act).astype(BF16)
            if n == 0:
                branch_ref[rows, :] = hidden
            else:
                branch_ref[rows, :] = jnp.zeros_like(hidden)
        grad_ref[...] = jnp.zeros(grad_ref.shape, F32)

    act = act_acc[...]
    cot = jnp.concatenate([cot_own_ref[...], cot_sib_ref[...]], axis=0)
    text = marks_ref[:, 8:9].astype(F32) > 0.0
    pre = jnp.where(text, mm(act, wu_ref[1]), mm(act, wu_ref[0]))
    inner, slope = gelu_parts(pre)
    grad_pre = jnp.where(text, mm(cot, wd_ref[1], NT), mm(cot, wd_ref[0], NT)) * slope
    inner_t = jnp.transpose(inner)
    text_row = turned(marks_ref[...])[8:9, :].astype(F32) > 0.0
    inner_t_ref[0] = jnp.where(text_row, 0.0, inner_t).astype(BF16)
    inner_t_ref[1] = jnp.where(text_row, inner_t, 0.0).astype(BF16)
    for e in range(2):
        mine = text if e == 1 else jnp.logical_not(text)
        inner_e = jnp.where(mine, inner, 0.0)
        grad_e = jnp.where(mine, grad_pre, 0.0).astype(BF16)
        branch_ref[...] += mm(inner_e.astype(BF16), wd_ref[e])
        grad_ref[...] += mm(grad_e, wu_ref[e], NT)
        slope_ref[e] = grad_e

    @pl.when(f == pl.num_programs(0) - 1)
    def _():
        out_ref[...] = branch_ref[:N, :]
        out_sib_ref[...] = branch_ref[N:, :].astype(BF16)
        grad_low_ref[...] = grad_ref[...].astype(BF16)


def experts(core, *operands):
    steps = 3
    shapes = [((N, 768), F32), ((N, 768), BF16), ((2 * N, 768), F32), ((2 * N, 768), BF16),
              ((2 * N, 768), F32), ((2 * N, 1), F32), ((768, 2 * N), BF16)]
    fixed = lambda shape: pl.BlockSpec(shape, lambda f, *_: (0,) * len(shape))
    return pl.pallas_call(
        expert_kernel,
        grid_spec=pltpu.PrefetchScalarGridSpec(
            num_scalar_prefetch=1,
            grid=(steps,),
            in_specs=[fixed(v.shape) for v in operands[:-2]] + [
                pl.BlockSpec((2, 768, FF_STEP), lambda f, at: (0, 0, at[CORE] * steps + f)),
                pl.BlockSpec((2, FF_STEP, 768), lambda f, at: (0, at[CORE] * steps + f, 0)),
            ],
            out_specs=[fixed(shape) for shape, _ in shapes] + [
                pl.BlockSpec((2, FF_STEP, 2 * N), lambda f, at: (0, f, 0)),
                pl.BlockSpec((2, 2 * N, FF_STEP), lambda f, at: (0, 0, f)),
            ],
            scratch_shapes=[pltpu.VMEM((2 * N, 768), BF16), pltpu.VMEM((2 * N, 768), F32)],
        ),
        out_shape=[jax.ShapeDtypeStruct(*v) for v in shapes] + [
            jax.ShapeDtypeStruct((2, steps * FF_STEP, 2 * N), BF16),
            jax.ShapeDtypeStruct((2, 2 * N, steps * FF_STEP), BF16)],
        compiler_params=pltpu.CompilerParams(
            vmem_limit_bytes=24 * 2**20, dimension_semantics=("arbitrary",)),
        cost_estimate=pl.CostEstimate(
            flops=8 * 2 * 512 * 768 * 1536 + 2 * 512 * 768 * 768, bytes_accessed=24 * 2**20,
            transcendentals=2 * 512 * 1536),
        name="experts",
    )(core, *operands)


def cells_kernel(g, at_slot, act_t_ref, grad_ref, inner_t_ref, cot_own_ref, cot_sib_ref, *refs):
    keep_ref, send_ref, up_acc, down_acc = refs[-4:]
    e = pl.program_id(0)
    up = mm(act_t_ref[...], grad_ref[...])
    up_acc[e, 0] = up[:, :256]
    up_acc[e, 1] = up[:, 256:]
    cot = jnp.concatenate([cot_own_ref[...], cot_sib_ref[...]], axis=0)
    down_acc[e] = mm(inner_t_ref[...], cot)

    def spill(target, base):
        def cell(i, carry):
            slot = g * 64 + base + i
            half = at_slot[192 + slot]
            rows = pl.ds(pl.multiple_of(at_slot[slot], 8), 24)
            below = pl.ds(pl.multiple_of(at_slot[384 + slot], 8), 24)
            target[i] = jnp.concatenate(
                [up_acc[0, half, rows, :], up_acc[1, half, rows, :],
                 down_acc[0, below, :], down_acc[1, below, :]], axis=0).astype(BF16)
            return carry
        lax.fori_loop(0, 32, cell, 0, unroll=4)

    @pl.when(e == 1)
    def _():
        spill(keep_ref, 0)
        spill(send_ref, 32)


def cells(g, table, act_t, grad_pre, inner_t, cot_own, cot_sib, gates):
    cot = pl.BlockSpec((N, 256), lambda e, t: (0, g))
    out = pl.BlockSpec((32, 96, 256), lambda e, t: (0, 0, 0))
    return pl.pallas_call(
        lambda *refs: cells_kernel(g, *refs),
        grid_spec=pltpu.PrefetchScalarGridSpec(
            num_scalar_prefetch=1,
            grid=(2,),
            in_specs=[
                pl.BlockSpec((768, 2 * N), lambda e, t: (0, 0)),
                pl.BlockSpec((None, 2 * N, FF_STEP), lambda e, t: (e, 0, g)),
                pl.BlockSpec((None, 1536, 2 * N), lambda e, t: (e, 0, 0)),
                cot, cot] + [ANYWHERE] * len(gates),
            out_specs=[out] * 2,
            scratch_shapes=[pltpu.VMEM((2, 2, 768, 256), F32), pltpu.VMEM((2, 1536, 256), F32)],
        ),
        out_shape=[jax.ShapeDtypeStruct((32, 96, 256), BF16)] * 2,
        compiler_params=pltpu.CompilerParams(
            vmem_limit_bytes=10 * 2**20, dimension_semantics=("arbitrary",)),
        cost_estimate=pl.CostEstimate(
            flops=4 * 2 * 512 * 768 * 512, bytes_accessed=8 * 2**20, transcendentals=0),
        name="cells",
    )(table, act_t, grad_pre, inner_t, cot_own, cot_sib, *gates)


def cell_places():
    table = np.zeros((32, 4, 4, 3, 4, 4, 4), np.int32)
    for r, s in np.ndindex(32, 4):
        here = {"z": r // 8, "y": r % 4, "x": (s // 2) * 2 + (r // 4) % 2}
        flips = (0, 1, 3, 2) if s % 2 else (0, 3, 1, 2)
        for g, order in enumerate(ORDERS):
            for slot in np.ndindex(4, 4, 4):
                at = {a: here[a] ^ flips[n] for a, n in zip(order, slot)}
                x_hi, x_lo = at["x"] // 2, at["x"] % 2
                table[(r, s, 0, g) + slot] = 24 * (at["z"] * 8 + x_lo * 4 + at["y"])
                table[(r, s, 1, g) + slot] = x_hi
                table[(r, s, 2, g) + slot] = 24 * (
                    (at["z"] % 2) * 32 + x_lo * 16 + at["y"] * 4 + x_hi * 2 + at["z"] // 2)
                table[(r, s, 3, g) + slot] = at["z"] * 16 + x_lo * 8 + at["y"] * 2 + x_hi
    coordinates = np.array([[n % 2, n % 4 // 2] + [0] * 126 for n in range(128)], np.int32)
    return np.concatenate([table.reshape(128, 768), coordinates], axis=1)


def add_up(parts):
    total = parts[0].astype(F32)
    for part in parts[1:]:
        total = total + part.astype(F32)
    return total.astype(BF16)


def in_hbm(values):
    return list(values)


def pass_kernel(gates, *refs):
    count = (len(refs) - gates) // 3
    for g in range(count):
        refs[2 * count + gates + g][...] = add_up([refs[2 * g][...], refs[2 * g + 1][...]])


ANYWHERE = pl.BlockSpec(memory_space=pl.ANY)


def pass_on(kept, arrived, name, gates=()):
    _, slots, rows, lanes = kept[0].shape
    block = max(slots // 4, 1)
    one = pl.BlockSpec((None, block, rows, lanes), lambda i: (1, i, 0, 0))
    return pl.pallas_call(
        lambda *refs: pass_kernel(len(gates), *refs),
        grid=(slots // block,),
        in_specs=[one] * (2 * len(kept)) + [ANYWHERE] * len(gates),
        out_specs=[pl.BlockSpec((block, rows, lanes), lambda i: (i, 0, 0))] * len(kept),
        out_shape=[jax.ShapeDtypeStruct((slots, rows, lanes), BF16)] * len(kept),
        compiler_params=pltpu.CompilerParams(vmem_limit_bytes=6 * 2**20),
        cost_estimate=pl.CostEstimate(
            flops=0, transcendentals=0, bytes_accessed=6 * len(kept) * slots * rows * lanes),
        name=name,
    )(*in_hbm([v for pair in zip(kept, arrived) for v in pair]), *gates)


def settle_kernel(groups, sizes, *refs):
    ins, outs = refs, refs[-2 * groups :]
    at = 0
    for g in range(groups):
        row = 0
        for size in sizes:
            for half in range(2):
                outs[2 * g + half][:, row : row + size, :] = add_up(
                    [ins[at + k][...] for k in range(3)])
                at += 3
            row += size


def settle(pieces, name):
    groups = len(pieces[0])
    sizes = [p[0][0].shape[2] for p in pieces]
    _, slots, _, lanes = pieces[0][0][0].shape
    half = slots // 2
    block = max(half // 4, 1)
    steps = half // block
    operands, specs = [], []
    for g in range(groups):
        for p, size in zip(pieces, sizes):
            for h in range(2):
                wide = pl.BlockSpec(
                    (None, block, size, lanes), lambda i, h=h: (0, i + h * steps, 0, 0))
                flat = pl.BlockSpec((block, size, lanes), lambda i, h=h: (i + h * steps, 0, 0))
                operands += list(p[g])
                specs += [wide, wide, flat]
    rows = sum(sizes)
    outs = pl.pallas_call(
        lambda *refs: settle_kernel(groups, sizes, *refs),
        grid=(steps,),
        in_specs=specs,
        out_specs=[pl.BlockSpec((block, rows, lanes), lambda i: (i, 0, 0))] * (2 * groups),
        out_shape=[jax.ShapeDtypeStruct((half, rows, lanes), BF16)] * (2 * groups),
        compiler_params=pltpu.CompilerParams(vmem_limit_bytes=8 * 2**20),
        cost_estimate=pl.CostEstimate(
            flops=0, transcendentals=0, bytes_accessed=8 * groups * slots * rows * lanes),
        name=name,
    )(*operands)
    shaped = [o.reshape(2, half // 2, rows, lanes) for o in outs]
    return shaped[0::2], shaped[1::2]


def finish_kernel(*refs):
    held_ref, down_ref = refs[-2:]
    for g in range(3):
        cell = add_up([refs[3 * g + k][...] for k in range(3)])
        held_ref[g, :48, :] = cell[:48]
        held_ref[g, 48:, :] = cell[96:]
        down_ref[g] = cell[48:96]


def finish(kept, first, second):
    wide = pl.BlockSpec((None, None, 128, 256), lambda i: (0, 0, 0, 0))
    flat = pl.BlockSpec((None, 128, 256), lambda i: (0, 0, 0))
    return pl.pallas_call(
        finish_kernel,
        grid=(1,),
        in_specs=[wide, wide, flat] * 3,
        out_specs=[pl.BlockSpec((3, 80, 256), lambda i: (0, 0, 0)),
                   pl.BlockSpec((3, 48, 256), lambda i: (0, 0, 0))],
        out_shape=[jax.ShapeDtypeStruct((3, 80, 256), BF16), jax.ShapeDtypeStruct((3, 48, 256), BF16)],
        compiler_params=pltpu.CompilerParams(vmem_limit_bytes=4 * 2**20),
        name="finish",
    )(*[v for g in range(3) for v in (kept[g], first[g], second[g])])


def after_kernel(values_ref, *refs):
    refs[-1][...] = values_ref[...]


def after(values, gates):
    return pl.pallas_call(
        after_kernel,
        in_specs=[WHOLE] + [ANYWHERE] * len(gates),
        out_specs=WHOLE,
        out_shape=jax.ShapeDtypeStruct(values.shape, values.dtype),
        compiler_params=pltpu.CompilerParams(vmem_limit_bytes=4 * 2**20),
        name="after",
    )(values, *gates)


def inputs_kernel(at_ref, q_ref, qb_ref, ka_ref, kb_ref, va_ref, vb_ref, own_ref, sib_ref, far_ref,
                  far_sib_ref, second_ref, wq_ref, wk_ref, wv_ref, keep_ref, send_ref, vec_ref):
    vectors = [jnp.zeros((1, 768), F32)] * 2
    wide = ((q_ref, qb_ref, wq_ref), (ka_ref, kb_ref, wk_ref), (va_ref, vb_ref, wv_ref))
    for n, ext_ref in enumerate((own_ref, sib_ref, far_ref, far_sib_ref)):
        rows = slice(n * N, (n + 1) * N)
        total = jnp.zeros((N, 768), F32)
        for a_ref, b_ref, w_ref in wide[0 if n < 2 else 1 :]:
            grads = jnp.concatenate([a_ref[rows, :], b_ref[rows, :]], axis=1)
            total += mm(grads, w_ref[...], NT)
        xhat, _ = normalize(ext_ref[:N, :].astype(F32))
        vectors[0] += jnp.sum(total * xhat, axis=0, keepdims=True)
        vectors[1] += jnp.sum(total, axis=0, keepdims=True)
        half = slice((n // 2) * N, (n // 2 + 1) * N)
        if n % 2 == 0:
            keep_ref[half, :] = total
        else:
            send_ref[half, :] = total.astype(BF16)
    vec_ref[0:1, :], vec_ref[1:2, :] = vectors
    vec_ref[2:4, :] = second_ref[...]


def input_partials(table, *operands):
    whole = lambda shape: pl.BlockSpec(shape, lambda i, *_: (0,) * len(shape))
    shapes = [((2 * N, 768), F32), ((2 * N, 768), BF16), ((4, 768), F32)]
    return pl.pallas_call(
        inputs_kernel,
        grid_spec=pltpu.PrefetchScalarGridSpec(
            num_scalar_prefetch=1,
            grid=(1,),
            in_specs=[whole(v.shape) for v in operands[:-1]]
            + [pl.BlockSpec((768, 384), lambda i, at, n=n: (0, 2 * n + at[CORE])) for n in range(3)],
            out_specs=[whole(shape) for shape, _ in shapes],
        ),
        out_shape=[jax.ShapeDtypeStruct(*v) for v in shapes],
        compiler_params=pltpu.CompilerParams(vmem_limit_bytes=8 * 2**20),
        cost_estimate=pl.CostEstimate(
            flops=2 * 768 * 384 * 512 * 5, bytes_accessed=8 * 2**20, transcendentals=0),
        name="input_partials",
    )(table, *operands, *[operands[-1]] * 2)


def tail_kernel(at_slot, act_ref, away_ref, q_ref, qb_ref, ka_ref, kb_ref, va_ref, vb_ref,
                att_own_ref, att_sib_ref, proj_ref, vec_ref, *refs):
    keeps, sends, acc, table = refs[-8:-5], refs[-5:-2], refs[-2], refs[-1]
    core = at_slot[CORE]

    def put(first, part, rows=slice(None)):
        for n in range(part.shape[1] // 128):
            column = first + n * 128
            lanes = slice(column % 256, column % 256 + 128)
            acc[column // 256, rows, lanes] = part[:, n * 128 : (n + 1) * 128]

    act, away = act_ref[...], away_ref[...]
    near_grads = jnp.concatenate([r[: 2 * N, :] for r in (q_ref, qb_ref, ka_ref, kb_ref, va_ref, vb_ref)], axis=1)
    away_grads = jnp.concatenate([r[2 * N :, :] for r in (ka_ref, kb_ref, va_ref, vb_ref)], axis=1)
    near = mm(act, near_grads, TN)
    put(0, near[:, :384])
    put(384, near[:, 384:] + mm(away, away_grads, TN))
    mine = pl.ds(pl.multiple_of(core * 384, 384), 384)
    other = pl.ds(pl.multiple_of((1 - core) * 384, 384), 384)
    put(1152, mm(att_own_ref[...], proj_ref[...], TN), mine)
    put(1152, mm(att_sib_ref[:N, :], proj_ref[N:, :], TN)
        + mm(att_sib_ref[N:, :], proj_ref[:N, :], TN), other)

    chip = lax.broadcasted_iota(jnp.int32, (64, 768), 0)
    owner = lax.broadcasted_iota(jnp.int32, (64, 768), 1) // 12
    feature = lax.broadcasted_iota(jnp.int32, (768, 128), 0) % 12
    lane = lax.broadcasted_iota(jnp.int32, (768, 128), 1)
    spread = jnp.zeros((64, 128), F32)
    for n in range(4):
        line = jnp.broadcast_to(vec_ref[n : n + 1, :], (64, 768))
        values = jnp.where(chip == owner, line, 0.0).astype(BF16)
        spread += mm(values, jnp.where(lane == feature + 12 * n, 1.0, 0.0).astype(BF16))
    table[...] = spread

    def spill(target, g, base):
        def cell(i, carry):
            slot = g * 64 + base + i
            rows = pl.ds(pl.multiple_of(at_slot[slot], 8), 24)
            part = acc[2 * g + at_slot[192 + slot], rows, :]
            if g == 0:
                row = table[pl.ds(at_slot[576 + slot], 1), :]
                extra = jnp.concatenate([jnp.broadcast_to(row, (8, 128)), jnp.zeros((8, 128), F32)], axis=1)
            else:
                extra = jnp.zeros((8, 256), F32)
            target[i] = jnp.concatenate([part, extra], axis=0).astype(BF16)
            return carry
        lax.fori_loop(0, 32, cell, 0, unroll=4)

    for g in range(3):
        spill(keeps[g], g, 0)
        spill(sends[g], g, 32)


def tail_cells(table, operands, gates):
    return pl.pallas_call(
        tail_kernel,
        in_specs=[SMALL] + [WHOLE] * len(operands) + [ANYWHERE] * len(gates),
        out_specs=[WHOLE] * 6,
        out_shape=[jax.ShapeDtypeStruct((32, 32, 256), BF16)] * 6,
        scratch_shapes=[pltpu.VMEM((6, 768, 256), F32), pltpu.VMEM((64, 128), F32)],
        compiler_params=pltpu.CompilerParams(vmem_limit_bytes=14 * 2**20),
        cost_estimate=pl.CostEstimate(
            flops=2 * 768 * 384 * 512 * 6, bytes_accessed=10 * 2**20, transcendentals=0),
        name="tail_cells",
    )(table, *operands, *gates)


def sum_core_kernel(own_ref, sib_ref, *refs):
    refs[-1][...] = (own_ref[...] + sib_ref[...].astype(F32)).astype(BF16)


def sum_core(own, sib, gates):
    half = pl.BlockSpec((N, 768), lambda i: (1, 0))
    return pl.pallas_call(
        sum_core_kernel,
        grid=(1,),
        in_specs=[half, half] + [ANYWHERE] * len(gates),
        out_specs=pl.BlockSpec((N, 768), lambda i: (0, 0)),
        out_shape=jax.ShapeDtypeStruct((N, 768), BF16),
        compiler_params=pltpu.CompilerParams(vmem_limit_bytes=4 * 2**20),
        name="sum_core",
    )(own, sib, *gates)


def token_kernel(tokens_ref, hidden_ref, own_ref, sib_ref, far_ref, gains_ref, out_own_ref,
                 out_sib_ref, grad_ref, out_ref):
    grad = own_ref[...] + sib_ref[...].astype(F32) + far_ref[...].astype(F32)
    xhat, factor = normalize(tokens_ref[...].astype(F32))
    grad_ref[...] = hidden_ref[...] + normalize_back(grad, xhat, factor, gains_ref[0:1, :])
    out_ref[...] = (out_own_ref[...] + out_sib_ref[...].astype(F32)).astype(BF16)


def token_grads(tokens, hidden, own, sib, far, gains, out_own, out_sib):
    half = pl.BlockSpec((N, 768), lambda i: (0, 0))
    return pl.pallas_call(
        token_kernel,
        grid=(1,),
        in_specs=[half] * 5 + [pl.BlockSpec((4, 768), lambda i: (0, 0))] + [half] * 2,
        out_specs=[half] * 2,
        out_shape=[jax.ShapeDtypeStruct((N, 768), F32), jax.ShapeDtypeStruct((N, 768), BF16)],
        compiler_params=pltpu.CompilerParams(vmem_limit_bytes=8 * 2**20),
        name="token_grads",
    )(tokens, hidden, own, sib, far, gains, out_own, out_sib)


def assemble_kernel(at_ref, own_ref, near_ref, away_ref, cross_ref, down_ref, up_ref, qkv_ref, out_ref,
                    vec_ref, below_ref, held):
    core, far = at_ref[CORE], at_ref[FAR]
    held[far * 2 + core] = own_ref[...]
    held[far * 2 + 1 - core] = near_ref[...]
    held[2 - far * 2 + core] = away_ref[...]
    held[2 - far * 2 + 1 - core] = cross_ref[...]
    line = held[far * 2, 0, 64:, :128].astype(F32) + held[far * 2 + 1, 0, 64:, :128].astype(F32)
    vec_ref[...] = jnp.where(core == 0, line, pltpu.roll(line, 122, 1))[8:]
    row = lax.broadcasted_iota(jnp.int32, (24, 80), 0)
    column = lax.broadcasted_iota(jnp.int32, (24, 80), 1)
    wanted = (row // 8) * 24 + far * 12 + core * 6 + row % 8
    select = jnp.where((column == wanted) & (row % 8 < 6), 1.0, 0.0).astype(BF16)
    for x_hi in range(2):
        for c in range(2):
            for g in range(3):
                rows = mm(select, held[x_hi * 2 + c, g])
                first = c * 1536 + g * 512 + x_hi * 256
                for e in range(2):
                    up_ref[e, :, first : first + 256] = rows[8 * e : 8 * e + 6] * UP_FACTORS[e]
                for n in range(2):
                    at = g * 512 + x_hi * 256 + n * 128
                    kind, within = at // 384, at % 384 + c * 384
                    part = rows[16:22, n * 128 : (n + 1) * 128]
                    if kind < 3:
                        qkv_ref[:, kind * 768 + within : kind * 768 + within + 128] = part
                    else:
                        out_ref[:, within : within + 128] = part
    for g in range(3):
        part = down_ref[g].astype(F32)
        for e in range(2):
            below_ref[e, :, g * 256 : (g + 1) * 256] = part[24 * e : 24 * e + 24] * UP_FACTORS[e]


def assemble(table, *parts):
    return pl.pallas_call(
        assemble_kernel,
        in_specs=[SMALL] + [WHOLE] * 5,
        out_specs=[WHOLE] * 5,
        out_shape=[
            jax.ShapeDtypeStruct((2, 6, 3072), F32),
            jax.ShapeDtypeStruct((6, 2304), F32),
            jax.ShapeDtypeStruct((6, 768), F32),
            jax.ShapeDtypeStruct((8, 128), F32),
            jax.ShapeDtypeStruct((2, 24, 768), F32),
        ],
        scratch_shapes=[pltpu.VMEM((4, 3, 80, 256), BF16)],
        compiler_params=pltpu.CompilerParams(vmem_limit_bytes=4 * 2**20),
        name="assemble",
    )(table, *parts)

def shards(tokens, first_gain, first_shift, w_qkv, w_out, second_gain, second_shift,
           w_up, w_down, modality, segments, partner, cotangent):
    table = lax.dynamic_index_in_dim(
        jnp.asarray(cell_places()), lax.axis_index(BOTH), 0, keepdims=False)
    gains = jnp.stack([first_gain, first_shift, second_gain, second_shift])

    own = marked(partner, tokens[0], segments, modality)
    away = swap_far(own)
    sib = swap_core(own)
    cot_own = cotangent[0]
    cot_sib = swap_core(cot_own)

    act1, marks, queries, k_near, v_near, qx = project(table, own, sib, gains, w_qkv, True)
    away_sib = swap_core(after(away, [qx]))
    act1_away, marks_away, k_away, v_away = project(table, away, away_sib, gains, w_qkv, False)
    attended, lse = attend_forward(
        queries, k_near, k_away, v_near, v_away, qx, marks, marks_away)
    attended_sib = swap_core(attended)

    out_own, out_sib, grad_act2, grad_low, xhat2, factor2, act_t, inner_t, grad_pre = experts(
        table, attended, attended_sib, own, sib, cot_own, cot_sib, marks, gains, w_out, w_up, w_down)
    grad_sib = swap_core(grad_low)
    ff_kept, ff_first, gates = [], [], []
    for g in range(3):
        keep, gone = cells(g, table, act_t, grad_pre, inner_t, cot_own, cot_sib, gates)
        ff_kept.append(keep.reshape(2, 16, 96, 256))
        ff_first.append(send(gone.reshape(2, 16, 96, 256), axis_step(ORDERS[g][0], True)))
        gates = [keep, grad_sib]
    hidden_grad, grad_att, proj_half, vectors = middle(
        table, grad_act2, grad_sib, xhat2, factor2, cot_own, cot_sib, gains, w_out)

    def along(stage, first, values):
        return [send(v, axis_step(ORDERS[g][stage], first)) for g, v in enumerate(values)]

    taken = (queries, k_near, k_away, v_near, v_away, grad_att, attended, qx, marks, marks_away, lse)
    q_a, k_a, v_a = attend_backward(taken, 0, 2, ())
    q_b, k_b, v_b = attend_backward(taken, 2, 1, ())
    partial_own, partial_low, vectors = input_partials(
        table, q_a, q_b, k_a, k_b, v_a, v_b, own, sib, away, away_sib, vectors, w_qkv)
    partial_sib = swap_core(partial_low)
    tail = tail_cells(table, (
        act1, act1_away, q_a, q_b, k_a, k_b, v_a, v_b, attended, attended_sib, proj_half, vectors), ())
    passed = pass_on(ff_kept, ff_first, "pass_first", [tail[0]])
    ff_second = along(0, False, passed)

    kept = [v.reshape(2, 16, 32, 256) for v in tail[:3]]
    first = along(0, True, [v.reshape(2, 16, 32, 256) for v in tail[3:]])
    second = along(0, False, pass_on(kept, first, "pass_tail"))
    kept, sent = settle(
        [list(zip(ff_kept, ff_first, ff_second)), list(zip(kept, first, second))], "settle_all")
    first = along(1, True, sent)
    second = along(1, False, pass_on(kept, first, "pass_second"))
    kept, sent = settle([list(zip(kept, first, second))], "settle_second")
    first = along(2, True, sent)
    passed = pass_on(kept, first, "pass_third")
    second = along(2, False, passed)
    from_far = swap_far(sum_core(partial_own, partial_sib, passed))
    held, down_held = finish(kept, first, second)

    near, beyond = swap_core(held), swap_far(held)
    cross = send(held, lambda x, y, z, c: (x ^ 2, y, z, 1 - c))
    below = send(down_held, lambda x, y, z, c: (x, y, 2 * c + z % 2, z // 2))
    up_grad, qkv_grad, out_grad, line, down_grad = assemble(
        table, held, near, beyond, cross, below)

    token_grad, layer_output = token_grads(
        tokens[0], hidden_grad, partial_own, partial_sib, from_far, gains, out_own, swap_core(out_sib))

    return (
        layer_output[None], token_grad[None], line[0, :6], line[0, 12:18], qkv_grad, out_grad,
        line[0, 24:30], line[0, 36:42], up_grad, down_grad)


def solution(mesh):
    cut = P("rows", "seq", None)
    flat = P(BOTH)
    placed = (cut,) + (P(),) * 8 + (P("rows", "seq"), P("rows", "seq"), P("rows", None), cut)
    return jax.shard_map(
        shards, mesh=mesh, in_specs=placed,
        out_specs=(cut, cut, flat, flat, P(BOTH, None), P(BOTH, None), flat, flat,
                   P(None, BOTH, None), P(None, BOTH, None)),
        check_vma=False)
```

```python
import jax
import jax.numpy as jnp
import numpy as np
from jax import lax
from jax.experimental import pallas as pl
from jax.experimental.pallas import tpu as pltpu
from jax.sharding import PartitionSpec as P

HD = 64
OWN = 6
CORE, FAR = 768, 769
IMG = 197
NIMG = 4
BOTH = ("rows", "seq")
F32 = jnp.float32
BF16 = jnp.bfloat16
MASKED = -1e30


def route(step):
    pairs = []
    for r in range(32):
        z, x_lo, y = r // 8, (r // 4) % 2, r % 4
        for s in range(4):
            x, c = (s // 2) * 2 + x_lo, s % 2
            tx, ty, tz, tc = step(x, y, z, c)
            target = (tz * 8 + (tx % 2) * 4 + ty) * 4 + (tx // 2) * 2 + tc
            pairs.append((r * 4 + s, target))
    return pairs


def send(values, step):
    return lax.ppermute(values, BOTH, route(step))


def swap_core(values):
    return send(values, lambda x, y, z, c: (x, y, z, 1 - c))


def swap_far(values):
    return send(values, lambda x, y, z, c: (x ^ 2, y, z, c))


def axis_step(axis, first):
    def step(x, y, z, c):
        flip = 1 if (c == 0) == first else 3
        at = {"x": x, "y": y, "z": z}
        at[axis] ^= flip
        return (at["x"], at["y"], at["z"], c)

    return step


UP_FACTORS = (1024 / (2 * 788), 1024 / (2 * 236))
ORDERS = (("x", "y", "z"), ("y", "z", "x"), ("z", "x", "y"))


def normalize(inputs):
    centred = inputs - jnp.mean(inputs, axis=-1, keepdims=True)
    factor = lax.rsqrt(jnp.mean(centred * centred, axis=-1, keepdims=True) + 1e-05)
    return centred * factor, factor


def normalize_back(grad, xhat, factor, gain):
    gy = grad * gain
    mean_gy = jnp.mean(gy, axis=-1, keepdims=True)
    mean_gx = jnp.mean(gy * xhat, axis=-1, keepdims=True)
    return factor * (gy - mean_gy - xhat * mean_gx)


SMALL = pl.BlockSpec(memory_space=pltpu.SMEM)
WHOLE = pl.BlockSpec(memory_space=pltpu.VMEM)
N = 256


def marked_kernel(partner, tokens_ref, segments_ref, modality_ref, out_ref):
    segments = segments_ref[...]
    tag = jnp.zeros(segments.shape, jnp.int32)
    for n in range(8):
        tag = jnp.where(segments == n, partner[0, n], tag)
    marks = jnp.concatenate(
        [tag, modality_ref[...], jnp.zeros((1, 256), jnp.int32)], axis=1).astype(F32)
    out_ref[:N, :] = tokens_ref[...]
    out_ref[N:, :] = jnp.concatenate([marks, jnp.zeros((15, 768), F32)], axis=0).astype(BF16)


def marked(partner, tokens, segments, modality):
    return pl.pallas_call(
        marked_kernel,
        in_specs=[SMALL, WHOLE, WHOLE, WHOLE],
        out_specs=WHOLE,
        out_shape=jax.ShapeDtypeStruct((N + 16, 768), BF16),
        compiler_params=pltpu.CompilerParams(vmem_limit_bytes=60 * 2**20),
        name="marked",
    )(partner, tokens, segments, modality)


def mark_lanes(ext):
    row = ext[N:, :].astype(F32)
    place = lax.broadcasted_iota(jnp.int32, (128, N), 0)
    tag = jnp.broadcast_to(row[:1, :N], (128, N))
    kind = jnp.broadcast_to(row[:1, N : 2 * N], (128, N))
    hot = jnp.where((place < NIMG) & (place.astype(F32) == tag), 1.0, 0.0)
    return jnp.transpose(jnp.where(place == 8, kind, hot))


def project_kernel(at_ref, near, a_ref, b_ref, gains_ref, *refs):
    count = 3 if near else 2
    weights, outs = refs[:count], refs[count:]
    for n, ext_ref in enumerate((a_ref, b_ref)):
        rows = slice(n * N, (n + 1) * N)
        ext = ext_ref[...]
        xhat, _ = normalize(ext[:N].astype(F32))
        act = (xhat * gains_ref[0:1, :] + gains_ref[1:2, :]).astype(BF16)
        outs[0][rows, :] = act
        marks = mark_lanes(ext)
        outs[1][rows, :] = marks.astype(BF16)
        for m in range(count):
            part = mm(act, weights[m][...])
            outs[2 + m][rows, :] = (0.125 * part if near and m == 0 else part).astype(BF16)
        if near:
            lane = lax.broadcasted_iota(jnp.int32, marks.shape, 1)
            outs[5][rows, :] = jnp.where((lane < NIMG) & (marks == 0.0), MASKED, 0.0).astype(BF16)


def project(table, first, second, gains, w_qkv, near):
    kinds = (0, 1, 2) if near else (1, 2)
    sizes = [768, 128] + [384] * len(kinds) + ([128] if near else [])
    whole = lambda shape: pl.BlockSpec(shape, lambda i, at: (0, 0))
    return pl.pallas_call(
        lambda at_ref, *refs: project_kernel(at_ref, near, *refs),
        grid_spec=pltpu.PrefetchScalarGridSpec(
            num_scalar_prefetch=1,
            grid=(1,),
            in_specs=[whole((N + 16, 768))] * 2 + [whole((4, 768))]
            + [pl.BlockSpec((768, 384), lambda i, at, n=n: (0, 2 * n + at[CORE])) for n in kinds],
            out_specs=[whole((2 * N, size)) for size in sizes],
        ),
        out_shape=[jax.ShapeDtypeStruct((2 * N, size), BF16) for size in sizes],
        compiler_params=pltpu.CompilerParams(vmem_limit_bytes=6 * 2**20),
        cost_estimate=pl.CostEstimate(
            flops=2 * 512 * 768 * 384 * len(kinds), bytes_accessed=4 * 2**20, transcendentals=0),
        name="project_near" if near else "project_away",
    )(table, first, second, gains, *[w_qkv] * len(kinds))


def middle_kernel(place, grad_ref, sib_ref, xhat_ref, factor_ref, cot_own_ref, cot_sib_ref,
                  gains_ref, w_out_ref, hidden_ref, att_ref, proj_ref, vec_ref):
    core = place[CORE]
    for n, cot_ref in enumerate((cot_own_ref, cot_sib_ref)):
        rows, other = slice(n * N, (n + 1) * N), slice((1 - n) * N, (2 - n) * N)
        grad = grad_ref[rows, :] + sib_ref[other, :].astype(F32)
        xhat = xhat_ref[rows, :]
        total = cot_ref[...].astype(F32) + normalize_back(grad, xhat, factor_ref[rows, :], gains_ref[2:3, :])
        low = total.astype(BF16)
        if n == 0:
            hidden_ref[...] = total
            vec_ref[0:1, :] = jnp.sum(grad * xhat, axis=0, keepdims=True)
            vec_ref[1:2, :] = jnp.sum(grad, axis=0, keepdims=True)
        mine = w_out_ref[pl.ds(pl.multiple_of(core * 384, 384), 384), :]
        att_ref[rows, :] = mm(low, mine, NT).astype(BF16)
        proj_ref[rows, :] = jnp.where(core == 0, low[:, :384], low[:, 384:])


def middle(place, *operands):
    return pl.pallas_call(
        middle_kernel,
        in_specs=[SMALL] + [WHOLE] * len(operands),
        out_specs=[WHOLE] * 4,
        out_shape=[
            jax.ShapeDtypeStruct((N, 768), F32),
            jax.ShapeDtypeStruct((2 * N, 384), BF16),
            jax.ShapeDtypeStruct((2 * N, 384), BF16),
            jax.ShapeDtypeStruct((2, 768), F32),
        ],
        compiler_params=pltpu.CompilerParams(vmem_limit_bytes=6 * 2**20),
        cost_estimate=pl.CostEstimate(
            flops=2 * 512 * 768 * 384, bytes_accessed=8 * 2**20, transcendentals=0),
        name="middle",
    )(place, *operands)


def gelu_parts(pre):
    phi = 0.5 * (1.0 + lax.erf(pre * 0.7071067811865476))
    slope = phi + pre * (0.3989422804014327 * jnp.exp(-0.5 * pre * pre))
    return pre * phi, slope


NT = (((1,), (1,)), ((), ()))
TN = (((0,), (0,)), ((), ()))
NN = (((1,), (0,)), ((), ()))


def mm(left, right, dims=NN):
    return lax.dot_general(left, right, dims, preferred_element_type=F32)


def head_lanes(shape, h):
    lane = lax.broadcasted_iota(jnp.int32, shape, len(shape) - 1)
    return (lane >= HD) == (h == 1)


def turned(values):
    return jnp.transpose(values.astype(F32)).astype(BF16)


def stacked(near_ref, away_ref):
    return jnp.concatenate([near_ref[...], away_ref[...]], axis=0)


def forward_kernel(q_ref, kn_ref, ka_ref, vn_ref, va_ref, qx_ref, xn_ref, xa_ref, out_ref, lse_ref):
    keys = jnp.concatenate([stacked(kn_ref, ka_ref), stacked(xn_ref, xa_ref)], axis=1)
    values = stacked(vn_ref, va_ref)
    q_pair = q_ref[...]
    lanes = head_lanes(q_pair.shape, 0)
    values_t = turned(values)
    value_rows = lax.broadcasted_iota(jnp.int32, values_t.shape, 0) < HD
    mixed = []
    for h in range(2):
        mine = lanes if h == 0 else jnp.logical_not(lanes)
        mine_values = value_rows if h == 0 else jnp.logical_not(value_rows)
        query = jnp.concatenate([jnp.where(mine, q_pair, 0), qx_ref[...]], axis=1)
        scores = mm(keys, query, NT)
        peak = jnp.max(scores, axis=0, keepdims=True)
        weights = jnp.exp(scores - peak).astype(BF16)
        both = mm(jnp.where(mine_values, values_t, 1), weights)
        total = both[127:128, :] if h == 0 else both[0:1, :]
        mixed.append(both * (1.0 / total))
        lse_ref[0, h : h + 1, :] = peak + jnp.log(total)
    out_rows = lax.broadcasted_iota(jnp.int32, mixed[0].shape, 0) < HD
    out_ref[...] = jnp.transpose(jnp.where(out_rows, mixed[0], mixed[1])).astype(BF16)


BY_PAIR = pl.BlockSpec((2 * N, 128), lambda p: (0, p))
FIXED = pl.BlockSpec((2 * N, 128), lambda p: (0, 0))


def attend_forward(*operands):
    return pl.pallas_call(
        forward_kernel,
        grid=(3,),
        in_specs=[BY_PAIR] * 5 + [FIXED] * 3,
        out_specs=[BY_PAIR, pl.BlockSpec((1, 2, 2 * N), lambda p: (p, 0, 0))],
        out_shape=[
            jax.ShapeDtypeStruct((2 * N, 384), BF16),
            jax.ShapeDtypeStruct((3, 2, 2 * N), F32),
        ],
        compiler_params=pltpu.CompilerParams(vmem_limit_bytes=6 * 2**20),
        cost_estimate=pl.CostEstimate(
            flops=2 * 2 * OWN * 512 * 1024 * 256, bytes_accessed=4 * 2**20,
            transcendentals=OWN * 512 * 1024),
        name="attend_forward",
    )(*operands)


def backward_kernel(q_ref, kn_ref, ka_ref, vn_ref, va_ref, do_ref, o_ref, qx_ref, xn_ref, xa_ref,
                    lse_ref, *refs):
    dq_ref, dk_ref, dv_ref = refs[-3:]
    k_pair, values = stacked(kn_ref, ka_ref), stacked(vn_ref, va_ref)
    keys = jnp.concatenate([k_pair, stacked(xn_ref, xa_ref)], axis=1)
    q_pair, grads = q_ref[...], do_ref[...]
    lanes = head_lanes(q_pair.shape, 0)
    product = grads.astype(F32) * o_ref[...].astype(F32)
    k_turned = turned(k_pair)
    rows = lax.broadcasted_iota(jnp.int32, (128, 2 * N), 0) < HD
    dq = jnp.zeros((128, 2 * N), F32)
    dk = jnp.zeros(k_pair.shape, F32)
    dv = jnp.zeros(k_pair.shape, F32)
    for h in range(2):
        mine = lanes if h == 0 else jnp.logical_not(lanes)
        q_head = jnp.where(mine, q_pair, 0)
        g_head = jnp.where(mine, grads, 0)
        dot_row = jnp.transpose(jnp.sum(jnp.where(mine, product, 0.0), axis=1, keepdims=True))
        scores = mm(keys, jnp.concatenate([q_head, qx_ref[...]], axis=1), NT)
        prob = jnp.exp(scores - lse_ref[0, h : h + 1, :])
        dv += mm(prob.astype(BF16), g_head)
        grad_prob = mm(values, g_head, NT)
        grad_scores = (prob * (grad_prob - dot_row)).astype(BF16)
        dk += mm(grad_scores, q_head)
        part = mm(k_turned, grad_scores)
        dq += jnp.where(rows if h == 0 else jnp.logical_not(rows), part, 0.0)
    dq_ref[...] = jnp.transpose(dq).astype(BF16) * jnp.asarray(0.125, BF16)
    dk_ref[...] = dk.astype(BF16)
    dv_ref[...] = dv.astype(BF16)


def attend_backward(operands, first, pairs, gates):
    by_pair = pl.BlockSpec((2 * N, 128), lambda p: (0, first + p))
    sizes = (2 * N, 4 * N, 4 * N)
    return pl.pallas_call(
        backward_kernel,
        grid=(pairs,),
        in_specs=[by_pair] * 7 + [FIXED] * 3
        + [pl.BlockSpec((1, 2, 2 * N), lambda p: (first + p, 0, 0))]
        + [pl.BlockSpec(memory_space=pl.ANY)] * len(gates),
        out_specs=[pl.BlockSpec((size, 128), lambda p: (0, p)) for size in sizes],
        out_shape=[jax.ShapeDtypeStruct((size, pairs * 128), BF16) for size in sizes],
        compiler_params=pltpu.CompilerParams(vmem_limit_bytes=10 * 2**20),
        cost_estimate=pl.CostEstimate(
            flops=2 * 5 * 2 * pairs * 512 * 1024 * 256, bytes_accessed=6 * 2**20,
            transcendentals=2 * pairs * 512 * 1024),
        name="attend_backward",
    )(*operands, *gates)


FF_STEP = 512
E_STEP = 256
EXPERT_MB = 40
CELLS_MB = 28


def expert_kernel(at_ref, att_own_ref, att_sib_ref, own_ref, sib_ref, cot_own_ref, cot_sib_ref,
                  marks_ref, gains_ref, w_out_ref, wu_ref, wd_ref,
                  hidden_ref, grad_ref, xhat_ref, factor_ref, act_t_ref, inner_t_ref, slope_ref,
                  act_acc):
    f = pl.program_id(0)
    core = at_ref[CORE]

    @pl.when(f == 0)
    def _():
        mine = w_out_ref[pl.ds(pl.multiple_of(core * 384, 384), 384), :]
        other = w_out_ref[pl.ds(pl.multiple_of((1 - core) * 384, 384), 384), :]
        for n, ext_ref in enumerate((own_ref, sib_ref)):
            rows, theirs = slice(n * N, (n + 1) * N), slice((1 - n) * N, (2 - n) * N)
            hidden = ext_ref[:N, :].astype(F32) + (
                mm(att_own_ref[rows, :], mine) + mm(att_sib_ref[theirs, :], other))
            xhat, factor = normalize(hidden)
            xhat_ref[rows, :] = xhat
            factor_ref[rows, :] = factor
            act = xhat * gains_ref[2:3, :] + gains_ref[3:4, :]
            act_acc[rows, :] = act.astype(BF16)
            act_t_ref[:, rows] = jnp.transpose(act).astype(BF16)
            if n == 0:
                hidden_ref[...] = hidden
        grad_ref[...] = jnp.zeros(grad_ref.shape, F32)

    act = act_acc[...]
    cot = jnp.concatenate([cot_own_ref[...], cot_sib_ref[...]], axis=0)
    text = marks_ref[:, 8:9].astype(F32) > 0.0
    pre = jnp.where(text, mm(act, wu_ref[1]), mm(act, wu_ref[0]))
    inner, slope = gelu_parts(pre)
    grad_pre = jnp.where(text, mm(cot, wd_ref[1], NT), mm(cot, wd_ref[0], NT)) * slope
    inner_t = jnp.transpose(inner)
    text_row = turned(marks_ref[...])[8:9, :].astype(F32) > 0.0
    inner_t_ref[0] = jnp.where(text_row, 0.0, inner_t).astype(BF16)
    inner_t_ref[1] = jnp.where(text_row, inner_t, 0.0).astype(BF16)
    slope_ref[0] = jnp.where(text, 0.0, grad_pre).astype(BF16)
    slope_ref[1] = jnp.where(text, grad_pre, 0.0).astype(BF16)
    grad_ref[...] += mm(slope_ref[0], wu_ref[0], NT) + mm(slope_ref[1], wu_ref[1], NT)


def experts(core, *operands):
    steps = 1536 // E_STEP
    shapes = [((N, 768), F32), ((2 * N, 768), F32), ((2 * N, 768), F32), ((2 * N, 1), F32),
              ((768, 2 * N), BF16)]
    fixed = lambda shape: pl.BlockSpec(shape, lambda f, *_: (0,) * len(shape))
    return pl.pallas_call(
        expert_kernel,
        grid_spec=pltpu.PrefetchScalarGridSpec(
            num_scalar_prefetch=1,
            grid=(steps,),
            in_specs=[fixed(v.shape) for v in operands[:-2]] + [
                pl.BlockSpec((2, 768, E_STEP), lambda f, at: (0, 0, at[CORE] * steps + f)),
                pl.BlockSpec((2, E_STEP, 768), lambda f, at: (0, at[CORE] * steps + f, 0)),
            ],
            out_specs=[fixed(shape) for shape, _ in shapes] + [
                pl.BlockSpec((2, E_STEP, 2 * N), lambda f, at: (0, f, 0)),
                pl.BlockSpec((2, 2 * N, E_STEP), lambda f, at: (0, 0, f)),
            ],
            scratch_shapes=[pltpu.VMEM((2 * N, 768), BF16)],
        ),
        out_shape=[jax.ShapeDtypeStruct(*v) for v in shapes] + [
            jax.ShapeDtypeStruct((2, 1536, 2 * N), BF16),
            jax.ShapeDtypeStruct((2, 2 * N, 1536), BF16)],
        compiler_params=pltpu.CompilerParams(
            vmem_limit_bytes=24 * 2**20, dimension_semantics=("arbitrary",)),
        cost_estimate=pl.CostEstimate(
            flops=6 * 2 * 512 * 768 * 1536 + 2 * 512 * 768 * 768, bytes_accessed=22 * 2**20,
            transcendentals=2 * 512 * 1536),
        name="experts",
    )(core, *operands)


def branch_kernel(at_ref, inner_t_ref, wd_ref, hidden_ref, *refs):
    own_ref, sib_ref, acc = refs[-3:]
    f = pl.program_id(0)
    part = mm(inner_t_ref[0], wd_ref[0], TN) + mm(inner_t_ref[1], wd_ref[1], TN)

    @pl.when(f == 0)
    def _():
        acc[...] = part

    @pl.when(f > 0)
    def _():
        acc[...] += part

    @pl.when(f == pl.num_programs(0) - 1)
    def _():
        own_ref[...] = hidden_ref[...] + acc[:N, :]
        sib_ref[...] = acc[N:, :].astype(BF16)


def branches(table, inner_t, w_down, hidden, gates):
    return pl.pallas_call(
        branch_kernel,
        grid_spec=pltpu.PrefetchScalarGridSpec(
            num_scalar_prefetch=1,
            grid=(3,),
            in_specs=[
                pl.BlockSpec((2, 512, 2 * N), lambda f, at: (0, f, 0)),
                pl.BlockSpec((2, 512, 768), lambda f, at: (0, at[CORE] * 3 + f, 0)),
                pl.BlockSpec((N, 768), lambda f, at: (0, 0))] + [ANYWHERE] * len(gates),
            out_specs=[pl.BlockSpec((N, 768), lambda f, at: (0, 0))] * 2,
            scratch_shapes=[pltpu.VMEM((2 * N, 768), F32)],
        ),
        out_shape=[jax.ShapeDtypeStruct((N, 768), F32), jax.ShapeDtypeStruct((N, 768), BF16)],
        compiler_params=pltpu.CompilerParams(
            vmem_limit_bytes=20 * 2**20, dimension_semantics=("arbitrary",)),
        cost_estimate=pl.CostEstimate(
            flops=2 * 2 * 512 * 768 * 1536, bytes_accessed=8 * 2**20, transcendentals=0),
        name="branches",
    )(table, inner_t, w_down, hidden, *gates)


def cells_kernel(g, at_slot, act_t_ref, grad_ref, inner_t_ref, cot_own_ref, cot_sib_ref, *refs):
    if g == 0:
        full_ref, keep_ref, send_ref, low_ref, up_acc, down_acc = refs
        low_ref[...] = full_ref[...].astype(BF16)
    else:
        keep_ref, send_ref, up_acc, down_acc = refs[-4:]
    e = pl.program_id(0)
    up = mm(act_t_ref[...], grad_ref[...])
    up_acc[e, 0] = up[:, :256]
    up_acc[e, 1] = up[:, 256:]
    cot = jnp.concatenate([cot_own_ref[...], cot_sib_ref[...]], axis=0)
    down_acc[e] = mm(inner_t_ref[...], cot)

    def spill(target, base):
        def cell(i, carry):
            slot = g * 64 + base + i
            half = at_slot[192 + slot]
            rows = pl.ds(pl.multiple_of(at_slot[slot], 8), 24)
            below = pl.ds(pl.multiple_of(at_slot[384 + slot], 8), 24)
            target[i] = jnp.concatenate(
                [up_acc[0, half, rows, :], up_acc[1, half, rows, :],
                 down_acc[0, below, :], down_acc[1, below, :]], axis=0).astype(BF16)
            return carry
        lax.fori_loop(0, 32, cell, 0, unroll=4)

    @pl.when(e == 1)
    def _():
        spill(keep_ref, 0)
        spill(send_ref, 32)


def cells(g, table, act_t, grad_pre, inner_t, cot_own, cot_sib, more):
    cot = pl.BlockSpec((N, 256), lambda e, t: (0, g))
    out = pl.BlockSpec((32, 96, 256), lambda e, t: (0, 0, 0))
    low = pl.BlockSpec((N, 768), lambda e, t: (e, 0))
    return pl.pallas_call(
        lambda *refs: cells_kernel(g, *refs),
        grid_spec=pltpu.PrefetchScalarGridSpec(
            num_scalar_prefetch=1,
            grid=(2,),
            in_specs=[
                pl.BlockSpec((768, 2 * N), lambda e, t: (0, 0)),
                pl.BlockSpec((None, 2 * N, FF_STEP), lambda e, t: (e, 0, g)),
                pl.BlockSpec((None, 1536, 2 * N), lambda e, t: (e, 0, 0)),
                cot, cot] + ([low] if g == 0 else [ANYWHERE] * len(more)),
            out_specs=[out] * 2 + [low] * (g == 0),
            scratch_shapes=[pltpu.VMEM((2, 2, 768, 256), F32), pltpu.VMEM((2, 1536, 256), F32)],
        ),
        out_shape=[jax.ShapeDtypeStruct((32, 96, 256), BF16)] * 2
        + [jax.ShapeDtypeStruct((2 * N, 768), BF16)] * (g == 0),
        compiler_params=pltpu.CompilerParams(
            vmem_limit_bytes=14 * 2**20, dimension_semantics=("arbitrary",)),
        cost_estimate=pl.CostEstimate(
            flops=4 * 2 * 512 * 768 * 512, bytes_accessed=8 * 2**20, transcendentals=0),
        name="cells",
    )(table, act_t, grad_pre, inner_t, cot_own, cot_sib, *more)


def cell_places():
    table = np.zeros((32, 4, 4, 3, 4, 4, 4), np.int32)
    for r, s in np.ndindex(32, 4):
        here = {"z": r // 8, "y": r % 4, "x": (s // 2) * 2 + (r // 4) % 2}
        flips = (0, 1, 3, 2) if s % 2 else (0, 3, 1, 2)
        for g, order in enumerate(ORDERS):
            for slot in np.ndindex(4, 4, 4):
                at = {a: here[a] ^ flips[n] for a, n in zip(order, slot)}
                x_hi, x_lo = at["x"] // 2, at["x"] % 2
                table[(r, s, 0, g) + slot] = 24 * (at["z"] * 8 + x_lo * 4 + at["y"])
                table[(r, s, 1, g) + slot] = x_hi
                table[(r, s, 2, g) + slot] = 24 * (
                    (at["z"] % 2) * 32 + x_lo * 16 + at["y"] * 4 + x_hi * 2 + at["z"] // 2)
                table[(r, s, 3, g) + slot] = at["z"] * 16 + x_lo * 8 + at["y"] * 2 + x_hi
    coordinates = np.array([[n % 2, n % 4 // 2] + [0] * 126 for n in range(128)], np.int32)
    return np.concatenate([table.reshape(128, 768), coordinates], axis=1)


def add_up(parts):
    total = parts[0].astype(F32)
    for part in parts[1:]:
        total = total + part.astype(F32)
    return total.astype(BF16)


def in_hbm(values):
    return list(values)


def pass_kernel(gates, *refs):
    count = (len(refs) - gates) // 3
    for g in range(count):
        refs[2 * count + gates + g][...] = add_up([refs[2 * g][...], refs[2 * g + 1][...]])


ANYWHERE = pl.BlockSpec(memory_space=pl.ANY)


def pass_on(kept, arrived, name, gates=()):
    _, slots, rows, lanes = kept[0].shape
    block = max(slots // 4, 1)
    one = pl.BlockSpec((None, block, rows, lanes), lambda i: (1, i, 0, 0))
    return pl.pallas_call(
        lambda *refs: pass_kernel(len(gates), *refs),
        grid=(slots // block,),
        in_specs=[one] * (2 * len(kept)) + [ANYWHERE] * len(gates),
        out_specs=[pl.BlockSpec((block, rows, lanes), lambda i: (i, 0, 0))] * len(kept),
        out_shape=[jax.ShapeDtypeStruct((slots, rows, lanes), BF16)] * len(kept),
        compiler_params=pltpu.CompilerParams(vmem_limit_bytes=6 * 2**20),
        cost_estimate=pl.CostEstimate(
            flops=0, transcendentals=0, bytes_accessed=6 * len(kept) * slots * rows * lanes),
        name=name,
    )(*in_hbm([v for pair in zip(kept, arrived) for v in pair]), *gates)


def settle_kernel(groups, sizes, *refs):
    ins, outs = refs, refs[-2 * groups :]
    at = 0
    for g in range(groups):
        row = 0
        for size in sizes:
            for half in range(2):
                outs[2 * g + half][:, row : row + size, :] = add_up(
                    [ins[at + k][...] for k in range(3)])
                at += 3
            row += size


def settle(pieces, name):
    groups = len(pieces[0])
    sizes = [p[0][0].shape[2] for p in pieces]
    _, slots, _, lanes = pieces[0][0][0].shape
    half = slots // 2
    block = max(half // 4, 1)
    steps = half // block
    operands, specs = [], []
    for g in range(groups):
        for p, size in zip(pieces, sizes):
            for h in range(2):
                wide = pl.BlockSpec(
                    (None, block, size, lanes), lambda i, h=h: (0, i + h * steps, 0, 0))
                flat = pl.BlockSpec((block, size, lanes), lambda i, h=h: (i + h * steps, 0, 0))
                operands += list(p[g])
                specs += [wide, wide, flat]
    rows = sum(sizes)
    outs = pl.pallas_call(
        lambda *refs: settle_kernel(groups, sizes, *refs),
        grid=(steps,),
        in_specs=specs,
        out_specs=[pl.BlockSpec((block, rows, lanes), lambda i: (i, 0, 0))] * (2 * groups),
        out_shape=[jax.ShapeDtypeStruct((half, rows, lanes), BF16)] * (2 * groups),
        compiler_params=pltpu.CompilerParams(vmem_limit_bytes=8 * 2**20),
        cost_estimate=pl.CostEstimate(
            flops=0, transcendentals=0, bytes_accessed=8 * groups * slots * rows * lanes),
        name=name,
    )(*operands)
    shaped = [o.reshape(2, half // 2, rows, lanes) for o in outs]
    return shaped[0::2], shaped[1::2]


def finish_kernel(*refs):
    held_ref, down_ref = refs[-2:]
    for g in range(3):
        cell = add_up([refs[3 * g + k][...] for k in range(3)])
        held_ref[g, :48, :] = cell[:48]
        held_ref[g, 48:, :] = cell[96:]
        down_ref[g] = cell[48:96]


def finish(kept, first, second, gates):
    wide = pl.BlockSpec((None, None, 128, 256), lambda i: (0, 0, 0, 0))
    flat = pl.BlockSpec((None, 128, 256), lambda i: (0, 0, 0))
    return pl.pallas_call(
        finish_kernel,
        grid=(1,),
        in_specs=[wide, wide, flat] * 3 + [ANYWHERE] * len(gates),
        out_specs=[pl.BlockSpec((3, 80, 256), lambda i: (0, 0, 0)),
                   pl.BlockSpec((3, 48, 256), lambda i: (0, 0, 0))],
        out_shape=[jax.ShapeDtypeStruct((3, 80, 256), BF16), jax.ShapeDtypeStruct((3, 48, 256), BF16)],
        compiler_params=pltpu.CompilerParams(vmem_limit_bytes=4 * 2**20),
        name="finish",
    )(*[v for g in range(3) for v in (kept[g], first[g], second[g])], *gates)


def after_kernel(values_ref, *refs):
    refs[-1][...] = values_ref[...]


def after(values, gates):
    return pl.pallas_call(
        after_kernel,
        in_specs=[WHOLE] + [ANYWHERE] * len(gates),
        out_specs=WHOLE,
        out_shape=jax.ShapeDtypeStruct(values.shape, values.dtype),
        compiler_params=pltpu.CompilerParams(vmem_limit_bytes=4 * 2**20),
        name="after",
    )(values, *gates)


def put(acc, first, part, rows=slice(None)):
    for n in range(part.shape[1] // 128):
        column = first + n * 128
        lanes = slice(column % 256, column % 256 + 128)
        acc[column // 256, rows, lanes] = part[:, n * 128 : (n + 1) * 128]


def spill_rows(target, acc, at_slot, g, base, extra):
    def cell(i, carry):
        slot = g * 64 + base + i
        rows = pl.ds(pl.multiple_of(at_slot[slot], 8), 24)
        part = acc[at_slot[192 + slot] + 2 * (g % 2), rows, :]
        target[i] = jnp.concatenate([part, extra(slot)], axis=0).astype(BF16)
        return carry
    lax.fori_loop(0, 32, cell, 0, unroll=4)


def tail_kernel(at_slot, act_ref, away_ref, q_ref, qb_ref, ka_ref, kb_ref, va_ref, *refs):
    keeps, sends, acc = refs[-5:-3], refs[-3:-1], refs[-1]
    act, away = act_ref[...], away_ref[...]
    near = mm(act, jnp.concatenate(
        [r[: 2 * N, :] for r in (q_ref, qb_ref, ka_ref, kb_ref, va_ref)], axis=1), TN)
    far = mm(away, jnp.concatenate(
        [r[2 * N :, :] for r in (ka_ref, kb_ref, va_ref)], axis=1), TN)
    put(acc, 0, near[:, :384])
    put(acc, 384, near[:, 384:] + far)
    for g in range(2):
        blank = lambda slot: jnp.zeros((8, 256), F32)
        spill_rows(keeps[g], acc, at_slot, g, 0, blank)
        spill_rows(sends[g], acc, at_slot, g, 32, blank)


def tail_cells(table, *operands):
    return pl.pallas_call(
        tail_kernel,
        in_specs=[SMALL] + [WHOLE] * len(operands),
        out_specs=[WHOLE] * 4,
        out_shape=[jax.ShapeDtypeStruct((32, 32, 256), BF16)] * 4,
        scratch_shapes=[pltpu.VMEM((4, 768, 256), F32)],
        compiler_params=pltpu.CompilerParams(vmem_limit_bytes=14 * 2**20),
        cost_estimate=pl.CostEstimate(
            flops=2 * 768 * 512 * (1024 + 640), bytes_accessed=8 * 2**20, transcendentals=0),
        name="tail_cells",
    )(table, *operands)


def inputs_kernel(at_slot, act_ref, away_ref, q_ref, qb_ref, ka_ref, kb_ref, va_ref, vb_ref,
                  att_own_ref, att_sib_ref, proj_ref, own_ref, sib_ref, far_ref, far_sib_ref,
                  second_ref, *refs):
    weights = refs[:3]
    keep_ref, send_ref, cell_keep, cell_send, acc, table = refs[-6:]
    core = at_slot[CORE]
    put(acc, 0, mm(act_ref[...], vb_ref[: 2 * N, :], TN) + mm(away_ref[...], vb_ref[2 * N :, :], TN))
    mine = pl.ds(pl.multiple_of(core * 384, 384), 384)
    other = pl.ds(pl.multiple_of((1 - core) * 384, 384), 384)
    put(acc, 128, mm(att_own_ref[...], proj_ref[...], TN), mine)
    put(acc, 128, mm(att_sib_ref[:N, :], proj_ref[N:, :], TN)
        + mm(att_sib_ref[N:, :], proj_ref[:N, :], TN), other)

    vectors = [jnp.zeros((1, 768), F32)] * 2 + [second_ref[0:1, :], second_ref[1:2, :]]
    wide = list(zip((q_ref, ka_ref, va_ref), (qb_ref, kb_ref, vb_ref), weights))
    for n, ext_ref in enumerate((own_ref, sib_ref, far_ref, far_sib_ref)):
        rows = slice(n * N, (n + 1) * N)
        total = jnp.zeros((N, 768), F32)
        for a_ref, b_ref, w_ref in wide[0 if n < 2 else 1 :]:
            grads = jnp.concatenate([a_ref[rows, :], b_ref[rows, :]], axis=1)
            total += mm(grads, w_ref[...], NT)
        xhat, _ = normalize(ext_ref[:N, :].astype(F32))
        vectors[0] += jnp.sum(total * xhat, axis=0, keepdims=True)
        vectors[1] += jnp.sum(total, axis=0, keepdims=True)
        half = slice((n // 2) * N, (n // 2 + 1) * N)
        if n % 2 == 0:
            keep_ref[half, :] = total
        else:
            send_ref[half, :] = total.astype(BF16)

    chip = lax.broadcasted_iota(jnp.int32, (64, 768), 0)
    owner = lax.broadcasted_iota(jnp.int32, (64, 768), 1) // 12
    feature = lax.broadcasted_iota(jnp.int32, (768, 128), 0) % 12
    lane = lax.broadcasted_iota(jnp.int32, (768, 128), 1)
    spread = jnp.zeros((64, 128), F32)
    for n in range(4):
        line = jnp.broadcast_to(vectors[n], (64, 768))
        values = jnp.where(chip == owner, line, 0.0).astype(BF16)
        spread += mm(values, jnp.where(lane == feature + 12 * n, 1.0, 0.0).astype(BF16))
    table[...] = spread

    def lines(slot):
        row = table[pl.ds(at_slot[576 + slot], 1), :]
        return jnp.concatenate(
            [jnp.broadcast_to(row, (8, 128)), jnp.zeros((8, 128), F32)], axis=1)

    spill_rows(cell_keep, acc, at_slot, 2, 0, lines)
    spill_rows(cell_send, acc, at_slot, 2, 32, lines)


def input_partials(table, operands, gates):
    whole = lambda shape: pl.BlockSpec(shape, lambda i, *_: (0,) * len(shape))
    shapes = [((2 * N, 768), F32), ((2 * N, 768), BF16)] + [((32, 32, 256), BF16)] * 2
    return pl.pallas_call(
        inputs_kernel,
        grid_spec=pltpu.PrefetchScalarGridSpec(
            num_scalar_prefetch=1,
            grid=(1,),
            in_specs=[whole(v.shape) for v in operands[:-1]]
            + [pl.BlockSpec((768, 384), lambda i, at, n=n: (0, 2 * n + at[CORE])) for n in range(3)]
            + [ANYWHERE] * len(gates),
            out_specs=[whole(shape) for shape, _ in shapes],
            scratch_shapes=[pltpu.VMEM((2, 768, 256), F32), pltpu.VMEM((64, 128), F32)],
        ),
        out_shape=[jax.ShapeDtypeStruct(*v) for v in shapes],
        compiler_params=pltpu.CompilerParams(vmem_limit_bytes=16 * 2**20),
        cost_estimate=pl.CostEstimate(
            flops=2 * 768 * 384 * 512 * 7, bytes_accessed=10 * 2**20, transcendentals=0),
        name="input_partials",
    )(table, *operands, *[operands[-1]] * 2, *gates)


def sum_core_kernel(own_ref, sib_ref, *refs):
    refs[-1][...] = (own_ref[...] + sib_ref[...].astype(F32)).astype(BF16)


def sum_core(own, sib, gates):
    half = pl.BlockSpec((N, 768), lambda i: (1, 0))
    return pl.pallas_call(
        sum_core_kernel,
        grid=(1,),
        in_specs=[half, half] + [ANYWHERE] * len(gates),
        out_specs=pl.BlockSpec((N, 768), lambda i: (0, 0)),
        out_shape=jax.ShapeDtypeStruct((N, 768), BF16),
        compiler_params=pltpu.CompilerParams(vmem_limit_bytes=4 * 2**20),
        name="sum_core",
    )(own, sib, *gates)


def token_kernel(tokens_ref, hidden_ref, own_ref, sib_ref, far_ref, gains_ref, out_own_ref,
                 out_sib_ref, grad_ref, out_ref):
    grad = own_ref[...] + sib_ref[...].astype(F32) + far_ref[...].astype(F32)
    xhat, factor = normalize(tokens_ref[...].astype(F32))
    grad_ref[...] = hidden_ref[...] + normalize_back(grad, xhat, factor, gains_ref[0:1, :])
    out_ref[...] = (out_own_ref[...] + out_sib_ref[...].astype(F32)).astype(BF16)


def token_grads(tokens, hidden, own, sib, far, gains, out_own, out_sib):
    half = pl.BlockSpec((N, 768), lambda i: (0, 0))
    return pl.pallas_call(
        token_kernel,
        grid=(1,),
        in_specs=[half] * 5 + [pl.BlockSpec((4, 768), lambda i: (0, 0))] + [half] * 2,
        out_specs=[half] * 2,
        out_shape=[jax.ShapeDtypeStruct((N, 768), F32), jax.ShapeDtypeStruct((N, 768), BF16)],
        compiler_params=pltpu.CompilerParams(vmem_limit_bytes=8 * 2**20),
        name="token_grads",
    )(tokens, hidden, own, sib, far, gains, out_own, out_sib)


def assemble_kernel(at_ref, own_ref, near_ref, away_ref, cross_ref, down_ref, up_ref, qkv_ref, out_ref,
                    vec_ref, below_ref, held):
    core, far = at_ref[CORE], at_ref[FAR]
    held[far * 2 + core] = own_ref[...]
    held[far * 2 + 1 - core] = near_ref[...]
    held[2 - far * 2 + core] = away_ref[...]
    held[2 - far * 2 + 1 - core] = cross_ref[...]
    line = held[far * 2, 2, 64:, :128].astype(F32) + held[far * 2 + 1, 2, 64:, :128].astype(F32)
    vec_ref[...] = jnp.where(core == 0, line, pltpu.roll(line, 122, 1))[8:]
    row = lax.broadcasted_iota(jnp.int32, (24, 80), 0)
    column = lax.broadcasted_iota(jnp.int32, (24, 80), 1)
    wanted = (row // 8) * 24 + far * 12 + core * 6 + row % 8
    select = jnp.where((column == wanted) & (row % 8 < 6), 1.0, 0.0).astype(BF16)
    for x_hi in range(2):
        for c in range(2):
            for g in range(3):
                rows = mm(select, held[x_hi * 2 + c, g])
                first = c * 1536 + g * 512 + x_hi * 256
                for e in range(2):
                    up_ref[e, :, first : first + 256] = rows[8 * e : 8 * e + 6] * UP_FACTORS[e]
                for n in range(2):
                    at = g * 512 + x_hi * 256 + n * 128
                    kind, within = at // 384, at % 384 + c * 384
                    part = rows[16:22, n * 128 : (n + 1) * 128]
                    if kind < 3:
                        qkv_ref[:, kind * 768 + within : kind * 768 + within + 128] = part
                    else:
                        out_ref[:, within : within + 128] = part
    for g in range(3):
        part = down_ref[g].astype(F32)
        for e in range(2):
            below_ref[e, :, g * 256 : (g + 1) * 256] = part[24 * e : 24 * e + 24] * UP_FACTORS[e]


def assemble(table, *parts):
    return pl.pallas_call(
        assemble_kernel,
        in_specs=[SMALL] + [WHOLE] * 5,
        out_specs=[WHOLE] * 5,
        out_shape=[
            jax.ShapeDtypeStruct((2, 6, 3072), F32),
            jax.ShapeDtypeStruct((6, 2304), F32),
            jax.ShapeDtypeStruct((6, 768), F32),
            jax.ShapeDtypeStruct((8, 128), F32),
            jax.ShapeDtypeStruct((2, 24, 768), F32),
        ],
        scratch_shapes=[pltpu.VMEM((4, 3, 80, 256), BF16)],
        compiler_params=pltpu.CompilerParams(vmem_limit_bytes=4 * 2**20),
        name="assemble",
    )(table, *parts)

def shards(tokens, first_gain, first_shift, w_qkv, w_out, second_gain, second_shift,
           w_up, w_down, modality, segments, partner, cotangent):
    table = lax.dynamic_index_in_dim(
        jnp.asarray(cell_places()), lax.axis_index(BOTH), 0, keepdims=False)
    gains = jnp.stack([first_gain, first_shift, second_gain, second_shift])

    own = marked(partner, tokens[0], segments, modality)
    away = swap_far(own)
    sib = swap_core(own)
    cot_own = cotangent[0]
    cot_sib = swap_core(cot_own)

    act1, marks, queries, k_near, v_near, qx = project(table, own, sib, gains, w_qkv, True)
    away_sib = swap_core(after(away, [qx]))
    act1_away, marks_away, k_away, v_away = project(table, away, away_sib, gains, w_qkv, False)
    attended, lse = attend_forward(
        queries, k_near, k_away, v_near, v_away, qx, marks, marks_away)
    attended_sib = swap_core(attended)

    hidden, grad_act2, xhat2, factor2, act_t, inner_t, grad_pre = experts(
        table, attended, attended_sib, own, sib, cot_own, cot_sib, marks, gains, w_out, w_up, w_down)
    ff_kept, ff_first, more = [], [], [grad_act2]
    for g in range(3):
        keep, gone, *low = cells(g, table, act_t, grad_pre, inner_t, cot_own, cot_sib, more)
        ff_kept.append(keep.reshape(2, 16, 96, 256))
        ff_first.append(send(gone.reshape(2, 16, 96, 256), axis_step(ORDERS[g][0], True)))
        if g == 0:
            grad_sib = swap_core(low[0])
        more = [keep] if g == 0 else [keep, grad_sib]
    hidden_grad, grad_att, proj_half, vectors = middle(
        table, grad_act2, grad_sib, xhat2, factor2, cot_own, cot_sib, gains, w_out)

    def along(stage, first, values):
        return [send(v, axis_step(ORDERS[g][stage], first)) for g, v in enumerate(values)]

    taken = (queries, k_near, k_away, v_near, v_away, grad_att, attended, qx, marks, marks_away, lse)
    q_a, k_a, v_a = attend_backward(taken, 0, 2, ())
    q_b, k_b, v_b = attend_backward(taken, 2, 1, ())
    cells_a = tail_cells(table, act1, act1_away, q_a, q_b, k_a, k_b, v_a)
    passed = pass_on(ff_kept, ff_first, "pass_first", [cells_a[0]])
    ff_second = along(0, False, passed)
    partial_own, partial_low, *cells_b = input_partials(table, (
        act1, act1_away, q_a, q_b, k_a, k_b, v_a, v_b, attended, attended_sib, proj_half,
        own, sib, away, away_sib, vectors, w_qkv), passed)
    partial_sib = swap_core(partial_low)
    out_own, out_sib = branches(table, inner_t, w_down, hidden, [cells_b[0]])

    kept = [v.reshape(2, 16, 32, 256) for v in (cells_a[0], cells_a[1], cells_b[0])]
    first = along(0, True, [v.reshape(2, 16, 32, 256) for v in (cells_a[2], cells_a[3], cells_b[1])])
    second = along(0, False, pass_on(kept, first, "pass_tail", [out_sib] + ff_second))
    kept, sent = settle(
        [list(zip(ff_kept, ff_first, ff_second)), list(zip(kept, first, second))], "settle_all")
    first = along(1, True, sent)
    second = along(1, False, pass_on(kept, first, "pass_second"))
    kept, sent = settle([list(zip(kept, first, second))], "settle_second")
    first = along(2, True, sent)
    from_far = swap_far(sum_core(partial_own, partial_sib, first))
    second = along(2, False, pass_on(kept, first, "pass_third"))
    held, down_held = finish(kept, first, second, [from_far])

    near, beyond = swap_core(held), swap_far(held)
    cross = send(held, lambda x, y, z, c: (x ^ 2, y, z, 1 - c))
    below = send(down_held, lambda x, y, z, c: (x, y, 2 * c + z % 2, z // 2))
    up_grad, qkv_grad, out_grad, line, down_grad = assemble(
        table, held, near, beyond, cross, below)

    token_grad, layer_output = token_grads(
        tokens[0], hidden_grad, partial_own, partial_sib, from_far, gains, out_own, swap_core(out_sib))

    return (
        layer_output[None], token_grad[None], line[0, :6], line[0, 12:18], qkv_grad, out_grad,
        line[0, 24:30], line[0, 36:42], up_grad, down_grad)


def solution(mesh):
    cut = P("rows", "seq", None)
    flat = P(BOTH)
    placed = (cut,) + (P(),) * 8 + (P("rows", "seq"), P("rows", "seq"), P("rows", None), cut)
    return jax.shard_map(
        shards, mesh=mesh, in_specs=placed,
        out_specs=(cut, cut, flat, flat, P(BOTH, None), P(BOTH, None), flat, flat,
                   P(None, BOTH, None), P(None, BOTH, None)),
        check_vma=False)
```

```python
import jax
import jax.numpy as jnp
import numpy as np
from jax import lax
from jax.experimental import pallas as pl
from jax.experimental.pallas import tpu as pltpu
from jax.sharding import PartitionSpec as P

HD = 64
OWN = 6
CORE, FAR = 768, 769
IMG = 197
NIMG = 4
BOTH = ("rows", "seq")
F32 = jnp.float32
BF16 = jnp.bfloat16
MASKED = -1e30


def route(step):
    pairs = []
    for r in range(32):
        z, x_lo, y = r // 8, (r // 4) % 2, r % 4
        for s in range(4):
            x, c = (s // 2) * 2 + x_lo, s % 2
            tx, ty, tz, tc = step(x, y, z, c)
            target = (tz * 8 + (tx % 2) * 4 + ty) * 4 + (tx // 2) * 2 + tc
            pairs.append((r * 4 + s, target))
    return pairs


def send(values, step):
    return lax.ppermute(values, BOTH, route(step))


def swap_core(values):
    return send(values, lambda x, y, z, c: (x, y, z, 1 - c))


def swap_far(values):
    return send(values, lambda x, y, z, c: (x ^ 2, y, z, c))


def axis_step(axis, first):
    def step(x, y, z, c):
        flip = 1 if (c == 0) == first else 3
        at = {"x": x, "y": y, "z": z}
        at[axis] ^= flip
        return (at["x"], at["y"], at["z"], c)

    return step


FLIPS = ((0, 3, 1, 2), (0, 1, 3, 2))


def direct_step(axis, slot):
    def step(x, y, z, c):
        at = {"x": x, "y": y, "z": z}
        at[axis] ^= FLIPS[c][slot]
        return (at["x"], at["y"], at["z"], c)

    return step


UP_FACTORS = (1024 / (2 * 788), 1024 / (2 * 236))
ORDERS = (("x", "y", "z"), ("y", "z", "x"), ("z", "x", "y"))


def exchange(blocks, stage):
    arrived = {}
    for slot in (3, 1, 2):
        for g in range(3):
            arrived[g, slot] = send(blocks[g][slot], direct_step(ORDERS[g][stage], slot))
    return [[blocks[g][0]] + [arrived[g, slot] for slot in (1, 2, 3)] for g in range(3)]


def normalize(inputs):
    centred = inputs - jnp.mean(inputs, axis=-1, keepdims=True)
    factor = lax.rsqrt(jnp.mean(centred * centred, axis=-1, keepdims=True) + 1e-05)
    return centred * factor, factor


def normalize_back(grad, xhat, factor, gain):
    gy = grad * gain
    mean_gy = jnp.mean(gy, axis=-1, keepdims=True)
    mean_gx = jnp.mean(gy * xhat, axis=-1, keepdims=True)
    return factor * (gy - mean_gy - xhat * mean_gx)


SMALL = pl.BlockSpec(memory_space=pltpu.SMEM)
WHOLE = pl.BlockSpec(memory_space=pltpu.VMEM)
N = 256


def marked_kernel(partner, tokens_ref, segments_ref, modality_ref, out_ref):
    segments = segments_ref[...]
    tag = jnp.zeros(segments.shape, jnp.int32)
    for n in range(8):
        tag = jnp.where(segments == n, partner[0, n], tag)
    marks = jnp.concatenate(
        [tag, modality_ref[...], jnp.zeros((1, 256), jnp.int32)], axis=1).astype(F32)
    out_ref[:N, :] = tokens_ref[...]
    out_ref[N:, :] = jnp.concatenate([marks, jnp.zeros((15, 768), F32)], axis=0).astype(BF16)


def marked(partner, tokens, segments, modality):
    return pl.pallas_call(
        marked_kernel,
        in_specs=[SMALL, WHOLE, WHOLE, WHOLE],
        out_specs=WHOLE,
        out_shape=jax.ShapeDtypeStruct((N + 16, 768), BF16),
        compiler_params=pltpu.CompilerParams(vmem_limit_bytes=60 * 2**20),
        name="marked",
    )(partner, tokens, segments, modality)


def mark_lanes(ext):
    row = ext[N:, :].astype(F32)
    place = lax.broadcasted_iota(jnp.int32, (128, N), 0)
    tag = jnp.broadcast_to(row[:1, :N], (128, N))
    kind = jnp.broadcast_to(row[:1, N : 2 * N], (128, N))
    hot = jnp.where((place < NIMG) & (place.astype(F32) == tag), 1.0, 0.0)
    return jnp.transpose(jnp.where(place == 8, kind, hot))


def project_kernel(at_ref, near, a_ref, b_ref, gains_ref, *refs):
    count = 3 if near else 2
    weights, outs = refs[:count], refs[count:]
    for n, ext_ref in enumerate((a_ref, b_ref)):
        rows = slice(n * N, (n + 1) * N)
        ext = ext_ref[...]
        xhat, _ = normalize(ext[:N].astype(F32))
        act = (xhat * gains_ref[0:1, :] + gains_ref[1:2, :]).astype(BF16)
        outs[0][rows, :] = act
        marks = mark_lanes(ext)
        outs[1][rows, :] = marks.astype(BF16)
        for m in range(count):
            part = mm(act, weights[m][...])
            outs[2 + m][rows, :] = (0.125 * part if near and m == 0 else part).astype(BF16)
        if near:
            lane = lax.broadcasted_iota(jnp.int32, marks.shape, 1)
            outs[5][rows, :] = jnp.where((lane < NIMG) & (marks == 0.0), MASKED, 0.0).astype(BF16)


def project(table, first, second, gains, w_qkv, near):
    kinds = (0, 1, 2) if near else (1, 2)
    sizes = [768, 128] + [384] * len(kinds) + ([128] if near else [])
    whole = lambda shape: pl.BlockSpec(shape, lambda i, at: (0, 0))
    return pl.pallas_call(
        lambda at_ref, *refs: project_kernel(at_ref, near, *refs),
        grid_spec=pltpu.PrefetchScalarGridSpec(
            num_scalar_prefetch=1,
            grid=(1,),
            in_specs=[whole((N + 16, 768))] * 2 + [whole((4, 768))]
            + [pl.BlockSpec((768, 384), lambda i, at, n=n: (0, 2 * n + at[CORE])) for n in kinds],
            out_specs=[whole((2 * N, size)) for size in sizes],
        ),
        out_shape=[jax.ShapeDtypeStruct((2 * N, size), BF16) for size in sizes],
        compiler_params=pltpu.CompilerParams(vmem_limit_bytes=6 * 2**20),
        cost_estimate=pl.CostEstimate(
            flops=2 * 512 * 768 * 384 * len(kinds), bytes_accessed=4 * 2**20, transcendentals=0),
        name="project_near" if near else "project_away",
    )(table, first, second, gains, *[w_qkv] * len(kinds))


def middle_kernel(place, grad_ref, sib_ref, xhat_ref, factor_ref, cot_own_ref, cot_sib_ref,
                  gains_ref, w_out_ref, hidden_ref, att_ref, proj_ref, vec_ref):
    core = place[CORE]
    for n, cot_ref in enumerate((cot_own_ref, cot_sib_ref)):
        rows, other = slice(n * N, (n + 1) * N), slice((1 - n) * N, (2 - n) * N)
        grad = grad_ref[rows, :] + sib_ref[other, :].astype(F32)
        xhat = xhat_ref[rows, :]
        total = cot_ref[...].astype(F32) + normalize_back(grad, xhat, factor_ref[rows, :], gains_ref[2:3, :])
        low = total.astype(BF16)
        if n == 0:
            hidden_ref[...] = total
            vec_ref[0:1, :] = jnp.sum(grad * xhat, axis=0, keepdims=True)
            vec_ref[1:2, :] = jnp.sum(grad, axis=0, keepdims=True)
        mine = w_out_ref[pl.ds(pl.multiple_of(core * 384, 384), 384), :]
        att_ref[rows, :] = mm(low, mine, NT).astype(BF16)
        proj_ref[rows, :] = jnp.where(core == 0, low[:, :384], low[:, 384:])


def middle(place, *operands):
    return pl.pallas_call(
        middle_kernel,
        in_specs=[SMALL] + [WHOLE] * len(operands),
        out_specs=[WHOLE] * 4,
        out_shape=[
            jax.ShapeDtypeStruct((N, 768), F32),
            jax.ShapeDtypeStruct((2 * N, 384), BF16),
            jax.ShapeDtypeStruct((2 * N, 384), BF16),
            jax.ShapeDtypeStruct((2, 768), F32),
        ],
        compiler_params=pltpu.CompilerParams(vmem_limit_bytes=6 * 2**20),
        cost_estimate=pl.CostEstimate(
            flops=2 * 512 * 768 * 384, bytes_accessed=8 * 2**20, transcendentals=0),
        name="middle",
    )(place, *operands)


def gelu_parts(pre):
    phi = 0.5 * (1.0 + lax.erf(pre * 0.7071067811865476))
    slope = phi + pre * (0.3989422804014327 * jnp.exp(-0.5 * pre * pre))
    return pre * phi, slope


NT = (((1,), (1,)), ((), ()))
TN = (((0,), (0,)), ((), ()))
NN = (((1,), (0,)), ((), ()))


def mm(left, right, dims=NN):
    return lax.dot_general(left, right, dims, preferred_element_type=F32)


def head_lanes(shape, h):
    lane = lax.broadcasted_iota(jnp.int32, shape, len(shape) - 1)
    return (lane >= HD) == (h == 1)


def turned(values):
    return jnp.transpose(values.astype(F32)).astype(BF16)


def stacked(near_ref, away_ref):
    return jnp.concatenate([near_ref[...], away_ref[...]], axis=0)


def forward_kernel(q_ref, kn_ref, ka_ref, vn_ref, va_ref, qx_ref, xn_ref, xa_ref, out_ref, lse_ref):
    keys = jnp.concatenate([stacked(kn_ref, ka_ref), stacked(xn_ref, xa_ref)], axis=1)
    values = stacked(vn_ref, va_ref)
    q_pair = q_ref[...]
    lanes = head_lanes(q_pair.shape, 0)
    values_t = turned(values)
    value_rows = lax.broadcasted_iota(jnp.int32, values_t.shape, 0) < HD
    mixed = []
    for h in range(2):
        mine = lanes if h == 0 else jnp.logical_not(lanes)
        mine_values = value_rows if h == 0 else jnp.logical_not(value_rows)
        query = jnp.concatenate([jnp.where(mine, q_pair, 0), qx_ref[...]], axis=1)
        scores = mm(keys, query, NT)
        peak = jnp.max(scores, axis=0, keepdims=True)
        weights = jnp.exp(scores - peak).astype(BF16)
        both = mm(jnp.where(mine_values, values_t, 1), weights)
        total = both[127:128, :] if h == 0 else both[0:1, :]
        mixed.append(both * (1.0 / total))
        lse_ref[0, h : h + 1, :] = peak + jnp.log(total)
    out_rows = lax.broadcasted_iota(jnp.int32, mixed[0].shape, 0) < HD
    out_ref[...] = jnp.transpose(jnp.where(out_rows, mixed[0], mixed[1])).astype(BF16)


BY_PAIR = pl.BlockSpec((2 * N, 128), lambda p: (0, p))
FIXED = pl.BlockSpec((2 * N, 128), lambda p: (0, 0))


def attend_forward(*operands):
    return pl.pallas_call(
        forward_kernel,
        grid=(3,),
        in_specs=[BY_PAIR] * 5 + [FIXED] * 3,
        out_specs=[BY_PAIR, pl.BlockSpec((1, 2, 2 * N), lambda p: (p, 0, 0))],
        out_shape=[
            jax.ShapeDtypeStruct((2 * N, 384), BF16),
            jax.ShapeDtypeStruct((3, 2, 2 * N), F32),
        ],
        compiler_params=pltpu.CompilerParams(vmem_limit_bytes=6 * 2**20),
        cost_estimate=pl.CostEstimate(
            flops=2 * 2 * OWN * 512 * 1024 * 256, bytes_accessed=4 * 2**20,
            transcendentals=OWN * 512 * 1024),
        name="attend_forward",
    )(*operands)


def backward_kernel(q_ref, kn_ref, ka_ref, vn_ref, va_ref, do_ref, o_ref, qx_ref, xn_ref, xa_ref,
                    lse_ref, *refs):
    dq_ref, dk_ref, dv_ref = refs[-3:]
    k_pair, values = stacked(kn_ref, ka_ref), stacked(vn_ref, va_ref)
    keys = jnp.concatenate([k_pair, stacked(xn_ref, xa_ref)], axis=1)
    q_pair, grads = q_ref[...], do_ref[...]
    lanes = head_lanes(q_pair.shape, 0)
    product = grads.astype(F32) * o_ref[...].astype(F32)
    k_turned = turned(k_pair)
    rows = lax.broadcasted_iota(jnp.int32, (128, 2 * N), 0) < HD
    dq = jnp.zeros((128, 2 * N), F32)
    dk = jnp.zeros(k_pair.shape, F32)
    dv = jnp.zeros(k_pair.shape, F32)
    for h in range(2):
        mine = lanes if h == 0 else jnp.logical_not(lanes)
        q_head = jnp.where(mine, q_pair, 0)
        g_head = jnp.where(mine, grads, 0)
        dot_row = jnp.transpose(jnp.sum(jnp.where(mine, product, 0.0), axis=1, keepdims=True))
        scores = mm(keys, jnp.concatenate([q_head, qx_ref[...]], axis=1), NT)
        prob = jnp.exp(scores - lse_ref[0, h : h + 1, :])
        dv += mm(prob.astype(BF16), g_head)
        grad_prob = mm(values, g_head, NT)
        grad_scores = (prob * (grad_prob - dot_row)).astype(BF16)
        dk += mm(grad_scores, q_head)
        part = mm(k_turned, grad_scores)
        dq += jnp.where(rows if h == 0 else jnp.logical_not(rows), part, 0.0)
    dq_ref[...] = jnp.transpose(dq).astype(BF16) * jnp.asarray(0.125, BF16)
    dk_ref[...] = dk.astype(BF16)
    dv_ref[...] = dv.astype(BF16)


def attend_backward(operands, first, pairs, gates):
    by_pair = pl.BlockSpec((2 * N, 128), lambda p: (0, first + p))
    sizes = (2 * N, 4 * N, 4 * N)
    return pl.pallas_call(
        backward_kernel,
        grid=(pairs,),
        in_specs=[by_pair] * 7 + [FIXED] * 3
        + [pl.BlockSpec((1, 2, 2 * N), lambda p: (first + p, 0, 0))]
        + [pl.BlockSpec(memory_space=pl.ANY)] * len(gates),
        out_specs=[pl.BlockSpec((size, 128), lambda p: (0, p)) for size in sizes],
        out_shape=[jax.ShapeDtypeStruct((size, pairs * 128), BF16) for size in sizes],
        compiler_params=pltpu.CompilerParams(vmem_limit_bytes=10 * 2**20),
        cost_estimate=pl.CostEstimate(
            flops=2 * 5 * 2 * pairs * 512 * 1024 * 256, bytes_accessed=6 * 2**20,
            transcendentals=2 * pairs * 512 * 1024),
        name="attend_backward",
    )(*operands, *gates)


FF_STEP = 512
E_STEP = 256
EXPERT_MB = 40
CELLS_MB = 28


def expert_kernel(at_ref, att_own_ref, att_sib_ref, own_ref, sib_ref, cot_own_ref, cot_sib_ref,
                  marks_ref, gains_ref, w_out_ref, wu_ref, wd_ref,
                  hidden_ref, grad_ref, xhat_ref, factor_ref, act_t_ref, inner_t_ref, slope_ref,
                  act_acc):
    f = pl.program_id(0)
    core = at_ref[CORE]

    @pl.when(f == 0)
    def _():
        mine = w_out_ref[pl.ds(pl.multiple_of(core * 384, 384), 384), :]
        other = w_out_ref[pl.ds(pl.multiple_of((1 - core) * 384, 384), 384), :]
        for n, ext_ref in enumerate((own_ref, sib_ref)):
            rows, theirs = slice(n * N, (n + 1) * N), slice((1 - n) * N, (2 - n) * N)
            hidden = ext_ref[:N, :].astype(F32) + (
                mm(att_own_ref[rows, :], mine) + mm(att_sib_ref[theirs, :], other))
            xhat, factor = normalize(hidden)
            xhat_ref[rows, :] = xhat
            factor_ref[rows, :] = factor
            act = xhat * gains_ref[2:3, :] + gains_ref[3:4, :]
            act_acc[rows, :] = act.astype(BF16)
            act_t_ref[:, rows] = jnp.transpose(act).astype(BF16)
            if n == 0:
                hidden_ref[...] = hidden
        grad_ref[...] = jnp.zeros(grad_ref.shape, F32)

    act = act_acc[...]
    cot = jnp.concatenate([cot_own_ref[...], cot_sib_ref[...]], axis=0)
    text = marks_ref[:, 8:9].astype(F32) > 0.0
    pre = jnp.where(text, mm(act, wu_ref[1]), mm(act, wu_ref[0]))
    inner, slope = gelu_parts(pre)
    grad_pre = jnp.where(text, mm(cot, wd_ref[1], NT), mm(cot, wd_ref[0], NT)) * slope
    inner_t = jnp.transpose(inner)
    text_row = turned(marks_ref[...])[8:9, :].astype(F32) > 0.0
    inner_t_ref[0] = jnp.where(text_row, 0.0, inner_t).astype(BF16)
    inner_t_ref[1] = jnp.where(text_row, inner_t, 0.0).astype(BF16)
    slope_ref[0] = jnp.where(text, 0.0, grad_pre).astype(BF16)
    slope_ref[1] = jnp.where(text, grad_pre, 0.0).astype(BF16)
    grad_ref[...] += mm(slope_ref[0], wu_ref[0], NT) + mm(slope_ref[1], wu_ref[1], NT)


def experts(core, *operands):
    steps = 1536 // E_STEP
    shapes = [((N, 768), F32), ((2 * N, 768), F32), ((2 * N, 768), F32), ((2 * N, 1), F32),
              ((768, 2 * N), BF16)]
    fixed = lambda shape: pl.BlockSpec(shape, lambda f, *_: (0,) * len(shape))
    return pl.pallas_call(
        expert_kernel,
        grid_spec=pltpu.PrefetchScalarGridSpec(
            num_scalar_prefetch=1,
            grid=(steps,),
            in_specs=[fixed(v.shape) for v in operands[:-2]] + [
                pl.BlockSpec((2, 768, E_STEP), lambda f, at: (0, 0, at[CORE] * steps + f)),
                pl.BlockSpec((2, E_STEP, 768), lambda f, at: (0, at[CORE] * steps + f, 0)),
            ],
            out_specs=[fixed(shape) for shape, _ in shapes] + [
                pl.BlockSpec((2, E_STEP, 2 * N), lambda f, at: (0, f, 0)),
                pl.BlockSpec((2, 2 * N, E_STEP), lambda f, at: (0, 0, f)),
            ],
            scratch_shapes=[pltpu.VMEM((2 * N, 768), BF16)],
        ),
        out_shape=[jax.ShapeDtypeStruct(*v) for v in shapes] + [
            jax.ShapeDtypeStruct((2, 1536, 2 * N), BF16),
            jax.ShapeDtypeStruct((2, 2 * N, 1536), BF16)],
        compiler_params=pltpu.CompilerParams(
            vmem_limit_bytes=24 * 2**20, dimension_semantics=("arbitrary",)),
        cost_estimate=pl.CostEstimate(
            flops=6 * 2 * 512 * 768 * 1536 + 2 * 512 * 768 * 768, bytes_accessed=22 * 2**20,
            transcendentals=2 * 512 * 1536),
        name="experts",
    )(core, *operands)


def branch_kernel(at_ref, inner_t_ref, wd_ref, hidden_ref, *refs):
    own_ref, sib_ref, acc = refs[-3:]
    f = pl.program_id(0)
    part = mm(inner_t_ref[0], wd_ref[0], TN) + mm(inner_t_ref[1], wd_ref[1], TN)

    @pl.when(f == 0)
    def _():
        acc[...] = part

    @pl.when(f > 0)
    def _():
        acc[...] += part

    @pl.when(f == pl.num_programs(0) - 1)
    def _():
        own_ref[...] = hidden_ref[...] + acc[:N, :]
        sib_ref[...] = acc[N:, :].astype(BF16)


def branches(table, inner_t, w_down, hidden, gates):
    return pl.pallas_call(
        branch_kernel,
        grid_spec=pltpu.PrefetchScalarGridSpec(
            num_scalar_prefetch=1,
            grid=(3,),
            in_specs=[
                pl.BlockSpec((2, 512, 2 * N), lambda f, at: (0, f, 0)),
                pl.BlockSpec((2, 512, 768), lambda f, at: (0, at[CORE] * 3 + f, 0)),
                pl.BlockSpec((N, 768), lambda f, at: (0, 0))] + [ANYWHERE] * len(gates),
            out_specs=[pl.BlockSpec((N, 768), lambda f, at: (0, 0))] * 2,
            scratch_shapes=[pltpu.VMEM((2 * N, 768), F32)],
        ),
        out_shape=[jax.ShapeDtypeStruct((N, 768), F32), jax.ShapeDtypeStruct((N, 768), BF16)],
        compiler_params=pltpu.CompilerParams(
            vmem_limit_bytes=20 * 2**20, dimension_semantics=("arbitrary",)),
        cost_estimate=pl.CostEstimate(
            flops=2 * 2 * 512 * 768 * 1536, bytes_accessed=8 * 2**20, transcendentals=0),
        name="branches",
    )(table, inner_t, w_down, hidden, *gates)


def cells_kernel(g, at_slot, act_t_ref, grad_ref, inner_t_ref, cot_own_ref, cot_sib_ref, *refs):
    if g == 0:
        full_ref, keep_ref, send_ref, low_ref, up_acc, down_acc = refs
        low_ref[...] = full_ref[...].astype(BF16)
    else:
        keep_ref, send_ref, up_acc, down_acc = refs[-4:]
    e = pl.program_id(0)
    up = mm(act_t_ref[...], grad_ref[...])
    up_acc[e, 0] = up[:, :256]
    up_acc[e, 1] = up[:, 256:]
    cot = jnp.concatenate([cot_own_ref[...], cot_sib_ref[...]], axis=0)
    down_acc[e] = mm(inner_t_ref[...], cot)

    def spill(target, base):
        def cell(i, carry):
            slot = g * 64 + base + i
            half = at_slot[192 + slot]
            rows = pl.ds(pl.multiple_of(at_slot[slot], 8), 24)
            below = pl.ds(pl.multiple_of(at_slot[384 + slot], 8), 24)
            target[i] = jnp.concatenate(
                [up_acc[0, half, rows, :], up_acc[1, half, rows, :],
                 down_acc[0, below, :], down_acc[1, below, :]], axis=0).astype(BF16)
            return carry
        lax.fori_loop(0, 32, cell, 0, unroll=4)

    @pl.when(e == 1)
    def _():
        spill(keep_ref, 0)
        spill(send_ref, 32)


def cells(g, table, act_t, grad_pre, inner_t, cot_own, cot_sib, more):
    cot = pl.BlockSpec((N, 256), lambda e, t: (0, g))
    out = pl.BlockSpec((32, 96, 256), lambda e, t: (0, 0, 0))
    low = pl.BlockSpec((N, 768), lambda e, t: (e, 0))
    return pl.pallas_call(
        lambda *refs: cells_kernel(g, *refs),
        grid_spec=pltpu.PrefetchScalarGridSpec(
            num_scalar_prefetch=1,
            grid=(2,),
            in_specs=[
                pl.BlockSpec((768, 2 * N), lambda e, t: (0, 0)),
                pl.BlockSpec((None, 2 * N, FF_STEP), lambda e, t: (e, 0, g)),
                pl.BlockSpec((None, 1536, 2 * N), lambda e, t: (e, 0, 0)),
                cot, cot] + ([low] if g == 0 else [ANYWHERE] * len(more)),
            out_specs=[out] * 2 + [low] * (g == 0),
            scratch_shapes=[pltpu.VMEM((2, 2, 768, 256), F32), pltpu.VMEM((2, 1536, 256), F32)],
        ),
        out_shape=[jax.ShapeDtypeStruct((32, 96, 256), BF16)] * 2
        + [jax.ShapeDtypeStruct((2 * N, 768), BF16)] * (g == 0),
        compiler_params=pltpu.CompilerParams(
            vmem_limit_bytes=14 * 2**20, dimension_semantics=("arbitrary",)),
        cost_estimate=pl.CostEstimate(
            flops=4 * 2 * 512 * 768 * 512, bytes_accessed=8 * 2**20, transcendentals=0),
        name="cells",
    )(table, act_t, grad_pre, inner_t, cot_own, cot_sib, *more)


def cell_places():
    table = np.zeros((32, 4, 4, 3, 4, 4, 4), np.int32)
    for r, s in np.ndindex(32, 4):
        here = {"z": r // 8, "y": r % 4, "x": (s // 2) * 2 + (r // 4) % 2}
        flips = FLIPS[s % 2]
        for g, order in enumerate(ORDERS):
            for slot in np.ndindex(4, 4, 4):
                at = {a: here[a] ^ flips[n] for a, n in zip(order, slot)}
                x_hi, x_lo = at["x"] // 2, at["x"] % 2
                table[(r, s, 0, g) + slot] = 24 * (at["z"] * 8 + x_lo * 4 + at["y"])
                table[(r, s, 1, g) + slot] = x_hi
                table[(r, s, 2, g) + slot] = 24 * (
                    (at["z"] % 2) * 32 + x_lo * 16 + at["y"] * 4 + x_hi * 2 + at["z"] // 2)
                table[(r, s, 3, g) + slot] = at["z"] * 16 + x_lo * 8 + at["y"] * 2 + x_hi
    coordinates = np.array([[n % 2, n % 4 // 2] + [0] * 126 for n in range(128)], np.int32)
    return np.concatenate([table.reshape(128, 768), coordinates], axis=1)


def add_up(parts):
    total = parts[0].astype(F32)
    for part in parts[1:]:
        total = total + part.astype(F32)
    return total.astype(BF16)


def in_hbm(values):
    return list(values)


def pass_kernel(gates, *refs):
    count = (len(refs) - gates) // 3
    for g in range(count):
        refs[2 * count + gates + g][...] = add_up([refs[2 * g][...], refs[2 * g + 1][...]])


ANYWHERE = pl.BlockSpec(memory_space=pl.ANY)


def pass_on(kept, arrived, name, gates=()):
    _, slots, rows, lanes = kept[0].shape
    block = max(slots // 4, 1)
    one = pl.BlockSpec((None, block, rows, lanes), lambda i: (1, i, 0, 0))
    return pl.pallas_call(
        lambda *refs: pass_kernel(len(gates), *refs),
        grid=(slots // block,),
        in_specs=[one] * (2 * len(kept)) + [ANYWHERE] * len(gates),
        out_specs=[pl.BlockSpec((block, rows, lanes), lambda i: (i, 0, 0))] * len(kept),
        out_shape=[jax.ShapeDtypeStruct((slots, rows, lanes), BF16)] * len(kept),
        compiler_params=pltpu.CompilerParams(vmem_limit_bytes=6 * 2**20),
        cost_estimate=pl.CostEstimate(
            flops=0, transcendentals=0, bytes_accessed=6 * len(kept) * slots * rows * lanes),
        name=name,
    )(*in_hbm([v for pair in zip(kept, arrived) for v in pair]), *gates)


def settle_kernel(counts, *refs):
    ins, outs = list(refs), refs[-12:]
    for g in range(3):
        row = 0
        for count in counts:
            parts = [ins.pop(0) for _ in range(count)]
            size = parts[0].shape[1]
            for n in range(4):
                @pl.when(pl.program_id(0) == n)
                def _():
                    outs[4 * g + n][:, row : row + size, :] = add_up([p[...] for p in parts])
            row += size


def settle(pieces, name, gates=()):
    operands = [v for g in range(3) for p in pieces for v in p[g]]
    rows = sum(p[0][0].shape[-2] for p in pieces)
    slots, lanes = pieces[0][0][-1].shape[0], pieces[0][0][-1].shape[-1]
    fourth = slots // 4
    spec = lambda v: (
        pl.BlockSpec((None, fourth) + v.shape[2:], lambda i: (0, i, 0, 0)) if len(v.shape) == 4
        else pl.BlockSpec((fourth,) + v.shape[1:], lambda i: (i, 0, 0)))
    outs = pl.pallas_call(
        lambda *refs: settle_kernel([len(p[0]) for p in pieces], *refs),
        grid=(4,),
        in_specs=[spec(v) for v in operands] + [ANYWHERE] * len(gates),
        out_specs=[pl.BlockSpec((fourth, rows, lanes), lambda i: (0, 0, 0))] * 12,
        out_shape=[jax.ShapeDtypeStruct((fourth, rows, lanes), BF16)] * 12,
        compiler_params=pltpu.CompilerParams(vmem_limit_bytes=14 * 2**20),
        cost_estimate=pl.CostEstimate(
            flops=0, transcendentals=0, bytes_accessed=10 * 3 * slots * rows * lanes),
        name=name,
    )(*operands, *gates)
    return [outs[4 * g : 4 * g + 4] for g in range(3)]


def finish_kernel(*refs):
    held_ref, down_ref = refs[-2:]
    for g in range(3):
        cell = add_up([refs[4 * g + k][0] for k in range(4)])
        held_ref[g, :48, :] = cell[:48]
        held_ref[g, 48:, :] = cell[96:]
        down_ref[g] = cell[48:96]


def finish(pieces, gates):
    return pl.pallas_call(
        finish_kernel,
        in_specs=[WHOLE] * 12 + [ANYWHERE] * len(gates),
        out_specs=[WHOLE] * 2,
        out_shape=[jax.ShapeDtypeStruct((3, 80, 256), BF16), jax.ShapeDtypeStruct((3, 48, 256), BF16)],
        compiler_params=pltpu.CompilerParams(vmem_limit_bytes=4 * 2**20),
        name="finish",
    )(*[v for piece in pieces for v in piece], *gates)


def after_kernel(values_ref, *refs):
    refs[-1][...] = values_ref[...]


def after(values, gates):
    return pl.pallas_call(
        after_kernel,
        in_specs=[WHOLE] + [ANYWHERE] * len(gates),
        out_specs=WHOLE,
        out_shape=jax.ShapeDtypeStruct(values.shape, values.dtype),
        compiler_params=pltpu.CompilerParams(vmem_limit_bytes=4 * 2**20),
        name="after",
    )(values, *gates)


def put(acc, first, part, rows=slice(None)):
    for n in range(part.shape[1] // 128):
        column = first + n * 128
        lanes = slice(column % 256, column % 256 + 128)
        acc[column // 256, rows, lanes] = part[:, n * 128 : (n + 1) * 128]


def spill_rows(targets, acc, at_slot, g, extra):
    for n, target in enumerate(targets):
        def cell(i, carry):
            slot = g * 64 + n * 16 + i
            rows = pl.ds(pl.multiple_of(at_slot[slot], 8), 24)
            part = acc[at_slot[192 + slot] + 2 * (g % 2), rows, :]
            target[i] = jnp.concatenate([part, extra(slot)], axis=0).astype(BF16)
            return carry
        lax.fori_loop(0, 16, cell, 0, unroll=4)


def tail_kernel(at_slot, act_ref, away_ref, q_ref, qb_ref, ka_ref, kb_ref, va_ref, *refs):
    targets, acc = refs[-9:-1], refs[-1]
    act, away = act_ref[...], away_ref[...]
    near = mm(act, jnp.concatenate(
        [r[: 2 * N, :] for r in (q_ref, qb_ref, ka_ref, kb_ref, va_ref)], axis=1), TN)
    far = mm(away, jnp.concatenate(
        [r[2 * N :, :] for r in (ka_ref, kb_ref, va_ref)], axis=1), TN)
    put(acc, 0, near[:, :384])
    put(acc, 384, near[:, 384:] + far)
    for g in range(2):
        blank = lambda slot: jnp.zeros((8, 256), F32)
        spill_rows(targets[4 * g : 4 * g + 4], acc, at_slot, g, blank)


def tail_cells(table, *operands):
    return pl.pallas_call(
        tail_kernel,
        in_specs=[SMALL] + [WHOLE] * len(operands),
        out_specs=[WHOLE] * 8,
        out_shape=[jax.ShapeDtypeStruct((16, 32, 256), BF16)] * 8,
        scratch_shapes=[pltpu.VMEM((4, 768, 256), F32)],
        compiler_params=pltpu.CompilerParams(vmem_limit_bytes=14 * 2**20),
        cost_estimate=pl.CostEstimate(
            flops=2 * 768 * 512 * (1024 + 640), bytes_accessed=8 * 2**20, transcendentals=0),
        name="tail_cells",
    )(table, *operands)


def inputs_kernel(at_slot, act_ref, away_ref, q_ref, qb_ref, ka_ref, kb_ref, va_ref, vb_ref,
                  att_own_ref, att_sib_ref, proj_ref, own_ref, sib_ref, far_ref, far_sib_ref,
                  second_ref, *refs):
    weights = refs[:3]
    keep_ref, send_ref, *targets, acc, table = refs[-8:]
    core = at_slot[CORE]
    put(acc, 0, mm(act_ref[...], vb_ref[: 2 * N, :], TN) + mm(away_ref[...], vb_ref[2 * N :, :], TN))
    mine = pl.ds(pl.multiple_of(core * 384, 384), 384)
    other = pl.ds(pl.multiple_of((1 - core) * 384, 384), 384)
    put(acc, 128, mm(att_own_ref[...], proj_ref[...], TN), mine)
    put(acc, 128, mm(att_sib_ref[:N, :], proj_ref[N:, :], TN)
        + mm(att_sib_ref[N:, :], proj_ref[:N, :], TN), other)

    vectors = [jnp.zeros((1, 768), F32)] * 2 + [second_ref[0:1, :], second_ref[1:2, :]]
    wide = list(zip((q_ref, ka_ref, va_ref), (qb_ref, kb_ref, vb_ref), weights))
    for n, ext_ref in enumerate((own_ref, sib_ref, far_ref, far_sib_ref)):
        rows = slice(n * N, (n + 1) * N)
        total = jnp.zeros((N, 768), F32)
        for a_ref, b_ref, w_ref in wide[0 if n < 2 else 1 :]:
            grads = jnp.concatenate([a_ref[rows, :], b_ref[rows, :]], axis=1)
            total += mm(grads, w_ref[...], NT)
        xhat, _ = normalize(ext_ref[:N, :].astype(F32))
        vectors[0] += jnp.sum(total * xhat, axis=0, keepdims=True)
        vectors[1] += jnp.sum(total, axis=0, keepdims=True)
        half = slice((n // 2) * N, (n // 2 + 1) * N)
        if n % 2 == 0:
            keep_ref[half, :] = total
        else:
            send_ref[half, :] = total.astype(BF16)

    chip = lax.broadcasted_iota(jnp.int32, (64, 768), 0)
    owner = lax.broadcasted_iota(jnp.int32, (64, 768), 1) // 12
    feature = lax.broadcasted_iota(jnp.int32, (768, 128), 0) % 12
    lane = lax.broadcasted_iota(jnp.int32, (768, 128), 1)
    spread = jnp.zeros((64, 128), F32)
    for n in range(4):
        line = jnp.broadcast_to(vectors[n], (64, 768))
        values = jnp.where(chip == owner, line, 0.0).astype(BF16)
        spread += mm(values, jnp.where(lane == feature + 12 * n, 1.0, 0.0).astype(BF16))
    table[...] = spread

    def lines(slot):
        row = table[pl.ds(at_slot[576 + slot], 1), :]
        return jnp.concatenate(
            [jnp.broadcast_to(row, (8, 128)), jnp.zeros((8, 128), F32)], axis=1)

    spill_rows(targets, acc, at_slot, 2, lines)


def input_partials(table, operands, gates):
    whole = lambda shape: pl.BlockSpec(shape, lambda i, *_: (0,) * len(shape))
    shapes = [((2 * N, 768), F32), ((2 * N, 768), BF16)] + [((16, 32, 256), BF16)] * 4
    return pl.pallas_call(
        inputs_kernel,
        grid_spec=pltpu.PrefetchScalarGridSpec(
            num_scalar_prefetch=1,
            grid=(1,),
            in_specs=[whole(v.shape) for v in operands[:-1]]
            + [pl.BlockSpec((768, 384), lambda i, at, n=n: (0, 2 * n + at[CORE])) for n in range(3)]
            + [ANYWHERE] * len(gates),
            out_specs=[whole(shape) for shape, _ in shapes],
            scratch_shapes=[pltpu.VMEM((2, 768, 256), F32), pltpu.VMEM((64, 128), F32)],
        ),
        out_shape=[jax.ShapeDtypeStruct(*v) for v in shapes],
        compiler_params=pltpu.CompilerParams(vmem_limit_bytes=16 * 2**20),
        cost_estimate=pl.CostEstimate(
            flops=2 * 768 * 384 * 512 * 7, bytes_accessed=10 * 2**20, transcendentals=0),
        name="input_partials",
    )(table, *operands, *[operands[-1]] * 2, *gates)


def sum_core_kernel(own_ref, sib_ref, *refs):
    refs[-1][...] = (own_ref[...] + sib_ref[...].astype(F32)).astype(BF16)


def sum_core(own, sib, gates):
    half = pl.BlockSpec((N, 768), lambda i: (1, 0))
    return pl.pallas_call(
        sum_core_kernel,
        grid=(1,),
        in_specs=[half, half] + [ANYWHERE] * len(gates),
        out_specs=pl.BlockSpec((N, 768), lambda i: (0, 0)),
        out_shape=jax.ShapeDtypeStruct((N, 768), BF16),
        compiler_params=pltpu.CompilerParams(vmem_limit_bytes=4 * 2**20),
        name="sum_core",
    )(own, sib, *gates)


def token_kernel(tokens_ref, hidden_ref, own_ref, sib_ref, far_ref, gains_ref, out_own_ref,
                 out_sib_ref, grad_ref, out_ref):
    grad = own_ref[...] + sib_ref[...].astype(F32) + far_ref[...].astype(F32)
    xhat, factor = normalize(tokens_ref[...].astype(F32))
    grad_ref[...] = hidden_ref[...] + normalize_back(grad, xhat, factor, gains_ref[0:1, :])
    out_ref[...] = (out_own_ref[...] + out_sib_ref[...].astype(F32)).astype(BF16)


def token_grads(tokens, hidden, own, sib, far, gains, out_own, out_sib):
    half = pl.BlockSpec((N, 768), lambda i: (0, 0))
    return pl.pallas_call(
        token_kernel,
        grid=(1,),
        in_specs=[half] * 5 + [pl.BlockSpec((4, 768), lambda i: (0, 0))] + [half] * 2,
        out_specs=[half] * 2,
        out_shape=[jax.ShapeDtypeStruct((N, 768), F32), jax.ShapeDtypeStruct((N, 768), BF16)],
        compiler_params=pltpu.CompilerParams(vmem_limit_bytes=8 * 2**20),
        name="token_grads",
    )(tokens, hidden, own, sib, far, gains, out_own, out_sib)


def assemble_kernel(at_ref, own_ref, near_ref, away_ref, cross_ref, down_ref, up_ref, qkv_ref, out_ref,
                    vec_ref, below_ref, held):
    core, far = at_ref[CORE], at_ref[FAR]
    held[far * 2 + core] = own_ref[...]
    held[far * 2 + 1 - core] = near_ref[...]
    held[2 - far * 2 + core] = away_ref[...]
    held[2 - far * 2 + 1 - core] = cross_ref[...]
    line = held[far * 2, 2, 64:, :128].astype(F32) + held[far * 2 + 1, 2, 64:, :128].astype(F32)
    vec_ref[...] = jnp.where(core == 0, line, pltpu.roll(line, 122, 1))[8:]
    row = lax.broadcasted_iota(jnp.int32, (24, 80), 0)
    column = lax.broadcasted_iota(jnp.int32, (24, 80), 1)
    wanted = (row // 8) * 24 + far * 12 + core * 6 + row % 8
    select = jnp.where((column == wanted) & (row % 8 < 6), 1.0, 0.0).astype(BF16)
    for x_hi in range(2):
        for c in range(2):
            for g in range(3):
                rows = mm(select, held[x_hi * 2 + c, g])
                first = c * 1536 + g * 512 + x_hi * 256
                for e in range(2):
                    up_ref[:, e, first : first + 256] = rows[8 * e : 8 * e + 6] * UP_FACTORS[e]
                for n in range(2):
                    at = g * 512 + x_hi * 256 + n * 128
                    kind, within = at // 384, at % 384 + c * 384
                    part = rows[16:22, n * 128 : (n + 1) * 128]
                    if kind < 3:
                        qkv_ref[:, kind * 768 + within : kind * 768 + within + 128] = part
                    else:
                        out_ref[:, within : within + 128] = part
    for g in range(3):
        part = down_ref[g].astype(F32)
        for e in range(2):
            below_ref[e, :, g * 256 : (g + 1) * 256] = part[24 * e : 24 * e + 24] * UP_FACTORS[e]


def assemble(table, *parts):
    return pl.pallas_call(
        assemble_kernel,
        in_specs=[SMALL] + [WHOLE] * 5,
        out_specs=[WHOLE] * 5,
        out_shape=[
            jax.ShapeDtypeStruct((6, 2, 3072), F32),
            jax.ShapeDtypeStruct((6, 2304), F32),
            jax.ShapeDtypeStruct((6, 768), F32),
            jax.ShapeDtypeStruct((8, 128), F32),
            jax.ShapeDtypeStruct((2, 24, 768), F32),
        ],
        scratch_shapes=[pltpu.VMEM((4, 3, 80, 256), BF16)],
        compiler_params=pltpu.CompilerParams(vmem_limit_bytes=4 * 2**20),
        name="assemble",
    )(table, *parts)

def shards(tokens, first_gain, first_shift, w_qkv, w_out, second_gain, second_shift,
           w_up, w_down, modality, segments, partner, cotangent):
    table = lax.dynamic_index_in_dim(
        jnp.asarray(cell_places()), lax.axis_index(BOTH), 0, keepdims=False)
    gains = jnp.stack([first_gain, first_shift, second_gain, second_shift])

    own = marked(partner, tokens[0], segments, modality)
    away = swap_far(own)
    sib = swap_core(own)
    cot_own = cotangent[0]
    cot_sib = swap_core(cot_own)

    act1, marks, queries, k_near, v_near, qx = project(table, own, sib, gains, w_qkv, True)
    away_sib = swap_core(after(away, [qx]))
    act1_away, marks_away, k_away, v_away = project(table, away, away_sib, gains, w_qkv, False)
    attended, lse = attend_forward(
        queries, k_near, k_away, v_near, v_away, qx, marks, marks_away)
    attended_sib = swap_core(attended)

    hidden, grad_act2, xhat2, factor2, act_t, inner_t, grad_pre = experts(
        table, attended, attended_sib, own, sib, cot_own, cot_sib, marks, gains, w_out, w_up, w_down)
    ff_kept, ff_first, more = [], [], [grad_act2]
    for g in range(3):
        keep, gone, *low = cells(g, table, act_t, grad_pre, inner_t, cot_own, cot_sib, more)
        ff_kept.append(keep.reshape(2, 16, 96, 256))
        ff_first.append(send(gone.reshape(2, 16, 96, 256), axis_step(ORDERS[g][0], True)))
        if g == 0:
            grad_sib = swap_core(low[0])
        more = [keep] if g == 0 else [keep, grad_sib]
    hidden_grad, grad_att, proj_half, vectors = middle(
        table, grad_act2, grad_sib, xhat2, factor2, cot_own, cot_sib, gains, w_out)

    def along(stage, first, values):
        return [send(v, axis_step(ORDERS[g][stage], first)) for g, v in enumerate(values)]

    taken = (queries, k_near, k_away, v_near, v_away, grad_att, attended, qx, marks, marks_away, lse)
    q_a, k_a, v_a = attend_backward(taken, 0, 2, ())
    q_b, k_b, v_b = attend_backward(taken, 2, 1, ())
    cells_a = tail_cells(table, act1, act1_away, q_a, q_b, k_a, k_b, v_a)
    passed = pass_on(ff_kept, ff_first, "pass_first", [cells_a[0]])
    ff_second = along(0, False, passed)
    partial_own, partial_low, *cells_b = input_partials(table, (
        act1, act1_away, q_a, q_b, k_a, k_b, v_a, v_b, attended, attended_sib, proj_half,
        own, sib, away, away_sib, vectors, w_qkv), passed)
    partial_sib = swap_core(partial_low)
    out_own, out_sib = branches(table, inner_t, w_down, hidden, [cells_b[0]])

    tail = exchange([cells_a[:4], cells_a[4:], cells_b], 0)
    blocks = settle([list(zip(ff_kept, ff_first, ff_second)), tail], "settle_first", [out_sib])
    blocks = settle([exchange(blocks, 1)], "settle_second")
    parts = exchange(blocks, 2)
    from_far = swap_far(sum_core(partial_own, partial_sib, [parts[0][3], parts[1][3], parts[2][3], parts[0][1], parts[1][1]]))
    held, down_held = finish(parts, [from_far])

    near, beyond = swap_core(held), swap_far(held)
    cross = send(held, lambda x, y, z, c: (x ^ 2, y, z, 1 - c))
    below = send(down_held, lambda x, y, z, c: (x, y, 2 * c + z % 2, z // 2))
    up_grad, qkv_grad, out_grad, line, down_grad = assemble(
        table, held, near, beyond, cross, below)

    token_grad, layer_output = token_grads(
        tokens[0], hidden_grad, partial_own, partial_sib, from_far, gains, out_own, swap_core(out_sib))

    return (
        layer_output[None], token_grad[None], line[0, :6], line[0, 12:18], qkv_grad, out_grad,
        line[0, 24:30], line[0, 36:42], up_grad.transpose(1, 0, 2), down_grad)


def solution(mesh):
    cut = P("rows", "seq", None)
    flat = P(BOTH)
    placed = (cut,) + (P(),) * 8 + (P("rows", "seq"), P("rows", "seq"), P("rows", None), cut)
    return jax.shard_map(
        shards, mesh=mesh, in_specs=placed,
        out_specs=(cut, cut, flat, flat, P(BOTH, None), P(BOTH, None), flat, flat,
                   P(None, BOTH, None), P(None, BOTH, None)),
        check_vma=False)
```

```python
import jax
import jax.numpy as jnp
import numpy as np
from jax import lax
from jax.experimental import pallas as pl
from jax.experimental.pallas import tpu as pltpu
from jax.sharding import PartitionSpec as P

HD = 64
OWN = 6
CORE, FAR = 768, 769
IMG = 197
NIMG = 4
BOTH = ("rows", "seq")
F32 = jnp.float32
BF16 = jnp.bfloat16
MASKED = -1e30


def route(step):
    pairs = []
    for r in range(32):
        z, x_lo, y = r // 8, (r // 4) % 2, r % 4
        for s in range(4):
            x, c = (s // 2) * 2 + x_lo, s % 2
            tx, ty, tz, tc = step(x, y, z, c)
            target = (tz * 8 + (tx % 2) * 4 + ty) * 4 + (tx // 2) * 2 + tc
            pairs.append((r * 4 + s, target))
    return pairs


def send(values, step):
    return lax.ppermute(values, BOTH, route(step))


def swap_core(values):
    return send(values, lambda x, y, z, c: (x, y, z, 1 - c))


def swap_far(values):
    return send(values, lambda x, y, z, c: (x ^ 2, y, z, c))


def axis_step(axis, first):
    def step(x, y, z, c):
        flip = 1 if (c == 0) == first else 3
        at = {"x": x, "y": y, "z": z}
        at[axis] ^= flip
        return (at["x"], at["y"], at["z"], c)

    return step


UP_FACTORS = (1024 / (2 * 788), 1024 / (2 * 236))
ORDERS = (("x", "y", "z"), ("y", "z", "x"), ("z", "x", "y"))


def normalize(inputs):
    centred = inputs - jnp.mean(inputs, axis=-1, keepdims=True)
    factor = lax.rsqrt(jnp.mean(centred * centred, axis=-1, keepdims=True) + 1e-05)
    return centred * factor, factor


def normalize_back(grad, xhat, factor, gain):
    gy = grad * gain
    mean_gy = jnp.mean(gy, axis=-1, keepdims=True)
    mean_gx = jnp.mean(gy * xhat, axis=-1, keepdims=True)
    return factor * (gy - mean_gy - xhat * mean_gx)


SMALL = pl.BlockSpec(memory_space=pltpu.SMEM)
WHOLE = pl.BlockSpec(memory_space=pltpu.VMEM)
N = 256


def marked_kernel(partner, tokens_ref, segments_ref, modality_ref, out_ref):
    segments = segments_ref[...]
    tag = jnp.zeros(segments.shape, jnp.int32)
    for n in range(8):
        tag = jnp.where(segments == n, partner[0, n], tag)
    marks = jnp.concatenate(
        [tag, modality_ref[...], jnp.zeros((1, 256), jnp.int32)], axis=1).astype(F32)
    out_ref[:N, :] = tokens_ref[...]
    out_ref[N:, :] = jnp.concatenate([marks, jnp.zeros((15, 768), F32)], axis=0).astype(BF16)


def marked(partner, tokens, segments, modality):
    return pl.pallas_call(
        marked_kernel,
        in_specs=[SMALL, WHOLE, WHOLE, WHOLE],
        out_specs=WHOLE,
        out_shape=jax.ShapeDtypeStruct((N + 16, 768), BF16),
        compiler_params=pltpu.CompilerParams(vmem_limit_bytes=60 * 2**20),
        name="marked",
    )(partner, tokens, segments, modality)


def mark_lanes(ext):
    row = ext[N:, :].astype(F32)
    place = lax.broadcasted_iota(jnp.int32, (128, N), 0)
    tag = jnp.broadcast_to(row[:1, :N], (128, N))
    kind = jnp.broadcast_to(row[:1, N : 2 * N], (128, N))
    hot = jnp.where((place < NIMG) & (place.astype(F32) == tag), 1.0, 0.0)
    return jnp.transpose(jnp.where(place == 8, kind, hot))


def project_kernel(at_ref, near, a_ref, b_ref, gains_ref, *refs):
    count = 3 if near else 2
    weights, outs = refs[:count], refs[count:]
    for n, ext_ref in enumerate((a_ref, b_ref)):
        rows = slice(n * N, (n + 1) * N)
        ext = ext_ref[...]
        xhat, _ = normalize(ext[:N].astype(F32))
        act = (xhat * gains_ref[0:1, :] + gains_ref[1:2, :]).astype(BF16)
        outs[0][rows, :] = act
        marks = mark_lanes(ext)
        outs[1][rows, :] = marks.astype(BF16)
        for m in range(count):
            part = mm(act, weights[m][...])
            outs[2 + m][rows, :] = (0.125 * part if near and m == 0 else part).astype(BF16)
        if near:
            lane = lax.broadcasted_iota(jnp.int32, marks.shape, 1)
            outs[5][rows, :] = jnp.where((lane < NIMG) & (marks == 0.0), MASKED, 0.0).astype(BF16)


def project(table, first, second, gains, w_qkv, near):
    kinds = (0, 1, 2) if near else (1, 2)
    sizes = [768, 128] + [384] * len(kinds) + ([128] if near else [])
    whole = lambda shape: pl.BlockSpec(shape, lambda i, at: (0, 0))
    return pl.pallas_call(
        lambda at_ref, *refs: project_kernel(at_ref, near, *refs),
        grid_spec=pltpu.PrefetchScalarGridSpec(
            num_scalar_prefetch=1,
            grid=(1,),
            in_specs=[whole((N + 16, 768))] * 2 + [whole((4, 768))]
            + [pl.BlockSpec((768, 384), lambda i, at, n=n: (0, 2 * n + at[CORE])) for n in kinds],
            out_specs=[whole((2 * N, size)) for size in sizes],
        ),
        out_shape=[jax.ShapeDtypeStruct((2 * N, size), BF16) for size in sizes],
        compiler_params=pltpu.CompilerParams(vmem_limit_bytes=6 * 2**20),
        cost_estimate=pl.CostEstimate(
            flops=2 * 512 * 768 * 384 * len(kinds), bytes_accessed=4 * 2**20, transcendentals=0),
        name="project_near" if near else "project_away",
    )(table, first, second, gains, *[w_qkv] * len(kinds))


def middle_kernel(place, grad_ref, sib_ref, xhat_ref, factor_ref, cot_own_ref, cot_sib_ref,
                  gains_ref, w_out_ref, hidden_ref, att_ref, proj_ref, vec_ref):
    core = place[CORE]
    for n, cot_ref in enumerate((cot_own_ref, cot_sib_ref)):
        rows, other = slice(n * N, (n + 1) * N), slice((1 - n) * N, (2 - n) * N)
        grad = grad_ref[rows, :] + sib_ref[other, :].astype(F32)
        xhat = xhat_ref[rows, :]
        total = cot_ref[...].astype(F32) + normalize_back(grad, xhat, factor_ref[rows, :], gains_ref[2:3, :])
        low = total.astype(BF16)
        if n == 0:
            hidden_ref[...] = total
            vec_ref[0:1, :] = jnp.sum(grad * xhat, axis=0, keepdims=True)
            vec_ref[1:2, :] = jnp.sum(grad, axis=0, keepdims=True)
        mine = w_out_ref[pl.ds(pl.multiple_of(core * 384, 384), 384), :]
        att_ref[rows, :] = mm(low, mine, NT).astype(BF16)
        proj_ref[rows, :] = jnp.where(core == 0, low[:, :384], low[:, 384:])


def middle(place, *operands):
    return pl.pallas_call(
        middle_kernel,
        in_specs=[SMALL] + [WHOLE] * len(operands),
        out_specs=[WHOLE] * 4,
        out_shape=[
            jax.ShapeDtypeStruct((N, 768), F32),
            jax.ShapeDtypeStruct((2 * N, 384), BF16),
            jax.ShapeDtypeStruct((2 * N, 384), BF16),
            jax.ShapeDtypeStruct((2, 768), F32),
        ],
        compiler_params=pltpu.CompilerParams(vmem_limit_bytes=6 * 2**20),
        cost_estimate=pl.CostEstimate(
            flops=2 * 512 * 768 * 384, bytes_accessed=8 * 2**20, transcendentals=0),
        name="middle",
    )(place, *operands)


def gelu_parts(pre):
    phi = 0.5 * (1.0 + lax.erf(pre * 0.7071067811865476))
    slope = phi + pre * (0.3989422804014327 * jnp.exp(-0.5 * pre * pre))
    return pre * phi, slope


NT = (((1,), (1,)), ((), ()))
TN = (((0,), (0,)), ((), ()))
NN = (((1,), (0,)), ((), ()))


def mm(left, right, dims=NN):
    return lax.dot_general(left, right, dims, preferred_element_type=F32)


def head_lanes(shape, h):
    lane = lax.broadcasted_iota(jnp.int32, shape, len(shape) - 1)
    return (lane >= HD) == (h == 1)


def turned(values):
    return jnp.transpose(values.astype(F32)).astype(BF16)


def stacked(near_ref, away_ref):
    return jnp.concatenate([near_ref[...], away_ref[...]], axis=0)


def forward_kernel(q_ref, kn_ref, ka_ref, vn_ref, va_ref, qx_ref, xn_ref, xa_ref, out_ref, lse_ref):
    keys = jnp.concatenate([stacked(kn_ref, ka_ref), stacked(xn_ref, xa_ref)], axis=1)
    values = stacked(vn_ref, va_ref)
    q_pair = q_ref[...]
    lanes = head_lanes(q_pair.shape, 0)
    values_t = turned(values)
    value_rows = lax.broadcasted_iota(jnp.int32, values_t.shape, 0) < HD
    mixed = []
    for h in range(2):
        mine = lanes if h == 0 else jnp.logical_not(lanes)
        mine_values = value_rows if h == 0 else jnp.logical_not(value_rows)
        query = jnp.concatenate([jnp.where(mine, q_pair, 0), qx_ref[...]], axis=1)
        scores = mm(keys, query, NT)
        peak = jnp.max(scores, axis=0, keepdims=True)
        weights = jnp.exp(scores - peak).astype(BF16)
        both = mm(jnp.where(mine_values, values_t, 1), weights)
        total = both[127:128, :] if h == 0 else both[0:1, :]
        mixed.append(both * (1.0 / total))
        lse_ref[0, h : h + 1, :] = peak + jnp.log(total)
    out_rows = lax.broadcasted_iota(jnp.int32, mixed[0].shape, 0) < HD
    out_ref[...] = jnp.transpose(jnp.where(out_rows, mixed[0], mixed[1])).astype(BF16)


BY_PAIR = pl.BlockSpec((2 * N, 128), lambda p: (0, p))
FIXED = pl.BlockSpec((2 * N, 128), lambda p: (0, 0))


def attend_forward(*operands):
    return pl.pallas_call(
        forward_kernel,
        grid=(3,),
        in_specs=[BY_PAIR] * 5 + [FIXED] * 3,
        out_specs=[BY_PAIR, pl.BlockSpec((1, 2, 2 * N), lambda p: (p, 0, 0))],
        out_shape=[
            jax.ShapeDtypeStruct((2 * N, 384), BF16),
            jax.ShapeDtypeStruct((3, 2, 2 * N), F32),
        ],
        compiler_params=pltpu.CompilerParams(vmem_limit_bytes=6 * 2**20),
        cost_estimate=pl.CostEstimate(
            flops=2 * 2 * OWN * 512 * 1024 * 256, bytes_accessed=4 * 2**20,
            transcendentals=OWN * 512 * 1024),
        name="attend_forward",
    )(*operands)


def backward_kernel(q_ref, kn_ref, ka_ref, vn_ref, va_ref, do_ref, o_ref, qx_ref, xn_ref, xa_ref,
                    lse_ref, *refs):
    dq_ref, dk_ref, dv_ref = refs[-3:]
    k_pair, values = stacked(kn_ref, ka_ref), stacked(vn_ref, va_ref)
    keys = jnp.concatenate([k_pair, stacked(xn_ref, xa_ref)], axis=1)
    q_pair, grads = q_ref[...], do_ref[...]
    lanes = head_lanes(q_pair.shape, 0)
    product = grads.astype(F32) * o_ref[...].astype(F32)
    k_turned = turned(k_pair)
    rows = lax.broadcasted_iota(jnp.int32, (128, 2 * N), 0) < HD
    dq = jnp.zeros((128, 2 * N), F32)
    dk = jnp.zeros(k_pair.shape, F32)
    dv = jnp.zeros(k_pair.shape, F32)
    for h in range(2):
        mine = lanes if h == 0 else jnp.logical_not(lanes)
        q_head = jnp.where(mine, q_pair, 0)
        g_head = jnp.where(mine, grads, 0)
        dot_row = jnp.transpose(jnp.sum(jnp.where(mine, product, 0.0), axis=1, keepdims=True))
        scores = mm(keys, jnp.concatenate([q_head, qx_ref[...]], axis=1), NT)
        prob = jnp.exp(scores - lse_ref[0, h : h + 1, :])
        dv += mm(prob.astype(BF16), g_head)
        grad_prob = mm(values, g_head, NT)
        grad_scores = (prob * (grad_prob - dot_row)).astype(BF16)
        dk += mm(grad_scores, q_head)
        part = mm(k_turned, grad_scores)
        dq += jnp.where(rows if h == 0 else jnp.logical_not(rows), part, 0.0)
    dq_ref[...] = jnp.transpose(dq).astype(BF16) * jnp.asarray(0.125, BF16)
    dk_ref[...] = dk.astype(BF16)
    dv_ref[...] = dv.astype(BF16)


def attend_backward(operands, first, pairs, gates):
    by_pair = pl.BlockSpec((2 * N, 128), lambda p: (0, first + p))
    sizes = (2 * N, 4 * N, 4 * N)
    return pl.pallas_call(
        backward_kernel,
        grid=(pairs,),
        in_specs=[by_pair] * 7 + [FIXED] * 3
        + [pl.BlockSpec((1, 2, 2 * N), lambda p: (first + p, 0, 0))]
        + [pl.BlockSpec(memory_space=pl.ANY)] * len(gates),
        out_specs=[pl.BlockSpec((size, 128), lambda p: (0, p)) for size in sizes],
        out_shape=[jax.ShapeDtypeStruct((size, pairs * 128), BF16) for size in sizes],
        compiler_params=pltpu.CompilerParams(vmem_limit_bytes=10 * 2**20),
        cost_estimate=pl.CostEstimate(
            flops=2 * 5 * 2 * pairs * 512 * 1024 * 256, bytes_accessed=6 * 2**20,
            transcendentals=2 * pairs * 512 * 1024),
        name="attend_backward",
    )(*operands, *gates)


FF_STEP = 512
E_STEP = 256
EXPERT_MB = 40
CELLS_MB = 28


def expert_kernel(at_ref, att_own_ref, att_sib_ref, own_ref, sib_ref, cot_own_ref, cot_sib_ref,
                  marks_ref, gains_ref, w_out_ref, wu_ref, wd_ref,
                  hidden_ref, grad_ref, xhat_ref, factor_ref, act_t_ref, inner_t_ref, slope_ref,
                  act_acc):
    f = pl.program_id(0)
    core = at_ref[CORE]

    @pl.when(f == 0)
    def _():
        mine = w_out_ref[pl.ds(pl.multiple_of(core * 384, 384), 384), :]
        other = w_out_ref[pl.ds(pl.multiple_of((1 - core) * 384, 384), 384), :]
        for n, ext_ref in enumerate((own_ref, sib_ref)):
            rows, theirs = slice(n * N, (n + 1) * N), slice((1 - n) * N, (2 - n) * N)
            hidden = ext_ref[:N, :].astype(F32) + (
                mm(att_own_ref[rows, :], mine) + mm(att_sib_ref[theirs, :], other))
            xhat, factor = normalize(hidden)
            xhat_ref[rows, :] = xhat
            factor_ref[rows, :] = factor
            act = xhat * gains_ref[2:3, :] + gains_ref[3:4, :]
            act_acc[rows, :] = act.astype(BF16)
            act_t_ref[:, rows] = jnp.transpose(act).astype(BF16)
            if n == 0:
                hidden_ref[...] = hidden
        grad_ref[...] = jnp.zeros(grad_ref.shape, F32)

    act = act_acc[...]
    cot = jnp.concatenate([cot_own_ref[...], cot_sib_ref[...]], axis=0)
    text = marks_ref[:, 8:9].astype(F32) > 0.0
    pre = jnp.where(text, mm(act, wu_ref[1]), mm(act, wu_ref[0]))
    inner, slope = gelu_parts(pre)
    grad_pre = jnp.where(text, mm(cot, wd_ref[1], NT), mm(cot, wd_ref[0], NT)) * slope
    inner_t = jnp.transpose(inner)
    text_row = turned(marks_ref[...])[8:9, :].astype(F32) > 0.0
    inner_t_ref[0] = jnp.where(text_row, 0.0, inner_t).astype(BF16)
    inner_t_ref[1] = jnp.where(text_row, inner_t, 0.0).astype(BF16)
    slope_ref[0] = jnp.where(text, 0.0, grad_pre).astype(BF16)
    slope_ref[1] = jnp.where(text, grad_pre, 0.0).astype(BF16)
    grad_ref[...] += mm(slope_ref[0], wu_ref[0], NT) + mm(slope_ref[1], wu_ref[1], NT)


def experts(core, *operands):
    steps = 1536 // E_STEP
    shapes = [((N, 768), F32), ((2 * N, 768), F32), ((2 * N, 768), F32), ((2 * N, 1), F32),
              ((768, 2 * N), BF16)]
    fixed = lambda shape: pl.BlockSpec(shape, lambda f, *_: (0,) * len(shape))
    return pl.pallas_call(
        expert_kernel,
        grid_spec=pltpu.PrefetchScalarGridSpec(
            num_scalar_prefetch=1,
            grid=(steps,),
            in_specs=[fixed(v.shape) for v in operands[:-2]] + [
                pl.BlockSpec((2, 768, E_STEP), lambda f, at: (0, 0, at[CORE] * steps + f)),
                pl.BlockSpec((2, E_STEP, 768), lambda f, at: (0, at[CORE] * steps + f, 0)),
            ],
            out_specs=[fixed(shape) for shape, _ in shapes] + [
                pl.BlockSpec((2, E_STEP, 2 * N), lambda f, at: (0, f, 0)),
                pl.BlockSpec((2, 2 * N, E_STEP), lambda f, at: (0, 0, f)),
            ],
            scratch_shapes=[pltpu.VMEM((2 * N, 768), BF16)],
        ),
        out_shape=[jax.ShapeDtypeStruct(*v) for v in shapes] + [
            jax.ShapeDtypeStruct((2, 1536, 2 * N), BF16),
            jax.ShapeDtypeStruct((2, 2 * N, 1536), BF16)],
        compiler_params=pltpu.CompilerParams(
            vmem_limit_bytes=24 * 2**20, dimension_semantics=("arbitrary",)),
        cost_estimate=pl.CostEstimate(
            flops=6 * 2 * 512 * 768 * 1536 + 2 * 512 * 768 * 768, bytes_accessed=22 * 2**20,
            transcendentals=2 * 512 * 1536),
        name="experts",
    )(core, *operands)


def branch_kernel(at_ref, inner_t_ref, wd_ref, hidden_ref, *refs):
    own_ref, sib_ref, acc = refs[-3:]
    f = pl.program_id(0)
    part = mm(inner_t_ref[0], wd_ref[0], TN) + mm(inner_t_ref[1], wd_ref[1], TN)

    @pl.when(f == 0)
    def _():
        acc[...] = part

    @pl.when(f > 0)
    def _():
        acc[...] += part

    @pl.when(f == pl.num_programs(0) - 1)
    def _():
        own_ref[...] = hidden_ref[...] + acc[:N, :]
        sib_ref[...] = acc[N:, :].astype(BF16)


def branches(table, inner_t, w_down, hidden, gates):
    return pl.pallas_call(
        branch_kernel,
        grid_spec=pltpu.PrefetchScalarGridSpec(
            num_scalar_prefetch=1,
            grid=(3,),
            in_specs=[
                pl.BlockSpec((2, 512, 2 * N), lambda f, at: (0, f, 0)),
                pl.BlockSpec((2, 512, 768), lambda f, at: (0, at[CORE] * 3 + f, 0)),
                pl.BlockSpec((N, 768), lambda f, at: (0, 0))] + [ANYWHERE] * len(gates),
            out_specs=[pl.BlockSpec((N, 768), lambda f, at: (0, 0))] * 2,
            scratch_shapes=[pltpu.VMEM((2 * N, 768), F32)],
        ),
        out_shape=[jax.ShapeDtypeStruct((N, 768), F32), jax.ShapeDtypeStruct((N, 768), BF16)],
        compiler_params=pltpu.CompilerParams(
            vmem_limit_bytes=20 * 2**20, dimension_semantics=("arbitrary",)),
        cost_estimate=pl.CostEstimate(
            flops=2 * 2 * 512 * 768 * 1536, bytes_accessed=8 * 2**20, transcendentals=0),
        name="branches",
    )(table, inner_t, w_down, hidden, *gates)


def cells_kernel(g, at_slot, act_t_ref, grad_ref, inner_t_ref, cot_own_ref, cot_sib_ref, *refs):
    if g == 0:
        full_ref, keep_ref, send_ref, low_ref, up_acc, down_acc = refs
        low_ref[...] = full_ref[...].astype(BF16)
    else:
        keep_ref, send_ref, up_acc, down_acc = refs[-4:]
    e = pl.program_id(0)
    up = mm(act_t_ref[...], grad_ref[...])
    up_acc[e, 0] = up[:, :256]
    up_acc[e, 1] = up[:, 256:]
    cot = jnp.concatenate([cot_own_ref[...], cot_sib_ref[...]], axis=0)
    down_acc[e] = mm(inner_t_ref[...], cot)

    def spill(target, base):
        def cell(i, carry):
            slot = g * 64 + base + i
            half = at_slot[192 + slot]
            rows = pl.ds(pl.multiple_of(at_slot[slot], 8), 24)
            below = pl.ds(pl.multiple_of(at_slot[384 + slot], 8), 24)
            target[i] = jnp.concatenate(
                [up_acc[0, half, rows, :], up_acc[1, half, rows, :],
                 down_acc[0, below, :], down_acc[1, below, :]], axis=0).astype(BF16)
            return carry
        lax.fori_loop(0, 32, cell, 0, unroll=4)

    @pl.when(e == 1)
    def _():
        spill(keep_ref, 0)
        spill(send_ref, 32)


def cells(g, table, act_t, grad_pre, inner_t, cot_own, cot_sib, more):
    cot = pl.BlockSpec((N, 256), lambda e, t: (0, g))
    out = pl.BlockSpec((32, 96, 256), lambda e, t: (0, 0, 0))
    low = pl.BlockSpec((N, 768), lambda e, t: (e, 0))
    return pl.pallas_call(
        lambda *refs: cells_kernel(g, *refs),
        grid_spec=pltpu.PrefetchScalarGridSpec(
            num_scalar_prefetch=1,
            grid=(2,),
            in_specs=[
                pl.BlockSpec((768, 2 * N), lambda e, t: (0, 0)),
                pl.BlockSpec((None, 2 * N, FF_STEP), lambda e, t: (e, 0, g)),
                pl.BlockSpec((None, 1536, 2 * N), lambda e, t: (e, 0, 0)),
                cot, cot] + ([low] if g == 0 else [ANYWHERE] * len(more)),
            out_specs=[out] * 2 + [low] * (g == 0),
            scratch_shapes=[pltpu.VMEM((2, 2, 768, 256), F32), pltpu.VMEM((2, 1536, 256), F32)],
        ),
        out_shape=[jax.ShapeDtypeStruct((32, 96, 256), BF16)] * 2
        + [jax.ShapeDtypeStruct((2 * N, 768), BF16)] * (g == 0),
        compiler_params=pltpu.CompilerParams(
            vmem_limit_bytes=14 * 2**20, dimension_semantics=("arbitrary",)),
        cost_estimate=pl.CostEstimate(
            flops=4 * 2 * 512 * 768 * 512, bytes_accessed=8 * 2**20, transcendentals=0),
        name="cells",
    )(table, act_t, grad_pre, inner_t, cot_own, cot_sib, *more)


def cell_places():
    table = np.zeros((32, 4, 4, 3, 4, 4, 4), np.int32)
    for r, s in np.ndindex(32, 4):
        here = {"z": r // 8, "y": r % 4, "x": (s // 2) * 2 + (r // 4) % 2}
        flips = (0, 1, 3, 2) if s % 2 else (0, 3, 1, 2)
        for g, order in enumerate(ORDERS):
            for slot in np.ndindex(4, 4, 4):
                at = {a: here[a] ^ flips[n] for a, n in zip(order, slot)}
                x_hi, x_lo = at["x"] // 2, at["x"] % 2
                table[(r, s, 0, g) + slot] = 24 * (at["z"] * 8 + x_lo * 4 + at["y"])
                table[(r, s, 1, g) + slot] = x_hi
                table[(r, s, 2, g) + slot] = 24 * (
                    (at["z"] % 2) * 32 + x_lo * 16 + at["y"] * 4 + x_hi * 2 + at["z"] // 2)
                table[(r, s, 3, g) + slot] = at["z"] * 16 + x_lo * 8 + at["y"] * 2 + x_hi
    coordinates = np.array([[n % 2, n % 4 // 2] + [0] * 126 for n in range(128)], np.int32)
    return np.concatenate([table.reshape(128, 768), coordinates], axis=1)


def add_up(parts):
    total = parts[0].astype(F32)
    for part in parts[1:]:
        total = total + part.astype(F32)
    return total.astype(BF16)


def in_hbm(values):
    return list(values)


def pass_kernel(gates, *refs):
    count = (len(refs) - gates) // 3
    for g in range(count):
        refs[2 * count + gates + g][...] = add_up([refs[2 * g][...], refs[2 * g + 1][...]])


ANYWHERE = pl.BlockSpec(memory_space=pl.ANY)


def pass_on(kept, arrived, name, gates=()):
    _, slots, rows, lanes = kept[0].shape
    block = max(slots // 4, 1)
    one = pl.BlockSpec((None, block, rows, lanes), lambda i: (1, i, 0, 0))
    return pl.pallas_call(
        lambda *refs: pass_kernel(len(gates), *refs),
        grid=(slots // block,),
        in_specs=[one] * (2 * len(kept)) + [ANYWHERE] * len(gates),
        out_specs=[pl.BlockSpec((block, rows, lanes), lambda i: (i, 0, 0))] * len(kept),
        out_shape=[jax.ShapeDtypeStruct((slots, rows, lanes), BF16)] * len(kept),
        compiler_params=pltpu.CompilerParams(vmem_limit_bytes=6 * 2**20),
        cost_estimate=pl.CostEstimate(
            flops=0, transcendentals=0, bytes_accessed=6 * len(kept) * slots * rows * lanes),
        name=name,
    )(*in_hbm([v for pair in zip(kept, arrived) for v in pair]), *gates)


def settle_kernel(groups, sizes, *refs):
    ins, outs = refs, refs[-2 * groups :]
    at = 0
    for g in range(groups):
        row = 0
        for size in sizes:
            for half in range(2):
                outs[2 * g + half][:, row : row + size, :] = add_up(
                    [ins[at + k][...] for k in range(3)])
                at += 3
            row += size


def settle(pieces, name, gates=()):
    groups = len(pieces[0])
    sizes = [p[0][0].shape[2] for p in pieces]
    _, slots, _, lanes = pieces[0][0][0].shape
    half = slots // 2
    block = max(half // 4, 1)
    steps = half // block
    operands, specs = [], []
    for g in range(groups):
        for p, size in zip(pieces, sizes):
            for h in range(2):
                wide = pl.BlockSpec(
                    (None, block, size, lanes), lambda i, h=h: (0, i + h * steps, 0, 0))
                flat = pl.BlockSpec((block, size, lanes), lambda i, h=h: (i + h * steps, 0, 0))
                operands += list(p[g])
                specs += [wide, wide, flat]
    rows = sum(sizes)
    outs = pl.pallas_call(
        lambda *refs: settle_kernel(groups, sizes, *refs),
        grid=(steps,),
        in_specs=specs + [ANYWHERE] * len(gates),
        out_specs=[pl.BlockSpec((block, rows, lanes), lambda i: (i, 0, 0))] * (2 * groups),
        out_shape=[jax.ShapeDtypeStruct((half, rows, lanes), BF16)] * (2 * groups),
        compiler_params=pltpu.CompilerParams(vmem_limit_bytes=8 * 2**20),
        cost_estimate=pl.CostEstimate(
            flops=0, transcendentals=0, bytes_accessed=8 * groups * slots * rows * lanes),
        name=name,
    )(*operands, *gates)
    shaped = [o.reshape(2, half // 2, rows, lanes) for o in outs]
    return shaped[0::2], shaped[1::2]


def finish_kernel(*refs):
    held_ref, down_ref = refs[-2:]
    for g in range(3):
        cell = add_up([refs[3 * g + k][...] for k in range(3)])
        held_ref[g, :48, :] = cell[:48]
        held_ref[g, 48:, :] = cell[96:]
        down_ref[g] = cell[48:96]


def finish(kept, first, second, gates):
    wide = pl.BlockSpec((None, None, 128, 256), lambda i: (0, 0, 0, 0))
    flat = pl.BlockSpec((None, 128, 256), lambda i: (0, 0, 0))
    return pl.pallas_call(
        finish_kernel,
        grid=(1,),
        in_specs=[wide, wide, flat] * 3 + [ANYWHERE] * len(gates),
        out_specs=[pl.BlockSpec((3, 80, 256), lambda i: (0, 0, 0)),
                   pl.BlockSpec((3, 48, 256), lambda i: (0, 0, 0))],
        out_shape=[jax.ShapeDtypeStruct((3, 80, 256), BF16), jax.ShapeDtypeStruct((3, 48, 256), BF16)],
        compiler_params=pltpu.CompilerParams(vmem_limit_bytes=4 * 2**20),
        name="finish",
    )(*[v for g in range(3) for v in (kept[g], first[g], second[g])], *gates)


def after_kernel(values_ref, *refs):
    refs[-1][...] = values_ref[...]


def after(values, gates):
    return pl.pallas_call(
        after_kernel,
        in_specs=[WHOLE] + [ANYWHERE] * len(gates),
        out_specs=WHOLE,
        out_shape=jax.ShapeDtypeStruct(values.shape, values.dtype),
        compiler_params=pltpu.CompilerParams(vmem_limit_bytes=4 * 2**20),
        name="after",
    )(values, *gates)


def put(acc, first, part, rows=slice(None)):
    for n in range(part.shape[1] // 128):
        column = first + n * 128
        lanes = slice(column % 256, column % 256 + 128)
        acc[column // 256, rows, lanes] = part[:, n * 128 : (n + 1) * 128]


def spill_rows(target, acc, at_slot, g, base, extra):
    def cell(i, carry):
        slot = g * 64 + base + i
        rows = pl.ds(pl.multiple_of(at_slot[slot], 8), 24)
        part = acc[at_slot[192 + slot] + 2 * (g % 2), rows, :]
        target[i] = jnp.concatenate([part, extra(slot)], axis=0).astype(BF16)
        return carry
    lax.fori_loop(0, 32, cell, 0, unroll=4)


def tail_kernel(at_slot, act_ref, away_ref, q_ref, qb_ref, ka_ref, kb_ref, va_ref, *refs):
    keeps, sends, acc = refs[-5:-3], refs[-3:-1], refs[-1]
    act, away = act_ref[...], away_ref[...]
    near = mm(act, jnp.concatenate(
        [r[: 2 * N, :] for r in (q_ref, qb_ref, ka_ref, kb_ref, va_ref)], axis=1), TN)
    far = mm(away, jnp.concatenate(
        [r[2 * N :, :] for r in (ka_ref, kb_ref, va_ref)], axis=1), TN)
    put(acc, 0, near[:, :384])
    put(acc, 384, near[:, 384:] + far)
    for g in range(2):
        blank = lambda slot: jnp.zeros((8, 256), F32)
        spill_rows(keeps[g], acc, at_slot, g, 0, blank)
        spill_rows(sends[g], acc, at_slot, g, 32, blank)


def tail_cells(table, *operands):
    return pl.pallas_call(
        tail_kernel,
        in_specs=[SMALL] + [WHOLE] * len(operands),
        out_specs=[WHOLE] * 4,
        out_shape=[jax.ShapeDtypeStruct((32, 32, 256), BF16)] * 4,
        scratch_shapes=[pltpu.VMEM((4, 768, 256), F32)],
        compiler_params=pltpu.CompilerParams(vmem_limit_bytes=14 * 2**20),
        cost_estimate=pl.CostEstimate(
            flops=2 * 768 * 512 * (1024 + 640), bytes_accessed=8 * 2**20, transcendentals=0),
        name="tail_cells",
    )(table, *operands)


def inputs_kernel(at_slot, act_ref, away_ref, q_ref, qb_ref, ka_ref, kb_ref, va_ref, vb_ref,
                  att_own_ref, att_sib_ref, proj_ref, own_ref, sib_ref, far_ref, far_sib_ref,
                  second_ref, *refs):
    weights = refs[:3]
    keep_ref, send_ref, cell_keep, cell_send, acc, table = refs[-6:]
    core = at_slot[CORE]
    put(acc, 0, mm(act_ref[...], vb_ref[: 2 * N, :], TN) + mm(away_ref[...], vb_ref[2 * N :, :], TN))
    mine = pl.ds(pl.multiple_of(core * 384, 384), 384)
    other = pl.ds(pl.multiple_of((1 - core) * 384, 384), 384)
    put(acc, 128, mm(att_own_ref[...], proj_ref[...], TN), mine)
    put(acc, 128, mm(att_sib_ref[:N, :], proj_ref[N:, :], TN)
        + mm(att_sib_ref[N:, :], proj_ref[:N, :], TN), other)

    vectors = [jnp.zeros((1, 768), F32)] * 2 + [second_ref[0:1, :], second_ref[1:2, :]]
    wide = list(zip((q_ref, ka_ref, va_ref), (qb_ref, kb_ref, vb_ref), weights))
    for n, ext_ref in enumerate((own_ref, sib_ref, far_ref, far_sib_ref)):
        rows = slice(n * N, (n + 1) * N)
        total = jnp.zeros((N, 768), F32)
        for a_ref, b_ref, w_ref in wide[0 if n < 2 else 1 :]:
            grads = jnp.concatenate([a_ref[rows, :], b_ref[rows, :]], axis=1)
            total += mm(grads, w_ref[...], NT)
        xhat, _ = normalize(ext_ref[:N, :].astype(F32))
        vectors[0] += jnp.sum(total * xhat, axis=0, keepdims=True)
        vectors[1] += jnp.sum(total, axis=0, keepdims=True)
        half = slice((n // 2) * N, (n // 2 + 1) * N)
        if n % 2 == 0:
            keep_ref[half, :] = total
        else:
            send_ref[half, :] = total.astype(BF16)

    chip = lax.broadcasted_iota(jnp.int32, (64, 768), 0)
    owner = lax.broadcasted_iota(jnp.int32, (64, 768), 1) // 12
    feature = lax.broadcasted_iota(jnp.int32, (768, 128), 0) % 12
    lane = lax.broadcasted_iota(jnp.int32, (768, 128), 1)
    spread = jnp.zeros((64, 128), F32)
    for n in range(4):
        line = jnp.broadcast_to(vectors[n], (64, 768))
        values = jnp.where(chip == owner, line, 0.0).astype(BF16)
        spread += mm(values, jnp.where(lane == feature + 12 * n, 1.0, 0.0).astype(BF16))
    table[...] = spread

    def lines(slot):
        row = table[pl.ds(at_slot[576 + slot], 1), :]
        return jnp.concatenate(
            [jnp.broadcast_to(row, (8, 128)), jnp.zeros((8, 128), F32)], axis=1)

    spill_rows(cell_keep, acc, at_slot, 2, 0, lines)
    spill_rows(cell_send, acc, at_slot, 2, 32, lines)


def input_partials(table, operands, gates):
    whole = lambda shape: pl.BlockSpec(shape, lambda i, *_: (0,) * len(shape))
    shapes = [((2 * N, 768), F32), ((2 * N, 768), BF16)] + [((32, 32, 256), BF16)] * 2
    return pl.pallas_call(
        inputs_kernel,
        grid_spec=pltpu.PrefetchScalarGridSpec(
            num_scalar_prefetch=1,
            grid=(1,),
            in_specs=[whole(v.shape) for v in operands[:-1]]
            + [pl.BlockSpec((768, 384), lambda i, at, n=n: (0, 2 * n + at[CORE])) for n in range(3)]
            + [ANYWHERE] * len(gates),
            out_specs=[whole(shape) for shape, _ in shapes],
            scratch_shapes=[pltpu.VMEM((2, 768, 256), F32), pltpu.VMEM((64, 128), F32)],
        ),
        out_shape=[jax.ShapeDtypeStruct(*v) for v in shapes],
        compiler_params=pltpu.CompilerParams(vmem_limit_bytes=16 * 2**20),
        cost_estimate=pl.CostEstimate(
            flops=2 * 768 * 384 * 512 * 7, bytes_accessed=10 * 2**20, transcendentals=0),
        name="input_partials",
    )(table, *operands, *[operands[-1]] * 2, *gates)


def sum_core_kernel(own_ref, sib_ref, *refs):
    refs[-1][...] = (own_ref[...] + sib_ref[...].astype(F32)).astype(BF16)


def sum_core(own, sib, gates):
    half = pl.BlockSpec((N, 768), lambda i: (1, 0))
    return pl.pallas_call(
        sum_core_kernel,
        grid=(1,),
        in_specs=[half, half] + [ANYWHERE] * len(gates),
        out_specs=pl.BlockSpec((N, 768), lambda i: (0, 0)),
        out_shape=jax.ShapeDtypeStruct((N, 768), BF16),
        compiler_params=pltpu.CompilerParams(vmem_limit_bytes=4 * 2**20),
        name="sum_core",
    )(own, sib, *gates)


def token_kernel(tokens_ref, hidden_ref, own_ref, sib_ref, far_ref, gains_ref, out_own_ref,
                 out_sib_ref, grad_ref, out_ref):
    grad = own_ref[...] + sib_ref[...].astype(F32) + far_ref[...].astype(F32)
    xhat, factor = normalize(tokens_ref[...].astype(F32))
    grad_ref[...] = hidden_ref[...] + normalize_back(grad, xhat, factor, gains_ref[0:1, :])
    out_ref[...] = (out_own_ref[...] + out_sib_ref[...].astype(F32)).astype(BF16)


def token_grads(tokens, hidden, own, sib, far, gains, out_own, out_sib):
    half = pl.BlockSpec((N, 768), lambda i: (0, 0))
    return pl.pallas_call(
        token_kernel,
        grid=(1,),
        in_specs=[half] * 5 + [pl.BlockSpec((4, 768), lambda i: (0, 0))] + [half] * 2,
        out_specs=[half] * 2,
        out_shape=[jax.ShapeDtypeStruct((N, 768), F32), jax.ShapeDtypeStruct((N, 768), BF16)],
        compiler_params=pltpu.CompilerParams(vmem_limit_bytes=8 * 2**20),
        name="token_grads",
    )(tokens, hidden, own, sib, far, gains, out_own, out_sib)


def assemble_kernel(at_ref, own_ref, near_ref, away_ref, cross_ref, down_ref, up_ref, qkv_ref, out_ref,
                    vec_ref, below_ref, held):
    core, far = at_ref[CORE], at_ref[FAR]
    held[far * 2 + core] = own_ref[...]
    held[far * 2 + 1 - core] = near_ref[...]
    held[2 - far * 2 + core] = away_ref[...]
    held[2 - far * 2 + 1 - core] = cross_ref[...]
    line = held[far * 2, 2, 64:, :128].astype(F32) + held[far * 2 + 1, 2, 64:, :128].astype(F32)
    vec_ref[...] = jnp.where(core == 0, line, pltpu.roll(line, 122, 1))[8:]
    row = lax.broadcasted_iota(jnp.int32, (24, 80), 0)
    column = lax.broadcasted_iota(jnp.int32, (24, 80), 1)
    wanted = (row // 8) * 24 + far * 12 + core * 6 + row % 8
    select = jnp.where((column == wanted) & (row % 8 < 6), 1.0, 0.0).astype(BF16)
    for x_hi in range(2):
        for c in range(2):
            for g in range(3):
                rows = mm(select, held[x_hi * 2 + c, g])
                first = c * 1536 + g * 512 + x_hi * 256
                for e in range(2):
                    up_ref[:, e, first : first + 256] = rows[8 * e : 8 * e + 6] * UP_FACTORS[e]
                for n in range(2):
                    at = g * 512 + x_hi * 256 + n * 128
                    kind, within = at // 384, at % 384 + c * 384
                    part = rows[16:22, n * 128 : (n + 1) * 128]
                    if kind < 3:
                        qkv_ref[:, kind * 768 + within : kind * 768 + within + 128] = part
                    else:
                        out_ref[:, within : within + 128] = part
    for g in range(3):
        part = down_ref[g].astype(F32)
        for e in range(2):
            below_ref[e, :, g * 256 : (g + 1) * 256] = part[24 * e : 24 * e + 24] * UP_FACTORS[e]


def assemble(table, *parts):
    return pl.pallas_call(
        assemble_kernel,
        in_specs=[SMALL] + [WHOLE] * 5,
        out_specs=[WHOLE] * 5,
        out_shape=[
            jax.ShapeDtypeStruct((6, 2, 3072), F32),
            jax.ShapeDtypeStruct((6, 2304), F32),
            jax.ShapeDtypeStruct((6, 768), F32),
            jax.ShapeDtypeStruct((8, 128), F32),
            jax.ShapeDtypeStruct((2, 24, 768), F32),
        ],
        scratch_shapes=[pltpu.VMEM((4, 3, 80, 256), BF16)],
        compiler_params=pltpu.CompilerParams(vmem_limit_bytes=4 * 2**20),
        name="assemble",
    )(table, *parts)

def shards(tokens, first_gain, first_shift, w_qkv, w_out, second_gain, second_shift,
           w_up, w_down, modality, segments, partner, cotangent):
    table = lax.dynamic_index_in_dim(
        jnp.asarray(cell_places()), lax.axis_index(BOTH), 0, keepdims=False)
    gains = jnp.stack([first_gain, first_shift, second_gain, second_shift])

    own = marked(partner, tokens[0], segments, modality)
    away = swap_far(own)
    sib = swap_core(own)
    cot_own = cotangent[0]
    cot_sib = swap_core(cot_own)

    act1, marks, queries, k_near, v_near, qx = project(table, own, sib, gains, w_qkv, True)
    away_sib = swap_core(after(away, [qx]))
    act1_away, marks_away, k_away, v_away = project(table, away, away_sib, gains, w_qkv, False)
    attended, lse = attend_forward(
        queries, k_near, k_away, v_near, v_away, qx, marks, marks_away)
    attended_sib = swap_core(attended)

    hidden, grad_act2, xhat2, factor2, act_t, inner_t, grad_pre = experts(
        table, attended, attended_sib, own, sib, cot_own, cot_sib, marks, gains, w_out, w_up, w_down)
    ff_kept, ff_first, more = [], [], [grad_act2]
    for g in range(3):
        keep, gone, *low = cells(g, table, act_t, grad_pre, inner_t, cot_own, cot_sib, more)
        ff_kept.append(keep.reshape(2, 16, 96, 256))
        ff_first.append(send(gone.reshape(2, 16, 96, 256), axis_step(ORDERS[g][0], True)))
        if g == 0:
            grad_sib = swap_core(low[0])
        more = [keep] if g == 0 else [keep, grad_sib]
    hidden_grad, grad_att, proj_half, vectors = middle(
        table, grad_act2, grad_sib, xhat2, factor2, cot_own, cot_sib, gains, w_out)

    def along(stage, first, values):
        return [send(v, axis_step(ORDERS[g][stage], first)) for g, v in enumerate(values)]

    taken = (queries, k_near, k_away, v_near, v_away, grad_att, attended, qx, marks, marks_away, lse)
    q_a, k_a, v_a = attend_backward(taken, 0, 2, ())
    q_b, k_b, v_b = attend_backward(taken, 2, 1, ())
    cells_a = tail_cells(table, act1, act1_away, q_a, q_b, k_a, k_b, v_a)
    partial_own, partial_low, *cells_b = input_partials(table, (
        act1, act1_away, q_a, q_b, k_a, k_b, v_a, v_b, attended, attended_sib, proj_half,
        own, sib, away, away_sib, vectors, w_qkv), ())
    kept = [v.reshape(2, 16, 32, 256) for v in (cells_a[0], cells_a[1], cells_b[0])]
    first = along(0, True, [v.reshape(2, 16, 32, 256) for v in (cells_a[2], cells_a[3], cells_b[1])])
    ff_second = along(0, False, pass_on(ff_kept, ff_first, "pass_first", [cells_b[0]]))
    partial_sib = swap_core(partial_low)
    passed = pass_on(kept, first, "pass_tail")
    second = along(0, False, passed)
    out_own, out_sib = branches(table, inner_t, w_down, hidden, passed)

    kept, sent = settle(
        [list(zip(ff_kept, ff_first, ff_second)), list(zip(kept, first, second))], "settle_all", [out_sib])
    first = along(1, True, sent)
    second = along(1, False, pass_on(kept, first, "pass_second"))
    kept, sent = settle([list(zip(kept, first, second))], "settle_second")
    first = along(2, True, sent)
    from_far = swap_far(sum_core(partial_own, partial_sib, first))
    second = along(2, False, pass_on(kept, first, "pass_third"))
    held, down_held = finish(kept, first, second, [from_far])

    near, beyond = swap_core(held), swap_far(held)
    cross = send(held, lambda x, y, z, c: (x ^ 2, y, z, 1 - c))
    below = send(down_held, lambda x, y, z, c: (x, y, 2 * c + z % 2, z // 2))
    up_grad, qkv_grad, out_grad, line, down_grad = assemble(
        table, held, near, beyond, cross, below)

    token_grad, layer_output = token_grads(
        tokens[0], hidden_grad, partial_own, partial_sib, from_far, gains, out_own, swap_core(out_sib))

    return (
        layer_output[None], token_grad[None], line[0, :6], line[0, 12:18], qkv_grad, out_grad,
        line[0, 24:30], line[0, 36:42], up_grad.transpose(1, 0, 2), down_grad)


def solution(mesh):
    cut = P("rows", "seq", None)
    flat = P(BOTH)
    placed = (cut,) + (P(),) * 8 + (P("rows", "seq"), P("rows", "seq"), P("rows", None), cut)
    return jax.shard_map(
        shards, mesh=mesh, in_specs=placed,
        out_specs=(cut, cut, flat, flat, P(BOTH, None), P(BOTH, None), flat, flat,
                   P(None, BOTH, None), P(None, BOTH, None)),
        check_vma=False)
```

```python
import jax
import jax.numpy as jnp
import numpy as np
from jax import lax
from jax.experimental import pallas as pl
from jax.experimental.pallas import tpu as pltpu
from jax.sharding import PartitionSpec as P

HD = 64
OWN = 6
CORE, FAR = 768, 769
IMG = 197
NIMG = 4
BOTH = ("rows", "seq")
F32 = jnp.float32
BF16 = jnp.bfloat16
MASKED = -1e30


def route(step):
    pairs = []
    for r in range(32):
        z, x_lo, y = r // 8, (r // 4) % 2, r % 4
        for s in range(4):
            x, c = (s // 2) * 2 + x_lo, s % 2
            tx, ty, tz, tc = step(x, y, z, c)
            target = (tz * 8 + (tx % 2) * 4 + ty) * 4 + (tx // 2) * 2 + tc
            pairs.append((r * 4 + s, target))
    return pairs


def send(values, step):
    return lax.ppermute(values, BOTH, route(step))


def swap_core(values):
    return send(values, lambda x, y, z, c: (x, y, z, 1 - c))


def swap_far(values):
    return send(values, lambda x, y, z, c: (x ^ 2, y, z, c))


def axis_step(axis, first):
    def step(x, y, z, c):
        flip = 1 if (c == 0) == first else 3
        at = {"x": x, "y": y, "z": z}
        at[axis] ^= flip
        return (at["x"], at["y"], at["z"], c)

    return step


UP_FACTORS = (1024 / (2 * 788), 1024 / (2 * 236))
ORDERS = (("x", "y", "z"), ("y", "z", "x"), ("z", "x", "y"))


def normalize(inputs):
    centred = inputs - jnp.mean(inputs, axis=-1, keepdims=True)
    factor = lax.rsqrt(jnp.mean(centred * centred, axis=-1, keepdims=True) + 1e-05)
    return centred * factor, factor


def normalize_back(grad, xhat, factor, gain):
    gy = grad * gain
    mean_gy = jnp.mean(gy, axis=-1, keepdims=True)
    mean_gx = jnp.mean(gy * xhat, axis=-1, keepdims=True)
    return factor * (gy - mean_gy - xhat * mean_gx)


SMALL = pl.BlockSpec(memory_space=pltpu.SMEM)
WHOLE = pl.BlockSpec(memory_space=pltpu.VMEM)
N = 256


def marked_kernel(partner, tokens_ref, segments_ref, modality_ref, out_ref, marks_ref):
    segments = segments_ref[...]
    tag = jnp.zeros(segments.shape, jnp.int32)
    for n in range(8):
        tag = jnp.where(segments == n, partner[0, n], tag)
    place = lax.broadcasted_iota(jnp.int32, (128, N), 0)
    hot = jnp.where((place < NIMG) & (place == jnp.broadcast_to(tag, (128, N))), 1.0, 0.0)
    kind = jnp.broadcast_to(modality_ref[...].astype(F32), (128, N))
    marks = jnp.transpose(jnp.where(place == 8, kind, hot)).astype(BF16)
    marks_ref[...] = marks
    out_ref[:, :768] = tokens_ref[...]
    out_ref[:, 768:] = marks


def marked(partner, tokens, segments, modality):
    return pl.pallas_call(
        marked_kernel,
        in_specs=[SMALL, WHOLE, WHOLE, WHOLE],
        out_specs=[WHOLE] * 2,
        out_shape=[jax.ShapeDtypeStruct((N, 896), BF16), jax.ShapeDtypeStruct((N, 128), BF16)],
        compiler_params=pltpu.CompilerParams(vmem_limit_bytes=60 * 2**20),
        name="marked",
    )(partner, tokens, segments, modality)


def project_kernel(at_ref, near, a_ref, b_ref, gains_ref, *refs):
    count = 3 if near else 2
    weights, outs = refs[:count], refs[count:]
    for n, ext_ref in enumerate((a_ref, b_ref)):
        rows = slice(n * N, (n + 1) * N)
        xhat, _ = normalize(ext_ref[:, :768].astype(F32))
        act = (xhat * gains_ref[0:1, :] + gains_ref[1:2, :]).astype(BF16)
        outs[0][rows, :] = act
        marks = ext_ref[:, 768:].astype(F32)
        outs[1][rows, :] = ext_ref[:, 768:]
        for m in range(count):
            part = mm(act, weights[m][...])
            outs[2 + m][rows, :] = (0.125 * part if near and m == 0 else part).astype(BF16)
        if near:
            lane = lax.broadcasted_iota(jnp.int32, marks.shape, 1)
            outs[5][rows, :] = jnp.where((lane < NIMG) & (marks == 0.0), MASKED, 0.0).astype(BF16)


def project(table, first, second, gains, w_qkv, near):
    kinds = (0, 1, 2) if near else (1, 2)
    sizes = [768, 128] + [384] * len(kinds) + ([128] if near else [])
    whole = lambda shape: pl.BlockSpec(shape, lambda i, at: (0, 0))
    return pl.pallas_call(
        lambda at_ref, *refs: project_kernel(at_ref, near, *refs),
        grid_spec=pltpu.PrefetchScalarGridSpec(
            num_scalar_prefetch=1,
            grid=(1,),
            in_specs=[whole((N, 896))] * 2 + [whole((4, 768))]
            + [pl.BlockSpec((768, 384), lambda i, at, n=n: (0, 2 * n + at[CORE])) for n in kinds],
            out_specs=[whole((2 * N, size)) for size in sizes],
        ),
        out_shape=[jax.ShapeDtypeStruct((2 * N, size), BF16) for size in sizes],
        compiler_params=pltpu.CompilerParams(vmem_limit_bytes=6 * 2**20),
        cost_estimate=pl.CostEstimate(
            flops=2 * 512 * 768 * 384 * len(kinds), bytes_accessed=4 * 2**20, transcendentals=0),
        name="project_near" if near else "project_away",
    )(table, first, second, gains, *[w_qkv] * len(kinds))


def middle_kernel(place, grad_ref, sib_ref, xhat_ref, factor_ref, cot_own_ref, cot_sib_ref,
                  gains_ref, w_out_ref, hidden_ref, att_ref, proj_ref, vec_ref):
    core = place[CORE]
    for n, cot_ref in enumerate((cot_own_ref, cot_sib_ref)):
        rows, other = slice(n * N, (n + 1) * N), slice((1 - n) * N, (2 - n) * N)
        grad = grad_ref[rows, :].astype(F32) + sib_ref[other, :].astype(F32)
        xhat = xhat_ref[rows, :].astype(F32)
        total = cot_ref[...].astype(F32) + normalize_back(grad, xhat, factor_ref[rows, :], gains_ref[2:3, :])
        low = total.astype(BF16)
        if n == 0:
            hidden_ref[...] = total
            vec_ref[0:1, :] = jnp.sum(grad * xhat, axis=0, keepdims=True)
            vec_ref[1:2, :] = jnp.sum(grad, axis=0, keepdims=True)
        mine = w_out_ref[pl.ds(pl.multiple_of(core * 384, 384), 384), :]
        att_ref[rows, :] = mm(low, mine, NT).astype(BF16)
        proj_ref[rows, :] = jnp.where(core == 0, low[:, :384], low[:, 384:])


def middle(place, *operands):
    return pl.pallas_call(
        middle_kernel,
        in_specs=[SMALL] + [WHOLE] * len(operands),
        out_specs=[WHOLE] * 4,
        out_shape=[
            jax.ShapeDtypeStruct((N, 768), F32),
            jax.ShapeDtypeStruct((2 * N, 384), BF16),
            jax.ShapeDtypeStruct((2 * N, 384), BF16),
            jax.ShapeDtypeStruct((2, 768), F32),
        ],
        compiler_params=pltpu.CompilerParams(vmem_limit_bytes=6 * 2**20),
        cost_estimate=pl.CostEstimate(
            flops=2 * 512 * 768 * 384, bytes_accessed=8 * 2**20, transcendentals=0),
        name="middle",
    )(place, *operands)


def gelu_parts(pre):
    phi = 0.5 * (1.0 + lax.erf(pre * 0.7071067811865476))
    slope = phi + pre * (0.3989422804014327 * jnp.exp(-0.5 * pre * pre))
    return pre * phi, slope


NT = (((1,), (1,)), ((), ()))
TN = (((0,), (0,)), ((), ()))
NN = (((1,), (0,)), ((), ()))


def mm(left, right, dims=NN):
    return lax.dot_general(left, right, dims, preferred_element_type=F32)


def head_lanes(shape, h):
    lane = lax.broadcasted_iota(jnp.int32, shape, len(shape) - 1)
    return (lane >= HD) == (h == 1)


def turned(values):
    return jnp.transpose(values.astype(F32)).astype(BF16)


def stacked(near_ref, away_ref):
    return jnp.concatenate([near_ref[...], away_ref[...]], axis=0)


def forward_kernel(q_ref, kn_ref, ka_ref, vn_ref, va_ref, qx_ref, xn_ref, xa_ref, out_ref, lse_ref):
    keys = jnp.concatenate([stacked(kn_ref, ka_ref), stacked(xn_ref, xa_ref)], axis=1)
    values = stacked(vn_ref, va_ref)
    q_pair = q_ref[...]
    lanes = head_lanes(q_pair.shape, 0)
    values_t = turned(values)
    value_rows = lax.broadcasted_iota(jnp.int32, values_t.shape, 0) < HD
    mixed = []
    for h in range(2):
        mine = lanes if h == 0 else jnp.logical_not(lanes)
        mine_values = value_rows if h == 0 else jnp.logical_not(value_rows)
        query = jnp.concatenate([jnp.where(mine, q_pair, 0), qx_ref[...]], axis=1)
        scores = mm(keys, query, NT)
        peak = jnp.max(scores, axis=0, keepdims=True)
        weights = jnp.exp(scores - peak).astype(BF16)
        both = mm(jnp.where(mine_values, values_t, 1), weights)
        total = both[127:128, :] if h == 0 else both[0:1, :]
        mixed.append(both * (1.0 / total))
        lse_ref[0, h : h + 1, :] = peak + jnp.log(total)
    out_rows = lax.broadcasted_iota(jnp.int32, mixed[0].shape, 0) < HD
    out_ref[...] = jnp.transpose(jnp.where(out_rows, mixed[0], mixed[1])).astype(BF16)


BY_PAIR = pl.BlockSpec((2 * N, 128), lambda p: (0, p))
FIXED = pl.BlockSpec((2 * N, 128), lambda p: (0, 0))


def attend_forward(*operands):
    return pl.pallas_call(
        forward_kernel,
        grid=(3,),
        in_specs=[BY_PAIR] * 5 + [FIXED] * 3,
        out_specs=[BY_PAIR, pl.BlockSpec((1, 2, 2 * N), lambda p: (p, 0, 0))],
        out_shape=[
            jax.ShapeDtypeStruct((2 * N, 384), BF16),
            jax.ShapeDtypeStruct((3, 2, 2 * N), F32),
        ],
        compiler_params=pltpu.CompilerParams(vmem_limit_bytes=6 * 2**20),
        cost_estimate=pl.CostEstimate(
            flops=2 * 2 * OWN * 512 * 1024 * 256, bytes_accessed=4 * 2**20,
            transcendentals=OWN * 512 * 1024),
        name="attend_forward",
    )(*operands)


def backward_kernel(q_ref, kn_ref, ka_ref, vn_ref, va_ref, do_ref, o_ref, qx_ref, xn_ref, xa_ref,
                    lse_ref, *refs):
    dq_ref, dk_ref, dv_ref = refs[-3:]
    k_pair, values = stacked(kn_ref, ka_ref), stacked(vn_ref, va_ref)
    keys = jnp.concatenate([k_pair, stacked(xn_ref, xa_ref)], axis=1)
    q_pair, grads = q_ref[...], do_ref[...]
    lanes = head_lanes(q_pair.shape, 0)
    product = grads.astype(F32) * o_ref[...].astype(F32)
    k_turned = turned(k_pair)
    rows = lax.broadcasted_iota(jnp.int32, (128, 2 * N), 0) < HD
    dq = jnp.zeros((128, 2 * N), F32)
    dk = jnp.zeros(k_pair.shape, F32)
    dv = jnp.zeros(k_pair.shape, F32)
    for h in range(2):
        mine = lanes if h == 0 else jnp.logical_not(lanes)
        q_head = jnp.where(mine, q_pair, 0)
        g_head = jnp.where(mine, grads, 0)
        dot_row = jnp.transpose(jnp.sum(jnp.where(mine, product, 0.0), axis=1, keepdims=True))
        scores = mm(keys, jnp.concatenate([q_head, qx_ref[...]], axis=1), NT)
        prob = jnp.exp(scores - lse_ref[0, h : h + 1, :])
        dv += mm(prob.astype(BF16), g_head)
        grad_prob = mm(values, g_head, NT)
        grad_scores = (prob * (grad_prob - dot_row)).astype(BF16)
        dk += mm(grad_scores, q_head)
        part = mm(k_turned, grad_scores)
        dq += jnp.where(rows if h == 0 else jnp.logical_not(rows), part, 0.0)
    dq_ref[...] = jnp.transpose(dq).astype(BF16) * jnp.asarray(0.125, BF16)
    dk_ref[...] = dk.astype(BF16)
    dv_ref[...] = dv.astype(BF16)


def attend_backward(operands, first, pairs, gates):
    by_pair = pl.BlockSpec((2 * N, 128), lambda p: (0, first + p))
    sizes = (2 * N, 4 * N, 4 * N)
    return pl.pallas_call(
        backward_kernel,
        grid=(pairs,),
        in_specs=[by_pair] * 7 + [FIXED] * 3
        + [pl.BlockSpec((1, 2, 2 * N), lambda p: (first + p, 0, 0))]
        + [pl.BlockSpec(memory_space=pl.ANY)] * len(gates),
        out_specs=[pl.BlockSpec((size, 128), lambda p: (0, p)) for size in sizes],
        out_shape=[jax.ShapeDtypeStruct((size, pairs * 128), BF16) for size in sizes],
        compiler_params=pltpu.CompilerParams(vmem_limit_bytes=10 * 2**20),
        cost_estimate=pl.CostEstimate(
            flops=2 * 5 * 2 * pairs * 512 * 1024 * 256, bytes_accessed=6 * 2**20,
            transcendentals=2 * pairs * 512 * 1024),
        name="attend_backward",
    )(*operands, *gates)


FF_STEP = 512
E_STEP = 512
EXPERT_MB = 40
CELLS_MB = 28


def expert_kernel(at_ref, att_own_ref, att_sib_ref, own_ref, sib_ref, cot_own_ref, cot_sib_ref,
                  marks_ref, gains_ref, w_out_ref, wu_ref, wd_ref,
                  hidden_ref, low_ref, xhat_ref, factor_ref, act_t_ref, inner_t_ref, slope_ref,
                  act_acc, grad_acc):
    f = pl.program_id(0)
    core = at_ref[CORE]

    @pl.when(f == 0)
    def _():
        mine = w_out_ref[pl.ds(pl.multiple_of(core * 384, 384), 384), :]
        other = w_out_ref[pl.ds(pl.multiple_of((1 - core) * 384, 384), 384), :]
        for n, ext_ref in enumerate((own_ref, sib_ref)):
            rows, theirs = slice(n * N, (n + 1) * N), slice((1 - n) * N, (2 - n) * N)
            hidden = ext_ref[:, :768].astype(F32) + (
                mm(att_own_ref[rows, :], mine) + mm(att_sib_ref[theirs, :], other))
            xhat, factor = normalize(hidden)
            xhat_ref[rows, :] = xhat.astype(BF16)
            factor_ref[rows, :] = factor
            act = xhat * gains_ref[2:3, :] + gains_ref[3:4, :]
            act_acc[rows, :] = act.astype(BF16)
            act_t_ref[:, rows] = jnp.transpose(act).astype(BF16)
            if n == 0:
                hidden_ref[...] = hidden
        grad_acc[...] = jnp.zeros(grad_acc.shape, F32)

    act = act_acc[...]
    cot = jnp.concatenate([cot_own_ref[...], cot_sib_ref[...]], axis=0)
    text = marks_ref[:, 8:9].astype(F32) > 0.0
    pre = jnp.where(text, mm(act, wu_ref[1]), mm(act, wu_ref[0]))
    inner, slope = gelu_parts(pre)
    grad_pre = jnp.where(text, mm(cot, wd_ref[1], NT), mm(cot, wd_ref[0], NT)) * slope
    inner_t_ref[...] = jnp.transpose(inner).astype(BF16)
    low = grad_pre.astype(BF16)
    slope_ref[...] = low
    zero = jnp.zeros((), BF16)
    grad_acc[...] += (mm(jnp.where(text, zero, low), wu_ref[0], NT)
                      + mm(jnp.where(text, low, zero), wu_ref[1], NT))

    @pl.when(f == pl.num_programs(0) - 1)
    def _():
        low_ref[...] = grad_acc[...].astype(BF16)


def experts(core, *operands):
    steps = 1536 // E_STEP
    shapes = [((N, 768), F32), ((2 * N, 768), BF16), ((2 * N, 768), BF16), ((2 * N, 1), F32),
              ((768, 2 * N), BF16)]
    fixed = lambda shape: pl.BlockSpec(shape, lambda f, *_: (0,) * len(shape))
    return pl.pallas_call(
        expert_kernel,
        grid_spec=pltpu.PrefetchScalarGridSpec(
            num_scalar_prefetch=1,
            grid=(steps,),
            in_specs=[fixed(v.shape) for v in operands[:-2]] + [
                pl.BlockSpec((2, 768, E_STEP), lambda f, at: (0, 0, at[CORE] * steps + f)),
                pl.BlockSpec((2, E_STEP, 768), lambda f, at: (0, at[CORE] * steps + f, 0)),
            ],
            out_specs=[fixed(shape) for shape, _ in shapes] + [
                pl.BlockSpec((E_STEP, 2 * N), lambda f, at: (f, 0)),
                pl.BlockSpec((2 * N, E_STEP), lambda f, at: (0, f)),
            ],
            scratch_shapes=[pltpu.VMEM((2 * N, 768), BF16), pltpu.VMEM((2 * N, 768), F32)],
        ),
        out_shape=[jax.ShapeDtypeStruct(*v) for v in shapes] + [
            jax.ShapeDtypeStruct((1536, 2 * N), BF16),
            jax.ShapeDtypeStruct((2 * N, 1536), BF16)],
        compiler_params=pltpu.CompilerParams(
            vmem_limit_bytes=18 * 2**20, dimension_semantics=("arbitrary",)),
        cost_estimate=pl.CostEstimate(
            flops=6 * 2 * 512 * 768 * 1536 + 2 * 512 * 768 * 768, bytes_accessed=22 * 2**20,
            transcendentals=2 * 512 * 1536),
        name="experts",
    )(core, *operands)


def kind_row(marks_ref):
    return turned(marks_ref[...])[8:9, :].astype(F32) > 0.0


def branch_kernel(at_ref, inner_t_ref, wd_ref, hidden_ref, marks_ref, *refs):
    own_ref, sib_ref, acc = refs[-3:]
    f = pl.program_id(0)
    text, inner_t, zero = kind_row(marks_ref), inner_t_ref[...], jnp.zeros((), BF16)
    part = (mm(jnp.where(text, zero, inner_t), wd_ref[0], TN)
            + mm(jnp.where(text, inner_t, zero), wd_ref[1], TN))

    @pl.when(f == 0)
    def _():
        acc[...] = part

    @pl.when(f > 0)
    def _():
        acc[...] += part

    @pl.when(f == pl.num_programs(0) - 1)
    def _():
        own_ref[...] = hidden_ref[...] + acc[:N, :]
        sib_ref[...] = acc[N:, :].astype(BF16)


def branches(table, inner_t, w_down, hidden, marks, gates):
    return pl.pallas_call(
        branch_kernel,
        grid_spec=pltpu.PrefetchScalarGridSpec(
            num_scalar_prefetch=1,
            grid=(3,),
            in_specs=[
                pl.BlockSpec((512, 2 * N), lambda f, at: (f, 0)),
                pl.BlockSpec((2, 512, 768), lambda f, at: (0, at[CORE] * 3 + f, 0)),
                pl.BlockSpec((N, 768), lambda f, at: (0, 0)),
                pl.BlockSpec((2 * N, 128), lambda f, at: (0, 0))] + [ANYWHERE] * len(gates),
            out_specs=[pl.BlockSpec((N, 768), lambda f, at: (0, 0))] * 2,
            scratch_shapes=[pltpu.VMEM((2 * N, 768), F32)],
        ),
        out_shape=[jax.ShapeDtypeStruct((N, 768), F32), jax.ShapeDtypeStruct((N, 768), BF16)],
        compiler_params=pltpu.CompilerParams(
            vmem_limit_bytes=20 * 2**20, dimension_semantics=("arbitrary",)),
        cost_estimate=pl.CostEstimate(
            flops=2 * 2 * 512 * 768 * 1536, bytes_accessed=8 * 2**20, transcendentals=0),
        name="branches",
    )(table, inner_t, w_down, hidden, marks, *gates)


def cells_kernel(g, at_slot, act_t_ref, grad_ref, inner_t_ref, cot_own_ref, cot_sib_ref, marks_ref,
                 *refs):
    if g == 0:
        full_ref, keep_ref, send_ref, low_ref, up_acc, down_acc = refs
        low_ref[...] = full_ref[...]
    else:
        keep_ref, send_ref, up_acc, down_acc = refs[-4:]
    e = pl.program_id(0)
    zero = jnp.zeros((), BF16)
    mine = (marks_ref[:, 8:9].astype(F32) > 0.0) == (e == 1)
    mine_row = kind_row(marks_ref) == (e == 1)
    up = mm(act_t_ref[...], jnp.where(mine, grad_ref[...], zero))
    up_acc[e, 0] = up[:, :256]
    up_acc[e, 1] = up[:, 256:]
    cot = jnp.concatenate([cot_own_ref[...], cot_sib_ref[...]], axis=0)
    down_acc[e] = mm(jnp.where(mine_row, inner_t_ref[...], zero), cot)

    def spill(target, base):
        def cell(i, carry):
            slot = g * 64 + base + i
            half = at_slot[192 + slot]
            rows = pl.ds(pl.multiple_of(at_slot[slot], 8), 24)
            below = pl.ds(pl.multiple_of(at_slot[384 + slot], 8), 24)
            target[i] = jnp.concatenate(
                [up_acc[0, half, rows, :], up_acc[1, half, rows, :],
                 down_acc[0, below, :], down_acc[1, below, :]], axis=0).astype(BF16)
            return carry
        lax.fori_loop(0, 32, cell, 0, unroll=4)

    @pl.when(e == 1)
    def _():
        spill(keep_ref, 0)
        spill(send_ref, 32)


def cells(g, table, act_t, grad_pre, inner_t, cot_own, cot_sib, marks, more):
    cot = pl.BlockSpec((N, 256), lambda e, t: (0, g))
    out = pl.BlockSpec((32, 96, 256), lambda e, t: (0, 0, 0))
    low = pl.BlockSpec((N, 768), lambda e, t: (e, 0))
    return pl.pallas_call(
        lambda *refs: cells_kernel(g, *refs),
        grid_spec=pltpu.PrefetchScalarGridSpec(
            num_scalar_prefetch=1,
            grid=(2,),
            in_specs=[
                pl.BlockSpec((768, 2 * N), lambda e, t: (0, 0)),
                pl.BlockSpec((2 * N, FF_STEP), lambda e, t: (0, g)),
                pl.BlockSpec((1536, 2 * N), lambda e, t: (0, 0)),
                cot, cot, pl.BlockSpec((2 * N, 128), lambda e, t: (0, 0))] + ([low] if g == 0 else [ANYWHERE] * len(more)),
            out_specs=[out] * 2 + [low] * (g == 0),
            scratch_shapes=[pltpu.VMEM((2, 2, 768, 256), F32), pltpu.VMEM((2, 1536, 256), F32)],
        ),
        out_shape=[jax.ShapeDtypeStruct((32, 96, 256), BF16)] * 2
        + [jax.ShapeDtypeStruct((2 * N, 768), BF16)] * (g == 0),
        compiler_params=pltpu.CompilerParams(
            vmem_limit_bytes=10 * 2**20, dimension_semantics=("arbitrary",)),
        cost_estimate=pl.CostEstimate(
            flops=4 * 2 * 512 * 768 * 512, bytes_accessed=8 * 2**20, transcendentals=0),
        name="cells",
    )(table, act_t, grad_pre, inner_t, cot_own, cot_sib, marks, *more)


def cell_places():
    table = np.zeros((32, 4, 4, 3, 4, 4, 4), np.int32)
    for r, s in np.ndindex(32, 4):
        here = {"z": r // 8, "y": r % 4, "x": (s // 2) * 2 + (r // 4) % 2}
        flips = (0, 1, 3, 2) if s % 2 else (0, 3, 1, 2)
        for g, order in enumerate(ORDERS):
            for slot in np.ndindex(4, 4, 4):
                at = {a: here[a] ^ flips[n] for a, n in zip(order, slot)}
                x_hi, x_lo = at["x"] // 2, at["x"] % 2
                table[(r, s, 0, g) + slot] = 24 * (at["z"] * 8 + x_lo * 4 + at["y"])
                table[(r, s, 1, g) + slot] = x_hi
                table[(r, s, 2, g) + slot] = 24 * (
                    (at["z"] % 2) * 32 + x_lo * 16 + at["y"] * 4 + x_hi * 2 + at["z"] // 2)
                table[(r, s, 3, g) + slot] = at["z"] * 16 + x_lo * 8 + at["y"] * 2 + x_hi
    coordinates = np.array([[n % 2, n % 4 // 2] + [0] * 126 for n in range(128)], np.int32)
    return np.concatenate([table.reshape(128, 768), coordinates], axis=1)


def add_up(parts):
    total = parts[0].astype(F32)
    for part in parts[1:]:
        total = total + part.astype(F32)
    return total.astype(BF16)


def in_hbm(values):
    return list(values)


def pass_kernel(gates, *refs):
    count = (len(refs) - gates) // 3
    for g in range(count):
        refs[2 * count + gates + g][...] = add_up([refs[2 * g][...], refs[2 * g + 1][...]])


ANYWHERE = pl.BlockSpec(memory_space=pl.ANY)


def pass_on(kept, arrived, name, gates=()):
    _, slots, rows, lanes = kept[0].shape
    block = max(slots // 4, 1)
    one = pl.BlockSpec((None, block, rows, lanes), lambda i: (1, i, 0, 0))
    return pl.pallas_call(
        lambda *refs: pass_kernel(len(gates), *refs),
        grid=(slots // block,),
        in_specs=[one] * (2 * len(kept)) + [ANYWHERE] * len(gates),
        out_specs=[pl.BlockSpec((block, rows, lanes), lambda i: (i, 0, 0))] * len(kept),
        out_shape=[jax.ShapeDtypeStruct((slots, rows, lanes), BF16)] * len(kept),
        compiler_params=pltpu.CompilerParams(vmem_limit_bytes=6 * 2**20),
        cost_estimate=pl.CostEstimate(
            flops=0, transcendentals=0, bytes_accessed=6 * len(kept) * slots * rows * lanes),
        name=name,
    )(*in_hbm([v for pair in zip(kept, arrived) for v in pair]), *gates)


def settle_kernel(groups, sizes, *refs):
    ins, outs = refs, refs[-2 * groups :]
    at = 0
    for g in range(groups):
        row = 0
        for size in sizes:
            for half in range(2):
                outs[2 * g + half][:, row : row + size, :] = add_up(
                    [ins[at + k][...] for k in range(3)])
                at += 3
            row += size


def settle(pieces, name, gates=()):
    groups = len(pieces[0])
    sizes = [p[0][0].shape[2] for p in pieces]
    _, slots, _, lanes = pieces[0][0][0].shape
    half = slots // 2
    block = max(half // 4, 1)
    steps = half // block
    operands, specs = [], []
    for g in range(groups):
        for p, size in zip(pieces, sizes):
            for h in range(2):
                wide = pl.BlockSpec(
                    (None, block, size, lanes), lambda i, h=h: (0, i + h * steps, 0, 0))
                flat = pl.BlockSpec((block, size, lanes), lambda i, h=h: (i + h * steps, 0, 0))
                operands += list(p[g])
                specs += [wide, wide, flat]
    rows = sum(sizes)
    outs = pl.pallas_call(
        lambda *refs: settle_kernel(groups, sizes, *refs),
        grid=(steps,),
        in_specs=specs + [ANYWHERE] * len(gates),
        out_specs=[pl.BlockSpec((block, rows, lanes), lambda i: (i, 0, 0))] * (2 * groups),
        out_shape=[jax.ShapeDtypeStruct((half, rows, lanes), BF16)] * (2 * groups),
        compiler_params=pltpu.CompilerParams(vmem_limit_bytes=8 * 2**20),
        cost_estimate=pl.CostEstimate(
            flops=0, transcendentals=0, bytes_accessed=8 * groups * slots * rows * lanes),
        name=name,
    )(*operands, *gates)
    shaped = [o.reshape(2, half // 2, rows, lanes) for o in outs]
    return shaped[0::2], shaped[1::2]


def finish_kernel(*refs):
    held_ref, down_ref = refs[-2:]
    for g in range(3):
        cell = add_up([refs[3 * g + k][...] for k in range(3)])
        held_ref[g, :48, :] = cell[:48]
        held_ref[g, 48:, :] = cell[96:]
        down_ref[g] = cell[48:96]


def finish(kept, first, second, gates):
    wide = pl.BlockSpec((None, None, 128, 256), lambda i: (0, 0, 0, 0))
    flat = pl.BlockSpec((None, 128, 256), lambda i: (0, 0, 0))
    return pl.pallas_call(
        finish_kernel,
        grid=(1,),
        in_specs=[wide, wide, flat] * 3 + [ANYWHERE] * len(gates),
        out_specs=[pl.BlockSpec((3, 80, 256), lambda i: (0, 0, 0)),
                   pl.BlockSpec((3, 48, 256), lambda i: (0, 0, 0))],
        out_shape=[jax.ShapeDtypeStruct((3, 80, 256), BF16), jax.ShapeDtypeStruct((3, 48, 256), BF16)],
        compiler_params=pltpu.CompilerParams(vmem_limit_bytes=4 * 2**20),
        name="finish",
    )(*[v for g in range(3) for v in (kept[g], first[g], second[g])], *gates)


def joined_kernel(values_ref, marks_ref, *refs):
    refs[-1][:, :768] = values_ref[...]
    refs[-1][:, 768:] = marks_ref[...]


def joined(values, marks, gates):
    return pl.pallas_call(
        joined_kernel,
        in_specs=[WHOLE] * 2 + [ANYWHERE] * len(gates),
        out_specs=WHOLE,
        out_shape=jax.ShapeDtypeStruct((N, 896), BF16),
        compiler_params=pltpu.CompilerParams(vmem_limit_bytes=4 * 2**20),
        name="joined",
    )(values, marks, *gates)


def put(acc, first, part, rows=slice(None)):
    for n in range(part.shape[1] // 128):
        column = first + n * 128
        lanes = slice(column % 256, column % 256 + 128)
        acc[column // 256, rows, lanes] = part[:, n * 128 : (n + 1) * 128]


def spill_rows(target, acc, at_slot, g, base, extra):
    def cell(i, carry):
        slot = g * 64 + base + i
        rows = pl.ds(pl.multiple_of(at_slot[slot], 8), 24)
        part = acc[at_slot[192 + slot] + 2 * (g % 2), rows, :]
        target[i] = jnp.concatenate([part, extra(slot)], axis=0).astype(BF16)
        return carry
    lax.fori_loop(0, 32, cell, 0, unroll=4)


def tail_kernel(at_slot, act_ref, away_ref, q_ref, qb_ref, ka_ref, kb_ref, va_ref, *refs):
    keeps, sends, acc = refs[-5:-3], refs[-3:-1], refs[-1]
    act, away = act_ref[...], away_ref[...]
    near = mm(act, jnp.concatenate(
        [r[: 2 * N, :] for r in (q_ref, qb_ref, ka_ref, kb_ref, va_ref)], axis=1), TN)
    far = mm(away, jnp.concatenate(
        [r[2 * N :, :] for r in (ka_ref, kb_ref, va_ref)], axis=1), TN)
    put(acc, 0, near[:, :384])
    put(acc, 384, near[:, 384:] + far)
    for g in range(2):
        blank = lambda slot: jnp.zeros((8, 256), F32)
        spill_rows(keeps[g], acc, at_slot, g, 0, blank)
        spill_rows(sends[g], acc, at_slot, g, 32, blank)


def tail_cells(table, *operands):
    return pl.pallas_call(
        tail_kernel,
        in_specs=[SMALL] + [WHOLE] * len(operands),
        out_specs=[WHOLE] * 4,
        out_shape=[jax.ShapeDtypeStruct((32, 32, 256), BF16)] * 4,
        scratch_shapes=[pltpu.VMEM((4, 768, 256), F32)],
        compiler_params=pltpu.CompilerParams(vmem_limit_bytes=14 * 2**20),
        cost_estimate=pl.CostEstimate(
            flops=2 * 768 * 512 * (1024 + 640), bytes_accessed=8 * 2**20, transcendentals=0),
        name="tail_cells",
    )(table, *operands)


def inputs_kernel(at_slot, act_ref, away_ref, q_ref, qb_ref, ka_ref, kb_ref, va_ref, vb_ref,
                  att_own_ref, att_sib_ref, proj_ref, own_ref, sib_ref, far_ref, far_sib_ref,
                  second_ref, *refs):
    weights = refs[:3]
    keep_ref, send_ref, cell_keep, cell_send, acc, table = refs[-6:]
    core = at_slot[CORE]
    put(acc, 0, mm(act_ref[...], vb_ref[: 2 * N, :], TN) + mm(away_ref[...], vb_ref[2 * N :, :], TN))
    mine = pl.ds(pl.multiple_of(core * 384, 384), 384)
    other = pl.ds(pl.multiple_of((1 - core) * 384, 384), 384)
    put(acc, 128, mm(att_own_ref[...], proj_ref[...], TN), mine)
    put(acc, 128, mm(att_sib_ref[:N, :], proj_ref[N:, :], TN)
        + mm(att_sib_ref[N:, :], proj_ref[:N, :], TN), other)

    vectors = [jnp.zeros((1, 768), F32)] * 2 + [second_ref[0:1, :], second_ref[1:2, :]]
    wide = list(zip((q_ref, ka_ref, va_ref), (qb_ref, kb_ref, vb_ref), weights))
    for n, ext_ref in enumerate((own_ref, sib_ref, far_ref, far_sib_ref)):
        rows = slice(n * N, (n + 1) * N)
        total = jnp.zeros((N, 768), F32)
        for a_ref, b_ref, w_ref in wide[0 if n < 2 else 1 :]:
            grads = jnp.concatenate([a_ref[rows, :], b_ref[rows, :]], axis=1)
            total += mm(grads, w_ref[...], NT)
        xhat, _ = normalize(ext_ref[:, :768].astype(F32))
        vectors[0] += jnp.sum(total * xhat, axis=0, keepdims=True)
        vectors[1] += jnp.sum(total, axis=0, keepdims=True)
        half = slice((n // 2) * N, (n // 2 + 1) * N)
        if n % 2 == 0:
            keep_ref[half, :] = total
        else:
            send_ref[half, :] = total.astype(BF16)

    chip = lax.broadcasted_iota(jnp.int32, (64, 768), 0)
    owner = lax.broadcasted_iota(jnp.int32, (64, 768), 1) // 12
    feature = lax.broadcasted_iota(jnp.int32, (768, 128), 0) % 12
    lane = lax.broadcasted_iota(jnp.int32, (768, 128), 1)
    spread = jnp.zeros((64, 128), F32)
    for n in range(4):
        line = jnp.broadcast_to(vectors[n], (64, 768))
        values = jnp.where(chip == owner, line, 0.0).astype(BF16)
        spread += mm(values, jnp.where(lane == feature + 12 * n, 1.0, 0.0).astype(BF16))
    table[...] = spread

    def lines(slot):
        row = table[pl.ds(at_slot[576 + slot], 1), :]
        return jnp.concatenate(
            [jnp.broadcast_to(row, (8, 128)), jnp.zeros((8, 128), F32)], axis=1)

    spill_rows(cell_keep, acc, at_slot, 2, 0, lines)
    spill_rows(cell_send, acc, at_slot, 2, 32, lines)


def input_partials(table, operands, gates):
    whole = lambda shape: pl.BlockSpec(shape, lambda i, *_: (0,) * len(shape))
    shapes = [((2 * N, 768), F32), ((2 * N, 768), BF16)] + [((32, 32, 256), BF16)] * 2
    return pl.pallas_call(
        inputs_kernel,
        grid_spec=pltpu.PrefetchScalarGridSpec(
            num_scalar_prefetch=1,
            grid=(1,),
            in_specs=[whole(v.shape) for v in operands[:-1]]
            + [pl.BlockSpec((768, 384), lambda i, at, n=n: (0, 2 * n + at[CORE])) for n in range(3)]
            + [ANYWHERE] * len(gates),
            out_specs=[whole(shape) for shape, _ in shapes],
            scratch_shapes=[pltpu.VMEM((2, 768, 256), F32), pltpu.VMEM((64, 128), F32)],
        ),
        out_shape=[jax.ShapeDtypeStruct(*v) for v in shapes],
        compiler_params=pltpu.CompilerParams(vmem_limit_bytes=16 * 2**20),
        cost_estimate=pl.CostEstimate(
            flops=2 * 768 * 384 * 512 * 7, bytes_accessed=10 * 2**20, transcendentals=0),
        name="input_partials",
    )(table, *operands, *[operands[-1]] * 2, *gates)


def sum_core_kernel(own_ref, sib_ref, *refs):
    refs[-1][...] = (own_ref[...] + sib_ref[...].astype(F32)).astype(BF16)


def sum_core(own, sib, gates):
    half = pl.BlockSpec((N, 768), lambda i: (1, 0))
    return pl.pallas_call(
        sum_core_kernel,
        grid=(1,),
        in_specs=[half, half] + [ANYWHERE] * len(gates),
        out_specs=pl.BlockSpec((N, 768), lambda i: (0, 0)),
        out_shape=jax.ShapeDtypeStruct((N, 768), BF16),
        compiler_params=pltpu.CompilerParams(vmem_limit_bytes=4 * 2**20),
        name="sum_core",
    )(own, sib, *gates)


def token_kernel(tokens_ref, hidden_ref, own_ref, sib_ref, far_ref, gains_ref, out_own_ref,
                 out_sib_ref, grad_ref, out_ref, flag_ref):
    grad = own_ref[...] + sib_ref[...].astype(F32) + far_ref[...].astype(F32)
    xhat, factor = normalize(tokens_ref[...].astype(F32))
    grad_ref[...] = hidden_ref[...] + normalize_back(grad, xhat, factor, gains_ref[0:1, :])
    out_ref[...] = (out_own_ref[...] + out_sib_ref[...].astype(F32)).astype(BF16)
    flag_ref[...] = jnp.zeros(flag_ref.shape, F32)


def token_grads(tokens, hidden, own, sib, far, gains, out_own, out_sib):
    half = pl.BlockSpec((N, 768), lambda i: (0, 0))
    return pl.pallas_call(
        token_kernel,
        grid=(1,),
        in_specs=[half] * 5 + [pl.BlockSpec((4, 768), lambda i: (0, 0))] + [half] * 2,
        out_specs=[half] * 2 + [pl.BlockSpec((8, 128), lambda i: (0, 0))],
        out_shape=[jax.ShapeDtypeStruct((N, 768), F32), jax.ShapeDtypeStruct((N, 768), BF16),
                   jax.ShapeDtypeStruct((8, 128), F32)],
        compiler_params=pltpu.CompilerParams(vmem_limit_bytes=8 * 2**20),
        name="token_grads",
    )(tokens, hidden, own, sib, far, gains, out_own, out_sib)


def assemble_kernel(at_ref, own_ref, near_ref, away_ref, cross_ref, down_ref, up_ref, qkv_ref, out_ref,
                    vec_ref, below_ref, held):
    core, far = at_ref[CORE], at_ref[FAR]
    held[far * 2 + core] = own_ref[...]
    held[far * 2 + 1 - core] = near_ref[...]
    held[2 - far * 2 + core] = away_ref[...]
    held[2 - far * 2 + 1 - core] = cross_ref[...]
    line = held[far * 2, 2, 64:, :128].astype(F32) + held[far * 2 + 1, 2, 64:, :128].astype(F32)
    vec_ref[...] = jnp.where(core == 0, line, pltpu.roll(line, 122, 1))[8:]
    row = lax.broadcasted_iota(jnp.int32, (24, 80), 0)
    column = lax.broadcasted_iota(jnp.int32, (24, 80), 1)
    wanted = (row // 8) * 24 + far * 12 + core * 6 + row % 8
    select = jnp.where((column == wanted) & (row % 8 < 6), 1.0, 0.0).astype(BF16)
    for x_hi in range(2):
        for c in range(2):
            for g in range(3):
                rows = mm(select, held[x_hi * 2 + c, g])
                first = c * 1536 + g * 512 + x_hi * 256
                for e in range(2):
                    up_ref[:, e, first : first + 256] = rows[8 * e : 8 * e + 6] * UP_FACTORS[e]
                for n in range(2):
                    at = g * 512 + x_hi * 256 + n * 128
                    kind, within = at // 384, at % 384 + c * 384
                    part = rows[16:22, n * 128 : (n + 1) * 128]
                    if kind < 3:
                        qkv_ref[:, kind * 768 + within : kind * 768 + within + 128] = part
                    else:
                        out_ref[:, within : within + 128] = part
    for g in range(3):
        part = down_ref[g].astype(F32)
        for e in range(2):
            below_ref[e, :, g * 256 : (g + 1) * 256] = part[24 * e : 24 * e + 24] * UP_FACTORS[e]


def assemble(table, *parts):
    return pl.pallas_call(
        assemble_kernel,
        in_specs=[SMALL] + [WHOLE] * 5,
        out_specs=[WHOLE] * 5,
        out_shape=[
            jax.ShapeDtypeStruct((6, 2, 3072), F32),
            jax.ShapeDtypeStruct((6, 2304), F32),
            jax.ShapeDtypeStruct((6, 768), F32),
            jax.ShapeDtypeStruct((8, 128), F32),
            jax.ShapeDtypeStruct((2, 24, 768), F32),
        ],
        scratch_shapes=[pltpu.VMEM((4, 3, 80, 256), BF16)],
        compiler_params=pltpu.CompilerParams(vmem_limit_bytes=4 * 2**20),
        name="assemble",
    )(table, *parts)

def shards(tokens, first_gain, first_shift, w_qkv, w_out, second_gain, second_shift,
           w_up, w_down, modality, segments, partner, cotangent):
    table = lax.dynamic_index_in_dim(
        jnp.asarray(cell_places()), lax.axis_index(BOTH), 0, keepdims=False)
    gains = jnp.stack([first_gain, first_shift, second_gain, second_shift])

    far_tokens = swap_far(tokens[0])
    own, own_marks = marked(partner, tokens[0], segments, modality)
    far_marks = swap_far(own_marks)
    sib = swap_core(own)
    cot_own = cotangent[0]
    cot_sib = swap_core(cot_own)

    act1, marks, queries, k_near, v_near, qx = project(table, own, sib, gains, w_qkv, True)
    away = joined(far_tokens, far_marks, [qx])
    away_sib = swap_core(away)
    act1_away, marks_away, k_away, v_away = project(table, away, away_sib, gains, w_qkv, False)
    attended, lse = attend_forward(
        queries, k_near, k_away, v_near, v_away, qx, marks, marks_away)
    attended_sib = swap_core(attended)

    hidden, grad_act2, xhat2, factor2, act_t, inner_t, grad_pre = experts(
        table, attended, attended_sib, own, sib, cot_own, cot_sib, marks, gains, w_out, w_up, w_down)
    ff_kept, ff_first, more = [], [], [grad_act2]
    for g in range(3):
        keep, gone, *low = cells(g, table, act_t, grad_pre, inner_t, cot_own, cot_sib, marks, more)
        ff_kept.append(keep.reshape(2, 16, 96, 256))
        ff_first.append(send(gone.reshape(2, 16, 96, 256), axis_step(ORDERS[g][0], True)))
        if g == 0:
            grad_sib = swap_core(low[0])
        more = [keep] if g == 0 else [keep, grad_sib]
    hidden_grad, grad_att, proj_half, vectors = middle(
        table, grad_act2, grad_sib, xhat2, factor2, cot_own, cot_sib, gains, w_out)

    def along(stage, first, values):
        return [send(v, axis_step(ORDERS[g][stage], first)) for g, v in enumerate(values)]

    taken = (queries, k_near, k_away, v_near, v_away, grad_att, attended, qx, marks, marks_away, lse)
    q_a, k_a, v_a = attend_backward(taken, 0, 2, ())
    q_b, k_b, v_b = attend_backward(taken, 2, 1, ())
    cells_a = tail_cells(table, act1, act1_away, q_a, q_b, k_a, k_b, v_a)
    partial_own, partial_low, *cells_b = input_partials(table, (
        act1, act1_away, q_a, q_b, k_a, k_b, v_a, v_b, attended, attended_sib, proj_half,
        own, sib, away, away_sib, vectors, w_qkv), [cells_a[0]])
    kept = [v.reshape(2, 16, 32, 256) for v in (cells_a[0], cells_a[1], cells_b[0])]
    first = along(0, True, [v.reshape(2, 16, 32, 256) for v in (cells_a[2], cells_a[3], cells_b[1])])
    ff_second = along(0, False, pass_on(ff_kept, ff_first, "pass_first", [cells_b[0]]))
    partial_sib = swap_core(partial_low)
    second = along(0, False, pass_on(kept, first, "pass_tail", [partial_sib]))

    kept, sent = settle(
        [list(zip(ff_kept, ff_first, ff_second)), list(zip(kept, first, second))], "settle_all")
    first = along(1, True, sent)
    from_far = swap_far(sum_core(partial_own, partial_sib, sent))
    passed = pass_on(kept, first, "pass_second", [from_far])
    second = along(1, False, passed)
    out_own, out_sib = branches(table, inner_t, w_down, hidden, marks, passed)
    kept, sent = settle([list(zip(kept, first, second))], "settle_second", [out_sib])
    first = along(2, True, sent)
    token_grad, layer_output, flag = token_grads(
        tokens[0], hidden_grad, partial_own, partial_sib, from_far, gains, out_own, swap_core(out_sib))
    second = along(2, False, pass_on(kept, first, "pass_third"))
    held, down_held = finish(kept, first, second, [flag])

    near, beyond = swap_core(held), swap_far(held)
    cross = send(held, lambda x, y, z, c: (x ^ 2, y, z, 1 - c))
    below = send(down_held, lambda x, y, z, c: (x, y, 2 * c + z % 2, z // 2))
    up_grad, qkv_grad, out_grad, line, down_grad = assemble(
        table, held, near, beyond, cross, below)

    return (
        layer_output[None], token_grad[None], line[0, :6], line[0, 12:18], qkv_grad, out_grad,
        line[0, 24:30], line[0, 36:42], up_grad.transpose(1, 0, 2), down_grad)


def solution(mesh):
    cut = P("rows", "seq", None)
    flat = P(BOTH)
    placed = (cut,) + (P(),) * 8 + (P("rows", "seq"), P("rows", "seq"), P("rows", None), cut)
    return jax.shard_map(
        shards, mesh=mesh, in_specs=placed,
        out_specs=(cut, cut, flat, flat, P(BOTH, None), P(BOTH, None), flat, flat,
                   P(None, BOTH, None), P(None, BOTH, None)),
        check_vma=False)
```

```python
import jax
import jax.numpy as jnp
import numpy as np
from jax import lax
from jax.experimental import pallas as pl
from jax.experimental.pallas import tpu as pltpu
from jax.sharding import PartitionSpec as P

HD = 64
OWN = 6
CORE, FAR = 768, 769
IMG = 197
NIMG = 4
BOTH = ("rows", "seq")
F32 = jnp.float32
BF16 = jnp.bfloat16
MASKED = -1e30


def route(step):
    pairs = []
    for r in range(32):
        z, x_lo, y = r // 8, (r // 4) % 2, r % 4
        for s in range(4):
            x, c = (s // 2) * 2 + x_lo, s % 2
            tx, ty, tz, tc = step(x, y, z, c)
            target = (tz * 8 + (tx % 2) * 4 + ty) * 4 + (tx // 2) * 2 + tc
            pairs.append((r * 4 + s, target))
    return pairs


def send(values, step):
    return lax.ppermute(values, BOTH, route(step))


def swap_core(values):
    return send(values, lambda x, y, z, c: (x, y, z, 1 - c))


def swap_far(values):
    return send(values, lambda x, y, z, c: (x ^ 2, y, z, c))


def axis_step(axis, first):
    def step(x, y, z, c):
        flip = 1 if (c == 0) == first else 3
        at = {"x": x, "y": y, "z": z}
        at[axis] ^= flip
        return (at["x"], at["y"], at["z"], c)

    return step


UP_FACTORS = (1024 / (2 * 788), 1024 / (2 * 236))
ORDERS = (("x", "y", "z"), ("y", "z", "x"), ("z", "x", "y"))


def normalize(inputs):
    centred = inputs - jnp.mean(inputs, axis=-1, keepdims=True)
    factor = lax.rsqrt(jnp.mean(centred * centred, axis=-1, keepdims=True) + 1e-05)
    return centred * factor, factor


def normalize_back(grad, xhat, factor, gain):
    gy = grad * gain
    mean_gy = jnp.mean(gy, axis=-1, keepdims=True)
    mean_gx = jnp.mean(gy * xhat, axis=-1, keepdims=True)
    return factor * (gy - mean_gy - xhat * mean_gx)


SMALL = pl.BlockSpec(memory_space=pltpu.SMEM)
WHOLE = pl.BlockSpec(memory_space=pltpu.VMEM)
N = 256


def marked_kernel(partner, tokens_ref, segments_ref, modality_ref, out_ref):
    segments = segments_ref[...]
    tag = jnp.zeros(segments.shape, jnp.int32)
    for n in range(8):
        tag = jnp.where(segments == n, partner[0, n], tag)
    marks = jnp.concatenate(
        [tag, modality_ref[...], jnp.zeros((1, 256), jnp.int32)], axis=1).astype(F32)
    out_ref[:N, :] = tokens_ref[...]
    out_ref[N:, :] = jnp.concatenate([marks, jnp.zeros((15, 768), F32)], axis=0).astype(BF16)


def marked(partner, tokens, segments, modality):
    return pl.pallas_call(
        marked_kernel,
        in_specs=[SMALL, WHOLE, WHOLE, WHOLE],
        out_specs=WHOLE,
        out_shape=jax.ShapeDtypeStruct((N + 16, 768), BF16),
        compiler_params=pltpu.CompilerParams(vmem_limit_bytes=60 * 2**20),
        name="marked",
    )(partner, tokens, segments, modality)


def mark_lanes(ext):
    row = ext[N:, :].astype(F32)
    place = lax.broadcasted_iota(jnp.int32, (128, N), 0)
    tag = jnp.broadcast_to(row[:1, :N], (128, N))
    kind = jnp.broadcast_to(row[:1, N : 2 * N], (128, N))
    hot = jnp.where((place < NIMG) & (place.astype(F32) == tag), 1.0, 0.0)
    return jnp.transpose(jnp.where(place == 8, kind, hot))


def project_kernel(at_ref, near, a_ref, b_ref, gains_ref, *refs):
    count = 3 if near else 2
    weights, outs = refs[:count], refs[count:]
    for n, ext_ref in enumerate((a_ref, b_ref)):
        rows = slice(n * N, (n + 1) * N)
        ext = ext_ref[...]
        xhat, _ = normalize(ext[:N].astype(F32))
        act = (xhat * gains_ref[0:1, :] + gains_ref[1:2, :]).astype(BF16)
        outs[0][rows, :] = act
        marks = mark_lanes(ext)
        outs[1][rows, :] = marks.astype(BF16)
        for m in range(count):
            part = mm(act, weights[m][...])
            outs[2 + m][rows, :] = (0.125 * part if near and m == 0 else part).astype(BF16)
        if near:
            lane = lax.broadcasted_iota(jnp.int32, marks.shape, 1)
            outs[5][rows, :] = jnp.where((lane < NIMG) & (marks == 0.0), MASKED, 0.0).astype(BF16)


def project(table, first, second, gains, w_qkv, near):
    kinds = (0, 1, 2) if near else (1, 2)
    sizes = [768, 128] + [384] * len(kinds) + ([128] if near else [])
    whole = lambda shape: pl.BlockSpec(shape, lambda i, at: (0, 0))
    return pl.pallas_call(
        lambda at_ref, *refs: project_kernel(at_ref, near, *refs),
        grid_spec=pltpu.PrefetchScalarGridSpec(
            num_scalar_prefetch=1,
            grid=(1,),
            in_specs=[whole((N + 16, 768))] * 2 + [whole((4, 768))]
            + [pl.BlockSpec((768, 384), lambda i, at, n=n: (0, 2 * n + at[CORE])) for n in kinds],
            out_specs=[whole((2 * N, size)) for size in sizes],
        ),
        out_shape=[jax.ShapeDtypeStruct((2 * N, size), BF16) for size in sizes],
        compiler_params=pltpu.CompilerParams(vmem_limit_bytes=6 * 2**20),
        cost_estimate=pl.CostEstimate(
            flops=2 * 512 * 768 * 384 * len(kinds), bytes_accessed=4 * 2**20, transcendentals=0),
        name="project_near" if near else "project_away",
    )(table, first, second, gains, *[w_qkv] * len(kinds))


def middle_kernel(place, grad_ref, sib_ref, xhat_ref, factor_ref, cot_own_ref, cot_sib_ref,
                  gains_ref, w_out_ref, hidden_ref, att_ref, proj_ref, vec_ref):
    core = place[CORE]
    for n, cot_ref in enumerate((cot_own_ref, cot_sib_ref)):
        rows, other = slice(n * N, (n + 1) * N), slice((1 - n) * N, (2 - n) * N)
        grad = grad_ref[rows, :].astype(F32) + sib_ref[other, :].astype(F32)
        xhat = xhat_ref[rows, :].astype(F32)
        total = cot_ref[...].astype(F32) + normalize_back(grad, xhat, factor_ref[rows, :], gains_ref[2:3, :])
        low = total.astype(BF16)
        if n == 0:
            hidden_ref[...] = total
            vec_ref[0:1, :] = jnp.sum(grad * xhat, axis=0, keepdims=True)
            vec_ref[1:2, :] = jnp.sum(grad, axis=0, keepdims=True)
        mine = w_out_ref[pl.ds(pl.multiple_of(core * 384, 384), 384), :]
        att_ref[rows, :] = mm(low, mine, NT).astype(BF16)
        proj_ref[rows, :] = jnp.where(core == 0, low[:, :384], low[:, 384:])


def middle(place, *operands):
    return pl.pallas_call(
        middle_kernel,
        in_specs=[SMALL] + [WHOLE] * len(operands),
        out_specs=[WHOLE] * 4,
        out_shape=[
            jax.ShapeDtypeStruct((N, 768), F32),
            jax.ShapeDtypeStruct((2 * N, 384), BF16),
            jax.ShapeDtypeStruct((2 * N, 384), BF16),
            jax.ShapeDtypeStruct((2, 768), F32),
        ],
        compiler_params=pltpu.CompilerParams(vmem_limit_bytes=6 * 2**20),
        cost_estimate=pl.CostEstimate(
            flops=2 * 512 * 768 * 384, bytes_accessed=8 * 2**20, transcendentals=0),
        name="middle",
    )(place, *operands)


def gelu_parts(pre):
    phi = 0.5 * (1.0 + lax.erf(pre * 0.7071067811865476))
    slope = phi + pre * (0.3989422804014327 * jnp.exp(-0.5 * pre * pre))
    return pre * phi, slope


NT = (((1,), (1,)), ((), ()))
TN = (((0,), (0,)), ((), ()))
NN = (((1,), (0,)), ((), ()))


def mm(left, right, dims=NN):
    return lax.dot_general(left, right, dims, preferred_element_type=F32)


def head_lanes(shape, h):
    lane = lax.broadcasted_iota(jnp.int32, shape, len(shape) - 1)
    return (lane >= HD) == (h == 1)


def turned(values):
    return jnp.transpose(values.astype(F32)).astype(BF16)


def stacked(near_ref, away_ref):
    return jnp.concatenate([near_ref[...], away_ref[...]], axis=0)


def forward_kernel(q_ref, kn_ref, ka_ref, vn_ref, va_ref, qx_ref, xn_ref, xa_ref, out_ref, lse_ref):
    keys = jnp.concatenate([stacked(kn_ref, ka_ref), stacked(xn_ref, xa_ref)], axis=1)
    values = stacked(vn_ref, va_ref)
    q_pair = q_ref[...]
    lanes = head_lanes(q_pair.shape, 0)
    values_t = turned(values)
    value_rows = lax.broadcasted_iota(jnp.int32, values_t.shape, 0) < HD
    mixed = []
    for h in range(2):
        mine = lanes if h == 0 else jnp.logical_not(lanes)
        mine_values = value_rows if h == 0 else jnp.logical_not(value_rows)
        query = jnp.concatenate([jnp.where(mine, q_pair, 0), qx_ref[...]], axis=1)
        scores = mm(keys, query, NT)
        peak = jnp.max(scores, axis=0, keepdims=True)
        weights = jnp.exp(scores - peak).astype(BF16)
        both = mm(jnp.where(mine_values, values_t, 1), weights)
        total = both[127:128, :] if h == 0 else both[0:1, :]
        mixed.append(both * (1.0 / total))
        lse_ref[0, h : h + 1, :] = peak + jnp.log(total)
    out_rows = lax.broadcasted_iota(jnp.int32, mixed[0].shape, 0) < HD
    out_ref[...] = jnp.transpose(jnp.where(out_rows, mixed[0], mixed[1])).astype(BF16)


BY_PAIR = pl.BlockSpec((2 * N, 128), lambda p: (0, p))
FIXED = pl.BlockSpec((2 * N, 128), lambda p: (0, 0))


def attend_forward(*operands):
    return pl.pallas_call(
        forward_kernel,
        grid=(3,),
        in_specs=[BY_PAIR] * 5 + [FIXED] * 3,
        out_specs=[BY_PAIR, pl.BlockSpec((1, 2, 2 * N), lambda p: (p, 0, 0))],
        out_shape=[
            jax.ShapeDtypeStruct((2 * N, 384), BF16),
            jax.ShapeDtypeStruct((3, 2, 2 * N), F32),
        ],
        compiler_params=pltpu.CompilerParams(vmem_limit_bytes=6 * 2**20),
        cost_estimate=pl.CostEstimate(
            flops=2 * 2 * OWN * 512 * 1024 * 256, bytes_accessed=4 * 2**20,
            transcendentals=OWN * 512 * 1024),
        name="attend_forward",
    )(*operands)


def backward_kernel(q_ref, kn_ref, ka_ref, vn_ref, va_ref, do_ref, o_ref, qx_ref, xn_ref, xa_ref,
                    lse_ref, *refs):
    dq_ref, dk_ref, dv_ref = refs[-3:]
    k_pair, values = stacked(kn_ref, ka_ref), stacked(vn_ref, va_ref)
    keys = jnp.concatenate([k_pair, stacked(xn_ref, xa_ref)], axis=1)
    q_pair, grads = q_ref[...], do_ref[...]
    lanes = head_lanes(q_pair.shape, 0)
    product = grads.astype(F32) * o_ref[...].astype(F32)
    k_turned = turned(k_pair)
    rows = lax.broadcasted_iota(jnp.int32, (128, 2 * N), 0) < HD
    dq = jnp.zeros((128, 2 * N), F32)
    dk = jnp.zeros(k_pair.shape, F32)
    dv = jnp.zeros(k_pair.shape, F32)
    for h in range(2):
        mine = lanes if h == 0 else jnp.logical_not(lanes)
        q_head = jnp.where(mine, q_pair, 0)
        g_head = jnp.where(mine, grads, 0)
        dot_row = jnp.transpose(jnp.sum(jnp.where(mine, product, 0.0), axis=1, keepdims=True))
        scores = mm(keys, jnp.concatenate([q_head, qx_ref[...]], axis=1), NT)
        prob = jnp.exp(scores - lse_ref[0, h : h + 1, :])
        dv += mm(prob.astype(BF16), g_head)
        grad_prob = mm(values, g_head, NT)
        grad_scores = (prob * (grad_prob - dot_row)).astype(BF16)
        dk += mm(grad_scores, q_head)
        part = mm(k_turned, grad_scores)
        dq += jnp.where(rows if h == 0 else jnp.logical_not(rows), part, 0.0)
    dq_ref[...] = jnp.transpose(dq).astype(BF16) * jnp.asarray(0.125, BF16)
    dk_ref[...] = dk.astype(BF16)
    dv_ref[...] = dv.astype(BF16)


def attend_backward(operands, first, pairs, gates):
    by_pair = pl.BlockSpec((2 * N, 128), lambda p: (0, first + p))
    sizes = (2 * N, 4 * N, 4 * N)
    return pl.pallas_call(
        backward_kernel,
        grid=(pairs,),
        in_specs=[by_pair] * 7 + [FIXED] * 3
        + [pl.BlockSpec((1, 2, 2 * N), lambda p: (first + p, 0, 0))]
        + [pl.BlockSpec(memory_space=pl.ANY)] * len(gates),
        out_specs=[pl.BlockSpec((size, 128), lambda p: (0, p)) for size in sizes],
        out_shape=[jax.ShapeDtypeStruct((size, pairs * 128), BF16) for size in sizes],
        compiler_params=pltpu.CompilerParams(vmem_limit_bytes=10 * 2**20),
        cost_estimate=pl.CostEstimate(
            flops=2 * 5 * 2 * pairs * 512 * 1024 * 256, bytes_accessed=6 * 2**20,
            transcendentals=2 * pairs * 512 * 1024),
        name="attend_backward",
    )(*operands, *gates)


FF_STEP = 512
E_STEP = 512
EXPERT_MB = 40
CELLS_MB = 28


def expert_kernel(at_ref, att_own_ref, att_sib_ref, own_ref, sib_ref, cot_own_ref, cot_sib_ref,
                  marks_ref, gains_ref, w_out_ref, wu_ref, wd_ref,
                  hidden_ref, low_ref, xhat_ref, factor_ref, act_t_ref, inner_t_ref, slope_ref,
                  act_acc, grad_acc):
    f = pl.program_id(0)
    core = at_ref[CORE]

    @pl.when(f == 0)
    def _():
        mine = w_out_ref[pl.ds(pl.multiple_of(core * 384, 384), 384), :]
        other = w_out_ref[pl.ds(pl.multiple_of((1 - core) * 384, 384), 384), :]
        for n, ext_ref in enumerate((own_ref, sib_ref)):
            rows, theirs = slice(n * N, (n + 1) * N), slice((1 - n) * N, (2 - n) * N)
            hidden = ext_ref[:N, :].astype(F32) + (
                mm(att_own_ref[rows, :], mine) + mm(att_sib_ref[theirs, :], other))
            xhat, factor = normalize(hidden)
            xhat_ref[rows, :] = xhat.astype(BF16)
            factor_ref[rows, :] = factor
            act = xhat * gains_ref[2:3, :] + gains_ref[3:4, :]
            act_acc[rows, :] = act.astype(BF16)
            act_t_ref[:, rows] = jnp.transpose(act).astype(BF16)
            if n == 0:
                hidden_ref[...] = hidden
        grad_acc[...] = jnp.zeros(grad_acc.shape, F32)

    act = act_acc[...]
    cot = jnp.concatenate([cot_own_ref[...], cot_sib_ref[...]], axis=0)
    text = marks_ref[:, 8:9].astype(F32) > 0.0
    pre = jnp.where(text, mm(act, wu_ref[1]), mm(act, wu_ref[0]))
    inner, slope = gelu_parts(pre)
    grad_pre = jnp.where(text, mm(cot, wd_ref[1], NT), mm(cot, wd_ref[0], NT)) * slope
    inner_t_ref[...] = jnp.transpose(inner).astype(BF16)
    low = grad_pre.astype(BF16)
    slope_ref[...] = low
    zero = jnp.zeros((), BF16)
    grad_acc[...] += (mm(jnp.where(text, zero, low), wu_ref[0], NT)
                      + mm(jnp.where(text, low, zero), wu_ref[1], NT))

    @pl.when(f == pl.num_programs(0) - 1)
    def _():
        low_ref[...] = grad_acc[...].astype(BF16)


def experts(core, *operands):
    steps = 1536 // E_STEP
    shapes = [((N, 768), F32), ((2 * N, 768), BF16), ((2 * N, 768), BF16), ((2 * N, 1), F32),
              ((768, 2 * N), BF16)]
    fixed = lambda shape: pl.BlockSpec(shape, lambda f, *_: (0,) * len(shape))
    return pl.pallas_call(
        expert_kernel,
        grid_spec=pltpu.PrefetchScalarGridSpec(
            num_scalar_prefetch=1,
            grid=(steps,),
            in_specs=[fixed(v.shape) for v in operands[:-2]] + [
                pl.BlockSpec((2, 768, E_STEP), lambda f, at: (0, 0, at[CORE] * steps + f)),
                pl.BlockSpec((2, E_STEP, 768), lambda f, at: (0, at[CORE] * steps + f, 0)),
            ],
            out_specs=[fixed(shape) for shape, _ in shapes] + [
                pl.BlockSpec((E_STEP, 2 * N), lambda f, at: (f, 0)),
                pl.BlockSpec((2 * N, E_STEP), lambda f, at: (0, f)),
            ],
            scratch_shapes=[pltpu.VMEM((2 * N, 768), BF16), pltpu.VMEM((2 * N, 768), F32)],
        ),
        out_shape=[jax.ShapeDtypeStruct(*v) for v in shapes] + [
            jax.ShapeDtypeStruct((1536, 2 * N), BF16),
            jax.ShapeDtypeStruct((2 * N, 1536), BF16)],
        compiler_params=pltpu.CompilerParams(
            vmem_limit_bytes=18 * 2**20, dimension_semantics=("arbitrary",)),
        cost_estimate=pl.CostEstimate(
            flops=6 * 2 * 512 * 768 * 1536 + 2 * 512 * 768 * 768, bytes_accessed=22 * 2**20,
            transcendentals=2 * 512 * 1536),
        name="experts",
    )(core, *operands)


def kind_row(marks_ref):
    return turned(marks_ref[...])[8:9, :].astype(F32) > 0.0


def branch_kernel(at_ref, inner_t_ref, wd_ref, hidden_ref, marks_ref, *refs):
    own_ref, sib_ref, acc = refs[-3:]
    f = pl.program_id(0)
    text, inner_t, zero = kind_row(marks_ref), inner_t_ref[...], jnp.zeros((), BF16)
    part = (mm(jnp.where(text, zero, inner_t), wd_ref[0], TN)
            + mm(jnp.where(text, inner_t, zero), wd_ref[1], TN))

    @pl.when(f == 0)
    def _():
        acc[...] = part

    @pl.when(f > 0)
    def _():
        acc[...] += part

    @pl.when(f == pl.num_programs(0) - 1)
    def _():
        own_ref[...] = hidden_ref[...] + acc[:N, :]
        sib_ref[...] = acc[N:, :].astype(BF16)


def branches(table, inner_t, w_down, hidden, marks, gates):
    return pl.pallas_call(
        branch_kernel,
        grid_spec=pltpu.PrefetchScalarGridSpec(
            num_scalar_prefetch=1,
            grid=(3,),
            in_specs=[
                pl.BlockSpec((512, 2 * N), lambda f, at: (f, 0)),
                pl.BlockSpec((2, 512, 768), lambda f, at: (0, at[CORE] * 3 + f, 0)),
                pl.BlockSpec((N, 768), lambda f, at: (0, 0)),
                pl.BlockSpec((2 * N, 128), lambda f, at: (0, 0))] + [ANYWHERE] * len(gates),
            out_specs=[pl.BlockSpec((N, 768), lambda f, at: (0, 0))] * 2,
            scratch_shapes=[pltpu.VMEM((2 * N, 768), F32)],
        ),
        out_shape=[jax.ShapeDtypeStruct((N, 768), F32), jax.ShapeDtypeStruct((N, 768), BF16)],
        compiler_params=pltpu.CompilerParams(
            vmem_limit_bytes=20 * 2**20, dimension_semantics=("arbitrary",)),
        cost_estimate=pl.CostEstimate(
            flops=2 * 2 * 512 * 768 * 1536, bytes_accessed=8 * 2**20, transcendentals=0),
        name="branches",
    )(table, inner_t, w_down, hidden, marks, *gates)


def cells_kernel(g, at_slot, act_t_ref, grad_ref, inner_t_ref, cot_own_ref, cot_sib_ref, marks_ref,
                 *refs):
    if g == 0:
        full_ref, keep_ref, send_ref, low_ref, up_acc, down_acc = refs
        low_ref[...] = full_ref[...]
    else:
        keep_ref, send_ref, up_acc, down_acc = refs[-4:]
    e = pl.program_id(0)
    zero = jnp.zeros((), BF16)
    mine = (marks_ref[:, 8:9].astype(F32) > 0.0) == (e == 1)
    mine_row = kind_row(marks_ref) == (e == 1)
    up = mm(act_t_ref[...], jnp.where(mine, grad_ref[...], zero))
    up_acc[e, 0] = up[:, :256]
    up_acc[e, 1] = up[:, 256:]
    cot = jnp.concatenate([cot_own_ref[...], cot_sib_ref[...]], axis=0)
    down_acc[e] = mm(jnp.where(mine_row, inner_t_ref[...], zero), cot)

    def spill(target, base):
        def cell(i, carry):
            slot = g * 64 + base + i
            half = at_slot[192 + slot]
            rows = pl.ds(pl.multiple_of(at_slot[slot], 8), 24)
            below = pl.ds(pl.multiple_of(at_slot[384 + slot], 8), 24)
            target[i] = jnp.concatenate(
                [up_acc[0, half, rows, :], up_acc[1, half, rows, :],
                 down_acc[0, below, :], down_acc[1, below, :]], axis=0).astype(BF16)
            return carry
        lax.fori_loop(0, 32, cell, 0, unroll=4)

    @pl.when(e == 1)
    def _():
        spill(keep_ref, 0)
        spill(send_ref, 32)


def cells(g, table, act_t, grad_pre, inner_t, cot_own, cot_sib, marks, more):
    cot = pl.BlockSpec((N, 256), lambda e, t: (0, g))
    out = pl.BlockSpec((32, 96, 256), lambda e, t: (0, 0, 0))
    low = pl.BlockSpec((N, 768), lambda e, t: (e, 0))
    return pl.pallas_call(
        lambda *refs: cells_kernel(g, *refs),
        grid_spec=pltpu.PrefetchScalarGridSpec(
            num_scalar_prefetch=1,
            grid=(2,),
            in_specs=[
                pl.BlockSpec((768, 2 * N), lambda e, t: (0, 0)),
                pl.BlockSpec((2 * N, FF_STEP), lambda e, t: (0, g)),
                pl.BlockSpec((1536, 2 * N), lambda e, t: (0, 0)),
                cot, cot, pl.BlockSpec((2 * N, 128), lambda e, t: (0, 0))] + ([low] if g == 0 else [ANYWHERE] * len(more)),
            out_specs=[out] * 2 + [low] * (g == 0),
            scratch_shapes=[pltpu.VMEM((2, 2, 768, 256), F32), pltpu.VMEM((2, 1536, 256), F32)],
        ),
        out_shape=[jax.ShapeDtypeStruct((32, 96, 256), BF16)] * 2
        + [jax.ShapeDtypeStruct((2 * N, 768), BF16)] * (g == 0),
        compiler_params=pltpu.CompilerParams(
            vmem_limit_bytes=10 * 2**20, dimension_semantics=("arbitrary",)),
        cost_estimate=pl.CostEstimate(
            flops=4 * 2 * 512 * 768 * 512, bytes_accessed=8 * 2**20, transcendentals=0),
        name="cells",
    )(table, act_t, grad_pre, inner_t, cot_own, cot_sib, marks, *more)


def cell_places():
    table = np.zeros((32, 4, 4, 3, 4, 4, 4), np.int32)
    for r, s in np.ndindex(32, 4):
        here = {"z": r // 8, "y": r % 4, "x": (s // 2) * 2 + (r // 4) % 2}
        flips = (0, 1, 3, 2) if s % 2 else (0, 3, 1, 2)
        for g, order in enumerate(ORDERS):
            for slot in np.ndindex(4, 4, 4):
                at = {a: here[a] ^ flips[n] for a, n in zip(order, slot)}
                x_hi, x_lo = at["x"] // 2, at["x"] % 2
                table[(r, s, 0, g) + slot] = 24 * (at["z"] * 8 + x_lo * 4 + at["y"])
                table[(r, s, 1, g) + slot] = x_hi
                table[(r, s, 2, g) + slot] = 24 * (
                    (at["z"] % 2) * 32 + x_lo * 16 + at["y"] * 4 + x_hi * 2 + at["z"] // 2)
                table[(r, s, 3, g) + slot] = at["z"] * 16 + x_lo * 8 + at["y"] * 2 + x_hi
    coordinates = np.array([[n % 2, n % 4 // 2] + [0] * 126 for n in range(128)], np.int32)
    return np.concatenate([table.reshape(128, 768), coordinates], axis=1)


def add_up(parts):
    total = parts[0].astype(F32)
    for part in parts[1:]:
        total = total + part.astype(F32)
    return total.astype(BF16)


def in_hbm(values):
    return list(values)


def pass_kernel(gates, *refs):
    count = (len(refs) - gates) // 3
    for g in range(count):
        refs[2 * count + gates + g][...] = add_up([refs[2 * g][...], refs[2 * g + 1][...]])


ANYWHERE = pl.BlockSpec(memory_space=pl.ANY)


def pass_on(kept, arrived, name, gates=()):
    _, slots, rows, lanes = kept[0].shape
    block = max(slots // 4, 1)
    one = pl.BlockSpec((None, block, rows, lanes), lambda i: (1, i, 0, 0))
    return pl.pallas_call(
        lambda *refs: pass_kernel(len(gates), *refs),
        grid=(slots // block,),
        in_specs=[one] * (2 * len(kept)) + [ANYWHERE] * len(gates),
        out_specs=[pl.BlockSpec((block, rows, lanes), lambda i: (i, 0, 0))] * len(kept),
        out_shape=[jax.ShapeDtypeStruct((slots, rows, lanes), BF16)] * len(kept),
        compiler_params=pltpu.CompilerParams(vmem_limit_bytes=6 * 2**20),
        cost_estimate=pl.CostEstimate(
            flops=0, transcendentals=0, bytes_accessed=6 * len(kept) * slots * rows * lanes),
        name=name,
    )(*in_hbm([v for pair in zip(kept, arrived) for v in pair]), *gates)


def settle_kernel(groups, sizes, *refs):
    ins, outs = refs, refs[-2 * groups :]
    at = 0
    for g in range(groups):
        row = 0
        for size in sizes:
            for half in range(2):
                outs[2 * g + half][:, row : row + size, :] = add_up(
                    [ins[at + k][...] for k in range(3)])
                at += 3
            row += size


def settle(pieces, name, gates=()):
    groups = len(pieces[0])
    sizes = [p[0][0].shape[2] for p in pieces]
    _, slots, _, lanes = pieces[0][0][0].shape
    half = slots // 2
    block = max(half // 4, 1)
    steps = half // block
    operands, specs = [], []
    for g in range(groups):
        for p, size in zip(pieces, sizes):
            for h in range(2):
                wide = pl.BlockSpec(
                    (None, block, size, lanes), lambda i, h=h: (0, i + h * steps, 0, 0))
                flat = pl.BlockSpec((block, size, lanes), lambda i, h=h: (i + h * steps, 0, 0))
                operands += list(p[g])
                specs += [wide, wide, flat]
    rows = sum(sizes)
    outs = pl.pallas_call(
        lambda *refs: settle_kernel(groups, sizes, *refs),
        grid=(steps,),
        in_specs=specs + [ANYWHERE] * len(gates),
        out_specs=[pl.BlockSpec((block, rows, lanes), lambda i: (i, 0, 0))] * (2 * groups),
        out_shape=[jax.ShapeDtypeStruct((half, rows, lanes), BF16)] * (2 * groups),
        compiler_params=pltpu.CompilerParams(vmem_limit_bytes=8 * 2**20),
        cost_estimate=pl.CostEstimate(
            flops=0, transcendentals=0, bytes_accessed=8 * groups * slots * rows * lanes),
        name=name,
    )(*operands, *gates)
    shaped = [o.reshape(2, half // 2, rows, lanes) for o in outs]
    return shaped[0::2], shaped[1::2]


def finish_kernel(*refs):
    held_ref, down_ref = refs[-2:]
    for g in range(3):
        cell = add_up([refs[3 * g + k][...] for k in range(3)])
        held_ref[g, :48, :] = cell[:48]
        held_ref[g, 48:, :] = cell[96:]
        down_ref[g] = cell[48:96]


def finish(kept, first, second, gates):
    wide = pl.BlockSpec((None, None, 128, 256), lambda i: (0, 0, 0, 0))
    flat = pl.BlockSpec((None, 128, 256), lambda i: (0, 0, 0))
    return pl.pallas_call(
        finish_kernel,
        grid=(1,),
        in_specs=[wide, wide, flat] * 3 + [ANYWHERE] * len(gates),
        out_specs=[pl.BlockSpec((3, 80, 256), lambda i: (0, 0, 0)),
                   pl.BlockSpec((3, 48, 256), lambda i: (0, 0, 0))],
        out_shape=[jax.ShapeDtypeStruct((3, 80, 256), BF16), jax.ShapeDtypeStruct((3, 48, 256), BF16)],
        compiler_params=pltpu.CompilerParams(vmem_limit_bytes=4 * 2**20),
        name="finish",
    )(*[v for g in range(3) for v in (kept[g], first[g], second[g])], *gates)


def after_kernel(values_ref, *refs):
    refs[-1][...] = values_ref[...]


def after(values, gates):
    return pl.pallas_call(
        after_kernel,
        in_specs=[WHOLE] + [ANYWHERE] * len(gates),
        out_specs=WHOLE,
        out_shape=jax.ShapeDtypeStruct(values.shape, values.dtype),
        compiler_params=pltpu.CompilerParams(vmem_limit_bytes=4 * 2**20),
        name="after",
    )(values, *gates)


def put(acc, first, part, rows=slice(None)):
    for n in range(part.shape[1] // 128):
        column = first + n * 128
        lanes = slice(column % 256, column % 256 + 128)
        acc[column // 256, rows, lanes] = part[:, n * 128 : (n + 1) * 128]


def spill_rows(target, acc, at_slot, g, base, extra):
    def cell(i, carry):
        slot = g * 64 + base + i
        rows = pl.ds(pl.multiple_of(at_slot[slot], 8), 24)
        part = acc[at_slot[192 + slot] + 2 * (g % 2), rows, :]
        target[i] = jnp.concatenate([part, extra(slot)], axis=0).astype(BF16)
        return carry
    lax.fori_loop(0, 32, cell, 0, unroll=4)


def tail_kernel(at_slot, act_ref, away_ref, q_ref, qb_ref, ka_ref, kb_ref, va_ref, *refs):
    keeps, sends, acc = refs[-5:-3], refs[-3:-1], refs[-1]
    act, away = act_ref[...], away_ref[...]
    near = mm(act, jnp.concatenate(
        [r[: 2 * N, :] for r in (q_ref, qb_ref, ka_ref, kb_ref, va_ref)], axis=1), TN)
    far = mm(away, jnp.concatenate(
        [r[2 * N :, :] for r in (ka_ref, kb_ref, va_ref)], axis=1), TN)
    put(acc, 0, near[:, :384])
    put(acc, 384, near[:, 384:] + far)
    for g in range(2):
        blank = lambda slot: jnp.zeros((8, 256), F32)
        spill_rows(keeps[g], acc, at_slot, g, 0, blank)
        spill_rows(sends[g], acc, at_slot, g, 32, blank)


def tail_cells(table, *operands):
    return pl.pallas_call(
        tail_kernel,
        in_specs=[SMALL] + [WHOLE] * len(operands),
        out_specs=[WHOLE] * 4,
        out_shape=[jax.ShapeDtypeStruct((32, 32, 256), BF16)] * 4,
        scratch_shapes=[pltpu.VMEM((4, 768, 256), F32)],
        compiler_params=pltpu.CompilerParams(vmem_limit_bytes=14 * 2**20),
        cost_estimate=pl.CostEstimate(
            flops=2 * 768 * 512 * (1024 + 640), bytes_accessed=8 * 2**20, transcendentals=0),
        name="tail_cells",
    )(table, *operands)


def inputs_kernel(at_slot, act_ref, away_ref, q_ref, qb_ref, ka_ref, kb_ref, va_ref, vb_ref,
                  att_own_ref, att_sib_ref, proj_ref, own_ref, sib_ref, far_ref, far_sib_ref,
                  second_ref, *refs):
    weights = refs[:3]
    keep_ref, send_ref, cell_keep, cell_send, acc, table = refs[-6:]
    core = at_slot[CORE]
    put(acc, 0, mm(act_ref[...], vb_ref[: 2 * N, :], TN) + mm(away_ref[...], vb_ref[2 * N :, :], TN))
    mine = pl.ds(pl.multiple_of(core * 384, 384), 384)
    other = pl.ds(pl.multiple_of((1 - core) * 384, 384), 384)
    put(acc, 128, mm(att_own_ref[...], proj_ref[...], TN), mine)
    put(acc, 128, mm(att_sib_ref[:N, :], proj_ref[N:, :], TN)
        + mm(att_sib_ref[N:, :], proj_ref[:N, :], TN), other)

    vectors = [jnp.zeros((1, 768), F32)] * 2 + [second_ref[0:1, :], second_ref[1:2, :]]
    wide = list(zip((q_ref, ka_ref, va_ref), (qb_ref, kb_ref, vb_ref), weights))
    for n, ext_ref in enumerate((own_ref, sib_ref, far_ref, far_sib_ref)):
        rows = slice(n * N, (n + 1) * N)
        total = jnp.zeros((N, 768), F32)
        for a_ref, b_ref, w_ref in wide[0 if n < 2 else 1 :]:
            grads = jnp.concatenate([a_ref[rows, :], b_ref[rows, :]], axis=1)
            total += mm(grads, w_ref[...], NT)
        xhat, _ = normalize(ext_ref[:N, :].astype(F32))
        vectors[0] += jnp.sum(total * xhat, axis=0, keepdims=True)
        vectors[1] += jnp.sum(total, axis=0, keepdims=True)
        half = slice((n // 2) * N, (n // 2 + 1) * N)
        if n % 2 == 0:
            keep_ref[half, :] = total
        else:
            send_ref[half, :] = total.astype(BF16)

    chip = lax.broadcasted_iota(jnp.int32, (64, 768), 0)
    owner = lax.broadcasted_iota(jnp.int32, (64, 768), 1) // 12
    feature = lax.broadcasted_iota(jnp.int32, (768, 128), 0) % 12
    lane = lax.broadcasted_iota(jnp.int32, (768, 128), 1)
    spread = jnp.zeros((64, 128), F32)
    for n in range(4):
        line = jnp.broadcast_to(vectors[n], (64, 768))
        values = jnp.where(chip == owner, line, 0.0).astype(BF16)
        spread += mm(values, jnp.where(lane == feature + 12 * n, 1.0, 0.0).astype(BF16))
    table[...] = spread

    def lines(slot):
        row = table[pl.ds(at_slot[576 + slot], 1), :]
        return jnp.concatenate(
            [jnp.broadcast_to(row, (8, 128)), jnp.zeros((8, 128), F32)], axis=1)

    spill_rows(cell_keep, acc, at_slot, 2, 0, lines)
    spill_rows(cell_send, acc, at_slot, 2, 32, lines)


def input_partials(table, operands, gates):
    whole = lambda shape: pl.BlockSpec(shape, lambda i, *_: (0,) * len(shape))
    shapes = [((2 * N, 768), F32), ((2 * N, 768), BF16)] + [((32, 32, 256), BF16)] * 2
    return pl.pallas_call(
        inputs_kernel,
        grid_spec=pltpu.PrefetchScalarGridSpec(
            num_scalar_prefetch=1,
            grid=(1,),
            in_specs=[whole(v.shape) for v in operands[:-1]]
            + [pl.BlockSpec((768, 384), lambda i, at, n=n: (0, 2 * n + at[CORE])) for n in range(3)]
            + [ANYWHERE] * len(gates),
            out_specs=[whole(shape) for shape, _ in shapes],
            scratch_shapes=[pltpu.VMEM((2, 768, 256), F32), pltpu.VMEM((64, 128), F32)],
        ),
        out_shape=[jax.ShapeDtypeStruct(*v) for v in shapes],
        compiler_params=pltpu.CompilerParams(vmem_limit_bytes=16 * 2**20),
        cost_estimate=pl.CostEstimate(
            flops=2 * 768 * 384 * 512 * 7, bytes_accessed=10 * 2**20, transcendentals=0),
        name="input_partials",
    )(table, *operands, *[operands[-1]] * 2, *gates)


def sum_core_kernel(own_ref, sib_ref, *refs):
    refs[-1][...] = (own_ref[...] + sib_ref[...].astype(F32)).astype(BF16)


def sum_core(own, sib, gates):
    half = pl.BlockSpec((N, 768), lambda i: (1, 0))
    return pl.pallas_call(
        sum_core_kernel,
        grid=(1,),
        in_specs=[half, half] + [ANYWHERE] * len(gates),
        out_specs=pl.BlockSpec((N, 768), lambda i: (0, 0)),
        out_shape=jax.ShapeDtypeStruct((N, 768), BF16),
        compiler_params=pltpu.CompilerParams(vmem_limit_bytes=4 * 2**20),
        name="sum_core",
    )(own, sib, *gates)


def token_kernel(tokens_ref, hidden_ref, own_ref, sib_ref, far_ref, gains_ref, out_own_ref,
                 out_sib_ref, grad_ref, out_ref):
    grad = own_ref[...] + sib_ref[...].astype(F32) + far_ref[...].astype(F32)
    xhat, factor = normalize(tokens_ref[...].astype(F32))
    grad_ref[...] = hidden_ref[...] + normalize_back(grad, xhat, factor, gains_ref[0:1, :])
    out_ref[...] = (out_own_ref[...] + out_sib_ref[...].astype(F32)).astype(BF16)


def token_grads(tokens, hidden, own, sib, far, gains, out_own, out_sib):
    half = pl.BlockSpec((N, 768), lambda i: (0, 0))
    return pl.pallas_call(
        token_kernel,
        grid=(1,),
        in_specs=[half] * 5 + [pl.BlockSpec((4, 768), lambda i: (0, 0))] + [half] * 2,
        out_specs=[half] * 2,
        out_shape=[jax.ShapeDtypeStruct((N, 768), F32), jax.ShapeDtypeStruct((N, 768), BF16)],
        compiler_params=pltpu.CompilerParams(vmem_limit_bytes=8 * 2**20),
        name="token_grads",
    )(tokens, hidden, own, sib, far, gains, out_own, out_sib)


def assemble_kernel(at_ref, own_ref, near_ref, away_ref, cross_ref, down_ref, up_ref, qkv_ref, out_ref,
                    vec_ref, below_ref, held):
    core, far = at_ref[CORE], at_ref[FAR]
    held[far * 2 + core] = own_ref[...]
    held[far * 2 + 1 - core] = near_ref[...]
    held[2 - far * 2 + core] = away_ref[...]
    held[2 - far * 2 + 1 - core] = cross_ref[...]
    line = held[far * 2, 2, 64:, :128].astype(F32) + held[far * 2 + 1, 2, 64:, :128].astype(F32)
    vec_ref[...] = jnp.where(core == 0, line, pltpu.roll(line, 122, 1))[8:]
    row = lax.broadcasted_iota(jnp.int32, (24, 80), 0)
    column = lax.broadcasted_iota(jnp.int32, (24, 80), 1)
    wanted = (row // 8) * 24 + far * 12 + core * 6 + row % 8
    select = jnp.where((column == wanted) & (row % 8 < 6), 1.0, 0.0).astype(BF16)
    for x_hi in range(2):
        for c in range(2):
            for g in range(3):
                rows = mm(select, held[x_hi * 2 + c, g])
                first = c * 1536 + g * 512 + x_hi * 256
                for e in range(2):
                    up_ref[:, e, first : first + 256] = rows[8 * e : 8 * e + 6] * UP_FACTORS[e]
                for n in range(2):
                    at = g * 512 + x_hi * 256 + n * 128
                    kind, within = at // 384, at % 384 + c * 384
                    part = rows[16:22, n * 128 : (n + 1) * 128]
                    if kind < 3:
                        qkv_ref[:, kind * 768 + within : kind * 768 + within + 128] = part
                    else:
                        out_ref[:, within : within + 128] = part
    for g in range(3):
        part = down_ref[g].astype(F32)
        for e in range(2):
            below_ref[e, :, g * 256 : (g + 1) * 256] = part[24 * e : 24 * e + 24] * UP_FACTORS[e]


def assemble(table, *parts):
    return pl.pallas_call(
        assemble_kernel,
        in_specs=[SMALL] + [WHOLE] * 5,
        out_specs=[WHOLE] * 5,
        out_shape=[
            jax.ShapeDtypeStruct((6, 2, 3072), F32),
            jax.ShapeDtypeStruct((6, 2304), F32),
            jax.ShapeDtypeStruct((6, 768), F32),
            jax.ShapeDtypeStruct((8, 128), F32),
            jax.ShapeDtypeStruct((2, 24, 768), F32),
        ],
        scratch_shapes=[pltpu.VMEM((4, 3, 80, 256), BF16)],
        compiler_params=pltpu.CompilerParams(vmem_limit_bytes=4 * 2**20),
        name="assemble",
    )(table, *parts)

def shards(tokens, first_gain, first_shift, w_qkv, w_out, second_gain, second_shift,
           w_up, w_down, modality, segments, partner, cotangent):
    table = lax.dynamic_index_in_dim(
        jnp.asarray(cell_places()), lax.axis_index(BOTH), 0, keepdims=False)
    gains = jnp.stack([first_gain, first_shift, second_gain, second_shift])

    own = marked(partner, tokens[0], segments, modality)
    away = swap_far(own)
    sib = swap_core(own)
    cot_own = cotangent[0]
    cot_sib = swap_core(cot_own)

    act1, marks, queries, k_near, v_near, qx = project(table, own, sib, gains, w_qkv, True)
    away_sib = swap_core(after(away, [qx]))
    act1_away, marks_away, k_away, v_away = project(table, away, away_sib, gains, w_qkv, False)
    attended, lse = attend_forward(
        queries, k_near, k_away, v_near, v_away, qx, marks, marks_away)
    attended_sib = swap_core(attended)

    hidden, grad_act2, xhat2, factor2, act_t, inner_t, grad_pre = experts(
        table, attended, attended_sib, own, sib, cot_own, cot_sib, marks, gains, w_out, w_up, w_down)
    ff_kept, ff_first, more = [], [], [grad_act2]
    for g in range(3):
        keep, gone, *low = cells(g, table, act_t, grad_pre, inner_t, cot_own, cot_sib, marks, more)
        ff_kept.append(keep.reshape(2, 16, 96, 256))
        ff_first.append(send(gone.reshape(2, 16, 96, 256), axis_step(ORDERS[g][0], True)))
        if g == 0:
            grad_sib = swap_core(low[0])
        more = [keep] if g == 0 else [keep, grad_sib]
    hidden_grad, grad_att, proj_half, vectors = middle(
        table, grad_act2, grad_sib, xhat2, factor2, cot_own, cot_sib, gains, w_out)

    def along(stage, first, values):
        return [send(v, axis_step(ORDERS[g][stage], first)) for g, v in enumerate(values)]

    taken = (queries, k_near, k_away, v_near, v_away, grad_att, attended, qx, marks, marks_away, lse)
    q_a, k_a, v_a = attend_backward(taken, 0, 2, ())
    q_b, k_b, v_b = attend_backward(taken, 2, 1, ())
    cells_a = tail_cells(table, act1, act1_away, q_a, q_b, k_a, k_b, v_a)
    partial_own, partial_low, *cells_b = input_partials(table, (
        act1, act1_away, q_a, q_b, k_a, k_b, v_a, v_b, attended, attended_sib, proj_half,
        own, sib, away, away_sib, vectors, w_qkv), ())
    kept = [v.reshape(2, 16, 32, 256) for v in (cells_a[0], cells_a[1], cells_b[0])]
    first = along(0, True, [v.reshape(2, 16, 32, 256) for v in (cells_a[2], cells_a[3], cells_b[1])])
    ff_second = along(0, False, pass_on(ff_kept, ff_first, "pass_first", [cells_b[0]]))
    partial_sib = swap_core(partial_low)
    passed = pass_on(kept, first, "pass_tail")
    second = along(0, False, passed)
    out_own, out_sib = branches(table, inner_t, w_down, hidden, marks, passed)

    kept, sent = settle(
        [list(zip(ff_kept, ff_first, ff_second)), list(zip(kept, first, second))], "settle_all", [out_sib])
    first = along(1, True, sent)
    second = along(1, False, pass_on(kept, first, "pass_second"))
    kept, sent = settle([list(zip(kept, first, second))], "settle_second")
    first = along(2, True, sent)
    from_far = swap_far(sum_core(partial_own, partial_sib, first))
    second = along(2, False, pass_on(kept, first, "pass_third"))
    held, down_held = finish(kept, first, second, [from_far])

    near, beyond = swap_core(held), swap_far(held)
    cross = send(held, lambda x, y, z, c: (x ^ 2, y, z, 1 - c))
    below = send(down_held, lambda x, y, z, c: (x, y, 2 * c + z % 2, z // 2))
    up_grad, qkv_grad, out_grad, line, down_grad = assemble(
        table, held, near, beyond, cross, below)

    token_grad, layer_output = token_grads(
        tokens[0], hidden_grad, partial_own, partial_sib, from_far, gains, out_own, swap_core(out_sib))

    return (
        layer_output[None], token_grad[None], line[0, :6], line[0, 12:18], qkv_grad, out_grad,
        line[0, 24:30], line[0, 36:42], up_grad.transpose(1, 0, 2), down_grad)


def solution(mesh):
    cut = P("rows", "seq", None)
    flat = P(BOTH)
    placed = (cut,) + (P(),) * 8 + (P("rows", "seq"), P("rows", "seq"), P("rows", None), cut)
    return jax.shard_map(
        shards, mesh=mesh, in_specs=placed,
        out_specs=(cut, cut, flat, flat, P(BOTH, None), P(BOTH, None), flat, flat,
                   P(None, BOTH, None), P(None, BOTH, None)),
        check_vma=False)
```

```python
import jax
import jax.numpy as jnp
import numpy as np
from jax import lax
from jax.experimental import pallas as pl
from jax.experimental.pallas import tpu as pltpu
from jax.sharding import PartitionSpec as P

HD = 64
OWN = 6
CORE, FAR = 768, 769
IMG = 197
NIMG = 4
BOTH = ("rows", "seq")
F32 = jnp.float32
BF16 = jnp.bfloat16
MASKED = -1e30


def route(step):
    pairs = []
    for r in range(32):
        z, x_lo, y = r // 8, (r // 4) % 2, r % 4
        for s in range(4):
            x, c = (s // 2) * 2 + x_lo, s % 2
            tx, ty, tz, tc = step(x, y, z, c)
            target = (tz * 8 + (tx % 2) * 4 + ty) * 4 + (tx // 2) * 2 + tc
            pairs.append((r * 4 + s, target))
    return pairs


def send(values, step):
    return lax.ppermute(values, BOTH, route(step))


def swap_core(values):
    return send(values, lambda x, y, z, c: (x, y, z, 1 - c))


def swap_far(values):
    return send(values, lambda x, y, z, c: (x ^ 2, y, z, c))


def axis_step(axis, first):
    def step(x, y, z, c):
        flip = 1 if (c == 0) == first else 3
        at = {"x": x, "y": y, "z": z}
        at[axis] ^= flip
        return (at["x"], at["y"], at["z"], c)

    return step


UP_FACTORS = (1024 / (2 * 788), 1024 / (2 * 236))
ORDERS = (("x", "y", "z"), ("y", "z", "x"), ("z", "x", "y"))


def normalize(inputs):
    centred = inputs - jnp.mean(inputs, axis=-1, keepdims=True)
    factor = lax.rsqrt(jnp.mean(centred * centred, axis=-1, keepdims=True) + 1e-05)
    return centred * factor, factor


def normalize_back(grad, xhat, factor, gain):
    gy = grad * gain
    mean_gy = jnp.mean(gy, axis=-1, keepdims=True)
    mean_gx = jnp.mean(gy * xhat, axis=-1, keepdims=True)
    return factor * (gy - mean_gy - xhat * mean_gx)


SMALL = pl.BlockSpec(memory_space=pltpu.SMEM)
WHOLE = pl.BlockSpec(memory_space=pltpu.VMEM)
N = 256


def marked_kernel(partner, tokens_ref, segments_ref, modality_ref, out_ref):
    segments = segments_ref[...]
    tag = jnp.zeros(segments.shape, jnp.int32)
    for n in range(8):
        tag = jnp.where(segments == n, partner[0, n], tag)
    marks = jnp.concatenate(
        [tag, modality_ref[...], jnp.zeros((1, 256), jnp.int32)], axis=1).astype(F32)
    out_ref[:N, :] = tokens_ref[...]
    out_ref[N:, :] = jnp.concatenate([marks, jnp.zeros((15, 768), F32)], axis=0).astype(BF16)


def marked(partner, tokens, segments, modality):
    return pl.pallas_call(
        marked_kernel,
        in_specs=[SMALL, WHOLE, WHOLE, WHOLE],
        out_specs=WHOLE,
        out_shape=jax.ShapeDtypeStruct((N + 16, 768), BF16),
        compiler_params=pltpu.CompilerParams(vmem_limit_bytes=60 * 2**20),
        name="marked",
    )(partner, tokens, segments, modality)


def mark_lanes(ext):
    row = ext[N:, :].astype(F32)
    place = lax.broadcasted_iota(jnp.int32, (128, N), 0)
    tag = jnp.broadcast_to(row[:1, :N], (128, N))
    kind = jnp.broadcast_to(row[:1, N : 2 * N], (128, N))
    hot = jnp.where((place < NIMG) & (place.astype(F32) == tag), 1.0, 0.0)
    return jnp.transpose(jnp.where(place == 8, kind, hot))


def project_kernel(at_ref, near, a_ref, b_ref, gains_ref, *refs):
    count = 3 if near else 2
    weights, outs = refs[:count], refs[count:]
    for n, ext_ref in enumerate((a_ref, b_ref)):
        rows = slice(n * N, (n + 1) * N)
        ext = ext_ref[...]
        xhat, _ = normalize(ext[:N].astype(F32))
        act = (xhat * gains_ref[0:1, :] + gains_ref[1:2, :]).astype(BF16)
        outs[0][rows, :] = act
        marks = mark_lanes(ext)
        outs[1][rows, :] = marks.astype(BF16)
        for m in range(count):
            part = mm(act, weights[m][...])
            outs[2 + m][rows, :] = (0.125 * part if near and m == 0 else part).astype(BF16)
        if near:
            lane = lax.broadcasted_iota(jnp.int32, marks.shape, 1)
            outs[5][rows, :] = jnp.where((lane < NIMG) & (marks == 0.0), MASKED, 0.0).astype(BF16)


def project(table, first, second, gains, w_qkv, near):
    kinds = (0, 1, 2) if near else (1, 2)
    sizes = [768, 128] + [384] * len(kinds) + ([128] if near else [])
    whole = lambda shape: pl.BlockSpec(shape, lambda i, at: (0, 0))
    return pl.pallas_call(
        lambda at_ref, *refs: project_kernel(at_ref, near, *refs),
        grid_spec=pltpu.PrefetchScalarGridSpec(
            num_scalar_prefetch=1,
            grid=(1,),
            in_specs=[whole((N + 16, 768))] * 2 + [whole((4, 768))]
            + [pl.BlockSpec((768, 384), lambda i, at, n=n: (0, 2 * n + at[CORE])) for n in kinds],
            out_specs=[whole((2 * N, size)) for size in sizes],
        ),
        out_shape=[jax.ShapeDtypeStruct((2 * N, size), BF16) for size in sizes],
        compiler_params=pltpu.CompilerParams(vmem_limit_bytes=6 * 2**20),
        cost_estimate=pl.CostEstimate(
            flops=2 * 512 * 768 * 384 * len(kinds), bytes_accessed=4 * 2**20, transcendentals=0),
        name="project_near" if near else "project_away",
    )(table, first, second, gains, *[w_qkv] * len(kinds))


def middle_kernel(place, grad_ref, sib_ref, xhat_ref, factor_ref, cot_own_ref, cot_sib_ref,
                  gains_ref, w_out_ref, hidden_ref, att_ref, proj_ref, vec_ref):
    core = place[CORE]
    for n, cot_ref in enumerate((cot_own_ref, cot_sib_ref)):
        rows, other = slice(n * N, (n + 1) * N), slice((1 - n) * N, (2 - n) * N)
        grad = grad_ref[rows, :].astype(F32) + sib_ref[other, :].astype(F32)
        xhat = xhat_ref[rows, :].astype(F32)
        total = cot_ref[...].astype(F32) + normalize_back(grad, xhat, factor_ref[rows, :], gains_ref[2:3, :])
        low = total.astype(BF16)
        if n == 0:
            hidden_ref[...] = total
            vec_ref[0:1, :] = jnp.sum(grad * xhat, axis=0, keepdims=True)
            vec_ref[1:2, :] = jnp.sum(grad, axis=0, keepdims=True)
        mine = w_out_ref[pl.ds(pl.multiple_of(core * 384, 384), 384), :]
        att_ref[rows, :] = mm(low, mine, NT).astype(BF16)
        proj_ref[rows, :] = jnp.where(core == 0, low[:, :384], low[:, 384:])


def middle(place, *operands):
    return pl.pallas_call(
        middle_kernel,
        in_specs=[SMALL] + [WHOLE] * len(operands),
        out_specs=[WHOLE] * 4,
        out_shape=[
            jax.ShapeDtypeStruct((N, 768), F32),
            jax.ShapeDtypeStruct((2 * N, 384), BF16),
            jax.ShapeDtypeStruct((2 * N, 384), BF16),
            jax.ShapeDtypeStruct((2, 768), F32),
        ],
        compiler_params=pltpu.CompilerParams(vmem_limit_bytes=6 * 2**20),
        cost_estimate=pl.CostEstimate(
            flops=2 * 512 * 768 * 384, bytes_accessed=8 * 2**20, transcendentals=0),
        name="middle",
    )(place, *operands)


def gelu_parts(pre):
    phi = 0.5 * (1.0 + lax.erf(pre * 0.7071067811865476))
    slope = phi + pre * (0.3989422804014327 * jnp.exp(-0.5 * pre * pre))
    return pre * phi, slope


NT = (((1,), (1,)), ((), ()))
TN = (((0,), (0,)), ((), ()))
NN = (((1,), (0,)), ((), ()))


def mm(left, right, dims=NN):
    return lax.dot_general(left, right, dims, preferred_element_type=F32)


def head_lanes(shape, h):
    lane = lax.broadcasted_iota(jnp.int32, shape, len(shape) - 1)
    return (lane >= HD) == (h == 1)


def turned(values):
    return jnp.transpose(values.astype(F32)).astype(BF16)


def stacked(near_ref, away_ref):
    return jnp.concatenate([near_ref[...], away_ref[...]], axis=0)


def forward_kernel(q_ref, kn_ref, ka_ref, vn_ref, va_ref, qx_ref, xn_ref, xa_ref, out_ref, lse_ref):
    keys = jnp.concatenate([stacked(kn_ref, ka_ref), stacked(xn_ref, xa_ref)], axis=1)
    values = stacked(vn_ref, va_ref)
    q_pair = q_ref[...]
    lanes = head_lanes(q_pair.shape, 0)
    values_t = turned(values)
    value_rows = lax.broadcasted_iota(jnp.int32, values_t.shape, 0) < HD
    mixed = []
    for h in range(2):
        mine = lanes if h == 0 else jnp.logical_not(lanes)
        mine_values = value_rows if h == 0 else jnp.logical_not(value_rows)
        query = jnp.concatenate([jnp.where(mine, q_pair, 0), qx_ref[...]], axis=1)
        scores = mm(keys, query, NT)
        peak = jnp.max(scores, axis=0, keepdims=True)
        weights = jnp.exp(scores - peak).astype(BF16)
        both = mm(jnp.where(mine_values, values_t, 1), weights)
        total = both[127:128, :] if h == 0 else both[0:1, :]
        mixed.append(both * (1.0 / total))
        lse_ref[0, h : h + 1, :] = peak + jnp.log(total)
    out_rows = lax.broadcasted_iota(jnp.int32, mixed[0].shape, 0) < HD
    out_ref[...] = jnp.transpose(jnp.where(out_rows, mixed[0], mixed[1])).astype(BF16)


BY_PAIR = pl.BlockSpec((2 * N, 128), lambda p: (0, p))
FIXED = pl.BlockSpec((2 * N, 128), lambda p: (0, 0))


def attend_forward(*operands):
    return pl.pallas_call(
        forward_kernel,
        grid=(3,),
        in_specs=[BY_PAIR] * 5 + [FIXED] * 3,
        out_specs=[BY_PAIR, pl.BlockSpec((1, 2, 2 * N), lambda p: (p, 0, 0))],
        out_shape=[
            jax.ShapeDtypeStruct((2 * N, 384), BF16),
            jax.ShapeDtypeStruct((3, 2, 2 * N), F32),
        ],
        compiler_params=pltpu.CompilerParams(vmem_limit_bytes=6 * 2**20),
        cost_estimate=pl.CostEstimate(
            flops=2 * 2 * OWN * 512 * 1024 * 256, bytes_accessed=4 * 2**20,
            transcendentals=OWN * 512 * 1024),
        name="attend_forward",
    )(*operands)


def backward_kernel(q_ref, kn_ref, ka_ref, vn_ref, va_ref, do_ref, o_ref, qx_ref, xn_ref, xa_ref,
                    lse_ref, *refs):
    dq_ref, dk_ref, dv_ref = refs[-3:]
    k_pair, values = stacked(kn_ref, ka_ref), stacked(vn_ref, va_ref)
    keys = jnp.concatenate([k_pair, stacked(xn_ref, xa_ref)], axis=1)
    q_pair, grads = q_ref[...], do_ref[...]
    lanes = head_lanes(q_pair.shape, 0)
    product = grads.astype(F32) * o_ref[...].astype(F32)
    k_turned = turned(k_pair)
    rows = lax.broadcasted_iota(jnp.int32, (128, 2 * N), 0) < HD
    dq = jnp.zeros((128, 2 * N), F32)
    dk = jnp.zeros(k_pair.shape, F32)
    dv = jnp.zeros(k_pair.shape, F32)
    for h in range(2):
        mine = lanes if h == 0 else jnp.logical_not(lanes)
        q_head = jnp.where(mine, q_pair, 0)
        g_head = jnp.where(mine, grads, 0)
        dot_row = jnp.transpose(jnp.sum(jnp.where(mine, product, 0.0), axis=1, keepdims=True))
        scores = mm(keys, jnp.concatenate([q_head, qx_ref[...]], axis=1), NT)
        prob = jnp.exp(scores - lse_ref[0, h : h + 1, :])
        dv += mm(prob.astype(BF16), g_head)
        grad_prob = mm(values, g_head, NT)
        grad_scores = (prob * (grad_prob - dot_row)).astype(BF16)
        dk += mm(grad_scores, q_head)
        part = mm(k_turned, grad_scores)
        dq += jnp.where(rows if h == 0 else jnp.logical_not(rows), part, 0.0)
    dq_ref[...] = jnp.transpose(dq).astype(BF16) * jnp.asarray(0.125, BF16)
    dk_ref[...] = dk.astype(BF16)
    dv_ref[...] = dv.astype(BF16)


def attend_backward(operands, first, pairs, gates):
    by_pair = pl.BlockSpec((2 * N, 128), lambda p: (0, first + p))
    sizes = (2 * N, 4 * N, 4 * N)
    return pl.pallas_call(
        backward_kernel,
        grid=(pairs,),
        in_specs=[by_pair] * 7 + [FIXED] * 3
        + [pl.BlockSpec((1, 2, 2 * N), lambda p: (first + p, 0, 0))]
        + [pl.BlockSpec(memory_space=pl.ANY)] * len(gates),
        out_specs=[pl.BlockSpec((size, 128), lambda p: (0, p)) for size in sizes],
        out_shape=[jax.ShapeDtypeStruct((size, pairs * 128), BF16) for size in sizes],
        compiler_params=pltpu.CompilerParams(vmem_limit_bytes=10 * 2**20),
        cost_estimate=pl.CostEstimate(
            flops=2 * 5 * 2 * pairs * 512 * 1024 * 256, bytes_accessed=6 * 2**20,
            transcendentals=2 * pairs * 512 * 1024),
        name="attend_backward",
    )(*operands, *gates)


FF_STEP = 512
E_STEP = 512
EXPERT_MB = 40
CELLS_MB = 28


def expert_kernel(at_ref, att_own_ref, att_sib_ref, own_ref, sib_ref, cot_own_ref, cot_sib_ref,
                  marks_ref, gains_ref, w_out_ref, wu_ref, wd_ref,
                  hidden_ref, low_ref, xhat_ref, factor_ref, act_t_ref, inner_t_ref, slope_ref,
                  act_acc, grad_acc):
    f = pl.program_id(0)
    core = at_ref[CORE]

    @pl.when(f == 0)
    def _():
        mine = w_out_ref[pl.ds(pl.multiple_of(core * 384, 384), 384), :]
        other = w_out_ref[pl.ds(pl.multiple_of((1 - core) * 384, 384), 384), :]
        for n, ext_ref in enumerate((own_ref, sib_ref)):
            rows, theirs = slice(n * N, (n + 1) * N), slice((1 - n) * N, (2 - n) * N)
            hidden = ext_ref[:N, :].astype(F32) + (
                mm(att_own_ref[rows, :], mine) + mm(att_sib_ref[theirs, :], other))
            xhat, factor = normalize(hidden)
            xhat_ref[rows, :] = xhat.astype(BF16)
            factor_ref[rows, :] = factor
            act = xhat * gains_ref[2:3, :] + gains_ref[3:4, :]
            act_acc[rows, :] = act.astype(BF16)
            act_t_ref[:, rows] = jnp.transpose(act).astype(BF16)
            if n == 0:
                hidden_ref[...] = hidden
        grad_acc[...] = jnp.zeros(grad_acc.shape, F32)

    act = act_acc[...]
    cot = jnp.concatenate([cot_own_ref[...], cot_sib_ref[...]], axis=0)
    text = marks_ref[:, 8:9].astype(F32) > 0.0
    pre = jnp.where(text, mm(act, wu_ref[1]), mm(act, wu_ref[0]))
    inner, slope = gelu_parts(pre)
    grad_pre = jnp.where(text, mm(cot, wd_ref[1], NT), mm(cot, wd_ref[0], NT)) * slope
    inner_t_ref[...] = jnp.transpose(inner).astype(BF16)
    low = grad_pre.astype(BF16)
    slope_ref[...] = low
    zero = jnp.zeros((), BF16)
    grad_acc[...] += (mm(jnp.where(text, zero, low), wu_ref[0], NT)
                      + mm(jnp.where(text, low, zero), wu_ref[1], NT))

    @pl.when(f == pl.num_programs(0) - 1)
    def _():
        low_ref[...] = grad_acc[...].astype(BF16)


def experts(core, *operands):
    steps = 1536 // E_STEP
    shapes = [((N, 768), F32), ((2 * N, 768), BF16), ((2 * N, 768), BF16), ((2 * N, 1), F32),
              ((768, 2 * N), BF16)]
    fixed = lambda shape: pl.BlockSpec(shape, lambda f, *_: (0,) * len(shape))
    return pl.pallas_call(
        expert_kernel,
        grid_spec=pltpu.PrefetchScalarGridSpec(
            num_scalar_prefetch=1,
            grid=(steps,),
            in_specs=[fixed(v.shape) for v in operands[:-2]] + [
                pl.BlockSpec((2, 768, E_STEP), lambda f, at: (0, 0, at[CORE] * steps + f)),
                pl.BlockSpec((2, E_STEP, 768), lambda f, at: (0, at[CORE] * steps + f, 0)),
            ],
            out_specs=[fixed(shape) for shape, _ in shapes] + [
                pl.BlockSpec((E_STEP, 2 * N), lambda f, at: (f, 0)),
                pl.BlockSpec((2 * N, E_STEP), lambda f, at: (0, f)),
            ],
            scratch_shapes=[pltpu.VMEM((2 * N, 768), BF16), pltpu.VMEM((2 * N, 768), F32)],
        ),
        out_shape=[jax.ShapeDtypeStruct(*v) for v in shapes] + [
            jax.ShapeDtypeStruct((1536, 2 * N), BF16),
            jax.ShapeDtypeStruct((2 * N, 1536), BF16)],
        compiler_params=pltpu.CompilerParams(
            vmem_limit_bytes=18 * 2**20, dimension_semantics=("arbitrary",)),
        cost_estimate=pl.CostEstimate(
            flops=6 * 2 * 512 * 768 * 1536 + 2 * 512 * 768 * 768, bytes_accessed=22 * 2**20,
            transcendentals=2 * 512 * 1536),
        name="experts",
    )(core, *operands)


def kind_row(marks_ref):
    return turned(marks_ref[...])[8:9, :].astype(F32) > 0.0


def branch_kernel(at_ref, inner_t_ref, wd_ref, hidden_ref, marks_ref, *refs):
    own_ref, sib_ref, acc = refs[-3:]
    f = pl.program_id(0)
    text, inner_t, zero = kind_row(marks_ref), inner_t_ref[...], jnp.zeros((), BF16)
    part = (mm(jnp.where(text, zero, inner_t), wd_ref[0], TN)
            + mm(jnp.where(text, inner_t, zero), wd_ref[1], TN))

    @pl.when(f == 0)
    def _():
        acc[...] = part

    @pl.when(f > 0)
    def _():
        acc[...] += part

    @pl.when(f == pl.num_programs(0) - 1)
    def _():
        own_ref[...] = hidden_ref[...] + acc[:N, :]
        sib_ref[...] = acc[N:, :].astype(BF16)


def branches(table, inner_t, w_down, hidden, marks, gates):
    return pl.pallas_call(
        branch_kernel,
        grid_spec=pltpu.PrefetchScalarGridSpec(
            num_scalar_prefetch=1,
            grid=(3,),
            in_specs=[
                pl.BlockSpec((512, 2 * N), lambda f, at: (f, 0)),
                pl.BlockSpec((2, 512, 768), lambda f, at: (0, at[CORE] * 3 + f, 0)),
                pl.BlockSpec((N, 768), lambda f, at: (0, 0)),
                pl.BlockSpec((2 * N, 128), lambda f, at: (0, 0))] + [ANYWHERE] * len(gates),
            out_specs=[pl.BlockSpec((N, 768), lambda f, at: (0, 0))] * 2,
            scratch_shapes=[pltpu.VMEM((2 * N, 768), F32)],
        ),
        out_shape=[jax.ShapeDtypeStruct((N, 768), F32), jax.ShapeDtypeStruct((N, 768), BF16)],
        compiler_params=pltpu.CompilerParams(
            vmem_limit_bytes=20 * 2**20, dimension_semantics=("arbitrary",)),
        cost_estimate=pl.CostEstimate(
            flops=2 * 2 * 512 * 768 * 1536, bytes_accessed=8 * 2**20, transcendentals=0),
        name="branches",
    )(table, inner_t, w_down, hidden, marks, *gates)


def cells_kernel(g, at_slot, act_t_ref, grad_ref, inner_t_ref, cot_own_ref, cot_sib_ref, marks_ref,
                 *refs):
    if g == 0:
        full_ref, keep_ref, send_ref, low_ref, up_acc, down_acc = refs
        low_ref[...] = full_ref[...]
    else:
        keep_ref, send_ref, up_acc, down_acc = refs[-4:]
    e = pl.program_id(0)
    zero = jnp.zeros((), BF16)
    mine = (marks_ref[:, 8:9].astype(F32) > 0.0) == (e == 1)
    mine_row = kind_row(marks_ref) == (e == 1)
    up = mm(act_t_ref[...], jnp.where(mine, grad_ref[...], zero))
    up_acc[e, 0] = up[:, :256]
    up_acc[e, 1] = up[:, 256:]
    cot = jnp.concatenate([cot_own_ref[...], cot_sib_ref[...]], axis=0)
    down_acc[e] = mm(jnp.where(mine_row, inner_t_ref[...], zero), cot)

    def spill(target, base):
        def cell(i, carry):
            slot = g * 64 + base + i
            half = at_slot[192 + slot]
            rows = pl.ds(pl.multiple_of(at_slot[slot], 8), 24)
            below = pl.ds(pl.multiple_of(at_slot[384 + slot], 8), 24)
            target[i] = jnp.concatenate(
                [up_acc[0, half, rows, :], up_acc[1, half, rows, :],
                 down_acc[0, below, :], down_acc[1, below, :]], axis=0).astype(BF16)
            return carry
        lax.fori_loop(0, 32, cell, 0, unroll=4)

    @pl.when(e == 1)
    def _():
        spill(keep_ref, 0)
        spill(send_ref, 32)


def cells(g, table, act_t, grad_pre, inner_t, cot_own, cot_sib, marks, more):
    cot = pl.BlockSpec((N, 256), lambda e, t: (0, g))
    out = pl.BlockSpec((32, 96, 256), lambda e, t: (0, 0, 0))
    low = pl.BlockSpec((N, 768), lambda e, t: (e, 0))
    return pl.pallas_call(
        lambda *refs: cells_kernel(g, *refs),
        grid_spec=pltpu.PrefetchScalarGridSpec(
            num_scalar_prefetch=1,
            grid=(2,),
            in_specs=[
                pl.BlockSpec((768, 2 * N), lambda e, t: (0, 0)),
                pl.BlockSpec((2 * N, FF_STEP), lambda e, t: (0, g)),
                pl.BlockSpec((1536, 2 * N), lambda e, t: (0, 0)),
                cot, cot, pl.BlockSpec((2 * N, 128), lambda e, t: (0, 0))] + ([low] if g == 0 else [ANYWHERE] * len(more)),
            out_specs=[out] * 2 + [low] * (g == 0),
            scratch_shapes=[pltpu.VMEM((2, 2, 768, 256), F32), pltpu.VMEM((2, 1536, 256), F32)],
        ),
        out_shape=[jax.ShapeDtypeStruct((32, 96, 256), BF16)] * 2
        + [jax.ShapeDtypeStruct((2 * N, 768), BF16)] * (g == 0),
        compiler_params=pltpu.CompilerParams(
            vmem_limit_bytes=10 * 2**20, dimension_semantics=("arbitrary",)),
        cost_estimate=pl.CostEstimate(
            flops=4 * 2 * 512 * 768 * 512, bytes_accessed=8 * 2**20, transcendentals=0),
        name="cells",
    )(table, act_t, grad_pre, inner_t, cot_own, cot_sib, marks, *more)


def cell_places():
    table = np.zeros((32, 4, 4, 3, 4, 4, 4), np.int32)
    for r, s in np.ndindex(32, 4):
        here = {"z": r // 8, "y": r % 4, "x": (s // 2) * 2 + (r // 4) % 2}
        flips = (0, 1, 3, 2) if s % 2 else (0, 3, 1, 2)
        for g, order in enumerate(ORDERS):
            for slot in np.ndindex(4, 4, 4):
                at = {a: here[a] ^ flips[n] for a, n in zip(order, slot)}
                x_hi, x_lo = at["x"] // 2, at["x"] % 2
                table[(r, s, 0, g) + slot] = 24 * (at["z"] * 8 + x_lo * 4 + at["y"])
                table[(r, s, 1, g) + slot] = x_hi
                table[(r, s, 2, g) + slot] = 24 * (
                    (at["z"] % 2) * 32 + x_lo * 16 + at["y"] * 4 + x_hi * 2 + at["z"] // 2)
                table[(r, s, 3, g) + slot] = at["z"] * 16 + x_lo * 8 + at["y"] * 2 + x_hi
    coordinates = np.array([[n % 2, n % 4 // 2] + [0] * 126 for n in range(128)], np.int32)
    return np.concatenate([table.reshape(128, 768), coordinates], axis=1)


def add_up(parts):
    total = parts[0].astype(F32)
    for part in parts[1:]:
        total = total + part.astype(F32)
    return total.astype(BF16)


def in_hbm(values):
    return list(values)


def pass_kernel(gates, *refs):
    count = (len(refs) - gates) // 3
    for g in range(count):
        refs[2 * count + gates + g][...] = add_up([refs[2 * g][...], refs[2 * g + 1][...]])


ANYWHERE = pl.BlockSpec(memory_space=pl.ANY)


def pass_on(kept, arrived, name, gates=()):
    _, slots, rows, lanes = kept[0].shape
    block = max(slots // 4, 1)
    one = pl.BlockSpec((None, block, rows, lanes), lambda i: (1, i, 0, 0))
    return pl.pallas_call(
        lambda *refs: pass_kernel(len(gates), *refs),
        grid=(slots // block,),
        in_specs=[one] * (2 * len(kept)) + [ANYWHERE] * len(gates),
        out_specs=[pl.BlockSpec((block, rows, lanes), lambda i: (i, 0, 0))] * len(kept),
        out_shape=[jax.ShapeDtypeStruct((slots, rows, lanes), BF16)] * len(kept),
        compiler_params=pltpu.CompilerParams(vmem_limit_bytes=6 * 2**20),
        cost_estimate=pl.CostEstimate(
            flops=0, transcendentals=0, bytes_accessed=6 * len(kept) * slots * rows * lanes),
        name=name,
    )(*in_hbm([v for pair in zip(kept, arrived) for v in pair]), *gates)


def settle_kernel(groups, sizes, *refs):
    ins, outs = refs, refs[-2 * groups :]
    at = 0
    for g in range(groups):
        row = 0
        for size in sizes:
            for half in range(2):
                outs[2 * g + half][:, row : row + size, :] = add_up(
                    [ins[at + k][...] for k in range(3)])
                at += 3
            row += size


def settle(pieces, name, gates=()):
    groups = len(pieces[0])
    sizes = [p[0][0].shape[2] for p in pieces]
    _, slots, _, lanes = pieces[0][0][0].shape
    half = slots // 2
    block = max(half // 4, 1)
    steps = half // block
    operands, specs = [], []
    for g in range(groups):
        for p, size in zip(pieces, sizes):
            for h in range(2):
                wide = pl.BlockSpec(
                    (None, block, size, lanes), lambda i, h=h: (0, i + h * steps, 0, 0))
                flat = pl.BlockSpec((block, size, lanes), lambda i, h=h: (i + h * steps, 0, 0))
                operands += list(p[g])
                specs += [wide, wide, flat]
    rows = sum(sizes)
    outs = pl.pallas_call(
        lambda *refs: settle_kernel(groups, sizes, *refs),
        grid=(steps,),
        in_specs=specs + [ANYWHERE] * len(gates),
        out_specs=[pl.BlockSpec((block, rows, lanes), lambda i: (i, 0, 0))] * (2 * groups),
        out_shape=[jax.ShapeDtypeStruct((half, rows, lanes), BF16)] * (2 * groups),
        compiler_params=pltpu.CompilerParams(vmem_limit_bytes=8 * 2**20),
        cost_estimate=pl.CostEstimate(
            flops=0, transcendentals=0, bytes_accessed=8 * groups * slots * rows * lanes),
        name=name,
    )(*operands, *gates)
    shaped = [o.reshape(2, half // 2, rows, lanes) for o in outs]
    return shaped[0::2], shaped[1::2]


def finish_kernel(*refs):
    held_ref, down_ref = refs[-2:]
    for g in range(3):
        cell = add_up([refs[3 * g + k][...] for k in range(3)])
        held_ref[g, :48, :] = cell[:48]
        held_ref[g, 48:, :] = cell[96:]
        down_ref[g] = cell[48:96]


def finish(kept, first, second, gates):
    wide = pl.BlockSpec((None, None, 128, 256), lambda i: (0, 0, 0, 0))
    flat = pl.BlockSpec((None, 128, 256), lambda i: (0, 0, 0))
    return pl.pallas_call(
        finish_kernel,
        grid=(1,),
        in_specs=[wide, wide, flat] * 3 + [ANYWHERE] * len(gates),
        out_specs=[pl.BlockSpec((3, 80, 256), lambda i: (0, 0, 0)),
                   pl.BlockSpec((3, 48, 256), lambda i: (0, 0, 0))],
        out_shape=[jax.ShapeDtypeStruct((3, 80, 256), BF16), jax.ShapeDtypeStruct((3, 48, 256), BF16)],
        compiler_params=pltpu.CompilerParams(vmem_limit_bytes=4 * 2**20),
        name="finish",
    )(*[v for g in range(3) for v in (kept[g], first[g], second[g])], *gates)


def after_kernel(values_ref, *refs):
    refs[-1][...] = values_ref[...]


def after(values, gates):
    return pl.pallas_call(
        after_kernel,
        in_specs=[WHOLE] + [ANYWHERE] * len(gates),
        out_specs=WHOLE,
        out_shape=jax.ShapeDtypeStruct(values.shape, values.dtype),
        compiler_params=pltpu.CompilerParams(vmem_limit_bytes=4 * 2**20),
        name="after",
    )(values, *gates)


def put(acc, first, part, rows=slice(None)):
    for n in range(part.shape[1] // 128):
        column = first + n * 128
        lanes = slice(column % 256, column % 256 + 128)
        acc[column // 256, rows, lanes] = part[:, n * 128 : (n + 1) * 128]


def spill_rows(target, acc, at_slot, g, base, extra):
    def cell(i, carry):
        slot = g * 64 + base + i
        rows = pl.ds(pl.multiple_of(at_slot[slot], 8), 24)
        part = acc[at_slot[192 + slot] + 2 * (g % 2), rows, :]
        target[i] = jnp.concatenate([part, extra(slot)], axis=0).astype(BF16)
        return carry
    lax.fori_loop(0, 32, cell, 0, unroll=4)


def tail_kernel(at_slot, act_ref, away_ref, q_ref, qb_ref, ka_ref, kb_ref, va_ref, *refs):
    keeps, sends, acc = refs[-5:-3], refs[-3:-1], refs[-1]
    act, away = act_ref[...], away_ref[...]
    near = mm(act, jnp.concatenate(
        [r[: 2 * N, :] for r in (q_ref, qb_ref, ka_ref, kb_ref, va_ref)], axis=1), TN)
    far = mm(away, jnp.concatenate(
        [r[2 * N :, :] for r in (ka_ref, kb_ref, va_ref)], axis=1), TN)
    put(acc, 0, near[:, :384])
    put(acc, 384, near[:, 384:] + far)
    for g in range(2):
        blank = lambda slot: jnp.zeros((8, 256), F32)
        spill_rows(keeps[g], acc, at_slot, g, 0, blank)
        spill_rows(sends[g], acc, at_slot, g, 32, blank)


def tail_cells(table, *operands):
    return pl.pallas_call(
        tail_kernel,
        in_specs=[SMALL] + [WHOLE] * len(operands),
        out_specs=[WHOLE] * 4,
        out_shape=[jax.ShapeDtypeStruct((32, 32, 256), BF16)] * 4,
        scratch_shapes=[pltpu.VMEM((4, 768, 256), F32)],
        compiler_params=pltpu.CompilerParams(vmem_limit_bytes=14 * 2**20),
        cost_estimate=pl.CostEstimate(
            flops=2 * 768 * 512 * (1024 + 640), bytes_accessed=8 * 2**20, transcendentals=0),
        name="tail_cells",
    )(table, *operands)


def inputs_kernel(at_slot, act_ref, away_ref, q_ref, qb_ref, ka_ref, kb_ref, va_ref, vb_ref,
                  att_own_ref, att_sib_ref, proj_ref, own_ref, sib_ref, far_ref, far_sib_ref,
                  second_ref, *refs):
    weights = refs[:3]
    keep_ref, send_ref, cell_keep, cell_send, acc, table = refs[-6:]
    core = at_slot[CORE]
    put(acc, 0, mm(act_ref[...], vb_ref[: 2 * N, :], TN) + mm(away_ref[...], vb_ref[2 * N :, :], TN))
    mine = pl.ds(pl.multiple_of(core * 384, 384), 384)
    other = pl.ds(pl.multiple_of((1 - core) * 384, 384), 384)
    put(acc, 128, mm(att_own_ref[...], proj_ref[...], TN), mine)
    put(acc, 128, mm(att_sib_ref[:N, :], proj_ref[N:, :], TN)
        + mm(att_sib_ref[N:, :], proj_ref[:N, :], TN), other)

    vectors = [jnp.zeros((1, 768), F32)] * 2 + [second_ref[0:1, :], second_ref[1:2, :]]
    wide = list(zip((q_ref, ka_ref, va_ref), (qb_ref, kb_ref, vb_ref), weights))
    for n, ext_ref in enumerate((own_ref, sib_ref, far_ref, far_sib_ref)):
        rows = slice(n * N, (n + 1) * N)
        total = jnp.zeros((N, 768), F32)
        for a_ref, b_ref, w_ref in wide[0 if n < 2 else 1 :]:
            grads = jnp.concatenate([a_ref[rows, :], b_ref[rows, :]], axis=1)
            total += mm(grads, w_ref[...], NT)
        xhat, _ = normalize(ext_ref[:N, :].astype(F32))
        vectors[0] += jnp.sum(total * xhat, axis=0, keepdims=True)
        vectors[1] += jnp.sum(total, axis=0, keepdims=True)
        half = slice((n // 2) * N, (n // 2 + 1) * N)
        if n % 2 == 0:
            keep_ref[half, :] = total
        else:
            send_ref[half, :] = total.astype(BF16)

    chip = lax.broadcasted_iota(jnp.int32, (64, 768), 0)
    owner = lax.broadcasted_iota(jnp.int32, (64, 768), 1) // 12
    feature = lax.broadcasted_iota(jnp.int32, (768, 128), 0) % 12
    lane = lax.broadcasted_iota(jnp.int32, (768, 128), 1)
    spread = jnp.zeros((64, 128), F32)
    for n in range(4):
        line = jnp.broadcast_to(vectors[n], (64, 768))
        values = jnp.where(chip == owner, line, 0.0).astype(BF16)
        spread += mm(values, jnp.where(lane == feature + 12 * n, 1.0, 0.0).astype(BF16))
    table[...] = spread

    def lines(slot):
        row = table[pl.ds(at_slot[576 + slot], 1), :]
        return jnp.concatenate(
            [jnp.broadcast_to(row, (8, 128)), jnp.zeros((8, 128), F32)], axis=1)

    spill_rows(cell_keep, acc, at_slot, 2, 0, lines)
    spill_rows(cell_send, acc, at_slot, 2, 32, lines)


def input_partials(table, operands, gates):
    whole = lambda shape: pl.BlockSpec(shape, lambda i, *_: (0,) * len(shape))
    shapes = [((2 * N, 768), F32), ((2 * N, 768), BF16)] + [((32, 32, 256), BF16)] * 2
    return pl.pallas_call(
        inputs_kernel,
        grid_spec=pltpu.PrefetchScalarGridSpec(
            num_scalar_prefetch=1,
            grid=(1,),
            in_specs=[whole(v.shape) for v in operands[:-1]]
            + [pl.BlockSpec((768, 384), lambda i, at, n=n: (0, 2 * n + at[CORE])) for n in range(3)]
            + [ANYWHERE] * len(gates),
            out_specs=[whole(shape) for shape, _ in shapes],
            scratch_shapes=[pltpu.VMEM((2, 768, 256), F32), pltpu.VMEM((64, 128), F32)],
        ),
        out_shape=[jax.ShapeDtypeStruct(*v) for v in shapes],
        compiler_params=pltpu.CompilerParams(vmem_limit_bytes=16 * 2**20),
        cost_estimate=pl.CostEstimate(
            flops=2 * 768 * 384 * 512 * 7, bytes_accessed=10 * 2**20, transcendentals=0),
        name="input_partials",
    )(table, *operands, *[operands[-1]] * 2, *gates)


def sum_core_kernel(own_ref, sib_ref, *refs):
    refs[-1][...] = (own_ref[...] + sib_ref[...].astype(F32)).astype(BF16)


def sum_core(own, sib, gates):
    half = pl.BlockSpec((N, 768), lambda i: (1, 0))
    return pl.pallas_call(
        sum_core_kernel,
        grid=(1,),
        in_specs=[half, half] + [ANYWHERE] * len(gates),
        out_specs=pl.BlockSpec((N, 768), lambda i: (0, 0)),
        out_shape=jax.ShapeDtypeStruct((N, 768), BF16),
        compiler_params=pltpu.CompilerParams(vmem_limit_bytes=4 * 2**20),
        name="sum_core",
    )(own, sib, *gates)


def token_kernel(tokens_ref, hidden_ref, own_ref, sib_ref, far_ref, gains_ref, out_own_ref,
                 out_sib_ref, grad_ref, out_ref):
    grad = own_ref[...] + sib_ref[...].astype(F32) + far_ref[...].astype(F32)
    xhat, factor = normalize(tokens_ref[...].astype(F32))
    grad_ref[...] = hidden_ref[...] + normalize_back(grad, xhat, factor, gains_ref[0:1, :])
    out_ref[...] = (out_own_ref[...] + out_sib_ref[...].astype(F32)).astype(BF16)


def token_grads(tokens, hidden, own, sib, far, gains, out_own, out_sib):
    half = pl.BlockSpec((N, 768), lambda i: (0, 0))
    return pl.pallas_call(
        token_kernel,
        grid=(1,),
        in_specs=[half] * 5 + [pl.BlockSpec((4, 768), lambda i: (0, 0))] + [half] * 2,
        out_specs=[half] * 2,
        out_shape=[jax.ShapeDtypeStruct((N, 768), F32), jax.ShapeDtypeStruct((N, 768), BF16)],
        compiler_params=pltpu.CompilerParams(vmem_limit_bytes=8 * 2**20),
        name="token_grads",
    )(tokens, hidden, own, sib, far, gains, out_own, out_sib)


def assemble_kernel(at_ref, own_ref, near_ref, away_ref, cross_ref, down_ref, up_ref, qkv_ref, out_ref,
                    vec_ref, below_ref, held):
    core, far = at_ref[CORE], at_ref[FAR]
    held[far * 2 + core] = own_ref[...]
    held[far * 2 + 1 - core] = near_ref[...]
    held[2 - far * 2 + core] = away_ref[...]
    held[2 - far * 2 + 1 - core] = cross_ref[...]
    line = held[far * 2, 2, 64:, :128].astype(F32) + held[far * 2 + 1, 2, 64:, :128].astype(F32)
    vec_ref[...] = jnp.where(core == 0, line, pltpu.roll(line, 122, 1))[8:]
    row = lax.broadcasted_iota(jnp.int32, (24, 80), 0)
    column = lax.broadcasted_iota(jnp.int32, (24, 80), 1)
    wanted = (row // 8) * 24 + far * 12 + core * 6 + row % 8
    select = jnp.where((column == wanted) & (row % 8 < 6), 1.0, 0.0).astype(BF16)
    for x_hi in range(2):
        for c in range(2):
            for g in range(3):
                rows = mm(select, held[x_hi * 2 + c, g])
                first = c * 1536 + g * 512 + x_hi * 256
                for e in range(2):
                    up_ref[:, e, first : first + 256] = rows[8 * e : 8 * e + 6] * UP_FACTORS[e]
                for n in range(2):
                    at = g * 512 + x_hi * 256 + n * 128
                    kind, within = at // 384, at % 384 + c * 384
                    part = rows[16:22, n * 128 : (n + 1) * 128]
                    if kind < 3:
                        qkv_ref[:, kind * 768 + within : kind * 768 + within + 128] = part
                    else:
                        out_ref[:, within : within + 128] = part
    for g in range(3):
        part = down_ref[g].astype(F32)
        for e in range(2):
            below_ref[e, :, g * 256 : (g + 1) * 256] = part[24 * e : 24 * e + 24] * UP_FACTORS[e]


def assemble(table, *parts):
    return pl.pallas_call(
        assemble_kernel,
        in_specs=[SMALL] + [WHOLE] * 5,
        out_specs=[WHOLE] * 5,
        out_shape=[
            jax.ShapeDtypeStruct((6, 2, 3072), F32),
            jax.ShapeDtypeStruct((6, 2304), F32),
            jax.ShapeDtypeStruct((6, 768), F32),
            jax.ShapeDtypeStruct((8, 128), F32),
            jax.ShapeDtypeStruct((2, 24, 768), F32),
        ],
        scratch_shapes=[pltpu.VMEM((4, 3, 80, 256), BF16)],
        compiler_params=pltpu.CompilerParams(vmem_limit_bytes=4 * 2**20),
        name="assemble",
    )(table, *parts)

def shards(tokens, first_gain, first_shift, w_qkv, w_out, second_gain, second_shift,
           w_up, w_down, modality, segments, partner, cotangent):
    table = lax.dynamic_index_in_dim(
        jnp.asarray(cell_places()), lax.axis_index(BOTH), 0, keepdims=False)
    gains = jnp.stack([first_gain, first_shift, second_gain, second_shift])

    own = marked(partner, tokens[0], segments, modality)
    away = swap_far(own)
    sib = swap_core(own)
    cot_own = cotangent[0]
    cot_sib = swap_core(cot_own)

    act1, marks, queries, k_near, v_near, qx = project(table, own, sib, gains, w_qkv, True)
    away_sib = swap_core(after(away, [qx]))
    act1_away, marks_away, k_away, v_away = project(table, away, away_sib, gains, w_qkv, False)
    attended, lse = attend_forward(
        queries, k_near, k_away, v_near, v_away, qx, marks, marks_away)
    attended_sib = swap_core(attended)

    hidden, grad_act2, xhat2, factor2, act_t, inner_t, grad_pre = experts(
        table, attended, attended_sib, own, sib, cot_own, cot_sib, marks, gains, w_out, w_up, w_down)
    ff_kept, ff_first, more = [], [], [grad_act2]
    for g in range(3):
        keep, gone, *low = cells(g, table, act_t, grad_pre, inner_t, cot_own, cot_sib, marks, more)
        ff_kept.append(keep.reshape(2, 16, 96, 256))
        ff_first.append(send(gone.reshape(2, 16, 96, 256), axis_step(ORDERS[g][0], True)))
        if g == 0:
            grad_sib = swap_core(low[0])
        more = [keep] if g == 0 else [keep, grad_sib]
    hidden_grad, grad_att, proj_half, vectors = middle(
        table, grad_act2, grad_sib, xhat2, factor2, cot_own, cot_sib, gains, w_out)

    def along(stage, first, values):
        return [send(v, axis_step(ORDERS[g][stage], first)) for g, v in enumerate(values)]

    taken = (queries, k_near, k_away, v_near, v_away, grad_att, attended, qx, marks, marks_away, lse)
    q_a, k_a, v_a = attend_backward(taken, 0, 2, ())
    q_b, k_b, v_b = attend_backward(taken, 2, 1, ())
    cells_a = tail_cells(table, act1, act1_away, q_a, q_b, k_a, k_b, v_a)
    partial_own, partial_low, *cells_b = input_partials(table, (
        act1, act1_away, q_a, q_b, k_a, k_b, v_a, v_b, attended, attended_sib, proj_half,
        own, sib, away, away_sib, vectors, w_qkv), ())
    kept = [v.reshape(2, 16, 32, 256) for v in (cells_a[0], cells_a[1], cells_b[0])]
    first = along(0, True, [v.reshape(2, 16, 32, 256) for v in (cells_a[2], cells_a[3], cells_b[1])])
    ff_second = along(0, False, pass_on(ff_kept, ff_first, "pass_first", [cells_b[0]]))
    partial_sib = swap_core(partial_low)
    passed = pass_on(kept, first, "pass_tail")
    second = along(0, False, passed)
    out_own, out_sib = branches(table, inner_t, w_down, hidden, marks, passed)

    kept, sent = settle(
        [list(zip(ff_kept, ff_first, ff_second)), list(zip(kept, first, second))], "settle_all", [out_sib])
    first = along(1, True, sent)
    passed = pass_on(kept, first, "pass_second")
    second = along(1, False, passed)
    from_far = swap_far(sum_core(partial_own, partial_sib, passed))
    kept, sent = settle([list(zip(kept, first, second))], "settle_second")
    first = along(2, True, sent)
    second = along(2, False, pass_on(kept, first, "pass_third", [from_far]))
    held, down_held = finish(kept, first, second, [])

    near, beyond = swap_core(held), swap_far(held)
    cross = send(held, lambda x, y, z, c: (x ^ 2, y, z, 1 - c))
    below = send(down_held, lambda x, y, z, c: (x, y, 2 * c + z % 2, z // 2))
    up_grad, qkv_grad, out_grad, line, down_grad = assemble(
        table, held, near, beyond, cross, below)

    token_grad, layer_output = token_grads(
        tokens[0], hidden_grad, partial_own, partial_sib, from_far, gains, out_own, swap_core(out_sib))

    return (
        layer_output[None], token_grad[None], line[0, :6], line[0, 12:18], qkv_grad, out_grad,
        line[0, 24:30], line[0, 36:42], up_grad.transpose(1, 0, 2), down_grad)


def solution(mesh):
    cut = P("rows", "seq", None)
    flat = P(BOTH)
    placed = (cut,) + (P(),) * 8 + (P("rows", "seq"), P("rows", "seq"), P("rows", None), cut)
    return jax.shard_map(
        shards, mesh=mesh, in_specs=placed,
        out_specs=(cut, cut, flat, flat, P(BOTH, None), P(BOTH, None), flat, flat,
                   P(None, BOTH, None), P(None, BOTH, None)),
        check_vma=False)
```

```python
import jax
import jax.numpy as jnp
import numpy as np
from jax import lax
from jax.experimental import pallas as pl
from jax.experimental.pallas import tpu as pltpu
from jax.sharding import PartitionSpec as P

HD = 64
OWN = 6
CORE, FAR = 768, 769
IMG = 197
NIMG = 4
BOTH = ("rows", "seq")
F32 = jnp.float32
BF16 = jnp.bfloat16
MASKED = -1e30


def route(step):
    pairs = []
    for r in range(32):
        z, x_lo, y = r // 8, (r // 4) % 2, r % 4
        for s in range(4):
            x, c = (s // 2) * 2 + x_lo, s % 2
            tx, ty, tz, tc = step(x, y, z, c)
            target = (tz * 8 + (tx % 2) * 4 + ty) * 4 + (tx // 2) * 2 + tc
            pairs.append((r * 4 + s, target))
    return pairs


def send(values, step):
    return lax.ppermute(values, BOTH, route(step))


def swap_core(values):
    return send(values, lambda x, y, z, c: (x, y, z, 1 - c))


def swap_far(values):
    return send(values, lambda x, y, z, c: (x ^ 2, y, z, c))


def axis_step(axis, first):
    def step(x, y, z, c):
        flip = 1 if (c == 0) == first else 3
        at = {"x": x, "y": y, "z": z}
        at[axis] ^= flip
        return (at["x"], at["y"], at["z"], c)

    return step


UP_FACTORS = (1024 / (2 * 788), 1024 / (2 * 236))
ORDERS = (("x", "y", "z"), ("y", "z", "x"), ("z", "x", "y"))


def normalize(inputs):
    centred = inputs - jnp.mean(inputs, axis=-1, keepdims=True)
    factor = lax.rsqrt(jnp.mean(centred * centred, axis=-1, keepdims=True) + 1e-05)
    return centred * factor, factor


def normalize_back(grad, xhat, factor, gain):
    gy = grad * gain
    mean_gy = jnp.mean(gy, axis=-1, keepdims=True)
    mean_gx = jnp.mean(gy * xhat, axis=-1, keepdims=True)
    return factor * (gy - mean_gy - xhat * mean_gx)


SMALL = pl.BlockSpec(memory_space=pltpu.SMEM)
WHOLE = pl.BlockSpec(memory_space=pltpu.VMEM)
N = 256


def marked_kernel(partner, tokens_ref, segments_ref, modality_ref, out_ref):
    segments = segments_ref[...]
    tag = jnp.zeros(segments.shape, jnp.int32)
    for n in range(8):
        tag = jnp.where(segments == n, partner[0, n], tag)
    marks = jnp.concatenate(
        [tag, modality_ref[...], jnp.zeros((1, 256), jnp.int32)], axis=1).astype(F32)
    out_ref[:N, :] = tokens_ref[...]
    out_ref[N:, :] = jnp.concatenate([marks, jnp.zeros((15, 768), F32)], axis=0).astype(BF16)


def marked(partner, tokens, segments, modality):
    return pl.pallas_call(
        marked_kernel,
        in_specs=[SMALL, WHOLE, WHOLE, WHOLE],
        out_specs=WHOLE,
        out_shape=jax.ShapeDtypeStruct((N + 16, 768), BF16),
        compiler_params=pltpu.CompilerParams(vmem_limit_bytes=60 * 2**20),
        name="marked",
    )(partner, tokens, segments, modality)


def mark_lanes(ext):
    row = ext[N:, :].astype(F32)
    place = lax.broadcasted_iota(jnp.int32, (128, N), 0)
    tag = jnp.broadcast_to(row[:1, :N], (128, N))
    kind = jnp.broadcast_to(row[:1, N : 2 * N], (128, N))
    hot = jnp.where((place < NIMG) & (place.astype(F32) == tag), 1.0, 0.0)
    return jnp.transpose(jnp.where(place == 8, kind, hot))


def project_kernel(at_ref, near, a_ref, b_ref, gains_ref, *refs):
    count = 3 if near else 2
    weights, outs = refs[:count], refs[count:]
    for n, ext_ref in enumerate((a_ref, b_ref)):
        rows = slice(n * N, (n + 1) * N)
        ext = ext_ref[...]
        xhat, _ = normalize(ext[:N].astype(F32))
        act = (xhat * gains_ref[0:1, :] + gains_ref[1:2, :]).astype(BF16)
        outs[0][rows, :] = act
        marks = mark_lanes(ext)
        outs[1][rows, :] = marks.astype(BF16)
        for m in range(count):
            part = mm(act, weights[m][...])
            outs[2 + m][rows, :] = (0.125 * part if near and m == 0 else part).astype(BF16)
        if near:
            lane = lax.broadcasted_iota(jnp.int32, marks.shape, 1)
            outs[5][rows, :] = jnp.where((lane < NIMG) & (marks == 0.0), MASKED, 0.0).astype(BF16)


def project(table, first, second, gains, w_qkv, near):
    kinds = (0, 1, 2) if near else (1, 2)
    sizes = [768, 128] + [384] * len(kinds) + ([128] if near else [])
    whole = lambda shape: pl.BlockSpec(shape, lambda i, at: (0, 0))
    return pl.pallas_call(
        lambda at_ref, *refs: project_kernel(at_ref, near, *refs),
        grid_spec=pltpu.PrefetchScalarGridSpec(
            num_scalar_prefetch=1,
            grid=(1,),
            in_specs=[whole((N + 16, 768))] * 2 + [whole((4, 768))]
            + [pl.BlockSpec((768, 384), lambda i, at, n=n: (0, 2 * n + at[CORE])) for n in kinds],
            out_specs=[whole((2 * N, size)) for size in sizes],
        ),
        out_shape=[jax.ShapeDtypeStruct((2 * N, size), BF16) for size in sizes],
        compiler_params=pltpu.CompilerParams(vmem_limit_bytes=6 * 2**20),
        cost_estimate=pl.CostEstimate(
            flops=2 * 512 * 768 * 384 * len(kinds), bytes_accessed=4 * 2**20, transcendentals=0),
        name="project_near" if near else "project_away",
    )(table, first, second, gains, *[w_qkv] * len(kinds))


def middle_kernel(place, grad_ref, sib_ref, xhat_ref, factor_ref, cot_own_ref, cot_sib_ref,
                  gains_ref, w_out_ref, hidden_ref, att_ref, proj_ref, vec_ref):
    core = place[CORE]
    for n, cot_ref in enumerate((cot_own_ref, cot_sib_ref)):
        rows, other = slice(n * N, (n + 1) * N), slice((1 - n) * N, (2 - n) * N)
        grad = grad_ref[rows, :].astype(F32) + sib_ref[other, :].astype(F32)
        xhat = xhat_ref[rows, :].astype(F32)
        total = cot_ref[...].astype(F32) + normalize_back(grad, xhat, factor_ref[rows, :], gains_ref[2:3, :])
        low = total.astype(BF16)
        if n == 0:
            hidden_ref[...] = total
            vec_ref[0:1, :] = jnp.sum(grad * xhat, axis=0, keepdims=True)
            vec_ref[1:2, :] = jnp.sum(grad, axis=0, keepdims=True)
        mine = w_out_ref[pl.ds(pl.multiple_of(core * 384, 384), 384), :]
        att_ref[rows, :] = mm(low, mine, NT).astype(BF16)
        proj_ref[rows, :] = jnp.where(core == 0, low[:, :384], low[:, 384:])


def middle(place, *operands):
    return pl.pallas_call(
        middle_kernel,
        in_specs=[SMALL] + [WHOLE] * len(operands),
        out_specs=[WHOLE] * 4,
        out_shape=[
            jax.ShapeDtypeStruct((N, 768), F32),
            jax.ShapeDtypeStruct((2 * N, 384), BF16),
            jax.ShapeDtypeStruct((2 * N, 384), BF16),
            jax.ShapeDtypeStruct((2, 768), F32),
        ],
        compiler_params=pltpu.CompilerParams(vmem_limit_bytes=6 * 2**20),
        cost_estimate=pl.CostEstimate(
            flops=2 * 512 * 768 * 384, bytes_accessed=8 * 2**20, transcendentals=0),
        name="middle",
    )(place, *operands)


def gelu_parts(pre):
    phi = 0.5 * (1.0 + lax.erf(pre * 0.7071067811865476))
    slope = phi + pre * (0.3989422804014327 * jnp.exp(-0.5 * pre * pre))
    return pre * phi, slope


NT = (((1,), (1,)), ((), ()))
TN = (((0,), (0,)), ((), ()))
NN = (((1,), (0,)), ((), ()))


def mm(left, right, dims=NN):
    return lax.dot_general(left, right, dims, preferred_element_type=F32)


def head_lanes(shape, h):
    lane = lax.broadcasted_iota(jnp.int32, shape, len(shape) - 1)
    return (lane >= HD) == (h == 1)


def turned(values):
    return jnp.transpose(values.astype(F32)).astype(BF16)


def stacked(near_ref, away_ref):
    return jnp.concatenate([near_ref[...], away_ref[...]], axis=0)


def forward_kernel(q_ref, kn_ref, ka_ref, vn_ref, va_ref, qx_ref, xn_ref, xa_ref, out_ref, lse_ref):
    keys = jnp.concatenate([stacked(kn_ref, ka_ref), stacked(xn_ref, xa_ref)], axis=1)
    values = stacked(vn_ref, va_ref)
    q_pair = q_ref[...]
    lanes = head_lanes(q_pair.shape, 0)
    values_t = turned(values)
    value_rows = lax.broadcasted_iota(jnp.int32, values_t.shape, 0) < HD
    mixed = []
    for h in range(2):
        mine = lanes if h == 0 else jnp.logical_not(lanes)
        mine_values = value_rows if h == 0 else jnp.logical_not(value_rows)
        query = jnp.concatenate([jnp.where(mine, q_pair, 0), qx_ref[...]], axis=1)
        scores = mm(keys, query, NT)
        peak = jnp.max(scores, axis=0, keepdims=True)
        weights = jnp.exp(scores - peak).astype(BF16)
        both = mm(jnp.where(mine_values, values_t, 1), weights)
        total = both[127:128, :] if h == 0 else both[0:1, :]
        mixed.append(both * (1.0 / total))
        lse_ref[0, h : h + 1, :] = peak + jnp.log(total)
    out_rows = lax.broadcasted_iota(jnp.int32, mixed[0].shape, 0) < HD
    out_ref[...] = jnp.transpose(jnp.where(out_rows, mixed[0], mixed[1])).astype(BF16)


BY_PAIR = pl.BlockSpec((2 * N, 128), lambda p: (0, p))
FIXED = pl.BlockSpec((2 * N, 128), lambda p: (0, 0))


def attend_forward(*operands):
    return pl.pallas_call(
        forward_kernel,
        grid=(3,),
        in_specs=[BY_PAIR] * 5 + [FIXED] * 3,
        out_specs=[BY_PAIR, pl.BlockSpec((1, 2, 2 * N), lambda p: (p, 0, 0))],
        out_shape=[
            jax.ShapeDtypeStruct((2 * N, 384), BF16),
            jax.ShapeDtypeStruct((3, 2, 2 * N), F32),
        ],
        compiler_params=pltpu.CompilerParams(vmem_limit_bytes=6 * 2**20),
        cost_estimate=pl.CostEstimate(
            flops=2 * 2 * OWN * 512 * 1024 * 256, bytes_accessed=4 * 2**20,
            transcendentals=OWN * 512 * 1024),
        name="attend_forward",
    )(*operands)


def backward_kernel(q_ref, kn_ref, ka_ref, vn_ref, va_ref, do_ref, o_ref, qx_ref, xn_ref, xa_ref,
                    lse_ref, *refs):
    dq_ref, dk_ref, dv_ref = refs[-3:]
    k_pair, values = stacked(kn_ref, ka_ref), stacked(vn_ref, va_ref)
    keys = jnp.concatenate([k_pair, stacked(xn_ref, xa_ref)], axis=1)
    q_pair, grads = q_ref[...], do_ref[...]
    lanes = head_lanes(q_pair.shape, 0)
    product = grads.astype(F32) * o_ref[...].astype(F32)
    k_turned = turned(k_pair)
    rows = lax.broadcasted_iota(jnp.int32, (128, 2 * N), 0) < HD
    dq = jnp.zeros((128, 2 * N), F32)
    dk = jnp.zeros(k_pair.shape, F32)
    dv = jnp.zeros(k_pair.shape, F32)
    for h in range(2):
        mine = lanes if h == 0 else jnp.logical_not(lanes)
        q_head = jnp.where(mine, q_pair, 0)
        g_head = jnp.where(mine, grads, 0)
        dot_row = jnp.transpose(jnp.sum(jnp.where(mine, product, 0.0), axis=1, keepdims=True))
        scores = mm(keys, jnp.concatenate([q_head, qx_ref[...]], axis=1), NT)
        prob = jnp.exp(scores - lse_ref[0, h : h + 1, :])
        dv += mm(prob.astype(BF16), g_head)
        grad_prob = mm(values, g_head, NT)
        grad_scores = (prob * (grad_prob - dot_row)).astype(BF16)
        dk += mm(grad_scores, q_head)
        part = mm(k_turned, grad_scores)
        dq += jnp.where(rows if h == 0 else jnp.logical_not(rows), part, 0.0)
    dq_ref[...] = jnp.transpose(dq).astype(BF16) * jnp.asarray(0.125, BF16)
    dk_ref[...] = dk.astype(BF16)
    dv_ref[...] = dv.astype(BF16)


def attend_backward(operands, first, pairs, gates):
    by_pair = pl.BlockSpec((2 * N, 128), lambda p: (0, first + p))
    sizes = (2 * N, 4 * N, 4 * N)
    return pl.pallas_call(
        backward_kernel,
        grid=(pairs,),
        in_specs=[by_pair] * 7 + [FIXED] * 3
        + [pl.BlockSpec((1, 2, 2 * N), lambda p: (first + p, 0, 0))]
        + [pl.BlockSpec(memory_space=pl.ANY)] * len(gates),
        out_specs=[pl.BlockSpec((size, 128), lambda p: (0, p)) for size in sizes],
        out_shape=[jax.ShapeDtypeStruct((size, pairs * 128), BF16) for size in sizes],
        compiler_params=pltpu.CompilerParams(vmem_limit_bytes=10 * 2**20),
        cost_estimate=pl.CostEstimate(
            flops=2 * 5 * 2 * pairs * 512 * 1024 * 256, bytes_accessed=6 * 2**20,
            transcendentals=2 * pairs * 512 * 1024),
        name="attend_backward",
    )(*operands, *gates)


FF_STEP = 512
E_STEP = 512
EXPERT_MB = 40
CELLS_MB = 28


def expert_kernel(at_ref, att_own_ref, att_sib_ref, own_ref, sib_ref, cot_own_ref, cot_sib_ref,
                  marks_ref, gains_ref, w_out_ref, wu_ref, wd_ref,
                  hidden_ref, low_ref, xhat_ref, factor_ref, act_t_ref, inner_t_ref, slope_ref,
                  act_acc, grad_acc):
    f = pl.program_id(0)
    core = at_ref[CORE]

    @pl.when(f == 0)
    def _():
        mine = w_out_ref[pl.ds(pl.multiple_of(core * 384, 384), 384), :]
        other = w_out_ref[pl.ds(pl.multiple_of((1 - core) * 384, 384), 384), :]
        for n, ext_ref in enumerate((own_ref, sib_ref)):
            rows, theirs = slice(n * N, (n + 1) * N), slice((1 - n) * N, (2 - n) * N)
            hidden = ext_ref[:N, :].astype(F32) + (
                mm(att_own_ref[rows, :], mine) + mm(att_sib_ref[theirs, :], other))
            xhat, factor = normalize(hidden)
            xhat_ref[rows, :] = xhat.astype(BF16)
            factor_ref[rows, :] = factor
            act = xhat * gains_ref[2:3, :] + gains_ref[3:4, :]
            act_acc[rows, :] = act.astype(BF16)
            act_t_ref[:, rows] = jnp.transpose(act).astype(BF16)
            if n == 0:
                hidden_ref[...] = hidden
        grad_acc[...] = jnp.zeros(grad_acc.shape, F32)

    act = act_acc[...]
    cot = jnp.concatenate([cot_own_ref[...], cot_sib_ref[...]], axis=0)
    text = marks_ref[:, 8:9].astype(F32) > 0.0
    pre = jnp.where(text, mm(act, wu_ref[1]), mm(act, wu_ref[0]))
    inner, slope = gelu_parts(pre)
    grad_pre = jnp.where(text, mm(cot, wd_ref[1], NT), mm(cot, wd_ref[0], NT)) * slope
    inner_t_ref[...] = jnp.transpose(inner).astype(BF16)
    low = grad_pre.astype(BF16)
    slope_ref[...] = low
    zero = jnp.zeros((), BF16)
    grad_acc[...] += (mm(jnp.where(text, zero, low), wu_ref[0], NT)
                      + mm(jnp.where(text, low, zero), wu_ref[1], NT))

    @pl.when(f == pl.num_programs(0) - 1)
    def _():
        low_ref[...] = grad_acc[...].astype(BF16)


def experts(core, *operands):
    steps = 1536 // E_STEP
    shapes = [((N, 768), F32), ((2 * N, 768), BF16), ((2 * N, 768), BF16), ((2 * N, 1), F32),
              ((768, 2 * N), BF16)]
    fixed = lambda shape: pl.BlockSpec(shape, lambda f, *_: (0,) * len(shape))
    return pl.pallas_call(
        expert_kernel,
        grid_spec=pltpu.PrefetchScalarGridSpec(
            num_scalar_prefetch=1,
            grid=(steps,),
            in_specs=[fixed(v.shape) for v in operands[:-2]] + [
                pl.BlockSpec((2, 768, E_STEP), lambda f, at: (0, 0, at[CORE] * steps + f)),
                pl.BlockSpec((2, E_STEP, 768), lambda f, at: (0, at[CORE] * steps + f, 0)),
            ],
            out_specs=[fixed(shape) for shape, _ in shapes] + [
                pl.BlockSpec((E_STEP, 2 * N), lambda f, at: (f, 0)),
                pl.BlockSpec((2 * N, E_STEP), lambda f, at: (0, f)),
            ],
            scratch_shapes=[pltpu.VMEM((2 * N, 768), BF16), pltpu.VMEM((2 * N, 768), F32)],
        ),
        out_shape=[jax.ShapeDtypeStruct(*v) for v in shapes] + [
            jax.ShapeDtypeStruct((1536, 2 * N), BF16),
            jax.ShapeDtypeStruct((2 * N, 1536), BF16)],
        compiler_params=pltpu.CompilerParams(
            vmem_limit_bytes=18 * 2**20, dimension_semantics=("arbitrary",)),
        cost_estimate=pl.CostEstimate(
            flops=6 * 2 * 512 * 768 * 1536 + 2 * 512 * 768 * 768, bytes_accessed=22 * 2**20,
            transcendentals=2 * 512 * 1536),
        name="experts",
    )(core, *operands)


def kind_row(marks_ref):
    return turned(marks_ref[...])[8:9, :].astype(F32) > 0.0


def branch_kernel(at_ref, inner_t_ref, wd_ref, hidden_ref, marks_ref, *refs):
    own_ref, sib_ref, acc = refs[-3:]
    f = pl.program_id(0)
    text, inner_t, zero = kind_row(marks_ref), inner_t_ref[...], jnp.zeros((), BF16)
    part = (mm(jnp.where(text, zero, inner_t), wd_ref[0], TN)
            + mm(jnp.where(text, inner_t, zero), wd_ref[1], TN))

    @pl.when(f == 0)
    def _():
        acc[...] = part

    @pl.when(f > 0)
    def _():
        acc[...] += part

    @pl.when(f == pl.num_programs(0) - 1)
    def _():
        own_ref[...] = hidden_ref[...] + acc[:N, :]
        sib_ref[...] = acc[N:, :].astype(BF16)


def branches(table, inner_t, w_down, hidden, marks, gates):
    return pl.pallas_call(
        branch_kernel,
        grid_spec=pltpu.PrefetchScalarGridSpec(
            num_scalar_prefetch=1,
            grid=(3,),
            in_specs=[
                pl.BlockSpec((512, 2 * N), lambda f, at: (f, 0)),
                pl.BlockSpec((2, 512, 768), lambda f, at: (0, at[CORE] * 3 + f, 0)),
                pl.BlockSpec((N, 768), lambda f, at: (0, 0)),
                pl.BlockSpec((2 * N, 128), lambda f, at: (0, 0))] + [ANYWHERE] * len(gates),
            out_specs=[pl.BlockSpec((N, 768), lambda f, at: (0, 0))] * 2,
            scratch_shapes=[pltpu.VMEM((2 * N, 768), F32)],
        ),
        out_shape=[jax.ShapeDtypeStruct((N, 768), F32), jax.ShapeDtypeStruct((N, 768), BF16)],
        compiler_params=pltpu.CompilerParams(
            vmem_limit_bytes=20 * 2**20, dimension_semantics=("arbitrary",)),
        cost_estimate=pl.CostEstimate(
            flops=2 * 2 * 512 * 768 * 1536, bytes_accessed=8 * 2**20, transcendentals=0),
        name="branches",
    )(table, inner_t, w_down, hidden, marks, *gates)


def cells_kernel(g, at_slot, act_t_ref, grad_ref, inner_t_ref, cot_own_ref, cot_sib_ref, marks_ref,
                 *refs):
    if g == 0:
        full_ref, keep_ref, send_ref, low_ref, up_acc, down_acc = refs
        low_ref[...] = full_ref[...]
    else:
        keep_ref, send_ref, up_acc, down_acc = refs[-4:]
    zero = jnp.zeros((), BF16)
    text, text_row = marks_ref[:, 8:9].astype(F32) > 0.0, kind_row(marks_ref)
    act_t, inner_t = act_t_ref[...], inner_t_ref[...]
    grad = grad_ref[:, g * FF_STEP : (g + 1) * FF_STEP]
    lanes = slice(g * 256, (g + 1) * 256)
    cot = jnp.concatenate([cot_own_ref[:, lanes], cot_sib_ref[:, lanes]], axis=0)
    for e in range(2):
        up = mm(act_t, jnp.where(text, grad, zero) if e else jnp.where(text, zero, grad))
        up_acc[e, 0] = up[:, :256]
        up_acc[e, 1] = up[:, 256:]
        down_acc[e] = mm(
            jnp.where(text_row, inner_t, zero) if e else jnp.where(text_row, zero, inner_t), cot)

    for n, target in enumerate((keep_ref, send_ref)):
        def cell(i, carry):
            slot = g * 64 + n * 32 + i
            half = at_slot[192 + slot]
            rows = pl.ds(pl.multiple_of(at_slot[slot], 8), 24)
            below = pl.ds(pl.multiple_of(at_slot[384 + slot], 8), 24)
            target[i] = jnp.concatenate(
                [up_acc[0, half, rows, :], up_acc[1, half, rows, :],
                 down_acc[0, below, :], down_acc[1, below, :]], axis=0).astype(BF16)
            return carry
        lax.fori_loop(0, 32, cell, 0, unroll=4)


def cells(g, table, act_t, grad_pre, inner_t, cot_own, cot_sib, marks, more):
    return pl.pallas_call(
        lambda *refs: cells_kernel(g, *refs),
        in_specs=[SMALL] + [WHOLE] * 6 + ([WHOLE] if g == 0 else [ANYWHERE] * len(more)),
        out_specs=[WHOLE] * (3 if g == 0 else 2),
        out_shape=[jax.ShapeDtypeStruct((32, 96, 256), BF16)] * 2
        + [jax.ShapeDtypeStruct((2 * N, 768), BF16)] * (g == 0),
        scratch_shapes=[pltpu.VMEM((2, 2, 768, 256), F32), pltpu.VMEM((2, 1536, 256), F32)],
        compiler_params=pltpu.CompilerParams(vmem_limit_bytes=10 * 2**20),
        cost_estimate=pl.CostEstimate(
            flops=4 * 2 * 512 * 768 * 512, bytes_accessed=8 * 2**20, transcendentals=0),
        name="cells",
    )(table, act_t, grad_pre, inner_t, cot_own, cot_sib, marks, *more)


def cell_places():
    table = np.zeros((32, 4, 4, 3, 4, 4, 4), np.int32)
    for r, s in np.ndindex(32, 4):
        here = {"z": r // 8, "y": r % 4, "x": (s // 2) * 2 + (r // 4) % 2}
        flips = (0, 1, 3, 2) if s % 2 else (0, 3, 1, 2)
        for g, order in enumerate(ORDERS):
            for slot in np.ndindex(4, 4, 4):
                at = {a: here[a] ^ flips[n] for a, n in zip(order, slot)}
                x_hi, x_lo = at["x"] // 2, at["x"] % 2
                table[(r, s, 0, g) + slot] = 24 * (at["z"] * 8 + x_lo * 4 + at["y"])
                table[(r, s, 1, g) + slot] = x_hi
                table[(r, s, 2, g) + slot] = 24 * (
                    (at["z"] % 2) * 32 + x_lo * 16 + at["y"] * 4 + x_hi * 2 + at["z"] // 2)
                table[(r, s, 3, g) + slot] = at["z"] * 16 + x_lo * 8 + at["y"] * 2 + x_hi
    coordinates = np.array([[n % 2, n % 4 // 2] + [0] * 126 for n in range(128)], np.int32)
    return np.concatenate([table.reshape(128, 768), coordinates], axis=1)


def add_up(parts):
    total = parts[0].astype(F32)
    for part in parts[1:]:
        total = total + part.astype(F32)
    return total.astype(BF16)


def in_hbm(values):
    return list(values)


def pass_kernel(gates, *refs):
    count = (len(refs) - gates) // 3
    for g in range(count):
        refs[2 * count + gates + g][...] = add_up([refs[2 * g][...], refs[2 * g + 1][...]])


ANYWHERE = pl.BlockSpec(memory_space=pl.ANY)


def pass_on(kept, arrived, name, gates=()):
    _, slots, rows, lanes = kept[0].shape
    block = max(slots // 4, 1)
    one = pl.BlockSpec((None, block, rows, lanes), lambda i: (1, i, 0, 0))
    return pl.pallas_call(
        lambda *refs: pass_kernel(len(gates), *refs),
        grid=(slots // block,),
        in_specs=[one] * (2 * len(kept)) + [ANYWHERE] * len(gates),
        out_specs=[pl.BlockSpec((block, rows, lanes), lambda i: (i, 0, 0))] * len(kept),
        out_shape=[jax.ShapeDtypeStruct((slots, rows, lanes), BF16)] * len(kept),
        compiler_params=pltpu.CompilerParams(vmem_limit_bytes=6 * 2**20),
        cost_estimate=pl.CostEstimate(
            flops=0, transcendentals=0, bytes_accessed=6 * len(kept) * slots * rows * lanes),
        name=name,
    )(*in_hbm([v for pair in zip(kept, arrived) for v in pair]), *gates)


def settle_kernel(groups, sizes, *refs):
    ins, outs = refs, refs[-2 * groups :]
    at = 0
    for g in range(groups):
        row = 0
        for size in sizes:
            for half in range(2):
                outs[2 * g + half][:, row : row + size, :] = add_up(
                    [ins[at + k][...] for k in range(3)])
                at += 3
            row += size


def settle(pieces, name, gates=()):
    groups = len(pieces[0])
    sizes = [p[0][0].shape[2] for p in pieces]
    _, slots, _, lanes = pieces[0][0][0].shape
    half = slots // 2
    block = max(half // 4, 1)
    steps = half // block
    operands, specs = [], []
    for g in range(groups):
        for p, size in zip(pieces, sizes):
            for h in range(2):
                wide = pl.BlockSpec(
                    (None, block, size, lanes), lambda i, h=h: (0, i + h * steps, 0, 0))
                flat = pl.BlockSpec((block, size, lanes), lambda i, h=h: (i + h * steps, 0, 0))
                operands += list(p[g])
                specs += [wide, wide, flat]
    rows = sum(sizes)
    outs = pl.pallas_call(
        lambda *refs: settle_kernel(groups, sizes, *refs),
        grid=(steps,),
        in_specs=specs + [ANYWHERE] * len(gates),
        out_specs=[pl.BlockSpec((block, rows, lanes), lambda i: (i, 0, 0))] * (2 * groups),
        out_shape=[jax.ShapeDtypeStruct((half, rows, lanes), BF16)] * (2 * groups),
        compiler_params=pltpu.CompilerParams(vmem_limit_bytes=8 * 2**20),
        cost_estimate=pl.CostEstimate(
            flops=0, transcendentals=0, bytes_accessed=8 * groups * slots * rows * lanes),
        name=name,
    )(*operands, *gates)
    shaped = [o.reshape(2, half // 2, rows, lanes) for o in outs]
    return shaped[0::2], shaped[1::2]


def finish_kernel(*refs):
    held_ref, down_ref = refs[-2:]
    for g in range(3):
        cell = add_up([refs[3 * g + k][...] for k in range(3)])
        held_ref[g, :48, :] = cell[:48]
        held_ref[g, 48:, :] = cell[96:]
        down_ref[g] = cell[48:96]


def finish(kept, first, second, gates):
    wide = pl.BlockSpec((None, None, 128, 256), lambda i: (0, 0, 0, 0))
    flat = pl.BlockSpec((None, 128, 256), lambda i: (0, 0, 0))
    return pl.pallas_call(
        finish_kernel,
        grid=(1,),
        in_specs=[wide, wide, flat] * 3 + [ANYWHERE] * len(gates),
        out_specs=[pl.BlockSpec((3, 80, 256), lambda i: (0, 0, 0)),
                   pl.BlockSpec((3, 48, 256), lambda i: (0, 0, 0))],
        out_shape=[jax.ShapeDtypeStruct((3, 80, 256), BF16), jax.ShapeDtypeStruct((3, 48, 256), BF16)],
        compiler_params=pltpu.CompilerParams(vmem_limit_bytes=4 * 2**20),
        name="finish",
    )(*[v for g in range(3) for v in (kept[g], first[g], second[g])], *gates)


def after_kernel(values_ref, *refs):
    refs[-1][...] = values_ref[...]


def after(values, gates):
    return pl.pallas_call(
        after_kernel,
        in_specs=[WHOLE] + [ANYWHERE] * len(gates),
        out_specs=WHOLE,
        out_shape=jax.ShapeDtypeStruct(values.shape, values.dtype),
        compiler_params=pltpu.CompilerParams(vmem_limit_bytes=4 * 2**20),
        name="after",
    )(values, *gates)


def put(acc, first, part, rows=slice(None)):
    for n in range(part.shape[1] // 128):
        column = first + n * 128
        lanes = slice(column % 256, column % 256 + 128)
        acc[column // 256, rows, lanes] = part[:, n * 128 : (n + 1) * 128]


def spill_rows(target, acc, at_slot, g, base, extra):
    def cell(i, carry):
        slot = g * 64 + base + i
        rows = pl.ds(pl.multiple_of(at_slot[slot], 8), 24)
        part = acc[at_slot[192 + slot] + 2 * (g % 2), rows, :]
        target[i] = jnp.concatenate([part, extra(slot)], axis=0).astype(BF16)
        return carry
    lax.fori_loop(0, 32, cell, 0, unroll=4)


def tail_kernel(at_slot, act_ref, away_ref, q_ref, qb_ref, ka_ref, kb_ref, va_ref, *refs):
    keeps, sends, acc = refs[-5:-3], refs[-3:-1], refs[-1]
    act, away = act_ref[...], away_ref[...]
    near = mm(act, jnp.concatenate(
        [r[: 2 * N, :] for r in (q_ref, qb_ref, ka_ref, kb_ref, va_ref)], axis=1), TN)
    far = mm(away, jnp.concatenate(
        [r[2 * N :, :] for r in (ka_ref, kb_ref, va_ref)], axis=1), TN)
    put(acc, 0, near[:, :384])
    put(acc, 384, near[:, 384:] + far)
    for g in range(2):
        blank = lambda slot: jnp.zeros((8, 256), F32)
        spill_rows(keeps[g], acc, at_slot, g, 0, blank)
        spill_rows(sends[g], acc, at_slot, g, 32, blank)


def tail_cells(table, *operands):
    return pl.pallas_call(
        tail_kernel,
        in_specs=[SMALL] + [WHOLE] * len(operands),
        out_specs=[WHOLE] * 4,
        out_shape=[jax.ShapeDtypeStruct((32, 32, 256), BF16)] * 4,
        scratch_shapes=[pltpu.VMEM((4, 768, 256), F32)],
        compiler_params=pltpu.CompilerParams(vmem_limit_bytes=14 * 2**20),
        cost_estimate=pl.CostEstimate(
            flops=2 * 768 * 512 * (1024 + 640), bytes_accessed=8 * 2**20, transcendentals=0),
        name="tail_cells",
    )(table, *operands)


def inputs_kernel(at_slot, act_ref, away_ref, q_ref, qb_ref, ka_ref, kb_ref, va_ref, vb_ref,
                  att_own_ref, att_sib_ref, proj_ref, own_ref, sib_ref, far_ref, far_sib_ref,
                  second_ref, *refs):
    weights = refs[:3]
    keep_ref, send_ref, cell_keep, cell_send, acc, table = refs[-6:]
    core = at_slot[CORE]
    put(acc, 0, mm(act_ref[...], vb_ref[: 2 * N, :], TN) + mm(away_ref[...], vb_ref[2 * N :, :], TN))
    mine = pl.ds(pl.multiple_of(core * 384, 384), 384)
    other = pl.ds(pl.multiple_of((1 - core) * 384, 384), 384)
    put(acc, 128, mm(att_own_ref[...], proj_ref[...], TN), mine)
    put(acc, 128, mm(att_sib_ref[:N, :], proj_ref[N:, :], TN)
        + mm(att_sib_ref[N:, :], proj_ref[:N, :], TN), other)

    vectors = [jnp.zeros((1, 768), F32)] * 2 + [second_ref[0:1, :], second_ref[1:2, :]]
    wide = list(zip((q_ref, ka_ref, va_ref), (qb_ref, kb_ref, vb_ref), weights))
    for n, ext_ref in enumerate((own_ref, sib_ref, far_ref, far_sib_ref)):
        rows = slice(n * N, (n + 1) * N)
        total = jnp.zeros((N, 768), F32)
        for a_ref, b_ref, w_ref in wide[0 if n < 2 else 1 :]:
            grads = jnp.concatenate([a_ref[rows, :], b_ref[rows, :]], axis=1)
            total += mm(grads, w_ref[...], NT)
        xhat, _ = normalize(ext_ref[:N, :].astype(F32))
        vectors[0] += jnp.sum(total * xhat, axis=0, keepdims=True)
        vectors[1] += jnp.sum(total, axis=0, keepdims=True)
        half = slice((n // 2) * N, (n // 2 + 1) * N)
        if n % 2 == 0:
            keep_ref[half, :] = total
        else:
            send_ref[half, :] = total.astype(BF16)

    chip = lax.broadcasted_iota(jnp.int32, (64, 768), 0)
    owner = lax.broadcasted_iota(jnp.int32, (64, 768), 1) // 12
    feature = lax.broadcasted_iota(jnp.int32, (768, 128), 0) % 12
    lane = lax.broadcasted_iota(jnp.int32, (768, 128), 1)
    spread = jnp.zeros((64, 128), F32)
    for n in range(4):
        line = jnp.broadcast_to(vectors[n], (64, 768))
        values = jnp.where(chip == owner, line, 0.0).astype(BF16)
        spread += mm(values, jnp.where(lane == feature + 12 * n, 1.0, 0.0).astype(BF16))
    table[...] = spread

    def lines(slot):
        row = table[pl.ds(at_slot[576 + slot], 1), :]
        return jnp.concatenate(
            [jnp.broadcast_to(row, (8, 128)), jnp.zeros((8, 128), F32)], axis=1)

    spill_rows(cell_keep, acc, at_slot, 2, 0, lines)
    spill_rows(cell_send, acc, at_slot, 2, 32, lines)


def input_partials(table, operands, gates):
    whole = lambda shape: pl.BlockSpec(shape, lambda i, *_: (0,) * len(shape))
    shapes = [((2 * N, 768), F32), ((2 * N, 768), BF16)] + [((32, 32, 256), BF16)] * 2
    return pl.pallas_call(
        inputs_kernel,
        grid_spec=pltpu.PrefetchScalarGridSpec(
            num_scalar_prefetch=1,
            grid=(1,),
            in_specs=[whole(v.shape) for v in operands[:-1]]
            + [pl.BlockSpec((768, 384), lambda i, at, n=n: (0, 2 * n + at[CORE])) for n in range(3)]
            + [ANYWHERE] * len(gates),
            out_specs=[whole(shape) for shape, _ in shapes],
            scratch_shapes=[pltpu.VMEM((2, 768, 256), F32), pltpu.VMEM((64, 128), F32)],
        ),
        out_shape=[jax.ShapeDtypeStruct(*v) for v in shapes],
        compiler_params=pltpu.CompilerParams(vmem_limit_bytes=16 * 2**20),
        cost_estimate=pl.CostEstimate(
            flops=2 * 768 * 384 * 512 * 7, bytes_accessed=10 * 2**20, transcendentals=0),
        name="input_partials",
    )(table, *operands, *[operands[-1]] * 2, *gates)


def sum_core_kernel(own_ref, sib_ref, *refs):
    refs[-1][...] = (own_ref[...] + sib_ref[...].astype(F32)).astype(BF16)


def sum_core(own, sib, gates):
    half = pl.BlockSpec((N, 768), lambda i: (1, 0))
    return pl.pallas_call(
        sum_core_kernel,
        grid=(1,),
        in_specs=[half, half] + [ANYWHERE] * len(gates),
        out_specs=pl.BlockSpec((N, 768), lambda i: (0, 0)),
        out_shape=jax.ShapeDtypeStruct((N, 768), BF16),
        compiler_params=pltpu.CompilerParams(vmem_limit_bytes=4 * 2**20),
        name="sum_core",
    )(own, sib, *gates)


def token_kernel(tokens_ref, hidden_ref, own_ref, sib_ref, far_ref, gains_ref, out_own_ref,
                 out_sib_ref, grad_ref, out_ref):
    grad = own_ref[...] + sib_ref[...].astype(F32) + far_ref[...].astype(F32)
    xhat, factor = normalize(tokens_ref[...].astype(F32))
    grad_ref[...] = hidden_ref[...] + normalize_back(grad, xhat, factor, gains_ref[0:1, :])
    out_ref[...] = (out_own_ref[...] + out_sib_ref[...].astype(F32)).astype(BF16)


def token_grads(tokens, hidden, own, sib, far, gains, out_own, out_sib):
    half = pl.BlockSpec((N, 768), lambda i: (0, 0))
    return pl.pallas_call(
        token_kernel,
        grid=(1,),
        in_specs=[half] * 5 + [pl.BlockSpec((4, 768), lambda i: (0, 0))] + [half] * 2,
        out_specs=[half] * 2,
        out_shape=[jax.ShapeDtypeStruct((N, 768), F32), jax.ShapeDtypeStruct((N, 768), BF16)],
        compiler_params=pltpu.CompilerParams(vmem_limit_bytes=8 * 2**20),
        name="token_grads",
    )(tokens, hidden, own, sib, far, gains, out_own, out_sib)


def assemble_kernel(at_ref, own_ref, near_ref, away_ref, cross_ref, down_ref, up_ref, qkv_ref, out_ref,
                    vec_ref, below_ref, held):
    core, far = at_ref[CORE], at_ref[FAR]
    held[far * 2 + core] = own_ref[...]
    held[far * 2 + 1 - core] = near_ref[...]
    held[2 - far * 2 + core] = away_ref[...]
    held[2 - far * 2 + 1 - core] = cross_ref[...]
    line = held[far * 2, 2, 64:, :128].astype(F32) + held[far * 2 + 1, 2, 64:, :128].astype(F32)
    vec_ref[...] = jnp.where(core == 0, line, pltpu.roll(line, 122, 1))[8:]
    row = lax.broadcasted_iota(jnp.int32, (24, 80), 0)
    column = lax.broadcasted_iota(jnp.int32, (24, 80), 1)
    wanted = (row // 8) * 24 + far * 12 + core * 6 + row % 8
    select = jnp.where((column == wanted) & (row % 8 < 6), 1.0, 0.0).astype(BF16)
    for x_hi in range(2):
        for c in range(2):
            for g in range(3):
                rows = mm(select, held[x_hi * 2 + c, g])
                first = c * 1536 + g * 512 + x_hi * 256
                for e in range(2):
                    up_ref[:, e, first : first + 256] = rows[8 * e : 8 * e + 6] * UP_FACTORS[e]
                for n in range(2):
                    at = g * 512 + x_hi * 256 + n * 128
                    kind, within = at // 384, at % 384 + c * 384
                    part = rows[16:22, n * 128 : (n + 1) * 128]
                    if kind < 3:
                        qkv_ref[:, kind * 768 + within : kind * 768 + within + 128] = part
                    else:
                        out_ref[:, within : within + 128] = part
    for g in range(3):
        part = down_ref[g].astype(F32)
        for e in range(2):
            below_ref[e, :, g * 256 : (g + 1) * 256] = part[24 * e : 24 * e + 24] * UP_FACTORS[e]


def assemble(table, *parts):
    return pl.pallas_call(
        assemble_kernel,
        in_specs=[SMALL] + [WHOLE] * 5,
        out_specs=[WHOLE] * 5,
        out_shape=[
            jax.ShapeDtypeStruct((6, 2, 3072), F32),
            jax.ShapeDtypeStruct((6, 2304), F32),
            jax.ShapeDtypeStruct((6, 768), F32),
            jax.ShapeDtypeStruct((8, 128), F32),
            jax.ShapeDtypeStruct((2, 24, 768), F32),
        ],
        scratch_shapes=[pltpu.VMEM((4, 3, 80, 256), BF16)],
        compiler_params=pltpu.CompilerParams(vmem_limit_bytes=4 * 2**20),
        name="assemble",
    )(table, *parts)

def shards(tokens, first_gain, first_shift, w_qkv, w_out, second_gain, second_shift,
           w_up, w_down, modality, segments, partner, cotangent):
    table = lax.dynamic_index_in_dim(
        jnp.asarray(cell_places()), lax.axis_index(BOTH), 0, keepdims=False)
    gains = jnp.stack([first_gain, first_shift, second_gain, second_shift])

    own = marked(partner, tokens[0], segments, modality)
    away = swap_far(own)
    sib = swap_core(own)
    cot_own = cotangent[0]
    cot_sib = swap_core(cot_own)

    act1, marks, queries, k_near, v_near, qx = project(table, own, sib, gains, w_qkv, True)
    away_sib = swap_core(after(away, [qx]))
    act1_away, marks_away, k_away, v_away = project(table, away, away_sib, gains, w_qkv, False)
    attended, lse = attend_forward(
        queries, k_near, k_away, v_near, v_away, qx, marks, marks_away)
    attended_sib = swap_core(attended)

    hidden, grad_act2, xhat2, factor2, act_t, inner_t, grad_pre = experts(
        table, attended, attended_sib, own, sib, cot_own, cot_sib, marks, gains, w_out, w_up, w_down)
    ff_kept, ff_first, more = [], [], [grad_act2]
    for g in range(3):
        keep, gone, *low = cells(g, table, act_t, grad_pre, inner_t, cot_own, cot_sib, marks, more)
        ff_kept.append(keep.reshape(2, 16, 96, 256))
        ff_first.append(send(gone.reshape(2, 16, 96, 256), axis_step(ORDERS[g][0], True)))
        if g == 0:
            grad_sib = swap_core(low[0])
        more = [keep] if g == 0 else [keep, grad_sib]
    hidden_grad, grad_att, proj_half, vectors = middle(
        table, grad_act2, grad_sib, xhat2, factor2, cot_own, cot_sib, gains, w_out)

    def along(stage, first, values):
        return [send(v, axis_step(ORDERS[g][stage], first)) for g, v in enumerate(values)]

    taken = (queries, k_near, k_away, v_near, v_away, grad_att, attended, qx, marks, marks_away, lse)
    q_a, k_a, v_a = attend_backward(taken, 0, 2, ())
    q_b, k_b, v_b = attend_backward(taken, 2, 1, ())
    cells_a = tail_cells(table, act1, act1_away, q_a, q_b, k_a, k_b, v_a)
    partial_own, partial_low, *cells_b = input_partials(table, (
        act1, act1_away, q_a, q_b, k_a, k_b, v_a, v_b, attended, attended_sib, proj_half,
        own, sib, away, away_sib, vectors, w_qkv), ())
    kept = [v.reshape(2, 16, 32, 256) for v in (cells_a[0], cells_a[1], cells_b[0])]
    first = along(0, True, [v.reshape(2, 16, 32, 256) for v in (cells_a[2], cells_a[3], cells_b[1])])
    ff_second = along(0, False, pass_on(ff_kept, ff_first, "pass_first", [cells_b[0]]))
    partial_sib = swap_core(partial_low)
    passed = pass_on(kept, first, "pass_tail")
    second = along(0, False, passed)
    out_own, out_sib = branches(table, inner_t, w_down, hidden, marks, passed)

    kept, sent = settle(
        [list(zip(ff_kept, ff_first, ff_second)), list(zip(kept, first, second))], "settle_all", [out_sib])
    first = along(1, True, sent)
    second = along(1, False, pass_on(kept, first, "pass_second"))
    kept, sent = settle([list(zip(kept, first, second))], "settle_second")
    first = along(2, True, sent)
    from_far = swap_far(sum_core(partial_own, partial_sib, first))
    second = along(2, False, pass_on(kept, first, "pass_third"))
    held, down_held = finish(kept, first, second, [from_far])

    near, beyond = swap_core(held), swap_far(held)
    cross = send(held, lambda x, y, z, c: (x ^ 2, y, z, 1 - c))
    below = send(down_held, lambda x, y, z, c: (x, y, 2 * c + z % 2, z // 2))
    up_grad, qkv_grad, out_grad, line, down_grad = assemble(
        table, held, near, beyond, cross, below)

    token_grad, layer_output = token_grads(
        tokens[0], hidden_grad, partial_own, partial_sib, from_far, gains, out_own, swap_core(out_sib))

    return (
        layer_output[None], token_grad[None], line[0, :6], line[0, 12:18], qkv_grad, out_grad,
        line[0, 24:30], line[0, 36:42], up_grad.transpose(1, 0, 2), down_grad)


def solution(mesh):
    cut = P("rows", "seq", None)
    flat = P(BOTH)
    placed = (cut,) + (P(),) * 8 + (P("rows", "seq"), P("rows", "seq"), P("rows", None), cut)
    return jax.shard_map(
        shards, mesh=mesh, in_specs=placed,
        out_specs=(cut, cut, flat, flat, P(BOTH, None), P(BOTH, None), flat, flat,
                   P(None, BOTH, None), P(None, BOTH, None)),
        check_vma=False)
```

```python
import jax
import jax.numpy as jnp
import numpy as np
from jax import lax
from jax.experimental import pallas as pl
from jax.experimental.pallas import tpu as pltpu
from jax.sharding import PartitionSpec as P

HD = 64
OWN = 6
CORE, FAR = 768, 769
IMG = 197
NIMG = 4
BOTH = ("rows", "seq")
F32 = jnp.float32
BF16 = jnp.bfloat16
MASKED = -1e30


def route(step):
    pairs = []
    for r in range(32):
        z, x_lo, y = r // 8, (r // 4) % 2, r % 4
        for s in range(4):
            x, c = (s // 2) * 2 + x_lo, s % 2
            tx, ty, tz, tc = step(x, y, z, c)
            target = (tz * 8 + (tx % 2) * 4 + ty) * 4 + (tx // 2) * 2 + tc
            pairs.append((r * 4 + s, target))
    return pairs


def send(values, step):
    return lax.ppermute(values, BOTH, route(step))


def swap_core(values):
    return send(values, lambda x, y, z, c: (x, y, z, 1 - c))


def swap_far(values):
    return send(values, lambda x, y, z, c: (x ^ 2, y, z, c))


def axis_step(axis, first):
    def step(x, y, z, c):
        flip = 1 if (c == 0) == first else 3
        at = {"x": x, "y": y, "z": z}
        at[axis] ^= flip
        return (at["x"], at["y"], at["z"], c)

    return step


UP_FACTORS = (1024 / (2 * 788), 1024 / (2 * 236))
ORDERS = (("x", "y", "z"), ("y", "z", "x"), ("z", "x", "y"))


def normalize(inputs):
    centred = inputs - jnp.mean(inputs, axis=-1, keepdims=True)
    factor = lax.rsqrt(jnp.mean(centred * centred, axis=-1, keepdims=True) + 1e-05)
    return centred * factor, factor


def normalize_back(grad, xhat, factor, gain):
    gy = grad * gain
    mean_gy = jnp.mean(gy, axis=-1, keepdims=True)
    mean_gx = jnp.mean(gy * xhat, axis=-1, keepdims=True)
    return factor * (gy - mean_gy - xhat * mean_gx)


SMALL = pl.BlockSpec(memory_space=pltpu.SMEM)
WHOLE = pl.BlockSpec(memory_space=pltpu.VMEM)
N = 256


def marked_kernel(partner, tokens_ref, segments_ref, modality_ref, out_ref):
    segments = segments_ref[...]
    tag = jnp.zeros(segments.shape, jnp.int32)
    for n in range(8):
        tag = jnp.where(segments == n, partner[0, n], tag)
    marks = jnp.concatenate(
        [tag, modality_ref[...], jnp.zeros((1, 256), jnp.int32)], axis=1).astype(F32)
    out_ref[:N, :] = tokens_ref[...]
    out_ref[N:, :] = jnp.concatenate([marks, jnp.zeros((15, 768), F32)], axis=0).astype(BF16)


def marked(partner, tokens, segments, modality):
    return pl.pallas_call(
        marked_kernel,
        in_specs=[SMALL, WHOLE, WHOLE, WHOLE],
        out_specs=WHOLE,
        out_shape=jax.ShapeDtypeStruct((N + 16, 768), BF16),
        compiler_params=pltpu.CompilerParams(vmem_limit_bytes=60 * 2**20),
        name="marked",
    )(partner, tokens, segments, modality)


def mark_lanes(ext):
    row = ext[N:, :].astype(F32)
    place = lax.broadcasted_iota(jnp.int32, (128, N), 0)
    tag = jnp.broadcast_to(row[:1, :N], (128, N))
    kind = jnp.broadcast_to(row[:1, N : 2 * N], (128, N))
    hot = jnp.where((place < NIMG) & (place.astype(F32) == tag), 1.0, 0.0)
    return jnp.transpose(jnp.where(place == 8, kind, hot))


def project_kernel(at_ref, near, a_ref, b_ref, gains_ref, *refs):
    count = 3 if near else 2
    weights, outs = refs[:count], refs[count:]
    for n, ext_ref in enumerate((a_ref, b_ref)):
        rows = slice(n * N, (n + 1) * N)
        ext = ext_ref[...]
        xhat, _ = normalize(ext[:N].astype(F32))
        act = (xhat * gains_ref[0:1, :] + gains_ref[1:2, :]).astype(BF16)
        outs[0][rows, :] = act
        marks = mark_lanes(ext)
        outs[1][rows, :] = marks.astype(BF16)
        for m in range(count):
            part = mm(act, weights[m][...])
            outs[2 + m][rows, :] = (0.125 * part if near and m == 0 else part).astype(BF16)
        if near:
            lane = lax.broadcasted_iota(jnp.int32, marks.shape, 1)
            outs[5][rows, :] = jnp.where((lane < NIMG) & (marks == 0.0), MASKED, 0.0).astype(BF16)


def project(table, first, second, gains, w_qkv, near):
    kinds = (0, 1, 2) if near else (1, 2)
    sizes = [768, 128] + [384] * len(kinds) + ([128] if near else [])
    whole = lambda shape: pl.BlockSpec(shape, lambda i, at: (0, 0))
    return pl.pallas_call(
        lambda at_ref, *refs: project_kernel(at_ref, near, *refs),
        grid_spec=pltpu.PrefetchScalarGridSpec(
            num_scalar_prefetch=1,
            grid=(1,),
            in_specs=[whole((N + 16, 768))] * 2 + [whole((4, 768))]
            + [pl.BlockSpec((768, 384), lambda i, at, n=n: (0, 2 * n + at[CORE])) for n in kinds],
            out_specs=[whole((2 * N, size)) for size in sizes],
        ),
        out_shape=[jax.ShapeDtypeStruct((2 * N, size), BF16) for size in sizes],
        compiler_params=pltpu.CompilerParams(vmem_limit_bytes=6 * 2**20),
        cost_estimate=pl.CostEstimate(
            flops=2 * 512 * 768 * 384 * len(kinds), bytes_accessed=4 * 2**20, transcendentals=0),
        name="project_near" if near else "project_away",
    )(table, first, second, gains, *[w_qkv] * len(kinds))


def middle_kernel(place, grad_ref, sib_ref, xhat_ref, factor_ref, cot_own_ref, cot_sib_ref,
                  gains_ref, w_out_ref, hidden_ref, att_ref, proj_ref, vec_ref):
    core = place[CORE]
    for n, cot_ref in enumerate((cot_own_ref, cot_sib_ref)):
        rows, other = slice(n * N, (n + 1) * N), slice((1 - n) * N, (2 - n) * N)
        grad = grad_ref[rows, :].astype(F32) + sib_ref[other, :].astype(F32)
        xhat = xhat_ref[rows, :].astype(F32)
        total = cot_ref[...].astype(F32) + normalize_back(grad, xhat, factor_ref[rows, :], gains_ref[2:3, :])
        low = total.astype(BF16)
        if n == 0:
            hidden_ref[...] = total
            vec_ref[0:1, :] = jnp.sum(grad * xhat, axis=0, keepdims=True)
            vec_ref[1:2, :] = jnp.sum(grad, axis=0, keepdims=True)
        mine = w_out_ref[pl.ds(pl.multiple_of(core * 384, 384), 384), :]
        att_ref[rows, :] = mm(low, mine, NT).astype(BF16)
        proj_ref[rows, :] = jnp.where(core == 0, low[:, :384], low[:, 384:])


def middle(place, *operands):
    return pl.pallas_call(
        middle_kernel,
        in_specs=[SMALL] + [WHOLE] * len(operands),
        out_specs=[WHOLE] * 4,
        out_shape=[
            jax.ShapeDtypeStruct((N, 768), F32),
            jax.ShapeDtypeStruct((2 * N, 384), BF16),
            jax.ShapeDtypeStruct((2 * N, 384), BF16),
            jax.ShapeDtypeStruct((2, 768), F32),
        ],
        compiler_params=pltpu.CompilerParams(vmem_limit_bytes=6 * 2**20),
        cost_estimate=pl.CostEstimate(
            flops=2 * 512 * 768 * 384, bytes_accessed=8 * 2**20, transcendentals=0),
        name="middle",
    )(place, *operands)


def gelu_parts(pre):
    phi = 0.5 * (1.0 + lax.erf(pre * 0.7071067811865476))
    slope = phi + pre * (0.3989422804014327 * jnp.exp(-0.5 * pre * pre))
    return pre * phi, slope


NT = (((1,), (1,)), ((), ()))
TN = (((0,), (0,)), ((), ()))
NN = (((1,), (0,)), ((), ()))


def mm(left, right, dims=NN):
    return lax.dot_general(left, right, dims, preferred_element_type=F32)


def head_lanes(shape, h):
    lane = lax.broadcasted_iota(jnp.int32, shape, len(shape) - 1)
    return (lane >= HD) == (h == 1)


def turned(values):
    return jnp.transpose(values.astype(F32)).astype(BF16)


def stacked(near_ref, away_ref):
    return jnp.concatenate([near_ref[...], away_ref[...]], axis=0)


def forward_kernel(q_ref, kn_ref, ka_ref, vn_ref, va_ref, qx_ref, xn_ref, xa_ref, out_ref, lse_ref):
    keys = jnp.concatenate([stacked(kn_ref, ka_ref), stacked(xn_ref, xa_ref)], axis=1)
    values = stacked(vn_ref, va_ref)
    q_pair = q_ref[...]
    lanes = head_lanes(q_pair.shape, 0)
    values_t = turned(values)
    value_rows = lax.broadcasted_iota(jnp.int32, values_t.shape, 0) < HD
    mixed = []
    for h in range(2):
        mine = lanes if h == 0 else jnp.logical_not(lanes)
        mine_values = value_rows if h == 0 else jnp.logical_not(value_rows)
        query = jnp.concatenate([jnp.where(mine, q_pair, 0), qx_ref[...]], axis=1)
        scores = mm(keys, query, NT)
        peak = jnp.max(scores, axis=0, keepdims=True)
        weights = jnp.exp(scores - peak).astype(BF16)
        both = mm(jnp.where(mine_values, values_t, 1), weights)
        total = both[127:128, :] if h == 0 else both[0:1, :]
        mixed.append(both * (1.0 / total))
        lse_ref[0, h : h + 1, :] = peak + jnp.log(total)
    out_rows = lax.broadcasted_iota(jnp.int32, mixed[0].shape, 0) < HD
    out_ref[...] = jnp.transpose(jnp.where(out_rows, mixed[0], mixed[1])).astype(BF16)


BY_PAIR = pl.BlockSpec((2 * N, 128), lambda p: (0, p))
FIXED = pl.BlockSpec((2 * N, 128), lambda p: (0, 0))


def attend_forward(*operands):
    return pl.pallas_call(
        forward_kernel,
        grid=(3,),
        in_specs=[BY_PAIR] * 5 + [FIXED] * 3,
        out_specs=[BY_PAIR, pl.BlockSpec((1, 2, 2 * N), lambda p: (p, 0, 0))],
        out_shape=[
            jax.ShapeDtypeStruct((2 * N, 384), BF16),
            jax.ShapeDtypeStruct((3, 2, 2 * N), F32),
        ],
        compiler_params=pltpu.CompilerParams(vmem_limit_bytes=6 * 2**20),
        cost_estimate=pl.CostEstimate(
            flops=2 * 2 * OWN * 512 * 1024 * 256, bytes_accessed=4 * 2**20,
            transcendentals=OWN * 512 * 1024),
        name="attend_forward",
    )(*operands)


def backward_kernel(q_ref, kn_ref, ka_ref, vn_ref, va_ref, do_ref, o_ref, qx_ref, xn_ref, xa_ref,
                    lse_ref, *refs):
    dq_ref, dk_ref, dv_ref = refs[-3:]
    k_pair, values = stacked(kn_ref, ka_ref), stacked(vn_ref, va_ref)
    keys = jnp.concatenate([k_pair, stacked(xn_ref, xa_ref)], axis=1)
    q_pair, grads = q_ref[...], do_ref[...]
    lanes = head_lanes(q_pair.shape, 0)
    product = grads.astype(F32) * o_ref[...].astype(F32)
    k_turned = turned(k_pair)
    rows = lax.broadcasted_iota(jnp.int32, (128, 2 * N), 0) < HD
    dq = jnp.zeros((128, 2 * N), F32)
    dk = jnp.zeros(k_pair.shape, F32)
    dv = jnp.zeros(k_pair.shape, F32)
    for h in range(2):
        mine = lanes if h == 0 else jnp.logical_not(lanes)
        q_head = jnp.where(mine, q_pair, 0)
        g_head = jnp.where(mine, grads, 0)
        dot_row = jnp.transpose(jnp.sum(jnp.where(mine, product, 0.0), axis=1, keepdims=True))
        scores = mm(keys, jnp.concatenate([q_head, qx_ref[...]], axis=1), NT)
        prob = jnp.exp(scores - lse_ref[0, h : h + 1, :])
        dv += mm(prob.astype(BF16), g_head)
        grad_prob = mm(values, g_head, NT)
        grad_scores = (prob * (grad_prob - dot_row)).astype(BF16)
        dk += mm(grad_scores, q_head)
        part = mm(k_turned, grad_scores)
        dq += jnp.where(rows if h == 0 else jnp.logical_not(rows), part, 0.0)
    dq_ref[...] = jnp.transpose(dq).astype(BF16) * jnp.asarray(0.125, BF16)
    dk_ref[...] = dk.astype(BF16)
    dv_ref[...] = dv.astype(BF16)


def attend_backward(operands, first, pairs, gates):
    by_pair = pl.BlockSpec((2 * N, 128), lambda p: (0, first + p))
    sizes = (2 * N, 4 * N, 4 * N)
    return pl.pallas_call(
        backward_kernel,
        grid=(pairs,),
        in_specs=[by_pair] * 7 + [FIXED] * 3
        + [pl.BlockSpec((1, 2, 2 * N), lambda p: (first + p, 0, 0))]
        + [pl.BlockSpec(memory_space=pl.ANY)] * len(gates),
        out_specs=[pl.BlockSpec((size, 128), lambda p: (0, p)) for size in sizes],
        out_shape=[jax.ShapeDtypeStruct((size, pairs * 128), BF16) for size in sizes],
        compiler_params=pltpu.CompilerParams(vmem_limit_bytes=10 * 2**20),
        cost_estimate=pl.CostEstimate(
            flops=2 * 5 * 2 * pairs * 512 * 1024 * 256, bytes_accessed=6 * 2**20,
            transcendentals=2 * pairs * 512 * 1024),
        name="attend_backward",
    )(*operands, *gates)


FF_STEP = 512
E_STEP = 512
EXPERT_MB = 40
CELLS_MB = 28


def expert_kernel(at_ref, att_own_ref, att_sib_ref, own_ref, sib_ref, cot_own_ref, cot_sib_ref,
                  marks_ref, gains_ref, w_out_ref, wu_ref, wd_ref,
                  hidden_ref, low_ref, xhat_ref, factor_ref, act_t_ref, inner_t_ref, slope_ref,
                  act_acc, grad_acc):
    f = pl.program_id(0)
    core = at_ref[CORE]

    @pl.when(f == 0)
    def _():
        mine = w_out_ref[pl.ds(pl.multiple_of(core * 384, 384), 384), :]
        other = w_out_ref[pl.ds(pl.multiple_of((1 - core) * 384, 384), 384), :]
        for n, ext_ref in enumerate((own_ref, sib_ref)):
            rows, theirs = slice(n * N, (n + 1) * N), slice((1 - n) * N, (2 - n) * N)
            hidden = ext_ref[:N, :].astype(F32) + (
                mm(att_own_ref[rows, :], mine) + mm(att_sib_ref[theirs, :], other))
            xhat, factor = normalize(hidden)
            xhat_ref[rows, :] = xhat.astype(BF16)
            factor_ref[rows, :] = factor
            act = xhat * gains_ref[2:3, :] + gains_ref[3:4, :]
            act_acc[rows, :] = act.astype(BF16)
            act_t_ref[:, rows] = jnp.transpose(act).astype(BF16)
            if n == 0:
                hidden_ref[...] = hidden
        grad_acc[...] = jnp.zeros(grad_acc.shape, F32)

    act = act_acc[...]
    cot = jnp.concatenate([cot_own_ref[...], cot_sib_ref[...]], axis=0)
    text = marks_ref[:, 8:9].astype(F32) > 0.0
    pre = jnp.where(text, mm(act, wu_ref[1]), mm(act, wu_ref[0]))
    inner, slope = gelu_parts(pre)
    grad_pre = jnp.where(text, mm(cot, wd_ref[1], NT), mm(cot, wd_ref[0], NT)) * slope
    inner_t_ref[...] = jnp.transpose(inner).astype(BF16)
    low = grad_pre.astype(BF16)
    slope_ref[...] = low
    zero = jnp.zeros((), BF16)
    grad_acc[...] += (mm(jnp.where(text, zero, low), wu_ref[0], NT)
                      + mm(jnp.where(text, low, zero), wu_ref[1], NT))

    @pl.when(f == pl.num_programs(0) - 1)
    def _():
        low_ref[...] = grad_acc[...].astype(BF16)


def experts(core, *operands):
    steps = 1536 // E_STEP
    shapes = [((N, 768), F32), ((2 * N, 768), BF16), ((2 * N, 768), BF16), ((2 * N, 1), F32),
              ((768, 2 * N), BF16)]
    fixed = lambda shape: pl.BlockSpec(shape, lambda f, *_: (0,) * len(shape))
    return pl.pallas_call(
        expert_kernel,
        grid_spec=pltpu.PrefetchScalarGridSpec(
            num_scalar_prefetch=1,
            grid=(steps,),
            in_specs=[fixed(v.shape) for v in operands[:-2]] + [
                pl.BlockSpec((2, 768, E_STEP), lambda f, at: (0, 0, at[CORE] * steps + f)),
                pl.BlockSpec((2, E_STEP, 768), lambda f, at: (0, at[CORE] * steps + f, 0)),
            ],
            out_specs=[fixed(shape) for shape, _ in shapes] + [
                pl.BlockSpec((E_STEP, 2 * N), lambda f, at: (f, 0)),
                pl.BlockSpec((2 * N, E_STEP), lambda f, at: (0, f)),
            ],
            scratch_shapes=[pltpu.VMEM((2 * N, 768), BF16), pltpu.VMEM((2 * N, 768), F32)],
        ),
        out_shape=[jax.ShapeDtypeStruct(*v) for v in shapes] + [
            jax.ShapeDtypeStruct((1536, 2 * N), BF16),
            jax.ShapeDtypeStruct((2 * N, 1536), BF16)],
        compiler_params=pltpu.CompilerParams(
            vmem_limit_bytes=18 * 2**20, dimension_semantics=("arbitrary",)),
        cost_estimate=pl.CostEstimate(
            flops=6 * 2 * 512 * 768 * 1536 + 2 * 512 * 768 * 768, bytes_accessed=22 * 2**20,
            transcendentals=2 * 512 * 1536),
        name="experts",
    )(core, *operands)


def kind_row(marks_ref):
    return turned(marks_ref[...])[8:9, :].astype(F32) > 0.0


def branch_kernel(at_ref, inner_t_ref, wd_ref, hidden_ref, marks_ref, *refs):
    own_ref, sib_ref, acc = refs[-3:]
    f = pl.program_id(0)
    text, inner_t, zero = kind_row(marks_ref), inner_t_ref[...], jnp.zeros((), BF16)
    part = (mm(jnp.where(text, zero, inner_t), wd_ref[0], TN)
            + mm(jnp.where(text, inner_t, zero), wd_ref[1], TN))

    @pl.when(f == 0)
    def _():
        acc[...] = part

    @pl.when(f > 0)
    def _():
        acc[...] += part

    @pl.when(f == pl.num_programs(0) - 1)
    def _():
        own_ref[...] = hidden_ref[...] + acc[:N, :]
        sib_ref[...] = acc[N:, :].astype(BF16)


def branches(table, inner_t, w_down, hidden, marks, gates):
    return pl.pallas_call(
        branch_kernel,
        grid_spec=pltpu.PrefetchScalarGridSpec(
            num_scalar_prefetch=1,
            grid=(3,),
            in_specs=[
                pl.BlockSpec((512, 2 * N), lambda f, at: (f, 0)),
                pl.BlockSpec((2, 512, 768), lambda f, at: (0, at[CORE] * 3 + f, 0)),
                pl.BlockSpec((N, 768), lambda f, at: (0, 0)),
                pl.BlockSpec((2 * N, 128), lambda f, at: (0, 0))] + [ANYWHERE] * len(gates),
            out_specs=[pl.BlockSpec((N, 768), lambda f, at: (0, 0))] * 2,
            scratch_shapes=[pltpu.VMEM((2 * N, 768), F32)],
        ),
        out_shape=[jax.ShapeDtypeStruct((N, 768), F32), jax.ShapeDtypeStruct((N, 768), BF16)],
        compiler_params=pltpu.CompilerParams(
            vmem_limit_bytes=20 * 2**20, dimension_semantics=("arbitrary",)),
        cost_estimate=pl.CostEstimate(
            flops=2 * 2 * 512 * 768 * 1536, bytes_accessed=8 * 2**20, transcendentals=0),
        name="branches",
    )(table, inner_t, w_down, hidden, marks, *gates)


def cells_kernel(g, at_slot, act_t_ref, grad_ref, inner_t_ref, cot_own_ref, cot_sib_ref, marks_ref,
                 *refs):
    if g == 0:
        full_ref, keep_ref, send_ref, low_ref, up_acc, down_acc = refs
        low_ref[...] = full_ref[...]
    else:
        keep_ref, send_ref, up_acc, down_acc = refs[-4:]
    zero = jnp.zeros((), BF16)
    text, text_row = marks_ref[:, 8:9].astype(F32) > 0.0, kind_row(marks_ref)
    act_t, inner_t = act_t_ref[...], inner_t_ref[...]
    grad = grad_ref[:, g * FF_STEP : (g + 1) * FF_STEP]
    lanes = slice(g * 256, (g + 1) * 256)
    cot = jnp.concatenate([cot_own_ref[:, lanes], cot_sib_ref[:, lanes]], axis=0)
    for e in range(2):
        up = mm(act_t, jnp.where(text, grad, zero) if e else jnp.where(text, zero, grad))
        up_acc[e, 0] = up[:, :256]
        up_acc[e, 1] = up[:, 256:]
        down_acc[e] = mm(
            jnp.where(text_row, inner_t, zero) if e else jnp.where(text_row, zero, inner_t), cot)

    for n, target in enumerate((keep_ref, send_ref)):
        def cell(i, carry):
            slot = g * 64 + n * 32 + i
            half = at_slot[192 + slot]
            rows = pl.ds(pl.multiple_of(at_slot[slot], 8), 24)
            below = pl.ds(pl.multiple_of(at_slot[384 + slot], 8), 24)
            target[i] = jnp.concatenate(
                [up_acc[0, half, rows, :], up_acc[1, half, rows, :],
                 down_acc[0, below, :], down_acc[1, below, :]], axis=0).astype(BF16)
            return carry
        lax.fori_loop(0, 32, cell, 0, unroll=4)


def cells(g, table, act_t, grad_pre, inner_t, cot_own, cot_sib, marks, more):
    return pl.pallas_call(
        lambda *refs: cells_kernel(g, *refs),
        in_specs=[SMALL] + [WHOLE] * 6 + ([WHOLE] if g == 0 else [ANYWHERE] * len(more)),
        out_specs=[WHOLE] * (3 if g == 0 else 2),
        out_shape=[jax.ShapeDtypeStruct((32, 96, 256), BF16)] * 2
        + [jax.ShapeDtypeStruct((2 * N, 768), BF16)] * (g == 0),
        scratch_shapes=[pltpu.VMEM((2, 2, 768, 256), F32), pltpu.VMEM((2, 1536, 256), F32)],
        compiler_params=pltpu.CompilerParams(vmem_limit_bytes=10 * 2**20),
        cost_estimate=pl.CostEstimate(
            flops=4 * 2 * 512 * 768 * 512, bytes_accessed=8 * 2**20, transcendentals=0),
        name="cells",
    )(table, act_t, grad_pre, inner_t, cot_own, cot_sib, marks, *more)


def cell_places():
    table = np.zeros((32, 4, 4, 3, 4, 4, 4), np.int32)
    for r, s in np.ndindex(32, 4):
        here = {"z": r // 8, "y": r % 4, "x": (s // 2) * 2 + (r // 4) % 2}
        flips = (0, 1, 3, 2) if s % 2 else (0, 3, 1, 2)
        for g, order in enumerate(ORDERS):
            for slot in np.ndindex(4, 4, 4):
                at = {a: here[a] ^ flips[n] for a, n in zip(order, slot)}
                x_hi, x_lo = at["x"] // 2, at["x"] % 2
                table[(r, s, 0, g) + slot] = 24 * (at["z"] * 8 + x_lo * 4 + at["y"])
                table[(r, s, 1, g) + slot] = x_hi
                table[(r, s, 2, g) + slot] = 24 * (
                    (at["z"] % 2) * 32 + x_lo * 16 + at["y"] * 4 + x_hi * 2 + at["z"] // 2)
                table[(r, s, 3, g) + slot] = at["z"] * 16 + x_lo * 8 + at["y"] * 2 + x_hi
    coordinates = np.array([[n % 2, n % 4 // 2] + [0] * 126 for n in range(128)], np.int32)
    return np.concatenate([table.reshape(128, 768), coordinates], axis=1)


def add_up(parts):
    total = parts[0].astype(F32)
    for part in parts[1:]:
        total = total + part.astype(F32)
    return total.astype(BF16)


def in_hbm(values):
    return list(values)


def pass_kernel(gates, *refs):
    count = (len(refs) - gates) // 3
    for g in range(count):
        refs[2 * count + gates + g][...] = add_up([refs[2 * g][...], refs[2 * g + 1][...]])


ANYWHERE = pl.BlockSpec(memory_space=pl.ANY)


def pass_on(kept, arrived, name, gates=()):
    _, slots, rows, lanes = kept[0].shape
    block = max(slots // 4, 1)
    one = pl.BlockSpec((None, block, rows, lanes), lambda i: (1, i, 0, 0))
    return pl.pallas_call(
        lambda *refs: pass_kernel(len(gates), *refs),
        grid=(slots // block,),
        in_specs=[one] * (2 * len(kept)) + [ANYWHERE] * len(gates),
        out_specs=[pl.BlockSpec((block, rows, lanes), lambda i: (i, 0, 0))] * len(kept),
        out_shape=[jax.ShapeDtypeStruct((slots, rows, lanes), BF16)] * len(kept),
        compiler_params=pltpu.CompilerParams(vmem_limit_bytes=6 * 2**20),
        cost_estimate=pl.CostEstimate(
            flops=0, transcendentals=0, bytes_accessed=6 * len(kept) * slots * rows * lanes),
        name=name,
    )(*in_hbm([v for pair in zip(kept, arrived) for v in pair]), *gates)


def settle_kernel(groups, sizes, *refs):
    ins, outs = refs, refs[-2 * groups :]
    at = 0
    for g in range(groups):
        row = 0
        for size in sizes:
            for half in range(2):
                outs[2 * g + half][:, row : row + size, :] = add_up(
                    [ins[at + k][...] for k in range(3)])
                at += 3
            row += size


def settle(pieces, name, gates=()):
    groups = len(pieces[0])
    sizes = [p[0][0].shape[2] for p in pieces]
    _, slots, _, lanes = pieces[0][0][0].shape
    half = slots // 2
    block = max(half // 4, 1)
    steps = half // block
    operands, specs = [], []
    for g in range(groups):
        for p, size in zip(pieces, sizes):
            for h in range(2):
                wide = pl.BlockSpec(
                    (None, block, size, lanes), lambda i, h=h: (0, i + h * steps, 0, 0))
                flat = pl.BlockSpec((block, size, lanes), lambda i, h=h: (i + h * steps, 0, 0))
                operands += list(p[g])
                specs += [wide, wide, flat]
    rows = sum(sizes)
    outs = pl.pallas_call(
        lambda *refs: settle_kernel(groups, sizes, *refs),
        grid=(steps,),
        in_specs=specs + [ANYWHERE] * len(gates),
        out_specs=[pl.BlockSpec((block, rows, lanes), lambda i: (i, 0, 0))] * (2 * groups),
        out_shape=[jax.ShapeDtypeStruct((half, rows, lanes), BF16)] * (2 * groups),
        compiler_params=pltpu.CompilerParams(vmem_limit_bytes=8 * 2**20),
        cost_estimate=pl.CostEstimate(
            flops=0, transcendentals=0, bytes_accessed=8 * groups * slots * rows * lanes),
        name=name,
    )(*operands, *gates)
    shaped = [o.reshape(2, half // 2, rows, lanes) for o in outs]
    return shaped[0::2], shaped[1::2]


def finish_kernel(count, at_ref, *refs):
    outs, down_ref = refs[-5:-1], refs[-1]
    core, far = at_ref[CORE], at_ref[FAR]
    row = lax.broadcasted_iota(jnp.int32, (24, 80), 0)
    column = lax.broadcasted_iota(jnp.int32, (24, 80), 1)
    picks = []
    for n in range(4):
        x_hi, c = far ^ (n // 2), core ^ (n % 2)
        wanted = jnp.where(row == 6, 72, (row // 8) * 24 + x_hi * 12 + c * 6 + row % 8)
        picks.append(jnp.where((column == wanted) & (row % 8 < 6 + (row == 6)), 1.0, 0.0).astype(BF16))
    for g in range(3):
        cell = add_up([refs[3 * g + k][...] for k in range(3)])
        shared = jnp.concatenate([cell[:48], cell[96:]], axis=0)
        for out, pick in zip(outs, picks):
            out[g] = mm(pick, shared).astype(BF16)
        down_ref[g] = cell[48:96]


def finish(table, kept, first, second, gates):
    wide = pl.BlockSpec((None, None, 128, 256), lambda i, t: (0, 0, 0, 0))
    flat = pl.BlockSpec((None, 128, 256), lambda i, t: (0, 0, 0))
    sizes = [24] * 4 + [48]
    return pl.pallas_call(
        lambda *refs: finish_kernel(9, *refs),
        grid_spec=pltpu.PrefetchScalarGridSpec(
            num_scalar_prefetch=1,
            grid=(1,),
            in_specs=[wide, wide, flat] * 3 + [ANYWHERE] * len(gates),
            out_specs=[pl.BlockSpec((3, size, 256), lambda i, t: (0, 0, 0)) for size in sizes],
        ),
        out_shape=[jax.ShapeDtypeStruct((3, size, 256), BF16) for size in sizes],
        compiler_params=pltpu.CompilerParams(vmem_limit_bytes=4 * 2**20),
        name="finish",
    )(table, *[v for g in range(3) for v in (kept[g], first[g], second[g])], *gates)


def after_kernel(values_ref, *refs):
    refs[-1][...] = values_ref[...]


def after(values, gates):
    return pl.pallas_call(
        after_kernel,
        in_specs=[WHOLE] + [ANYWHERE] * len(gates),
        out_specs=WHOLE,
        out_shape=jax.ShapeDtypeStruct(values.shape, values.dtype),
        compiler_params=pltpu.CompilerParams(vmem_limit_bytes=4 * 2**20),
        name="after",
    )(values, *gates)


def put(acc, first, part, rows=slice(None)):
    for n in range(part.shape[1] // 128):
        column = first + n * 128
        lanes = slice(column % 256, column % 256 + 128)
        acc[column // 256, rows, lanes] = part[:, n * 128 : (n + 1) * 128]


def spill_rows(target, acc, at_slot, g, base, extra):
    def cell(i, carry):
        slot = g * 64 + base + i
        rows = pl.ds(pl.multiple_of(at_slot[slot], 8), 24)
        part = acc[at_slot[192 + slot] + 2 * (g % 2), rows, :]
        target[i] = jnp.concatenate([part, extra(slot)], axis=0).astype(BF16)
        return carry
    lax.fori_loop(0, 32, cell, 0, unroll=4)


def tail_kernel(at_slot, act_ref, away_ref, q_ref, qb_ref, ka_ref, kb_ref, va_ref, *refs):
    keeps, sends, acc = refs[-5:-3], refs[-3:-1], refs[-1]
    act, away = act_ref[...], away_ref[...]
    near = mm(act, jnp.concatenate(
        [r[: 2 * N, :] for r in (q_ref, qb_ref, ka_ref, kb_ref, va_ref)], axis=1), TN)
    far = mm(away, jnp.concatenate(
        [r[2 * N :, :] for r in (ka_ref, kb_ref, va_ref)], axis=1), TN)
    put(acc, 0, near[:, :384])
    put(acc, 384, near[:, 384:] + far)
    for g in range(2):
        blank = lambda slot: jnp.zeros((8, 256), F32)
        spill_rows(keeps[g], acc, at_slot, g, 0, blank)
        spill_rows(sends[g], acc, at_slot, g, 32, blank)


def tail_cells(table, *operands):
    return pl.pallas_call(
        tail_kernel,
        in_specs=[SMALL] + [WHOLE] * len(operands),
        out_specs=[WHOLE] * 4,
        out_shape=[jax.ShapeDtypeStruct((32, 32, 256), BF16)] * 4,
        scratch_shapes=[pltpu.VMEM((4, 768, 256), F32)],
        compiler_params=pltpu.CompilerParams(vmem_limit_bytes=14 * 2**20),
        cost_estimate=pl.CostEstimate(
            flops=2 * 768 * 512 * (1024 + 640), bytes_accessed=8 * 2**20, transcendentals=0),
        name="tail_cells",
    )(table, *operands)


def inputs_kernel(at_slot, act_ref, away_ref, q_ref, qb_ref, ka_ref, kb_ref, va_ref, vb_ref,
                  att_own_ref, att_sib_ref, proj_ref, own_ref, sib_ref, far_ref, far_sib_ref,
                  second_ref, *refs):
    weights = refs[:3]
    keep_ref, send_ref, cell_keep, cell_send, acc, table = refs[-6:]
    core = at_slot[CORE]
    put(acc, 0, mm(act_ref[...], vb_ref[: 2 * N, :], TN) + mm(away_ref[...], vb_ref[2 * N :, :], TN))
    mine = pl.ds(pl.multiple_of(core * 384, 384), 384)
    other = pl.ds(pl.multiple_of((1 - core) * 384, 384), 384)
    put(acc, 128, mm(att_own_ref[...], proj_ref[...], TN), mine)
    put(acc, 128, mm(att_sib_ref[:N, :], proj_ref[N:, :], TN)
        + mm(att_sib_ref[N:, :], proj_ref[:N, :], TN), other)

    vectors = [jnp.zeros((1, 768), F32)] * 2 + [second_ref[0:1, :], second_ref[1:2, :]]
    wide = list(zip((q_ref, ka_ref, va_ref), (qb_ref, kb_ref, vb_ref), weights))
    for n, ext_ref in enumerate((own_ref, sib_ref, far_ref, far_sib_ref)):
        rows = slice(n * N, (n + 1) * N)
        total = jnp.zeros((N, 768), F32)
        for a_ref, b_ref, w_ref in wide[0 if n < 2 else 1 :]:
            grads = jnp.concatenate([a_ref[rows, :], b_ref[rows, :]], axis=1)
            total += mm(grads, w_ref[...], NT)
        xhat, _ = normalize(ext_ref[:N, :].astype(F32))
        vectors[0] += jnp.sum(total * xhat, axis=0, keepdims=True)
        vectors[1] += jnp.sum(total, axis=0, keepdims=True)
        half = slice((n // 2) * N, (n // 2 + 1) * N)
        if n % 2 == 0:
            keep_ref[half, :] = total
        else:
            send_ref[half, :] = total.astype(BF16)

    chip = lax.broadcasted_iota(jnp.int32, (64, 768), 0)
    owner = lax.broadcasted_iota(jnp.int32, (64, 768), 1) // 12
    feature = lax.broadcasted_iota(jnp.int32, (768, 128), 0) % 12
    lane = lax.broadcasted_iota(jnp.int32, (768, 128), 1)
    spread = jnp.zeros((64, 128), F32)
    for n in range(4):
        line = jnp.broadcast_to(vectors[n], (64, 768))
        values = jnp.where(chip == owner, line, 0.0).astype(BF16)
        spread += mm(values, jnp.where(lane == feature + 12 * n, 1.0, 0.0).astype(BF16))
    table[...] = spread

    def lines(slot):
        row = table[pl.ds(at_slot[576 + slot], 1), :]
        return jnp.concatenate(
            [jnp.broadcast_to(row, (8, 128)), jnp.zeros((8, 128), F32)], axis=1)

    spill_rows(cell_keep, acc, at_slot, 2, 0, lines)
    spill_rows(cell_send, acc, at_slot, 2, 32, lines)


def input_partials(table, operands, gates):
    whole = lambda shape: pl.BlockSpec(shape, lambda i, *_: (0,) * len(shape))
    shapes = [((2 * N, 768), F32), ((2 * N, 768), BF16)] + [((32, 32, 256), BF16)] * 2
    return pl.pallas_call(
        inputs_kernel,
        grid_spec=pltpu.PrefetchScalarGridSpec(
            num_scalar_prefetch=1,
            grid=(1,),
            in_specs=[whole(v.shape) for v in operands[:-1]]
            + [pl.BlockSpec((768, 384), lambda i, at, n=n: (0, 2 * n + at[CORE])) for n in range(3)]
            + [ANYWHERE] * len(gates),
            out_specs=[whole(shape) for shape, _ in shapes],
            scratch_shapes=[pltpu.VMEM((2, 768, 256), F32), pltpu.VMEM((64, 128), F32)],
        ),
        out_shape=[jax.ShapeDtypeStruct(*v) for v in shapes],
        compiler_params=pltpu.CompilerParams(vmem_limit_bytes=16 * 2**20),
        cost_estimate=pl.CostEstimate(
            flops=2 * 768 * 384 * 512 * 7, bytes_accessed=10 * 2**20, transcendentals=0),
        name="input_partials",
    )(table, *operands, *[operands[-1]] * 2, *gates)


def sum_core_kernel(own_ref, sib_ref, *refs):
    refs[-1][...] = (own_ref[...] + sib_ref[...].astype(F32)).astype(BF16)


def sum_core(own, sib, gates):
    half = pl.BlockSpec((N, 768), lambda i: (1, 0))
    return pl.pallas_call(
        sum_core_kernel,
        grid=(1,),
        in_specs=[half, half] + [ANYWHERE] * len(gates),
        out_specs=pl.BlockSpec((N, 768), lambda i: (0, 0)),
        out_shape=jax.ShapeDtypeStruct((N, 768), BF16),
        compiler_params=pltpu.CompilerParams(vmem_limit_bytes=4 * 2**20),
        name="sum_core",
    )(own, sib, *gates)


def token_kernel(tokens_ref, hidden_ref, own_ref, sib_ref, far_ref, gains_ref, out_own_ref,
                 out_sib_ref, grad_ref, out_ref):
    grad = own_ref[...] + sib_ref[...].astype(F32) + far_ref[...].astype(F32)
    xhat, factor = normalize(tokens_ref[...].astype(F32))
    grad_ref[...] = hidden_ref[...] + normalize_back(grad, xhat, factor, gains_ref[0:1, :])
    out_ref[...] = (out_own_ref[...] + out_sib_ref[...].astype(F32)).astype(BF16)


def token_grads(tokens, hidden, own, sib, far, gains, out_own, out_sib):
    half = pl.BlockSpec((N, 768), lambda i: (0, 0))
    return pl.pallas_call(
        token_kernel,
        grid=(1,),
        in_specs=[half] * 5 + [pl.BlockSpec((4, 768), lambda i: (0, 0))] + [half] * 2,
        out_specs=[half] * 2,
        out_shape=[jax.ShapeDtypeStruct((N, 768), F32), jax.ShapeDtypeStruct((N, 768), BF16)],
        compiler_params=pltpu.CompilerParams(vmem_limit_bytes=8 * 2**20),
        name="token_grads",
    )(tokens, hidden, own, sib, far, gains, out_own, out_sib)


def assemble_kernel(at_ref, own_ref, near_ref, away_ref, cross_ref, down_ref, up_ref, qkv_ref, out_ref,
                    vec_ref, below_ref, held):
    core, far = at_ref[CORE], at_ref[FAR]
    held[far * 2 + core] = own_ref[...]
    held[far * 2 + 1 - core] = near_ref[...]
    held[2 - far * 2 + core] = away_ref[...]
    held[2 - far * 2 + 1 - core] = cross_ref[...]
    line = own_ref[2, :8, :128].astype(F32) + near_ref[2, :8, :128].astype(F32)
    vec_ref[...] = jnp.where(core == 0, line, pltpu.roll(line, 122, 1))
    for x_hi in range(2):
        for c in range(2):
            for g in range(3):
                rows = held[x_hi * 2 + c, g].astype(F32)
                first = c * 1536 + g * 512 + x_hi * 256
                for e in range(2):
                    up_ref[:, e, first : first + 256] = rows[8 * e : 8 * e + 6] * UP_FACTORS[e]
                for n in range(2):
                    at = g * 512 + x_hi * 256 + n * 128
                    kind, within = at // 384, at % 384 + c * 384
                    part = rows[16:22, n * 128 : (n + 1) * 128]
                    if kind < 3:
                        qkv_ref[:, kind * 768 + within : kind * 768 + within + 128] = part
                    else:
                        out_ref[:, within : within + 128] = part
    for g in range(3):
        part = down_ref[g].astype(F32)
        for e in range(2):
            below_ref[e, :, g * 256 : (g + 1) * 256] = part[24 * e : 24 * e + 24] * UP_FACTORS[e]


def assemble(table, *parts):
    return pl.pallas_call(
        assemble_kernel,
        in_specs=[SMALL] + [WHOLE] * 5,
        out_specs=[WHOLE] * 5,
        out_shape=[
            jax.ShapeDtypeStruct((6, 2, 3072), F32),
            jax.ShapeDtypeStruct((6, 2304), F32),
            jax.ShapeDtypeStruct((6, 768), F32),
            jax.ShapeDtypeStruct((8, 128), F32),
            jax.ShapeDtypeStruct((2, 24, 768), F32),
        ],
        scratch_shapes=[pltpu.VMEM((4, 3, 24, 256), BF16)],
        compiler_params=pltpu.CompilerParams(vmem_limit_bytes=4 * 2**20),
        name="assemble",
    )(table, *parts)

def shards(tokens, first_gain, first_shift, w_qkv, w_out, second_gain, second_shift,
           w_up, w_down, modality, segments, partner, cotangent):
    table = lax.dynamic_index_in_dim(
        jnp.asarray(cell_places()), lax.axis_index(BOTH), 0, keepdims=False)
    gains = jnp.stack([first_gain, first_shift, second_gain, second_shift])

    own = marked(partner, tokens[0], segments, modality)
    away = swap_far(own)
    sib = swap_core(own)
    cot_own = cotangent[0]
    cot_sib = swap_core(cot_own)

    act1, marks, queries, k_near, v_near, qx = project(table, own, sib, gains, w_qkv, True)
    away_sib = swap_core(after(away, [qx]))
    act1_away, marks_away, k_away, v_away = project(table, away, away_sib, gains, w_qkv, False)
    attended, lse = attend_forward(
        queries, k_near, k_away, v_near, v_away, qx, marks, marks_away)
    attended_sib = swap_core(attended)

    hidden, grad_act2, xhat2, factor2, act_t, inner_t, grad_pre = experts(
        table, attended, attended_sib, own, sib, cot_own, cot_sib, marks, gains, w_out, w_up, w_down)
    ff_kept, ff_first, more = [], [], [grad_act2]
    for g in range(3):
        keep, gone, *low = cells(g, table, act_t, grad_pre, inner_t, cot_own, cot_sib, marks, more)
        ff_kept.append(keep.reshape(2, 16, 96, 256))
        ff_first.append(send(gone.reshape(2, 16, 96, 256), axis_step(ORDERS[g][0], True)))
        if g == 0:
            grad_sib = swap_core(low[0])
        more = [keep] if g == 0 else [keep, grad_sib]
    hidden_grad, grad_att, proj_half, vectors = middle(
        table, grad_act2, grad_sib, xhat2, factor2, cot_own, cot_sib, gains, w_out)

    def along(stage, first, values):
        return [send(v, axis_step(ORDERS[g][stage], first)) for g, v in enumerate(values)]

    taken = (queries, k_near, k_away, v_near, v_away, grad_att, attended, qx, marks, marks_away, lse)
    q_a, k_a, v_a = attend_backward(taken, 0, 2, ())
    q_b, k_b, v_b = attend_backward(taken, 2, 1, ())
    cells_a = tail_cells(table, act1, act1_away, q_a, q_b, k_a, k_b, v_a)
    partial_own, partial_low, *cells_b = input_partials(table, (
        act1, act1_away, q_a, q_b, k_a, k_b, v_a, v_b, attended, attended_sib, proj_half,
        own, sib, away, away_sib, vectors, w_qkv), ())
    kept = [v.reshape(2, 16, 32, 256) for v in (cells_a[0], cells_a[1], cells_b[0])]
    first = along(0, True, [v.reshape(2, 16, 32, 256) for v in (cells_a[2], cells_a[3], cells_b[1])])
    ff_second = along(0, False, pass_on(ff_kept, ff_first, "pass_first", [cells_b[0]]))
    partial_sib = swap_core(partial_low)
    passed = pass_on(kept, first, "pass_tail")
    second = along(0, False, passed)
    out_own, out_sib = branches(table, inner_t, w_down, hidden, marks, passed)

    kept, sent = settle(
        [list(zip(ff_kept, ff_first, ff_second)), list(zip(kept, first, second))], "settle_all", [out_sib])
    first = along(1, True, sent)
    second = along(1, False, pass_on(kept, first, "pass_second"))
    kept, sent = settle([list(zip(kept, first, second))], "settle_second")
    first = along(2, True, sent)
    from_far = swap_far(sum_core(partial_own, partial_sib, first))
    second = along(2, False, pass_on(kept, first, "pass_third"))
    held, *shares, down_held = finish(table, kept, first, second, [from_far])

    near, beyond = swap_core(shares[0]), swap_far(shares[1])
    cross = send(shares[2], lambda x, y, z, c: (x ^ 2, y, z, 1 - c))
    below = send(down_held, lambda x, y, z, c: (x, y, 2 * c + z % 2, z // 2))
    up_grad, qkv_grad, out_grad, line, down_grad = assemble(
        table, held, near, beyond, cross, below)

    token_grad, layer_output = token_grads(
        tokens[0], hidden_grad, partial_own, partial_sib, from_far, gains, out_own, swap_core(out_sib))

    return (
        layer_output[None], token_grad[None], line[6, :6], line[6, 12:18], qkv_grad, out_grad,
        line[6, 24:30], line[6, 36:42], up_grad.transpose(1, 0, 2), down_grad)


def solution(mesh):
    cut = P("rows", "seq", None)
    flat = P(BOTH)
    placed = (cut,) + (P(),) * 8 + (P("rows", "seq"), P("rows", "seq"), P("rows", None), cut)
    return jax.shard_map(
        shards, mesh=mesh, in_specs=placed,
        out_specs=(cut, cut, flat, flat, P(BOTH, None), P(BOTH, None), flat, flat,
                   P(None, BOTH, None), P(None, BOTH, None)),
        check_vma=False)
```

```python
import jax
import jax.numpy as jnp
import numpy as np
from jax import lax
from jax.experimental import pallas as pl
from jax.experimental.pallas import tpu as pltpu
from jax.sharding import PartitionSpec as P

HD = 64
OWN = 6
CORE, FAR = 768, 769
IMG = 197
NIMG = 4
BOTH = ("rows", "seq")
F32 = jnp.float32
BF16 = jnp.bfloat16
MASKED = -1e30


def route(step):
    pairs = []
    for r in range(32):
        z, x_lo, y = r // 8, (r // 4) % 2, r % 4
        for s in range(4):
            x, c = (s // 2) * 2 + x_lo, s % 2
            tx, ty, tz, tc = step(x, y, z, c)
            target = (tz * 8 + (tx % 2) * 4 + ty) * 4 + (tx // 2) * 2 + tc
            pairs.append((r * 4 + s, target))
    return pairs


def send(values, step):
    return lax.ppermute(values, BOTH, route(step))


def swap_core(values):
    return send(values, lambda x, y, z, c: (x, y, z, 1 - c))


def swap_far(values):
    return send(values, lambda x, y, z, c: (x ^ 2, y, z, c))


def axis_step(axis, first):
    def step(x, y, z, c):
        flip = 1 if (c == 0) == first else 3
        at = {"x": x, "y": y, "z": z}
        at[axis] ^= flip
        return (at["x"], at["y"], at["z"], c)

    return step


UP_FACTORS = (1024 / (2 * 788), 1024 / (2 * 236))
ORDERS = (("x", "y", "z"), ("y", "z", "x"), ("z", "x", "y"))


def normalize(inputs):
    centred = inputs - jnp.mean(inputs, axis=-1, keepdims=True)
    factor = lax.rsqrt(jnp.mean(centred * centred, axis=-1, keepdims=True) + 1e-05)
    return centred * factor, factor


def normalize_back(grad, xhat, factor, gain):
    gy = grad * gain
    mean_gy = jnp.mean(gy, axis=-1, keepdims=True)
    mean_gx = jnp.mean(gy * xhat, axis=-1, keepdims=True)
    return factor * (gy - mean_gy - xhat * mean_gx)


SMALL = pl.BlockSpec(memory_space=pltpu.SMEM)
WHOLE = pl.BlockSpec(memory_space=pltpu.VMEM)
N = 256


def marked_kernel(partner, tokens_ref, segments_ref, modality_ref, out_ref):
    segments = segments_ref[...]
    tag = jnp.zeros(segments.shape, jnp.int32)
    for n in range(8):
        tag = jnp.where(segments == n, partner[0, n], tag)
    marks = jnp.concatenate(
        [tag, modality_ref[...], jnp.zeros((1, 256), jnp.int32)], axis=1).astype(F32)
    out_ref[:N, :] = tokens_ref[...]
    out_ref[N:, :] = jnp.concatenate([marks, jnp.zeros((15, 768), F32)], axis=0).astype(BF16)


def marked(partner, tokens, segments, modality):
    return pl.pallas_call(
        marked_kernel,
        in_specs=[SMALL, WHOLE, WHOLE, WHOLE],
        out_specs=WHOLE,
        out_shape=jax.ShapeDtypeStruct((N + 16, 768), BF16),
        compiler_params=pltpu.CompilerParams(vmem_limit_bytes=60 * 2**20),
        name="marked",
    )(partner, tokens, segments, modality)


def mark_lanes(ext):
    row = ext[N:, :].astype(F32)
    place = lax.broadcasted_iota(jnp.int32, (128, N), 0)
    tag = jnp.broadcast_to(row[:1, :N], (128, N))
    kind = jnp.broadcast_to(row[:1, N : 2 * N], (128, N))
    hot = jnp.where((place < NIMG) & (place.astype(F32) == tag), 1.0, 0.0)
    return jnp.transpose(jnp.where(place == 8, kind, hot))


def project_kernel(at_ref, near, a_ref, b_ref, gains_ref, *refs):
    count = 3 if near else 2
    weights, outs = refs[:count], refs[count:]
    for n, ext_ref in enumerate((a_ref, b_ref)):
        rows = slice(n * N, (n + 1) * N)
        ext = ext_ref[...]
        xhat, _ = normalize(ext[:N].astype(F32))
        act = (xhat * gains_ref[0:1, :] + gains_ref[1:2, :]).astype(BF16)
        outs[0][rows, :] = act
        marks = mark_lanes(ext)
        outs[1][rows, :] = marks.astype(BF16)
        for m in range(count):
            part = mm(act, weights[m][...])
            outs[2 + m][rows, :] = (0.125 * part if near and m == 0 else part).astype(BF16)
        if near:
            lane = lax.broadcasted_iota(jnp.int32, marks.shape, 1)
            outs[5][rows, :] = jnp.where((lane < NIMG) & (marks == 0.0), MASKED, 0.0).astype(BF16)


def project(table, first, second, gains, w_qkv, near):
    kinds = (0, 1, 2) if near else (1, 2)
    sizes = [768, 128] + [384] * len(kinds) + ([128] if near else [])
    whole = lambda shape: pl.BlockSpec(shape, lambda i, at: (0, 0))
    return pl.pallas_call(
        lambda at_ref, *refs: project_kernel(at_ref, near, *refs),
        grid_spec=pltpu.PrefetchScalarGridSpec(
            num_scalar_prefetch=1,
            grid=(1,),
            in_specs=[whole((N + 16, 768))] * 2 + [whole((4, 768))]
            + [pl.BlockSpec((768, 384), lambda i, at, n=n: (0, 2 * n + at[CORE])) for n in kinds],
            out_specs=[whole((2 * N, size)) for size in sizes],
        ),
        out_shape=[jax.ShapeDtypeStruct((2 * N, size), BF16) for size in sizes],
        compiler_params=pltpu.CompilerParams(vmem_limit_bytes=6 * 2**20),
        cost_estimate=pl.CostEstimate(
            flops=2 * 512 * 768 * 384 * len(kinds), bytes_accessed=4 * 2**20, transcendentals=0),
        name="project_near" if near else "project_away",
    )(table, first, second, gains, *[w_qkv] * len(kinds))


def middle_kernel(place, grad_ref, sib_ref, xhat_ref, factor_ref, cot_own_ref, cot_sib_ref,
                  gains_ref, w_out_ref, hidden_ref, att_ref, proj_ref, vec_ref):
    core = place[CORE]
    for n, cot_ref in enumerate((cot_own_ref, cot_sib_ref)):
        rows, other = slice(n * N, (n + 1) * N), slice((1 - n) * N, (2 - n) * N)
        grad = grad_ref[rows, :].astype(F32) + sib_ref[other, :].astype(F32)
        xhat = xhat_ref[rows, :].astype(F32)
        total = cot_ref[...].astype(F32) + normalize_back(grad, xhat, factor_ref[rows, :], gains_ref[2:3, :])
        low = total.astype(BF16)
        if n == 0:
            hidden_ref[...] = total
            vec_ref[0:1, :] = jnp.sum(grad * xhat, axis=0, keepdims=True)
            vec_ref[1:2, :] = jnp.sum(grad, axis=0, keepdims=True)
        mine = w_out_ref[pl.ds(pl.multiple_of(core * 384, 384), 384), :]
        att_ref[rows, :] = mm(low, mine, NT).astype(BF16)
        proj_ref[rows, :] = jnp.where(core == 0, low[:, :384], low[:, 384:])


def middle(place, *operands):
    return pl.pallas_call(
        middle_kernel,
        in_specs=[SMALL] + [WHOLE] * len(operands),
        out_specs=[WHOLE] * 4,
        out_shape=[
            jax.ShapeDtypeStruct((N, 768), F32),
            jax.ShapeDtypeStruct((2 * N, 384), BF16),
            jax.ShapeDtypeStruct((2 * N, 384), BF16),
            jax.ShapeDtypeStruct((2, 768), F32),
        ],
        compiler_params=pltpu.CompilerParams(vmem_limit_bytes=6 * 2**20),
        cost_estimate=pl.CostEstimate(
            flops=2 * 512 * 768 * 384, bytes_accessed=8 * 2**20, transcendentals=0),
        name="middle",
    )(place, *operands)


def gelu_parts(pre):
    phi = 0.5 * (1.0 + lax.erf(pre * 0.7071067811865476))
    slope = phi + pre * (0.3989422804014327 * jnp.exp(-0.5 * pre * pre))
    return pre * phi, slope


NT = (((1,), (1,)), ((), ()))
TN = (((0,), (0,)), ((), ()))
NN = (((1,), (0,)), ((), ()))


def mm(left, right, dims=NN):
    return lax.dot_general(left, right, dims, preferred_element_type=F32)


def head_lanes(shape, h):
    lane = lax.broadcasted_iota(jnp.int32, shape, len(shape) - 1)
    return (lane >= HD) == (h == 1)


def turned(values):
    return jnp.transpose(values.astype(F32)).astype(BF16)


def stacked(near_ref, away_ref):
    return jnp.concatenate([near_ref[...], away_ref[...]], axis=0)


def forward_kernel(q_ref, kn_ref, ka_ref, vn_ref, va_ref, qx_ref, xn_ref, xa_ref, out_ref, lse_ref):
    keys = jnp.concatenate([stacked(kn_ref, ka_ref), stacked(xn_ref, xa_ref)], axis=1)
    values = stacked(vn_ref, va_ref)
    q_pair = q_ref[...]
    lanes = head_lanes(q_pair.shape, 0)
    values_t = turned(values)
    value_rows = lax.broadcasted_iota(jnp.int32, values_t.shape, 0) < HD
    mixed = []
    for h in range(2):
        mine = lanes if h == 0 else jnp.logical_not(lanes)
        mine_values = value_rows if h == 0 else jnp.logical_not(value_rows)
        query = jnp.concatenate([jnp.where(mine, q_pair, 0), qx_ref[...]], axis=1)
        scores = mm(keys, query, NT)
        peak = jnp.max(scores, axis=0, keepdims=True)
        weights = jnp.exp(scores - peak).astype(BF16)
        both = mm(jnp.where(mine_values, values_t, 1), weights)
        total = both[127:128, :] if h == 0 else both[0:1, :]
        mixed.append(both * (1.0 / total))
        lse_ref[0, h : h + 1, :] = peak + jnp.log(total)
    out_rows = lax.broadcasted_iota(jnp.int32, mixed[0].shape, 0) < HD
    out_ref[...] = jnp.transpose(jnp.where(out_rows, mixed[0], mixed[1])).astype(BF16)


BY_PAIR = pl.BlockSpec((2 * N, 128), lambda p: (0, p))
FIXED = pl.BlockSpec((2 * N, 128), lambda p: (0, 0))


def attend_forward(*operands):
    return pl.pallas_call(
        forward_kernel,
        grid=(3,),
        in_specs=[BY_PAIR] * 5 + [FIXED] * 3,
        out_specs=[BY_PAIR, pl.BlockSpec((1, 2, 2 * N), lambda p: (p, 0, 0))],
        out_shape=[
            jax.ShapeDtypeStruct((2 * N, 384), BF16),
            jax.ShapeDtypeStruct((3, 2, 2 * N), F32),
        ],
        compiler_params=pltpu.CompilerParams(vmem_limit_bytes=6 * 2**20),
        cost_estimate=pl.CostEstimate(
            flops=2 * 2 * OWN * 512 * 1024 * 256, bytes_accessed=4 * 2**20,
            transcendentals=OWN * 512 * 1024),
        name="attend_forward",
    )(*operands)


def backward_kernel(q_ref, kn_ref, ka_ref, vn_ref, va_ref, do_ref, o_ref, qx_ref, xn_ref, xa_ref,
                    lse_ref, *refs):
    dq_ref, dk_ref, dv_ref = refs[-3:]
    k_pair, values = stacked(kn_ref, ka_ref), stacked(vn_ref, va_ref)
    keys = jnp.concatenate([k_pair, stacked(xn_ref, xa_ref)], axis=1)
    q_pair, grads = q_ref[...], do_ref[...]
    lanes = head_lanes(q_pair.shape, 0)
    product = grads.astype(F32) * o_ref[...].astype(F32)
    k_turned = turned(k_pair)
    rows = lax.broadcasted_iota(jnp.int32, (128, 2 * N), 0) < HD
    dq = jnp.zeros((128, 2 * N), F32)
    dk = jnp.zeros(k_pair.shape, F32)
    dv = jnp.zeros(k_pair.shape, F32)
    for h in range(2):
        mine = lanes if h == 0 else jnp.logical_not(lanes)
        q_head = jnp.where(mine, q_pair, 0)
        g_head = jnp.where(mine, grads, 0)
        dot_row = jnp.transpose(jnp.sum(jnp.where(mine, product, 0.0), axis=1, keepdims=True))
        scores = mm(keys, jnp.concatenate([q_head, qx_ref[...]], axis=1), NT)
        prob = jnp.exp(scores - lse_ref[0, h : h + 1, :])
        dv += mm(prob.astype(BF16), g_head)
        grad_prob = mm(values, g_head, NT)
        grad_scores = (prob * (grad_prob - dot_row)).astype(BF16)
        dk += mm(grad_scores, q_head)
        part = mm(k_turned, grad_scores)
        dq += jnp.where(rows if h == 0 else jnp.logical_not(rows), part, 0.0)
    dq_ref[...] = jnp.transpose(dq).astype(BF16) * jnp.asarray(0.125, BF16)
    dk_ref[...] = dk.astype(BF16)
    dv_ref[...] = dv.astype(BF16)


def attend_backward(operands, first, pairs, gates):
    by_pair = pl.BlockSpec((2 * N, 128), lambda p: (0, first + p))
    sizes = (2 * N, 4 * N, 4 * N)
    return pl.pallas_call(
        backward_kernel,
        grid=(pairs,),
        in_specs=[by_pair] * 7 + [FIXED] * 3
        + [pl.BlockSpec((1, 2, 2 * N), lambda p: (first + p, 0, 0))]
        + [pl.BlockSpec(memory_space=pl.ANY)] * len(gates),
        out_specs=[pl.BlockSpec((size, 128), lambda p: (0, p)) for size in sizes],
        out_shape=[jax.ShapeDtypeStruct((size, pairs * 128), BF16) for size in sizes],
        compiler_params=pltpu.CompilerParams(vmem_limit_bytes=10 * 2**20),
        cost_estimate=pl.CostEstimate(
            flops=2 * 5 * 2 * pairs * 512 * 1024 * 256, bytes_accessed=6 * 2**20,
            transcendentals=2 * pairs * 512 * 1024),
        name="attend_backward",
    )(*operands, *gates)


FF_STEP = 512
E_STEP = 512
EXPERT_MB = 40
CELLS_MB = 28


def expert_kernel(at_ref, att_own_ref, att_sib_ref, own_ref, sib_ref, cot_own_ref, cot_sib_ref,
                  marks_ref, gains_ref, w_out_ref, wu_ref, wd_ref,
                  hidden_ref, low_ref, xhat_ref, factor_ref, act_t_ref, inner_t_ref, slope_ref,
                  act_acc, grad_acc):
    f = pl.program_id(0)
    core = at_ref[CORE]

    @pl.when(f == 0)
    def _():
        mine = w_out_ref[pl.ds(pl.multiple_of(core * 384, 384), 384), :]
        other = w_out_ref[pl.ds(pl.multiple_of((1 - core) * 384, 384), 384), :]
        for n, ext_ref in enumerate((own_ref, sib_ref)):
            rows, theirs = slice(n * N, (n + 1) * N), slice((1 - n) * N, (2 - n) * N)
            hidden = ext_ref[:N, :].astype(F32) + (
                mm(att_own_ref[rows, :], mine) + mm(att_sib_ref[theirs, :], other))
            xhat, factor = normalize(hidden)
            xhat_ref[rows, :] = xhat.astype(BF16)
            factor_ref[rows, :] = factor
            act = xhat * gains_ref[2:3, :] + gains_ref[3:4, :]
            act_acc[rows, :] = act.astype(BF16)
            act_t_ref[:, rows] = jnp.transpose(act).astype(BF16)
            if n == 0:
                hidden_ref[...] = hidden
        grad_acc[...] = jnp.zeros(grad_acc.shape, F32)

    act = act_acc[...]
    cot = jnp.concatenate([cot_own_ref[...], cot_sib_ref[...]], axis=0)
    text = marks_ref[:, 8:9].astype(F32) > 0.0
    pre = jnp.where(text, mm(act, wu_ref[1]), mm(act, wu_ref[0]))
    inner, slope = gelu_parts(pre)
    grad_pre = jnp.where(text, mm(cot, wd_ref[1], NT), mm(cot, wd_ref[0], NT)) * slope
    inner_t_ref[...] = jnp.transpose(inner).astype(BF16)
    low = grad_pre.astype(BF16)
    slope_ref[...] = low
    zero = jnp.zeros((), BF16)
    grad_acc[...] += (mm(jnp.where(text, zero, low), wu_ref[0], NT)
                      + mm(jnp.where(text, low, zero), wu_ref[1], NT))

    @pl.when(f == pl.num_programs(0) - 1)
    def _():
        low_ref[...] = grad_acc[...].astype(BF16)


def experts(core, *operands):
    steps = 1536 // E_STEP
    shapes = [((N, 768), F32), ((2 * N, 768), BF16), ((2 * N, 768), BF16), ((2 * N, 1), F32),
              ((768, 2 * N), BF16)]
    fixed = lambda shape: pl.BlockSpec(shape, lambda f, *_: (0,) * len(shape))
    return pl.pallas_call(
        expert_kernel,
        grid_spec=pltpu.PrefetchScalarGridSpec(
            num_scalar_prefetch=1,
            grid=(steps,),
            in_specs=[fixed(v.shape) for v in operands[:-2]] + [
                pl.BlockSpec((2, 768, E_STEP), lambda f, at: (0, 0, at[CORE] * steps + f)),
                pl.BlockSpec((2, E_STEP, 768), lambda f, at: (0, at[CORE] * steps + f, 0)),
            ],
            out_specs=[fixed(shape) for shape, _ in shapes] + [
                pl.BlockSpec((E_STEP, 2 * N), lambda f, at: (f, 0)),
                pl.BlockSpec((2 * N, E_STEP), lambda f, at: (0, f)),
            ],
            scratch_shapes=[pltpu.VMEM((2 * N, 768), BF16), pltpu.VMEM((2 * N, 768), F32)],
        ),
        out_shape=[jax.ShapeDtypeStruct(*v) for v in shapes] + [
            jax.ShapeDtypeStruct((1536, 2 * N), BF16),
            jax.ShapeDtypeStruct((2 * N, 1536), BF16)],
        compiler_params=pltpu.CompilerParams(
            vmem_limit_bytes=18 * 2**20, dimension_semantics=("arbitrary",)),
        cost_estimate=pl.CostEstimate(
            flops=6 * 2 * 512 * 768 * 1536 + 2 * 512 * 768 * 768, bytes_accessed=22 * 2**20,
            transcendentals=2 * 512 * 1536),
        name="experts",
    )(core, *operands)


def kind_row(marks_ref):
    return turned(marks_ref[...])[8:9, :].astype(F32) > 0.0


def branch_kernel(at_ref, inner_t_ref, wd_ref, hidden_ref, marks_ref, *refs):
    own_ref, sib_ref, acc = refs[-3:]
    f = pl.program_id(0)
    text, inner_t, zero = kind_row(marks_ref), inner_t_ref[...], jnp.zeros((), BF16)
    part = (mm(jnp.where(text, zero, inner_t), wd_ref[0], TN)
            + mm(jnp.where(text, inner_t, zero), wd_ref[1], TN))

    @pl.when(f == 0)
    def _():
        acc[...] = part

    @pl.when(f > 0)
    def _():
        acc[...] += part

    @pl.when(f == pl.num_programs(0) - 1)
    def _():
        own_ref[...] = hidden_ref[...] + acc[:N, :]
        sib_ref[...] = acc[N:, :].astype(BF16)


def branches(table, inner_t, w_down, hidden, marks, gates):
    return pl.pallas_call(
        branch_kernel,
        grid_spec=pltpu.PrefetchScalarGridSpec(
            num_scalar_prefetch=1,
            grid=(3,),
            in_specs=[
                pl.BlockSpec((512, 2 * N), lambda f, at: (f, 0)),
                pl.BlockSpec((2, 512, 768), lambda f, at: (0, at[CORE] * 3 + f, 0)),
                pl.BlockSpec((N, 768), lambda f, at: (0, 0)),
                pl.BlockSpec((2 * N, 128), lambda f, at: (0, 0))] + [ANYWHERE] * len(gates),
            out_specs=[pl.BlockSpec((N, 768), lambda f, at: (0, 0))] * 2,
            scratch_shapes=[pltpu.VMEM((2 * N, 768), F32)],
        ),
        out_shape=[jax.ShapeDtypeStruct((N, 768), F32), jax.ShapeDtypeStruct((N, 768), BF16)],
        compiler_params=pltpu.CompilerParams(
            vmem_limit_bytes=20 * 2**20, dimension_semantics=("arbitrary",)),
        cost_estimate=pl.CostEstimate(
            flops=2 * 2 * 512 * 768 * 1536, bytes_accessed=8 * 2**20, transcendentals=0),
        name="branches",
    )(table, inner_t, w_down, hidden, marks, *gates)


def cells_kernel(g, at_slot, act_t_ref, grad_ref, inner_t_ref, cot_own_ref, cot_sib_ref, marks_ref,
                 *refs):
    if g == 0:
        full_ref, keep_ref, send_ref, low_ref, up_acc, down_acc = refs
        low_ref[...] = full_ref[...]
    else:
        keep_ref, send_ref, up_acc, down_acc = refs[-4:]
    zero = jnp.zeros((), BF16)
    text, text_row = marks_ref[:, 8:9].astype(F32) > 0.0, kind_row(marks_ref)
    act_t, inner_t = act_t_ref[...], inner_t_ref[...]
    grad = grad_ref[:, g * FF_STEP : (g + 1) * FF_STEP]
    lanes = slice(g * 256, (g + 1) * 256)
    cot = jnp.concatenate([cot_own_ref[:, lanes], cot_sib_ref[:, lanes]], axis=0)
    for e in range(2):
        up = mm(act_t, jnp.where(text, grad, zero) if e else jnp.where(text, zero, grad))
        up_acc[e, 0] = up[:, :256]
        up_acc[e, 1] = up[:, 256:]
        down_acc[e] = mm(
            jnp.where(text_row, inner_t, zero) if e else jnp.where(text_row, zero, inner_t), cot)

    for n, target in enumerate((keep_ref, send_ref)):
        def cell(i, carry):
            slot = g * 64 + n * 32 + i
            half = at_slot[192 + slot]
            rows = pl.ds(pl.multiple_of(at_slot[slot], 8), 24)
            below = pl.ds(pl.multiple_of(at_slot[384 + slot], 8), 24)
            target[i] = jnp.concatenate(
                [up_acc[0, half, rows, :], up_acc[1, half, rows, :],
                 down_acc[0, below, :], down_acc[1, below, :]], axis=0).astype(BF16)
            return carry
        lax.fori_loop(0, 32, cell, 0, unroll=4)


def cells(g, table, act_t, grad_pre, inner_t, cot_own, cot_sib, marks, more):
    return pl.pallas_call(
        lambda *refs: cells_kernel(g, *refs),
        in_specs=[SMALL] + [WHOLE] * 6 + ([WHOLE] if g == 0 else [ANYWHERE] * len(more)),
        out_specs=[WHOLE] * (3 if g == 0 else 2),
        out_shape=[jax.ShapeDtypeStruct((32, 96, 256), BF16)] * 2
        + [jax.ShapeDtypeStruct((2 * N, 768), BF16)] * (g == 0),
        scratch_shapes=[pltpu.VMEM((2, 2, 768, 256), F32), pltpu.VMEM((2, 1536, 256), F32)],
        compiler_params=pltpu.CompilerParams(vmem_limit_bytes=10 * 2**20),
        cost_estimate=pl.CostEstimate(
            flops=4 * 2 * 512 * 768 * 512, bytes_accessed=8 * 2**20, transcendentals=0),
        name="cells",
    )(table, act_t, grad_pre, inner_t, cot_own, cot_sib, marks, *more)


def cell_places():
    table = np.zeros((32, 4, 4, 3, 4, 4, 4), np.int32)
    for r, s in np.ndindex(32, 4):
        here = {"z": r // 8, "y": r % 4, "x": (s // 2) * 2 + (r // 4) % 2}
        flips = (0, 1, 3, 2) if s % 2 else (0, 3, 1, 2)
        for g, order in enumerate(ORDERS):
            for slot in np.ndindex(4, 4, 4):
                at = {a: here[a] ^ flips[n] for a, n in zip(order, slot)}
                x_hi, x_lo = at["x"] // 2, at["x"] % 2
                table[(r, s, 0, g) + slot] = 24 * (at["z"] * 8 + x_lo * 4 + at["y"])
                table[(r, s, 1, g) + slot] = x_hi
                table[(r, s, 2, g) + slot] = 24 * (
                    (at["z"] % 2) * 32 + x_lo * 16 + at["y"] * 4 + x_hi * 2 + at["z"] // 2)
                table[(r, s, 3, g) + slot] = at["z"] * 16 + x_lo * 8 + at["y"] * 2 + x_hi
    coordinates = np.array([[n % 2, n % 4 // 2] + [0] * 126 for n in range(128)], np.int32)
    return np.concatenate([table.reshape(128, 768), coordinates], axis=1)


def add_up(parts):
    total = parts[0].astype(F32)
    for part in parts[1:]:
        total = total + part.astype(F32)
    return total.astype(BF16)


def in_hbm(values):
    return list(values)


def pass_kernel(gates, *refs):
    count = (len(refs) - gates) // 3
    for g in range(count):
        refs[2 * count + gates + g][...] = add_up([refs[2 * g][...], refs[2 * g + 1][...]])


ANYWHERE = pl.BlockSpec(memory_space=pl.ANY)


def pass_on(kept, arrived, name, gates=()):
    kept, arrived = ([v[g] for g in (1, 2, 0)] for v in (kept, arrived))
    _, slots, rows, lanes = kept[0].shape
    block = max(slots // 4, 1)
    one = pl.BlockSpec((None, block, rows, lanes), lambda i: (1, i, 0, 0))
    passed = pl.pallas_call(
        lambda *refs: pass_kernel(len(gates), *refs),
        grid=(slots // block,),
        in_specs=[one] * (2 * len(kept)) + [ANYWHERE] * len(gates),
        out_specs=[pl.BlockSpec((block, rows, lanes), lambda i: (i, 0, 0))] * len(kept),
        out_shape=[jax.ShapeDtypeStruct((slots, rows, lanes), BF16)] * len(kept),
        compiler_params=pltpu.CompilerParams(vmem_limit_bytes=6 * 2**20),
        cost_estimate=pl.CostEstimate(
            flops=0, transcendentals=0, bytes_accessed=6 * len(kept) * slots * rows * lanes),
        name=name,
    )(*in_hbm([v for pair in zip(kept, arrived) for v in pair]), *gates)
    return [passed[n] for n in (2, 0, 1)]


def settle_kernel(groups, sizes, *refs):
    ins, outs = refs, refs[-2 * groups :]
    at = 0
    for g in range(groups):
        row = 0
        for size in sizes:
            for half in range(2):
                outs[2 * g + half][:, row : row + size, :] = add_up(
                    [ins[at + k][...] for k in range(3)])
                at += 3
            row += size


def settle(pieces, name, gates=()):
    pieces = [[p[g] for g in (1, 2, 0)] for p in pieces]
    groups = len(pieces[0])
    sizes = [p[0][0].shape[2] for p in pieces]
    _, slots, _, lanes = pieces[0][0][0].shape
    half = slots // 2
    block = max(half // 4, 1)
    steps = half // block
    operands, specs = [], []
    for g in range(groups):
        for p, size in zip(pieces, sizes):
            for h in range(2):
                wide = pl.BlockSpec(
                    (None, block, size, lanes), lambda i, h=h: (0, i + h * steps, 0, 0))
                flat = pl.BlockSpec((block, size, lanes), lambda i, h=h: (i + h * steps, 0, 0))
                operands += list(p[g])
                specs += [wide, wide, flat]
    rows = sum(sizes)
    outs = pl.pallas_call(
        lambda *refs: settle_kernel(groups, sizes, *refs),
        grid=(steps,),
        in_specs=specs + [ANYWHERE] * len(gates),
        out_specs=[pl.BlockSpec((block, rows, lanes), lambda i: (i, 0, 0))] * (2 * groups),
        out_shape=[jax.ShapeDtypeStruct((half, rows, lanes), BF16)] * (2 * groups),
        compiler_params=pltpu.CompilerParams(vmem_limit_bytes=8 * 2**20),
        cost_estimate=pl.CostEstimate(
            flops=0, transcendentals=0, bytes_accessed=8 * groups * slots * rows * lanes),
        name=name,
    )(*operands, *gates)
    shaped = [o.reshape(2, half // 2, rows, lanes) for o in outs]
    return [[shaped[2 * n + h] for n in (2, 0, 1)] for h in range(2)]


def finish_kernel(count, at_ref, *refs):
    outs, down_ref = refs[-5:-1], refs[-1]
    core, far = at_ref[CORE], at_ref[FAR]
    row = lax.broadcasted_iota(jnp.int32, (24, 80), 0)
    column = lax.broadcasted_iota(jnp.int32, (24, 80), 1)
    picks = []
    for n in range(4):
        x_hi, c = far ^ (n // 2), core ^ (n % 2)
        wanted = jnp.where(row == 6, 72, (row // 8) * 24 + x_hi * 12 + c * 6 + row % 8)
        picks.append(jnp.where((column == wanted) & (row % 8 < 6 + (row == 6)), 1.0, 0.0).astype(BF16))
    for g in range(3):
        cell = add_up([refs[3 * g + k][...] for k in range(3)])
        shared = jnp.concatenate([cell[:48], cell[96:]], axis=0)
        for out, pick in zip(outs, picks):
            out[g] = mm(pick, shared).astype(BF16)
        down_ref[g] = cell[48:96]


def finish(table, kept, first, second, gates):
    wide = pl.BlockSpec((None, None, 128, 256), lambda i, t: (0, 0, 0, 0))
    flat = pl.BlockSpec((None, 128, 256), lambda i, t: (0, 0, 0))
    sizes = [24] * 4 + [48]
    return pl.pallas_call(
        lambda *refs: finish_kernel(9, *refs),
        grid_spec=pltpu.PrefetchScalarGridSpec(
            num_scalar_prefetch=1,
            grid=(1,),
            in_specs=[wide, wide, flat] * 3 + [ANYWHERE] * len(gates),
            out_specs=[pl.BlockSpec((3, size, 256), lambda i, t: (0, 0, 0)) for size in sizes],
        ),
        out_shape=[jax.ShapeDtypeStruct((3, size, 256), BF16) for size in sizes],
        compiler_params=pltpu.CompilerParams(vmem_limit_bytes=4 * 2**20),
        name="finish",
    )(table, *[v for g in range(3) for v in (kept[g], first[g], second[g])], *gates)


def after_kernel(values_ref, *refs):
    refs[-1][...] = values_ref[...]


def after(values, gates):
    return pl.pallas_call(
        after_kernel,
        in_specs=[WHOLE] + [ANYWHERE] * len(gates),
        out_specs=WHOLE,
        out_shape=jax.ShapeDtypeStruct(values.shape, values.dtype),
        compiler_params=pltpu.CompilerParams(vmem_limit_bytes=4 * 2**20),
        name="after",
    )(values, *gates)


def put(acc, first, part, rows=slice(None)):
    for n in range(part.shape[1] // 128):
        column = first + n * 128
        lanes = slice(column % 256, column % 256 + 128)
        acc[column // 256, rows, lanes] = part[:, n * 128 : (n + 1) * 128]


def spill_rows(target, acc, at_slot, g, base, extra):
    block = 2 * (g - 1) if g else 0

    def cell(i, carry):
        slot = g * 64 + base + i
        rows = pl.ds(pl.multiple_of(at_slot[slot], 8), 24)
        part = acc[at_slot[192 + slot] + block, rows, :]
        target[i] = jnp.concatenate([part, extra(slot)], axis=0).astype(BF16)
        return carry
    lax.fori_loop(0, 32, cell, 0, unroll=4)


def tail_kernel(at_slot, act_ref, away_ref, q_ref, qb_ref, ka_ref, kb_ref, va_ref, *refs):
    keeps, sends, acc = refs[-5:-3], refs[-3:-1], refs[-1]
    act, away = act_ref[...], away_ref[...]
    near = mm(act, jnp.concatenate(
        [r[: 2 * N, :] for r in (q_ref, qb_ref, ka_ref, kb_ref, va_ref)], axis=1), TN)
    far = mm(away, jnp.concatenate(
        [r[2 * N :, :] for r in (ka_ref, kb_ref, va_ref)], axis=1), TN)
    put(acc, 0, near[:, :384])
    put(acc, 384, near[:, 384:] + far)
    blank = lambda slot: jnp.zeros((8, 256), F32)
    for n in range(2):
        spill_rows(keeps[n], acc, at_slot, n + 1, 0, blank)
        spill_rows(sends[n], acc, at_slot, n + 1, 32, blank)


def tail_cells(table, *operands):
    return pl.pallas_call(
        tail_kernel,
        in_specs=[SMALL] + [WHOLE] * len(operands),
        out_specs=[WHOLE] * 4,
        out_shape=[jax.ShapeDtypeStruct((32, 32, 256), BF16)] * 4,
        scratch_shapes=[pltpu.VMEM((4, 768, 256), F32)],
        compiler_params=pltpu.CompilerParams(vmem_limit_bytes=14 * 2**20),
        cost_estimate=pl.CostEstimate(
            flops=2 * 768 * 512 * (1024 + 640), bytes_accessed=8 * 2**20, transcendentals=0),
        name="tail_cells",
    )(table, *operands)


def inputs_kernel(at_slot, act_ref, away_ref, q_ref, qb_ref, ka_ref, kb_ref, va_ref, vb_ref,
                  att_own_ref, att_sib_ref, proj_ref, own_ref, sib_ref, far_ref, far_sib_ref,
                  second_ref, *refs):
    weights = refs[:3]
    keep_ref, send_ref, cell_keep, cell_send, acc, table = refs[-6:]
    core = at_slot[CORE]
    put(acc, 0, mm(act_ref[...], vb_ref[: 2 * N, :], TN) + mm(away_ref[...], vb_ref[2 * N :, :], TN))
    mine = pl.ds(pl.multiple_of(core * 384, 384), 384)
    other = pl.ds(pl.multiple_of((1 - core) * 384, 384), 384)
    put(acc, 128, mm(att_own_ref[...], proj_ref[...], TN), mine)
    put(acc, 128, mm(att_sib_ref[:N, :], proj_ref[N:, :], TN)
        + mm(att_sib_ref[N:, :], proj_ref[:N, :], TN), other)

    vectors = [jnp.zeros((1, 768), F32)] * 2 + [second_ref[0:1, :], second_ref[1:2, :]]
    wide = list(zip((q_ref, ka_ref, va_ref), (qb_ref, kb_ref, vb_ref), weights))
    for n, ext_ref in enumerate((own_ref, sib_ref, far_ref, far_sib_ref)):
        rows = slice(n * N, (n + 1) * N)
        total = jnp.zeros((N, 768), F32)
        for a_ref, b_ref, w_ref in wide[0 if n < 2 else 1 :]:
            grads = jnp.concatenate([a_ref[rows, :], b_ref[rows, :]], axis=1)
            total += mm(grads, w_ref[...], NT)
        xhat, _ = normalize(ext_ref[:N, :].astype(F32))
        vectors[0] += jnp.sum(total * xhat, axis=0, keepdims=True)
        vectors[1] += jnp.sum(total, axis=0, keepdims=True)
        half = slice((n // 2) * N, (n // 2 + 1) * N)
        if n % 2 == 0:
            keep_ref[half, :] = total
        else:
            send_ref[half, :] = total.astype(BF16)

    chip = lax.broadcasted_iota(jnp.int32, (64, 768), 0)
    owner = lax.broadcasted_iota(jnp.int32, (64, 768), 1) // 12
    feature = lax.broadcasted_iota(jnp.int32, (768, 128), 0) % 12
    lane = lax.broadcasted_iota(jnp.int32, (768, 128), 1)
    spread = jnp.zeros((64, 128), F32)
    for n in range(4):
        line = jnp.broadcast_to(vectors[n], (64, 768))
        values = jnp.where(chip == owner, line, 0.0).astype(BF16)
        spread += mm(values, jnp.where(lane == feature + 12 * n, 1.0, 0.0).astype(BF16))
    table[...] = spread

    def lines(slot):
        row = table[pl.ds(at_slot[576 + slot], 1), :]
        return jnp.concatenate(
            [jnp.broadcast_to(row, (8, 128)), jnp.zeros((8, 128), F32)], axis=1)

    spill_rows(cell_keep, acc, at_slot, 0, 0, lines)
    spill_rows(cell_send, acc, at_slot, 0, 32, lines)


def input_partials(table, operands, gates):
    whole = lambda shape: pl.BlockSpec(shape, lambda i, *_: (0,) * len(shape))
    shapes = [((2 * N, 768), F32), ((2 * N, 768), BF16)] + [((32, 32, 256), BF16)] * 2
    return pl.pallas_call(
        inputs_kernel,
        grid_spec=pltpu.PrefetchScalarGridSpec(
            num_scalar_prefetch=1,
            grid=(1,),
            in_specs=[whole(v.shape) for v in operands[:-1]]
            + [pl.BlockSpec((768, 384), lambda i, at, n=n: (0, 2 * n + at[CORE])) for n in range(3)]
            + [ANYWHERE] * len(gates),
            out_specs=[whole(shape) for shape, _ in shapes],
            scratch_shapes=[pltpu.VMEM((2, 768, 256), F32), pltpu.VMEM((64, 128), F32)],
        ),
        out_shape=[jax.ShapeDtypeStruct(*v) for v in shapes],
        compiler_params=pltpu.CompilerParams(vmem_limit_bytes=16 * 2**20),
        cost_estimate=pl.CostEstimate(
            flops=2 * 768 * 384 * 512 * 7, bytes_accessed=10 * 2**20, transcendentals=0),
        name="input_partials",
    )(table, *operands, *[operands[-1]] * 2, *gates)


def sum_core_kernel(own_ref, sib_ref, *refs):
    refs[-1][...] = (own_ref[...] + sib_ref[...].astype(F32)).astype(BF16)


def sum_core(own, sib, gates):
    half = pl.BlockSpec((N, 768), lambda i: (1, 0))
    return pl.pallas_call(
        sum_core_kernel,
        grid=(1,),
        in_specs=[half, half] + [ANYWHERE] * len(gates),
        out_specs=pl.BlockSpec((N, 768), lambda i: (0, 0)),
        out_shape=jax.ShapeDtypeStruct((N, 768), BF16),
        compiler_params=pltpu.CompilerParams(vmem_limit_bytes=4 * 2**20),
        name="sum_core",
    )(own, sib, *gates)


def token_kernel(tokens_ref, hidden_ref, own_ref, sib_ref, far_ref, gains_ref, out_own_ref,
                 out_sib_ref, grad_ref, out_ref):
    grad = own_ref[...] + sib_ref[...].astype(F32) + far_ref[...].astype(F32)
    xhat, factor = normalize(tokens_ref[...].astype(F32))
    grad_ref[...] = hidden_ref[...] + normalize_back(grad, xhat, factor, gains_ref[0:1, :])
    out_ref[...] = (out_own_ref[...] + out_sib_ref[...].astype(F32)).astype(BF16)


def token_grads(tokens, hidden, own, sib, far, gains, out_own, out_sib):
    half = pl.BlockSpec((N, 768), lambda i: (0, 0))
    return pl.pallas_call(
        token_kernel,
        grid=(1,),
        in_specs=[half] * 5 + [pl.BlockSpec((4, 768), lambda i: (0, 0))] + [half] * 2,
        out_specs=[half] * 2,
        out_shape=[jax.ShapeDtypeStruct((N, 768), F32), jax.ShapeDtypeStruct((N, 768), BF16)],
        compiler_params=pltpu.CompilerParams(vmem_limit_bytes=8 * 2**20),
        name="token_grads",
    )(tokens, hidden, own, sib, far, gains, out_own, out_sib)


def assemble_kernel(at_ref, own_ref, near_ref, away_ref, cross_ref, down_ref, up_ref, qkv_ref, out_ref,
                    vec_ref, below_ref, held):
    core, far = at_ref[CORE], at_ref[FAR]
    held[far * 2 + core] = own_ref[...]
    held[far * 2 + 1 - core] = near_ref[...]
    held[2 - far * 2 + core] = away_ref[...]
    held[2 - far * 2 + 1 - core] = cross_ref[...]
    line = own_ref[0, :8, :128].astype(F32) + near_ref[0, :8, :128].astype(F32)
    vec_ref[...] = jnp.where(core == 0, line, pltpu.roll(line, 122, 1))
    for x_hi in range(2):
        for c in range(2):
            for g in range(3):
                rows = held[x_hi * 2 + c, g].astype(F32)
                first = c * 1536 + g * 512 + x_hi * 256
                for e in range(2):
                    up_ref[:, e, first : first + 256] = rows[8 * e : 8 * e + 6] * UP_FACTORS[e]
                for n in range(2):
                    at = (g + 2) % 3 * 512 + x_hi * 256 + n * 128
                    kind, within = at // 384, at % 384 + c * 384
                    part = rows[16:22, n * 128 : (n + 1) * 128]
                    if kind < 3:
                        qkv_ref[:, kind * 768 + within : kind * 768 + within + 128] = part
                    else:
                        out_ref[:, within : within + 128] = part
    for g in range(3):
        part = down_ref[g].astype(F32)
        for e in range(2):
            below_ref[e, :, g * 256 : (g + 1) * 256] = part[24 * e : 24 * e + 24] * UP_FACTORS[e]


def assemble(table, *parts):
    return pl.pallas_call(
        assemble_kernel,
        in_specs=[SMALL] + [WHOLE] * 5,
        out_specs=[WHOLE] * 5,
        out_shape=[
            jax.ShapeDtypeStruct((6, 2, 3072), F32),
            jax.ShapeDtypeStruct((6, 2304), F32),
            jax.ShapeDtypeStruct((6, 768), F32),
            jax.ShapeDtypeStruct((8, 128), F32),
            jax.ShapeDtypeStruct((2, 24, 768), F32),
        ],
        scratch_shapes=[pltpu.VMEM((4, 3, 24, 256), BF16)],
        compiler_params=pltpu.CompilerParams(vmem_limit_bytes=4 * 2**20),
        name="assemble",
    )(table, *parts)

def shards(tokens, first_gain, first_shift, w_qkv, w_out, second_gain, second_shift,
           w_up, w_down, modality, segments, partner, cotangent):
    table = lax.dynamic_index_in_dim(
        jnp.asarray(cell_places()), lax.axis_index(BOTH), 0, keepdims=False)
    gains = jnp.stack([first_gain, first_shift, second_gain, second_shift])

    own = marked(partner, tokens[0], segments, modality)
    away = swap_far(own)
    sib = swap_core(own)
    cot_own = cotangent[0]
    cot_sib = swap_core(cot_own)

    act1, marks, queries, k_near, v_near, qx = project(table, own, sib, gains, w_qkv, True)
    away_sib = swap_core(after(away, [qx]))
    act1_away, marks_away, k_away, v_away = project(table, away, away_sib, gains, w_qkv, False)
    attended, lse = attend_forward(
        queries, k_near, k_away, v_near, v_away, qx, marks, marks_away)
    attended_sib = swap_core(attended)

    hidden, grad_act2, xhat2, factor2, act_t, inner_t, grad_pre = experts(
        table, attended, attended_sib, own, sib, cot_own, cot_sib, marks, gains, w_out, w_up, w_down)
    ff_kept, ff_first, more = [], [], [grad_act2]
    for g in range(3):
        keep, gone, *low = cells(g, table, act_t, grad_pre, inner_t, cot_own, cot_sib, marks, more)
        ff_kept.append(keep.reshape(2, 16, 96, 256))
        ff_first.append(send(gone.reshape(2, 16, 96, 256), axis_step(ORDERS[g][0], True)))
        if g == 0:
            grad_sib = swap_core(low[0])
        more = [keep] if g == 0 else [keep, grad_sib]
    hidden_grad, grad_att, proj_half, vectors = middle(
        table, grad_act2, grad_sib, xhat2, factor2, cot_own, cot_sib, gains, w_out)

    def along(stage, first, values):
        sent = {g: send(values[g], axis_step(ORDERS[g][stage], first)) for g in (1, 2, 0)}
        return [sent[g] for g in range(3)]

    taken = (queries, k_near, k_away, v_near, v_away, grad_att, attended, qx, marks, marks_away, lse)
    q_a, k_a, v_a = attend_backward(taken, 0, 2, ())
    q_b, k_b, v_b = attend_backward(taken, 2, 1, ())
    cells_a = tail_cells(table, act1, act1_away, q_a, q_b, k_a, k_b, v_a)
    partial_own, partial_low, *cells_b = input_partials(table, (
        act1, act1_away, q_a, q_b, k_a, k_b, v_a, v_b, attended, attended_sib, proj_half,
        own, sib, away, away_sib, vectors, w_qkv), ())
    kept = [v.reshape(2, 16, 32, 256) for v in (cells_b[0], cells_a[0], cells_a[1])]
    first = along(0, True, [v.reshape(2, 16, 32, 256) for v in (cells_b[1], cells_a[2], cells_a[3])])
    ff_second = along(0, False, pass_on(ff_kept, ff_first, "pass_first", [cells_b[0]]))
    partial_sib = swap_core(partial_low)
    passed = pass_on(kept, first, "pass_tail")
    second = along(0, False, passed)
    out_own, out_sib = branches(table, inner_t, w_down, hidden, marks, passed)

    kept, sent = settle(
        [list(zip(ff_kept, ff_first, ff_second)), list(zip(kept, first, second))], "settle_all", [out_sib])
    first = along(1, True, sent)
    second = along(1, False, pass_on(kept, first, "pass_second"))
    kept, sent = settle([list(zip(kept, first, second))], "settle_second")
    first = along(2, True, sent)
    from_far = swap_far(sum_core(partial_own, partial_sib, first))
    second = along(2, False, pass_on(kept, first, "pass_third"))
    held, *shares, down_held = finish(table, kept, first, second, [from_far])

    near, beyond = swap_core(shares[0]), swap_far(shares[1])
    cross = send(shares[2], lambda x, y, z, c: (x ^ 2, y, z, 1 - c))
    below = send(down_held, lambda x, y, z, c: (x, y, 2 * c + z % 2, z // 2))
    up_grad, qkv_grad, out_grad, line, down_grad = assemble(
        table, held, near, beyond, cross, below)

    token_grad, layer_output = token_grads(
        tokens[0], hidden_grad, partial_own, partial_sib, from_far, gains, out_own, swap_core(out_sib))

    return (
        layer_output[None], token_grad[None], line[6, :6], line[6, 12:18], qkv_grad, out_grad,
        line[6, 24:30], line[6, 36:42], up_grad.transpose(1, 0, 2), down_grad)


def solution(mesh):
    cut = P("rows", "seq", None)
    flat = P(BOTH)
    placed = (cut,) + (P(),) * 8 + (P("rows", "seq"), P("rows", "seq"), P("rows", None), cut)
    return jax.shard_map(
        shards, mesh=mesh, in_specs=placed,
        out_specs=(cut, cut, flat, flat, P(BOTH, None), P(BOTH, None), flat, flat,
                   P(None, BOTH, None), P(None, BOTH, None)),
        check_vma=False)
```

```python
import jax
import jax.numpy as jnp
import numpy as np
from jax import lax
from jax.experimental import pallas as pl
from jax.experimental.pallas import tpu as pltpu
from jax.sharding import PartitionSpec as P

HD = 64
OWN = 6
CORE, FAR = 768, 769
IMG = 197
NIMG = 4
BOTH = ("rows", "seq")
F32 = jnp.float32
BF16 = jnp.bfloat16
MASKED = -1e30


def route(step):
    pairs = []
    for r in range(32):
        z, x_lo, y = r // 8, (r // 4) % 2, r % 4
        for s in range(4):
            x, c = (s // 2) * 2 + x_lo, s % 2
            tx, ty, tz, tc = step(x, y, z, c)
            target = (tz * 8 + (tx % 2) * 4 + ty) * 4 + (tx // 2) * 2 + tc
            pairs.append((r * 4 + s, target))
    return pairs


def send(values, step):
    return lax.ppermute(values, BOTH, route(step))


def swap_core(values):
    return send(values, lambda x, y, z, c: (x, y, z, 1 - c))


def swap_far(values):
    return send(values, lambda x, y, z, c: (x ^ 2, y, z, c))


def axis_step(axis, first):
    def step(x, y, z, c):
        flip = 1 if (c == 0) == first else 3
        at = {"x": x, "y": y, "z": z}
        at[axis] ^= flip
        return (at["x"], at["y"], at["z"], c)

    return step


UP_FACTORS = (1024 / (2 * 788), 1024 / (2 * 236))
ORDERS = (("x", "y", "z"), ("y", "z", "x"), ("z", "x", "y"))


def wide(vector_ref):
    return vector_ref[...].reshape(1, 768)


LINE = pl.BlockSpec((768,), lambda *_: (0,))


def normalize(inputs):
    centred = inputs - jnp.mean(inputs, axis=-1, keepdims=True)
    factor = lax.rsqrt(jnp.mean(centred * centred, axis=-1, keepdims=True) + 1e-05)
    return centred * factor, factor


def normalize_back(grad, xhat, factor, gain):
    gy = grad * gain
    mean_gy = jnp.mean(gy, axis=-1, keepdims=True)
    mean_gx = jnp.mean(gy * xhat, axis=-1, keepdims=True)
    return factor * (gy - mean_gy - xhat * mean_gx)


SMALL = pl.BlockSpec(memory_space=pltpu.SMEM)
WHOLE = pl.BlockSpec(memory_space=pltpu.VMEM)
N = 256


def marked_kernel(partner, tokens_ref, segments_ref, modality_ref, out_ref):
    segments = segments_ref[...]
    tag = jnp.zeros(segments.shape, jnp.int32)
    for n in range(8):
        tag = jnp.where(segments == n, partner[0, n], tag)
    marks = jnp.concatenate(
        [tag, modality_ref[...], jnp.zeros((1, 256), jnp.int32)], axis=1).astype(F32)
    out_ref[:N, :] = tokens_ref[...]
    out_ref[N:, :] = jnp.concatenate([marks, jnp.zeros((15, 768), F32)], axis=0).astype(BF16)


def marked(partner, tokens, segments, modality):
    return pl.pallas_call(
        marked_kernel,
        in_specs=[SMALL, WHOLE, WHOLE, WHOLE],
        out_specs=WHOLE,
        out_shape=jax.ShapeDtypeStruct((N + 16, 768), BF16),
        compiler_params=pltpu.CompilerParams(vmem_limit_bytes=60 * 2**20),
        name="marked",
    )(partner, tokens, segments, modality)


def mark_lanes(ext):
    row = ext[N:, :].astype(F32)
    place = lax.broadcasted_iota(jnp.int32, (128, N), 0)
    tag = jnp.broadcast_to(row[:1, :N], (128, N))
    kind = jnp.broadcast_to(row[:1, N : 2 * N], (128, N))
    hot = jnp.where((place < NIMG) & (place.astype(F32) == tag), 1.0, 0.0)
    return jnp.transpose(jnp.where(place == 8, kind, hot))


def project_kernel(at_ref, near, a_ref, b_ref, gain_ref, shift_ref, *refs):
    count = 3 if near else 2
    weights, outs = refs[:count], refs[count:]
    for n, ext_ref in enumerate((a_ref, b_ref)):
        rows = slice(n * N, (n + 1) * N)
        ext = ext_ref[...]
        xhat, _ = normalize(ext[:N].astype(F32))
        act = (xhat * wide(gain_ref) + wide(shift_ref)).astype(BF16)
        outs[0][rows, :] = act
        marks = mark_lanes(ext)
        outs[1][rows, :] = marks.astype(BF16)
        for m in range(count):
            part = mm(act, weights[m][...])
            outs[2 + m][rows, :] = (0.125 * part if near and m == 0 else part).astype(BF16)
        if near:
            lane = lax.broadcasted_iota(jnp.int32, marks.shape, 1)
            outs[5][rows, :] = jnp.where((lane < NIMG) & (marks == 0.0), MASKED, 0.0).astype(BF16)


def project(table, first, second, gain, shift, w_qkv, near):
    kinds = (0, 1, 2) if near else (1, 2)
    sizes = [768, 128] + [384] * len(kinds) + ([128] if near else [])
    whole = lambda shape: pl.BlockSpec(shape, lambda i, at: (0, 0))
    return pl.pallas_call(
        lambda at_ref, *refs: project_kernel(at_ref, near, *refs),
        grid_spec=pltpu.PrefetchScalarGridSpec(
            num_scalar_prefetch=1,
            grid=(1,),
            in_specs=[whole((N + 16, 768))] * 2 + [LINE] * 2
            + [pl.BlockSpec((768, 384), lambda i, at, n=n: (0, 2 * n + at[CORE])) for n in kinds],
            out_specs=[whole((2 * N, size)) for size in sizes],
        ),
        out_shape=[jax.ShapeDtypeStruct((2 * N, size), BF16) for size in sizes],
        compiler_params=pltpu.CompilerParams(vmem_limit_bytes=6 * 2**20),
        cost_estimate=pl.CostEstimate(
            flops=2 * 512 * 768 * 384 * len(kinds), bytes_accessed=4 * 2**20, transcendentals=0),
        name="project_near" if near else "project_away",
    )(table, first, second, gain, shift, *[w_qkv] * len(kinds))


def middle_kernel(place, grad_ref, sib_ref, xhat_ref, factor_ref, cot_own_ref, cot_sib_ref,
                  gain_ref, w_out_ref, hidden_ref, att_ref, proj_ref, vec_ref):
    core = place[CORE]
    for n, cot_ref in enumerate((cot_own_ref, cot_sib_ref)):
        rows, other = slice(n * N, (n + 1) * N), slice((1 - n) * N, (2 - n) * N)
        grad = grad_ref[rows, :].astype(F32) + sib_ref[other, :].astype(F32)
        xhat = xhat_ref[rows, :].astype(F32)
        total = cot_ref[...].astype(F32) + normalize_back(grad, xhat, factor_ref[rows, :], wide(gain_ref))
        low = total.astype(BF16)
        if n == 0:
            hidden_ref[...] = total
            vec_ref[0:1, :] = jnp.sum(grad * xhat, axis=0, keepdims=True)
            vec_ref[1:2, :] = jnp.sum(grad, axis=0, keepdims=True)
        mine = w_out_ref[pl.ds(pl.multiple_of(core * 384, 384), 384), :]
        att_ref[rows, :] = mm(low, mine, NT).astype(BF16)
        proj_ref[rows, :] = jnp.where(core == 0, low[:, :384], low[:, 384:])


def middle(place, *operands):
    return pl.pallas_call(
        middle_kernel,
        in_specs=[SMALL] + [WHOLE] * len(operands),
        out_specs=[WHOLE] * 4,
        out_shape=[
            jax.ShapeDtypeStruct((N, 768), F32),
            jax.ShapeDtypeStruct((2 * N, 384), BF16),
            jax.ShapeDtypeStruct((2 * N, 384), BF16),
            jax.ShapeDtypeStruct((2, 768), F32),
        ],
        compiler_params=pltpu.CompilerParams(vmem_limit_bytes=6 * 2**20),
        cost_estimate=pl.CostEstimate(
            flops=2 * 512 * 768 * 384, bytes_accessed=8 * 2**20, transcendentals=0),
        name="middle",
    )(place, *operands)


def gelu_parts(pre):
    phi = 0.5 * (1.0 + lax.erf(pre * 0.7071067811865476))
    slope = phi + pre * (0.3989422804014327 * jnp.exp(-0.5 * pre * pre))
    return pre * phi, slope


NT = (((1,), (1,)), ((), ()))
TN = (((0,), (0,)), ((), ()))
NN = (((1,), (0,)), ((), ()))


def mm(left, right, dims=NN):
    return lax.dot_general(left, right, dims, preferred_element_type=F32)


def head_lanes(shape, h):
    lane = lax.broadcasted_iota(jnp.int32, shape, len(shape) - 1)
    return (lane >= HD) == (h == 1)


def turned(values):
    return jnp.transpose(values.astype(F32)).astype(BF16)


def stacked(near_ref, away_ref):
    return jnp.concatenate([near_ref[...], away_ref[...]], axis=0)


def half_attention(q_ref, k_ref, v_ref, qx_ref, x_ref, h, peak_before):
    q_pair = q_ref[...]
    mine = head_lanes(q_pair.shape, 0) if h == 0 else jnp.logical_not(head_lanes(q_pair.shape, 0))
    query = jnp.concatenate([jnp.where(mine, q_pair, 0), qx_ref[...]], axis=1)
    scores = mm(jnp.concatenate([k_ref[...], x_ref[...]], axis=1), query, NT)
    peak = jnp.max(scores, axis=0, keepdims=True)
    if peak_before is not None:
        peak = jnp.maximum(peak, peak_before)
    weights = jnp.exp(scores - peak).astype(BF16)
    values_t = turned(v_ref[...])
    rows = lax.broadcasted_iota(jnp.int32, values_t.shape, 0) < HD
    left = jnp.where(rows, values_t, 1) if h == 0 else jnp.where(rows, 1, values_t)
    return mm(left, weights), peak


def near_kernel(q_ref, k_ref, v_ref, qx_ref, x_ref, both_ref, peak_ref):
    for h in range(2):
        both, peak = half_attention(q_ref, k_ref, v_ref, qx_ref, x_ref, h, None)
        both_ref[0, h] = both
        peak_ref[0, h : h + 1, :] = peak


def forward_kernel(q_ref, k_ref, v_ref, qx_ref, x_ref, both_ref, peak_ref, out_ref, lse_ref):
    mixed = []
    for h in range(2):
        before = peak_ref[0, h : h + 1, :]
        both, peak = half_attention(q_ref, k_ref, v_ref, qx_ref, x_ref, h, before)
        both = both + both_ref[0, h] * jnp.exp(before - peak)
        total = both[127:128, :] if h == 0 else both[0:1, :]
        mixed.append(both * (1.0 / total))
        lse_ref[0, h : h + 1, :] = peak + jnp.log(total)
    rows = lax.broadcasted_iota(jnp.int32, mixed[0].shape, 0) < HD
    out_ref[...] = jnp.transpose(jnp.where(rows, mixed[0], mixed[1])).astype(BF16)


BY_PAIR = pl.BlockSpec((2 * N, 128), lambda p: (0, p))
FIXED = pl.BlockSpec((2 * N, 128), lambda p: (0, 0))


PAIR_LINES = pl.BlockSpec((1, 2, 2 * N), lambda p: (p, 0, 0))
PAIR_BOTH = pl.BlockSpec((1, 2, 128, 2 * N), lambda p: (p, 0, 0, 0))


def attend_near(*operands):
    return pl.pallas_call(
        near_kernel,
        grid=(3,),
        in_specs=[BY_PAIR] * 3 + [FIXED] * 2,
        out_specs=[PAIR_BOTH, PAIR_LINES],
        out_shape=[
            jax.ShapeDtypeStruct((3, 2, 128, 2 * N), F32),
            jax.ShapeDtypeStruct((3, 2, 2 * N), F32),
        ],
        compiler_params=pltpu.CompilerParams(vmem_limit_bytes=8 * 2**20),
        cost_estimate=pl.CostEstimate(
            flops=2 * OWN * 512 * 1024 * 256, bytes_accessed=4 * 2**20,
            transcendentals=OWN * 512 * 512),
        name="attend_near",
    )(*operands)


def attend_forward(*operands):
    return pl.pallas_call(
        forward_kernel,
        grid=(3,),
        in_specs=[BY_PAIR] * 3 + [FIXED] * 2 + [PAIR_BOTH, PAIR_LINES],
        out_specs=[BY_PAIR, PAIR_LINES],
        out_shape=[
            jax.ShapeDtypeStruct((2 * N, 384), BF16),
            jax.ShapeDtypeStruct((3, 2, 2 * N), F32),
        ],
        compiler_params=pltpu.CompilerParams(vmem_limit_bytes=8 * 2**20),
        cost_estimate=pl.CostEstimate(
            flops=2 * OWN * 512 * 1024 * 256, bytes_accessed=5 * 2**20,
            transcendentals=OWN * 512 * 512),
        name="attend_forward",
    )(*operands)


def backward_kernel(q_ref, kn_ref, ka_ref, vn_ref, va_ref, do_ref, o_ref, qx_ref, xn_ref, xa_ref,
                    lse_ref, *refs):
    dq_ref, dk_ref, dv_ref = refs[-3:]
    k_pair, values = stacked(kn_ref, ka_ref), stacked(vn_ref, va_ref)
    keys = jnp.concatenate([k_pair, stacked(xn_ref, xa_ref)], axis=1)
    q_pair, grads = q_ref[...], do_ref[...]
    lanes = head_lanes(q_pair.shape, 0)
    product = grads.astype(F32) * o_ref[...].astype(F32)
    k_turned = turned(k_pair)
    rows = lax.broadcasted_iota(jnp.int32, (128, 2 * N), 0) < HD
    dq = jnp.zeros((128, 2 * N), F32)
    dk = jnp.zeros(k_pair.shape, F32)
    dv = jnp.zeros(k_pair.shape, F32)
    for h in range(2):
        mine = lanes if h == 0 else jnp.logical_not(lanes)
        q_head = jnp.where(mine, q_pair, 0)
        g_head = jnp.where(mine, grads, 0)
        dot_row = jnp.transpose(jnp.sum(jnp.where(mine, product, 0.0), axis=1, keepdims=True))
        scores = mm(keys, jnp.concatenate([q_head, qx_ref[...]], axis=1), NT)
        prob = jnp.exp(scores - lse_ref[0, h : h + 1, :])
        dv += mm(prob.astype(BF16), g_head)
        grad_prob = mm(values, g_head, NT)
        grad_scores = (prob * (grad_prob - dot_row)).astype(BF16)
        dk += mm(grad_scores, q_head)
        part = mm(k_turned, grad_scores)
        dq += jnp.where(rows if h == 0 else jnp.logical_not(rows), part, 0.0)
    dq_ref[...] = jnp.transpose(dq).astype(BF16) * jnp.asarray(0.125, BF16)
    dk_ref[...] = dk.astype(BF16)
    dv_ref[...] = dv.astype(BF16)


def attend_backward(operands, first, pairs, gates):
    by_pair = pl.BlockSpec((2 * N, 128), lambda p: (0, first + p))
    sizes = (2 * N, 4 * N, 4 * N)
    return pl.pallas_call(
        backward_kernel,
        grid=(pairs,),
        in_specs=[by_pair] * 7 + [FIXED] * 3
        + [pl.BlockSpec((1, 2, 2 * N), lambda p: (first + p, 0, 0))]
        + [pl.BlockSpec(memory_space=pl.ANY)] * len(gates),
        out_specs=[pl.BlockSpec((size, 128), lambda p: (0, p)) for size in sizes],
        out_shape=[jax.ShapeDtypeStruct((size, pairs * 128), BF16) for size in sizes],
        compiler_params=pltpu.CompilerParams(vmem_limit_bytes=10 * 2**20),
        cost_estimate=pl.CostEstimate(
            flops=2 * 5 * 2 * pairs * 512 * 1024 * 256, bytes_accessed=6 * 2**20,
            transcendentals=2 * pairs * 512 * 1024),
        name="attend_backward",
    )(*operands, *gates)


FF_STEP = 512
E_STEP = 512
EXPERT_MB = 40
CELLS_MB = 28


def expert_kernel(at_ref, att_own_ref, att_sib_ref, own_ref, sib_ref, cot_own_ref, cot_sib_ref,
                  marks_ref, gain_ref, shift_ref, w_out_ref, wu_ref, wd_ref,
                  hidden_ref, low_ref, xhat_ref, factor_ref, act_t_ref, inner_t_ref, slope_ref,
                  act_acc, grad_acc):
    f = pl.program_id(0)
    core = at_ref[CORE]

    @pl.when(f == 0)
    def _():
        mine = w_out_ref[pl.ds(pl.multiple_of(core * 384, 384), 384), :]
        other = w_out_ref[pl.ds(pl.multiple_of((1 - core) * 384, 384), 384), :]
        for n, ext_ref in enumerate((own_ref, sib_ref)):
            rows, theirs = slice(n * N, (n + 1) * N), slice((1 - n) * N, (2 - n) * N)
            hidden = ext_ref[:N, :].astype(F32) + (
                mm(att_own_ref[rows, :], mine) + mm(att_sib_ref[theirs, :], other))
            xhat, factor = normalize(hidden)
            xhat_ref[rows, :] = xhat.astype(BF16)
            factor_ref[rows, :] = factor
            act = xhat * wide(gain_ref) + wide(shift_ref)
            act_acc[rows, :] = act.astype(BF16)
            act_t_ref[:, rows] = jnp.transpose(act).astype(BF16)
            if n == 0:
                hidden_ref[...] = hidden
        grad_acc[...] = jnp.zeros(grad_acc.shape, F32)

    act = act_acc[...]
    cot = jnp.concatenate([cot_own_ref[...], cot_sib_ref[...]], axis=0)
    text = marks_ref[:, 8:9].astype(F32) > 0.0
    pre = jnp.where(text, mm(act, wu_ref[1]), mm(act, wu_ref[0]))
    inner, slope = gelu_parts(pre)
    grad_pre = jnp.where(text, mm(cot, wd_ref[1], NT), mm(cot, wd_ref[0], NT)) * slope
    inner_t_ref[...] = jnp.transpose(inner).astype(BF16)
    low = grad_pre.astype(BF16)
    slope_ref[...] = low
    zero = jnp.zeros((), BF16)
    grad_acc[...] += (mm(jnp.where(text, zero, low), wu_ref[0], NT)
                      + mm(jnp.where(text, low, zero), wu_ref[1], NT))

    @pl.when(f == pl.num_programs(0) - 1)
    def _():
        low_ref[...] = grad_acc[...].astype(BF16)


def experts(core, *operands):
    steps = 1536 // E_STEP
    shapes = [((N, 768), F32), ((2 * N, 768), BF16), ((2 * N, 768), BF16), ((2 * N, 1), F32),
              ((768, 2 * N), BF16)]
    fixed = lambda shape: pl.BlockSpec(shape, lambda f, *_: (0,) * len(shape))
    return pl.pallas_call(
        expert_kernel,
        grid_spec=pltpu.PrefetchScalarGridSpec(
            num_scalar_prefetch=1,
            grid=(steps,),
            in_specs=[fixed(v.shape) for v in operands[:-2]] + [
                pl.BlockSpec((2, 768, E_STEP), lambda f, at: (0, 0, at[CORE] * steps + f)),
                pl.BlockSpec((2, E_STEP, 768), lambda f, at: (0, at[CORE] * steps + f, 0)),
            ],
            out_specs=[fixed(shape) for shape, _ in shapes] + [
                pl.BlockSpec((E_STEP, 2 * N), lambda f, at: (f, 0)),
                pl.BlockSpec((2 * N, E_STEP), lambda f, at: (0, f)),
            ],
            scratch_shapes=[pltpu.VMEM((2 * N, 768), BF16), pltpu.VMEM((2 * N, 768), F32)],
        ),
        out_shape=[jax.ShapeDtypeStruct(*v) for v in shapes] + [
            jax.ShapeDtypeStruct((1536, 2 * N), BF16),
            jax.ShapeDtypeStruct((2 * N, 1536), BF16)],
        compiler_params=pltpu.CompilerParams(
            vmem_limit_bytes=18 * 2**20, dimension_semantics=("arbitrary",)),
        cost_estimate=pl.CostEstimate(
            flops=6 * 2 * 512 * 768 * 1536 + 2 * 512 * 768 * 768, bytes_accessed=22 * 2**20,
            transcendentals=2 * 512 * 1536),
        name="experts",
    )(core, *operands)


def kind_row(marks_ref):
    return turned(marks_ref[...])[8:9, :].astype(F32) > 0.0


def branch_kernel(at_ref, inner_t_ref, wd_ref, hidden_ref, marks_ref, *refs):
    own_ref, sib_ref, acc = refs[-3:]
    f = pl.program_id(0)
    text, inner_t, zero = kind_row(marks_ref), inner_t_ref[...], jnp.zeros((), BF16)
    part = (mm(jnp.where(text, zero, inner_t), wd_ref[0], TN)
            + mm(jnp.where(text, inner_t, zero), wd_ref[1], TN))

    @pl.when(f == 0)
    def _():
        acc[...] = part

    @pl.when(f > 0)
    def _():
        acc[...] += part

    @pl.when(f == pl.num_programs(0) - 1)
    def _():
        own_ref[...] = hidden_ref[...] + acc[:N, :]
        sib_ref[...] = acc[N:, :].astype(BF16)


def branches(table, inner_t, w_down, hidden, marks, gates):
    return pl.pallas_call(
        branch_kernel,
        grid_spec=pltpu.PrefetchScalarGridSpec(
            num_scalar_prefetch=1,
            grid=(3,),
            in_specs=[
                pl.BlockSpec((512, 2 * N), lambda f, at: (f, 0)),
                pl.BlockSpec((2, 512, 768), lambda f, at: (0, at[CORE] * 3 + f, 0)),
                pl.BlockSpec((N, 768), lambda f, at: (0, 0)),
                pl.BlockSpec((2 * N, 128), lambda f, at: (0, 0))] + [ANYWHERE] * len(gates),
            out_specs=[pl.BlockSpec((N, 768), lambda f, at: (0, 0))] * 2,
            scratch_shapes=[pltpu.VMEM((2 * N, 768), F32)],
        ),
        out_shape=[jax.ShapeDtypeStruct((N, 768), F32), jax.ShapeDtypeStruct((N, 768), BF16)],
        compiler_params=pltpu.CompilerParams(
            vmem_limit_bytes=20 * 2**20, dimension_semantics=("arbitrary",)),
        cost_estimate=pl.CostEstimate(
            flops=2 * 2 * 512 * 768 * 1536, bytes_accessed=8 * 2**20, transcendentals=0),
        name="branches",
    )(table, inner_t, w_down, hidden, marks, *gates)


def cells_kernel(g, at_slot, act_t_ref, grad_ref, inner_t_ref, cot_own_ref, cot_sib_ref, marks_ref,
                 *refs):
    if g == 0:
        full_ref, keep_ref, send_ref, low_ref, up_acc, down_acc = refs
        low_ref[...] = full_ref[...]
    else:
        keep_ref, send_ref, up_acc, down_acc = refs[-4:]
    zero = jnp.zeros((), BF16)
    text, text_row = marks_ref[:, 8:9].astype(F32) > 0.0, kind_row(marks_ref)
    act_t, inner_t = act_t_ref[...], inner_t_ref[...]
    grad = grad_ref[:, g * FF_STEP : (g + 1) * FF_STEP]
    lanes = slice(g * 256, (g + 1) * 256)
    cot = jnp.concatenate([cot_own_ref[:, lanes], cot_sib_ref[:, lanes]], axis=0)
    for e in range(2):
        up = mm(act_t, jnp.where(text, grad, zero) if e else jnp.where(text, zero, grad))
        up_acc[e, 0] = up[:, :256]
        up_acc[e, 1] = up[:, 256:]
        down_acc[e] = mm(
            jnp.where(text_row, inner_t, zero) if e else jnp.where(text_row, zero, inner_t), cot)

    for n, target in enumerate((keep_ref, send_ref)):
        def cell(i, carry):
            slot = g * 64 + n * 32 + i
            half = at_slot[192 + slot]
            rows = pl.ds(pl.multiple_of(at_slot[slot], 8), 24)
            below = pl.ds(pl.multiple_of(at_slot[384 + slot], 8), 24)
            target[i] = jnp.concatenate(
                [up_acc[0, half, rows, :], up_acc[1, half, rows, :],
                 down_acc[0, below, :], down_acc[1, below, :]], axis=0).astype(BF16)
            return carry
        lax.fori_loop(0, 32, cell, 0, unroll=4)


def cells(g, table, act_t, grad_pre, inner_t, cot_own, cot_sib, marks, more):
    return pl.pallas_call(
        lambda *refs: cells_kernel(g, *refs),
        in_specs=[SMALL] + [WHOLE] * 6 + ([WHOLE] if g == 0 else [ANYWHERE] * len(more)),
        out_specs=[WHOLE] * (3 if g == 0 else 2),
        out_shape=[jax.ShapeDtypeStruct((32, 96, 256), BF16)] * 2
        + [jax.ShapeDtypeStruct((2 * N, 768), BF16)] * (g == 0),
        scratch_shapes=[pltpu.VMEM((2, 2, 768, 256), F32), pltpu.VMEM((2, 1536, 256), F32)],
        compiler_params=pltpu.CompilerParams(vmem_limit_bytes=10 * 2**20),
        cost_estimate=pl.CostEstimate(
            flops=4 * 2 * 512 * 768 * 512, bytes_accessed=8 * 2**20, transcendentals=0),
        name="cells",
    )(table, act_t, grad_pre, inner_t, cot_own, cot_sib, marks, *more)


def cell_places():
    table = np.zeros((32, 4, 4, 3, 4, 4, 4), np.int32)
    for r, s in np.ndindex(32, 4):
        here = {"z": r // 8, "y": r % 4, "x": (s // 2) * 2 + (r // 4) % 2}
        flips = (0, 1, 3, 2) if s % 2 else (0, 3, 1, 2)
        for g, order in enumerate(ORDERS):
            for slot in np.ndindex(4, 4, 4):
                at = {a: here[a] ^ flips[n] for a, n in zip(order, slot)}
                x_hi, x_lo = at["x"] // 2, at["x"] % 2
                table[(r, s, 0, g) + slot] = 24 * (at["z"] * 8 + x_lo * 4 + at["y"])
                table[(r, s, 1, g) + slot] = x_hi
                table[(r, s, 2, g) + slot] = 24 * (
                    (at["z"] % 2) * 32 + x_lo * 16 + at["y"] * 4 + x_hi * 2 + at["z"] // 2)
                table[(r, s, 3, g) + slot] = at["z"] * 16 + x_lo * 8 + at["y"] * 2 + x_hi
    coordinates = np.array([[n % 2, n % 4 // 2] + [0] * 126 for n in range(128)], np.int32)
    return np.concatenate([table.reshape(128, 768), coordinates], axis=1)


def add_up(parts):
    total = parts[0].astype(F32)
    for part in parts[1:]:
        total = total + part.astype(F32)
    return total.astype(BF16)


def in_hbm(values):
    return list(values)


def pass_kernel(gates, *refs):
    count = (len(refs) - gates) // 3
    for g in range(count):
        refs[2 * count + gates + g][...] = add_up([refs[2 * g][...], refs[2 * g + 1][...]])


ANYWHERE = pl.BlockSpec(memory_space=pl.ANY)


def pass_on(kept, arrived, name, gates=()):
    kept, arrived = ([v[g] for g in (1, 2, 0)] for v in (kept, arrived))
    _, slots, rows, lanes = kept[0].shape
    block = max(slots // 4, 1)
    one = pl.BlockSpec((None, block, rows, lanes), lambda i: (1, i, 0, 0))
    passed = pl.pallas_call(
        lambda *refs: pass_kernel(len(gates), *refs),
        grid=(slots // block,),
        in_specs=[one] * (2 * len(kept)) + [ANYWHERE] * len(gates),
        out_specs=[pl.BlockSpec((block, rows, lanes), lambda i: (i, 0, 0))] * len(kept),
        out_shape=[jax.ShapeDtypeStruct((slots, rows, lanes), BF16)] * len(kept),
        compiler_params=pltpu.CompilerParams(vmem_limit_bytes=6 * 2**20),
        cost_estimate=pl.CostEstimate(
            flops=0, transcendentals=0, bytes_accessed=6 * len(kept) * slots * rows * lanes),
        name=name,
    )(*in_hbm([v for pair in zip(kept, arrived) for v in pair]), *gates)
    return [passed[n] for n in (2, 0, 1)]


def settle_kernel(groups, sizes, *refs):
    ins, outs = refs, refs[-2 * groups :]
    at = 0
    for g in range(groups):
        row = 0
        for size in sizes:
            for half in range(2):
                outs[2 * g + half][:, row : row + size, :] = add_up(
                    [ins[at + k][...] for k in range(3)])
                at += 3
            row += size


def settle(pieces, name, gates=()):
    pieces = [[p[g] for g in (1, 2, 0)] for p in pieces]
    groups = len(pieces[0])
    sizes = [p[0][0].shape[2] for p in pieces]
    _, slots, _, lanes = pieces[0][0][0].shape
    half = slots // 2
    block = max(half // 4, 1)
    steps = half // block
    operands, specs = [], []
    for g in range(groups):
        for p, size in zip(pieces, sizes):
            for h in range(2):
                wide = pl.BlockSpec(
                    (None, block, size, lanes), lambda i, h=h: (0, i + h * steps, 0, 0))
                flat = pl.BlockSpec((block, size, lanes), lambda i, h=h: (i + h * steps, 0, 0))
                operands += list(p[g])
                specs += [wide, wide, flat]
    rows = sum(sizes)
    outs = pl.pallas_call(
        lambda *refs: settle_kernel(groups, sizes, *refs),
        grid=(steps,),
        in_specs=specs + [ANYWHERE] * len(gates),
        out_specs=[pl.BlockSpec((block, rows, lanes), lambda i: (i, 0, 0))] * (2 * groups),
        out_shape=[jax.ShapeDtypeStruct((half, rows, lanes), BF16)] * (2 * groups),
        compiler_params=pltpu.CompilerParams(vmem_limit_bytes=8 * 2**20),
        cost_estimate=pl.CostEstimate(
            flops=0, transcendentals=0, bytes_accessed=8 * groups * slots * rows * lanes),
        name=name,
    )(*operands, *gates)
    shaped = [o.reshape(2, half // 2, rows, lanes) for o in outs]
    return [[shaped[2 * n + h] for n in (2, 0, 1)] for h in range(2)]


def finish_kernel(count, at_ref, *refs):
    outs, down_ref = refs[-5:-1], refs[-1]
    core, far = at_ref[CORE], at_ref[FAR]
    row = lax.broadcasted_iota(jnp.int32, (24, 80), 0)
    column = lax.broadcasted_iota(jnp.int32, (24, 80), 1)
    picks = []
    for n in range(4):
        x_hi, c = far ^ (n // 2), core ^ (n % 2)
        wanted = jnp.where(row == 6, 72, (row // 8) * 24 + x_hi * 12 + c * 6 + row % 8)
        picks.append(jnp.where((column == wanted) & (row % 8 < 6 + (row == 6)), 1.0, 0.0).astype(BF16))
    for g in range(3):
        cell = add_up([refs[3 * g + k][...] for k in range(3)])
        shared = jnp.concatenate([cell[:48], cell[96:]], axis=0)
        for out, pick in zip(outs, picks):
            out[g] = mm(pick, shared).astype(BF16)
        down_ref[g] = cell[48:96]


def finish(table, kept, first, second, gates):
    wide = pl.BlockSpec((None, None, 128, 256), lambda i, t: (0, 0, 0, 0))
    flat = pl.BlockSpec((None, 128, 256), lambda i, t: (0, 0, 0))
    sizes = [24] * 4 + [48]
    return pl.pallas_call(
        lambda *refs: finish_kernel(9, *refs),
        grid_spec=pltpu.PrefetchScalarGridSpec(
            num_scalar_prefetch=1,
            grid=(1,),
            in_specs=[wide, wide, flat] * 3 + [ANYWHERE] * len(gates),
            out_specs=[pl.BlockSpec((3, size, 256), lambda i, t: (0, 0, 0)) for size in sizes],
        ),
        out_shape=[jax.ShapeDtypeStruct((3, size, 256), BF16) for size in sizes],
        compiler_params=pltpu.CompilerParams(vmem_limit_bytes=4 * 2**20),
        name="finish",
    )(table, *[v for g in range(3) for v in (kept[g], first[g], second[g])], *gates)


def after_kernel(values_ref, *refs):
    refs[-1][...] = values_ref[...]


def after(values, gates):
    return pl.pallas_call(
        after_kernel,
        in_specs=[WHOLE] + [ANYWHERE] * len(gates),
        out_specs=WHOLE,
        out_shape=jax.ShapeDtypeStruct(values.shape, values.dtype),
        compiler_params=pltpu.CompilerParams(vmem_limit_bytes=4 * 2**20),
        name="after",
    )(values, *gates)


def put(acc, first, part, rows=slice(None)):
    for n in range(part.shape[1] // 128):
        column = first + n * 128
        lanes = slice(column % 256, column % 256 + 128)
        acc[column // 256, rows, lanes] = part[:, n * 128 : (n + 1) * 128]


def spill_rows(target, acc, at_slot, g, base, extra):
    block = 2 * (g - 1) if g else 0

    def cell(i, carry):
        slot = g * 64 + base + i
        rows = pl.ds(pl.multiple_of(at_slot[slot], 8), 24)
        part = acc[at_slot[192 + slot] + block, rows, :]
        target[i] = jnp.concatenate([part, extra(slot)], axis=0).astype(BF16)
        return carry
    lax.fori_loop(0, 32, cell, 0, unroll=4)


def tail_kernel(at_slot, act_ref, away_ref, q_ref, qb_ref, ka_ref, kb_ref, va_ref, *refs):
    keeps, sends, acc = refs[-5:-3], refs[-3:-1], refs[-1]
    act, away = act_ref[...], away_ref[...]
    near = mm(act, jnp.concatenate(
        [r[: 2 * N, :] for r in (q_ref, qb_ref, ka_ref, kb_ref, va_ref)], axis=1), TN)
    far = mm(away, jnp.concatenate(
        [r[2 * N :, :] for r in (ka_ref, kb_ref, va_ref)], axis=1), TN)
    put(acc, 0, near[:, :384])
    put(acc, 384, near[:, 384:] + far)
    blank = lambda slot: jnp.zeros((8, 256), F32)
    for n in range(2):
        spill_rows(keeps[n], acc, at_slot, n + 1, 0, blank)
        spill_rows(sends[n], acc, at_slot, n + 1, 32, blank)


def tail_cells(table, *operands):
    return pl.pallas_call(
        tail_kernel,
        in_specs=[SMALL] + [WHOLE] * len(operands),
        out_specs=[WHOLE] * 4,
        out_shape=[jax.ShapeDtypeStruct((32, 32, 256), BF16)] * 4,
        scratch_shapes=[pltpu.VMEM((4, 768, 256), F32)],
        compiler_params=pltpu.CompilerParams(vmem_limit_bytes=14 * 2**20),
        cost_estimate=pl.CostEstimate(
            flops=2 * 768 * 512 * (1024 + 640), bytes_accessed=8 * 2**20, transcendentals=0),
        name="tail_cells",
    )(table, *operands)


def inputs_kernel(at_slot, act_ref, away_ref, q_ref, qb_ref, ka_ref, kb_ref, va_ref, vb_ref,
                  att_own_ref, att_sib_ref, proj_ref, own_ref, sib_ref, far_ref, far_sib_ref,
                  second_ref, *refs):
    weights = refs[:3]
    keep_ref, send_ref, cell_keep, cell_send, acc, table = refs[-6:]
    core = at_slot[CORE]
    put(acc, 0, mm(act_ref[...], vb_ref[: 2 * N, :], TN) + mm(away_ref[...], vb_ref[2 * N :, :], TN))
    mine = pl.ds(pl.multiple_of(core * 384, 384), 384)
    other = pl.ds(pl.multiple_of((1 - core) * 384, 384), 384)
    put(acc, 128, mm(att_own_ref[...], proj_ref[...], TN), mine)
    put(acc, 128, mm(att_sib_ref[:N, :], proj_ref[N:, :], TN)
        + mm(att_sib_ref[N:, :], proj_ref[:N, :], TN), other)

    vectors = [jnp.zeros((1, 768), F32)] * 2 + [second_ref[0:1, :], second_ref[1:2, :]]
    wide = list(zip((q_ref, ka_ref, va_ref), (qb_ref, kb_ref, vb_ref), weights))
    for n, ext_ref in enumerate((own_ref, sib_ref, far_ref, far_sib_ref)):
        rows = slice(n * N, (n + 1) * N)
        total = jnp.zeros((N, 768), F32)
        for a_ref, b_ref, w_ref in wide[0 if n < 2 else 1 :]:
            grads = jnp.concatenate([a_ref[rows, :], b_ref[rows, :]], axis=1)
            total += mm(grads, w_ref[...], NT)
        xhat, _ = normalize(ext_ref[:N, :].astype(F32))
        vectors[0] += jnp.sum(total * xhat, axis=0, keepdims=True)
        vectors[1] += jnp.sum(total, axis=0, keepdims=True)
        half = slice((n // 2) * N, (n // 2 + 1) * N)
        if n % 2 == 0:
            keep_ref[half, :] = total
        else:
            send_ref[half, :] = total.astype(BF16)

    chip = lax.broadcasted_iota(jnp.int32, (64, 768), 0)
    owner = lax.broadcasted_iota(jnp.int32, (64, 768), 1) // 12
    feature = lax.broadcasted_iota(jnp.int32, (768, 128), 0) % 12
    lane = lax.broadcasted_iota(jnp.int32, (768, 128), 1)
    spread = jnp.zeros((64, 128), F32)
    for n in range(4):
        line = jnp.broadcast_to(vectors[n], (64, 768))
        values = jnp.where(chip == owner, line, 0.0).astype(BF16)
        spread += mm(values, jnp.where(lane == feature + 12 * n, 1.0, 0.0).astype(BF16))
    table[...] = spread

    def lines(slot):
        row = table[pl.ds(at_slot[576 + slot], 1), :]
        return jnp.concatenate(
            [jnp.broadcast_to(row, (8, 128)), jnp.zeros((8, 128), F32)], axis=1)

    spill_rows(cell_keep, acc, at_slot, 0, 0, lines)
    spill_rows(cell_send, acc, at_slot, 0, 32, lines)


def input_partials(table, operands, gates):
    whole = lambda shape: pl.BlockSpec(shape, lambda i, *_: (0,) * len(shape))
    shapes = [((2 * N, 768), F32), ((2 * N, 768), BF16)] + [((32, 32, 256), BF16)] * 2
    return pl.pallas_call(
        inputs_kernel,
        grid_spec=pltpu.PrefetchScalarGridSpec(
            num_scalar_prefetch=1,
            grid=(1,),
            in_specs=[whole(v.shape) for v in operands[:-1]]
            + [pl.BlockSpec((768, 384), lambda i, at, n=n: (0, 2 * n + at[CORE])) for n in range(3)]
            + [ANYWHERE] * len(gates),
            out_specs=[whole(shape) for shape, _ in shapes],
            scratch_shapes=[pltpu.VMEM((2, 768, 256), F32), pltpu.VMEM((64, 128), F32)],
        ),
        out_shape=[jax.ShapeDtypeStruct(*v) for v in shapes],
        compiler_params=pltpu.CompilerParams(vmem_limit_bytes=16 * 2**20),
        cost_estimate=pl.CostEstimate(
            flops=2 * 768 * 384 * 512 * 7, bytes_accessed=10 * 2**20, transcendentals=0),
        name="input_partials",
    )(table, *operands, *[operands[-1]] * 2, *gates)


def sum_core_kernel(own_ref, sib_ref, *refs):
    refs[-1][...] = (own_ref[...] + sib_ref[...].astype(F32)).astype(BF16)


def sum_core(own, sib, gates):
    half = pl.BlockSpec((N, 768), lambda i: (1, 0))
    return pl.pallas_call(
        sum_core_kernel,
        grid=(1,),
        in_specs=[half, half] + [ANYWHERE] * len(gates),
        out_specs=pl.BlockSpec((N, 768), lambda i: (0, 0)),
        out_shape=jax.ShapeDtypeStruct((N, 768), BF16),
        compiler_params=pltpu.CompilerParams(vmem_limit_bytes=4 * 2**20),
        name="sum_core",
    )(own, sib, *gates)


def token_kernel(tokens_ref, hidden_ref, own_ref, sib_ref, far_ref, gain_ref, out_own_ref,
                 out_sib_ref, grad_ref, out_ref):
    grad = own_ref[...] + sib_ref[...].astype(F32) + far_ref[...].astype(F32)
    xhat, factor = normalize(tokens_ref[...].astype(F32))
    grad_ref[...] = hidden_ref[...] + normalize_back(grad, xhat, factor, wide(gain_ref))
    out_ref[...] = (out_own_ref[...] + out_sib_ref[...].astype(F32)).astype(BF16)


def token_grads(tokens, hidden, own, sib, far, gain, out_own, out_sib):
    half = pl.BlockSpec((N, 768), lambda i: (0, 0))
    return pl.pallas_call(
        token_kernel,
        grid=(1,),
        in_specs=[half] * 5 + [LINE] + [half] * 2,
        out_specs=[half] * 2,
        out_shape=[jax.ShapeDtypeStruct((N, 768), F32), jax.ShapeDtypeStruct((N, 768), BF16)],
        compiler_params=pltpu.CompilerParams(vmem_limit_bytes=8 * 2**20),
        name="token_grads",
    )(tokens, hidden, own, sib, far, gain, out_own, out_sib)


def assemble_kernel(at_ref, own_ref, near_ref, away_ref, cross_ref, down_ref, up_ref, qkv_ref, out_ref,
                    vec_ref, below_ref, held):
    core, far = at_ref[CORE], at_ref[FAR]
    held[far * 2 + core] = own_ref[...]
    held[far * 2 + 1 - core] = near_ref[...]
    held[2 - far * 2 + core] = away_ref[...]
    held[2 - far * 2 + 1 - core] = cross_ref[...]
    line = own_ref[0, :8, :128].astype(F32) + near_ref[0, :8, :128].astype(F32)
    vec_ref[...] = jnp.where(core == 0, line, pltpu.roll(line, 122, 1))
    for x_hi in range(2):
        for c in range(2):
            for g in range(3):
                rows = held[x_hi * 2 + c, g].astype(F32)
                first = c * 1536 + g * 512 + x_hi * 256
                for e in range(2):
                    up_ref[:, e, first : first + 256] = rows[8 * e : 8 * e + 6] * UP_FACTORS[e]
                for n in range(2):
                    at = (g + 2) % 3 * 512 + x_hi * 256 + n * 128
                    kind, within = at // 384, at % 384 + c * 384
                    part = rows[16:22, n * 128 : (n + 1) * 128]
                    if kind < 3:
                        qkv_ref[:, kind * 768 + within : kind * 768 + within + 128] = part
                    else:
                        out_ref[:, within : within + 128] = part
    for g in range(3):
        part = down_ref[g].astype(F32)
        for e in range(2):
            below_ref[e, :, g * 256 : (g + 1) * 256] = part[24 * e : 24 * e + 24] * UP_FACTORS[e]


def assemble(table, *parts):
    return pl.pallas_call(
        assemble_kernel,
        in_specs=[SMALL] + [WHOLE] * 5,
        out_specs=[WHOLE] * 5,
        out_shape=[
            jax.ShapeDtypeStruct((6, 2, 3072), F32),
            jax.ShapeDtypeStruct((6, 2304), F32),
            jax.ShapeDtypeStruct((6, 768), F32),
            jax.ShapeDtypeStruct((8, 128), F32),
            jax.ShapeDtypeStruct((2, 24, 768), F32),
        ],
        scratch_shapes=[pltpu.VMEM((4, 3, 24, 256), BF16)],
        compiler_params=pltpu.CompilerParams(vmem_limit_bytes=4 * 2**20),
        name="assemble",
    )(table, *parts)

def shards(tokens, first_gain, first_shift, w_qkv, w_out, second_gain, second_shift,
           w_up, w_down, modality, segments, partner, cotangent):
    table = lax.dynamic_index_in_dim(
        jnp.asarray(cell_places()), lax.axis_index(BOTH), 0, keepdims=False)

    own = marked(partner, tokens[0], segments, modality)
    away = swap_far(own)
    sib = swap_core(own)
    cot_own = cotangent[0]
    cot_sib = swap_core(cot_own)

    act1, marks, queries, k_near, v_near, qx = project(table, own, sib, first_gain, first_shift, w_qkv, True)
    near_both, near_peak = attend_near(queries, k_near, v_near, qx, marks)
    away_sib = swap_core(after(away, [near_peak]))
    act1_away, marks_away, k_away, v_away = project(table, away, away_sib, first_gain, first_shift, w_qkv, False)
    attended, lse = attend_forward(queries, k_away, v_away, qx, marks_away, near_both, near_peak)
    attended_sib = swap_core(attended)

    hidden, grad_act2, xhat2, factor2, act_t, inner_t, grad_pre = experts(
        table, attended, attended_sib, own, sib, cot_own, cot_sib, marks, second_gain, second_shift, w_out,
        w_up, w_down)
    ff_kept, ff_first, more = [], [], [grad_act2]
    for g in range(3):
        keep, gone, *low = cells(g, table, act_t, grad_pre, inner_t, cot_own, cot_sib, marks, more)
        ff_kept.append(keep.reshape(2, 16, 96, 256))
        ff_first.append(send(gone.reshape(2, 16, 96, 256), axis_step(ORDERS[g][0], True)))
        if g == 0:
            grad_sib = swap_core(low[0])
        more = [keep] if g == 0 else [keep, grad_sib]
    hidden_grad, grad_att, proj_half, vectors = middle(
        table, grad_act2, grad_sib, xhat2, factor2, cot_own, cot_sib, second_gain, w_out)

    def along(stage, first, values):
        sent = {g: send(values[g], axis_step(ORDERS[g][stage], first)) for g in (1, 2, 0)}
        return [sent[g] for g in range(3)]

    taken = (queries, k_near, k_away, v_near, v_away, grad_att, attended, qx, marks, marks_away, lse)
    q_a, k_a, v_a = attend_backward(taken, 0, 2, ())
    q_b, k_b, v_b = attend_backward(taken, 2, 1, ())
    cells_a = tail_cells(table, act1, act1_away, q_a, q_b, k_a, k_b, v_a)
    partial_own, partial_low, *cells_b = input_partials(table, (
        act1, act1_away, q_a, q_b, k_a, k_b, v_a, v_b, attended, attended_sib, proj_half,
        own, sib, away, away_sib, vectors, w_qkv), ())
    kept = [v.reshape(2, 16, 32, 256) for v in (cells_b[0], cells_a[0], cells_a[1])]
    first = along(0, True, [v.reshape(2, 16, 32, 256) for v in (cells_b[1], cells_a[2], cells_a[3])])
    ff_second = along(0, False, pass_on(ff_kept, ff_first, "pass_first", [cells_b[0]]))
    partial_sib = swap_core(partial_low)
    passed = pass_on(kept, first, "pass_tail")
    second = along(0, False, passed)
    out_own, out_sib = branches(table, inner_t, w_down, hidden, marks, passed)

    kept, sent = settle(
        [list(zip(ff_kept, ff_first, ff_second)), list(zip(kept, first, second))], "settle_all", [out_sib])
    first = along(1, True, sent)
    second = along(1, False, pass_on(kept, first, "pass_second"))
    kept, sent = settle([list(zip(kept, first, second))], "settle_second")
    first = along(2, True, sent)
    from_far = swap_far(sum_core(partial_own, partial_sib, first))
    second = along(2, False, pass_on(kept, first, "pass_third"))
    held, *shares, down_held = finish(table, kept, first, second, [from_far])

    near, beyond = swap_core(shares[0]), swap_far(shares[1])
    cross = send(shares[2], lambda x, y, z, c: (x ^ 2, y, z, 1 - c))
    below = send(down_held, lambda x, y, z, c: (x, y, 2 * c + z % 2, z // 2))
    up_grad, qkv_grad, out_grad, line, down_grad = assemble(
        table, held, near, beyond, cross, below)

    token_grad, layer_output = token_grads(
        tokens[0], hidden_grad, partial_own, partial_sib, from_far, first_gain, out_own, swap_core(out_sib))

    return (
        layer_output[None], token_grad[None], line[6, :6], line[6, 12:18], qkv_grad, out_grad,
        line[6, 24:30], line[6, 36:42], up_grad.transpose(1, 0, 2), down_grad)


def solution(mesh):
    cut = P("rows", "seq", None)
    flat = P(BOTH)
    placed = (cut,) + (P(),) * 8 + (P("rows", "seq"), P("rows", "seq"), P("rows", None), cut)
    return jax.shard_map(
        shards, mesh=mesh, in_specs=placed,
        out_specs=(cut, cut, flat, flat, P(BOTH, None), P(BOTH, None), flat, flat,
                   P(None, BOTH, None), P(None, BOTH, None)),
        check_vma=False)
```

```python
import jax
import jax.numpy as jnp
import numpy as np
from jax import lax
from jax.experimental import pallas as pl
from jax.experimental.pallas import tpu as pltpu
from jax.sharding import PartitionSpec as P

HD = 64
OWN = 6
CORE, FAR = 768, 769
IMG = 197
NIMG = 4
BOTH = ("rows", "seq")
F32 = jnp.float32
BF16 = jnp.bfloat16
MASKED = -1e30


def route(step):
    pairs = []
    for r in range(32):
        z, x_lo, y = r // 8, (r // 4) % 2, r % 4
        for s in range(4):
            x, c = (s // 2) * 2 + x_lo, s % 2
            tx, ty, tz, tc = step(x, y, z, c)
            target = (tz * 8 + (tx % 2) * 4 + ty) * 4 + (tx // 2) * 2 + tc
            pairs.append((r * 4 + s, target))
    return pairs


def send(values, step):
    return lax.ppermute(values, BOTH, route(step))


def swap_core(values):
    return send(values, lambda x, y, z, c: (x, y, z, 1 - c))


def swap_far(values):
    return send(values, lambda x, y, z, c: (x ^ 2, y, z, c))


def axis_step(axis, first):
    def step(x, y, z, c):
        flip = 1 if (c == 0) == first else 3
        at = {"x": x, "y": y, "z": z}
        at[axis] ^= flip
        return (at["x"], at["y"], at["z"], c)

    return step


UP_FACTORS = (1024 / (2 * 788), 1024 / (2 * 236))
ORDERS = (("x", "y", "z"), ("y", "z", "x"), ("z", "x", "y"))


def in_hbm(values):
    return pltpu.with_memory_space_constraint(values, pltpu.HBM)


def wide(vector_ref):
    return vector_ref[...].reshape(1, 768)


LINE = pl.BlockSpec((768,), lambda *_: (0,))


def normalize(inputs):
    centred = inputs - jnp.mean(inputs, axis=-1, keepdims=True)
    factor = lax.rsqrt(jnp.mean(centred * centred, axis=-1, keepdims=True) + 1e-05)
    return centred * factor, factor


def normalize_back(grad, xhat, factor, gain):
    gy = grad * gain
    mean_gy = jnp.mean(gy, axis=-1, keepdims=True)
    mean_gx = jnp.mean(gy * xhat, axis=-1, keepdims=True)
    return factor * (gy - mean_gy - xhat * mean_gx)


SMALL = pl.BlockSpec(memory_space=pltpu.SMEM)
WHOLE = pl.BlockSpec(memory_space=pltpu.VMEM)
N = 256


def marked_kernel(partner, tokens_ref, segments_ref, modality_ref, out_ref):
    segments = segments_ref[...]
    tag = jnp.zeros(segments.shape, jnp.int32)
    for n in range(8):
        tag = jnp.where(segments == n, partner[0, n], tag)
    marks = jnp.concatenate(
        [tag, modality_ref[...], jnp.zeros((1, 256), jnp.int32)], axis=1).astype(F32)
    out_ref[:N, :] = tokens_ref[...]
    out_ref[N:, :] = jnp.concatenate([marks, jnp.zeros((15, 768), F32)], axis=0).astype(BF16)


def marked(partner, tokens, segments, modality):
    return pl.pallas_call(
        marked_kernel,
        in_specs=[SMALL, WHOLE, WHOLE, WHOLE],
        out_specs=WHOLE,
        out_shape=jax.ShapeDtypeStruct((N + 16, 768), BF16),
        compiler_params=pltpu.CompilerParams(vmem_limit_bytes=60 * 2**20),
        name="marked",
    )(partner, tokens, segments, modality)


def mark_lanes(ext):
    row = ext[N:, :].astype(F32)
    place = lax.broadcasted_iota(jnp.int32, (128, N), 0)
    tag = jnp.broadcast_to(row[:1, :N], (128, N))
    kind = jnp.broadcast_to(row[:1, N : 2 * N], (128, N))
    hot = jnp.where((place < NIMG) & (place.astype(F32) == tag), 1.0, 0.0)
    return jnp.transpose(jnp.where(place == 8, kind, hot))


def project_kernel(at_ref, near, a_ref, b_ref, gain_ref, shift_ref, *refs):
    count = 3 if near else 2
    weights, outs = refs[:count], refs[count:]
    for n, ext_ref in enumerate((a_ref, b_ref)):
        rows = slice(n * N, (n + 1) * N)
        ext = ext_ref[...]
        xhat, _ = normalize(ext[:N].astype(F32))
        act = (xhat * wide(gain_ref) + wide(shift_ref)).astype(BF16)
        outs[0][rows, :] = act
        marks = mark_lanes(ext)
        outs[1][rows, :] = marks.astype(BF16)
        for m in range(count):
            part = mm(act, weights[m][...])
            outs[2 + m][rows, :] = (0.125 * part if near and m == 0 else part).astype(BF16)
        if near:
            lane = lax.broadcasted_iota(jnp.int32, marks.shape, 1)
            outs[5][rows, :] = jnp.where((lane < NIMG) & (marks == 0.0), MASKED, 0.0).astype(BF16)


def project(table, first, second, gain, shift, w_qkv, near):
    kinds = (0, 1, 2) if near else (1, 2)
    sizes = [768, 128] + [384] * len(kinds) + ([128] if near else [])
    whole = lambda shape: pl.BlockSpec(shape, lambda i, at: (0, 0))
    return pl.pallas_call(
        lambda at_ref, *refs: project_kernel(at_ref, near, *refs),
        grid_spec=pltpu.PrefetchScalarGridSpec(
            num_scalar_prefetch=1,
            grid=(1,),
            in_specs=[whole((N + 16, 768))] * 2 + [LINE] * 2
            + [pl.BlockSpec((768, 384), lambda i, at, n=n: (0, 2 * n + at[CORE])) for n in kinds],
            out_specs=[whole((2 * N, size)) for size in sizes],
        ),
        out_shape=[jax.ShapeDtypeStruct((2 * N, size), BF16) for size in sizes],
        compiler_params=pltpu.CompilerParams(vmem_limit_bytes=6 * 2**20),
        cost_estimate=pl.CostEstimate(
            flops=2 * 512 * 768 * 384 * len(kinds), bytes_accessed=4 * 2**20, transcendentals=0),
        name="project_near" if near else "project_away",
    )(table, first, second, gain, shift, *[w_qkv] * len(kinds))


def middle_kernel(place, grad_ref, sib_ref, xhat_ref, factor_ref, cot_own_ref, cot_sib_ref,
                  gain_ref, w_out_ref, hidden_ref, att_ref, proj_ref, vec_ref):
    core = place[CORE]
    for n, cot_ref in enumerate((cot_own_ref, cot_sib_ref)):
        rows, other = slice(n * N, (n + 1) * N), slice((1 - n) * N, (2 - n) * N)
        grad = grad_ref[rows, :].astype(F32) + sib_ref[other, :].astype(F32)
        xhat = xhat_ref[rows, :].astype(F32)
        total = cot_ref[...].astype(F32) + normalize_back(grad, xhat, factor_ref[rows, :], wide(gain_ref))
        low = total.astype(BF16)
        if n == 0:
            hidden_ref[...] = total
            vec_ref[0:1, :] = jnp.sum(grad * xhat, axis=0, keepdims=True)
            vec_ref[1:2, :] = jnp.sum(grad, axis=0, keepdims=True)
        mine = w_out_ref[pl.ds(pl.multiple_of(core * 384, 384), 384), :]
        att_ref[rows, :] = mm(low, mine, NT).astype(BF16)
        proj_ref[rows, :] = jnp.where(core == 0, low[:, :384], low[:, 384:])


def middle(place, *operands):
    return pl.pallas_call(
        middle_kernel,
        in_specs=[SMALL] + [WHOLE] * len(operands),
        out_specs=[WHOLE] * 4,
        out_shape=[
            jax.ShapeDtypeStruct((N, 768), F32),
            jax.ShapeDtypeStruct((2 * N, 384), BF16),
            jax.ShapeDtypeStruct((2 * N, 384), BF16),
            jax.ShapeDtypeStruct((2, 768), F32),
        ],
        compiler_params=pltpu.CompilerParams(vmem_limit_bytes=6 * 2**20),
        cost_estimate=pl.CostEstimate(
            flops=2 * 512 * 768 * 384, bytes_accessed=8 * 2**20, transcendentals=0),
        name="middle",
    )(place, *operands)


def gelu_parts(pre):
    phi = 0.5 * (1.0 + lax.erf(pre * 0.7071067811865476))
    slope = phi + pre * (0.3989422804014327 * jnp.exp(-0.5 * pre * pre))
    return pre * phi, slope


NT = (((1,), (1,)), ((), ()))
TN = (((0,), (0,)), ((), ()))
NN = (((1,), (0,)), ((), ()))


def mm(left, right, dims=NN):
    return lax.dot_general(left, right, dims, preferred_element_type=F32)


def head_lanes(shape, h):
    lane = lax.broadcasted_iota(jnp.int32, shape, len(shape) - 1)
    return (lane >= HD) == (h == 1)


def turned(values):
    return jnp.transpose(values.astype(F32)).astype(BF16)


def stacked(near_ref, away_ref):
    return jnp.concatenate([near_ref[...], away_ref[...]], axis=0)


def half_attention(q_ref, k_ref, v_ref, qx_ref, x_ref, h, peak_before):
    q_pair = q_ref[...]
    mine = head_lanes(q_pair.shape, 0) if h == 0 else jnp.logical_not(head_lanes(q_pair.shape, 0))
    query = jnp.concatenate([jnp.where(mine, q_pair, 0), qx_ref[...]], axis=1)
    scores = mm(jnp.concatenate([k_ref[...], x_ref[...]], axis=1), query, NT)
    peak = jnp.max(scores, axis=0, keepdims=True)
    if peak_before is not None:
        peak = jnp.maximum(peak, peak_before)
    weights = jnp.exp(scores - peak).astype(BF16)
    values_t = turned(v_ref[...])
    rows = lax.broadcasted_iota(jnp.int32, values_t.shape, 0) < HD
    left = jnp.where(rows, values_t, 1) if h == 0 else jnp.where(rows, 1, values_t)
    return mm(left, weights), peak


def near_kernel(q_ref, k_ref, v_ref, qx_ref, x_ref, both_ref, peak_ref):
    for h in range(2):
        both, peak = half_attention(q_ref, k_ref, v_ref, qx_ref, x_ref, h, None)
        both_ref[0, h] = both
        peak_ref[0, h : h + 1, :] = peak


def forward_kernel(q_ref, k_ref, v_ref, qx_ref, x_ref, both_ref, peak_ref, out_ref, lse_ref):
    mixed = []
    for h in range(2):
        before = peak_ref[0, h : h + 1, :]
        both, peak = half_attention(q_ref, k_ref, v_ref, qx_ref, x_ref, h, before)
        both = both + both_ref[0, h] * jnp.exp(before - peak)
        total = both[127:128, :] if h == 0 else both[0:1, :]
        mixed.append(both * (1.0 / total))
        lse_ref[0, h : h + 1, :] = peak + jnp.log(total)
    rows = lax.broadcasted_iota(jnp.int32, mixed[0].shape, 0) < HD
    out_ref[...] = jnp.transpose(jnp.where(rows, mixed[0], mixed[1])).astype(BF16)


BY_PAIR = pl.BlockSpec((2 * N, 128), lambda p: (0, p))
FIXED = pl.BlockSpec((2 * N, 128), lambda p: (0, 0))


PAIR_LINES = pl.BlockSpec((1, 2, 2 * N), lambda p: (p, 0, 0))
PAIR_BOTH = pl.BlockSpec((1, 2, 128, 2 * N), lambda p: (p, 0, 0, 0))


def attend_near(*operands):
    return pl.pallas_call(
        near_kernel,
        grid=(3,),
        in_specs=[BY_PAIR] * 3 + [FIXED] * 2,
        out_specs=[PAIR_BOTH, PAIR_LINES],
        out_shape=[
            jax.ShapeDtypeStruct((3, 2, 128, 2 * N), F32),
            jax.ShapeDtypeStruct((3, 2, 2 * N), F32),
        ],
        compiler_params=pltpu.CompilerParams(vmem_limit_bytes=8 * 2**20),
        cost_estimate=pl.CostEstimate(
            flops=2 * OWN * 512 * 1024 * 256, bytes_accessed=4 * 2**20,
            transcendentals=OWN * 512 * 512),
        name="attend_near",
    )(*operands)


def attend_forward(*operands):
    return pl.pallas_call(
        forward_kernel,
        grid=(3,),
        in_specs=[BY_PAIR] * 3 + [FIXED] * 2 + [PAIR_BOTH, PAIR_LINES],
        out_specs=[BY_PAIR, PAIR_LINES],
        out_shape=[
            jax.ShapeDtypeStruct((2 * N, 384), BF16),
            jax.ShapeDtypeStruct((3, 2, 2 * N), F32),
        ],
        compiler_params=pltpu.CompilerParams(vmem_limit_bytes=8 * 2**20),
        cost_estimate=pl.CostEstimate(
            flops=2 * OWN * 512 * 1024 * 256, bytes_accessed=5 * 2**20,
            transcendentals=OWN * 512 * 512),
        name="attend_forward",
    )(*operands)


def backward_kernel(q_ref, kn_ref, ka_ref, vn_ref, va_ref, do_ref, o_ref, qx_ref, xn_ref, xa_ref,
                    lse_ref, *refs):
    dq_ref, dk_ref, dv_ref = refs[-3:]
    k_pair, values = stacked(kn_ref, ka_ref), stacked(vn_ref, va_ref)
    keys = jnp.concatenate([k_pair, stacked(xn_ref, xa_ref)], axis=1)
    q_pair, grads = q_ref[...], do_ref[...]
    lanes = head_lanes(q_pair.shape, 0)
    product = grads.astype(F32) * o_ref[...].astype(F32)
    k_turned = turned(k_pair)
    rows = lax.broadcasted_iota(jnp.int32, (128, 2 * N), 0) < HD
    dq = jnp.zeros((128, 2 * N), F32)
    dk = jnp.zeros(k_pair.shape, F32)
    dv = jnp.zeros(k_pair.shape, F32)
    for h in range(2):
        mine = lanes if h == 0 else jnp.logical_not(lanes)
        q_head = jnp.where(mine, q_pair, 0)
        g_head = jnp.where(mine, grads, 0)
        dot_row = jnp.transpose(jnp.sum(jnp.where(mine, product, 0.0), axis=1, keepdims=True))
        scores = mm(keys, jnp.concatenate([q_head, qx_ref[...]], axis=1), NT)
        prob = jnp.exp(scores - lse_ref[0, h : h + 1, :])
        dv += mm(prob.astype(BF16), g_head)
        grad_prob = mm(values, g_head, NT)
        grad_scores = (prob * (grad_prob - dot_row)).astype(BF16)
        dk += mm(grad_scores, q_head)
        part = mm(k_turned, grad_scores)
        dq += jnp.where(rows if h == 0 else jnp.logical_not(rows), part, 0.0)
    dq_ref[...] = jnp.transpose(dq).astype(BF16) * jnp.asarray(0.125, BF16)
    dk_ref[...] = dk.astype(BF16)
    dv_ref[...] = dv.astype(BF16)


def attend_backward(operands, first, pairs, gates):
    by_pair = pl.BlockSpec((2 * N, 128), lambda p: (0, first + p))
    sizes = (2 * N, 4 * N, 4 * N)
    return pl.pallas_call(
        backward_kernel,
        grid=(pairs,),
        in_specs=[by_pair] * 7 + [FIXED] * 3
        + [pl.BlockSpec((1, 2, 2 * N), lambda p: (first + p, 0, 0))]
        + [pl.BlockSpec(memory_space=pl.ANY)] * len(gates),
        out_specs=[pl.BlockSpec((size, 128), lambda p: (0, p)) for size in sizes],
        out_shape=[jax.ShapeDtypeStruct((size, pairs * 128), BF16) for size in sizes],
        compiler_params=pltpu.CompilerParams(vmem_limit_bytes=10 * 2**20),
        cost_estimate=pl.CostEstimate(
            flops=2 * 5 * 2 * pairs * 512 * 1024 * 256, bytes_accessed=6 * 2**20,
            transcendentals=2 * pairs * 512 * 1024),
        name="attend_backward",
    )(*operands, *gates)


FF_STEP = 512
E_STEP = 512
EXPERT_MB = 40
CELLS_MB = 28


def expert_kernel(at_ref, att_own_ref, att_sib_ref, own_ref, sib_ref, cot_own_ref, cot_sib_ref,
                  marks_ref, gain_ref, shift_ref, w_out_ref, wu_ref, wd_ref,
                  hidden_ref, low_ref, xhat_ref, factor_ref, act_t_ref, inner_t_ref, slope_ref,
                  act_acc, grad_acc):
    f = pl.program_id(0)
    core = at_ref[CORE]

    @pl.when(f == 0)
    def _():
        mine = w_out_ref[pl.ds(pl.multiple_of(core * 384, 384), 384), :]
        other = w_out_ref[pl.ds(pl.multiple_of((1 - core) * 384, 384), 384), :]
        for n, ext_ref in enumerate((own_ref, sib_ref)):
            rows, theirs = slice(n * N, (n + 1) * N), slice((1 - n) * N, (2 - n) * N)
            hidden = ext_ref[:N, :].astype(F32) + (
                mm(att_own_ref[rows, :], mine) + mm(att_sib_ref[theirs, :], other))
            xhat, factor = normalize(hidden)
            xhat_ref[rows, :] = xhat.astype(BF16)
            factor_ref[rows, :] = factor
            act = xhat * wide(gain_ref) + wide(shift_ref)
            act_acc[rows, :] = act.astype(BF16)
            act_t_ref[:, rows] = jnp.transpose(act).astype(BF16)
            if n == 0:
                hidden_ref[...] = hidden
        grad_acc[...] = jnp.zeros(grad_acc.shape, F32)

    act = act_acc[...]
    cot = jnp.concatenate([cot_own_ref[...], cot_sib_ref[...]], axis=0)
    text = marks_ref[:, 8:9].astype(F32) > 0.0
    pre = jnp.where(text, mm(act, wu_ref[1]), mm(act, wu_ref[0]))
    inner, slope = gelu_parts(pre)
    grad_pre = jnp.where(text, mm(cot, wd_ref[1], NT), mm(cot, wd_ref[0], NT)) * slope
    inner_t_ref[...] = jnp.transpose(inner).astype(BF16)
    low = grad_pre.astype(BF16)
    slope_ref[...] = low
    zero = jnp.zeros((), BF16)
    grad_acc[...] += (mm(jnp.where(text, zero, low), wu_ref[0], NT)
                      + mm(jnp.where(text, low, zero), wu_ref[1], NT))

    @pl.when(f == pl.num_programs(0) - 1)
    def _():
        low_ref[...] = grad_acc[...].astype(BF16)


def experts(core, *operands):
    steps = 1536 // E_STEP
    shapes = [((N, 768), F32), ((2 * N, 768), BF16), ((2 * N, 768), BF16), ((2 * N, 1), F32),
              ((768, 2 * N), BF16)]
    fixed = lambda shape: pl.BlockSpec(shape, lambda f, *_: (0,) * len(shape))
    return pl.pallas_call(
        expert_kernel,
        grid_spec=pltpu.PrefetchScalarGridSpec(
            num_scalar_prefetch=1,
            grid=(steps,),
            in_specs=[fixed(v.shape) for v in operands[:-2]] + [
                pl.BlockSpec((2, 768, E_STEP), lambda f, at: (0, 0, at[CORE] * steps + f)),
                pl.BlockSpec((2, E_STEP, 768), lambda f, at: (0, at[CORE] * steps + f, 0)),
            ],
            out_specs=[fixed(shape) for shape, _ in shapes] + [
                pl.BlockSpec((E_STEP, 2 * N), lambda f, at: (f, 0)),
                pl.BlockSpec((2 * N, E_STEP), lambda f, at: (0, f)),
            ],
            scratch_shapes=[pltpu.VMEM((2 * N, 768), BF16), pltpu.VMEM((2 * N, 768), F32)],
        ),
        out_shape=[jax.ShapeDtypeStruct(*v) for v in shapes] + [
            jax.ShapeDtypeStruct((1536, 2 * N), BF16),
            jax.ShapeDtypeStruct((2 * N, 1536), BF16)],
        compiler_params=pltpu.CompilerParams(
            vmem_limit_bytes=18 * 2**20, dimension_semantics=("arbitrary",)),
        cost_estimate=pl.CostEstimate(
            flops=6 * 2 * 512 * 768 * 1536 + 2 * 512 * 768 * 768, bytes_accessed=22 * 2**20,
            transcendentals=2 * 512 * 1536),
        name="experts",
    )(core, *operands)


def kind_row(marks_ref):
    return turned(marks_ref[...])[8:9, :].astype(F32) > 0.0


def branch_kernel(at_ref, inner_t_ref, wd_ref, hidden_ref, marks_ref, *refs):
    own_ref, sib_ref, acc = refs[-3:]
    f = pl.program_id(0)
    text, inner_t, zero = kind_row(marks_ref), inner_t_ref[...], jnp.zeros((), BF16)
    part = (mm(jnp.where(text, zero, inner_t), wd_ref[0], TN)
            + mm(jnp.where(text, inner_t, zero), wd_ref[1], TN))

    @pl.when(f == 0)
    def _():
        acc[...] = part

    @pl.when(f > 0)
    def _():
        acc[...] += part

    @pl.when(f == pl.num_programs(0) - 1)
    def _():
        own_ref[...] = hidden_ref[...] + acc[:N, :]
        sib_ref[...] = acc[N:, :].astype(BF16)


def branches(table, inner_t, w_down, hidden, marks, gates):
    return pl.pallas_call(
        branch_kernel,
        grid_spec=pltpu.PrefetchScalarGridSpec(
            num_scalar_prefetch=1,
            grid=(3,),
            in_specs=[
                pl.BlockSpec((512, 2 * N), lambda f, at: (f, 0)),
                pl.BlockSpec((2, 512, 768), lambda f, at: (0, at[CORE] * 3 + f, 0)),
                pl.BlockSpec((N, 768), lambda f, at: (0, 0)),
                pl.BlockSpec((2 * N, 128), lambda f, at: (0, 0))] + [ANYWHERE] * len(gates),
            out_specs=[pl.BlockSpec((N, 768), lambda f, at: (0, 0))] * 2,
            scratch_shapes=[pltpu.VMEM((2 * N, 768), F32)],
        ),
        out_shape=[jax.ShapeDtypeStruct((N, 768), F32), jax.ShapeDtypeStruct((N, 768), BF16)],
        compiler_params=pltpu.CompilerParams(
            vmem_limit_bytes=20 * 2**20, dimension_semantics=("arbitrary",)),
        cost_estimate=pl.CostEstimate(
            flops=2 * 2 * 512 * 768 * 1536, bytes_accessed=8 * 2**20, transcendentals=0),
        name="branches",
    )(table, inner_t, w_down, hidden, marks, *gates)


def cells_kernel(g, at_slot, act_t_ref, grad_ref, inner_t_ref, cot_own_ref, cot_sib_ref, marks_ref,
                 *refs):
    if g == 0:
        full_ref, keep_ref, send_ref, low_ref, up_acc, down_acc = refs
        low_ref[...] = full_ref[...]
    else:
        keep_ref, send_ref, up_acc, down_acc = refs[-4:]
    zero = jnp.zeros((), BF16)
    text, text_row = marks_ref[:, 8:9].astype(F32) > 0.0, kind_row(marks_ref)
    act_t, inner_t = act_t_ref[...], inner_t_ref[...]
    grad = grad_ref[:, g * FF_STEP : (g + 1) * FF_STEP]
    lanes = slice(g * 256, (g + 1) * 256)
    cot = jnp.concatenate([cot_own_ref[:, lanes], cot_sib_ref[:, lanes]], axis=0)
    for e in range(2):
        up = mm(act_t, jnp.where(text, grad, zero) if e else jnp.where(text, zero, grad))
        up_acc[e, 0] = up[:, :256]
        up_acc[e, 1] = up[:, 256:]
        down_acc[e] = mm(
            jnp.where(text_row, inner_t, zero) if e else jnp.where(text_row, zero, inner_t), cot)

    for n, target in enumerate((keep_ref, send_ref)):
        def cell(i, carry):
            slot = g * 64 + n * 32 + i
            half = at_slot[192 + slot]
            rows = pl.ds(pl.multiple_of(at_slot[slot], 8), 24)
            below = pl.ds(pl.multiple_of(at_slot[384 + slot], 8), 24)
            target[i] = jnp.concatenate(
                [up_acc[0, half, rows, :], up_acc[1, half, rows, :],
                 down_acc[0, below, :], down_acc[1, below, :]], axis=0).astype(BF16)
            return carry
        lax.fori_loop(0, 32, cell, 0, unroll=4)


def cells(g, table, act_t, grad_pre, inner_t, cot_own, cot_sib, marks, more):
    return pl.pallas_call(
        lambda *refs: cells_kernel(g, *refs),
        in_specs=[SMALL] + [WHOLE] * 6 + ([WHOLE] if g == 0 else [ANYWHERE] * len(more)),
        out_specs=[WHOLE] * (3 if g == 0 else 2),
        out_shape=[jax.ShapeDtypeStruct((32, 96, 256), BF16)] * 2
        + [jax.ShapeDtypeStruct((2 * N, 768), BF16)] * (g == 0),
        scratch_shapes=[pltpu.VMEM((2, 2, 768, 256), F32), pltpu.VMEM((2, 1536, 256), F32)],
        compiler_params=pltpu.CompilerParams(vmem_limit_bytes=10 * 2**20),
        cost_estimate=pl.CostEstimate(
            flops=4 * 2 * 512 * 768 * 512, bytes_accessed=8 * 2**20, transcendentals=0),
        name="cells",
    )(table, act_t, grad_pre, inner_t, cot_own, cot_sib, marks, *more)


def cell_places():
    table = np.zeros((32, 4, 4, 3, 4, 4, 4), np.int32)
    for r, s in np.ndindex(32, 4):
        here = {"z": r // 8, "y": r % 4, "x": (s // 2) * 2 + (r // 4) % 2}
        flips = (0, 1, 3, 2) if s % 2 else (0, 3, 1, 2)
        for g, order in enumerate(ORDERS):
            for slot in np.ndindex(4, 4, 4):
                at = {a: here[a] ^ flips[n] for a, n in zip(order, slot)}
                x_hi, x_lo = at["x"] // 2, at["x"] % 2
                table[(r, s, 0, g) + slot] = 24 * (at["z"] * 8 + x_lo * 4 + at["y"])
                table[(r, s, 1, g) + slot] = x_hi
                table[(r, s, 2, g) + slot] = 24 * (
                    (at["z"] % 2) * 32 + x_lo * 16 + at["y"] * 4 + x_hi * 2 + at["z"] // 2)
                table[(r, s, 3, g) + slot] = at["z"] * 16 + x_lo * 8 + at["y"] * 2 + x_hi
    coordinates = np.array([[n % 2, n % 4 // 2] + [0] * 126 for n in range(128)], np.int32)
    return np.concatenate([table.reshape(128, 768), coordinates], axis=1)


def add_up(parts):
    total = parts[0].astype(F32)
    for part in parts[1:]:
        total = total + part.astype(F32)
    return total.astype(BF16)


def pass_kernel(gates, *refs):
    count = (len(refs) - gates) // 3
    for g in range(count):
        refs[2 * count + gates + g][...] = add_up([refs[2 * g][...], refs[2 * g + 1][...]])


ANYWHERE = pl.BlockSpec(memory_space=pl.ANY)


def pass_on(kept, arrived, name, gates=()):
    kept, arrived = ([v[g] for g in (1, 2, 0)] for v in (kept, arrived))
    _, slots, rows, lanes = kept[0].shape
    block = max(slots // 4, 1)
    one = pl.BlockSpec((None, block, rows, lanes), lambda i: (1, i, 0, 0))
    passed = pl.pallas_call(
        lambda *refs: pass_kernel(len(gates), *refs),
        grid=(slots // block,),
        in_specs=[one] * (2 * len(kept)) + [ANYWHERE] * len(gates),
        out_specs=[pl.BlockSpec((block, rows, lanes), lambda i: (i, 0, 0))] * len(kept),
        out_shape=[jax.ShapeDtypeStruct((slots, rows, lanes), BF16)] * len(kept),
        compiler_params=pltpu.CompilerParams(vmem_limit_bytes=6 * 2**20),
        cost_estimate=pl.CostEstimate(
            flops=0, transcendentals=0, bytes_accessed=6 * len(kept) * slots * rows * lanes),
        name=name,
    )(*[v for pair in zip(kept, arrived) for v in pair], *gates)
    return [passed[n] for n in (2, 0, 1)]


def settle_kernel(groups, sizes, *refs):
    ins, outs = refs, refs[-2 * groups :]
    at = 0
    for g in range(groups):
        row = 0
        for size in sizes:
            for half in range(2):
                outs[2 * g + half][:, row : row + size, :] = add_up(
                    [ins[at + k][...] for k in range(3)])
                at += 3
            row += size


def settle(pieces, name, gates=()):
    pieces = [[p[g] for g in (1, 2, 0)] for p in pieces]
    groups = len(pieces[0])
    sizes = [p[0][0].shape[2] for p in pieces]
    _, slots, _, lanes = pieces[0][0][0].shape
    half = slots // 2
    block = max(half // 4, 1)
    steps = half // block
    operands, specs = [], []
    for g in range(groups):
        for p, size in zip(pieces, sizes):
            for h in range(2):
                wide = pl.BlockSpec(
                    (None, block, size, lanes), lambda i, h=h: (0, i + h * steps, 0, 0))
                flat = pl.BlockSpec((block, size, lanes), lambda i, h=h: (i + h * steps, 0, 0))
                operands += list(p[g])
                specs += [wide, wide, flat]
    rows = sum(sizes)
    outs = pl.pallas_call(
        lambda *refs: settle_kernel(groups, sizes, *refs),
        grid=(steps,),
        in_specs=specs + [ANYWHERE] * len(gates),
        out_specs=[pl.BlockSpec((block, rows, lanes), lambda i: (i, 0, 0))] * (2 * groups),
        out_shape=[jax.ShapeDtypeStruct((half, rows, lanes), BF16)] * (2 * groups),
        compiler_params=pltpu.CompilerParams(vmem_limit_bytes=8 * 2**20),
        cost_estimate=pl.CostEstimate(
            flops=0, transcendentals=0, bytes_accessed=8 * groups * slots * rows * lanes),
        name=name,
    )(*operands, *gates)
    shaped = [o.reshape(2, half // 2, rows, lanes) for o in outs]
    return [[shaped[2 * n + h] for n in (2, 0, 1)] for h in range(2)]


def finish_kernel(count, at_ref, *refs):
    outs, down_ref = refs[-5:-1], refs[-1]
    core, far = at_ref[CORE], at_ref[FAR]
    row = lax.broadcasted_iota(jnp.int32, (24, 80), 0)
    column = lax.broadcasted_iota(jnp.int32, (24, 80), 1)
    picks = []
    for n in range(4):
        x_hi, c = far ^ (n // 2), core ^ (n % 2)
        wanted = jnp.where(row == 6, 72, (row // 8) * 24 + x_hi * 12 + c * 6 + row % 8)
        picks.append(jnp.where((column == wanted) & (row % 8 < 6 + (row == 6)), 1.0, 0.0).astype(BF16))
    for g in range(3):
        cell = add_up([refs[3 * g + k][...] for k in range(3)])
        shared = jnp.concatenate([cell[:48], cell[96:]], axis=0)
        for out, pick in zip(outs, picks):
            out[g] = mm(pick, shared).astype(BF16)
        down_ref[g] = cell[48:96]


def finish(table, kept, first, second, gates):
    wide = pl.BlockSpec((None, None, 128, 256), lambda i, t: (0, 0, 0, 0))
    flat = pl.BlockSpec((None, 128, 256), lambda i, t: (0, 0, 0))
    sizes = [24] * 4 + [48]
    return pl.pallas_call(
        lambda *refs: finish_kernel(9, *refs),
        grid_spec=pltpu.PrefetchScalarGridSpec(
            num_scalar_prefetch=1,
            grid=(1,),
            in_specs=[wide, wide, flat] * 3 + [ANYWHERE] * len(gates),
            out_specs=[pl.BlockSpec((3, size, 256), lambda i, t: (0, 0, 0)) for size in sizes],
        ),
        out_shape=[jax.ShapeDtypeStruct((3, size, 256), BF16) for size in sizes],
        compiler_params=pltpu.CompilerParams(vmem_limit_bytes=4 * 2**20),
        name="finish",
    )(table, *[v for g in range(3) for v in (kept[g], first[g], second[g])], *gates)


def after_kernel(values_ref, *refs):
    refs[-1][...] = values_ref[...]


def after(values, gates):
    return pl.pallas_call(
        after_kernel,
        in_specs=[WHOLE] + [ANYWHERE] * len(gates),
        out_specs=WHOLE,
        out_shape=jax.ShapeDtypeStruct(values.shape, values.dtype),
        compiler_params=pltpu.CompilerParams(vmem_limit_bytes=4 * 2**20),
        name="after",
    )(values, *gates)


def put(acc, first, part, rows=slice(None)):
    for n in range(part.shape[1] // 128):
        column = first + n * 128
        lanes = slice(column % 256, column % 256 + 128)
        acc[column // 256, rows, lanes] = part[:, n * 128 : (n + 1) * 128]


def spill_rows(target, acc, at_slot, g, base, extra):
    block = 2 * (g - 1) if g else 0

    def cell(i, carry):
        slot = g * 64 + base + i
        rows = pl.ds(pl.multiple_of(at_slot[slot], 8), 24)
        part = acc[at_slot[192 + slot] + block, rows, :]
        target[i] = jnp.concatenate([part, extra(slot)], axis=0).astype(BF16)
        return carry
    lax.fori_loop(0, 32, cell, 0, unroll=4)


def tail_kernel(at_slot, act_ref, away_ref, q_ref, qb_ref, ka_ref, kb_ref, va_ref, *refs):
    keeps, sends, acc = refs[-5:-3], refs[-3:-1], refs[-1]
    act, away = act_ref[...], away_ref[...]
    near = mm(act, jnp.concatenate(
        [r[: 2 * N, :] for r in (q_ref, qb_ref, ka_ref, kb_ref, va_ref)], axis=1), TN)
    far = mm(away, jnp.concatenate(
        [r[2 * N :, :] for r in (ka_ref, kb_ref, va_ref)], axis=1), TN)
    put(acc, 0, near[:, :384])
    put(acc, 384, near[:, 384:] + far)
    blank = lambda slot: jnp.zeros((8, 256), F32)
    for n in range(2):
        spill_rows(keeps[n], acc, at_slot, n + 1, 0, blank)
        spill_rows(sends[n], acc, at_slot, n + 1, 32, blank)


def tail_cells(table, *operands):
    return pl.pallas_call(
        tail_kernel,
        in_specs=[SMALL] + [WHOLE] * len(operands),
        out_specs=[WHOLE] * 4,
        out_shape=[jax.ShapeDtypeStruct((32, 32, 256), BF16)] * 4,
        scratch_shapes=[pltpu.VMEM((4, 768, 256), F32)],
        compiler_params=pltpu.CompilerParams(vmem_limit_bytes=14 * 2**20),
        cost_estimate=pl.CostEstimate(
            flops=2 * 768 * 512 * (1024 + 640), bytes_accessed=8 * 2**20, transcendentals=0),
        name="tail_cells",
    )(table, *operands)


def inputs_kernel(at_slot, act_ref, away_ref, q_ref, qb_ref, ka_ref, kb_ref, va_ref, vb_ref,
                  att_own_ref, att_sib_ref, proj_ref, own_ref, sib_ref, far_ref, far_sib_ref,
                  second_ref, *refs):
    weights = refs[:3]
    keep_ref, send_ref, cell_keep, cell_send, acc, table = refs[-6:]
    core = at_slot[CORE]
    put(acc, 0, mm(act_ref[...], vb_ref[: 2 * N, :], TN) + mm(away_ref[...], vb_ref[2 * N :, :], TN))
    mine = pl.ds(pl.multiple_of(core * 384, 384), 384)
    other = pl.ds(pl.multiple_of((1 - core) * 384, 384), 384)
    put(acc, 128, mm(att_own_ref[...], proj_ref[...], TN), mine)
    put(acc, 128, mm(att_sib_ref[:N, :], proj_ref[N:, :], TN)
        + mm(att_sib_ref[N:, :], proj_ref[:N, :], TN), other)

    vectors = [jnp.zeros((1, 768), F32)] * 2 + [second_ref[0:1, :], second_ref[1:2, :]]
    wide = list(zip((q_ref, ka_ref, va_ref), (qb_ref, kb_ref, vb_ref), weights))
    for n, ext_ref in enumerate((own_ref, sib_ref, far_ref, far_sib_ref)):
        rows = slice(n * N, (n + 1) * N)
        total = jnp.zeros((N, 768), F32)
        for a_ref, b_ref, w_ref in wide[0 if n < 2 else 1 :]:
            grads = jnp.concatenate([a_ref[rows, :], b_ref[rows, :]], axis=1)
            total += mm(grads, w_ref[...], NT)
        xhat, _ = normalize(ext_ref[:N, :].astype(F32))
        vectors[0] += jnp.sum(total * xhat, axis=0, keepdims=True)
        vectors[1] += jnp.sum(total, axis=0, keepdims=True)
        half = slice((n // 2) * N, (n // 2 + 1) * N)
        if n % 2 == 0:
            keep_ref[half, :] = total
        else:
            send_ref[half, :] = total.astype(BF16)

    chip = lax.broadcasted_iota(jnp.int32, (64, 768), 0)
    owner = lax.broadcasted_iota(jnp.int32, (64, 768), 1) // 12
    feature = lax.broadcasted_iota(jnp.int32, (768, 128), 0) % 12
    lane = lax.broadcasted_iota(jnp.int32, (768, 128), 1)
    spread = jnp.zeros((64, 128), F32)
    for n in range(4):
        line = jnp.broadcast_to(vectors[n], (64, 768))
        values = jnp.where(chip == owner, line, 0.0).astype(BF16)
        spread += mm(values, jnp.where(lane == feature + 12 * n, 1.0, 0.0).astype(BF16))
    table[...] = spread

    def lines(slot):
        row = table[pl.ds(at_slot[576 + slot], 1), :]
        return jnp.concatenate(
            [jnp.broadcast_to(row, (8, 128)), jnp.zeros((8, 128), F32)], axis=1)

    spill_rows(cell_keep, acc, at_slot, 0, 0, lines)
    spill_rows(cell_send, acc, at_slot, 0, 32, lines)


def input_partials(table, operands, gates):
    whole = lambda shape: pl.BlockSpec(shape, lambda i, *_: (0,) * len(shape))
    shapes = [((2 * N, 768), F32), ((2 * N, 768), BF16)] + [((32, 32, 256), BF16)] * 2
    return pl.pallas_call(
        inputs_kernel,
        grid_spec=pltpu.PrefetchScalarGridSpec(
            num_scalar_prefetch=1,
            grid=(1,),
            in_specs=[whole(v.shape) for v in operands[:-1]]
            + [pl.BlockSpec((768, 384), lambda i, at, n=n: (0, 2 * n + at[CORE])) for n in range(3)]
            + [ANYWHERE] * len(gates),
            out_specs=[whole(shape) for shape, _ in shapes],
            scratch_shapes=[pltpu.VMEM((2, 768, 256), F32), pltpu.VMEM((64, 128), F32)],
        ),
        out_shape=[jax.ShapeDtypeStruct(*v) for v in shapes],
        compiler_params=pltpu.CompilerParams(vmem_limit_bytes=16 * 2**20),
        cost_estimate=pl.CostEstimate(
            flops=2 * 768 * 384 * 512 * 7, bytes_accessed=10 * 2**20, transcendentals=0),
        name="input_partials",
    )(table, *operands, *[operands[-1]] * 2, *gates)


def sum_core_kernel(own_ref, sib_ref, *refs):
    refs[-1][...] = (own_ref[...] + sib_ref[...].astype(F32)).astype(BF16)


def sum_core(own, sib, gates):
    half = pl.BlockSpec((N, 768), lambda i: (1, 0))
    return pl.pallas_call(
        sum_core_kernel,
        grid=(1,),
        in_specs=[half, half] + [ANYWHERE] * len(gates),
        out_specs=pl.BlockSpec((N, 768), lambda i: (0, 0)),
        out_shape=jax.ShapeDtypeStruct((N, 768), BF16),
        compiler_params=pltpu.CompilerParams(vmem_limit_bytes=4 * 2**20),
        name="sum_core",
    )(own, sib, *gates)


def token_kernel(tokens_ref, hidden_ref, own_ref, sib_ref, far_ref, gain_ref, out_own_ref,
                 out_sib_ref, grad_ref, out_ref):
    grad = own_ref[...] + sib_ref[...].astype(F32) + far_ref[...].astype(F32)
    xhat, factor = normalize(tokens_ref[...].astype(F32))
    grad_ref[...] = hidden_ref[...] + normalize_back(grad, xhat, factor, wide(gain_ref))
    out_ref[...] = (out_own_ref[...] + out_sib_ref[...].astype(F32)).astype(BF16)


def token_grads(tokens, hidden, own, sib, far, gain, out_own, out_sib):
    half = pl.BlockSpec((N, 768), lambda i: (0, 0))
    return pl.pallas_call(
        token_kernel,
        grid=(1,),
        in_specs=[half] * 5 + [LINE] + [half] * 2,
        out_specs=[half] * 2,
        out_shape=[jax.ShapeDtypeStruct((N, 768), F32), jax.ShapeDtypeStruct((N, 768), BF16)],
        compiler_params=pltpu.CompilerParams(vmem_limit_bytes=8 * 2**20),
        name="token_grads",
    )(tokens, hidden, own, sib, far, gain, out_own, out_sib)


def assemble_kernel(at_ref, own_ref, near_ref, away_ref, cross_ref, down_ref, up_ref, qkv_ref, out_ref,
                    vec_ref, below_ref, held):
    core, far = at_ref[CORE], at_ref[FAR]
    held[far * 2 + core] = own_ref[...]
    held[far * 2 + 1 - core] = near_ref[...]
    held[2 - far * 2 + core] = away_ref[...]
    held[2 - far * 2 + 1 - core] = cross_ref[...]
    line = own_ref[0, :8, :128].astype(F32) + near_ref[0, :8, :128].astype(F32)
    vec_ref[...] = jnp.where(core == 0, line, pltpu.roll(line, 122, 1))
    for x_hi in range(2):
        for c in range(2):
            for g in range(3):
                rows = held[x_hi * 2 + c, g].astype(F32)
                first = c * 1536 + g * 512 + x_hi * 256
                for e in range(2):
                    up_ref[:, e, first : first + 256] = rows[8 * e : 8 * e + 6] * UP_FACTORS[e]
                for n in range(2):
                    at = (g + 2) % 3 * 512 + x_hi * 256 + n * 128
                    kind, within = at // 384, at % 384 + c * 384
                    part = rows[16:22, n * 128 : (n + 1) * 128]
                    if kind < 3:
                        qkv_ref[:, kind * 768 + within : kind * 768 + within + 128] = part
                    else:
                        out_ref[:, within : within + 128] = part
    for g in range(3):
        part = down_ref[g].astype(F32)
        for e in range(2):
            below_ref[e, :, g * 256 : (g + 1) * 256] = part[24 * e : 24 * e + 24] * UP_FACTORS[e]


def assemble(table, *parts):
    return pl.pallas_call(
        assemble_kernel,
        in_specs=[SMALL] + [WHOLE] * 5,
        out_specs=[WHOLE] * 5,
        out_shape=[
            jax.ShapeDtypeStruct((6, 2, 3072), F32),
            jax.ShapeDtypeStruct((6, 2304), F32),
            jax.ShapeDtypeStruct((6, 768), F32),
            jax.ShapeDtypeStruct((8, 128), F32),
            jax.ShapeDtypeStruct((2, 24, 768), F32),
        ],
        scratch_shapes=[pltpu.VMEM((4, 3, 24, 256), BF16)],
        compiler_params=pltpu.CompilerParams(vmem_limit_bytes=4 * 2**20),
        name="assemble",
    )(table, *parts)

def shards(tokens, first_gain, first_shift, w_qkv, w_out, second_gain, second_shift,
           w_up, w_down, modality, segments, partner, cotangent):
    table = lax.dynamic_index_in_dim(
        jnp.asarray(cell_places()), lax.axis_index(BOTH), 0, keepdims=False)

    own = marked(partner, tokens[0], segments, modality)
    away = swap_far(own)
    sib = swap_core(own)
    cot_own = cotangent[0]
    cot_sib = swap_core(cot_own)

    act1, marks, queries, k_near, v_near, qx = project(
        table, own, sib, first_gain, first_shift, in_hbm(w_qkv), True)
    near_both, near_peak = attend_near(queries, k_near, v_near, qx, marks)
    away_sib = swap_core(after(away, [near_peak]))
    act1_away, marks_away, k_away, v_away = project(table, away, away_sib, first_gain, first_shift, w_qkv, False)
    attended, lse = attend_forward(queries, k_away, v_away, qx, marks_away, near_both, near_peak)
    attended_sib = swap_core(attended)

    hidden, grad_act2, xhat2, factor2, act_t, inner_t, grad_pre = experts(
        table, attended, attended_sib, own, sib, cot_own, cot_sib, marks, second_gain, second_shift, w_out,
        in_hbm(w_up), in_hbm(w_down))
    ff_kept, ff_first, more = [], [], [grad_act2]
    for g in range(3):
        keep, gone, *low = cells(g, table, act_t, grad_pre, inner_t, cot_own, cot_sib, marks, more)
        ff_kept.append(keep.reshape(2, 16, 96, 256))
        ff_first.append(send(gone.reshape(2, 16, 96, 256), axis_step(ORDERS[g][0], True)))
        if g == 0:
            grad_sib = swap_core(low[0])
        more = [keep] if g == 0 else [keep, grad_sib]
    hidden_grad, grad_att, proj_half, vectors = middle(
        table, grad_act2, grad_sib, xhat2, factor2, cot_own, cot_sib, second_gain, w_out)

    def along(stage, first, values):
        sent = {g: send(values[g], axis_step(ORDERS[g][stage], first)) for g in (1, 2, 0)}
        return [sent[g] for g in range(3)]

    taken = (queries, k_near, k_away, v_near, v_away, grad_att, attended, qx, marks, marks_away, lse)
    q_a, k_a, v_a = attend_backward(taken, 0, 2, ())
    q_b, k_b, v_b = attend_backward(taken, 2, 1, ())
    cells_a = tail_cells(table, act1, act1_away, q_a, q_b, k_a, k_b, v_a)
    partial_own, partial_low, *cells_b = input_partials(table, (
        act1, act1_away, q_a, q_b, k_a, k_b, v_a, v_b, attended, attended_sib, proj_half,
        own, sib, away, away_sib, vectors, w_qkv), ())
    kept = [v.reshape(2, 16, 32, 256) for v in (cells_b[0], cells_a[0], cells_a[1])]
    first = along(0, True, [v.reshape(2, 16, 32, 256) for v in (cells_b[1], cells_a[2], cells_a[3])])
    ff_second = along(0, False, pass_on(ff_kept, ff_first, "pass_first", [cells_b[0]]))
    partial_sib = swap_core(partial_low)
    passed = pass_on(kept, first, "pass_tail")
    second = along(0, False, passed)
    out_own, out_sib = branches(table, inner_t, w_down, hidden, marks, passed)

    kept, sent = settle(
        [list(zip(ff_kept, ff_first, ff_second)), list(zip(kept, first, second))], "settle_all", [out_sib])
    first = along(1, True, sent)
    second = along(1, False, pass_on(kept, first, "pass_second"))
    kept, sent = settle([list(zip(kept, first, second))], "settle_second")
    first = along(2, True, sent)
    from_far = swap_far(sum_core(partial_own, partial_sib, first))
    second = along(2, False, pass_on(kept, first, "pass_third"))
    held, *shares, down_held = finish(table, kept, first, second, [from_far])

    near, beyond = swap_core(shares[0]), swap_far(shares[1])
    cross = send(shares[2], lambda x, y, z, c: (x ^ 2, y, z, 1 - c))
    below = send(down_held, lambda x, y, z, c: (x, y, 2 * c + z % 2, z // 2))
    up_grad, qkv_grad, out_grad, line, down_grad = assemble(
        table, held, near, beyond, cross, below)

    token_grad, layer_output = token_grads(
        tokens[0], hidden_grad, partial_own, partial_sib, from_far, first_gain, out_own, swap_core(out_sib))

    return (
        layer_output[None], token_grad[None], line[6, :6], line[6, 12:18], qkv_grad, out_grad,
        line[6, 24:30], line[6, 36:42], up_grad.transpose(1, 0, 2), down_grad)


def solution(mesh):
    cut = P("rows", "seq", None)
    flat = P(BOTH)
    placed = (cut,) + (P(),) * 8 + (P("rows", "seq"), P("rows", "seq"), P("rows", None), cut)
    return jax.shard_map(
        shards, mesh=mesh, in_specs=placed,
        out_specs=(cut, cut, flat, flat, P(BOTH, None), P(BOTH, None), flat, flat,
                   P(None, BOTH, None), P(None, BOTH, None)),
        check_vma=False)
```

```python
import jax
import jax.numpy as jnp
import numpy as np
from jax import lax
from jax.experimental import pallas as pl
from jax.experimental.pallas import tpu as pltpu
from jax.sharding import PartitionSpec as P

HD = 64
OWN = 6
CORE, FAR = 768, 769
IMG = 197
NIMG = 4
BOTH = ("rows", "seq")
F32 = jnp.float32
BF16 = jnp.bfloat16
MASKED = -1e30


def route(step):
    pairs = []
    for r in range(32):
        z, x_lo, y = r // 8, (r // 4) % 2, r % 4
        for s in range(4):
            x, c = (s // 2) * 2 + x_lo, s % 2
            tx, ty, tz, tc = step(x, y, z, c)
            target = (tz * 8 + (tx % 2) * 4 + ty) * 4 + (tx // 2) * 2 + tc
            pairs.append((r * 4 + s, target))
    return pairs


def send(values, step):
    return lax.ppermute(values, BOTH, route(step))


def swap_core(values):
    return send(values, lambda x, y, z, c: (x, y, z, 1 - c))


def swap_far(values):
    return send(values, lambda x, y, z, c: (x ^ 2, y, z, c))


def axis_step(axis, first):
    def step(x, y, z, c):
        flip = 1 if (c == 0) == first else 3
        at = {"x": x, "y": y, "z": z}
        at[axis] ^= flip
        return (at["x"], at["y"], at["z"], c)

    return step


UP_FACTORS = (1024 / (2 * 788), 1024 / (2 * 236))
ORDERS = (("x", "y", "z"), ("y", "z", "x"), ("z", "x", "y"))


def in_hbm(values):
    return pltpu.with_memory_space_constraint(values, pltpu.HBM)


def wide(vector_ref):
    return vector_ref[...].reshape(1, 768)


LINE = pl.BlockSpec((768,), lambda *_: (0,))


def normalize(inputs):
    centred = inputs - jnp.mean(inputs, axis=-1, keepdims=True)
    factor = lax.rsqrt(jnp.mean(centred * centred, axis=-1, keepdims=True) + 1e-05)
    return centred * factor, factor


def normalize_back(grad, xhat, factor, gain):
    gy = grad * gain
    mean_gy = jnp.mean(gy, axis=-1, keepdims=True)
    mean_gx = jnp.mean(gy * xhat, axis=-1, keepdims=True)
    return factor * (gy - mean_gy - xhat * mean_gx)


SMALL = pl.BlockSpec(memory_space=pltpu.SMEM)
WHOLE = pl.BlockSpec(memory_space=pltpu.VMEM)
N = 256


def marked_kernel(partner, tokens_ref, segments_ref, modality_ref, out_ref):
    segments = segments_ref[...]
    tag = jnp.zeros(segments.shape, jnp.int32)
    for n in range(8):
        tag = jnp.where(segments == n, partner[0, n], tag)
    marks = jnp.concatenate(
        [tag, modality_ref[...], jnp.zeros((1, 256), jnp.int32)], axis=1).astype(F32)
    out_ref[:N, :] = tokens_ref[...]
    out_ref[N:, :] = jnp.concatenate([marks, jnp.zeros((15, 768), F32)], axis=0).astype(BF16)


def marked(partner, tokens, segments, modality):
    return pl.pallas_call(
        marked_kernel,
        in_specs=[SMALL, WHOLE, WHOLE, WHOLE],
        out_specs=WHOLE,
        out_shape=jax.ShapeDtypeStruct((N + 16, 768), BF16),
        compiler_params=pltpu.CompilerParams(vmem_limit_bytes=60 * 2**20),
        name="marked",
    )(partner, tokens, segments, modality)


def mark_lanes(ext):
    row = ext[N:, :].astype(F32)
    place = lax.broadcasted_iota(jnp.int32, (128, N), 0)
    tag = jnp.broadcast_to(row[:1, :N], (128, N))
    kind = jnp.broadcast_to(row[:1, N : 2 * N], (128, N))
    hot = jnp.where((place < NIMG) & (place.astype(F32) == tag), 1.0, 0.0)
    return jnp.transpose(jnp.where(place == 8, kind, hot))


def project_kernel(at_ref, near, a_ref, b_ref, gain_ref, shift_ref, *refs):
    count = 3 if near else 2
    weights, outs = refs[:count], refs[count:]
    for n, ext_ref in enumerate((a_ref, b_ref)):
        rows = slice(n * N, (n + 1) * N)
        ext = ext_ref[...]
        xhat, _ = normalize(ext[:N].astype(F32))
        act = (xhat * wide(gain_ref) + wide(shift_ref)).astype(BF16)
        outs[0][rows, :] = act
        marks = mark_lanes(ext)
        outs[1][rows, :] = marks.astype(BF16)
        for m in range(count):
            part = mm(act, weights[m][...])
            outs[2 + m][rows, :] = (0.125 * part if near and m == 0 else part).astype(BF16)
        if near:
            lane = lax.broadcasted_iota(jnp.int32, marks.shape, 1)
            outs[5][rows, :] = jnp.where((lane < NIMG) & (marks == 0.0), MASKED, 0.0).astype(BF16)


def project(table, first, second, gain, shift, w_qkv, near):
    kinds = (0, 1, 2) if near else (1, 2)
    sizes = [768, 128] + [384] * len(kinds) + ([128] if near else [])
    whole = lambda shape: pl.BlockSpec(shape, lambda i, at: (0, 0))
    return pl.pallas_call(
        lambda at_ref, *refs: project_kernel(at_ref, near, *refs),
        grid_spec=pltpu.PrefetchScalarGridSpec(
            num_scalar_prefetch=1,
            grid=(1,),
            in_specs=[whole((N + 16, 768))] * 2 + [LINE] * 2
            + [pl.BlockSpec((768, 384), lambda i, at, n=n: (0, 2 * n + at[CORE])) for n in kinds],
            out_specs=[whole((2 * N, size)) for size in sizes],
        ),
        out_shape=[jax.ShapeDtypeStruct((2 * N, size), BF16) for size in sizes],
        compiler_params=pltpu.CompilerParams(vmem_limit_bytes=6 * 2**20),
        cost_estimate=pl.CostEstimate(
            flops=2 * 512 * 768 * 384 * len(kinds), bytes_accessed=4 * 2**20, transcendentals=0),
        name="project_near" if near else "project_away",
    )(table, first, second, gain, shift, *[w_qkv] * len(kinds))


def middle_kernel(place, grad_ref, sib_ref, xhat_ref, factor_ref, cot_own_ref, cot_sib_ref,
                  gain_ref, w_out_ref, hidden_ref, att_ref, proj_ref, vec_ref):
    core = place[CORE]
    for n, cot_ref in enumerate((cot_own_ref, cot_sib_ref)):
        rows, other = slice(n * N, (n + 1) * N), slice((1 - n) * N, (2 - n) * N)
        grad = grad_ref[rows, :].astype(F32) + sib_ref[other, :].astype(F32)
        xhat = xhat_ref[rows, :].astype(F32)
        total = cot_ref[...].astype(F32) + normalize_back(grad, xhat, factor_ref[rows, :], wide(gain_ref))
        low = total.astype(BF16)
        if n == 0:
            hidden_ref[...] = total
            vec_ref[0:1, :] = jnp.sum(grad * xhat, axis=0, keepdims=True)
            vec_ref[1:2, :] = jnp.sum(grad, axis=0, keepdims=True)
        mine = w_out_ref[pl.ds(pl.multiple_of(core * 384, 384), 384), :]
        att_ref[rows, :] = mm(low, mine, NT).astype(BF16)
        proj_ref[rows, :] = jnp.where(core == 0, low[:, :384], low[:, 384:])


def middle(place, *operands):
    return pl.pallas_call(
        middle_kernel,
        in_specs=[SMALL] + [WHOLE] * len(operands),
        out_specs=[WHOLE] * 4,
        out_shape=[
            jax.ShapeDtypeStruct((N, 768), F32),
            jax.ShapeDtypeStruct((2 * N, 384), BF16),
            jax.ShapeDtypeStruct((2 * N, 384), BF16),
            jax.ShapeDtypeStruct((2, 768), F32),
        ],
        compiler_params=pltpu.CompilerParams(vmem_limit_bytes=6 * 2**20),
        cost_estimate=pl.CostEstimate(
            flops=2 * 512 * 768 * 384, bytes_accessed=8 * 2**20, transcendentals=0),
        name="middle",
    )(place, *operands)


def gelu_parts(pre):
    phi = 0.5 * (1.0 + lax.erf(pre * 0.7071067811865476))
    slope = phi + pre * (0.3989422804014327 * jnp.exp(-0.5 * pre * pre))
    return pre * phi, slope


NT = (((1,), (1,)), ((), ()))
TN = (((0,), (0,)), ((), ()))
NN = (((1,), (0,)), ((), ()))


def mm(left, right, dims=NN):
    return lax.dot_general(left, right, dims, preferred_element_type=F32)


def head_lanes(shape, h):
    lane = lax.broadcasted_iota(jnp.int32, shape, len(shape) - 1)
    return (lane >= HD) == (h == 1)


def turned(values):
    return jnp.transpose(values.astype(F32)).astype(BF16)


def stacked(near_ref, away_ref):
    return jnp.concatenate([near_ref[...], away_ref[...]], axis=0)


def half_attention(q_ref, k_ref, v_ref, qx_ref, x_ref, h, peak_before):
    q_pair = q_ref[...]
    mine = head_lanes(q_pair.shape, 0) if h == 0 else jnp.logical_not(head_lanes(q_pair.shape, 0))
    query = jnp.concatenate([jnp.where(mine, q_pair, 0), qx_ref[...]], axis=1)
    scores = mm(jnp.concatenate([k_ref[...], x_ref[...]], axis=1), query, NT)
    peak = jnp.max(scores, axis=0, keepdims=True)
    if peak_before is not None:
        peak = jnp.maximum(peak, peak_before)
    weights = jnp.exp(scores - peak).astype(BF16)
    values_t = turned(v_ref[...])
    rows = lax.broadcasted_iota(jnp.int32, values_t.shape, 0) < HD
    left = jnp.where(rows, values_t, 1) if h == 0 else jnp.where(rows, 1, values_t)
    return mm(left, weights), peak


def near_kernel(q_ref, k_ref, v_ref, qx_ref, x_ref, both_ref, peak_ref):
    for h in range(2):
        both, peak = half_attention(q_ref, k_ref, v_ref, qx_ref, x_ref, h, None)
        both_ref[0, h] = both
        peak_ref[0, h : h + 1, :] = peak


def forward_kernel(q_ref, k_ref, v_ref, qx_ref, x_ref, both_ref, peak_ref, out_ref, lse_ref):
    mixed = []
    for h in range(2):
        before = peak_ref[0, h : h + 1, :]
        both, peak = half_attention(q_ref, k_ref, v_ref, qx_ref, x_ref, h, before)
        both = both + both_ref[0, h] * jnp.exp(before - peak)
        total = both[127:128, :] if h == 0 else both[0:1, :]
        mixed.append(both * (1.0 / total))
        lse_ref[0, h : h + 1, :] = peak + jnp.log(total)
    rows = lax.broadcasted_iota(jnp.int32, mixed[0].shape, 0) < HD
    out_ref[...] = jnp.transpose(jnp.where(rows, mixed[0], mixed[1])).astype(BF16)


BY_PAIR = pl.BlockSpec((2 * N, 128), lambda p: (0, p))
FIXED = pl.BlockSpec((2 * N, 128), lambda p: (0, 0))


PAIR_LINES = pl.BlockSpec((1, 2, 2 * N), lambda p: (p, 0, 0))
PAIR_BOTH = pl.BlockSpec((1, 2, 128, 2 * N), lambda p: (p, 0, 0, 0))


def attend_near(*operands):
    return pl.pallas_call(
        near_kernel,
        grid=(3,),
        in_specs=[BY_PAIR] * 3 + [FIXED] * 2,
        out_specs=[PAIR_BOTH, PAIR_LINES],
        out_shape=[
            jax.ShapeDtypeStruct((3, 2, 128, 2 * N), F32),
            jax.ShapeDtypeStruct((3, 2, 2 * N), F32),
        ],
        compiler_params=pltpu.CompilerParams(vmem_limit_bytes=8 * 2**20),
        cost_estimate=pl.CostEstimate(
            flops=2 * OWN * 512 * 1024 * 256, bytes_accessed=4 * 2**20,
            transcendentals=OWN * 512 * 512),
        name="attend_near",
    )(*operands)


def attend_forward(*operands):
    return pl.pallas_call(
        forward_kernel,
        grid=(3,),
        in_specs=[BY_PAIR] * 3 + [FIXED] * 2 + [PAIR_BOTH, PAIR_LINES],
        out_specs=[BY_PAIR, PAIR_LINES],
        out_shape=[
            jax.ShapeDtypeStruct((2 * N, 384), BF16),
            jax.ShapeDtypeStruct((3, 2, 2 * N), F32),
        ],
        compiler_params=pltpu.CompilerParams(vmem_limit_bytes=8 * 2**20),
        cost_estimate=pl.CostEstimate(
            flops=2 * OWN * 512 * 1024 * 256, bytes_accessed=5 * 2**20,
            transcendentals=OWN * 512 * 512),
        name="attend_forward",
    )(*operands)


def backward_kernel(q_ref, kn_ref, ka_ref, vn_ref, va_ref, do_ref, o_ref, qx_ref, xn_ref, xa_ref,
                    lse_ref, *refs):
    dq_ref, dk_ref, dv_ref = refs[-3:]
    k_pair, values = stacked(kn_ref, ka_ref), stacked(vn_ref, va_ref)
    keys = jnp.concatenate([k_pair, stacked(xn_ref, xa_ref)], axis=1)
    q_pair, grads = q_ref[...], do_ref[...]
    lanes = head_lanes(q_pair.shape, 0)
    product = grads.astype(F32) * o_ref[...].astype(F32)
    k_turned = turned(k_pair)
    rows = lax.broadcasted_iota(jnp.int32, (128, 2 * N), 0) < HD
    dq = jnp.zeros((128, 2 * N), F32)
    dk = jnp.zeros(k_pair.shape, F32)
    dv = jnp.zeros(k_pair.shape, F32)
    for h in range(2):
        mine = lanes if h == 0 else jnp.logical_not(lanes)
        q_head = jnp.where(mine, q_pair, 0)
        g_head = jnp.where(mine, grads, 0)
        dot_row = jnp.transpose(jnp.sum(jnp.where(mine, product, 0.0), axis=1, keepdims=True))
        scores = mm(keys, jnp.concatenate([q_head, qx_ref[...]], axis=1), NT)
        prob = jnp.exp(scores - lse_ref[0, h : h + 1, :])
        dv += mm(prob.astype(BF16), g_head)
        grad_prob = mm(values, g_head, NT)
        grad_scores = (prob * (grad_prob - dot_row)).astype(BF16)
        dk += mm(grad_scores, q_head)
        part = mm(k_turned, grad_scores)
        dq += jnp.where(rows if h == 0 else jnp.logical_not(rows), part, 0.0)
    dq_ref[...] = jnp.transpose(dq).astype(BF16) * jnp.asarray(0.125, BF16)
    dk_ref[...] = dk.astype(BF16)
    dv_ref[...] = dv.astype(BF16)


def attend_backward(operands, first, pairs, gates):
    by_pair = pl.BlockSpec((2 * N, 128), lambda p: (0, first + p))
    sizes = (2 * N, 4 * N, 4 * N)
    return pl.pallas_call(
        backward_kernel,
        grid=(pairs,),
        in_specs=[by_pair] * 7 + [FIXED] * 3
        + [pl.BlockSpec((1, 2, 2 * N), lambda p: (first + p, 0, 0))]
        + [pl.BlockSpec(memory_space=pl.ANY)] * len(gates),
        out_specs=[pl.BlockSpec((size, 128), lambda p: (0, p)) for size in sizes],
        out_shape=[jax.ShapeDtypeStruct((size, pairs * 128), BF16) for size in sizes],
        compiler_params=pltpu.CompilerParams(vmem_limit_bytes=10 * 2**20),
        cost_estimate=pl.CostEstimate(
            flops=2 * 5 * 2 * pairs * 512 * 1024 * 256, bytes_accessed=6 * 2**20,
            transcendentals=2 * pairs * 512 * 1024),
        name="attend_backward",
    )(*operands, *gates)


FF_STEP = 512
E_STEP = 512
EXPERT_MB = 40
CELLS_MB = 28


def expert_kernel(at_ref, att_own_ref, att_sib_ref, own_ref, sib_ref, cot_own_ref, cot_sib_ref,
                  marks_ref, gain_ref, shift_ref, w_out_ref, wu_ref, wd_ref,
                  hidden_ref, low_ref, xhat_ref, factor_ref, act_t_ref, inner_t_ref, slope_ref,
                  act_acc, grad_acc):
    f = pl.program_id(0)
    core = at_ref[CORE]

    @pl.when(f == 0)
    def _():
        mine = w_out_ref[pl.ds(pl.multiple_of(core * 384, 384), 384), :]
        other = w_out_ref[pl.ds(pl.multiple_of((1 - core) * 384, 384), 384), :]
        for n, ext_ref in enumerate((own_ref, sib_ref)):
            rows, theirs = slice(n * N, (n + 1) * N), slice((1 - n) * N, (2 - n) * N)
            hidden = ext_ref[:N, :].astype(F32) + (
                mm(att_own_ref[rows, :], mine) + mm(att_sib_ref[theirs, :], other))
            xhat, factor = normalize(hidden)
            xhat_ref[rows, :] = xhat.astype(BF16)
            factor_ref[rows, :] = factor
            act = xhat * wide(gain_ref) + wide(shift_ref)
            act_acc[rows, :] = act.astype(BF16)
            act_t_ref[:, rows] = jnp.transpose(act).astype(BF16)
            if n == 0:
                hidden_ref[...] = hidden
        grad_acc[...] = jnp.zeros(grad_acc.shape, F32)

    act = act_acc[...]
    cot = jnp.concatenate([cot_own_ref[...], cot_sib_ref[...]], axis=0)
    text = marks_ref[:, 8:9].astype(F32) > 0.0
    pre = jnp.where(text, mm(act, wu_ref[1]), mm(act, wu_ref[0]))
    inner, slope = gelu_parts(pre)
    grad_pre = jnp.where(text, mm(cot, wd_ref[1], NT), mm(cot, wd_ref[0], NT)) * slope
    inner_t_ref[...] = jnp.transpose(inner).astype(BF16)
    low = grad_pre.astype(BF16)
    slope_ref[...] = low
    zero = jnp.zeros((), BF16)
    grad_acc[...] += (mm(jnp.where(text, zero, low), wu_ref[0], NT)
                      + mm(jnp.where(text, low, zero), wu_ref[1], NT))

    @pl.when(f == pl.num_programs(0) - 1)
    def _():
        low_ref[...] = grad_acc[...].astype(BF16)


def experts(core, *operands):
    steps = 1536 // E_STEP
    shapes = [((N, 768), F32), ((2 * N, 768), BF16), ((2 * N, 768), BF16), ((2 * N, 1), F32),
              ((768, 2 * N), BF16)]
    fixed = lambda shape: pl.BlockSpec(shape, lambda f, *_: (0,) * len(shape))
    return pl.pallas_call(
        expert_kernel,
        grid_spec=pltpu.PrefetchScalarGridSpec(
            num_scalar_prefetch=1,
            grid=(steps,),
            in_specs=[fixed(v.shape) for v in operands[:-2]] + [
                pl.BlockSpec((2, 768, E_STEP), lambda f, at: (0, 0, at[CORE] * steps + f)),
                pl.BlockSpec((2, E_STEP, 768), lambda f, at: (0, at[CORE] * steps + f, 0)),
            ],
            out_specs=[fixed(shape) for shape, _ in shapes] + [
                pl.BlockSpec((E_STEP, 2 * N), lambda f, at: (f, 0)),
                pl.BlockSpec((2 * N, E_STEP), lambda f, at: (0, f)),
            ],
            scratch_shapes=[pltpu.VMEM((2 * N, 768), BF16), pltpu.VMEM((2 * N, 768), F32)],
        ),
        out_shape=[jax.ShapeDtypeStruct(*v) for v in shapes] + [
            jax.ShapeDtypeStruct((1536, 2 * N), BF16),
            jax.ShapeDtypeStruct((2 * N, 1536), BF16)],
        compiler_params=pltpu.CompilerParams(
            vmem_limit_bytes=18 * 2**20, dimension_semantics=("arbitrary",)),
        cost_estimate=pl.CostEstimate(
            flops=6 * 2 * 512 * 768 * 1536 + 2 * 512 * 768 * 768, bytes_accessed=22 * 2**20,
            transcendentals=2 * 512 * 1536),
        name="experts",
    )(core, *operands)


def kind_row(marks_ref):
    return turned(marks_ref[...])[8:9, :].astype(F32) > 0.0


def branch_kernel(at_ref, inner_t_ref, wd_ref, hidden_ref, marks_ref, *refs):
    own_ref, sib_ref, acc = refs[-3:]
    f = pl.program_id(0)
    text, inner_t, zero = kind_row(marks_ref), inner_t_ref[...], jnp.zeros((), BF16)
    part = (mm(jnp.where(text, zero, inner_t), wd_ref[0], TN)
            + mm(jnp.where(text, inner_t, zero), wd_ref[1], TN))

    @pl.when(f == 0)
    def _():
        acc[...] = part

    @pl.when(f > 0)
    def _():
        acc[...] += part

    @pl.when(f == pl.num_programs(0) - 1)
    def _():
        own_ref[...] = hidden_ref[...] + acc[:N, :]
        sib_ref[...] = acc[N:, :].astype(BF16)


def branches(table, inner_t, w_down, hidden, marks, gates):
    return pl.pallas_call(
        branch_kernel,
        grid_spec=pltpu.PrefetchScalarGridSpec(
            num_scalar_prefetch=1,
            grid=(3,),
            in_specs=[
                pl.BlockSpec((512, 2 * N), lambda f, at: (f, 0)),
                pl.BlockSpec((2, 512, 768), lambda f, at: (0, at[CORE] * 3 + f, 0)),
                pl.BlockSpec((N, 768), lambda f, at: (0, 0)),
                pl.BlockSpec((2 * N, 128), lambda f, at: (0, 0))] + [ANYWHERE] * len(gates),
            out_specs=[pl.BlockSpec((N, 768), lambda f, at: (0, 0))] * 2,
            scratch_shapes=[pltpu.VMEM((2 * N, 768), F32)],
        ),
        out_shape=[jax.ShapeDtypeStruct((N, 768), F32), jax.ShapeDtypeStruct((N, 768), BF16)],
        compiler_params=pltpu.CompilerParams(
            vmem_limit_bytes=20 * 2**20, dimension_semantics=("arbitrary",)),
        cost_estimate=pl.CostEstimate(
            flops=2 * 2 * 512 * 768 * 1536, bytes_accessed=8 * 2**20, transcendentals=0),
        name="branches",
    )(table, inner_t, w_down, hidden, marks, *gates)


def cells_kernel(g, at_slot, act_t_ref, grad_ref, inner_t_ref, cot_own_ref, cot_sib_ref, marks_ref,
                 *refs):
    if g == 0:
        full_ref, keep_ref, send_ref, low_ref, up_acc, down_acc = refs
        low_ref[...] = full_ref[...]
    else:
        keep_ref, send_ref, up_acc, down_acc = refs[-4:]
    zero = jnp.zeros((), BF16)
    text, text_row = marks_ref[:, 8:9].astype(F32) > 0.0, kind_row(marks_ref)
    act_t, inner_t = act_t_ref[...], inner_t_ref[...]
    grad = grad_ref[:, g * FF_STEP : (g + 1) * FF_STEP]
    lanes = slice(g * 256, (g + 1) * 256)
    cot = jnp.concatenate([cot_own_ref[:, lanes], cot_sib_ref[:, lanes]], axis=0)
    for e in range(2):
        up = mm(act_t, jnp.where(text, grad, zero) if e else jnp.where(text, zero, grad))
        up_acc[e, 0] = up[:, :256]
        up_acc[e, 1] = up[:, 256:]
        down_acc[e] = mm(
            jnp.where(text_row, inner_t, zero) if e else jnp.where(text_row, zero, inner_t), cot)

    for n, target in enumerate((keep_ref, send_ref)):
        def cell(i, carry):
            slot = g * 64 + n * 32 + i
            half = at_slot[192 + slot]
            rows = pl.ds(pl.multiple_of(at_slot[slot], 8), 24)
            below = pl.ds(pl.multiple_of(at_slot[384 + slot], 8), 24)
            target[i] = jnp.concatenate(
                [up_acc[0, half, rows, :], up_acc[1, half, rows, :],
                 down_acc[0, below, :], down_acc[1, below, :]], axis=0).astype(BF16)
            return carry
        lax.fori_loop(0, 32, cell, 0, unroll=4)


def cells(g, table, act_t, grad_pre, inner_t, cot_own, cot_sib, marks, more):
    return pl.pallas_call(
        lambda *refs: cells_kernel(g, *refs),
        in_specs=[SMALL] + [WHOLE] * 6 + ([WHOLE] if g == 0 else [ANYWHERE] * len(more)),
        out_specs=[WHOLE] * (3 if g == 0 else 2),
        out_shape=[jax.ShapeDtypeStruct((32, 96, 256), BF16)] * 2
        + [jax.ShapeDtypeStruct((2 * N, 768), BF16)] * (g == 0),
        scratch_shapes=[pltpu.VMEM((2, 2, 768, 256), F32), pltpu.VMEM((2, 1536, 256), F32)],
        compiler_params=pltpu.CompilerParams(vmem_limit_bytes=10 * 2**20),
        cost_estimate=pl.CostEstimate(
            flops=4 * 2 * 512 * 768 * 512, bytes_accessed=8 * 2**20, transcendentals=0),
        name="cells",
    )(table, act_t, grad_pre, inner_t, cot_own, cot_sib, marks, *more)


def cell_places():
    table = np.zeros((32, 4, 4, 3, 4, 4, 4), np.int32)
    for r, s in np.ndindex(32, 4):
        here = {"z": r // 8, "y": r % 4, "x": (s // 2) * 2 + (r // 4) % 2}
        flips = (0, 1, 3, 2) if s % 2 else (0, 3, 1, 2)
        for g, order in enumerate(ORDERS):
            for slot in np.ndindex(4, 4, 4):
                at = {a: here[a] ^ flips[n] for a, n in zip(order, slot)}
                x_hi, x_lo = at["x"] // 2, at["x"] % 2
                table[(r, s, 0, g) + slot] = 24 * (at["z"] * 8 + x_lo * 4 + at["y"])
                table[(r, s, 1, g) + slot] = x_hi
                table[(r, s, 2, g) + slot] = 24 * (
                    (at["z"] % 2) * 32 + x_lo * 16 + at["y"] * 4 + x_hi * 2 + at["z"] // 2)
                table[(r, s, 3, g) + slot] = at["z"] * 16 + x_lo * 8 + at["y"] * 2 + x_hi
    coordinates = np.array([[n % 2, n % 4 // 2] + [0] * 126 for n in range(128)], np.int32)
    return np.concatenate([table.reshape(128, 768), coordinates], axis=1)


def add_up(parts):
    total = parts[0].astype(F32)
    for part in parts[1:]:
        total = total + part.astype(F32)
    return total.astype(BF16)


def pass_kernel(gates, *refs):
    count = (len(refs) - gates) // 3
    for g in range(count):
        refs[2 * count + gates + g][...] = add_up([refs[2 * g][...], refs[2 * g + 1][...]])


ANYWHERE = pl.BlockSpec(memory_space=pl.ANY)


def pass_on(kept, arrived, name, gates=()):
    kept, arrived = ([v[g] for g in (1, 2, 0)] for v in (kept, arrived))
    _, slots, rows, lanes = kept[0].shape
    block = max(slots // 4, 1)
    one = pl.BlockSpec((None, block, rows, lanes), lambda i: (1, i, 0, 0))
    passed = pl.pallas_call(
        lambda *refs: pass_kernel(len(gates), *refs),
        grid=(slots // block,),
        in_specs=[one] * (2 * len(kept)) + [ANYWHERE] * len(gates),
        out_specs=[pl.BlockSpec((block, rows, lanes), lambda i: (i, 0, 0))] * len(kept),
        out_shape=[jax.ShapeDtypeStruct((slots, rows, lanes), BF16)] * len(kept),
        compiler_params=pltpu.CompilerParams(vmem_limit_bytes=6 * 2**20),
        cost_estimate=pl.CostEstimate(
            flops=0, transcendentals=0, bytes_accessed=6 * len(kept) * slots * rows * lanes),
        name=name,
    )(*[v for pair in zip(kept, arrived) for v in pair], *gates)
    return [passed[n] for n in (2, 0, 1)]


def settle_kernel(groups, sizes, *refs):
    ins, outs = refs, refs[-2 * groups :]
    at = 0
    for g in range(groups):
        row = 0
        for size in sizes:
            for half in range(2):
                outs[2 * g + half][:, row : row + size, :] = add_up(
                    [ins[at + k][...] for k in range(3)])
                at += 3
            row += size


def settle(pieces, name, gates=()):
    pieces = [[p[g] for g in (1, 2, 0)] for p in pieces]
    groups = len(pieces[0])
    sizes = [p[0][0].shape[2] for p in pieces]
    _, slots, _, lanes = pieces[0][0][0].shape
    half = slots // 2
    block = max(half // 4, 1)
    steps = half // block
    operands, specs = [], []
    for g in range(groups):
        for p, size in zip(pieces, sizes):
            for h in range(2):
                wide = pl.BlockSpec(
                    (None, block, size, lanes), lambda i, h=h: (0, i + h * steps, 0, 0))
                flat = pl.BlockSpec((block, size, lanes), lambda i, h=h: (i + h * steps, 0, 0))
                operands += list(p[g])
                specs += [wide, wide, flat]
    rows = sum(sizes)
    outs = pl.pallas_call(
        lambda *refs: settle_kernel(groups, sizes, *refs),
        grid=(steps,),
        in_specs=specs + [ANYWHERE] * len(gates),
        out_specs=[pl.BlockSpec((block, rows, lanes), lambda i: (i, 0, 0))] * (2 * groups),
        out_shape=[jax.ShapeDtypeStruct((half, rows, lanes), BF16)] * (2 * groups),
        compiler_params=pltpu.CompilerParams(vmem_limit_bytes=8 * 2**20),
        cost_estimate=pl.CostEstimate(
            flops=0, transcendentals=0, bytes_accessed=8 * groups * slots * rows * lanes),
        name=name,
    )(*operands, *gates)
    shaped = [o.reshape(2, half // 2, rows, lanes) for o in outs]
    return [[shaped[2 * n + h] for n in (2, 0, 1)] for h in range(2)]


def finish_kernel(count, at_ref, *refs):
    outs, down_ref = refs[-5:-1], refs[-1]
    core, far = at_ref[CORE], at_ref[FAR]
    row = lax.broadcasted_iota(jnp.int32, (24, 80), 0)
    column = lax.broadcasted_iota(jnp.int32, (24, 80), 1)
    picks = []
    for n in range(4):
        x_hi, c = far ^ (n // 2), core ^ (n % 2)
        wanted = jnp.where(row == 6, 72, (row // 8) * 24 + x_hi * 12 + c * 6 + row % 8)
        picks.append(jnp.where((column == wanted) & (row % 8 < 6 + (row == 6)), 1.0, 0.0).astype(BF16))
    for g in range(3):
        cell = add_up([refs[3 * g + k][...] for k in range(3)])
        shared = jnp.concatenate([cell[:48], cell[96:]], axis=0)
        for out, pick in zip(outs, picks):
            rows = jnp.concatenate([mm(pick, shared), jnp.zeros((40, 256), F32)], axis=0)
            out[g] = rows.astype(BF16)
        down_ref[g] = cell[48:96]


def finish(table, kept, first, second, gates):
    wide = pl.BlockSpec((None, None, 128, 256), lambda i, t: (0, 0, 0, 0))
    flat = pl.BlockSpec((None, 128, 256), lambda i, t: (0, 0, 0))
    sizes = [64] * 4 + [48]
    return pl.pallas_call(
        lambda *refs: finish_kernel(9, *refs),
        grid_spec=pltpu.PrefetchScalarGridSpec(
            num_scalar_prefetch=1,
            grid=(1,),
            in_specs=[wide, wide, flat] * 3 + [ANYWHERE] * len(gates),
            out_specs=[pl.BlockSpec((3, size, 256), lambda i, t: (0, 0, 0)) for size in sizes],
        ),
        out_shape=[jax.ShapeDtypeStruct((3, size, 256), BF16) for size in sizes],
        compiler_params=pltpu.CompilerParams(vmem_limit_bytes=4 * 2**20),
        name="finish",
    )(table, *[v for g in range(3) for v in (kept[g], first[g], second[g])], *gates)


def after_kernel(values_ref, *refs):
    refs[-1][...] = values_ref[...]


def after(values, gates):
    return pl.pallas_call(
        after_kernel,
        in_specs=[WHOLE] + [ANYWHERE] * len(gates),
        out_specs=WHOLE,
        out_shape=jax.ShapeDtypeStruct(values.shape, values.dtype),
        compiler_params=pltpu.CompilerParams(vmem_limit_bytes=4 * 2**20),
        name="after",
    )(values, *gates)


def put(acc, first, part, rows=slice(None)):
    for n in range(part.shape[1] // 128):
        column = first + n * 128
        lanes = slice(column % 256, column % 256 + 128)
        acc[column // 256, rows, lanes] = part[:, n * 128 : (n + 1) * 128]


def spill_rows(target, acc, at_slot, g, base, extra):
    block = 2 * (g - 1) if g else 0

    def cell(i, carry):
        slot = g * 64 + base + i
        rows = pl.ds(pl.multiple_of(at_slot[slot], 8), 24)
        part = acc[at_slot[192 + slot] + block, rows, :]
        target[i] = jnp.concatenate([part, extra(slot)], axis=0).astype(BF16)
        return carry
    lax.fori_loop(0, 32, cell, 0, unroll=4)


def tail_kernel(at_slot, act_ref, away_ref, q_ref, qb_ref, ka_ref, kb_ref, va_ref, *refs):
    keeps, sends, acc = refs[-5:-3], refs[-3:-1], refs[-1]
    act, away = act_ref[...], away_ref[...]
    near = mm(act, jnp.concatenate(
        [r[: 2 * N, :] for r in (q_ref, qb_ref, ka_ref, kb_ref, va_ref)], axis=1), TN)
    far = mm(away, jnp.concatenate(
        [r[2 * N :, :] for r in (ka_ref, kb_ref, va_ref)], axis=1), TN)
    put(acc, 0, near[:, :384])
    put(acc, 384, near[:, 384:] + far)
    blank = lambda slot: jnp.zeros((8, 256), F32)
    for n in range(2):
        spill_rows(keeps[n], acc, at_slot, n + 1, 0, blank)
        spill_rows(sends[n], acc, at_slot, n + 1, 32, blank)


def tail_cells(table, *operands):
    return pl.pallas_call(
        tail_kernel,
        in_specs=[SMALL] + [WHOLE] * len(operands),
        out_specs=[WHOLE] * 4,
        out_shape=[jax.ShapeDtypeStruct((32, 32, 256), BF16)] * 4,
        scratch_shapes=[pltpu.VMEM((4, 768, 256), F32)],
        compiler_params=pltpu.CompilerParams(vmem_limit_bytes=14 * 2**20),
        cost_estimate=pl.CostEstimate(
            flops=2 * 768 * 512 * (1024 + 640), bytes_accessed=8 * 2**20, transcendentals=0),
        name="tail_cells",
    )(table, *operands)


def inputs_kernel(at_slot, act_ref, away_ref, q_ref, qb_ref, ka_ref, kb_ref, va_ref, vb_ref,
                  att_own_ref, att_sib_ref, proj_ref, own_ref, sib_ref, far_ref, far_sib_ref,
                  second_ref, *refs):
    weights = refs[:3]
    keep_ref, send_ref, cell_keep, cell_send, acc, table = refs[-6:]
    core = at_slot[CORE]
    put(acc, 0, mm(act_ref[...], vb_ref[: 2 * N, :], TN) + mm(away_ref[...], vb_ref[2 * N :, :], TN))
    mine = pl.ds(pl.multiple_of(core * 384, 384), 384)
    other = pl.ds(pl.multiple_of((1 - core) * 384, 384), 384)
    put(acc, 128, mm(att_own_ref[...], proj_ref[...], TN), mine)
    put(acc, 128, mm(att_sib_ref[:N, :], proj_ref[N:, :], TN)
        + mm(att_sib_ref[N:, :], proj_ref[:N, :], TN), other)

    vectors = [jnp.zeros((1, 768), F32)] * 2 + [second_ref[0:1, :], second_ref[1:2, :]]
    wide = list(zip((q_ref, ka_ref, va_ref), (qb_ref, kb_ref, vb_ref), weights))
    for n, ext_ref in enumerate((own_ref, sib_ref, far_ref, far_sib_ref)):
        rows = slice(n * N, (n + 1) * N)
        total = jnp.zeros((N, 768), F32)
        for a_ref, b_ref, w_ref in wide[0 if n < 2 else 1 :]:
            grads = jnp.concatenate([a_ref[rows, :], b_ref[rows, :]], axis=1)
            total += mm(grads, w_ref[...], NT)
        xhat, _ = normalize(ext_ref[:N, :].astype(F32))
        vectors[0] += jnp.sum(total * xhat, axis=0, keepdims=True)
        vectors[1] += jnp.sum(total, axis=0, keepdims=True)
        half = slice((n // 2) * N, (n // 2 + 1) * N)
        if n % 2 == 0:
            keep_ref[half, :] = total
        else:
            send_ref[half, :] = total.astype(BF16)

    chip = lax.broadcasted_iota(jnp.int32, (64, 768), 0)
    owner = lax.broadcasted_iota(jnp.int32, (64, 768), 1) // 12
    feature = lax.broadcasted_iota(jnp.int32, (768, 128), 0) % 12
    lane = lax.broadcasted_iota(jnp.int32, (768, 128), 1)
    spread = jnp.zeros((64, 128), F32)
    for n in range(4):
        line = jnp.broadcast_to(vectors[n], (64, 768))
        values = jnp.where(chip == owner, line, 0.0).astype(BF16)
        spread += mm(values, jnp.where(lane == feature + 12 * n, 1.0, 0.0).astype(BF16))
    table[...] = spread

    def lines(slot):
        row = table[pl.ds(at_slot[576 + slot], 1), :]
        return jnp.concatenate(
            [jnp.broadcast_to(row, (8, 128)), jnp.zeros((8, 128), F32)], axis=1)

    spill_rows(cell_keep, acc, at_slot, 0, 0, lines)
    spill_rows(cell_send, acc, at_slot, 0, 32, lines)


def input_partials(table, operands, gates):
    whole = lambda shape: pl.BlockSpec(shape, lambda i, *_: (0,) * len(shape))
    shapes = [((2 * N, 768), F32), ((2 * N, 768), BF16)] + [((32, 32, 256), BF16)] * 2
    return pl.pallas_call(
        inputs_kernel,
        grid_spec=pltpu.PrefetchScalarGridSpec(
            num_scalar_prefetch=1,
            grid=(1,),
            in_specs=[whole(v.shape) for v in operands[:-1]]
            + [pl.BlockSpec((768, 384), lambda i, at, n=n: (0, 2 * n + at[CORE])) for n in range(3)]
            + [ANYWHERE] * len(gates),
            out_specs=[whole(shape) for shape, _ in shapes],
            scratch_shapes=[pltpu.VMEM((2, 768, 256), F32), pltpu.VMEM((64, 128), F32)],
        ),
        out_shape=[jax.ShapeDtypeStruct(*v) for v in shapes],
        compiler_params=pltpu.CompilerParams(vmem_limit_bytes=16 * 2**20),
        cost_estimate=pl.CostEstimate(
            flops=2 * 768 * 384 * 512 * 7, bytes_accessed=10 * 2**20, transcendentals=0),
        name="input_partials",
    )(table, *operands, *[operands[-1]] * 2, *gates)


def sum_core_kernel(own_ref, sib_ref, *refs):
    refs[-1][...] = (own_ref[...] + sib_ref[...].astype(F32)).astype(BF16)


def sum_core(own, sib, gates):
    half = pl.BlockSpec((N, 768), lambda i: (1, 0))
    return pl.pallas_call(
        sum_core_kernel,
        grid=(1,),
        in_specs=[half, half] + [ANYWHERE] * len(gates),
        out_specs=pl.BlockSpec((N, 768), lambda i: (0, 0)),
        out_shape=jax.ShapeDtypeStruct((N, 768), BF16),
        compiler_params=pltpu.CompilerParams(vmem_limit_bytes=4 * 2**20),
        name="sum_core",
    )(own, sib, *gates)


def token_kernel(tokens_ref, hidden_ref, own_ref, sib_ref, far_ref, gain_ref, out_own_ref,
                 out_sib_ref, grad_ref, out_ref):
    grad = own_ref[...] + sib_ref[...].astype(F32) + far_ref[...].astype(F32)
    xhat, factor = normalize(tokens_ref[...].astype(F32))
    grad_ref[...] = hidden_ref[...] + normalize_back(grad, xhat, factor, wide(gain_ref))
    out_ref[...] = (out_own_ref[...] + out_sib_ref[...].astype(F32)).astype(BF16)


def token_grads(tokens, hidden, own, sib, far, gain, out_own, out_sib):
    half = pl.BlockSpec((N, 768), lambda i: (0, 0))
    return pl.pallas_call(
        token_kernel,
        grid=(1,),
        in_specs=[half] * 5 + [LINE] + [half] * 2,
        out_specs=[half] * 2,
        out_shape=[jax.ShapeDtypeStruct((N, 768), F32), jax.ShapeDtypeStruct((N, 768), BF16)],
        compiler_params=pltpu.CompilerParams(vmem_limit_bytes=8 * 2**20),
        name="token_grads",
    )(tokens, hidden, own, sib, far, gain, out_own, out_sib)


def assemble_kernel(at_ref, own_ref, near_ref, away_ref, cross_ref, down_ref, up_ref, qkv_ref, out_ref,
                    vec_ref, below_ref, held):
    core, far = at_ref[CORE], at_ref[FAR]
    held[far * 2 + core] = own_ref[...]
    held[far * 2 + 1 - core] = near_ref[...]
    held[2 - far * 2 + core] = away_ref[...]
    held[2 - far * 2 + 1 - core] = cross_ref[...]
    line = own_ref[0, :8, :128].astype(F32) + near_ref[0, :8, :128].astype(F32)
    vec_ref[...] = jnp.where(core == 0, line, pltpu.roll(line, 122, 1))
    for x_hi in range(2):
        for c in range(2):
            for g in range(3):
                rows = held[x_hi * 2 + c, g, :32].astype(F32)
                first = c * 1536 + g * 512 + x_hi * 256
                for e in range(2):
                    up_ref[:, e, first : first + 256] = rows[8 * e : 8 * e + 6] * UP_FACTORS[e]
                for n in range(2):
                    at = (g + 2) % 3 * 512 + x_hi * 256 + n * 128
                    kind, within = at // 384, at % 384 + c * 384
                    part = rows[16:22, n * 128 : (n + 1) * 128]
                    if kind < 3:
                        qkv_ref[:, kind * 768 + within : kind * 768 + within + 128] = part
                    else:
                        out_ref[:, within : within + 128] = part
    for g in range(3):
        part = down_ref[g].astype(F32)
        for e in range(2):
            below_ref[e, :, g * 256 : (g + 1) * 256] = part[24 * e : 24 * e + 24] * UP_FACTORS[e]


def assemble(table, *parts):
    return pl.pallas_call(
        assemble_kernel,
        in_specs=[SMALL] + [WHOLE] * 5,
        out_specs=[WHOLE] * 5,
        out_shape=[
            jax.ShapeDtypeStruct((6, 2, 3072), F32),
            jax.ShapeDtypeStruct((6, 2304), F32),
            jax.ShapeDtypeStruct((6, 768), F32),
            jax.ShapeDtypeStruct((8, 128), F32),
            jax.ShapeDtypeStruct((2, 24, 768), F32),
        ],
        scratch_shapes=[pltpu.VMEM((4, 3, 64, 256), BF16)],
        compiler_params=pltpu.CompilerParams(vmem_limit_bytes=4 * 2**20),
        name="assemble",
    )(table, *parts)

def shards(tokens, first_gain, first_shift, w_qkv, w_out, second_gain, second_shift,
           w_up, w_down, modality, segments, partner, cotangent):
    table = lax.dynamic_index_in_dim(
        jnp.asarray(cell_places()), lax.axis_index(BOTH), 0, keepdims=False)

    own = marked(partner, tokens[0], segments, modality)
    away = swap_far(own)
    sib = swap_core(own)
    cot_own = cotangent[0]
    cot_sib = swap_core(cot_own)

    act1, marks, queries, k_near, v_near, qx = project(
        table, own, sib, first_gain, first_shift, in_hbm(w_qkv), True)
    near_both, near_peak = attend_near(queries, k_near, v_near, qx, marks)
    away_sib = swap_core(after(away, [near_peak]))
    act1_away, marks_away, k_away, v_away = project(table, away, away_sib, first_gain, first_shift, w_qkv, False)
    attended, lse = attend_forward(queries, k_away, v_away, qx, marks_away, near_both, near_peak)
    attended_sib = swap_core(attended)

    hidden, grad_act2, xhat2, factor2, act_t, inner_t, grad_pre = experts(
        table, attended, attended_sib, own, sib, cot_own, cot_sib, marks, second_gain, second_shift, w_out,
        in_hbm(w_up), in_hbm(w_down))
    ff_kept, ff_first, more = [], [], [grad_act2]
    for g in range(3):
        keep, gone, *low = cells(g, table, act_t, grad_pre, inner_t, cot_own, cot_sib, marks, more)
        ff_kept.append(keep.reshape(2, 16, 96, 256))
        ff_first.append(send(gone.reshape(2, 16, 96, 256), axis_step(ORDERS[g][0], True)))
        if g == 0:
            grad_sib = swap_core(low[0])
        more = [keep] if g == 0 else [keep, grad_sib]
    hidden_grad, grad_att, proj_half, vectors = middle(
        table, grad_act2, grad_sib, xhat2, factor2, cot_own, cot_sib, second_gain, w_out)

    def along(stage, first, values):
        sent = {g: send(values[g], axis_step(ORDERS[g][stage], first)) for g in (1, 2, 0)}
        return [sent[g] for g in range(3)]

    taken = (queries, k_near, k_away, v_near, v_away, grad_att, attended, qx, marks, marks_away, lse)
    q_a, k_a, v_a = attend_backward(taken, 0, 2, ())
    q_b, k_b, v_b = attend_backward(taken, 2, 1, ())
    cells_a = tail_cells(table, act1, act1_away, q_a, q_b, k_a, k_b, v_a)
    partial_own, partial_low, *cells_b = input_partials(table, (
        act1, act1_away, q_a, q_b, k_a, k_b, v_a, v_b, attended, attended_sib, proj_half,
        own, sib, away, away_sib, vectors, w_qkv), ())
    kept = [v.reshape(2, 16, 32, 256) for v in (cells_b[0], cells_a[0], cells_a[1])]
    first = along(0, True, [v.reshape(2, 16, 32, 256) for v in (cells_b[1], cells_a[2], cells_a[3])])
    ff_second = along(0, False, pass_on(ff_kept, ff_first, "pass_first", [cells_b[0]]))
    partial_sib = swap_core(partial_low)
    passed = pass_on(kept, first, "pass_tail")
    second = along(0, False, passed)
    out_own, out_sib = branches(table, inner_t, w_down, hidden, marks, passed)

    kept, sent = settle(
        [list(zip(ff_kept, ff_first, ff_second)), list(zip(kept, first, second))], "settle_all", [out_sib])
    first = along(1, True, sent)
    second = along(1, False, pass_on(kept, first, "pass_second"))
    kept, sent = settle([list(zip(kept, first, second))], "settle_second")
    first = along(2, True, sent)
    from_far = swap_far(sum_core(partial_own, partial_sib, first))
    second = along(2, False, pass_on(kept, first, "pass_third"))
    held, *shares, down_held = finish(table, kept, first, second, [from_far])

    near, beyond = swap_core(shares[0]), swap_far(shares[1])
    cross = send(shares[2], lambda x, y, z, c: (x ^ 2, y, z, 1 - c))
    below = send(down_held, lambda x, y, z, c: (x, y, 2 * c + z % 2, z // 2))
    up_grad, qkv_grad, out_grad, line, down_grad = assemble(
        table, held, near, beyond, cross, below)

    token_grad, layer_output = token_grads(
        tokens[0], hidden_grad, partial_own, partial_sib, from_far, first_gain, out_own, swap_core(out_sib))

    return (
        layer_output[None], token_grad[None], line[6, :6], line[6, 12:18], qkv_grad, out_grad,
        line[6, 24:30], line[6, 36:42], up_grad.transpose(1, 0, 2), down_grad)


def solution(mesh):
    cut = P("rows", "seq", None)
    flat = P(BOTH)
    placed = (cut,) + (P(),) * 8 + (P("rows", "seq"), P("rows", "seq"), P("rows", None), cut)
    return jax.shard_map(
        shards, mesh=mesh, in_specs=placed,
        out_specs=(cut, cut, flat, flat, P(BOTH, None), P(BOTH, None), flat, flat,
                   P(None, BOTH, None), P(None, BOTH, None)),
        check_vma=False)
```

```python
import jax
import jax.numpy as jnp
import numpy as np
from jax import lax
from jax.experimental import pallas as pl
from jax.experimental.pallas import tpu as pltpu
from jax.sharding import PartitionSpec as P

HD = 64
OWN = 6
CORE, FAR = 768, 769
IMG = 197
NIMG = 4
BOTH = ("rows", "seq")
F32 = jnp.float32
BF16 = jnp.bfloat16
MASKED = -1e30


def route(step):
    pairs = []
    for r in range(32):
        z, x_lo, y = r // 8, (r // 4) % 2, r % 4
        for s in range(4):
            x, c = (s // 2) * 2 + x_lo, s % 2
            tx, ty, tz, tc = step(x, y, z, c)
            target = (tz * 8 + (tx % 2) * 4 + ty) * 4 + (tx // 2) * 2 + tc
            pairs.append((r * 4 + s, target))
    return pairs


def send(values, step):
    return lax.ppermute(values, BOTH, route(step))


def swap_core(values):
    return send(values, lambda x, y, z, c: (x, y, z, 1 - c))


def swap_far(values):
    return send(values, lambda x, y, z, c: (x ^ 2, y, z, c))


def axis_step(axis, first):
    def step(x, y, z, c):
        flip = 1 if (c == 0) == first else 3
        at = {"x": x, "y": y, "z": z}
        at[axis] ^= flip
        return (at["x"], at["y"], at["z"], c)

    return step


UP_FACTORS = (1024 / (2 * 788), 1024 / (2 * 236))
ORDERS = (("x", "y", "z"), ("y", "z", "x"), ("z", "x", "y"))


def in_hbm(values):
    return pltpu.with_memory_space_constraint(values, pltpu.HBM)


def wide(vector_ref):
    return vector_ref[...].reshape(1, 768)


LINE = pl.BlockSpec((768,), lambda *_: (0,))


def normalize(inputs):
    centred = inputs - jnp.mean(inputs, axis=-1, keepdims=True)
    factor = lax.rsqrt(jnp.mean(centred * centred, axis=-1, keepdims=True) + 1e-05)
    return centred * factor, factor


def normalize_back(grad, xhat, factor, gain):
    gy = grad * gain
    mean_gy = jnp.mean(gy, axis=-1, keepdims=True)
    mean_gx = jnp.mean(gy * xhat, axis=-1, keepdims=True)
    return factor * (gy - mean_gy - xhat * mean_gx)


SMALL = pl.BlockSpec(memory_space=pltpu.SMEM)
WHOLE = pl.BlockSpec(memory_space=pltpu.VMEM)
N = 256


def marked_kernel(partner, tokens_ref, segments_ref, modality_ref, out_ref):
    segments = segments_ref[...]
    tag = jnp.zeros(segments.shape, jnp.int32)
    for n in range(8):
        tag = jnp.where(segments == n, partner[0, n], tag)
    marks = jnp.concatenate(
        [tag, modality_ref[...], jnp.zeros((1, 256), jnp.int32)], axis=1).astype(F32)
    out_ref[:N, :] = tokens_ref[...]
    out_ref[N:, :] = jnp.concatenate([marks, jnp.zeros((15, 768), F32)], axis=0).astype(BF16)


def marked(partner, tokens, segments, modality):
    return pl.pallas_call(
        marked_kernel,
        in_specs=[SMALL, WHOLE, WHOLE, WHOLE],
        out_specs=WHOLE,
        out_shape=jax.ShapeDtypeStruct((N + 16, 768), BF16),
        compiler_params=pltpu.CompilerParams(vmem_limit_bytes=6 * 2**20),
        name="marked",
    )(partner, tokens, segments, modality)


def mark_lanes(ext):
    row = ext[N:, :].astype(F32)
    place = lax.broadcasted_iota(jnp.int32, (128, N), 0)
    tag = jnp.broadcast_to(row[:1, :N], (128, N))
    kind = jnp.broadcast_to(row[:1, N : 2 * N], (128, N))
    hot = jnp.where((place < NIMG) & (place.astype(F32) == tag), 1.0, 0.0)
    return jnp.transpose(jnp.where(place == 8, kind, hot))


def project_kernel(at_ref, near, a_ref, b_ref, gain_ref, shift_ref, *refs):
    count = 3 if near else 2
    weights, outs = refs[:count], refs[count:]
    for n, ext_ref in enumerate((a_ref, b_ref)):
        rows = slice(n * N, (n + 1) * N)
        ext = ext_ref[...]
        xhat, _ = normalize(ext[:N].astype(F32))
        act = (xhat * wide(gain_ref) + wide(shift_ref)).astype(BF16)
        outs[0][rows, :] = act
        marks = mark_lanes(ext)
        outs[1][rows, :] = marks.astype(BF16)
        for m in range(count):
            part = mm(act, weights[m][...])
            outs[2 + m][rows, :] = (0.125 * part if near and m == 0 else part).astype(BF16)
        if near:
            lane = lax.broadcasted_iota(jnp.int32, marks.shape, 1)
            outs[5][rows, :] = jnp.where((lane < NIMG) & (marks == 0.0), MASKED, 0.0).astype(BF16)


def project(table, first, second, gain, shift, w_qkv, near):
    kinds = (0, 1, 2) if near else (1, 2)
    sizes = [768, 128] + [384] * len(kinds) + ([128] if near else [])
    whole = lambda shape: pl.BlockSpec(shape, lambda i, at: (0, 0))
    return pl.pallas_call(
        lambda at_ref, *refs: project_kernel(at_ref, near, *refs),
        grid_spec=pltpu.PrefetchScalarGridSpec(
            num_scalar_prefetch=1,
            grid=(1,),
            in_specs=[whole((N + 16, 768))] * 2 + [LINE] * 2
            + [pl.BlockSpec((768, 384), lambda i, at, n=n: (0, 2 * n + at[CORE])) for n in kinds],
            out_specs=[whole((2 * N, size)) for size in sizes],
        ),
        out_shape=[jax.ShapeDtypeStruct((2 * N, size), BF16) for size in sizes],
        compiler_params=pltpu.CompilerParams(vmem_limit_bytes=6 * 2**20),
        cost_estimate=pl.CostEstimate(
            flops=2 * 512 * 768 * 384 * len(kinds), bytes_accessed=4 * 2**20, transcendentals=0),
        name="project_near" if near else "project_away",
    )(table, first, second, gain, shift, *[w_qkv] * len(kinds))


def middle_kernel(place, grad_ref, sib_ref, xhat_ref, factor_ref, cot_own_ref, cot_sib_ref,
                  gain_ref, w_out_ref, hidden_ref, att_ref, proj_ref, vec_ref):
    core = place[CORE]
    for n, cot_ref in enumerate((cot_own_ref, cot_sib_ref)):
        rows, other = slice(n * N, (n + 1) * N), slice((1 - n) * N, (2 - n) * N)
        grad = grad_ref[rows, :].astype(F32) + sib_ref[other, :].astype(F32)
        xhat = xhat_ref[rows, :].astype(F32)
        total = cot_ref[...].astype(F32) + normalize_back(grad, xhat, factor_ref[rows, :], wide(gain_ref))
        low = total.astype(BF16)
        if n == 0:
            hidden_ref[...] = total
            vec_ref[0:1, :] = jnp.sum(grad * xhat, axis=0, keepdims=True)
            vec_ref[1:2, :] = jnp.sum(grad, axis=0, keepdims=True)
        mine = w_out_ref[pl.ds(pl.multiple_of(core * 384, 384), 384), :]
        att_ref[rows, :] = mm(low, mine, NT).astype(BF16)
        proj_ref[rows, :] = jnp.where(core == 0, low[:, :384], low[:, 384:])


def middle(place, *operands):
    return pl.pallas_call(
        middle_kernel,
        in_specs=[SMALL] + [WHOLE] * len(operands),
        out_specs=[WHOLE] * 4,
        out_shape=[
            jax.ShapeDtypeStruct((N, 768), F32),
            jax.ShapeDtypeStruct((2 * N, 384), BF16),
            jax.ShapeDtypeStruct((2 * N, 384), BF16),
            jax.ShapeDtypeStruct((2, 768), F32),
        ],
        compiler_params=pltpu.CompilerParams(vmem_limit_bytes=6 * 2**20),
        cost_estimate=pl.CostEstimate(
            flops=2 * 512 * 768 * 384, bytes_accessed=8 * 2**20, transcendentals=0),
        name="middle",
    )(place, *operands)


def gelu_parts(pre):
    phi = 0.5 * (1.0 + lax.erf(pre * 0.7071067811865476))
    slope = phi + pre * (0.3989422804014327 * jnp.exp(-0.5 * pre * pre))
    return pre * phi, slope


NT = (((1,), (1,)), ((), ()))
TN = (((0,), (0,)), ((), ()))
NN = (((1,), (0,)), ((), ()))


def mm(left, right, dims=NN):
    return lax.dot_general(left, right, dims, preferred_element_type=F32)


def head_lanes(shape, h):
    lane = lax.broadcasted_iota(jnp.int32, shape, len(shape) - 1)
    return (lane >= HD) == (h == 1)


def turned(values):
    return jnp.transpose(values.astype(F32)).astype(BF16)


def stacked(near_ref, away_ref):
    return jnp.concatenate([near_ref[...], away_ref[...]], axis=0)


def half_attention(q_ref, k_ref, v_ref, qx_ref, x_ref, h, peak_before):
    q_pair = q_ref[...]
    mine = head_lanes(q_pair.shape, 0) if h == 0 else jnp.logical_not(head_lanes(q_pair.shape, 0))
    query = jnp.concatenate([jnp.where(mine, q_pair, 0), qx_ref[...]], axis=1)
    scores = mm(jnp.concatenate([k_ref[...], x_ref[...]], axis=1), query, NT)
    peak = jnp.max(scores, axis=0, keepdims=True)
    if peak_before is not None:
        peak = jnp.maximum(peak, peak_before)
    weights = jnp.exp(scores - peak).astype(BF16)
    values_t = turned(v_ref[...])
    rows = lax.broadcasted_iota(jnp.int32, values_t.shape, 0) < HD
    left = jnp.where(rows, values_t, 1) if h == 0 else jnp.where(rows, 1, values_t)
    return mm(left, weights), peak


def near_kernel(q_ref, k_ref, v_ref, qx_ref, x_ref, both_ref, peak_ref):
    for h in range(2):
        both, peak = half_attention(q_ref, k_ref, v_ref, qx_ref, x_ref, h, None)
        both_ref[0, h] = both
        peak_ref[0, h : h + 1, :] = peak


def forward_kernel(q_ref, k_ref, v_ref, qx_ref, x_ref, both_ref, peak_ref, out_ref, lse_ref):
    mixed = []
    for h in range(2):
        before = peak_ref[0, h : h + 1, :]
        both, peak = half_attention(q_ref, k_ref, v_ref, qx_ref, x_ref, h, before)
        both = both + both_ref[0, h] * jnp.exp(before - peak)
        total = both[127:128, :] if h == 0 else both[0:1, :]
        mixed.append(both * (1.0 / total))
        lse_ref[0, h : h + 1, :] = peak + jnp.log(total)
    rows = lax.broadcasted_iota(jnp.int32, mixed[0].shape, 0) < HD
    out_ref[...] = jnp.transpose(jnp.where(rows, mixed[0], mixed[1])).astype(BF16)


BY_PAIR = pl.BlockSpec((2 * N, 128), lambda p: (0, p))
FIXED = pl.BlockSpec((2 * N, 128), lambda p: (0, 0))


PAIR_LINES = pl.BlockSpec((1, 2, 2 * N), lambda p: (p, 0, 0))
PAIR_BOTH = pl.BlockSpec((1, 2, 128, 2 * N), lambda p: (p, 0, 0, 0))


def attend_near(*operands):
    return pl.pallas_call(
        near_kernel,
        grid=(3,),
        in_specs=[BY_PAIR] * 3 + [FIXED] * 2,
        out_specs=[PAIR_BOTH, PAIR_LINES],
        out_shape=[
            jax.ShapeDtypeStruct((3, 2, 128, 2 * N), F32),
            jax.ShapeDtypeStruct((3, 2, 2 * N), F32),
        ],
        compiler_params=pltpu.CompilerParams(vmem_limit_bytes=8 * 2**20),
        cost_estimate=pl.CostEstimate(
            flops=2 * OWN * 512 * 1024 * 256, bytes_accessed=4 * 2**20,
            transcendentals=OWN * 512 * 512),
        name="attend_near",
    )(*operands)


def attend_forward(*operands):
    return pl.pallas_call(
        forward_kernel,
        grid=(3,),
        in_specs=[BY_PAIR] * 3 + [FIXED] * 2 + [PAIR_BOTH, PAIR_LINES],
        out_specs=[BY_PAIR, PAIR_LINES],
        out_shape=[
            jax.ShapeDtypeStruct((2 * N, 384), BF16),
            jax.ShapeDtypeStruct((3, 2, 2 * N), F32),
        ],
        compiler_params=pltpu.CompilerParams(vmem_limit_bytes=8 * 2**20),
        cost_estimate=pl.CostEstimate(
            flops=2 * OWN * 512 * 1024 * 256, bytes_accessed=5 * 2**20,
            transcendentals=OWN * 512 * 512),
        name="attend_forward",
    )(*operands)


def backward_kernel(q_ref, kn_ref, ka_ref, vn_ref, va_ref, do_ref, o_ref, qx_ref, xn_ref, xa_ref,
                    lse_ref, *refs):
    dq_ref, dk_ref, dv_ref = refs[-3:]
    k_pair, values = stacked(kn_ref, ka_ref), stacked(vn_ref, va_ref)
    keys = jnp.concatenate([k_pair, stacked(xn_ref, xa_ref)], axis=1)
    q_pair, grads = q_ref[...], do_ref[...]
    lanes = head_lanes(q_pair.shape, 0)
    product = grads.astype(F32) * o_ref[...].astype(F32)
    k_turned = turned(k_pair)
    rows = lax.broadcasted_iota(jnp.int32, (128, 2 * N), 0) < HD
    dq = jnp.zeros((128, 2 * N), F32)
    dk = jnp.zeros(k_pair.shape, F32)
    dv = jnp.zeros(k_pair.shape, F32)
    for h in range(2):
        mine = lanes if h == 0 else jnp.logical_not(lanes)
        q_head = jnp.where(mine, q_pair, 0)
        g_head = jnp.where(mine, grads, 0)
        dot_row = jnp.transpose(jnp.sum(jnp.where(mine, product, 0.0), axis=1, keepdims=True))
        scores = mm(keys, jnp.concatenate([q_head, qx_ref[...]], axis=1), NT)
        prob = jnp.exp(scores - lse_ref[0, h : h + 1, :])
        dv += mm(prob.astype(BF16), g_head)
        grad_prob = mm(values, g_head, NT)
        grad_scores = (prob * (grad_prob - dot_row)).astype(BF16)
        dk += mm(grad_scores, q_head)
        part = mm(k_turned, grad_scores)
        dq += jnp.where(rows if h == 0 else jnp.logical_not(rows), part, 0.0)
    dq_ref[...] = jnp.transpose(dq).astype(BF16) * jnp.asarray(0.125, BF16)
    dk_ref[...] = dk.astype(BF16)
    dv_ref[...] = dv.astype(BF16)


def attend_backward(operands, first, pairs, gates):
    by_pair = pl.BlockSpec((2 * N, 128), lambda p: (0, first + p))
    sizes = (2 * N, 4 * N, 4 * N)
    return pl.pallas_call(
        backward_kernel,
        grid=(pairs,),
        in_specs=[by_pair] * 7 + [FIXED] * 3
        + [pl.BlockSpec((1, 2, 2 * N), lambda p: (first + p, 0, 0))]
        + [pl.BlockSpec(memory_space=pl.ANY)] * len(gates),
        out_specs=[pl.BlockSpec((size, 128), lambda p: (0, p)) for size in sizes],
        out_shape=[jax.ShapeDtypeStruct((size, pairs * 128), BF16) for size in sizes],
        compiler_params=pltpu.CompilerParams(vmem_limit_bytes=10 * 2**20),
        cost_estimate=pl.CostEstimate(
            flops=2 * 5 * 2 * pairs * 512 * 1024 * 256, bytes_accessed=6 * 2**20,
            transcendentals=2 * pairs * 512 * 1024),
        name="attend_backward",
    )(*operands, *gates)


FF_STEP = 512
E_STEP = 512
EXPERT_MB = 40
CELLS_MB = 28


def expert_kernel(at_ref, att_own_ref, att_sib_ref, own_ref, sib_ref, cot_own_ref, cot_sib_ref,
                  marks_ref, gain_ref, shift_ref, w_out_ref, wu_ref, wd_ref,
                  hidden_ref, low_ref, xhat_ref, factor_ref, act_t_ref, inner_t_ref, slope_ref,
                  act_acc, grad_acc):
    f = pl.program_id(0)
    core = at_ref[CORE]

    @pl.when(f == 0)
    def _():
        mine = w_out_ref[pl.ds(pl.multiple_of(core * 384, 384), 384), :]
        other = w_out_ref[pl.ds(pl.multiple_of((1 - core) * 384, 384), 384), :]
        for n, ext_ref in enumerate((own_ref, sib_ref)):
            rows, theirs = slice(n * N, (n + 1) * N), slice((1 - n) * N, (2 - n) * N)
            hidden = ext_ref[:N, :].astype(F32) + (
                mm(att_own_ref[rows, :], mine) + mm(att_sib_ref[theirs, :], other))
            xhat, factor = normalize(hidden)
            xhat_ref[rows, :] = xhat.astype(BF16)
            factor_ref[rows, :] = factor
            act = xhat * wide(gain_ref) + wide(shift_ref)
            act_acc[rows, :] = act.astype(BF16)
            act_t_ref[:, rows] = jnp.transpose(act).astype(BF16)
            if n == 0:
                hidden_ref[...] = hidden
        grad_acc[...] = jnp.zeros(grad_acc.shape, F32)

    act = act_acc[...]
    cot = jnp.concatenate([cot_own_ref[...], cot_sib_ref[...]], axis=0)
    text = marks_ref[:, 8:9].astype(F32) > 0.0
    pre = jnp.where(text, mm(act, wu_ref[1]), mm(act, wu_ref[0]))
    inner, slope = gelu_parts(pre)
    grad_pre = jnp.where(text, mm(cot, wd_ref[1], NT), mm(cot, wd_ref[0], NT)) * slope
    inner_t_ref[...] = jnp.transpose(inner).astype(BF16)
    low = grad_pre.astype(BF16)
    slope_ref[...] = low
    zero = jnp.zeros((), BF16)
    grad_acc[...] += (mm(jnp.where(text, zero, low), wu_ref[0], NT)
                      + mm(jnp.where(text, low, zero), wu_ref[1], NT))

    @pl.when(f == pl.num_programs(0) - 1)
    def _():
        low_ref[...] = grad_acc[...].astype(BF16)


def experts(core, *operands):
    steps = 1536 // E_STEP
    shapes = [((N, 768), F32), ((2 * N, 768), BF16), ((2 * N, 768), BF16), ((2 * N, 1), F32),
              ((768, 2 * N), BF16)]
    fixed = lambda shape: pl.BlockSpec(shape, lambda f, *_: (0,) * len(shape))
    return pl.pallas_call(
        expert_kernel,
        grid_spec=pltpu.PrefetchScalarGridSpec(
            num_scalar_prefetch=1,
            grid=(steps,),
            in_specs=[fixed(v.shape) for v in operands[:-2]] + [
                pl.BlockSpec((2, 768, E_STEP), lambda f, at: (0, 0, at[CORE] * steps + f)),
                pl.BlockSpec((2, E_STEP, 768), lambda f, at: (0, at[CORE] * steps + f, 0)),
            ],
            out_specs=[fixed(shape) for shape, _ in shapes] + [
                pl.BlockSpec((E_STEP, 2 * N), lambda f, at: (f, 0)),
                pl.BlockSpec((2 * N, E_STEP), lambda f, at: (0, f)),
            ],
            scratch_shapes=[pltpu.VMEM((2 * N, 768), BF16), pltpu.VMEM((2 * N, 768), F32)],
        ),
        out_shape=[jax.ShapeDtypeStruct(*v) for v in shapes] + [
            jax.ShapeDtypeStruct((1536, 2 * N), BF16),
            jax.ShapeDtypeStruct((2 * N, 1536), BF16)],
        compiler_params=pltpu.CompilerParams(
            vmem_limit_bytes=18 * 2**20, dimension_semantics=("arbitrary",)),
        cost_estimate=pl.CostEstimate(
            flops=6 * 2 * 512 * 768 * 1536 + 2 * 512 * 768 * 768, bytes_accessed=22 * 2**20,
            transcendentals=2 * 512 * 1536),
        name="experts",
    )(core, *operands)


def kind_row(marks_ref):
    return turned(marks_ref[...])[8:9, :].astype(F32) > 0.0


def branch_kernel(at_ref, inner_t_ref, wd_ref, hidden_ref, marks_ref, *refs):
    own_ref, sib_ref, acc = refs[-3:]
    f = pl.program_id(0)
    text, inner_t, zero = kind_row(marks_ref), inner_t_ref[...], jnp.zeros((), BF16)
    part = (mm(jnp.where(text, zero, inner_t), wd_ref[0], TN)
            + mm(jnp.where(text, inner_t, zero), wd_ref[1], TN))

    @pl.when(f == 0)
    def _():
        acc[...] = part

    @pl.when(f > 0)
    def _():
        acc[...] += part

    @pl.when(f == pl.num_programs(0) - 1)
    def _():
        own_ref[...] = hidden_ref[...] + acc[:N, :]
        sib_ref[...] = acc[N:, :].astype(BF16)


def branches(table, inner_t, w_down, hidden, marks, gates):
    return pl.pallas_call(
        branch_kernel,
        grid_spec=pltpu.PrefetchScalarGridSpec(
            num_scalar_prefetch=1,
            grid=(3,),
            in_specs=[
                pl.BlockSpec((512, 2 * N), lambda f, at: (f, 0)),
                pl.BlockSpec((2, 512, 768), lambda f, at: (0, at[CORE] * 3 + f, 0)),
                pl.BlockSpec((N, 768), lambda f, at: (0, 0)),
                pl.BlockSpec((2 * N, 128), lambda f, at: (0, 0))] + [ANYWHERE] * len(gates),
            out_specs=[pl.BlockSpec((N, 768), lambda f, at: (0, 0))] * 2,
            scratch_shapes=[pltpu.VMEM((2 * N, 768), F32)],
        ),
        out_shape=[jax.ShapeDtypeStruct((N, 768), F32), jax.ShapeDtypeStruct((N, 768), BF16)],
        compiler_params=pltpu.CompilerParams(
            vmem_limit_bytes=20 * 2**20, dimension_semantics=("arbitrary",)),
        cost_estimate=pl.CostEstimate(
            flops=2 * 2 * 512 * 768 * 1536, bytes_accessed=8 * 2**20, transcendentals=0),
        name="branches",
    )(table, inner_t, w_down, hidden, marks, *gates)


def cells_kernel(g, at_slot, act_t_ref, grad_ref, inner_t_ref, cot_own_ref, cot_sib_ref, marks_ref,
                 *refs):
    if g == 0:
        full_ref, keep_ref, send_ref, low_ref, up_acc, down_acc = refs
        low_ref[...] = full_ref[...]
    else:
        keep_ref, send_ref, up_acc, down_acc = refs[-4:]
    zero = jnp.zeros((), BF16)
    text, text_row = marks_ref[:, 8:9].astype(F32) > 0.0, kind_row(marks_ref)
    act_t, inner_t = act_t_ref[...], inner_t_ref[...]
    grad = grad_ref[:, g * FF_STEP : (g + 1) * FF_STEP]
    lanes = slice(g * 256, (g + 1) * 256)
    cot = jnp.concatenate([cot_own_ref[:, lanes], cot_sib_ref[:, lanes]], axis=0)
    for e in range(2):
        up = mm(act_t, jnp.where(text, grad, zero) if e else jnp.where(text, zero, grad))
        up_acc[e, 0] = up[:, :256]
        up_acc[e, 1] = up[:, 256:]
        down_acc[e] = mm(
            jnp.where(text_row, inner_t, zero) if e else jnp.where(text_row, zero, inner_t), cot)

    for n, target in enumerate((keep_ref, send_ref)):
        def cell(i, carry):
            slot = g * 64 + n * 32 + i
            half = at_slot[192 + slot]
            rows = pl.ds(pl.multiple_of(at_slot[slot], 8), 24)
            below = pl.ds(pl.multiple_of(at_slot[384 + slot], 8), 24)
            target[i] = jnp.concatenate(
                [up_acc[0, half, rows, :], up_acc[1, half, rows, :],
                 down_acc[0, below, :], down_acc[1, below, :]], axis=0).astype(BF16)
            return carry
        lax.fori_loop(0, 32, cell, 0, unroll=4)


def cells(g, table, act_t, grad_pre, inner_t, cot_own, cot_sib, marks, more):
    return pl.pallas_call(
        lambda *refs: cells_kernel(g, *refs),
        in_specs=[SMALL] + [WHOLE] * 6 + ([WHOLE] if g == 0 else [ANYWHERE] * len(more)),
        out_specs=[WHOLE] * (3 if g == 0 else 2),
        out_shape=[jax.ShapeDtypeStruct((32, 96, 256), BF16)] * 2
        + [jax.ShapeDtypeStruct((2 * N, 768), BF16)] * (g == 0),
        scratch_shapes=[pltpu.VMEM((2, 2, 768, 256), F32), pltpu.VMEM((2, 1536, 256), F32)],
        compiler_params=pltpu.CompilerParams(vmem_limit_bytes=10 * 2**20),
        cost_estimate=pl.CostEstimate(
            flops=4 * 2 * 512 * 768 * 512, bytes_accessed=8 * 2**20, transcendentals=0),
        name="cells",
    )(table, act_t, grad_pre, inner_t, cot_own, cot_sib, marks, *more)


def cell_places():
    table = np.zeros((32, 4, 4, 3, 4, 4, 4), np.int32)
    for r, s in np.ndindex(32, 4):
        here = {"z": r // 8, "y": r % 4, "x": (s // 2) * 2 + (r // 4) % 2}
        flips = (0, 1, 3, 2) if s % 2 else (0, 3, 1, 2)
        for g, order in enumerate(ORDERS):
            for slot in np.ndindex(4, 4, 4):
                at = {a: here[a] ^ flips[n] for a, n in zip(order, slot)}
                x_hi, x_lo = at["x"] // 2, at["x"] % 2
                table[(r, s, 0, g) + slot] = 24 * (at["z"] * 8 + x_lo * 4 + at["y"])
                table[(r, s, 1, g) + slot] = x_hi
                table[(r, s, 2, g) + slot] = 24 * (
                    (at["z"] % 2) * 32 + x_lo * 16 + at["y"] * 4 + x_hi * 2 + at["z"] // 2)
                table[(r, s, 3, g) + slot] = at["z"] * 16 + x_lo * 8 + at["y"] * 2 + x_hi
    coordinates = np.array([[n % 2, n % 4 // 2] + [0] * 126 for n in range(128)], np.int32)
    return np.concatenate([table.reshape(128, 768), coordinates], axis=1)


def add_up(parts):
    total = parts[0].astype(F32)
    for part in parts[1:]:
        total = total + part.astype(F32)
    return total.astype(BF16)


def pass_kernel(gates, *refs):
    count = (len(refs) - gates) // 3
    for g in range(count):
        refs[2 * count + gates + g][...] = add_up([refs[2 * g][...], refs[2 * g + 1][...]])


ANYWHERE = pl.BlockSpec(memory_space=pl.ANY)


def pass_on(kept, arrived, name, gates=()):
    kept, arrived = ([v[g] for g in (1, 2, 0)] for v in (kept, arrived))
    _, slots, rows, lanes = kept[0].shape
    block = max(slots // 4, 1)
    one = pl.BlockSpec((None, block, rows, lanes), lambda i: (1, i, 0, 0))
    passed = pl.pallas_call(
        lambda *refs: pass_kernel(len(gates), *refs),
        grid=(slots // block,),
        in_specs=[one] * (2 * len(kept)) + [ANYWHERE] * len(gates),
        out_specs=[pl.BlockSpec((block, rows, lanes), lambda i: (i, 0, 0))] * len(kept),
        out_shape=[jax.ShapeDtypeStruct((slots, rows, lanes), BF16)] * len(kept),
        compiler_params=pltpu.CompilerParams(vmem_limit_bytes=6 * 2**20),
        cost_estimate=pl.CostEstimate(
            flops=0, transcendentals=0, bytes_accessed=6 * len(kept) * slots * rows * lanes),
        name=name,
    )(*[v for pair in zip(kept, arrived) for v in pair], *gates)
    return [passed[n] for n in (2, 0, 1)]


def settle_kernel(groups, sizes, *refs):
    ins, outs = refs, refs[-2 * groups :]
    at = 0
    for g in range(groups):
        row = 0
        for size in sizes:
            for half in range(2):
                outs[2 * g + half][:, row : row + size, :] = add_up(
                    [ins[at + k][...] for k in range(3)])
                at += 3
            row += size


def settle(pieces, name, gates=()):
    pieces = [[p[g] for g in (1, 2, 0)] for p in pieces]
    groups = len(pieces[0])
    sizes = [p[0][0].shape[2] for p in pieces]
    _, slots, _, lanes = pieces[0][0][0].shape
    half = slots // 2
    block = max(half // 4, 1)
    steps = half // block
    operands, specs = [], []
    for g in range(groups):
        for p, size in zip(pieces, sizes):
            for h in range(2):
                wide = pl.BlockSpec(
                    (None, block, size, lanes), lambda i, h=h: (0, i + h * steps, 0, 0))
                flat = pl.BlockSpec((block, size, lanes), lambda i, h=h: (i + h * steps, 0, 0))
                operands += list(p[g])
                specs += [wide, wide, flat]
    rows = sum(sizes)
    outs = pl.pallas_call(
        lambda *refs: settle_kernel(groups, sizes, *refs),
        grid=(steps,),
        in_specs=specs + [ANYWHERE] * len(gates),
        out_specs=[pl.BlockSpec((block, rows, lanes), lambda i: (i, 0, 0))] * (2 * groups),
        out_shape=[jax.ShapeDtypeStruct((half, rows, lanes), BF16)] * (2 * groups),
        compiler_params=pltpu.CompilerParams(vmem_limit_bytes=8 * 2**20),
        cost_estimate=pl.CostEstimate(
            flops=0, transcendentals=0, bytes_accessed=8 * groups * slots * rows * lanes),
        name=name,
    )(*operands, *gates)
    shaped = [o.reshape(2, half // 2, rows, lanes) for o in outs]
    return [[shaped[2 * n + h] for n in (2, 0, 1)] for h in range(2)]


def finish_kernel(count, at_ref, *refs):
    outs, down_ref = refs[-5:-1], refs[-1]
    core, far = at_ref[CORE], at_ref[FAR]
    row = lax.broadcasted_iota(jnp.int32, (24, 80), 0)
    column = lax.broadcasted_iota(jnp.int32, (24, 80), 1)
    picks = []
    for n in range(4):
        x_hi, c = far ^ (n // 2), core ^ (n % 2)
        wanted = jnp.where(row == 6, 72, (row // 8) * 24 + x_hi * 12 + c * 6 + row % 8)
        picks.append(jnp.where((column == wanted) & (row % 8 < 6 + (row == 6)), 1.0, 0.0).astype(BF16))
    for g in range(3):
        cell = add_up([refs[3 * g + k][...] for k in range(3)])
        shared = jnp.concatenate([cell[:48], cell[96:]], axis=0)
        for out, pick in zip(outs, picks):
            rows = jnp.concatenate([mm(pick, shared), jnp.zeros((40, 256), F32)], axis=0)
            out[g] = rows.astype(BF16)
        down_ref[g] = cell[48:96]


def finish(table, kept, first, second, gates):
    wide = pl.BlockSpec((None, None, 128, 256), lambda i, t: (0, 0, 0, 0))
    flat = pl.BlockSpec((None, 128, 256), lambda i, t: (0, 0, 0))
    sizes = [64] * 4 + [48]
    return pl.pallas_call(
        lambda *refs: finish_kernel(9, *refs),
        grid_spec=pltpu.PrefetchScalarGridSpec(
            num_scalar_prefetch=1,
            grid=(1,),
            in_specs=[wide, wide, flat] * 3 + [ANYWHERE] * len(gates),
            out_specs=[pl.BlockSpec((3, size, 256), lambda i, t: (0, 0, 0)) for size in sizes],
        ),
        out_shape=[jax.ShapeDtypeStruct((3, size, 256), BF16) for size in sizes],
        compiler_params=pltpu.CompilerParams(vmem_limit_bytes=4 * 2**20),
        name="finish",
    )(table, *[v for g in range(3) for v in (kept[g], first[g], second[g])], *gates)


def after_kernel(values_ref, *refs):
    refs[-1][...] = values_ref[...]


def after(values, gates):
    return pl.pallas_call(
        after_kernel,
        in_specs=[WHOLE] + [ANYWHERE] * len(gates),
        out_specs=WHOLE,
        out_shape=jax.ShapeDtypeStruct(values.shape, values.dtype),
        compiler_params=pltpu.CompilerParams(vmem_limit_bytes=4 * 2**20),
        name="after",
    )(values, *gates)


def put(acc, first, part, rows=slice(None)):
    for n in range(part.shape[1] // 128):
        column = first + n * 128
        lanes = slice(column % 256, column % 256 + 128)
        acc[column // 256, rows, lanes] = part[:, n * 128 : (n + 1) * 128]


def spill_rows(target, acc, at_slot, g, base, extra):
    block = 2 * (g - 1) if g else 0

    def cell(i, carry):
        slot = g * 64 + base + i
        rows = pl.ds(pl.multiple_of(at_slot[slot], 8), 24)
        part = acc[at_slot[192 + slot] + block, rows, :]
        target[i] = jnp.concatenate([part, extra(slot)], axis=0).astype(BF16)
        return carry
    lax.fori_loop(0, 32, cell, 0, unroll=4)


def tail_kernel(at_slot, act_ref, away_ref, q_ref, qb_ref, ka_ref, kb_ref, va_ref, *refs):
    keeps, sends, acc = refs[-5:-3], refs[-3:-1], refs[-1]
    act, away = act_ref[...], away_ref[...]
    near = mm(act, jnp.concatenate(
        [r[: 2 * N, :] for r in (q_ref, qb_ref, ka_ref, kb_ref, va_ref)], axis=1), TN)
    far = mm(away, jnp.concatenate(
        [r[2 * N :, :] for r in (ka_ref, kb_ref, va_ref)], axis=1), TN)
    put(acc, 0, near[:, :384])
    put(acc, 384, near[:, 384:] + far)
    blank = lambda slot: jnp.zeros((8, 256), F32)
    for n in range(2):
        spill_rows(keeps[n], acc, at_slot, n + 1, 0, blank)
        spill_rows(sends[n], acc, at_slot, n + 1, 32, blank)


def tail_cells(table, *operands):
    return pl.pallas_call(
        tail_kernel,
        in_specs=[SMALL] + [WHOLE] * len(operands),
        out_specs=[WHOLE] * 4,
        out_shape=[jax.ShapeDtypeStruct((32, 32, 256), BF16)] * 4,
        scratch_shapes=[pltpu.VMEM((4, 768, 256), F32)],
        compiler_params=pltpu.CompilerParams(vmem_limit_bytes=14 * 2**20),
        cost_estimate=pl.CostEstimate(
            flops=2 * 768 * 512 * (1024 + 640), bytes_accessed=8 * 2**20, transcendentals=0),
        name="tail_cells",
    )(table, *operands)


def inputs_kernel(at_slot, act_ref, away_ref, q_ref, qb_ref, ka_ref, kb_ref, va_ref, vb_ref,
                  att_own_ref, att_sib_ref, proj_ref, own_ref, sib_ref, far_ref, far_sib_ref,
                  second_ref, *refs):
    weights = refs[:3]
    keep_ref, send_ref, cell_keep, cell_send, acc, table = refs[-6:]
    core = at_slot[CORE]
    put(acc, 0, mm(act_ref[...], vb_ref[: 2 * N, :], TN) + mm(away_ref[...], vb_ref[2 * N :, :], TN))
    mine = pl.ds(pl.multiple_of(core * 384, 384), 384)
    other = pl.ds(pl.multiple_of((1 - core) * 384, 384), 384)
    put(acc, 128, mm(att_own_ref[...], proj_ref[...], TN), mine)
    put(acc, 128, mm(att_sib_ref[:N, :], proj_ref[N:, :], TN)
        + mm(att_sib_ref[N:, :], proj_ref[:N, :], TN), other)

    vectors = [jnp.zeros((1, 768), F32)] * 2 + [second_ref[0:1, :], second_ref[1:2, :]]
    wide = list(zip((q_ref, ka_ref, va_ref), (qb_ref, kb_ref, vb_ref), weights))
    for n, ext_ref in enumerate((own_ref, sib_ref, far_ref, far_sib_ref)):
        rows = slice(n * N, (n + 1) * N)
        total = jnp.zeros((N, 768), F32)
        for a_ref, b_ref, w_ref in wide[0 if n < 2 else 1 :]:
            grads = jnp.concatenate([a_ref[rows, :], b_ref[rows, :]], axis=1)
            total += mm(grads, w_ref[...], NT)
        xhat, _ = normalize(ext_ref[:N, :].astype(F32))
        vectors[0] += jnp.sum(total * xhat, axis=0, keepdims=True)
        vectors[1] += jnp.sum(total, axis=0, keepdims=True)
        half = slice((n // 2) * N, (n // 2 + 1) * N)
        if n % 2 == 0:
            keep_ref[half, :] = total
        else:
            send_ref[half, :] = total.astype(BF16)

    chip = lax.broadcasted_iota(jnp.int32, (64, 768), 0)
    owner = lax.broadcasted_iota(jnp.int32, (64, 768), 1) // 12
    feature = lax.broadcasted_iota(jnp.int32, (768, 128), 0) % 12
    lane = lax.broadcasted_iota(jnp.int32, (768, 128), 1)
    spread = jnp.zeros((64, 128), F32)
    for n in range(4):
        line = jnp.broadcast_to(vectors[n], (64, 768))
        values = jnp.where(chip == owner, line, 0.0).astype(BF16)
        spread += mm(values, jnp.where(lane == feature + 12 * n, 1.0, 0.0).astype(BF16))
    table[...] = spread

    def lines(slot):
        row = table[pl.ds(at_slot[576 + slot], 1), :]
        return jnp.concatenate(
            [jnp.broadcast_to(row, (8, 128)), jnp.zeros((8, 128), F32)], axis=1)

    spill_rows(cell_keep, acc, at_slot, 0, 0, lines)
    spill_rows(cell_send, acc, at_slot, 0, 32, lines)


def input_partials(table, operands, gates):
    whole = lambda shape: pl.BlockSpec(shape, lambda i, *_: (0,) * len(shape))
    shapes = [((2 * N, 768), F32), ((2 * N, 768), BF16)] + [((32, 32, 256), BF16)] * 2
    return pl.pallas_call(
        inputs_kernel,
        grid_spec=pltpu.PrefetchScalarGridSpec(
            num_scalar_prefetch=1,
            grid=(1,),
            in_specs=[whole(v.shape) for v in operands[:-1]]
            + [pl.BlockSpec((768, 384), lambda i, at, n=n: (0, 2 * n + at[CORE])) for n in range(3)]
            + [ANYWHERE] * len(gates),
            out_specs=[whole(shape) for shape, _ in shapes],
            scratch_shapes=[pltpu.VMEM((2, 768, 256), F32), pltpu.VMEM((64, 128), F32)],
        ),
        out_shape=[jax.ShapeDtypeStruct(*v) for v in shapes],
        compiler_params=pltpu.CompilerParams(vmem_limit_bytes=16 * 2**20),
        cost_estimate=pl.CostEstimate(
            flops=2 * 768 * 384 * 512 * 7, bytes_accessed=10 * 2**20, transcendentals=0),
        name="input_partials",
    )(table, *operands, *[operands[-1]] * 2, *gates)


def sum_core_kernel(own_ref, sib_ref, *refs):
    refs[-1][...] = (own_ref[...] + sib_ref[...].astype(F32)).astype(BF16)


def sum_core(own, sib, gates):
    half = pl.BlockSpec((N, 768), lambda i: (1, 0))
    return pl.pallas_call(
        sum_core_kernel,
        grid=(1,),
        in_specs=[half, half] + [ANYWHERE] * len(gates),
        out_specs=pl.BlockSpec((N, 768), lambda i: (0, 0)),
        out_shape=jax.ShapeDtypeStruct((N, 768), BF16),
        compiler_params=pltpu.CompilerParams(vmem_limit_bytes=4 * 2**20),
        name="sum_core",
    )(own, sib, *gates)


def token_kernel(tokens_ref, hidden_ref, own_ref, sib_ref, far_ref, gain_ref, out_own_ref,
                 out_sib_ref, grad_ref, out_ref):
    grad = own_ref[...] + sib_ref[...].astype(F32) + far_ref[...].astype(F32)
    xhat, factor = normalize(tokens_ref[...].astype(F32))
    grad_ref[...] = hidden_ref[...] + normalize_back(grad, xhat, factor, wide(gain_ref))
    out_ref[...] = (out_own_ref[...] + out_sib_ref[...].astype(F32)).astype(BF16)


def token_grads(tokens, hidden, own, sib, far, gain, out_own, out_sib):
    half = pl.BlockSpec((N, 768), lambda i: (0, 0))
    return pl.pallas_call(
        token_kernel,
        grid=(1,),
        in_specs=[half] * 5 + [LINE] + [half] * 2,
        out_specs=[half] * 2,
        out_shape=[jax.ShapeDtypeStruct((N, 768), F32), jax.ShapeDtypeStruct((N, 768), BF16)],
        compiler_params=pltpu.CompilerParams(vmem_limit_bytes=8 * 2**20),
        name="token_grads",
    )(tokens, hidden, own, sib, far, gain, out_own, out_sib)


def assemble_kernel(at_ref, own_ref, near_ref, away_ref, cross_ref, down_ref, up_ref, qkv_ref, out_ref,
                    vec_ref, below_ref, held):
    core, far = at_ref[CORE], at_ref[FAR]
    held[far * 2 + core] = own_ref[...]
    held[far * 2 + 1 - core] = near_ref[...]
    held[2 - far * 2 + core] = away_ref[...]
    held[2 - far * 2 + 1 - core] = cross_ref[...]
    line = own_ref[0, :8, :128].astype(F32) + near_ref[0, :8, :128].astype(F32)
    vec_ref[...] = jnp.where(core == 0, line, pltpu.roll(line, 122, 1))
    for x_hi in range(2):
        for c in range(2):
            for g in range(3):
                rows = held[x_hi * 2 + c, g, :32].astype(F32)
                first = c * 1536 + g * 512 + x_hi * 256
                for e in range(2):
                    up_ref[:, e, first : first + 256] = rows[8 * e : 8 * e + 6] * UP_FACTORS[e]
                for n in range(2):
                    at = (g + 2) % 3 * 512 + x_hi * 256 + n * 128
                    kind, within = at // 384, at % 384 + c * 384
                    part = rows[16:22, n * 128 : (n + 1) * 128]
                    if kind < 3:
                        qkv_ref[:, kind * 768 + within : kind * 768 + within + 128] = part
                    else:
                        out_ref[:, within : within + 128] = part
    for g in range(3):
        part = down_ref[g].astype(F32)
        for e in range(2):
            below_ref[e, :, g * 256 : (g + 1) * 256] = part[24 * e : 24 * e + 24] * UP_FACTORS[e]


def assemble(table, *parts):
    return pl.pallas_call(
        assemble_kernel,
        in_specs=[SMALL] + [WHOLE] * 5,
        out_specs=[WHOLE] * 5,
        out_shape=[
            jax.ShapeDtypeStruct((6, 2, 3072), F32),
            jax.ShapeDtypeStruct((6, 2304), F32),
            jax.ShapeDtypeStruct((6, 768), F32),
            jax.ShapeDtypeStruct((8, 128), F32),
            jax.ShapeDtypeStruct((2, 24, 768), F32),
        ],
        scratch_shapes=[pltpu.VMEM((4, 3, 64, 256), BF16)],
        compiler_params=pltpu.CompilerParams(vmem_limit_bytes=4 * 2**20),
        name="assemble",
    )(table, *parts)

def shards(tokens, first_gain, first_shift, w_qkv, w_out, second_gain, second_shift,
           w_up, w_down, modality, segments, partner, cotangent):
    table = lax.dynamic_index_in_dim(
        jnp.asarray(cell_places()), lax.axis_index(BOTH), 0, keepdims=False)

    own = marked(*(in_hbm(v) for v in (partner, tokens[0], segments, modality)))
    away = swap_far(own)
    sib = swap_core(own)
    cot_own = cotangent[0]
    cot_sib = swap_core(cot_own)

    act1, marks, queries, k_near, v_near, qx = project(
        table, own, sib, in_hbm(first_gain), in_hbm(first_shift), in_hbm(w_qkv), True)
    near_both, near_peak = attend_near(queries, k_near, v_near, qx, marks)
    away_sib = swap_core(after(away, [near_peak]))
    act1_away, marks_away, k_away, v_away = project(table, away, away_sib, first_gain, first_shift, w_qkv, False)
    attended, lse = attend_forward(queries, k_away, v_away, qx, marks_away, near_both, near_peak)
    attended_sib = swap_core(attended)

    hidden, grad_act2, xhat2, factor2, act_t, inner_t, grad_pre = experts(
        table, attended, attended_sib, own, sib, cot_own, cot_sib, marks, second_gain, second_shift, w_out,
        in_hbm(w_up), in_hbm(w_down))
    ff_kept, ff_first, more = [], [], [grad_act2]
    for g in range(3):
        keep, gone, *low = cells(g, table, act_t, grad_pre, inner_t, cot_own, cot_sib, marks, more)
        ff_kept.append(keep.reshape(2, 16, 96, 256))
        ff_first.append(send(gone.reshape(2, 16, 96, 256), axis_step(ORDERS[g][0], True)))
        if g == 0:
            grad_sib = swap_core(low[0])
        more = [keep] if g == 0 else [keep, grad_sib]
    hidden_grad, grad_att, proj_half, vectors = middle(
        table, grad_act2, grad_sib, xhat2, factor2, cot_own, cot_sib, second_gain, w_out)

    def along(stage, first, values):
        sent = {g: send(values[g], axis_step(ORDERS[g][stage], first)) for g in (1, 2, 0)}
        return [sent[g] for g in range(3)]

    taken = (queries, k_near, k_away, v_near, v_away, grad_att, attended, qx, marks, marks_away, lse)
    q_a, k_a, v_a = attend_backward(taken, 0, 2, ())
    q_b, k_b, v_b = attend_backward(taken, 2, 1, ())
    cells_a = tail_cells(table, act1, act1_away, q_a, q_b, k_a, k_b, v_a)
    partial_own, partial_low, *cells_b = input_partials(table, (
        act1, act1_away, q_a, q_b, k_a, k_b, v_a, v_b, attended, attended_sib, proj_half,
        own, sib, away, away_sib, vectors, w_qkv), ())
    kept = [v.reshape(2, 16, 32, 256) for v in (cells_b[0], cells_a[0], cells_a[1])]
    first = along(0, True, [v.reshape(2, 16, 32, 256) for v in (cells_b[1], cells_a[2], cells_a[3])])
    ff_second = along(0, False, pass_on(ff_kept, ff_first, "pass_first", [cells_b[0]]))
    partial_sib = swap_core(partial_low)
    passed = pass_on(kept, first, "pass_tail")
    second = along(0, False, passed)
    out_own, out_sib = branches(table, inner_t, w_down, hidden, marks, passed)

    kept, sent = settle(
        [list(zip(ff_kept, ff_first, ff_second)), list(zip(kept, first, second))], "settle_all", [out_sib])
    first = along(1, True, sent)
    second = along(1, False, pass_on(kept, first, "pass_second"))
    kept, sent = settle([list(zip(kept, first, second))], "settle_second")
    first = along(2, True, sent)
    from_far = swap_far(sum_core(partial_own, partial_sib, first))
    second = along(2, False, pass_on(kept, first, "pass_third"))
    held, *shares, down_held = finish(table, kept, first, second, [from_far])

    near, beyond = swap_core(shares[0]), swap_far(shares[1])
    cross = send(shares[2], lambda x, y, z, c: (x ^ 2, y, z, 1 - c))
    below = send(down_held, lambda x, y, z, c: (x, y, 2 * c + z % 2, z // 2))
    up_grad, qkv_grad, out_grad, line, down_grad = assemble(
        table, held, near, beyond, cross, below)

    token_grad, layer_output = token_grads(
        tokens[0], hidden_grad, partial_own, partial_sib, from_far, first_gain, out_own, swap_core(out_sib))

    return (
        layer_output[None], token_grad[None], line[6, :6], line[6, 12:18], qkv_grad, out_grad,
        line[6, 24:30], line[6, 36:42], up_grad.transpose(1, 0, 2), down_grad)


def solution(mesh):
    cut = P("rows", "seq", None)
    flat = P(BOTH)
    placed = (cut,) + (P(),) * 8 + (P("rows", "seq"), P("rows", "seq"), P("rows", None), cut)
    return jax.shard_map(
        shards, mesh=mesh, in_specs=placed,
        out_specs=(cut, cut, flat, flat, P(BOTH, None), P(BOTH, None), flat, flat,
                   P(None, BOTH, None), P(None, BOTH, None)),
        check_vma=False)
```
